32 devices in a mesh: row: 8 (over y, x, core), col: 4 (over z).
Axes of the slice: x: 2, y: 2, z: 4, core: 2. Of those that a mesh axis runs over, the one named last changes fastest.
Arguments:
- frame_first: float32 [4, 2048, 1024], P(None, 'row', 'col'), may hold values from -10 to 10
- frame_second: float32 [4, 2048, 1024], P(None, 'row', 'col'), may hold values from -10 to 10
- shifts: int32 [8, 4, 2], P('row', 'col'), may hold values from -4 to 4, as said below
Outputs:
- flow_field: float32 [2, 2048, 1024], P(None, 'row', 'col')
- coarse_flow: float32 [2, 256, 128], P(None, 'row', 'col')
The draws below stay inside these ranges and needn't reach their ends.
Inputs may be any that keep to these rules, and one draw needn't show every extreme that they name: `shifts`: some tile has displacement 4 along rows and some tile -4 along columns.
All inputs are finite; a program needn't handle non-finite values.
Results may differ from the reference program's by a relative error of at most 0.0003.
Values sent between devices are 32-bit elements; how exact they have to be, the bound alone decides.
No kernel may reach another device: no remote copies, remote signals or barrier semaphores. Data moves between devices by JAX's collectives and lax.ppermute only.
A program may use at most 64 MiB of HBM per device.

```python
import math
import jax
import jax.numpy as jnp
from jax import lax

BANDS = 4
TH = 256
TW = 256
FACTOR = 8
MAXD = 4
ITERS_C = 3
ITERS_F = 3
TILES_R = 8
TILES_C = 4
NX = 2048
NY = 1024
CNX = 256
CNY = 128


def wave_pattern(key, shift_rows, shift_cols):
    periods = jax.random.uniform(jax.random.fold_in(key, 11), (BANDS, 3, 2), jnp.float32, 24.0, 160.0)
    phases = jax.random.uniform(jax.random.fold_in(key, 12), (BANDS, 3, 2), jnp.float32, 0.0, 2.0 * math.pi)
    amplitudes = jax.random.uniform(jax.random.fold_in(key, 13), (BANDS, 3), jnp.float32, 0.5, 1.5)
    row_coords = jnp.arange(NX, dtype=jnp.float32)[None, :, None] + shift_rows
    col_coords = jnp.arange(NY, dtype=jnp.float32)[None, None, :] + shift_cols
    pattern = jnp.zeros((BANDS, NX, NY), jnp.float32)
    for term_index in range(3):
        along_rows = jnp.sin(2.0 * math.pi * row_coords / periods[:, term_index, 0][:, None, None] + phases[:, term_index, 0][:, None, None])
        along_cols = jnp.cos(2.0 * math.pi * col_coords / periods[:, term_index, 1][:, None, None] + phases[:, term_index, 1][:, None, None])
        pattern = pattern + amplitudes[:, term_index][:, None, None] * along_rows * along_cols
    return pattern


def noise_field(key):
    return 0.7 * jax.random.truncated_normal(key, -4.0, 4.0, (BANDS, NX, NY), jnp.float32)


def draw_frame_first(key, part):
    return wave_pattern(key, 0.0, 0.0) + noise_field(jax.random.fold_in(key, 1))


def draw_frame_second(key, part):
    return wave_pattern(key, 1.5, -2.5) + noise_field(jax.random.fold_in(key, 2))


def draw_shifts(key, part):
    values = jax.random.randint(jax.random.fold_in(key, 21), (TILES_R, TILES_C, 2), -MAXD, MAXD + 1, dtype=jnp.int32)
    return values.at[0, 0, 0].set(MAXD).at[0, 0, 1].set(-MAXD)


def setup_inputs(seed: int = 0) -> dict:
    streams_of = jax.random.split(jax.random.key(seed), 4)
    frame_first = draw_frame_first(jax.random.fold_in(streams_of[3], 71), 0)
    frame_second = draw_frame_second(jax.random.fold_in(streams_of[3], 71), 0)
    shifts = draw_shifts(jax.random.fold_in(streams_of[3], 71), 0)
    return {"frame_first": frame_first, "frame_second": frame_second, "shifts": shifts}


tau_step = 0.25
sigma_step = 0.25
data_weight = 0.3
smooth_weight = 0.3

def diff_rows(field_in):
    padded = jnp.pad(field_in, ((0, 0), (1, 1), (0, 0)))
    return 0.5 * (padded[:, 2:, :] - padded[:, :-2, :])

def diff_cols(field_in):
    padded = jnp.pad(field_in, ((0, 0), (0, 0), (1, 1)))
    return 0.5 * (padded[:, :, 2:] - padded[:, :, :-2])

def primal_dual(initial, grad_rows, grad_cols, offset, iterations):
    flow_now = initial
    extrapolated = initial
    dual_rows = jnp.zeros_like(initial)
    dual_cols = jnp.zeros_like(initial)
    dual_data = jnp.zeros_like(offset)
    for iteration in range(iterations):
        dual_rows = dual_rows + sigma_step * diff_rows(extrapolated)
        dual_cols = dual_cols + sigma_step * diff_cols(extrapolated)
        shrink_factor = jnp.maximum(1.0, jnp.sqrt(dual_rows * dual_rows + dual_cols * dual_cols) / smooth_weight)
        dual_rows = dual_rows / shrink_factor
        dual_cols = dual_cols / shrink_factor
        residual = offset + grad_rows * extrapolated[0:1] + grad_cols * extrapolated[1:2]
        dual_data = jnp.clip(dual_data + sigma_step * residual, -data_weight, data_weight)
        divergence = diff_rows(dual_rows) + diff_cols(dual_cols)
        data_pull = jnp.stack([lax.optimization_barrier(jnp.sum(dual_data * grad_rows, axis=0)), lax.optimization_barrier(jnp.sum(dual_data * grad_cols, axis=0))])
        flow_next = flow_now + tau_step * (divergence - data_pull)
        extrapolated = 2.0 * flow_next - flow_now
        flow_now = flow_next
    return flow_now

def reference(frame_first, frame_second, shifts):
    band_count = frame_first.shape[0]
    coarse_first = frame_first.reshape(band_count, CNX, FACTOR, CNY, FACTOR).mean(axis=(2, 4))
    coarse_second = frame_second.reshape(band_count, CNX, FACTOR, CNY, FACTOR).mean(axis=(2, 4))
    coarse_result = primal_dual(jnp.zeros((2, CNX, CNY), jnp.float32), diff_rows(coarse_second), diff_cols(coarse_second), coarse_second - coarse_first, ITERS_C)
    initial = FACTOR * jnp.repeat(jnp.repeat(coarse_result, FACTOR, axis=1), FACTOR, axis=2)
    rim_width = MAXD + 1
    padded = jnp.pad(frame_second, ((0, 0), (rim_width, rim_width), (rim_width, rim_width)))
    row_ids = jnp.arange(TILES_R, dtype=jnp.int32)
    col_ids = jnp.arange(TILES_C, dtype=jnp.int32)

    def tile_window(tile_row, tile_col):
        offsets = shifts[tile_row, tile_col]
        corner = (jnp.int32(0), (tile_row * TH + MAXD + offsets[0]).astype(jnp.int32), (tile_col * TW + MAXD + offsets[1]).astype(jnp.int32))
        return lax.dynamic_slice(padded, corner, (band_count, TH + 2, TW + 2))

    def window_row(tile_row):

        def window_one(tile_col):
            return tile_window(tile_row, tile_col)
        return jax.vmap(window_one)(col_ids)
    windows = jax.vmap(window_row)(row_ids)

    def assemble(blocks):
        return blocks.transpose(2, 0, 3, 1, 4).reshape(band_count, NX, NY)
    warped = assemble(windows[:, :, :, 1:-1, 1:-1])
    grad_rows = assemble(0.5 * (windows[:, :, :, 2:, 1:-1] - windows[:, :, :, :-2, 1:-1]))
    grad_cols = assemble(0.5 * (windows[:, :, :, 1:-1, 2:] - windows[:, :, :, 1:-1, :-2]))
    offset = warped - frame_first - grad_rows * initial[0:1] - grad_cols * initial[1:2]
    flow_result = primal_dual(initial, grad_rows, grad_cols, offset, ITERS_F)
    return (flow_result, coarse_result)
```

```python
import functools

import jax
import jax.numpy as jnp
from jax import lax
from jax.experimental import pallas as pl
from jax.experimental.pallas import tpu as pltpu
from jax.sharding import PartitionSpec as P

FACTOR = 8
MAXD = 4
STEPS = 3
LANES = 128
COLUMNS = 2 * LANES
HALF = 64
SUB = 8
DEPTH = 4
REACH = DEPTH + MAXD + 1
SLOT = 16
C_SECOND = 6
C_FIRST = 5
LEAD = 8
MARGIN = 48
GUARD = 8
LIMIT = 0.3
ALPHA = 0.3

E8 = 0
E1 = 96
F4 = 112
CS = 160
CF = CS + 4 * C_SECOND
META = 208
ROW_MESSAGE = 216


def lanes_of():
    return lax.broadcasted_iota(jnp.int32, (SUB, LANES), 1)


def turn(x, amount):
    amount = amount % LANES
    return x if amount == 0 else pltpu.roll(x, amount, 1)


def split_dot(x, exact):
    high = x.astype(jnp.bfloat16)
    rest = x - high.astype(jnp.float32)
    middle = rest.astype(jnp.bfloat16)
    low = (rest - middle.astype(jnp.float32)).astype(jnp.bfloat16)
    parts = [jnp.dot(part, exact, preferred_element_type=jnp.float32) for part in (low, middle, high)]
    return parts[0] + parts[1] + parts[2]


def scalar_at(ref, row, lane):
    return ref[row : row + 1, lane : lane + 1][0, 0]


def int_at(ref, row, lane):
    return scalar_at(ref, row, lane).astype(jnp.int32)


def first_kernel(second_0, second_1, first_0, first_1, shifts, coarse, to_left, to_right, up, down, sums):
    seconds, firsts = (second_0, second_1), (first_0, first_1)
    bands, height, _ = second_0.shape
    width = COLUMNS
    coarse_height = height // FACTOR
    coarse_width = width // FACTOR
    lane = lanes_of()
    for image, refs in enumerate((seconds, firsts)):
        for band in range(bands):
            plane = image * bands + band
            for tile, ref in enumerate(refs):
                total = ref[band, pl.ds(0, coarse_height, stride=FACTOR), :]
                for k in range(1, FACTOR):
                    total = total + ref[band, pl.ds(k, coarse_height, stride=FACTOR), :]
                at = slice(tile * LANES, (tile + 1) * LANES)
                sums[plane * coarse_height : (plane + 1) * coarse_height, at] = total
    cell = lax.broadcasted_iota(jnp.int32, (width, LANES), 0)
    place = lax.broadcasted_iota(jnp.int32, (width, LANES), 1)
    weights = jnp.where(place - LEAD == cell // FACTOR, 1.0 / (FACTOR * FACTOR), 0.0).astype(jnp.bfloat16)
    means = split_dot(sums[...], weights)
    coarse[...] = means.reshape(2 * bands, coarse_height, LANES)

    def pack(step, carry):
        row = pl.multiple_of(step * SUB, SUB)
        for target, second, first, second_from, first_from in (
            (to_left, second_0, first_0, 0, 0),
            (to_right, second_1, first_1, LANES - REACH, LANES - DEPTH),
        ):
            packed = jnp.zeros((SUB, LANES), jnp.float32)
            for half in range(2):
                rows = pl.ds(row + half * (height // 2), SUB)
                for band in range(bands):
                    at = half * HALF + band * SLOT
                    packed = jnp.where(lane >= at, turn(second[band, rows, :], at - second_from), packed)
                    packed = jnp.where(lane >= at + REACH, turn(first[band, rows, :], at + REACH - first_from), packed)
            target[pl.ds(row, SUB), :] = packed
        return carry

    lax.fori_loop(0, height // 2 // SUB, pack, 0)

    base = height // 2
    for target, start in ((to_left, LEAD), (to_right, LEAD + coarse_width - C_SECOND)):
        for step in range(coarse_height // SUB):
            rows = slice(step * SUB, (step + 1) * SUB)
            packed = jnp.zeros((SUB, LANES), jnp.float32)
            for plane in range(2 * bands):
                at = plane * SLOT
                packed = jnp.where(lane >= at, turn(coarse[plane, rows, :], at - start), packed)
            target[base + step * SUB : base + (step + 1) * SUB, :] = packed
        meta = base + coarse_height
        shift_rows = shifts[0, 0, 0].astype(jnp.float32)
        shift_cols = shifts[0, 0, 1].astype(jnp.float32)
        target[meta : meta + SUB, :] = jnp.where(lane < 32, shift_rows, jnp.where(lane < 64, shift_cols, 1.0))

    up[...] = jnp.zeros_like(up)
    down[...] = jnp.zeros_like(down)
    for band in range(bands):
        for tile in range(2):
            second, first = seconds[tile], firsts[tile]
            k = band * 3 + tile
            up[E8 + 8 * k : E8 + 8 * k + 8, :] = second[band, 0:8, :]
            up[E1 + k : E1 + k + 1, :] = second[band, 8:9, :]
            up[F4 + 4 * k : F4 + 4 * k + 4, :] = first[band, 0:4, :]
            down[E8 + 8 * k : E8 + 8 * k + 8, :] = second[band, height - 8 : height, :]
            down[E1 + k : E1 + k + 1, :] = second[band, height - 9 : height - 8, :]
            down[F4 + 4 * k : F4 + 4 * k + 4, :] = first[band, height - 4 : height, :]


def side_second(from_left, from_right, rows, half, band, lane):
    at = half * HALF + band * SLOT
    right = turn(from_right[rows, :], -at)
    left = turn(from_left[rows, :], LANES - REACH - at)
    return jnp.where(lane < HALF, right, left)


def side_first(from_left, from_right, rows, half, band, lane):
    at = half * HALF + band * SLOT + REACH
    right = turn(from_right[rows, :], -at)
    left = turn(from_left[rows, :], LANES - DEPTH - at)
    return jnp.where(lane < HALF, right, left)


def second_kernel(coarse, from_left, from_right, up_part, down_part, shifts, up, down, wide):
    planes_coarse, coarse_height, _ = coarse.shape
    bands = planes_coarse // 2
    base = from_left.shape[0] - SUB - coarse_height
    height = 2 * base
    coarse_width = COLUMNS // FACTOR
    lane = lanes_of()
    for plane in range(planes_coarse):
        at = plane * SLOT
        for step in range(coarse_height // SUB):
            rows = slice(step * SUB, (step + 1) * SUB)
            from_rows = slice(base + step * SUB, base + (step + 1) * SUB)
            right = turn(from_right[from_rows, :], LEAD + coarse_width - at)
            left = turn(from_left[from_rows, :], LEAD - C_SECOND - at)
            wide[plane, rows, :] = jnp.where(
                lane < LEAD, left, jnp.where(lane < LEAD + coarse_width, coarse[plane, rows, :], right)
            )
    up[...] = up_part[...]
    down[...] = down_part[...]
    side = 2
    planes = 3
    for band in range(bands):
        k = band * planes + side
        top = side_second(from_left, from_right, slice(0, 8), 0, band, lane)
        up[E8 + 8 * k : E8 + 8 * k + 8, :] = top
        top = side_second(from_left, from_right, slice(8, 16), 0, band, lane)
        up[E1 + k : E1 + k + 1, :] = top[0:1]
        top = side_first(from_left, from_right, slice(0, 8), 0, band, lane)
        up[F4 + 4 * k : F4 + 4 * k + 4, :] = top[0:4]
        end = base
        low = side_second(from_left, from_right, slice(end - 8, end), 1, band, lane)
        down[E8 + 8 * k : E8 + 8 * k + 8, :] = low
        low = side_second(from_left, from_right, slice(end - 16, end - 8), 1, band, lane)
        down[E1 + k : E1 + k + 1, :] = low[7:8]
        low = side_first(from_left, from_right, slice(end - 8, end), 1, band, lane)
        down[F4 + 4 * k : F4 + 4 * k + 4, :] = low[4:8]
        for at, plane, count in ((CS, band, C_SECOND), (CF, bands + band, C_FIRST)):
            up[at + count * band : at + count * band + count, :] = wide[plane, 0:count, :]
            down[at + count * band : at + count * band + count, :] = wide[
                plane, coarse_height - count : coarse_height, :
            ]
    meta = base + coarse_height
    left = from_left[meta : meta + SUB, :]
    right = from_right[meta : meta + SUB, :]
    shift_rows = shifts[0, 0, 0].astype(jnp.float32)
    shift_cols = shifts[0, 0, 1].astype(jnp.float32)
    packed = jnp.where(lane < 16, shift_rows, jnp.where(lane < 32, shift_cols, 1.0))
    packed = jnp.where(lane >= 48, turn(left, 48), packed)
    packed = jnp.where(lane >= 64, turn(left, 32), packed)
    packed = jnp.where(lane >= 80, turn(right, 80), packed)
    packed = jnp.where(lane >= 96, turn(right, 64), packed)
    up[META : META + SUB, :] = packed
    down[META : META + SUB, :] = packed


def coarse_flow_of(second, first, mask):
    def along_rows(x):
        size = x.shape[0]
        return pltpu.roll(x, size - 1, 0) - pltpu.roll(x, 1, 0)

    def along_cols(x):
        return pltpu.roll(x, LANES - 1, 1) - pltpu.roll(x, 1, 1)

    grad_rows = [0.125 * along_rows(x) for x in second]
    grad_cols = [0.125 * along_cols(x) for x in second]
    offset = [0.25 * (x - y) for x, y in zip(second, first)]
    data = [jnp.clip(x, -LIMIT, LIMIT) for x in offset]

    def pull(duals, grads):
        total = duals[0] * grads[0]
        for x, y in zip(duals[1:], grads[1:]):
            total = total + x * y
        return total

    flow = [-mask * pull(data, grad_rows), -mask * pull(data, grad_cols)]
    extrapolated = [2.0 * x for x in flow]
    dual_rows = [0.0, 0.0]
    dual_cols = [0.0, 0.0]
    for step in range(1, STEPS):
        for c in range(2):
            rows = dual_rows[c] + 0.125 * along_rows(extrapolated[c])
            cols = dual_cols[c] + 0.125 * along_cols(extrapolated[c])
            norm = jnp.maximum(rows * rows + cols * cols, 1e-30)
            scale = jnp.minimum(mask, ALPHA * lax.rsqrt(norm))
            dual_rows[c] = rows * scale
            dual_cols[c] = cols * scale
        data = [
            jnp.clip(q + o + g * extrapolated[0] + h * extrapolated[1], -LIMIT, LIMIT)
            for q, o, g, h in zip(data, offset, grad_rows, grad_cols)
        ]
        pulls = [pull(data, grad_rows), pull(data, grad_cols)]
        for c in range(2):
            divergence = along_rows(dual_rows[c]) + along_cols(dual_cols[c])
            following = flow[c] + mask * (0.125 * divergence - pulls[c])
            extrapolated[c] = 2.0 * following - flow[c]
            flow[c] = following
    return flow


def upsample(flow, width, target):
    coarse_width = width // FACTOR
    total = width + LANES
    source = lax.broadcasted_iota(jnp.int32, (LANES, total), 0)
    cell = lax.broadcasted_iota(jnp.int32, (LANES, total), 1)
    wanted = jnp.where(
        cell < width + FACTOR, LEAD + cell // FACTOR, jnp.where(cell >= total - FACTOR, LEAD - 1, -1)
    )
    spread = jnp.where(source == wanted, float(FACTOR), 0.0).astype(jnp.bfloat16)
    rows = flow[0].shape[0]
    wide = split_dot(jnp.concatenate(flow, axis=0), spread)
    for c in range(2):
        for tile in range(total // LANES):
            target[c, tile] = wide[c * rows : (c + 1) * rows, tile * LANES : (tile + 1) * LANES]


def data_terms(extended, band, base, firsts, centre, right, left, lane):
    def rows_of(tile, shift):
        start = base + shift
        here = extended[tile][band, pl.ds(start, SUB), :]
        below = extended[tile][band, pl.ds(start + 1, SUB), :]
        above = extended[tile][band, pl.ds(start - 1, SUB), :]
        return here, below - above

    def rolled(x, shift):
        return pltpu.roll(x, lax.rem(LANES - shift, LANES), 1)

    results = []
    here, change = zip(*[rows_of(tile, centre[0]) for tile in range(3)])

    def shifted(fields, shift):
        turned = [rolled(x, shift) for x in fields]
        over = lane + shift >= LANES
        under = lane + shift < 0
        return [
            jnp.where(over, turned[tile + 1], jnp.where(under, turned[tile - 1], turned[tile]))
            for tile in range(2)
        ]

    warped = shifted(here, centre[1])
    grad_rows = shifted(change, centre[1])
    after = shifted(here, centre[1] + 1)
    before = shifted(here, centre[1] - 1)

    low = lane < HALF
    one_here, one_change = rows_of(1, right[0])
    two_here, two_change = rows_of(2, right[0])
    right_here = jnp.where(low, two_here, one_here)
    right_change = jnp.where(low, two_change, one_change)
    zero_here, zero_change = rows_of(0, left[0])
    two_here, two_change = rows_of(2, left[0])
    left_here = jnp.where(low, zero_here, two_here)
    left_change = jnp.where(low, zero_change, two_change)

    def both(x, y, shift):
        return jnp.where(low, rolled(x, right[1] + shift), rolled(y, left[1] + shift))

    warped.append(both(right_here, left_here, 0))
    grad_rows.append(both(right_change, left_change, 0))
    after.append(both(right_here, left_here, 1))
    before.append(both(right_here, left_here, -1))
    for tile in range(3):
        results.append(
            (
                0.25 * (warped[tile] - firsts[tile]),
                0.125 * grad_rows[tile],
                0.125 * (after[tile] - before[tile]),
            )
        )
    return results


def fine_steps(groups, initial, extrap, dual_rows, dual_cols, change, dual_data, offset, grad_rows, grad_cols, mask_of, emit):
    lane = lanes_of()
    first_lane = lane == 0
    last_lane = lane == LANES - 1
    bands = offset.shape[0]

    def columns(fields):
        ahead = [pltpu.roll(x, LANES - 1, 1) for x in fields]
        behind = [pltpu.roll(x, 1, 1) for x in fields]
        return [
            jnp.where(last_lane, ahead[(tile + 1) % 3], ahead[tile])
            - jnp.where(first_lane, behind[(tile + 2) % 3], behind[tile])
            for tile in range(3)
        ]

    for step in range(STEPS):
        source = initial if step == 0 else extrap
        final = step == STEPS - 1

        def dual(k, source=source, step=step):
            row = pl.multiple_of(GUARD + k * SUB, SUB)
            masks = mask_of(k)
            for c in range(2):
                here = [source[c, tile, pl.ds(row, SUB), :] for tile in range(3)]
                along = columns(here)
                for tile in range(3):
                    rows = 0.125 * (
                        source[c, tile, pl.ds(row + 1, SUB), :] - source[c, tile, pl.ds(row - 1, SUB), :]
                    )
                    cols = 0.125 * along[tile]
                    if step > 0:
                        rows = rows + dual_rows[c, tile, pl.ds(row, SUB), :]
                        cols = cols + dual_cols[c, tile, pl.ds(row, SUB), :]
                    norm = jnp.maximum(rows * rows + cols * cols, 1e-30)
                    scale = jnp.minimum(masks[tile], ALPHA * lax.rsqrt(norm))
                    dual_rows[c, tile, pl.ds(row, SUB), :] = rows * scale
                    dual_cols[c, tile, pl.ds(row, SUB), :] = cols * scale

        def primal(k, step=step, final=final):
            row = pl.multiple_of(GUARD + k * SUB, SUB)
            own = pl.ds(pl.multiple_of(k * SUB, SUB), SUB)
            masks = mask_of(k)
            along = [columns([dual_cols[c, tile, pl.ds(row, SUB), :] for tile in range(3)]) for c in range(2)]
            for tile in range(3):
                if final and tile == 2:
                    continue
                start = [initial[c, tile, pl.ds(row, SUB), :] for c in range(2)]
                if step > 0:
                    moved = [extrap[c, tile, pl.ds(row, SUB), :] - start[c] for c in range(2)]
                pulls = [None, None]
                for band in range(bands):
                    gradient = (grad_rows[band, tile, own, :], grad_cols[band, tile, own, :])
                    value = offset[band, tile, own, :]
                    if step > 0:
                        value = value + gradient[0] * moved[0] + gradient[1] * moved[1]
                        value = value + dual_data[band, tile, own, :]
                    value = jnp.clip(value, -LIMIT, LIMIT)
                    if not final:
                        dual_data[band, tile, own, :] = value
                    for c in range(2):
                        term = value * gradient[c]
                        pulls[c] = term if pulls[c] is None else pulls[c] + term
                for c in range(2):
                    divergence = (
                        dual_rows[c, tile, pl.ds(row + 1, SUB), :]
                        - dual_rows[c, tile, pl.ds(row - 1, SUB), :]
                        + along[c][tile]
                    )
                    moving = masks[tile] * (0.125 * divergence - pulls[c])
                    if step == 0:
                        change[c, tile, own, :] = moving
                        extrap[c, tile, pl.ds(row, SUB), :] = start[c] + 2.0 * moving
                    else:
                        old = change[c, tile, own, :]
                        new = old + moving
                        if final:
                            emit(k, c, tile, start[c] + new)
                        else:
                            change[c, tile, own, :] = new
                            extrap[c, tile, pl.ds(row, SUB), :] = start[c] + (2.0 * new - old)

        dual(0)

        def body(k, carry, dual=dual, primal=primal):
            dual(k)
            primal(k - 1)
            return carry

        lax.fori_loop(1, groups, body, 0)
        primal(groups - 1)


def clear_guards(ref, groups):
    for c in range(2):
        for tile in range(3):
            zero = jnp.zeros((GUARD, LANES), jnp.float32)
            ref[c, tile, 0:GUARD, :] = zero
            ref[c, tile, GUARD + groups * SUB : GUARD + groups * SUB + GUARD, :] = zero


def fine_scratch(bands, groups):
    guarded = pltpu.VMEM((2, 3, groups * SUB + 2 * GUARD, LANES), jnp.float32)
    plain = pltpu.VMEM((2, 3, groups * SUB, LANES), jnp.float32)
    per_band = pltpu.VMEM((bands, 3, groups * SUB, LANES), jnp.float32)
    return [guarded, guarded, guarded, guarded, plain, per_band, per_band, per_band, per_band]


def inner_kernel(
    second_0, second_1, first_0, first_1, from_left, from_right, wide, shifts, middle, side, spread,
    initial, extrap, dual_rows, dual_cols, change, dual_data, offset, grad_rows, grad_cols,
):
    bands, height, _ = second_0.shape
    width = COLUMNS
    firsts_refs = (first_0, first_1)
    extended = (second_0, second_1, side)
    coarse_height = height // FACTOR
    coarse_width = width // FACTOR
    begin = MARGIN - SUB
    groups = (height - 2 * begin) // SUB
    lane = lanes_of()
    meta = height // 2 + coarse_height
    centre = (shifts[0, 0, 0], shifts[0, 0, 1])
    right = (int_at(from_right, meta, 0), int_at(from_right, meta, 32))
    left = (int_at(from_left, meta, 0), int_at(from_left, meta, 32))
    side_mask = jnp.where(lane < HALF, scalar_at(from_right, meta, 64), scalar_at(from_left, meta, 64))

    for half in range(2):

        def fill(step, carry, half=half):
            row = pl.multiple_of(step * SUB, SUB)
            into = pl.ds(row + half * (height // 2), SUB)
            for band in range(bands):
                side[band, into, :] = side_second(from_left, from_right, pl.ds(row, SUB), half, band, lane)
            return carry

        lax.fori_loop(0, height // 2 // SUB, fill, 0)

    for half in range(2):
        count = groups // 2

        def terms(step, carry, half=half, count=count):
            row = pl.multiple_of(begin + (step + half * count) * SUB, SUB)
            own = pl.ds(pl.multiple_of((step + half * count) * SUB, SUB), SUB)
            message = pl.ds(pl.multiple_of(row - half * (height // 2), SUB), SUB)
            for band in range(bands):
                firsts = [ref[band, pl.ds(row, SUB), :] for ref in firsts_refs]
                firsts.append(side_first(from_left, from_right, message, half, band, lane))
                results = data_terms(extended, band, row, firsts, centre, right, left, lane)
                for tile in range(3):
                    offset[band, tile, own, :] = results[tile][0]
                    grad_rows[band, tile, own, :] = results[tile][1]
                    grad_cols[band, tile, own, :] = results[tile][2]
            return carry

        lax.fori_loop(0, count, terms, 0)

    mask = jnp.where(
        lane < LEAD,
        scalar_at(from_left, meta, 64),
        jnp.where(lane < LEAD + coarse_width, 1.0, scalar_at(from_right, meta, 64)),
    )
    mask = jnp.concatenate([mask] * (coarse_height // SUB), axis=0)
    flow = coarse_flow_of(
        [wide[band] for band in range(bands)], [wide[bands + band] for band in range(bands)], mask
    )
    upsample(flow, width, spread)
    clear_guards(initial, groups)
    clear_guards(extrap, groups)
    clear_guards(dual_rows, groups)
    for k in range(groups):
        row = GUARD + k * SUB
        cell = begin // FACTOR + k
        for c in range(2):
            for tile in range(3):
                initial[c, tile, row : row + SUB, :] = jnp.broadcast_to(
                    spread[c, tile, cell : cell + 1, :], (SUB, LANES)
                )

    def emit(k, c, tile, value):
        row = pl.multiple_of(jnp.clip(k - 1, 0, groups - 3) * SUB, SUB)

        @pl.when((k > 0) & (k < groups - 1))
        def _():
            middle[c, pl.ds(row, SUB), tile * LANES : (tile + 1) * LANES] = value

    ones = jnp.ones((SUB, LANES), jnp.float32)
    fine_steps(
        groups, initial, extrap, dual_rows, dual_cols, change, dual_data, offset, grad_rows, grad_cols,
        lambda k: (ones, ones, side_mask), emit,
    )


def outer_kernel(
    second_top, second_bottom, first_top, first_bottom, from_left, from_right, from_up, from_down, wide, middle, shifts,
    flow_out, coarse_out, extended, firsts_ref, tall, spread,
    initial, extrap, dual_rows, dual_cols, change, dual_data, offset, grad_rows, grad_cols,
):
    bands, block, width = second_top.shape
    height = flow_out.shape[1]
    coarse_height = height // FACTOR
    coarse_width = width // FACTOR
    each = (MARGIN + 2 * SUB) // SUB
    groups = 2 * each
    part = block + 16
    lane = lanes_of()
    meta = height // 2 + coarse_height

    def keep(step, carry):
        row = pl.multiple_of(step * SUB, SUB)
        for c in range(2):
            flow_out[c, pl.ds(MARGIN + row, SUB), :] = middle[c, pl.ds(row, SUB), :]
        return carry

    lax.fori_loop(0, (height - 2 * MARGIN) // SUB, keep, 0)

    own_right = (int_at(from_right, meta, 0), int_at(from_right, meta, 32))
    own_left = (int_at(from_left, meta, 0), int_at(from_left, meta, 32))
    has_right = scalar_at(from_right, meta, 64)
    has_left = scalar_at(from_left, meta, 64)
    side_mask = jnp.where(lane < HALF, has_right, has_left)
    has_up = scalar_at(from_up, META, 32)
    has_down = scalar_at(from_down, META, 32)

    def trio(message):
        return (
            (int_at(message, META, 0), int_at(message, META, 16)),
            (int_at(message, META, 80), int_at(message, META, 96)),
            (int_at(message, META, 48), int_at(message, META, 64)),
        )

    own = ((shifts[0, 0, 0], shifts[0, 0, 1]), own_right, own_left)
    above = trio(from_up)
    below = trio(from_down)

    zero = jnp.zeros((SUB, LANES), jnp.float32)
    for band in range(bands):
        for tile in range(3):
            k = band * 3 + tile
            extended[band, tile, 0:8, :] = zero
            extended[band, tile, 2 * part - 8 : 2 * part, :] = zero
            extended[band, tile, 7:8, :] = from_up[E1 + k : E1 + k + 1, :]
            extended[band, tile, 8:16, :] = from_up[E8 + 8 * k : E8 + 8 * k + 8, :]
            extended[band, tile, 2 * part - 16 : 2 * part - 8, :] = from_down[E8 + 8 * k : E8 + 8 * k + 8, :]
            extended[band, tile, 2 * part - 8 : 2 * part - 7, :] = from_down[E1 + k : E1 + k + 1, :]
            firsts_ref[band, tile, 0:4, :] = zero[0:4]
            firsts_ref[band, tile, 4:8, :] = from_up[F4 + 4 * k : F4 + 4 * k + 4, :]
            end = groups * SUB
            firsts_ref[band, tile, end - 8 : end - 4, :] = from_down[F4 + 4 * k : F4 + 4 * k + 4, :]
            firsts_ref[band, tile, end - 4 : end, :] = zero[0:4]

    def fill(step, carry):
        row = pl.multiple_of(step * SUB, SUB)
        rows = pl.ds(row, SUB)
        message = pl.ds(pl.multiple_of(height // 2 - block + row, SUB), SUB)
        for band in range(bands):
            for tile in range(2):
                at = slice(tile * LANES, (tile + 1) * LANES)
                extended[band, tile, pl.ds(16 + row, SUB), :] = second_top[band, rows, at]
                extended[band, tile, pl.ds(part + row, SUB), :] = second_bottom[band, rows, at]
            extended[band, 2, pl.ds(16 + row, SUB), :] = side_second(from_left, from_right, rows, 0, band, lane)
            extended[band, 2, pl.ds(part + row, SUB), :] = side_second(from_left, from_right, message, 1, band, lane)
        return carry

    lax.fori_loop(0, block // SUB, fill, 0)

    def fill_first(step, carry):
        row = pl.multiple_of(step * SUB, SUB)
        low_row = pl.multiple_of(SUB + row, SUB)
        message = pl.ds(pl.multiple_of(height // 2 - block + SUB + row, SUB), SUB)
        for band in range(bands):
            for tile in range(2):
                at = slice(tile * LANES, (tile + 1) * LANES)
                firsts_ref[band, tile, pl.ds(SUB + row, SUB), :] = first_top[band, pl.ds(row, SUB), at]
                firsts_ref[band, tile, pl.ds(each * SUB + row, SUB), :] = first_bottom[band, pl.ds(low_row, SUB), at]
            firsts_ref[band, 2, pl.ds(SUB + row, SUB), :] = side_first(
                from_left, from_right, pl.ds(row, SUB), 0, band, lane
            )
            firsts_ref[band, 2, pl.ds(each * SUB + row, SUB), :] = side_first(
                from_left, from_right, message, 1, band, lane
            )
        return carry

    lax.fori_loop(0, each - 1, fill_first, 0)

    planes = [extended.at[:, tile] for tile in range(3)]

    def terms(k, carry):
        base = SUB + k * SUB + jnp.where(k >= each, 16, 0)
        rows = pl.ds(pl.multiple_of(k * SUB, SUB), SUB)

        def choose(i, j):
            return jnp.where(k == 0, above[i][j], jnp.where(k == groups - 1, below[i][j], own[i][j]))

        centre, right, left = [(choose(i, 0), choose(i, 1)) for i in range(3)]
        for band in range(bands):
            firsts = [firsts_ref[band, tile, rows, :] for tile in range(3)]
            results = data_terms(planes, band, base, firsts, centre, right, left, lane)
            for tile in range(3):
                offset[band, tile, rows, :] = results[tile][0]
                grad_rows[band, tile, rows, :] = results[tile][1]
                grad_cols[band, tile, rows, :] = results[tile][2]
        return carry

    lax.fori_loop(0, groups, terms, 0)

    rows_total = coarse_height + 2 * LEAD
    for band in range(bands):
        for plane, at, count in ((band, CS, C_SECOND), (bands + band, CF, C_FIRST)):
            start = at + count * band
            tall[plane, 0:LEAD, :] = zero
            tall[plane, LEAD - count : LEAD, :] = from_up[start : start + count, :]
            tall[plane, LEAD : LEAD + coarse_height, :] = wide[plane]
            tall[plane, LEAD + coarse_height : rows_total, :] = zero
            tall[plane, LEAD + coarse_height : LEAD + coarse_height + count, :] = from_down[start : start + count, :]
    across = jnp.where(lane < LEAD, has_left, jnp.where(lane < LEAD + coarse_width, 1.0, has_right))
    mask = jnp.concatenate([across * has_up] + [across] * (coarse_height // SUB) + [across * has_down], axis=0)
    flow = coarse_flow_of(
        [tall[band] for band in range(bands)], [tall[bands + band] for band in range(bands)], mask
    )
    for c in range(2):
        coarse_out[c] = turn(flow[c][LEAD : LEAD + coarse_height], -LEAD)[:, :coarse_width]
    upsample(flow, width, spread)
    clear_guards(initial, groups)
    clear_guards(extrap, groups)
    clear_guards(dual_rows, groups)
    for k in range(groups):
        row = GUARD + k * SUB
        cell = LEAD - 1 + k if k < each else rows_total - LEAD + 1 - groups + k
        for c in range(2):
            for tile in range(3):
                initial[c, tile, row : row + SUB, :] = jnp.broadcast_to(
                    spread[c, tile, cell : cell + 1, :], (SUB, LANES)
                )

    ones = jnp.ones((SUB, LANES), jnp.float32)

    def mask_of(k):
        row_mask = jnp.where(k == 0, has_up, jnp.where(k == groups - 1, has_down, 1.0))
        plain = ones * row_mask
        return (plain, plain, side_mask * row_mask)

    def emit(k, c, tile, value):
        keep_top = (k > 0) & (k < each - 1)
        keep_bottom = (k > each) & (k < groups - 1)
        row = jnp.where(k < each, (k - 1) * SUB, height - (groups - 1 - k) * SUB)
        row = pl.multiple_of(jnp.clip(row, 0, height - SUB), SUB)

        @pl.when(keep_top | keep_bottom)
        def _():
            flow_out[c, pl.ds(row, SUB), tile * LANES : (tile + 1) * LANES] = value

    fine_steps(
        groups, initial, extrap, dual_rows, dual_cols, change, dual_data, offset, grad_rows, grad_cols, mask_of, emit
    )


def exchange(to_before, to_after, axis):
    count = lax.axis_size(axis)
    from_after = lax.ppermute(to_before, axis, [(i + 1, i) for i in range(count - 1)])
    from_before = lax.ppermute(to_after, axis, [(i, i + 1) for i in range(count - 1)])
    return from_after, from_before


def local(frame_first, frame_second, shifts):
    bands, height, width = frame_first.shape
    assert width == COLUMNS and height % LANES == 0
    coarse_height = height // FACTOR
    coarse_width = width // FACTOR
    vmem = pl.BlockSpec(memory_space=pltpu.VMEM)
    smem = pl.BlockSpec(memory_space=pltpu.SMEM)
    shape = jax.ShapeDtypeStruct
    params = pltpu.CompilerParams(vmem_limit_bytes=48 * 1024 * 1024)
    message_rows = height // 2 + coarse_height + SUB
    col_message = shape((message_rows, LANES), jnp.float32)
    row_message = shape((ROW_MESSAGE, LANES), jnp.float32)
    coarse_shape = shape((2 * bands, coarse_height, LANES), jnp.float32)

    columns_0 = pl.BlockSpec((bands, height, LANES), lambda i: (0, 0, 0))
    columns_1 = pl.BlockSpec((bands, height, LANES), lambda i: (0, 0, 1))

    def whole(array):
        return pl.BlockSpec(array.shape, lambda i: (0,) * len(array.shape))

    coarse, to_left, to_right, up_part, down_part = pl.pallas_call(
        first_kernel,
        grid=(1,),
        out_shape=(coarse_shape, col_message, col_message, row_message, row_message),
        in_specs=[columns_0, columns_1, columns_0, columns_1, smem],
        out_specs=tuple(whole(x) for x in (coarse_shape, col_message, col_message, row_message, row_message)),
        scratch_shapes=[pltpu.VMEM((2 * bands * coarse_height, width), jnp.float32)],
        compiler_params=params,
        name="means_and_messages",
    )(frame_second, frame_second, frame_first, frame_first, shifts)

    from_right, from_left = exchange(to_left, to_right, "col")

    up, down, wide = pl.pallas_call(
        second_kernel,
        out_shape=(row_message, row_message, coarse_shape),
        in_specs=[vmem] * 5 + [smem],
        out_specs=(vmem,) * 3,
        compiler_params=params,
        name="row_messages",
    )(coarse, from_left, from_right, up_part, down_part, shifts)

    from_down, from_up = exchange(up, down, "row")

    begin = MARGIN - SUB
    inner_groups = (height - 2 * begin) // SUB
    middle_shape = shape((2, height - 2 * MARGIN, width), jnp.float32)
    middle = pl.pallas_call(
        inner_kernel,
        grid=(1,),
        out_shape=middle_shape,
        in_specs=[columns_0, columns_1, columns_0, columns_1]
        + [whole(x) for x in (from_left, from_right, wide)]
        + [smem],
        out_specs=whole(middle_shape),
        scratch_shapes=[
            pltpu.VMEM((bands, height, LANES), jnp.float32),
            pltpu.VMEM((2, 3, coarse_height, LANES), jnp.float32),
        ]
        + fine_scratch(bands, inner_groups),
        compiler_params=params,
        cost_estimate=pl.CostEstimate(flops=40_000_000, bytes_accessed=3_000_000, transcendentals=0),
        name="inner_rows",
    )(frame_second, frame_second, frame_first, frame_first, from_left, from_right, wide, shifts)

    block = 64
    outer_groups = 2 * (MARGIN + 2 * SUB) // SUB
    top = pl.BlockSpec((bands, block, width), lambda i: (0, 0, 0))
    bottom = pl.BlockSpec((bands, block, width), lambda i: (0, height // block - 1, 0))
    flow, coarse_flow = pl.pallas_call(
        outer_kernel,
        grid=(1,),
        out_shape=(
            shape((2, height, width), jnp.float32),
            shape((2, coarse_height, coarse_width), jnp.float32),
        ),
        in_specs=[
            top, bottom, top, bottom,
            *[whole(x) for x in (from_left, from_right, from_up, from_down, wide, middle)],
            smem,
        ],
        out_specs=(
            pl.BlockSpec((2, height, width), lambda i: (0, 0, 0)),
            pl.BlockSpec((2, coarse_height, coarse_width), lambda i: (0, 0, 0)),
        ),
        scratch_shapes=[
            pltpu.VMEM((bands, 3, 2 * (block + 16), LANES), jnp.float32),
            pltpu.VMEM((bands, 3, outer_groups * SUB, LANES), jnp.float32),
            pltpu.VMEM((2 * bands, coarse_height + 2 * LEAD, LANES), jnp.float32),
            pltpu.VMEM((2, 3, coarse_height + 2 * LEAD, LANES), jnp.float32),
        ]
        + fine_scratch(bands, outer_groups),
        compiler_params=params,
        name="outer_rows",
    )(
        frame_second, frame_second, frame_first, frame_first, from_left, from_right, from_up, from_down, wide, middle, shifts
    )
    return (flow, coarse_flow)


def solution(mesh):
    return jax.shard_map(
        local,
        mesh=mesh,
        in_specs=(P(None, "row", "col"), P(None, "row", "col"), P("row", "col", None)),
        out_specs=(P(None, "row", "col"), P(None, "row", "col")),
        check_vma=False,
    )
```

```python
import functools

import jax
import jax.numpy as jnp
from jax import lax
from jax.experimental import pallas as pl
from jax.experimental.pallas import tpu as pltpu
from jax.sharding import PartitionSpec as P

FACTOR = 8
MAXD = 4
STEPS = 3
LANES = 128
COLUMNS = 2 * LANES
HALF = 64
SUB = 8
DEPTH = 4
REACH = DEPTH + MAXD + 1
SLOT = 16
C_SECOND = 6
C_FIRST = 5
LEAD = 8
MARGIN = 48
GUARD = 8
LIMIT = 0.3
ALPHA = 0.3

E8 = 0
E1 = 96
F4 = 112
CS = 160
CF = CS + 4 * C_SECOND
META = 208
ROW_MESSAGE = 216

COARSE_A = REACH + DEPTH
COARSE_B = SLOT + REACH + DEPTH
SHIFT_R = 2 * SLOT + REACH + DEPTH
SHIFT_C = SHIFT_R + 1
EXISTS = SHIFT_R + 2


def lanes_of():
    return lax.broadcasted_iota(jnp.int32, (SUB, LANES), 1)


def turn(x, amount):
    amount = amount % LANES
    return x if amount == 0 else pltpu.roll(x, amount, 1)


def split_dot(x, exact):
    high = x.astype(jnp.bfloat16)
    rest = x - high.astype(jnp.float32)
    middle = rest.astype(jnp.bfloat16)
    low = (rest - middle.astype(jnp.float32)).astype(jnp.bfloat16)
    parts = [jnp.dot(part, exact, preferred_element_type=jnp.float32) for part in (low, middle, high)]
    return parts[0] + parts[1] + parts[2]


def scalar_at(ref, row, lane):
    return ref[row : row + 1, lane : lane + 1][0, 0]


def int_at(ref, row, lane):
    return scalar_at(ref, row, lane).astype(jnp.int32)


def first_kernel(
    second_hbm, first_hbm, shifts_hbm, second_0, second_1, first_0, first_1, coarse, to_left, to_right, up, down,
    sums, shifts, sems, shift_sem,
):
    seconds, firsts = (second_0, second_1), (first_0, first_1)
    bands, height, _ = second_0.shape
    width = COLUMNS
    coarse_height = height // FACTOR
    coarse_width = width // FACTOR
    lane = lanes_of()
    get_shifts = pltpu.make_async_copy(shifts_hbm, shifts, shift_sem)
    get_shifts.start()
    copies = []
    for image, (source, refs) in enumerate(((second_hbm, seconds), (first_hbm, firsts))):
        for band in range(bands):
            for tile, ref in enumerate(refs):
                copy = pltpu.make_async_copy(
                    source.at[band, :, pl.ds(tile * LANES, LANES)], ref.at[band], sems.at[image, band, tile]
                )
                copy.start()
                copies.append((image * bands + band, tile, ref, band, copy))
    cell = lax.broadcasted_iota(jnp.int32, (width, LANES), 0)
    place = lax.broadcasted_iota(jnp.int32, (width, LANES), 1)
    weights = jnp.where(place - LEAD == cell // FACTOR, 1.0 / (FACTOR * FACTOR), 0.0).astype(jnp.bfloat16)
    for plane, tile, ref, band, copy in copies:
        copy.wait()
        total = ref[band, pl.ds(0, coarse_height, stride=FACTOR), :]
        for k in range(1, FACTOR):
            total = total + ref[band, pl.ds(k, coarse_height, stride=FACTOR), :]
        at = slice(tile * LANES, (tile + 1) * LANES)
        sums[plane * coarse_height : (plane + 1) * coarse_height, at] = total
    coarse[...] = split_dot(sums[...], weights)
    get_shifts.wait()
    shift_rows = shifts[0, 0, 0].astype(jnp.float32)
    shift_cols = shifts[0, 0, 1].astype(jnp.float32)

    def pack(step, carry):
        row = pl.multiple_of(step * SUB, SUB)
        for target, second, first, second_from, first_from, coarse_from in (
            (to_left, second_0, first_0, 0, 0, LEAD),
            (to_right, second_1, first_1, LANES - REACH, LANES - DEPTH, LEAD + coarse_width - C_SECOND),
        ):
            packed = jnp.zeros((SUB, LANES), jnp.float32)
            for half in range(2):
                rows = pl.ds(row + half * (height // 2), SUB)
                cells = coarse[rows, :]
                for band in range(bands):
                    at = half * HALF + band * SLOT
                    packed = jnp.where(lane >= at, turn(second[band, rows, :], at - second_from), packed)
                    packed = jnp.where(lane >= at + REACH, turn(first[band, rows, :], at + REACH - first_from), packed)
                    at = half * HALF
                    if band == 0:
                        packed = jnp.where(lane >= at + COARSE_A, turn(cells, at + COARSE_A - coarse_from), packed)
                    if band == 1:
                        packed = jnp.where(lane >= at + COARSE_B, turn(cells, at + COARSE_B - coarse_from - 3), packed)
                    if band == 2:
                        packed = jnp.where(lane >= at + SHIFT_R, shift_rows, packed)
                        packed = jnp.where(lane >= at + SHIFT_C, shift_cols, packed)
                        packed = jnp.where(lane >= at + EXISTS, 1.0, packed)
            target[pl.ds(row, SUB), :] = packed
        return carry

    lax.fori_loop(0, height // 2 // SUB, pack, 0, unroll=2)

    up[...] = jnp.zeros_like(up)
    down[...] = jnp.zeros_like(down)
    for band in range(bands):
        for tile in range(2):
            second, first = seconds[tile], firsts[tile]
            k = band * 3 + tile
            up[E8 + 8 * k : E8 + 8 * k + 8, :] = second[band, 0:8, :]
            up[E1 + k : E1 + k + 1, :] = second[band, 8:9, :]
            up[F4 + 4 * k : F4 + 4 * k + 4, :] = first[band, 0:4, :]
            down[E8 + 8 * k : E8 + 8 * k + 8, :] = second[band, height - 8 : height, :]
            down[E1 + k : E1 + k + 1, :] = second[band, height - 9 : height - 8, :]
            down[F4 + 4 * k : F4 + 4 * k + 4, :] = first[band, height - 4 : height, :]


def low_lanes(x):
    return lax.broadcasted_iota(jnp.int32, x.shape, 1) < HALF


def side_second(from_left, from_right, rows, half, band):
    at = half * HALF + band * SLOT
    right = turn(from_right[rows, :], -at)
    left = turn(from_left[rows, :], LANES - REACH - at)
    return jnp.where(low_lanes(right), right, left)


def side_first(from_left, from_right, rows, half, band):
    at = half * HALF + band * SLOT + REACH
    right = turn(from_right[rows, :], -at)
    left = turn(from_left[rows, :], LANES - DEPTH - at)
    return jnp.where(low_lanes(right), right, left)


def column_meta(message):
    return (int_at(message, 0, SHIFT_R), int_at(message, 0, SHIFT_C)), scalar_at(message, 0, EXISTS)


def second_kernel(coarse, to_left, from_left, from_right, up_part, down_part, up, down, wide):
    planes_coarse, coarse_height, _ = wide.shape
    bands = planes_coarse // 2
    end = from_left.shape[0]
    coarse_width = COLUMNS // FACTOR
    lane = lanes_of()
    for plane in range(planes_coarse):
        half, block = divmod(plane, planes_coarse // 2)
        for step in range(coarse_height // SUB):
            own = slice(plane * coarse_height + step * SUB, plane * coarse_height + (step + 1) * SUB)
            rows = slice(block * coarse_height + step * SUB, block * coarse_height + (step + 1) * SUB)
            at = half * HALF
            left = from_left[rows, :]
            right = from_right[rows, :]
            start = LEAD - C_SECOND
            cells = turn(left, start - at - COARSE_A)
            cells = jnp.where(lane >= start + 3, turn(left, start + 3 - at - COARSE_B), cells)
            cells = jnp.where(lane >= LEAD, coarse[own, :], cells)
            start = LEAD + coarse_width
            cells = jnp.where(lane >= start, turn(right, start - at - COARSE_A), cells)
            cells = jnp.where(lane >= start + 3, turn(right, start + 3 - at - COARSE_B), cells)
            wide[plane, step * SUB : (step + 1) * SUB, :] = cells
    up[...] = up_part[...]
    down[...] = down_part[...]
    for band in range(bands):
        k = band * 3 + 2
        up[E8 + 8 * k : E8 + 8 * k + 8, :] = side_second(from_left, from_right, slice(0, 8), 0, band)
        up[E1 + k : E1 + k + 1, :] = side_second(from_left, from_right, slice(8, 16), 0, band)[0:1]
        up[F4 + 4 * k : F4 + 4 * k + 4, :] = side_first(from_left, from_right, slice(0, 8), 0, band)[0:4]
        down[E8 + 8 * k : E8 + 8 * k + 8, :] = side_second(from_left, from_right, slice(end - 8, end), 1, band)
        down[E1 + k : E1 + k + 1, :] = side_second(from_left, from_right, slice(end - 16, end - 8), 1, band)[7:8]
        down[F4 + 4 * k : F4 + 4 * k + 4, :] = side_first(from_left, from_right, slice(end - 8, end), 1, band)[4:8]
        for at, plane, count in ((CS, band, C_SECOND), (CF, bands + band, C_FIRST)):
            up[at + count * band : at + count * band + count, :] = wide[plane, 0:count, :]
            down[at + count * band : at + count * band + count, :] = wide[
                plane, coarse_height - count : coarse_height, :
            ]
    packed = jnp.ones((SUB, LANES), jnp.float32)
    for message, at in ((to_left, 0), (from_left, 48), (from_right, 80)):
        meta = message[0:SUB, :]
        rows = jnp.broadcast_to(meta[:, SHIFT_R : SHIFT_R + 1], (SUB, LANES))
        cols = jnp.broadcast_to(meta[:, SHIFT_C : SHIFT_C + 1], (SUB, LANES))
        packed = jnp.where(lane >= at, rows, packed)
        packed = jnp.where(lane >= at + 16, cols, packed)
        if at == 0:
            packed = jnp.where(lane >= 32, 1.0, packed)
    up[META : META + SUB, :] = packed
    down[META : META + SUB, :] = packed


def coarse_flow_of(second, first, mask):
    def along_rows(x):
        size = x.shape[0]
        return pltpu.roll(x, size - 1, 0) - pltpu.roll(x, 1, 0)

    def along_cols(x):
        return pltpu.roll(x, LANES - 1, 1) - pltpu.roll(x, 1, 1)

    grad_rows = [0.125 * along_rows(x) for x in second]
    grad_cols = [0.125 * along_cols(x) for x in second]
    offset = [0.25 * (x - y) for x, y in zip(second, first)]
    data = [jnp.clip(x, -LIMIT, LIMIT) for x in offset]

    def pull(duals, grads):
        total = duals[0] * grads[0]
        for x, y in zip(duals[1:], grads[1:]):
            total = total + x * y
        return total

    flow = [-mask * pull(data, grad_rows), -mask * pull(data, grad_cols)]
    extrapolated = [2.0 * x for x in flow]
    dual_rows = [0.0, 0.0]
    dual_cols = [0.0, 0.0]
    for step in range(1, STEPS):
        for c in range(2):
            rows = dual_rows[c] + 0.125 * along_rows(extrapolated[c])
            cols = dual_cols[c] + 0.125 * along_cols(extrapolated[c])
            norm = jnp.maximum(rows * rows + cols * cols, 1e-30)
            scale = jnp.minimum(mask, ALPHA * lax.rsqrt(norm))
            dual_rows[c] = rows * scale
            dual_cols[c] = cols * scale
        data = [
            jnp.clip(q + o + g * extrapolated[0] + h * extrapolated[1], -LIMIT, LIMIT)
            for q, o, g, h in zip(data, offset, grad_rows, grad_cols)
        ]
        pulls = [pull(data, grad_rows), pull(data, grad_cols)]
        for c in range(2):
            divergence = along_rows(dual_rows[c]) + along_cols(dual_cols[c])
            following = flow[c] + mask * (0.125 * divergence - pulls[c])
            extrapolated[c] = 2.0 * following - flow[c]
            flow[c] = following
    return flow


def upsample(flow, width, target):
    coarse_width = width // FACTOR
    total = width + LANES
    source = lax.broadcasted_iota(jnp.int32, (LANES, total), 0)
    cell = lax.broadcasted_iota(jnp.int32, (LANES, total), 1)
    wanted = jnp.where(
        cell < width + FACTOR, LEAD + cell // FACTOR, jnp.where(cell >= total - FACTOR, LEAD - 1, -1)
    )
    spread = jnp.where(source == wanted, float(FACTOR), 0.0).astype(jnp.bfloat16)
    rows = flow[0].shape[0]
    wide = split_dot(jnp.concatenate(flow, axis=0), spread)
    for c in range(2):
        for tile in range(total // LANES):
            target[c, tile] = wide[c * rows : (c + 1) * rows, tile * LANES : (tile + 1) * LANES]


def data_terms(extended, band, base, firsts, centre, right, left, lane):
    def rows_of(tile, shift):
        start = base + shift
        here = extended[tile][band, pl.ds(start, SUB), :]
        below = extended[tile][band, pl.ds(start + 1, SUB), :]
        above = extended[tile][band, pl.ds(start - 1, SUB), :]
        return here, below - above

    def rolled(x, shift):
        return pltpu.roll(x, lax.rem(LANES - shift, LANES), 1)

    results = []
    here, change = zip(*[rows_of(tile, centre[0]) for tile in range(3)])

    def shifted(fields, shift):
        turned = [rolled(x, shift) for x in fields]
        over = lane + shift >= LANES
        under = lane + shift < 0
        return [
            jnp.where(over, turned[tile + 1], jnp.where(under, turned[tile - 1], turned[tile]))
            for tile in range(2)
        ]

    warped = shifted(here, centre[1])
    grad_rows = shifted(change, centre[1])
    after = shifted(here, centre[1] + 1)
    before = shifted(here, centre[1] - 1)

    low = lane < HALF
    one_here, one_change = rows_of(1, right[0])
    two_here, two_change = rows_of(2, right[0])
    right_here = jnp.where(low, two_here, one_here)
    right_change = jnp.where(low, two_change, one_change)
    zero_here, zero_change = rows_of(0, left[0])
    two_here, two_change = rows_of(2, left[0])
    left_here = jnp.where(low, zero_here, two_here)
    left_change = jnp.where(low, zero_change, two_change)

    def both(x, y, shift):
        return jnp.where(low, rolled(x, right[1] + shift), rolled(y, left[1] + shift))

    warped.append(both(right_here, left_here, 0))
    grad_rows.append(both(right_change, left_change, 0))
    after.append(both(right_here, left_here, 1))
    before.append(both(right_here, left_here, -1))
    for tile in range(3):
        results.append(
            (
                0.25 * (warped[tile] - firsts[tile]),
                0.125 * grad_rows[tile],
                0.125 * (after[tile] - before[tile]),
            )
        )
    return results


def fine_steps(rows_total, chunk, initial, extrap, dual_rows, dual_cols, change, dual_data, offset, grad_rows, grad_cols, masks_of, result):
    lane = lax.broadcasted_iota(jnp.int32, (chunk, LANES), 1)
    first_lane = lane == 0
    last_lane = lane == LANES - 1
    bands = offset.shape[0]
    chunks = rows_total // chunk
    both = [(c, tile) for c in range(2) for tile in range(3)]

    def columns(fields):
        ahead = [pltpu.roll(x, LANES - 1, 1) for x in fields]
        behind = [pltpu.roll(x, 1, 1) for x in fields]
        return [
            jnp.where(last_lane, ahead[(tile + 1) % 3], ahead[tile])
            - jnp.where(first_lane, behind[(tile + 2) % 3], behind[tile])
            for tile in range(3)
        ]

    for step in range(STEPS):
        source = initial if step == 0 else extrap
        final = step == STEPS - 1

        def dual(k, source=source, step=step):
            row = pl.multiple_of(GUARD + k * chunk, SUB)
            own = pl.ds(pl.multiple_of(k * chunk, SUB), chunk)
            at = pl.ds(row, chunk)
            main, side = masks_of(own)
            masks = (main, main, side)
            here = [[source[c, tile, at, :] for tile in range(3)] for c in range(2)]
            along = [columns(here[c]) for c in range(2)]
            values = []
            for c, tile in both:
                rows = 0.125 * (
                    source[c, tile, pl.ds(row + 1, chunk), :] - source[c, tile, pl.ds(row - 1, chunk), :]
                )
                cols = 0.125 * along[c][tile]
                if step > 0:
                    rows = rows + dual_rows[c, tile, at, :]
                    cols = cols + dual_cols[c, tile, own, :]
                norm = jnp.maximum(rows * rows + cols * cols, 1e-30)
                scale = jnp.minimum(masks[tile], ALPHA * lax.rsqrt(norm))
                values.append((rows * scale, cols * scale))
            for (c, tile), (rows, cols) in zip(both, values):
                dual_rows[c, tile, at, :] = rows
                dual_cols[c, tile, own, :] = cols

        def primal(k, step=step, final=final):
            row = pl.multiple_of(GUARD + k * chunk, SUB)
            own = pl.ds(pl.multiple_of(k * chunk, SUB), chunk)
            at = pl.ds(row, chunk)
            main, side = masks_of(own)
            masks = (main, main, side)
            along = [columns([dual_cols[c, tile, own, :] for tile in range(3)]) for c in range(2)]
            for tile in range(2 if final else 3):
                start = [initial[c, tile, at, :] for c in range(2)]
                if step > 0:
                    moved = [extrap[c, tile, at, :] - start[c] for c in range(2)]
                pulls = [None, None]
                duals = []
                for band in range(bands):
                    gradient = (grad_rows[band, tile, own, :], grad_cols[band, tile, own, :])
                    value = offset[band, tile, own, :]
                    if step > 0:
                        value = value + gradient[0] * moved[0] + gradient[1] * moved[1]
                        value = value + dual_data[band, tile, own, :]
                    value = jnp.clip(value, -LIMIT, LIMIT)
                    duals.append(value)
                    for c in range(2):
                        term = value * gradient[c]
                        pulls[c] = term if pulls[c] is None else pulls[c] + term
                movings = []
                for c in range(2):
                    divergence = (
                        dual_rows[c, tile, pl.ds(row + 1, chunk), :]
                        - dual_rows[c, tile, pl.ds(row - 1, chunk), :]
                        + along[c][tile]
                    )
                    movings.append(masks[tile] * (0.125 * divergence - pulls[c]))
                if step > 0:
                    olds = [change[c, tile, own, :] for c in range(2)]
                for c in range(2):
                    if step == 0:
                        change[c, tile, own, :] = movings[c]
                        extrap[c, tile, at, :] = start[c] + 2.0 * movings[c]
                    else:
                        new = olds[c] + movings[c]
                        if final:
                            result[c, own, tile * LANES : (tile + 1) * LANES] = start[c] + new
                        else:
                            change[c, tile, own, :] = new
                            extrap[c, tile, at, :] = start[c] + (2.0 * new - olds[c])
                if not final:
                    for band in range(bands):
                        dual_data[band, tile, own, :] = duals[band]

        dual(0)

        def body(k, carry, dual=dual, primal=primal):
            dual(k)
            primal(k - 1)
            return carry

        lax.fori_loop(1, chunks, body, 0)
        primal(chunks - 1)


def clear_guards(ref):
    rows = ref.shape[2]
    zero = jnp.zeros((GUARD, LANES), jnp.float32)
    for c in range(2):
        for tile in range(3):
            ref[c, tile, 0:GUARD, :] = zero
            ref[c, tile, rows - GUARD : rows, :] = zero


def fine_scratch(bands, rows):
    guarded = pltpu.VMEM((2, 3, rows + 2 * GUARD, LANES), jnp.float32)
    plain = pltpu.VMEM((2, 3, rows, LANES), jnp.float32)
    per_band = pltpu.VMEM((bands, 3, rows, LANES), jnp.float32)
    return [guarded, guarded, guarded, plain, plain, per_band, per_band, per_band, per_band]


def store_terms(results, band, own, offset, grad_rows, grad_cols):
    for tile in range(3):
        offset[band, tile, own, :] = results[tile][0]
        grad_rows[band, tile, own, :] = results[tile][1]
        grad_cols[band, tile, own, :] = results[tile][2]


def inner_kernel(
    second_0, second_1, first_0, first_1, from_left, from_right, wide, up, middle, side, spread,
    initial, extrap, dual_rows, dual_cols, change, dual_data, offset, grad_rows, grad_cols,
):
    bands, height, _ = second_0.shape
    width = COLUMNS
    firsts_refs = (first_0, first_1)
    extended = (second_0, second_1, side)
    coarse_height = height // FACTOR
    coarse_width = width // FACTOR
    begin = MARGIN - SUB
    rows_total = height - 2 * begin
    groups = rows_total // SUB
    lane = lanes_of()
    centre = (int_at(up, META, 0), int_at(up, META, 16))
    right, has_right = column_meta(from_right)
    left, has_left = column_meta(from_left)

    def fill(step, carry):
        rows = pl.ds(pl.multiple_of(step * SUB, SUB), SUB)
        for half in range(2):
            into = pl.ds(pl.multiple_of(step * SUB + half * (height // 2), SUB), SUB)
            for band in range(bands):
                side[band, into, :] = side_second(from_left, from_right, rows, half, band)
        return carry

    lax.fori_loop(0, height // 2 // SUB, fill, 0, unroll=2)

    def terms(step, carry):
        for half in range(2):
            own_row = pl.multiple_of((step + half * (groups // 2)) * SUB, SUB)
            row = pl.multiple_of(begin + own_row, SUB)
            message = pl.ds(pl.multiple_of(row - half * (height // 2), SUB), SUB)
            for band in range(bands):
                firsts = [ref[band, pl.ds(row, SUB), :] for ref in firsts_refs]
                firsts.append(side_first(from_left, from_right, message, half, band))
                results = data_terms(extended, band, row, firsts, centre, right, left, lane)
                store_terms(results, band, pl.ds(own_row, SUB), offset, grad_rows, grad_cols)
        return carry

    lax.fori_loop(0, groups // 2, terms, 0)

    mask = jnp.where(lane < LEAD, has_left, jnp.where(lane < LEAD + coarse_width, 1.0, has_right))
    mask = jnp.concatenate([mask] * (coarse_height // SUB), axis=0)
    flow = coarse_flow_of(
        [wide[band] for band in range(bands)], [wide[bands + band] for band in range(bands)], mask
    )
    upsample(flow, width, spread)
    clear_guards(initial)
    clear_guards(extrap)
    clear_guards(dual_rows)
    for k in range(groups):
        row = GUARD + k * SUB
        cell = begin // FACTOR + k
        for c in range(2):
            for tile in range(3):
                initial[c, tile, row : row + SUB, :] = jnp.broadcast_to(
                    spread[c, tile, cell : cell + 1, :], (SUB, LANES)
                )

    chunk = 2 * SUB
    ones = jnp.ones((chunk, LANES), jnp.float32)
    side_mask = jnp.where(low_lanes(ones), has_right, has_left)
    fine_steps(
        rows_total, chunk, initial, extrap, dual_rows, dual_cols, change, dual_data, offset, grad_rows, grad_cols,
        lambda own: (ones, side_mask), middle,
    )


def outer_kernel(
    second_0, second_1, first_0, first_1, from_left, from_right, from_up, from_down, wide, middle, up,
    flow_out, coarse_out, extended, firsts_ref, tall, spread, masks, result, coarse_result, sems,
    initial, extrap, dual_rows, dual_cols, change, dual_data, offset, grad_rows, grad_cols,
):
    bands, height, _ = second_0.shape
    width = COLUMNS
    coarse_height = height // FACTOR
    coarse_width = width // FACTOR
    each = MARGIN + 2 * SUB
    rows_total = 2 * each
    block = each
    part = block + 16
    lane = lanes_of()
    begin = MARGIN - SUB

    put_middle = pltpu.make_async_copy(
        middle.at[:, pl.ds(SUB, height - 2 * MARGIN), :], flow_out.at[:, pl.ds(MARGIN, height - 2 * MARGIN), :], sems.at[0]
    )
    put_middle.start()

    own = (int_at(up, META, 0), int_at(up, META, 16))
    own_right, has_right = column_meta(from_right)
    own_left, has_left = column_meta(from_left)
    has_up = scalar_at(from_up, META, 32)
    has_down = scalar_at(from_down, META, 32)

    def trio(message):
        return (
            (int_at(message, META, 0), int_at(message, META, 16)),
            (int_at(message, META, 80), int_at(message, META, 96)),
            (int_at(message, META, 48), int_at(message, META, 64)),
        )

    above = trio(from_up)
    below = trio(from_down)

    zero = jnp.zeros((SUB, LANES), jnp.float32)
    tall_rows = coarse_height + 2 * LEAD
    for band in range(bands):
        for plane, at, count in ((band, CS, C_SECOND), (bands + band, CF, C_FIRST)):
            start = at + count * band
            tall[plane, 0:LEAD, :] = zero
            tall[plane, LEAD - count : LEAD, :] = from_up[start : start + count, :]
            tall[plane, LEAD : LEAD + coarse_height, :] = wide[plane]
            tall[plane, LEAD + coarse_height : tall_rows, :] = zero
            tall[plane, LEAD + coarse_height : LEAD + coarse_height + count, :] = from_down[start : start + count, :]
    across = jnp.where(lane < LEAD, has_left, jnp.where(lane < LEAD + coarse_width, 1.0, has_right))
    mask = jnp.concatenate([across * has_up] + [across] * (coarse_height // SUB) + [across * has_down], axis=0)
    flow = coarse_flow_of(
        [tall[band] for band in range(bands)], [tall[bands + band] for band in range(bands)], mask
    )
    for c in range(2):
        coarse_result[c] = turn(flow[c][LEAD : LEAD + coarse_height], -LEAD)[:, :coarse_width]
    put_coarse = pltpu.make_async_copy(coarse_result, coarse_out, sems.at[1])
    put_coarse.start()
    upsample(flow, width, spread)
    clear_guards(initial)
    clear_guards(extrap)
    clear_guards(dual_rows)
    for k in range(rows_total // SUB):
        row = GUARD + k * SUB
        cell = LEAD - 1 + k if k < each // SUB else tall_rows - LEAD + 1 - rows_total // SUB + k
        for c in range(2):
            for tile in range(3):
                initial[c, tile, row : row + SUB, :] = jnp.broadcast_to(
                    spread[c, tile, cell : cell + 1, :], (SUB, LANES)
                )

    for band in range(bands):
        for tile in range(3):
            k = band * 3 + tile
            extended[tile, band, 0:8, :] = zero
            extended[tile, band, 2 * part - 8 : 2 * part, :] = zero
            extended[tile, band, 7:8, :] = from_up[E1 + k : E1 + k + 1, :]
            extended[tile, band, 8:16, :] = from_up[E8 + 8 * k : E8 + 8 * k + 8, :]
            extended[tile, band, 2 * part - 16 : 2 * part - 8, :] = from_down[E8 + 8 * k : E8 + 8 * k + 8, :]
            extended[tile, band, 2 * part - 8 : 2 * part - 7, :] = from_down[E1 + k : E1 + k + 1, :]
            firsts_ref[0, tile, band, 0:4, :] = zero[0:4]
            firsts_ref[0, tile, band, 4:8, :] = from_up[F4 + 4 * k : F4 + 4 * k + 4, :]
            firsts_ref[1, tile, band, 0:4, :] = from_down[F4 + 4 * k : F4 + 4 * k + 4, :]
            firsts_ref[1, tile, band, 4:8, :] = zero[0:4]

    def fill(step, carry):
        row = pl.multiple_of(step * SUB, SUB)
        top = pl.ds(row, SUB)
        bottom = pl.ds(pl.multiple_of(height - block + row, SUB), SUB)
        message = pl.ds(pl.multiple_of(height // 2 - block + row, SUB), SUB)
        for band in range(bands):
            for tile, ref in enumerate((second_0, second_1)):
                extended[tile, band, pl.ds(16 + row, SUB), :] = ref[band, top, :]
                extended[tile, band, pl.ds(part + row, SUB), :] = ref[band, bottom, :]
            extended[2, band, pl.ds(16 + row, SUB), :] = side_second(from_left, from_right, top, 0, band)
            extended[2, band, pl.ds(part + row, SUB), :] = side_second(from_left, from_right, message, 1, band)
        return carry

    lax.fori_loop(0, block // SUB, fill, 0)

    planes = [extended.at[tile] for tile in range(3)]
    for band in range(bands):
        for end, base, at, (centre, right, left) in (
            (0, SUB, 0, above),
            (1, 2 * part - 2 * SUB, rows_total - SUB, below),
        ):
            firsts = [firsts_ref[end, tile, band] for tile in range(3)]
            results = data_terms(planes, band, base, firsts, centre, right, left, lane)
            store_terms(results, band, slice(at, at + SUB), offset, grad_rows, grad_cols)

    def terms(step, carry):
        row = pl.multiple_of(step * SUB, SUB)
        for half in range(2):
            if half == 0:
                base = 2 * SUB + row
                source = row
                message = row
                at = SUB + row
            else:
                base = part + SUB + row
                source = height - each + SUB + row
                message = height // 2 - each + SUB + row
                at = each + row
            source = pl.ds(pl.multiple_of(source, SUB), SUB)
            message = pl.ds(pl.multiple_of(message, SUB), SUB)
            for band in range(bands):
                firsts = [ref[band, source, :] for ref in (first_0, first_1)]
                firsts.append(side_first(from_left, from_right, message, half, band))
                results = data_terms(planes, band, base, firsts, own, own_right, own_left, lane)
                store_terms(results, band, pl.ds(pl.multiple_of(at, SUB), SUB), offset, grad_rows, grad_cols)
        return carry

    lax.fori_loop(0, each // SUB - 1, terms, 0)

    ones = jnp.ones((rows_total, LANES), jnp.float32)
    sides = jnp.where(low_lanes(ones), has_right, has_left)
    for i, value in enumerate((ones, sides)):
        masks[i] = value
        masks[i, 0:SUB, :] = value[0:SUB] * has_up
        masks[i, rows_total - SUB : rows_total, :] = value[0:SUB] * has_down

    fine_steps(
        rows_total, 2 * SUB, initial, extrap, dual_rows, dual_cols, change, dual_data, offset, grad_rows, grad_cols,
        lambda own: (masks[0, own, :], masks[1, own, :]), result,
    )
    put_top = pltpu.make_async_copy(result.at[:, pl.ds(SUB, MARGIN), :], flow_out.at[:, pl.ds(0, MARGIN), :], sems.at[2])
    put_bottom = pltpu.make_async_copy(
        result.at[:, pl.ds(each + SUB, MARGIN), :], flow_out.at[:, pl.ds(height - MARGIN, MARGIN), :], sems.at[3]
    )
    put_top.start()
    put_bottom.start()
    put_middle.wait()
    put_coarse.wait()
    put_top.wait()
    put_bottom.wait()


def exchange(to_before, to_after, axis):
    count = lax.axis_size(axis)
    from_after = lax.ppermute(to_before, axis, [(i + 1, i) for i in range(count - 1)])
    from_before = lax.ppermute(to_after, axis, [(i, i + 1) for i in range(count - 1)])
    return from_after, from_before


def local(frame_first, frame_second, shifts):
    bands, height, width = frame_first.shape
    assert bands == 4 and width == COLUMNS and height % LANES == 0
    coarse_height = height // FACTOR
    coarse_width = width // FACTOR
    vmem = pl.BlockSpec(memory_space=pltpu.VMEM)
    hbm = pl.BlockSpec(memory_space=pltpu.HBM)
    params = pltpu.CompilerParams(vmem_limit_bytes=48 * 1024 * 1024)

    def shape(*sizes):
        return jax.ShapeDtypeStruct(sizes, jnp.float32)

    plane = shape(bands, height, LANES)
    column_message = shape(height // 2, LANES)
    row_message = shape(ROW_MESSAGE, LANES)

    *frames, coarse, to_left, to_right, up_part, down_part = pl.pallas_call(
        first_kernel,
        out_shape=(
            *[plane] * 4, shape(2 * bands * coarse_height, LANES),
            column_message, column_message, row_message, row_message,
        ),
        in_specs=[hbm] * 3,
        out_specs=(vmem,) * 9,
        scratch_shapes=[
            pltpu.VMEM((2 * bands * coarse_height, width), jnp.float32),
            pltpu.SMEM((1, 1, 2), jnp.int32),
            pltpu.SemaphoreType.DMA((2, bands, 2)),
            pltpu.SemaphoreType.DMA,
        ],
        compiler_params=params,
        name="means_and_messages",
    )(frame_second, frame_first, shifts)

    from_right, from_left = exchange(to_left, to_right, "col")

    up, down, wide = pl.pallas_call(
        second_kernel,
        out_shape=(row_message, row_message, shape(2 * bands, coarse_height, LANES)),
        in_specs=[vmem] * 6,
        out_specs=(vmem,) * 3,
        compiler_params=params,
        name="row_messages",
    )(coarse, to_left, from_left, from_right, up_part, down_part)

    from_down, from_up = exchange(up, down, "row")

    inner_rows = height - 2 * (MARGIN - SUB)
    middle = pl.pallas_call(
        inner_kernel,
        out_shape=shape(2, inner_rows, width),
        in_specs=[vmem] * 8,
        out_specs=vmem,
        scratch_shapes=[
            pltpu.VMEM((bands, height, LANES), jnp.float32),
            pltpu.VMEM((2, 3, coarse_height, LANES), jnp.float32),
        ]
        + fine_scratch(bands, inner_rows),
        compiler_params=params,
        cost_estimate=pl.CostEstimate(flops=40_000_000, bytes_accessed=3_000_000, transcendentals=0),
        name="inner_rows",
    )(*frames, from_left, from_right, wide, up)

    each = MARGIN + 2 * SUB
    tall_rows = coarse_height + 2 * LEAD
    flow, coarse_flow = pl.pallas_call(
        outer_kernel,
        out_shape=(shape(2, height, width), shape(2, coarse_height, coarse_width)),
        in_specs=[vmem] * 11,
        out_specs=(hbm, hbm),
        scratch_shapes=[
            pltpu.VMEM((3, bands, 2 * (each + 16), LANES), jnp.float32),
            pltpu.VMEM((2, 3, bands, SUB, LANES), jnp.float32),
            pltpu.VMEM((2 * bands, tall_rows, LANES), jnp.float32),
            pltpu.VMEM((2, 3, tall_rows, LANES), jnp.float32),
            pltpu.VMEM((2, 2 * each, LANES), jnp.float32),
            pltpu.VMEM((2, 2 * each, width), jnp.float32),
            pltpu.VMEM((2, coarse_height, coarse_width), jnp.float32),
            pltpu.SemaphoreType.DMA((4,)),
        ]
        + fine_scratch(bands, 2 * each),
        compiler_params=params,
        name="outer_rows",
    )(*frames, from_left, from_right, from_up, from_down, wide, middle, up)
    return (flow, coarse_flow)


def solution(mesh):
    return jax.shard_map(
        local,
        mesh=mesh,
        in_specs=(P(None, "row", "col"), P(None, "row", "col"), P("row", "col", None)),
        out_specs=(P(None, "row", "col"), P(None, "row", "col")),
        check_vma=False,
    )
```

```python
import functools

import jax
import jax.numpy as jnp
from jax import lax
from jax.experimental import pallas as pl
from jax.experimental.pallas import tpu as pltpu
from jax.sharding import PartitionSpec as P

FACTOR = 8
MAXD = 4
STEPS = 3
LANES = 128
COLUMNS = 2 * LANES
HALF = 64
SUB = 8
DEPTH = 4
REACH = DEPTH + MAXD + 1
SLOT = 16
C_SECOND = 6
C_FIRST = 5
LEAD = 8
MARGIN = 48
GUARD = 8
BEGIN = 32
EACH = MARGIN + 16
CHUNK = 32
LIMIT = 0.3
ALPHA = 0.3

E8 = 0
E1 = 96
F4 = 112
CS = 160
CF = CS + 4 * C_SECOND
META = 208
ROW_MESSAGE = 216

COARSE_A = REACH + DEPTH
COARSE_B = SLOT + REACH + DEPTH
SHIFT_R = 2 * SLOT + REACH + DEPTH
SHIFT_C = SHIFT_R + 1
EXISTS = SHIFT_R + 2


def lanes_of():
    return lax.broadcasted_iota(jnp.int32, (SUB, LANES), 1)


def turn(x, amount):
    amount = amount % LANES
    return x if amount == 0 else pltpu.roll(x, amount, 1)


def split_dot(x, exact):
    high = x.astype(jnp.bfloat16)
    rest = x - high.astype(jnp.float32)
    middle = rest.astype(jnp.bfloat16)
    low = (rest - middle.astype(jnp.float32)).astype(jnp.bfloat16)
    parts = [jnp.dot(part, exact, preferred_element_type=jnp.float32) for part in (low, middle, high)]
    return parts[0] + parts[1] + parts[2]


def scalar_at(ref, row, lane):
    return ref[row : row + 1, lane : lane + 1][0, 0]


def int_at(ref, row, lane):
    return scalar_at(ref, row, lane).astype(jnp.int32)


def is_even(axis, like):
    return jnp.broadcast_to(lax.axis_index(axis) % 2, like.shape) == 0


def first_kernel(
    second_hbm, first_hbm, shifts_hbm, second_0, second_1, first_0, first_1, coarse, swap_0, swap_1, own_meta, up, down,
    sums, shifts, sems, shift_sem,
):
    seconds, firsts = (second_0, second_1), (first_0, first_1)
    bands, height, _ = second_0.shape
    width = COLUMNS
    coarse_height = height // FACTOR
    coarse_width = width // FACTOR
    lane = lanes_of()
    get_shifts = pltpu.make_async_copy(shifts_hbm, shifts, shift_sem)
    get_shifts.start()
    copies = []
    for image, (source, refs) in enumerate(((second_hbm, seconds), (first_hbm, firsts))):
        for band in range(bands):
            for tile, ref in enumerate(refs):
                copy = pltpu.make_async_copy(
                    source.at[band, :, pl.ds(tile * LANES, LANES)], ref.at[band], sems.at[image, band, tile]
                )
                copy.start()
                copies.append((image * bands + band, tile, ref, band, copy))
    cell = lax.broadcasted_iota(jnp.int32, (width, LANES), 0)
    place = lax.broadcasted_iota(jnp.int32, (width, LANES), 1)
    weights = jnp.where(place - LEAD == cell // FACTOR, 1.0 / (FACTOR * FACTOR), 0.0).astype(jnp.bfloat16)
    for plane, tile, ref, band, copy in copies:
        copy.wait()
        total = ref[band, pl.ds(0, coarse_height, stride=FACTOR), :]
        for k in range(1, FACTOR):
            total = total + ref[band, pl.ds(k, coarse_height, stride=FACTOR), :]
        at = slice(tile * LANES, (tile + 1) * LANES)
        sums[plane * coarse_height : (plane + 1) * coarse_height, at] = total
    coarse[...] = split_dot(sums[...], weights)
    get_shifts.wait()
    shift_rows = shifts[0, 0, 0].astype(jnp.float32)
    shift_cols = shifts[0, 0, 1].astype(jnp.float32)

    even = is_even("col", lane)

    def pack(step, carry):
        row = pl.multiple_of(step * SUB, SUB)
        messages = []
        for second, first, second_from, first_from, coarse_from in (
            (second_0, first_0, 0, 0, LEAD),
            (second_1, first_1, LANES - REACH, LANES - DEPTH, LEAD + coarse_width - C_SECOND),
        ):
            packed = jnp.zeros((SUB, LANES), jnp.float32)
            for half in range(2):
                rows = pl.ds(row + half * (height // 2), SUB)
                cells = coarse[rows, :]
                for band in range(bands):
                    at = half * HALF + band * SLOT
                    packed = jnp.where(lane >= at, turn(second[band, rows, :], at - second_from), packed)
                    packed = jnp.where(lane >= at + REACH, turn(first[band, rows, :], at + REACH - first_from), packed)
                    at = half * HALF
                    if band == 0:
                        packed = jnp.where(lane >= at + COARSE_A, turn(cells, at + COARSE_A - coarse_from), packed)
                    if band == 1:
                        packed = jnp.where(lane >= at + COARSE_B, turn(cells, at + COARSE_B - coarse_from - 3), packed)
                    if band == 2:
                        packed = jnp.where(lane >= at + SHIFT_R, shift_rows, packed)
                        packed = jnp.where(lane >= at + SHIFT_C, shift_cols, packed)
                        packed = jnp.where(lane >= at + EXISTS, 1.0, packed)
            messages.append(packed)
        to_left, to_right = messages
        swap_0[pl.ds(row, SUB), :] = jnp.where(even, to_right, to_left)
        swap_1[pl.ds(row, SUB), :] = jnp.where(even, to_left, to_right)
        return carry

    lax.fori_loop(0, height // 2 // SUB, pack, 0, unroll=2)
    own_meta[...] = jnp.where(lane < HALF, shift_rows, shift_cols)

    up[...] = jnp.zeros_like(up)
    down[...] = jnp.zeros_like(down)
    for band in range(bands):
        for tile in range(2):
            second, first = seconds[tile], firsts[tile]
            k = band * 3 + tile
            up[E8 + 8 * k : E8 + 8 * k + 8, :] = second[band, 0:8, :]
            up[E1 + k : E1 + k + 1, :] = second[band, 8:9, :]
            up[F4 + 4 * k : F4 + 4 * k + 4, :] = first[band, 0:4, :]
            down[E8 + 8 * k : E8 + 8 * k + 8, :] = second[band, height - 8 : height, :]
            down[E1 + k : E1 + k + 1, :] = second[band, height - 9 : height - 8, :]
            down[F4 + 4 * k : F4 + 4 * k + 4, :] = first[band, height - 4 : height, :]


def low_lanes(x):
    return lax.broadcasted_iota(jnp.int32, x.shape, 1) < HALF


def side_second(from_left, from_right, rows, half, band):
    at = half * HALF + band * SLOT
    right = turn(from_right[rows, :], -at)
    left = turn(from_left[rows, :], LANES - REACH - at)
    return jnp.where(low_lanes(right), right, left)


def side_first(from_left, from_right, rows, half, band):
    at = half * HALF + band * SLOT + REACH
    right = turn(from_right[rows, :], -at)
    left = turn(from_left[rows, :], LANES - DEPTH - at)
    return jnp.where(low_lanes(right), right, left)


def column_meta(message):
    return (int_at(message, 0, SHIFT_R), int_at(message, 0, SHIFT_C)), scalar_at(message, 0, EXISTS)


def second_kernel(
    coarse, own_meta, got_0, got_1, up_part, down_part, swap_0, swap_1, from_left, from_right, wide, up, down
):
    even = is_even("col", got_0)
    from_right[...] = jnp.where(even, got_0[...], got_1[...])
    from_left[...] = jnp.where(even, got_1[...], got_0[...])
    planes_coarse, coarse_height, _ = wide.shape
    bands = planes_coarse // 2
    end = from_left.shape[0]
    coarse_width = COLUMNS // FACTOR
    lane = lanes_of()
    for plane in range(planes_coarse):
        half, block = divmod(plane, planes_coarse // 2)
        for step in range(coarse_height // SUB):
            own = slice(plane * coarse_height + step * SUB, plane * coarse_height + (step + 1) * SUB)
            rows = slice(block * coarse_height + step * SUB, block * coarse_height + (step + 1) * SUB)
            at = half * HALF
            left = from_left[rows, :]
            right = from_right[rows, :]
            start = LEAD - C_SECOND
            cells = turn(left, start - at - COARSE_A)
            cells = jnp.where(lane >= start + 3, turn(left, start + 3 - at - COARSE_B), cells)
            cells = jnp.where(lane >= LEAD, coarse[own, :], cells)
            start = LEAD + coarse_width
            cells = jnp.where(lane >= start, turn(right, start - at - COARSE_A), cells)
            cells = jnp.where(lane >= start + 3, turn(right, start + 3 - at - COARSE_B), cells)
            wide[plane, step * SUB : (step + 1) * SUB, :] = cells
    up[...] = up_part[...]
    down[...] = down_part[...]
    for band in range(bands):
        k = band * 3 + 2
        up[E8 + 8 * k : E8 + 8 * k + 8, :] = side_second(from_left, from_right, slice(0, 8), 0, band)
        up[E1 + k : E1 + k + 1, :] = side_second(from_left, from_right, slice(8, 16), 0, band)[0:1]
        up[F4 + 4 * k : F4 + 4 * k + 4, :] = side_first(from_left, from_right, slice(0, 8), 0, band)[0:4]
        down[E8 + 8 * k : E8 + 8 * k + 8, :] = side_second(from_left, from_right, slice(end - 8, end), 1, band)
        down[E1 + k : E1 + k + 1, :] = side_second(from_left, from_right, slice(end - 16, end - 8), 1, band)[7:8]
        down[F4 + 4 * k : F4 + 4 * k + 4, :] = side_first(from_left, from_right, slice(end - 8, end), 1, band)[4:8]
        for at, plane, count in ((CS, band, C_SECOND), (CF, bands + band, C_FIRST)):
            up[at + count * band : at + count * band + count, :] = wide[plane, 0:count, :]
            down[at + count * band : at + count * band + count, :] = wide[
                plane, coarse_height - count : coarse_height, :
            ]
    packed = jnp.where(lane < 16, own_meta[...], jnp.where(lane < 32, turn(own_meta[...], HALF), 1.0))
    for message, at in ((from_left, 48), (from_right, 80)):
        meta = message[0:SUB, :]
        rows = jnp.broadcast_to(meta[:, SHIFT_R : SHIFT_R + 1], (SUB, LANES))
        cols = jnp.broadcast_to(meta[:, SHIFT_C : SHIFT_C + 1], (SUB, LANES))
        packed = jnp.where(lane >= at, rows, packed)
        packed = jnp.where(lane >= at + 16, cols, packed)
    up[META : META + SUB, :] = packed
    down[META : META + SUB, :] = packed
    even = is_even("row", up)
    swap_0[...] = jnp.where(even, down[...], up[...])
    swap_1[...] = jnp.where(even, up[...], down[...])


def coarse_flow_of(second, first, mask):
    def along_rows(x):
        size = x.shape[0]
        return pltpu.roll(x, size - 1, 0) - pltpu.roll(x, 1, 0)

    def along_cols(x):
        return pltpu.roll(x, LANES - 1, 1) - pltpu.roll(x, 1, 1)

    grad_rows = [0.125 * along_rows(x) for x in second]
    grad_cols = [0.125 * along_cols(x) for x in second]
    offset = [0.25 * (x - y) for x, y in zip(second, first)]
    data = [jnp.clip(x, -LIMIT, LIMIT) for x in offset]

    def pull(duals, grads):
        total = duals[0] * grads[0]
        for x, y in zip(duals[1:], grads[1:]):
            total = total + x * y
        return total

    flow = [-mask * pull(data, grad_rows), -mask * pull(data, grad_cols)]
    extrapolated = [2.0 * x for x in flow]
    dual_rows = [0.0, 0.0]
    dual_cols = [0.0, 0.0]
    for step in range(1, STEPS):
        for c in range(2):
            rows = dual_rows[c] + 0.125 * along_rows(extrapolated[c])
            cols = dual_cols[c] + 0.125 * along_cols(extrapolated[c])
            norm = jnp.maximum(rows * rows + cols * cols, 1e-30)
            scale = jnp.minimum(mask, ALPHA * lax.rsqrt(norm))
            dual_rows[c] = rows * scale
            dual_cols[c] = cols * scale
        data = [
            jnp.clip(q + o + g * extrapolated[0] + h * extrapolated[1], -LIMIT, LIMIT)
            for q, o, g, h in zip(data, offset, grad_rows, grad_cols)
        ]
        pulls = [pull(data, grad_rows), pull(data, grad_cols)]
        for c in range(2):
            divergence = along_rows(dual_rows[c]) + along_cols(dual_cols[c])
            following = flow[c] + mask * (0.125 * divergence - pulls[c])
            extrapolated[c] = 2.0 * following - flow[c]
            flow[c] = following
    return flow


def upsample(flow, width, target):
    coarse_width = width // FACTOR
    total = width + LANES
    source = lax.broadcasted_iota(jnp.int32, (LANES, total), 0)
    cell = lax.broadcasted_iota(jnp.int32, (LANES, total), 1)
    wanted = jnp.where(
        cell < width + FACTOR, LEAD + cell // FACTOR, jnp.where(cell >= total - FACTOR, LEAD - 1, -1)
    )
    spread = jnp.where(source == wanted, float(FACTOR), 0.0).astype(jnp.bfloat16)
    rows = flow[0].shape[0]
    wide = split_dot(jnp.concatenate(flow, axis=0), spread)
    for c in range(2):
        for tile in range(total // LANES):
            target[c, tile] = wide[c * rows : (c + 1) * rows, tile * LANES : (tile + 1) * LANES]


def data_terms(extended, band, base, firsts, centre, right, left, lane, side_mask):
    def rows_of(tile, shift):
        start = base + shift
        here = extended[tile][band, pl.ds(start, SUB), :]
        below = extended[tile][band, pl.ds(start + 1, SUB), :]
        above = extended[tile][band, pl.ds(start - 1, SUB), :]
        return here, below - above

    def rolled(x, shift):
        return pltpu.roll(x, lax.rem(LANES - shift, LANES), 1)

    results = []
    here, change = zip(*[rows_of(tile, centre[0]) for tile in range(3)])

    def shifted(fields, shift):
        turned = [rolled(x, shift) for x in fields]
        over = lane + shift >= LANES
        under = lane + shift < 0
        return [
            jnp.where(over, turned[tile + 1], jnp.where(under, turned[tile - 1], turned[tile]))
            for tile in range(2)
        ]

    warped = shifted(here, centre[1])
    grad_rows = shifted(change, centre[1])
    after = shifted(here, centre[1] + 1)
    before = shifted(here, centre[1] - 1)

    low = lane < HALF
    one_here, one_change = rows_of(1, right[0])
    two_here, two_change = rows_of(2, right[0])
    right_here = jnp.where(low, two_here, one_here)
    right_change = jnp.where(low, two_change, one_change)
    zero_here, zero_change = rows_of(0, left[0])
    two_here, two_change = rows_of(2, left[0])
    left_here = jnp.where(low, zero_here, two_here)
    left_change = jnp.where(low, zero_change, two_change)

    def both(x, y, shift):
        return jnp.where(low, rolled(x, right[1] + shift), rolled(y, left[1] + shift))

    warped.append(both(right_here, left_here, 0))
    grad_rows.append(both(right_change, left_change, 0))
    after.append(both(right_here, left_here, 1))
    before.append(both(right_here, left_here, -1))
    for tile in range(3):
        factor = 0.125 if tile < 2 else 0.125 * side_mask
        results.append(
            (
                0.25 * (warped[tile] - firsts[tile]),
                factor * grad_rows[tile],
                factor * (after[tile] - before[tile]),
            )
        )
    return results


def fine_steps(rows_total, chunk, initial, extrap, dual_rows, dual_cols, change, dual_data, offset, grad_rows, grad_cols, masks_of, result):
    lane = lax.broadcasted_iota(jnp.int32, (chunk, LANES), 1)
    first_lane = lane == 0
    last_lane = lane == LANES - 1
    bands = offset.shape[0]
    chunks = rows_total // chunk
    both = [(c, tile) for c in range(2) for tile in range(3)]

    def columns(fields):
        ahead = [pltpu.roll(x, LANES - 1, 1) for x in fields]
        behind = [pltpu.roll(x, 1, 1) for x in fields]
        return [
            jnp.where(last_lane, ahead[(tile + 1) % 3], ahead[tile])
            - jnp.where(first_lane, behind[(tile + 2) % 3], behind[tile])
            for tile in range(3)
        ]

    for step in range(STEPS):
        source = initial if step == 0 else extrap
        final = step == STEPS - 1

        def dual(k, source=source, step=step):
            row = pl.multiple_of(GUARD + k * chunk, SUB)
            own = pl.ds(pl.multiple_of(k * chunk, SUB), chunk)
            at = pl.ds(row, chunk)
            main, side = masks_of(own)
            masks = (main, main, side)
            here = [[source[c, tile, at, :] for tile in range(3)] for c in range(2)]
            along = [columns(here[c]) for c in range(2)]
            values = []
            for c, tile in both:
                rows = source[c, tile, pl.ds(row + 1, chunk), :] - source[c, tile, pl.ds(row - 1, chunk), :]
                cols = along[c][tile]
                if step > 0:
                    rows = rows + dual_rows[c, tile, at, :]
                    cols = cols + dual_cols[c, tile, own, :]
                norm = jnp.maximum(rows * rows + cols * cols, 1e-30)
                scale = jnp.minimum(masks[tile], (8.0 * ALPHA) * lax.rsqrt(norm))
                values.append((rows * scale, cols * scale))
            for (c, tile), (rows, cols) in zip(both, values):
                dual_rows[c, tile, at, :] = rows
                dual_cols[c, tile, own, :] = cols

        def primal(k, step=step, final=final):
            row = pl.multiple_of(GUARD + k * chunk, SUB)
            own = pl.ds(pl.multiple_of(k * chunk, SUB), chunk)
            at = pl.ds(row, chunk)
            main, side = masks_of(own)
            masks = (main, main, side)
            along = [columns([dual_cols[c, tile, own, :] for tile in range(3)]) for c in range(2)]
            for tile in range(2 if final else 3):
                start = [initial[c, tile, at, :] for c in range(2)]
                if step > 0:
                    moved = [extrap[c, tile, at, :] - start[c] for c in range(2)]
                pulls = [None, None]
                duals = []
                for band in range(bands):
                    gradient = (grad_rows[band, tile, own, :], grad_cols[band, tile, own, :])
                    value = offset[band, tile, own, :]
                    if step > 0:
                        value = value + gradient[0] * moved[0] + gradient[1] * moved[1]
                        value = value + dual_data[band, tile, own, :]
                    value = jnp.clip(value, -LIMIT, LIMIT)
                    duals.append(value)
                    for c in range(2):
                        term = value * gradient[c]
                        pulls[c] = term if pulls[c] is None else pulls[c] + term
                movings = []
                for c in range(2):
                    divergence = (
                        dual_rows[c, tile, pl.ds(row + 1, chunk), :]
                        - dual_rows[c, tile, pl.ds(row - 1, chunk), :]
                        + along[c][tile]
                    )
                    movings.append((masks[tile] * (1.0 / 64.0)) * divergence - pulls[c])
                if step > 0:
                    olds = [change[c, tile, own, :] for c in range(2)]
                for c in range(2):
                    if step == 0:
                        change[c, tile, own, :] = movings[c]
                        extrap[c, tile, at, :] = start[c] + 2.0 * movings[c]
                    else:
                        new = olds[c] + movings[c]
                        if final:
                            result[c, own, tile * LANES : (tile + 1) * LANES] = start[c] + new
                        else:
                            change[c, tile, own, :] = new
                            extrap[c, tile, at, :] = start[c] + (new + movings[c])
                if not final:
                    for band in range(bands):
                        dual_data[band, tile, own, :] = duals[band]

        dual(0)

        def body(k, carry, dual=dual, primal=primal):
            dual(k)
            primal(k - 1)
            return carry

        lax.fori_loop(1, chunks, body, 0)
        primal(chunks - 1)


def clear_guards(ref):
    rows = ref.shape[2]
    zero = jnp.zeros((GUARD, LANES), jnp.float32)
    for c in range(2):
        for tile in range(3):
            ref[c, tile, 0:GUARD, :] = zero
            ref[c, tile, rows - GUARD : rows, :] = zero


def fine_scratch(bands, rows):
    guarded = pltpu.VMEM((2, 3, rows + 2 * GUARD, LANES), jnp.float32)
    plain = pltpu.VMEM((2, 3, rows, LANES), jnp.float32)
    per_band = pltpu.VMEM((bands, 3, rows, LANES), jnp.float32)
    return [guarded, guarded, guarded, plain, plain, per_band, per_band, per_band, per_band]


def store_terms(results, band, own, offset, grad_rows, grad_cols):
    for tile in range(3):
        offset[band, tile, own, :] = results[tile][0]
        grad_rows[band, tile, own, :] = results[tile][1]
        grad_cols[band, tile, own, :] = results[tile][2]


def inner_kernel(
    second_0, second_1, first_0, first_1, from_left, from_right, wide, own_meta,
    middle, outer_offset, outer_grad_rows, outer_grad_cols, side, spread,
    initial, extrap, dual_rows, dual_cols, change, dual_data, offset, grad_rows, grad_cols,
):
    bands, height, _ = second_0.shape
    width = COLUMNS
    firsts_refs = (first_0, first_1)
    extended = (second_0, second_1, side)
    coarse_height = height // FACTOR
    coarse_width = width // FACTOR
    rows_total = height - 2 * BEGIN
    groups = height // SUB
    lane = lanes_of()
    centre = (int_at(own_meta, 0, 0), int_at(own_meta, 0, HALF))
    right, has_right = column_meta(from_right)
    left, has_left = column_meta(from_left)
    side_mask = jnp.where(lane < HALF, has_right, has_left)

    def fill(step, carry):
        rows = pl.ds(pl.multiple_of(step * SUB, SUB), SUB)
        values = [
            (half, band, side_second(from_left, from_right, rows, half, band)) for half in range(2) for band in range(bands)
        ]
        for half, band, value in values:
            side[band, pl.ds(pl.multiple_of(step * SUB + half * (height // 2), SUB), SUB), :] = value
        return carry

    lax.fori_loop(0, height // 2 // SUB, fill, 0, unroll=2)

    def terms(step, carry, to_inner, to_outer):
        for half in range(2):
            row = step * SUB if half == 0 else (groups - 1 - step) * SUB
            row = pl.multiple_of(row, SUB)
            message = pl.ds(pl.multiple_of(row - half * (height // 2), SUB), SUB)
            results = []
            for band in range(bands):
                firsts = [ref[band, pl.ds(row, SUB), :] for ref in firsts_refs]
                firsts.append(side_first(from_left, from_right, message, half, band))
                results.append(data_terms(extended, band, row, firsts, centre, right, left, lane, side_mask))
            for band in range(bands):
                if to_inner:
                    own = pl.ds(pl.multiple_of(row - BEGIN, SUB), SUB)
                    store_terms(results[band], band, own, offset, grad_rows, grad_cols)
                if to_outer:
                    at = row + SUB if half == 0 else row - (height - 2 * EACH + SUB)
                    own = pl.ds(pl.multiple_of(at, SUB), SUB)
                    store_terms(results[band], band, own, outer_offset, outer_grad_rows, outer_grad_cols)
        return carry

    first_inner = BEGIN // SUB
    end_outer = EACH // SUB - 1
    lax.fori_loop(1, first_inner, functools.partial(terms, to_inner=False, to_outer=True), 0)
    lax.fori_loop(first_inner, end_outer, functools.partial(terms, to_inner=True, to_outer=True), 0)
    lax.fori_loop(end_outer, groups // 2, functools.partial(terms, to_inner=True, to_outer=False), 0)

    mask = jnp.where(lane < LEAD, has_left, jnp.where(lane < LEAD + coarse_width, 1.0, has_right))
    mask = jnp.concatenate([mask] * (coarse_height // SUB), axis=0)
    flow = coarse_flow_of(
        [wide[band] for band in range(bands)], [wide[bands + band] for band in range(bands)], mask
    )
    upsample(flow, width, spread)
    clear_guards(initial)
    clear_guards(extrap)
    clear_guards(dual_rows)
    for k in range(rows_total // SUB):
        row = GUARD + k * SUB
        cell = BEGIN // FACTOR + k
        for c in range(2):
            for tile in range(3):
                initial[c, tile, row : row + SUB, :] = jnp.broadcast_to(
                    spread[c, tile, cell : cell + 1, :], (SUB, LANES)
                )

    ones = jnp.ones((CHUNK, LANES), jnp.float32)
    side_masks = jnp.where(low_lanes(ones), has_right, has_left)
    fine_steps(
        rows_total, CHUNK, initial, extrap, dual_rows, dual_cols, change, dual_data, offset, grad_rows, grad_cols,
        lambda own: (ones, side_masks), middle,
    )


def outer_kernel(
    second_0, second_1, first_0, first_1, from_left, from_right, wide, got_0, got_1, middle, own_meta,
    _offset, _grad_rows, _grad_cols,
    flow_out, coarse_out, offset, grad_rows, grad_cols,
    from_up, from_down, extended, tall, spread, masks, result, coarse_result, sems,
    initial, extrap, dual_rows, dual_cols, change, dual_data,
):
    bands, height, _ = second_0.shape
    width = COLUMNS
    coarse_height = height // FACTOR
    coarse_width = width // FACTOR
    rows_total = 2 * EACH
    lane = lanes_of()

    put_middle = pltpu.make_async_copy(
        middle.at[:, pl.ds(MARGIN - BEGIN, height - 2 * MARGIN), :],
        flow_out.at[:, pl.ds(MARGIN, height - 2 * MARGIN), :],
        sems.at[0],
    )
    put_middle.start()

    even = is_even("row", got_0)
    from_down[...] = jnp.where(even, got_0[...], got_1[...])
    from_up[...] = jnp.where(even, got_1[...], got_0[...])

    own = (int_at(own_meta, 0, 0), int_at(own_meta, 0, HALF))
    own_right, has_right = column_meta(from_right)
    own_left, has_left = column_meta(from_left)
    has_up = scalar_at(from_up, META, 32)
    has_down = scalar_at(from_down, META, 32)
    side_mask = jnp.where(lane < HALF, has_right, has_left)

    def trio(message):
        return (
            (int_at(message, META, 0), int_at(message, META, 16)),
            (int_at(message, META, 80), int_at(message, META, 96)),
            (int_at(message, META, 48), int_at(message, META, 64)),
        )

    above = trio(from_up)
    below = trio(from_down)

    zero = jnp.zeros((SUB, LANES), jnp.float32)
    tall_rows = coarse_height + 2 * LEAD
    for band in range(bands):
        for plane, at, count in ((band, CS, C_SECOND), (bands + band, CF, C_FIRST)):
            start = at + count * band
            tall[plane, 0:LEAD, :] = zero
            tall[plane, LEAD - count : LEAD, :] = from_up[start : start + count, :]
            tall[plane, LEAD : LEAD + coarse_height, :] = wide[plane]
            tall[plane, LEAD + coarse_height : tall_rows, :] = zero
            tall[plane, LEAD + coarse_height : LEAD + coarse_height + count, :] = from_down[start : start + count, :]
    across = jnp.where(lane < LEAD, has_left, jnp.where(lane < LEAD + coarse_width, 1.0, has_right))
    mask = jnp.concatenate([across * has_up] + [across] * (coarse_height // SUB) + [across * has_down], axis=0)
    flow = coarse_flow_of(
        [tall[band] for band in range(bands)], [tall[bands + band] for band in range(bands)], mask
    )
    for c in range(2):
        coarse_result[c] = turn(flow[c][LEAD : LEAD + coarse_height], -LEAD)[:, :coarse_width]
    put_coarse = pltpu.make_async_copy(coarse_result, coarse_out, sems.at[1])
    put_coarse.start()
    upsample(flow, width, spread)
    clear_guards(initial)
    clear_guards(extrap)
    clear_guards(dual_rows)
    for k in range(rows_total // SUB):
        row = GUARD + k * SUB
        cell = LEAD - 1 + k if k < EACH // SUB else tall_rows - LEAD + 1 - rows_total // SUB + k
        for c in range(2):
            for tile in range(3):
                initial[c, tile, row : row + SUB, :] = jnp.broadcast_to(
                    spread[c, tile, cell : cell + 1, :], (SUB, LANES)
                )

    for end in range(2):
        message = (from_up, from_down)[end]
        for band in range(bands):
            for tile in range(3):
                k = band * 3 + tile
                eight = message[E8 + 8 * k : E8 + 8 * k + 8, :]
                one = message[E1 + k : E1 + k + 1, :]
                source = (second_0, second_1, None)[tile]
                if end == 0:
                    extended[end, tile, band, 0:8, :] = zero
                    extended[end, tile, band, 7:8, :] = one
                    extended[end, tile, band, 8:16, :] = eight
                    if source is None:
                        own_rows = side_second(from_left, from_right, slice(0, 24), 0, band)
                    else:
                        own_rows = source[band, 0:24, :]
                    extended[end, tile, band, 16:40, :] = own_rows
                else:
                    if source is None:
                        own_rows = side_second(from_left, from_right, slice(height // 2 - 24, height // 2), 1, band)
                    else:
                        own_rows = source[band, height - 24 : height, :]
                    extended[end, tile, band, 0:24, :] = own_rows
                    extended[end, tile, band, 24:32, :] = eight
                    extended[end, tile, band, 32:40, :] = zero
                    extended[end, tile, band, 32:33, :] = one
    for end in range(2):
        planes = [extended.at[end, tile] for tile in range(3)]
        message = (from_up, from_down)[end]
        exists = (has_up, has_down)[end]
        halo_at, own_at = ((0, SUB), (rows_total - SUB, rows_total - 2 * SUB))[end]
        halo_base, own_base = ((SUB, 2 * SUB), (3 * SUB, 2 * SUB))[end]
        centre, right, left = (above, below)[end]
        quarter = jnp.zeros((DEPTH, LANES), jnp.float32)
        for band in range(bands):
            firsts = []
            for tile in range(3):
                k = band * 3 + tile
                four = message[F4 + 4 * k : F4 + 4 * k + 4, :]
                firsts.append(jnp.concatenate([quarter, four] if end == 0 else [four, quarter], axis=0))
            results = data_terms(planes, band, halo_base, firsts, centre, right, left, lane, side_mask)
            results = [(x, exists * y, exists * z) for x, y, z in results]
            store_terms(results, band, slice(halo_at, halo_at + SUB), offset, grad_rows, grad_cols)
            rows = slice(0, SUB) if end == 0 else slice(height - SUB, height)
            message_rows = slice(0, SUB) if end == 0 else slice(height // 2 - SUB, height // 2)
            firsts = [ref[band, rows, :] for ref in (first_0, first_1)]
            firsts.append(side_first(from_left, from_right, message_rows, end, band))
            results = data_terms(planes, band, own_base, firsts, own, own_right, own_left, lane, side_mask)
            store_terms(results, band, slice(own_at, own_at + SUB), offset, grad_rows, grad_cols)

    ones = jnp.ones((rows_total, LANES), jnp.float32)
    sides = jnp.where(low_lanes(ones), has_right, has_left)
    for i, value in enumerate((ones, sides)):
        masks[i] = value
        masks[i, 0:SUB, :] = value[0:SUB] * has_up
        masks[i, rows_total - SUB : rows_total, :] = value[0:SUB] * has_down

    fine_steps(
        rows_total, CHUNK, initial, extrap, dual_rows, dual_cols, change, dual_data, offset, grad_rows, grad_cols,
        lambda own: (masks[0, own, :], masks[1, own, :]), result,
    )
    put_top = pltpu.make_async_copy(result.at[:, pl.ds(SUB, MARGIN), :], flow_out.at[:, pl.ds(0, MARGIN), :], sems.at[2])
    put_bottom = pltpu.make_async_copy(
        result.at[:, pl.ds(EACH + SUB, MARGIN), :], flow_out.at[:, pl.ds(height - MARGIN, MARGIN), :], sems.at[3]
    )
    put_top.start()
    put_bottom.start()
    put_middle.wait()
    put_coarse.wait()
    put_top.wait()
    put_bottom.wait()


def exchange(swap_0, swap_1, axis):
    count = lax.axis_size(axis)
    got = []
    for start, message in ((0, swap_0), (1, swap_1)):
        pairs = [(i, i + 1) for i in range(start, count - 1, 2)]
        got.append(lax.ppermute(message, axis, pairs + [(j, i) for i, j in pairs]))
    return got


def local(frame_first, frame_second, shifts):
    bands, height, width = frame_first.shape
    assert bands == 4 and width == COLUMNS and height % LANES == 0
    coarse_height = height // FACTOR
    coarse_width = width // FACTOR
    vmem = pl.BlockSpec(memory_space=pltpu.VMEM)
    hbm = pl.BlockSpec(memory_space=pltpu.HBM)
    params = pltpu.CompilerParams(vmem_limit_bytes=40 * 1024 * 1024)

    def shape(*sizes):
        return jax.ShapeDtypeStruct(sizes, jnp.float32)

    plane = shape(bands, height, LANES)
    column_message = shape(height // 2, LANES)
    row_message = shape(ROW_MESSAGE, LANES)
    meta = shape(SUB, LANES)

    *frames, coarse, swap_0, swap_1, own_meta, up_part, down_part = pl.pallas_call(
        first_kernel,
        out_shape=(
            *[plane] * 4, shape(2 * bands * coarse_height, LANES),
            column_message, column_message, meta, row_message, row_message,
        ),
        in_specs=[hbm] * 3,
        out_specs=(vmem,) * 10,
        scratch_shapes=[
            pltpu.VMEM((2 * bands * coarse_height, width), jnp.float32),
            pltpu.SMEM((1, 1, 2), jnp.int32),
            pltpu.SemaphoreType.DMA((2, bands, 2)),
            pltpu.SemaphoreType.DMA,
        ],
        compiler_params=params,
        name="means_and_messages",
    )(*[pltpu.with_memory_space_constraint(x, pltpu.HBM) for x in (frame_second, frame_first, shifts)])

    got_0, got_1 = exchange(swap_0, swap_1, "col")

    swap_0, swap_1, from_left, from_right, wide = pl.pallas_call(
        second_kernel,
        out_shape=(row_message, row_message, column_message, column_message, shape(2 * bands, coarse_height, LANES)),
        in_specs=[vmem] * 6,
        out_specs=(vmem,) * 5,
        scratch_shapes=[pltpu.VMEM((ROW_MESSAGE, LANES), jnp.float32)] * 2,
        compiler_params=params,
        name="row_messages",
    )(coarse, own_meta, got_0, got_1, up_part, down_part)

    got_0, got_1 = exchange(swap_0, swap_1, "row")

    inner_rows = height - 2 * BEGIN
    outer_terms = shape(bands, 3, 2 * EACH, LANES)
    middle, *terms = pl.pallas_call(
        inner_kernel,
        out_shape=(shape(2, inner_rows, width), outer_terms, outer_terms, outer_terms),
        in_specs=[vmem] * 8,
        out_specs=(vmem,) * 4,
        scratch_shapes=[
            pltpu.VMEM((bands, height, LANES), jnp.float32),
            pltpu.VMEM((2, 3, coarse_height, LANES), jnp.float32),
        ]
        + fine_scratch(bands, inner_rows),
        compiler_params=params,
        cost_estimate=pl.CostEstimate(flops=40_000_000, bytes_accessed=3_000_000, transcendentals=0),
        name="inner_rows",
    )(*frames, from_left, from_right, wide, own_meta)

    tall_rows = coarse_height + 2 * LEAD
    flow, coarse_flow, *_ = pl.pallas_call(
        outer_kernel,
        out_shape=(shape(2, height, width), shape(2, coarse_height, coarse_width), outer_terms, outer_terms, outer_terms),
        in_specs=[vmem] * 14,
        out_specs=(hbm, hbm, vmem, vmem, vmem),
        input_output_aliases={11: 2, 12: 3, 13: 4},
        scratch_shapes=[
            pltpu.VMEM((ROW_MESSAGE, LANES), jnp.float32),
            pltpu.VMEM((ROW_MESSAGE, LANES), jnp.float32),
            pltpu.VMEM((2, 3, bands, 40, LANES), jnp.float32),
            pltpu.VMEM((2 * bands, tall_rows, LANES), jnp.float32),
            pltpu.VMEM((2, 3, tall_rows, LANES), jnp.float32),
            pltpu.VMEM((2, 2 * EACH, LANES), jnp.float32),
            pltpu.VMEM((2, 2 * EACH, width), jnp.float32),
            pltpu.VMEM((2, coarse_height, coarse_width), jnp.float32),
            pltpu.SemaphoreType.DMA((4,)),
        ]
        + fine_scratch(bands, 2 * EACH)[:6],
        compiler_params=params,
        name="outer_rows",
    )(*frames, from_left, from_right, wide, got_0, got_1, middle, own_meta, *terms)
    return (flow, coarse_flow)


def solution(mesh):
    return jax.shard_map(
        local,
        mesh=mesh,
        in_specs=(P(None, "row", "col"), P(None, "row", "col"), P("row", "col", None)),
        out_specs=(P(None, "row", "col"), P(None, "row", "col")),
        check_vma=False,
    )
```

```python
import functools

import jax
import jax.numpy as jnp
from jax import lax
from jax.experimental import pallas as pl
from jax.experimental.pallas import tpu as pltpu
from jax.sharding import PartitionSpec as P

FACTOR = 8
MAXD = 4
STEPS = 3
LANES = 128
COLUMNS = 2 * LANES
HALF = 64
SUB = 8
DEPTH = 4
REACH = DEPTH + MAXD + 1
SLOT = 16
C_SECOND = 6
C_FIRST = 5
LEAD = 8
MARGIN = 48
GUARD = 8
BEGIN = 32
EACH = MARGIN + 16
LIMIT = 0.3
ALPHA = 0.3

S_MID = 55
S_RIGHT = 110
S_LEFT = LANES - REACH
S_TURN = COLUMNS - S_RIGHT - LANES
NEAR = 8

E8 = 0
E1 = 96
F4 = 112
CS = 160
CF = CS + 4 * C_SECOND
META = 208
ROW_MESSAGE = 216

COARSE_A = REACH + DEPTH
COARSE_B = SLOT + REACH + DEPTH
SHIFT_R = 2 * SLOT + REACH + DEPTH
SHIFT_C = SHIFT_R + 1
EXISTS = SHIFT_R + 2


def lanes_of(rows=SUB):
    return lax.broadcasted_iota(jnp.int32, (rows, LANES), 1)


def lanes_like(x):
    return lax.broadcasted_iota(jnp.int32, x.shape, 1)


def turn(x, amount):
    amount = amount % LANES
    return x if amount == 0 else pltpu.roll(x, amount, 1)


def turn_back(x, shift):
    return pltpu.roll(x, lax.rem(LANES - shift, LANES), 1)


def split_dot(x, exact):
    high = x.astype(jnp.bfloat16)
    rest = x - high.astype(jnp.float32)
    middle = rest.astype(jnp.bfloat16)
    low = (rest - middle.astype(jnp.float32)).astype(jnp.bfloat16)
    parts = [jnp.dot(part, exact, preferred_element_type=jnp.float32) for part in (low, middle, high)]
    return parts[0] + parts[1] + parts[2]


def scalar_at(ref, row, lane):
    return ref[row : row + 1, lane : lane + 1][0, 0]


def int_at(ref, row, lane):
    return scalar_at(ref, row, lane).astype(jnp.int32)


def is_even(axis, like):
    return jnp.broadcast_to(lax.axis_index(axis) % 2, like.shape) == 0


def aligned(row):
    return pl.ds(pl.multiple_of(row, SUB), SUB)


def pack_message(target, to_right, seconds, firsts, coarse, shift_rows, shift_cols):
    bands, height, _ = seconds[0].shape
    second, first = seconds[int(to_right)], firsts[int(to_right)]
    second_from = LANES - REACH if to_right else 0
    first_from = LANES - DEPTH if to_right else 0
    coarse_from = LEAD + COLUMNS // FACTOR - C_SECOND if to_right else LEAD
    lane = lanes_of()

    def pack(step, carry):
        packed = jnp.zeros((SUB, LANES), jnp.float32)
        for half in range(2):
            rows = aligned(step * SUB + half * (height // 2))
            cells = coarse[rows, :]
            base = half * HALF
            for band in range(bands):
                at = base + band * SLOT
                packed = jnp.where(lane >= at, turn(second[band, rows, :], at - second_from), packed)
                packed = jnp.where(lane >= at + REACH, turn(first[band, rows, :], at + REACH - first_from), packed)
                if band == 0:
                    packed = jnp.where(lane >= base + COARSE_A, turn(cells, base + COARSE_A - coarse_from), packed)
                if band == 1:
                    packed = jnp.where(lane >= base + COARSE_B, turn(cells, base + COARSE_B - coarse_from - 3), packed)
                if band == 2:
                    packed = jnp.where(lane >= base + SHIFT_R, shift_rows, packed)
                    packed = jnp.where(lane >= base + SHIFT_C, shift_cols, packed)
                    packed = jnp.where(lane >= base + EXISTS, 1.0, packed)
        target[aligned(step * SUB), :] = packed
        return carry

    lax.fori_loop(0, height // 2 // SUB, pack, 0, unroll=4)


def column_meta(message):
    return (int_at(message, 0, SHIFT_R), int_at(message, 0, SHIFT_C)), scalar_at(message, 0, EXISTS)


def strip_second(base, from_left, from_right, rows, half, band):
    at = half * HALF + band * SLOT
    lane = lanes_like(base)
    cells = jnp.where(lane >= S_RIGHT, turn(from_right[rows, :], S_RIGHT - at), base)
    return jnp.where(lane >= S_LEFT, turn(from_left[rows, :], S_LEFT - at), cells)


def strip_first(base, from_left, from_right, rows, half, band):
    at = half * HALF + band * SLOT + REACH
    lane = lanes_like(base)
    cells = jnp.where(lane >= S_RIGHT, turn(from_right[rows, :], S_RIGHT - at), base)
    return jnp.where(lane >= S_LEFT, turn(from_left[rows, :], LANES - DEPTH - at), cells)


def strip_own(planes):
    return jnp.where(lanes_like(planes[0]) < S_MID, planes[0], turn(planes[1], -S_TURN))


def first_kernel(
    second_hbm, first_hbm, shifts_hbm, second_0, second_1, first_0, first_1, coarse, swap, own_meta,
    sums, shifts, sems, shift_sem,
):
    seconds, firsts = (second_0, second_1), (first_0, first_1)
    bands, height, _ = second_0.shape
    width = COLUMNS
    coarse_height = height // FACTOR
    lane = lanes_of()
    get_shifts = pltpu.make_async_copy(shifts_hbm, shifts, shift_sem)
    get_shifts.start()
    copies = []
    for image, (source, refs) in enumerate(((second_hbm, seconds), (first_hbm, firsts))):
        for band in range(bands):
            for tile, ref in enumerate(refs):
                copy = pltpu.make_async_copy(
                    source.at[band, :, pl.ds(tile * LANES, LANES)], ref.at[band], sems.at[image, band, tile]
                )
                copy.start()
                copies.append((image * bands + band, tile, ref, band, copy))
    cell = lax.broadcasted_iota(jnp.int32, (width, LANES), 0)
    place = lax.broadcasted_iota(jnp.int32, (width, LANES), 1)
    weights = jnp.where(place - LEAD == cell // FACTOR, 1.0 / (FACTOR * FACTOR), 0.0).astype(jnp.bfloat16)
    for plane, tile, ref, band, copy in copies:
        copy.wait()
        total = ref[band, pl.ds(0, coarse_height, stride=FACTOR), :]
        for k in range(1, FACTOR):
            total = total + ref[band, pl.ds(k, coarse_height, stride=FACTOR), :]
        at = slice(tile * LANES, (tile + 1) * LANES)
        sums[plane * coarse_height : (plane + 1) * coarse_height, at] = total
    coarse[...] = split_dot(sums[...], weights)
    get_shifts.wait()
    shift_rows = shifts[0, 0, 0].astype(jnp.float32)
    shift_cols = shifts[0, 0, 1].astype(jnp.float32)
    own_meta[...] = jnp.where(lane < HALF, shift_rows, shift_cols)
    odd = lax.axis_index("col") % 2

    @pl.when(odd == 0)
    def _():
        pack_message(swap, True, seconds, firsts, coarse, shift_rows, shift_cols)

    @pl.when(odd == 1)
    def _():
        pack_message(swap, False, seconds, firsts, coarse, shift_rows, shift_cols)


def message_kernel(
    coarse, own_meta, got_0, got_1, up_part, down_part, _whole, swap_0, swap_1, from_left, from_right, wide, up, down
):
    even = is_even("col", got_0)
    from_right[...] = jnp.where(even, got_0[...], got_1[...])
    from_left[...] = jnp.where(even, got_1[...], got_0[...])
    planes_coarse, coarse_height, _ = wide.shape
    bands = planes_coarse // 2
    end = from_left.shape[0]
    coarse_width = COLUMNS // FACTOR
    lane = lanes_of()
    for plane in range(planes_coarse):
        half, block = divmod(plane, planes_coarse // 2)
        for step in range(coarse_height // SUB):
            own = slice(plane * coarse_height + step * SUB, plane * coarse_height + (step + 1) * SUB)
            rows = slice(block * coarse_height + step * SUB, block * coarse_height + (step + 1) * SUB)
            at = half * HALF
            left = from_left[rows, :]
            right = from_right[rows, :]
            start = LEAD - C_SECOND
            cells = turn(left, start - at - COARSE_A)
            cells = jnp.where(lane >= start + 3, turn(left, start + 3 - at - COARSE_B), cells)
            cells = jnp.where(lane >= LEAD, coarse[own, :], cells)
            start = LEAD + coarse_width
            cells = jnp.where(lane >= start, turn(right, start - at - COARSE_A), cells)
            cells = jnp.where(lane >= start + 3, turn(right, start + 3 - at - COARSE_B), cells)
            wide[plane, step * SUB : (step + 1) * SUB, :] = cells
    up[...] = up_part[...]
    down[...] = down_part[...]
    for band in range(bands):
        k = band * 3 + 2
        for target, half, near, next_rows, row_of in (
            (up, 0, slice(0, 8), slice(8, 16), 0),
            (down, 1, slice(end - 8, end), slice(end - 16, end - 8), 7),
        ):
            at = slice(E8 + 8 * k, E8 + 8 * k + 8)
            target[at, :] = strip_second(target[at, :], from_left, from_right, near, half, band)
            one = jnp.broadcast_to(target[E1 + k : E1 + k + 1, :], (SUB, LANES))
            one = strip_second(one, from_left, from_right, next_rows, half, band)
            target[E1 + k : E1 + k + 1, :] = one[row_of : row_of + 1]
            four = target[F4 + 4 * k : F4 + 4 * k + 4, :]
            four = strip_first(jnp.concatenate([four, four], axis=0), from_left, from_right, near, half, band)
            target[F4 + 4 * k : F4 + 4 * k + 4, :] = four[4 * half : 4 * half + 4]
        for at, plane, count in ((CS, band, C_SECOND), (CF, bands + band, C_FIRST)):
            up[at + count * band : at + count * band + count, :] = wide[plane, 0:count, :]
            down[at + count * band : at + count * band + count, :] = wide[
                plane, coarse_height - count : coarse_height, :
            ]
    packed = jnp.where(lane < 16, own_meta[...], jnp.where(lane < 32, turn(own_meta[...], HALF), 1.0))
    for message, at in ((from_left, 48), (from_right, 80)):
        meta = message[0:SUB, :]
        rows = jnp.broadcast_to(meta[:, SHIFT_R : SHIFT_R + 1], (SUB, LANES))
        cols = jnp.broadcast_to(meta[:, SHIFT_C : SHIFT_C + 1], (SUB, LANES))
        packed = jnp.where(lane >= at, rows, packed)
        packed = jnp.where(lane >= at + 16, cols, packed)
    up[META : META + SUB, :] = packed
    down[META : META + SUB, :] = packed
    even = is_even("row", up)
    swap_0[...] = jnp.where(even, down[...], up[...])
    swap_1[...] = jnp.where(even, up[...], down[...])


def coarse_flow_of(second, first, mask):
    def along_rows(x):
        size = x.shape[0]
        return pltpu.roll(x, size - 1, 0) - pltpu.roll(x, 1, 0)

    def along_cols(x):
        return pltpu.roll(x, LANES - 1, 1) - pltpu.roll(x, 1, 1)

    grad_rows = [0.125 * along_rows(x) for x in second]
    grad_cols = [0.125 * along_cols(x) for x in second]
    offset = [0.25 * (x - y) for x, y in zip(second, first)]
    data = [jnp.clip(x, -LIMIT, LIMIT) for x in offset]

    def pull(duals, grads):
        total = duals[0] * grads[0]
        for x, y in zip(duals[1:], grads[1:]):
            total = total + x * y
        return total

    flow = [-mask * pull(data, grad_rows), -mask * pull(data, grad_cols)]
    extrapolated = [2.0 * x for x in flow]
    dual_rows = [0.0, 0.0]
    dual_cols = [0.0, 0.0]
    for step in range(1, STEPS):
        for c in range(2):
            rows = dual_rows[c] + 0.125 * along_rows(extrapolated[c])
            cols = dual_cols[c] + 0.125 * along_cols(extrapolated[c])
            norm = jnp.maximum(rows * rows + cols * cols, 1e-30)
            scale = jnp.minimum(mask, ALPHA * lax.rsqrt(norm))
            dual_rows[c] = rows * scale
            dual_cols[c] = cols * scale
        data = [
            jnp.clip(q + o + g * extrapolated[0] + h * extrapolated[1], -LIMIT, LIMIT)
            for q, o, g, h in zip(data, offset, grad_rows, grad_cols)
        ]
        pulls = [pull(data, grad_rows), pull(data, grad_cols)]
        for c in range(2):
            divergence = along_rows(dual_rows[c]) + along_cols(dual_cols[c])
            following = flow[c] + mask * (0.125 * divergence - pulls[c])
            extrapolated[c] = 2.0 * following - flow[c]
            flow[c] = following
    return flow


def columns_of_planes(planes):
    whole = lax.broadcasted_iota(jnp.int32, (LANES, COLUMNS), 1)
    lane = lax.broadcasted_iota(jnp.int32, (LANES, LANES), 1)
    strip = jnp.where(lane < S_MID, lane, jnp.where(lane < S_LEFT, lane + (COLUMNS - S_RIGHT), lane - LANES))
    return jnp.concatenate([x for x, wanted in ((whole, "whole"), (strip, "strip")) if wanted in planes], axis=1)


def upsample(flow, planes, target):
    column = columns_of_planes(planes)
    source = lax.broadcasted_iota(jnp.int32, column.shape, 0)
    spread = jnp.where(source - LEAD == lax.shift_right_arithmetic(column, 3), float(FACTOR), 0.0).astype(jnp.bfloat16)
    rows = flow[0].shape[0]
    wide = split_dot(jnp.concatenate(flow, axis=0), spread)
    for c in range(2):
        for tile in range(column.shape[1] // LANES):
            target[c, tile] = wide[c * rows : (c + 1) * rows, tile * LANES : (tile + 1) * LANES]


def repeat_rows(spread, initial, cells):
    for k, cell in enumerate(cells):
        row = GUARD + k * SUB
        for c in range(2):
            for tile in range(initial.shape[1]):
                initial[c, tile, row : row + SUB, :] = jnp.broadcast_to(
                    spread[c, tile, cell : cell + 1, :], (SUB, LANES)
                )


def shift_whole(here, shift):
    turned = [turn_back(x, shift) for x in here]
    lane = lanes_like(here[0])
    return [
        jnp.where(lane + shift >= LANES, turned[1], turned[0]),
        jnp.where(lane + shift < 0, turned[0], turned[1]),
    ]


def columns_whole(fields):
    lane = lanes_like(fields[0])
    ahead = [pltpu.roll(x, LANES - 1, 1) for x in fields]
    behind = [pltpu.roll(x, 1, 1) for x in fields]
    return [
        jnp.where(lane == LANES - 1, ahead[1], ahead[0]) - behind[0],
        ahead[1] - jnp.where(lane == 0, behind[0], behind[1]),
    ]


def columns_strip(field):
    return pltpu.roll(field, LANES - 1, 1) - pltpu.roll(field, 1, 1)


def strip_windows(window, own_whole, centre, right, left):
    near = turn_back(window(centre[0]), centre[1])
    beyond_left = turn_back(window(left[0]), left[1])
    beyond_right = turn_back(window(right[0]), right[1])
    lane = lanes_like(near)
    is_left = lane >= S_LEFT
    beyond = jnp.where(is_left | (lane < S_MID), beyond_left, beyond_right)
    is_beyond = lane >= S_RIGHT
    is_near = (lane < NEAR) | (lane >= S_RIGHT - NEAR)
    values = []
    for outside, edge, own in (
        (beyond, near, own_whole[0]),
        (columns_strip(beyond), columns_strip(near), own_whole[1]),
    ):
        values.append(jnp.where(is_beyond, outside, jnp.where(is_near, edge, own)))
    return values


def fine_steps(
    rows_total, chunk, columns, initial, extrap, dual_rows, dual_cols, change, dual_data,
    offsets, grads_rows, grads_cols, masks_of, result,
):
    planes = len(offsets)
    bands = offsets[0].shape[0]
    chunks = rows_total // chunk
    both = [(c, tile) for c in range(2) for tile in range(planes)]

    for step in range(STEPS):
        source = initial if step == 0 else extrap
        final = step == STEPS - 1

        def dual(k, source=source, step=step):
            row = GUARD + k * chunk if isinstance(k, int) else pl.multiple_of(GUARD + k * chunk, SUB)
            own = pl.ds(k * chunk if isinstance(k, int) else pl.multiple_of(k * chunk, SUB), chunk)
            at = pl.ds(row, chunk)
            masks = masks_of(own)
            along = [columns([source[c, tile, at, :] for tile in range(planes)]) for c in range(2)]
            values = []
            for c, tile in both:
                rows = source[c, tile, pl.ds(row + 1, chunk), :] - source[c, tile, pl.ds(row - 1, chunk), :]
                cols = along[c][tile]
                if step > 0:
                    rows = rows + dual_rows[c, tile, at, :]
                    cols = cols + dual_cols[c, tile, own, :]
                norm = jnp.maximum(rows * rows + cols * cols, 1e-30)
                scale = jnp.minimum(masks[tile], (8.0 * ALPHA) * lax.rsqrt(norm))
                values.append((rows * scale, cols * scale))
            for (c, tile), (rows, cols) in zip(both, values):
                dual_rows[c, tile, at, :] = rows
                dual_cols[c, tile, own, :] = cols

        def primal(k, step=step, final=final):
            row = GUARD + k * chunk if isinstance(k, int) else pl.multiple_of(GUARD + k * chunk, SUB)
            own = pl.ds(k * chunk if isinstance(k, int) else pl.multiple_of(k * chunk, SUB), chunk)
            at = pl.ds(row, chunk)
            masks = masks_of(own)
            along = [columns([dual_cols[c, tile, own, :] for tile in range(planes)]) for c in range(2)]
            for tile in range(planes):
                start = [initial[c, tile, at, :] for c in range(2)]
                if step > 0:
                    moved = [extrap[c, tile, at, :] - start[c] for c in range(2)]
                pulls = [None, None]
                duals = []
                for band in range(bands):
                    gradient = (grads_rows[tile][band, own, :], grads_cols[tile][band, own, :])
                    value = offsets[tile][band, own, :]
                    if step > 0:
                        value = value + gradient[0] * moved[0] + gradient[1] * moved[1]
                        value = value + dual_data[band, tile, own, :]
                    value = jnp.clip(value, -LIMIT, LIMIT)
                    duals.append(value)
                    for c in range(2):
                        term = value * gradient[c]
                        pulls[c] = term if pulls[c] is None else pulls[c] + term
                movings = []
                for c in range(2):
                    divergence = (
                        dual_rows[c, tile, pl.ds(row + 1, chunk), :]
                        - dual_rows[c, tile, pl.ds(row - 1, chunk), :]
                        + along[c][tile]
                    )
                    movings.append((masks[tile] * (1.0 / 64.0)) * divergence - pulls[c])
                if step > 0:
                    olds = [change[c, tile, own, :] for c in range(2)]
                for c in range(2):
                    if step == 0:
                        change[c, tile, own, :] = movings[c]
                        extrap[c, tile, at, :] = start[c] + 2.0 * movings[c]
                    else:
                        new = olds[c] + movings[c]
                        if final:
                            result[c, tile, own, :] = start[c] + new
                        else:
                            change[c, tile, own, :] = new
                            extrap[c, tile, at, :] = start[c] + (new + movings[c])
                if not final:
                    for band in range(bands):
                        dual_data[band, tile, own, :] = duals[band]

        dual(0)

        def body(k, carry, dual=dual, primal=primal):
            dual(k)
            primal(k - 1)
            return carry

        lax.fori_loop(1, chunks, body, 0)
        primal(chunks - 1)


def clear_guards(*refs):
    for ref in refs:
        rows = ref.shape[2]
        zero = jnp.zeros((GUARD, LANES), jnp.float32)
        for c in range(2):
            for tile in range(ref.shape[1]):
                ref[c, tile, 0:GUARD, :] = zero
                ref[c, tile, rows - GUARD : rows, :] = zero


def fine_scratch(bands, planes, rows):
    guarded = pltpu.VMEM((2, planes, rows + 2 * GUARD, LANES), jnp.float32)
    plain = pltpu.VMEM((2, planes, rows, LANES), jnp.float32)
    return [guarded, guarded, guarded, plain, plain, pltpu.VMEM((bands, planes, rows, LANES), jnp.float32)]


def to_inner(row):
    return aligned(row - BEGIN)


def to_outer(row, half, height):
    return aligned(row + SUB if half == 0 else row - (height - 2 * EACH + SUB))


def group_loops(height, body):
    groups = height // SUB

    def step_of(step, carry, inner, outer):
        body(pl.multiple_of(step * SUB, SUB), 0, inner, outer)
        body(pl.multiple_of((groups - 1 - step) * SUB, SUB), 1, inner, outer)
        return carry

    first_inner = BEGIN // SUB
    end_outer = EACH // SUB - 1
    lax.fori_loop(1, first_inner, functools.partial(step_of, inner=False, outer=True), 0)
    lax.fori_loop(first_inner, end_outer, functools.partial(step_of, inner=True, outer=True), 0)
    lax.fori_loop(end_outer, groups // 2, functools.partial(step_of, inner=True, outer=False), 0)


def whole_terms_kernel(
    second_0, second_1, first_0, first_1, coarse, own_meta,
    swap, offset, grad_rows, grad_cols, outer_offset, outer_grad_rows, outer_grad_cols,
    strip_e, strip_f, strip_w, strip_c, up, down, moved,
):
    seconds, firsts = (second_0, second_1), (first_0, first_1)
    bands, height, _ = second_0.shape
    shift_rows, shift_cols = scalar_at(own_meta, 0, 0), scalar_at(own_meta, 0, HALF)
    centre = (shift_rows.astype(jnp.int32), shift_cols.astype(jnp.int32))
    odd = lax.axis_index("col") % 2

    @pl.when(odd == 1)
    def _():
        pack_message(swap, True, seconds, firsts, coarse, shift_rows, shift_cols)

    @pl.when(odd == 0)
    def _():
        pack_message(swap, False, seconds, firsts, coarse, shift_rows, shift_cols)

    def windows(band, row):
        here = [ref[band, pl.ds(row + centre[0], SUB), :] for ref in seconds]
        return shift_whole(here, centre[1])

    for row in (SUB // 2, height - SUB - SUB // 2):
        for band in range(bands):
            values = windows(band, row)
            for tile in range(2):
                moved[tile, band, row : row + SUB, :] = values[tile]
            strip_w[band, row : row + SUB, :] = strip_own(values)

    def values_of(row, half, inner, outer):
        results = []
        for band in range(bands):
            values = windows(band, row)
            along = columns_whole(values)
            own = [ref[band, pl.ds(row, SUB), :] for ref in firsts]
            raw = [ref[band, pl.ds(row, SUB), :] for ref in seconds]
            results.append((
                values,
                [0.25 * (x - y) for x, y in zip(values, own)],
                [0.125 * x for x in along],
                strip_own(values), strip_own(along), strip_own(own), strip_own(raw),
            ))
        rows = pl.ds(row, SUB)
        for band in range(bands):
            values, offsets, gradients, w, c, f, e = results[band]
            for tile in range(2):
                moved[tile, band, rows, :] = values[tile]
                if inner:
                    offset[tile, band, to_inner(row), :] = offsets[tile]
                    grad_cols[tile, band, to_inner(row), :] = gradients[tile]
                if outer:
                    at = to_outer(row, half, height)
                    outer_offset[tile, band, at, :] = offsets[tile]
                    outer_grad_cols[tile, band, at, :] = gradients[tile]
            strip_w[band, rows, :] = w
            strip_c[band, rows, :] = c
            strip_f[band, rows, :] = f
            strip_e[band, rows, :] = e

    group_loops(height, values_of)
    for row in (0, height - SUB):
        rows = slice(row, row + SUB)
        for band in range(bands):
            strip_f[band, rows, :] = strip_own([ref[band, rows, :] for ref in firsts])
            strip_e[band, rows, :] = strip_own([ref[band, rows, :] for ref in seconds])

    def row_gradients(row, half, inner, outer):
        for tile in range(2):
            for band in range(bands):
                value = 0.125 * (
                    moved[tile, band, pl.ds(row + 1, SUB), :] - moved[tile, band, pl.ds(row - 1, SUB), :]
                )
                if inner:
                    grad_rows[tile, band, to_inner(row), :] = value
                if outer:
                    outer_grad_rows[tile, band, to_outer(row, half, height), :] = value

    group_loops(height, row_gradients)

    up[...] = jnp.zeros_like(up)
    down[...] = jnp.zeros_like(down)
    for band in range(bands):
        for tile in range(3):
            second = (second_0, second_1, strip_e)[tile]
            first = (first_0, first_1, strip_f)[tile]
            k = band * 3 + tile
            up[E8 + 8 * k : E8 + 8 * k + 8, :] = second[band, 0:8, :]
            up[E1 + k : E1 + k + 1, :] = second[band, 8:9, :]
            up[F4 + 4 * k : F4 + 4 * k + 4, :] = first[band, 0:4, :]
            down[E8 + 8 * k : E8 + 8 * k + 8, :] = second[band, height - 8 : height, :]
            down[E1 + k : E1 + k + 1, :] = second[band, height - 9 : height - 8, :]
            down[F4 + 4 * k : F4 + 4 * k + 4, :] = first[band, height - 4 : height, :]


def whole_steps_kernel(
    coarse, offset, grad_rows, grad_cols, result, spread, initial, extrap, dual_rows, dual_cols, change, dual_data
):
    bands = offset.shape[1]
    coarse_height = coarse.shape[0] // (2 * bands)
    rows_total = result.shape[2]
    planes = [coarse[k * coarse_height : (k + 1) * coarse_height, :] for k in range(2 * bands)]
    flow = coarse_flow_of(planes[:bands], planes[bands:], 1.0)
    upsample(flow, ("whole",), spread)
    clear_guards(initial, extrap, dual_rows)
    repeat_rows(spread, initial, [BEGIN // FACTOR + k for k in range(rows_total // SUB)])
    fine_steps(
        rows_total, 32, columns_whole, initial, extrap, dual_rows, dual_cols, change, dual_data,
        *[[ref.at[tile] for tile in range(2)] for ref in (offset, grad_rows, grad_cols)],
        lambda own: (1.0, 1.0), result,
    )


def strip_kernel(
    strip_e, strip_f, strip_w, strip_c, from_left, from_right, wide, own_meta, whole,
    middle, strip_second_out, strip_first_out, outer_offset, outer_grad_rows, outer_grad_cols,
    moved, offset, grad_rows, grad_cols, result, spread, initial, extrap, dual_rows, dual_cols, change, dual_data,
):
    bands, height, _ = strip_e.shape
    coarse_height = height // FACTOR
    coarse_width = COLUMNS // FACTOR
    rows_total = height - 2 * BEGIN
    lane = lanes_of()
    centre = (int_at(own_meta, 0, 0), int_at(own_meta, 0, HALF))
    right, has_right = column_meta(from_right)
    left, has_left = column_meta(from_left)
    exists = jnp.where(lane < S_RIGHT, 1.0, jnp.where(lane < S_LEFT, has_right, has_left))
    factor = 0.125 * exists

    def fill(step, carry):
        rows = aligned(step * SUB)
        values = []
        for half in range(2):
            into = aligned(step * SUB + half * (height // 2))
            for band in range(bands):
                values.append((
                    band, into,
                    strip_second(strip_e[band, into, :], from_left, from_right, rows, half, band),
                    strip_first(strip_f[band, into, :], from_left, from_right, rows, half, band),
                ))
        for band, into, second, first in values:
            strip_second_out[band, into, :] = second
            strip_first_out[band, into, :] = first
        return carry

    lax.fori_loop(0, height // 2 // SUB, fill, 0)

    def windows(band, row, along):
        return strip_windows(
            lambda shift: strip_second_out[band, pl.ds(row + shift, SUB), :],
            (strip_w[band, pl.ds(row, SUB), :], along), centre, right, left,
        )

    for row in (SUB // 2, height - SUB - SUB // 2):
        for band in range(bands):
            moved[band, row : row + SUB, :] = windows(band, row, strip_w[band, pl.ds(row, SUB), :])[0]

    def values_of(row, half, inner, outer):
        rows = pl.ds(row, SUB)
        results = []
        for band in range(bands):
            value, along = windows(band, row, strip_c[band, rows, :])
            results.append((value, 0.25 * (value - strip_first_out[band, rows, :]), factor * along))
        for band in range(bands):
            value, shifted, gradient = results[band]
            moved[band, rows, :] = value
            if inner:
                offset[band, to_inner(row), :] = shifted
                grad_cols[band, to_inner(row), :] = gradient
            if outer:
                outer_offset[band, to_outer(row, half, height), :] = shifted
                outer_grad_cols[band, to_outer(row, half, height), :] = gradient

    group_loops(height, values_of)

    def row_gradients(row, half, inner, outer):
        for band in range(bands):
            value = factor * (moved[band, pl.ds(row + 1, SUB), :] - moved[band, pl.ds(row - 1, SUB), :])
            if inner:
                grad_rows[band, to_inner(row), :] = value
            if outer:
                outer_grad_rows[band, to_outer(row, half, height), :] = value

    group_loops(height, row_gradients)

    mask = jnp.where(lane < LEAD, has_left, jnp.where(lane < LEAD + coarse_width, 1.0, has_right))
    mask = jnp.concatenate([mask] * (coarse_height // SUB), axis=0)
    flow = coarse_flow_of(
        [wide[band] for band in range(bands)], [wide[bands + band] for band in range(bands)], mask
    )
    upsample(flow, ("strip",), spread)
    clear_guards(initial, extrap, dual_rows)
    repeat_rows(spread, initial, [BEGIN // FACTOR + k for k in range(rows_total // SUB)])

    chunk = 64
    masks = jnp.concatenate([exists] * (chunk // SUB), axis=0)
    fine_steps(
        rows_total, chunk, lambda fields: [columns_strip(fields[0])],
        initial, extrap, dual_rows, dual_cols, change, dual_data, [offset], [grad_rows], [grad_cols],
        lambda own: (masks,), result,
    )
    join(lambda c, tile, rows: whole[c, tile, rows, :], lambda c, rows: result[c, 0, rows, :], middle)


def join(whole, strip, target):
    lane = lanes_of()

    def step_of(step, carry):
        rows = aligned(step * SUB)
        for c in range(2):
            edge = strip(c, rows)
            target[c, rows, 0:LANES] = jnp.where(lane < MARGIN, edge, whole(c, 0, rows))
            target[c, rows, LANES:COLUMNS] = jnp.where(lane >= LANES - MARGIN, turn(edge, S_TURN), whole(c, 1, rows))
        return carry

    lax.fori_loop(0, target.shape[1] // SUB, step_of, 0, unroll=4)


def outer_kernel(
    second_0, second_1, first_0, first_1, strip_e, strip_f, from_left, from_right, wide, got_0, got_1, middle, own_meta,
    _wo, _wr, _wc, _so, _sr, _sc,
    flow_out, coarse_out, whole_offset, whole_rows, whole_cols, strip_offset, strip_rows, strip_cols,
    from_up, from_down, extended, tall, spread, masks, result, joined, coarse_result, sems,
    initial, extrap, dual_rows, dual_cols, change, dual_data,
):
    bands, height, _ = second_0.shape
    coarse_height = height // FACTOR
    coarse_width = COLUMNS // FACTOR
    rows_total = 2 * EACH
    lane = lanes_of()

    put_middle = pltpu.make_async_copy(
        middle.at[:, pl.ds(MARGIN - BEGIN, height - 2 * MARGIN), :],
        flow_out.at[:, pl.ds(MARGIN, height - 2 * MARGIN), :],
        sems.at[0],
    )
    put_middle.start()

    even = is_even("row", got_0)
    from_down[...] = jnp.where(even, got_0[...], got_1[...])
    from_up[...] = jnp.where(even, got_1[...], got_0[...])

    own = (int_at(own_meta, 0, 0), int_at(own_meta, 0, HALF))
    own_right, has_right = column_meta(from_right)
    own_left, has_left = column_meta(from_left)
    has_up = scalar_at(from_up, META, 32)
    has_down = scalar_at(from_down, META, 32)
    exists = jnp.where(lane < S_RIGHT, 1.0, jnp.where(lane < S_LEFT, has_right, has_left))

    def trio(message):
        return (
            (int_at(message, META, 0), int_at(message, META, 16)),
            (int_at(message, META, 80), int_at(message, META, 96)),
            (int_at(message, META, 48), int_at(message, META, 64)),
        )

    above = trio(from_up)
    below = trio(from_down)

    zero = jnp.zeros((SUB, LANES), jnp.float32)
    tall_rows = coarse_height + 2 * LEAD
    for band in range(bands):
        for plane, at, count in ((band, CS, C_SECOND), (bands + band, CF, C_FIRST)):
            start = at + count * band
            tall[plane, 0:LEAD, :] = zero
            tall[plane, LEAD - count : LEAD, :] = from_up[start : start + count, :]
            tall[plane, LEAD : LEAD + coarse_height, :] = wide[plane]
            tall[plane, LEAD + coarse_height : tall_rows, :] = zero
            tall[plane, LEAD + coarse_height : LEAD + coarse_height + count, :] = from_down[start : start + count, :]
    across = jnp.where(lane < LEAD, has_left, jnp.where(lane < LEAD + coarse_width, 1.0, has_right))
    mask = jnp.concatenate([across * has_up] + [across] * (coarse_height // SUB) + [across * has_down], axis=0)
    flow = coarse_flow_of(
        [tall[band] for band in range(bands)], [tall[bands + band] for band in range(bands)], mask
    )
    for c in range(2):
        coarse_result[c] = turn(flow[c][LEAD : LEAD + coarse_height], -LEAD)[:, :coarse_width]
    put_coarse = pltpu.make_async_copy(coarse_result, coarse_out, sems.at[1])
    put_coarse.start()
    upsample(flow, ("whole", "strip"), spread)
    clear_guards(initial, extrap, dual_rows)
    each = EACH // SUB
    repeat_rows(
        spread, initial,
        [LEAD - 1 + k for k in range(each)] + [tall_rows - LEAD + 1 - each + k for k in range(each)],
    )

    for end in range(2):
        message = (from_up, from_down)[end]
        for band in range(bands):
            for tile in range(3):
                k = band * 3 + tile
                eight = message[E8 + 8 * k : E8 + 8 * k + 8, :]
                one = message[E1 + k : E1 + k + 1, :]
                source = (second_0, second_1, strip_e)[tile]
                if end == 0:
                    extended[end, tile, band, 0:8, :] = zero
                    extended[end, tile, band, 7:8, :] = one
                    extended[end, tile, band, 8:16, :] = eight
                    extended[end, tile, band, 16:40, :] = source[band, 0:24, :]
                else:
                    extended[end, tile, band, 0:24, :] = source[band, height - 24 : height, :]
                    extended[end, tile, band, 24:32, :] = eight
                    extended[end, tile, band, 32:40, :] = zero
                    extended[end, tile, band, 32:33, :] = one
    quarter = jnp.zeros((DEPTH, LANES), jnp.float32)
    for end in range(2):
        message = (from_up, from_down)[end]
        edge_exists = (has_up, has_down)[end]
        halo_at, own_at = ((0, SUB), (rows_total - SUB, rows_total - 2 * SUB))[end]
        halo_base, own_base = ((SUB, 2 * SUB), (3 * SUB, 2 * SUB))[end]
        own_rows = slice(0, SUB) if end == 0 else slice(height - SUB, height)
        for at, base, shifts, halo in (
            (halo_at, halo_base, (above, below)[end], True),
            (own_at, own_base, (own, own_right, own_left), False),
        ):
            centre = shifts[0]
            factor = 0.125 * edge_exists if halo else 0.125
            rows = slice(at, at + SUB)
            for band in range(bands):

                def here(tile, shift, band=band, end=end, base=base):
                    return extended[end, tile, band, pl.ds(base + shift, SUB), :]

                def down_up(tile, shift, here=here):
                    return here(tile, shift + 1) - here(tile, shift - 1)

                firsts = []
                for tile in range(3):
                    k = band * 3 + tile
                    if halo:
                        four = message[F4 + 4 * k : F4 + 4 * k + 4, :]
                        firsts.append(jnp.concatenate([quarter, four] if end == 0 else [four, quarter], axis=0))
                    else:
                        firsts.append((first_0, first_1, strip_f)[tile][band, own_rows, :])
                values = shift_whole([here(tile, centre[0]) for tile in range(2)], centre[1])
                changes = shift_whole([down_up(tile, centre[0]) for tile in range(2)], centre[1])
                along = columns_whole(values)
                for tile in range(2):
                    whole_offset[tile, band, rows, :] = 0.25 * (values[tile] - firsts[tile])
                    whole_rows[tile, band, rows, :] = factor * changes[tile]
                    whole_cols[tile, band, rows, :] = factor * along[tile]
                value, across_cols = strip_windows(
                    lambda shift, here=here: here(2, shift), (strip_own(values), strip_own(along)), *shifts
                )
                change_rows, _ = strip_windows(
                    lambda shift, down_up=down_up: down_up(2, shift), (strip_own(changes), value), *shifts
                )
                strip_offset[band, rows, :] = 0.25 * (value - firsts[2])
                strip_rows[band, rows, :] = (factor * exists) * change_rows
                strip_cols[band, rows, :] = (factor * exists) * across_cols

    for i, value in enumerate((jnp.ones((SUB, LANES), jnp.float32), exists)):
        masks[i] = jnp.concatenate([value * has_up] + [value] * (rows_total // SUB - 2) + [value * has_down], axis=0)

    def masks_of(rows):
        whole = masks[0, rows, :]
        return (whole, whole, masks[1, rows, :])

    fine_steps(
        rows_total, 32, lambda fields: columns_whole(fields[:2]) + [columns_strip(fields[2])],
        initial, extrap, dual_rows, dual_cols, change, dual_data,
        [whole_offset.at[0], whole_offset.at[1], strip_offset],
        [whole_rows.at[0], whole_rows.at[1], strip_rows],
        [whole_cols.at[0], whole_cols.at[1], strip_cols],
        masks_of, result,
    )
    join(lambda c, tile, rows: result[c, tile, rows, :], lambda c, rows: result[c, 2, rows, :], joined)
    put_top = pltpu.make_async_copy(joined.at[:, pl.ds(SUB, MARGIN), :], flow_out.at[:, pl.ds(0, MARGIN), :], sems.at[2])
    put_bottom = pltpu.make_async_copy(
        joined.at[:, pl.ds(EACH + SUB, MARGIN), :], flow_out.at[:, pl.ds(height - MARGIN, MARGIN), :], sems.at[3]
    )
    put_top.start()
    put_bottom.start()
    put_middle.wait()
    put_coarse.wait()
    put_top.wait()
    put_bottom.wait()


def swap_with(message, axis, start):
    count = lax.axis_size(axis)
    pairs = [(i, i + 1) for i in range(start, count - 1, 2)]
    return lax.ppermute(message, axis, pairs + [(j, i) for i, j in pairs])


def local(frame_first, frame_second, shifts):
    bands, height, width = frame_first.shape
    assert bands == 4 and width == COLUMNS and height % LANES == 0
    coarse_height = height // FACTOR
    coarse_width = width // FACTOR
    vmem = pl.BlockSpec(memory_space=pltpu.VMEM)
    hbm = pl.BlockSpec(memory_space=pltpu.HBM)
    tall_rows = coarse_height + 2 * LEAD
    inner_rows = height - 2 * BEGIN

    def shape(*sizes):
        return jax.ShapeDtypeStruct(sizes, jnp.float32)

    def scratch(*sizes):
        return pltpu.VMEM(sizes, jnp.float32)

    def call(kernel, name, arguments, outs, scratches=(), flops=1_000_000, **more):
        more = {"in_specs": [vmem] * len(arguments), "out_specs": (vmem,) * len(outs), **more}
        return pl.pallas_call(
            kernel,
            out_shape=tuple(outs),
            scratch_shapes=list(scratches),
            compiler_params=pltpu.CompilerParams(vmem_limit_bytes=24 * 1024 * 1024),
            cost_estimate=pl.CostEstimate(flops=flops, bytes_accessed=1_000_000, transcendentals=0),
            name=name,
            **more,
        )(*arguments)

    plane = shape(bands, height, LANES)
    column_message = shape(height // 2, LANES)
    row_message = shape(ROW_MESSAGE, LANES)
    inner_whole = shape(2, bands, inner_rows, LANES)
    outer_whole = shape(2, bands, 2 * EACH, LANES)
    outer_strip = shape(bands, 2 * EACH, LANES)

    *frames, coarse, swap, own_meta = call(
        first_kernel,
        "means_and_message",
        [pltpu.with_memory_space_constraint(x, pltpu.HBM) for x in (frame_second, frame_first, shifts)],
        [*[plane] * 4, shape(2 * bands * coarse_height, LANES), column_message, shape(SUB, LANES)],
        [
            scratch(2 * bands * coarse_height, width),
            pltpu.SMEM((1, 1, 2), jnp.int32),
            pltpu.SemaphoreType.DMA((2, bands, 2)),
            pltpu.SemaphoreType.DMA,
        ],
        in_specs=[hbm] * 3,
    )
    got_0 = swap_with(swap, "col", 0)

    swap, *whole_terms, strip_e, strip_f, strip_w, strip_c, up_part, down_part = call(
        whole_terms_kernel,
        "whole_terms",
        [*frames, coarse, own_meta],
        [column_message, *[inner_whole] * 3, *[outer_whole] * 3, *[plane] * 4, row_message, row_message],
        [scratch(2, bands, height, LANES)],
        flops=8_000_000,
    )
    got_1 = swap_with(swap, "col", 1)

    (whole,) = call(
        whole_steps_kernel,
        "whole_steps",
        [coarse, *whole_terms[:3]],
        [shape(2, 2, inner_rows, LANES)],
        [scratch(2, 2, coarse_height, LANES), *fine_scratch(bands, 2, inner_rows)],
        flops=20_000_000,
    )

    swap_0, swap_1, from_left, from_right, wide = call(
        message_kernel,
        "row_messages",
        [coarse, own_meta, got_0, got_1, up_part, down_part, whole],
        [row_message, row_message, column_message, column_message, shape(2 * bands, coarse_height, LANES)],
        [scratch(ROW_MESSAGE, LANES)] * 2,
    )
    got_0 = swap_with(swap_0, "row", 0)
    got_1 = swap_with(swap_1, "row", 1)

    middle, strip_e, strip_f, *strip_terms = call(
        strip_kernel,
        "strip",
        [strip_e, strip_f, strip_w, strip_c, from_left, from_right, wide, own_meta, whole],
        [shape(2, inner_rows, width), plane, plane, *[outer_strip] * 3],
        [
            scratch(bands, height, LANES),
            *[scratch(bands, inner_rows, LANES)] * 3,
            scratch(2, 1, inner_rows, LANES),
            scratch(2, 1, coarse_height, LANES),
            *fine_scratch(bands, 1, inner_rows),
        ],
        flops=16_000_000,
    )

    flow, coarse_flow, *_ = call(
        outer_kernel,
        "outer_rows",
        [
            *frames, strip_e, strip_f, from_left, from_right, wide, got_0, got_1, middle, own_meta,
            *whole_terms[3:], *strip_terms,
        ],
        [shape(2, height, width), shape(2, coarse_height, coarse_width), *[outer_whole] * 3, *[outer_strip] * 3],
        [
            scratch(ROW_MESSAGE, LANES),
            scratch(ROW_MESSAGE, LANES),
            scratch(2, 3, bands, 40, LANES),
            scratch(2 * bands, tall_rows, LANES),
            scratch(2, 3, tall_rows, LANES),
            scratch(2, 2 * EACH, LANES),
            scratch(2, 3, 2 * EACH, LANES),
            scratch(2, 2 * EACH, width),
            scratch(2, coarse_height, coarse_width),
            pltpu.SemaphoreType.DMA((4,)),
            *fine_scratch(bands, 3, 2 * EACH),
        ],
        out_specs=(hbm, hbm) + (vmem,) * 6,
        input_output_aliases={13 + k: 2 + k for k in range(6)},
    )
    return (flow, coarse_flow)


def solution(mesh):
    return jax.shard_map(
        local,
        mesh=mesh,
        in_specs=(P(None, "row", "col"), P(None, "row", "col"), P("row", "col", None)),
        out_specs=(P(None, "row", "col"), P(None, "row", "col")),
        check_vma=False,
    )
```

```python
import functools

import jax
import jax.numpy as jnp
from jax import lax
from jax.experimental import pallas as pl
from jax.experimental.pallas import tpu as pltpu
from jax.sharding import PartitionSpec as P

FACTOR = 8
MAXD = 4
STEPS = 3
LANES = 128
COLUMNS = 2 * LANES
HALF = 64
SUB = 8
DEPTH = 4
REACH = DEPTH + MAXD + 1
SLOT = 16
C_SECOND = 6
C_FIRST = 5
LEAD = 8
MARGIN = 48
EDGE = 46
GUARD = 8
HALO = 8
BLOCK = 48
BEGIN = 32
EACH = MARGIN + 16
LIMIT = 0.3
ALPHA = 0.3

S_MID = 55
S_RIGHT = 110
S_LEFT = LANES - REACH
S_TURN = COLUMNS - S_RIGHT - LANES

E8 = 0
E1 = 96
F4 = 112
CS = 160
CF = CS + 4 * C_SECOND
META = 208
ROW_MESSAGE = 216

COARSE_A = REACH + DEPTH
COARSE_B = SLOT + REACH + DEPTH
SHIFT_R = 2 * SLOT + REACH + DEPTH
SHIFT_C = SHIFT_R + 1
EXISTS = SHIFT_R + 2


def lanes_of(rows=SUB):
    return lax.broadcasted_iota(jnp.int32, (rows, LANES), 1)


def lanes_like(x):
    return lax.broadcasted_iota(jnp.int32, x.shape, 1)


def turn(x, amount):
    amount = amount % LANES
    return x if amount == 0 else pltpu.roll(x, amount, 1)


def turn_back(x, shift):
    return pltpu.roll(x, lax.rem(LANES - shift, LANES), 1)


def split_dot(x, exact):
    high = x.astype(jnp.bfloat16)
    rest = x - high.astype(jnp.float32)
    middle = rest.astype(jnp.bfloat16)
    low = (rest - middle.astype(jnp.float32)).astype(jnp.bfloat16)
    parts = [jnp.dot(part, exact, preferred_element_type=jnp.float32) for part in (low, middle, high)]
    return parts[0] + parts[1] + parts[2]


def scalar_at(ref, row, lane):
    return ref[row : row + 1, lane : lane + 1][0, 0]


def int_at(ref, row, lane):
    return scalar_at(ref, row, lane).astype(jnp.int32)


def is_even(axis, like):
    return jnp.broadcast_to(lax.axis_index(axis) % 2, like.shape) == 0


def without_wrap(message, axis, count):
    place = jnp.broadcast_to(lax.axis_index(axis), message.shape)
    return jnp.where((place > 0) & (place < count - 1), message[...], 0.0)


def aligned(row):
    return pl.ds(pl.multiple_of(row, SUB), SUB)


def pack_message(target, to_right, seconds, firsts, coarse, shift_rows, shift_cols):
    bands, height, _ = seconds[0].shape
    second, first = seconds[int(to_right)], firsts[int(to_right)]
    second_from = LANES - REACH if to_right else 0
    first_from = LANES - DEPTH if to_right else 0
    coarse_from = LEAD + COLUMNS // FACTOR - C_SECOND if to_right else LEAD
    lane = lanes_of()

    def pack(step, carry):
        packed = jnp.zeros((SUB, LANES), jnp.float32)
        for half in range(2):
            rows = aligned(step * SUB + half * (height // 2))
            cells = coarse[rows, :]
            base = half * HALF
            for band in range(bands):
                at = base + band * SLOT
                packed = jnp.where(lane >= at, turn(second[band, rows, :], at - second_from), packed)
                packed = jnp.where(lane >= at + REACH, turn(first[band, rows, :], at + REACH - first_from), packed)
                if band == 0:
                    packed = jnp.where(lane >= base + COARSE_A, turn(cells, base + COARSE_A - coarse_from), packed)
                if band == 1:
                    packed = jnp.where(lane >= base + COARSE_B, turn(cells, base + COARSE_B - coarse_from - 3), packed)
                if band == 2:
                    packed = jnp.where(lane >= base + SHIFT_R, shift_rows, packed)
                    packed = jnp.where(lane >= base + SHIFT_C, shift_cols, packed)
                    packed = jnp.where(lane >= base + EXISTS, 1.0, packed)
        target[aligned(step * SUB), :] = packed
        return carry

    lax.fori_loop(0, height // 2 // SUB, pack, 0, unroll=4)


def column_meta(message):
    return (int_at(message, 0, SHIFT_R), int_at(message, 0, SHIFT_C)), scalar_at(message, 0, EXISTS)


def strip_second(base, from_left, from_right, rows, half, band):
    at = half * HALF + band * SLOT
    lane = lanes_like(base)
    cells = jnp.where(lane >= S_RIGHT, turn(from_right[rows, :], S_RIGHT - at), base)
    return jnp.where(lane >= S_LEFT, turn(from_left[rows, :], S_LEFT - at), cells)


def strip_first(base, from_left, from_right, rows, half, band):
    at = half * HALF + band * SLOT + REACH
    lane = lanes_like(base)
    cells = jnp.where(lane >= S_RIGHT, turn(from_right[rows, :], S_RIGHT - at), base)
    return jnp.where(lane >= S_LEFT, turn(from_left[rows, :], LANES - DEPTH - at), cells)


def strip_own(planes):
    return jnp.where(lanes_like(planes[0]) < S_MID, planes[0], turn(planes[1], -S_TURN))


def first_kernel(
    second_hbm, first_hbm, shifts_hbm, second_0, second_1, first_0, first_1, coarse, swap, own_meta,
    sums, shifts, sems, shift_sem,
):
    seconds, firsts = (second_0, second_1), (first_0, first_1)
    bands, height, _ = second_0.shape
    width = COLUMNS
    coarse_height = height // FACTOR
    lane = lanes_of()
    get_shifts = pltpu.make_async_copy(shifts_hbm, shifts, shift_sem)
    get_shifts.start()
    copies = []
    for image, (source, refs) in enumerate(((second_hbm, seconds), (first_hbm, firsts))):
        for band in range(bands):
            for tile, ref in enumerate(refs):
                copy = pltpu.make_async_copy(
                    source.at[band, :, pl.ds(tile * LANES, LANES)], ref.at[band], sems.at[image, band, tile]
                )
                copy.start()
                copies.append((image * bands + band, tile, ref, band, copy))
    cell = lax.broadcasted_iota(jnp.int32, (width, LANES), 0)
    place = lax.broadcasted_iota(jnp.int32, (width, LANES), 1)
    weights = jnp.where(place - LEAD == cell // FACTOR, 1.0 / (FACTOR * FACTOR), 0.0).astype(jnp.bfloat16)
    for plane, tile, ref, band, copy in copies:
        copy.wait()
        total = ref[band, pl.ds(0, coarse_height, stride=FACTOR), :]
        for k in range(1, FACTOR):
            total = total + ref[band, pl.ds(k, coarse_height, stride=FACTOR), :]
        at = slice(tile * LANES, (tile + 1) * LANES)
        sums[plane * coarse_height : (plane + 1) * coarse_height, at] = total
    coarse[...] = split_dot(sums[...], weights)
    get_shifts.wait()
    shift_rows = shifts[0, 0, 0].astype(jnp.float32)
    shift_cols = shifts[0, 0, 1].astype(jnp.float32)
    own_meta[...] = jnp.where(lane < HALF, shift_rows, shift_cols)
    odd = lax.axis_index("col") % 2

    @pl.when(odd == 0)
    def _():
        pack_message(swap, True, seconds, firsts, coarse, shift_rows, shift_cols)

    @pl.when(odd == 1)
    def _():
        pack_message(swap, False, seconds, firsts, coarse, shift_rows, shift_cols)


def message_kernel(
    count, coarse, own_meta, got_0, got_1, up_part, down_part, _whole, swap_0, swap_1, from_left, from_right, wide, up, down
):
    other = without_wrap(got_1, "col", count)
    even = is_even("col", got_0)
    from_right[...] = jnp.where(even, got_0[...], other)
    from_left[...] = jnp.where(even, other, got_0[...])
    planes_coarse, coarse_height, _ = wide.shape
    bands = planes_coarse // 2
    end = from_left.shape[0]
    coarse_width = COLUMNS // FACTOR
    lane = lanes_of()
    for plane in range(planes_coarse):
        half, block = divmod(plane, planes_coarse // 2)
        for step in range(coarse_height // SUB):
            own = slice(plane * coarse_height + step * SUB, plane * coarse_height + (step + 1) * SUB)
            rows = slice(block * coarse_height + step * SUB, block * coarse_height + (step + 1) * SUB)
            at = half * HALF
            left = from_left[rows, :]
            right = from_right[rows, :]
            start = LEAD - C_SECOND
            cells = turn(left, start - at - COARSE_A)
            cells = jnp.where(lane >= start + 3, turn(left, start + 3 - at - COARSE_B), cells)
            cells = jnp.where(lane >= LEAD, coarse[own, :], cells)
            start = LEAD + coarse_width
            cells = jnp.where(lane >= start, turn(right, start - at - COARSE_A), cells)
            cells = jnp.where(lane >= start + 3, turn(right, start + 3 - at - COARSE_B), cells)
            wide[plane, step * SUB : (step + 1) * SUB, :] = cells
    up[...] = up_part[...]
    down[...] = down_part[...]
    for band in range(bands):
        k = band * 3 + 2
        for target, half, near, next_rows, row_of in (
            (up, 0, slice(0, 8), slice(8, 16), 0),
            (down, 1, slice(end - 8, end), slice(end - 16, end - 8), 7),
        ):
            at = slice(E8 + 8 * k, E8 + 8 * k + 8)
            target[at, :] = strip_second(target[at, :], from_left, from_right, near, half, band)
            one = jnp.broadcast_to(target[E1 + k : E1 + k + 1, :], (SUB, LANES))
            one = strip_second(one, from_left, from_right, next_rows, half, band)
            target[E1 + k : E1 + k + 1, :] = one[row_of : row_of + 1]
            four = target[F4 + 4 * k : F4 + 4 * k + 4, :]
            four = strip_first(jnp.concatenate([four, four], axis=0), from_left, from_right, near, half, band)
            target[F4 + 4 * k : F4 + 4 * k + 4, :] = four[4 * half : 4 * half + 4]
        for at, plane, count in ((CS, band, C_SECOND), (CF, bands + band, C_FIRST)):
            up[at + count * band : at + count * band + count, :] = wide[plane, 0:count, :]
            down[at + count * band : at + count * band + count, :] = wide[
                plane, coarse_height - count : coarse_height, :
            ]
    packed = jnp.where(lane < 16, own_meta[...], jnp.where(lane < 32, turn(own_meta[...], HALF), 1.0))
    for message, at in ((from_left, 48), (from_right, 80)):
        meta = message[0:SUB, :]
        rows = jnp.broadcast_to(meta[:, SHIFT_R : SHIFT_R + 1], (SUB, LANES))
        cols = jnp.broadcast_to(meta[:, SHIFT_C : SHIFT_C + 1], (SUB, LANES))
        packed = jnp.where(lane >= at, rows, packed)
        packed = jnp.where(lane >= at + 16, cols, packed)
    up[META : META + SUB, :] = packed
    down[META : META + SUB, :] = packed
    even = is_even("row", up)
    swap_0[...] = jnp.where(even, down[...], up[...])
    swap_1[...] = jnp.where(even, up[...], down[...])


def coarse_flow_of(second, first, mask):
    def along_rows(x):
        size = x.shape[0]
        return pltpu.roll(x, size - 1, 0) - pltpu.roll(x, 1, 0)

    def along_cols(x):
        return pltpu.roll(x, LANES - 1, 1) - pltpu.roll(x, 1, 1)

    grad_rows = [0.125 * along_rows(x) for x in second]
    grad_cols = [0.125 * along_cols(x) for x in second]
    offset = [0.25 * (x - y) for x, y in zip(second, first)]
    data = [jnp.clip(x, -LIMIT, LIMIT) for x in offset]

    def pull(duals, grads):
        total = duals[0] * grads[0]
        for x, y in zip(duals[1:], grads[1:]):
            total = total + x * y
        return total

    flow = [-mask * pull(data, grad_rows), -mask * pull(data, grad_cols)]
    extrapolated = [2.0 * x for x in flow]
    dual_rows = [0.0, 0.0]
    dual_cols = [0.0, 0.0]
    for step in range(1, STEPS):
        for c in range(2):
            rows = dual_rows[c] + 0.125 * along_rows(extrapolated[c])
            cols = dual_cols[c] + 0.125 * along_cols(extrapolated[c])
            norm = jnp.maximum(rows * rows + cols * cols, 1e-30)
            scale = jnp.minimum(mask, ALPHA * lax.rsqrt(norm))
            dual_rows[c] = rows * scale
            dual_cols[c] = cols * scale
        data = [
            jnp.clip(q + o + g * extrapolated[0] + h * extrapolated[1], -LIMIT, LIMIT)
            for q, o, g, h in zip(data, offset, grad_rows, grad_cols)
        ]
        pulls = [pull(data, grad_rows), pull(data, grad_cols)]
        for c in range(2):
            divergence = along_rows(dual_rows[c]) + along_cols(dual_cols[c])
            following = flow[c] + mask * (0.125 * divergence - pulls[c])
            extrapolated[c] = 2.0 * following - flow[c]
            flow[c] = following
    return flow


def columns_of_planes(planes):
    whole = lax.broadcasted_iota(jnp.int32, (LANES, COLUMNS), 1)
    lane = lax.broadcasted_iota(jnp.int32, (LANES, LANES), 1)
    strip = jnp.where(lane < S_MID, lane, jnp.where(lane < S_LEFT, lane + (COLUMNS - S_RIGHT), lane - LANES))
    return jnp.concatenate([x for x, wanted in ((whole, "whole"), (strip, "strip")) if wanted in planes], axis=1)


def upsample(flow, planes, target):
    column = columns_of_planes(planes)
    source = lax.broadcasted_iota(jnp.int32, column.shape, 0)
    spread = jnp.where(source - LEAD == lax.shift_right_arithmetic(column, 3), float(FACTOR), 0.0).astype(jnp.bfloat16)
    rows = flow[0].shape[0]
    wide = split_dot(jnp.concatenate(flow, axis=0), spread)
    for c in range(2):
        for tile in range(column.shape[1] // LANES):
            target[c, tile] = wide[c * rows : (c + 1) * rows, tile * LANES : (tile + 1) * LANES]


def repeat_rows(spread, initial, cells):
    for k, cell in enumerate(cells):
        row = GUARD + k * SUB
        for c in range(2):
            for tile in range(initial.shape[1]):
                initial[c, tile, row : row + SUB, :] = jnp.broadcast_to(
                    spread[c, tile, cell : cell + 1, :], (SUB, LANES)
                )


def shift_whole(here, shift):
    turned = [turn_back(x, shift) for x in here]
    lane = lanes_like(here[0])
    return [
        jnp.where(lane + shift >= LANES, turned[1], turned[0]),
        jnp.where(lane + shift < 0, turned[0], turned[1]),
    ]


def edge_lanes(rows):
    lane = lanes_of(rows)
    return lane == LANES - 1, lane == 0


def columns_whole(fields, edges):
    last, first = edges
    ahead = [pltpu.roll(x, LANES - 1, 1) for x in fields]
    behind = [pltpu.roll(x, 1, 1) for x in fields]
    return [
        jnp.where(last, ahead[1], ahead[0]) - behind[0],
        ahead[1] - jnp.where(first, behind[0], behind[1]),
    ]


def columns_strip(field):
    return pltpu.roll(field, LANES - 1, 1) - pltpu.roll(field, 1, 1)


def strip_windows(window, centre, right, left):
    own = turn_back(window(centre[0]), centre[1])
    beyond_left = turn_back(window(left[0]), left[1])
    beyond_right = turn_back(window(right[0]), right[1])
    lane = lanes_like(own)
    beyond = jnp.where((lane >= S_LEFT) | (lane < S_MID), beyond_left, beyond_right)
    is_beyond = lane >= S_RIGHT
    return jnp.where(is_beyond, beyond, own), jnp.where(is_beyond, columns_strip(beyond), columns_strip(own))


def fine_steps(
    rows_total, chunk, columns, initial, extrap, dual_rows, dual_cols, change, dual_data,
    offsets, grads_rows, grads_cols, data_row, masks_of, result,
):
    planes = len(offsets)
    bands = offsets[0].shape[0]
    chunks = rows_total // chunk
    both = [(c, tile) for c in range(2) for tile in range(planes)]

    for step in range(STEPS):
        source = initial if step == 0 else extrap
        final = step == STEPS - 1

        def dual(k, source=source, step=step):
            row = GUARD + k * chunk if isinstance(k, int) else pl.multiple_of(GUARD + k * chunk, SUB)
            own = pl.ds(k * chunk if isinstance(k, int) else pl.multiple_of(k * chunk, SUB), chunk)
            at = pl.ds(row, chunk)
            masks = masks_of(own)
            along = [columns([source[c, tile, at, :] for tile in range(planes)]) for c in range(2)]
            values = []
            for c, tile in both:
                rows = source[c, tile, pl.ds(row + 1, chunk), :] - source[c, tile, pl.ds(row - 1, chunk), :]
                cols = along[c][tile]
                if step > 0:
                    rows = rows + dual_rows[c, tile, at, :]
                    cols = cols + dual_cols[c, tile, own, :]
                norm = jnp.maximum(rows * rows + cols * cols, 1e-30)
                scale = jnp.minimum(masks[tile], (8.0 * ALPHA) * lax.rsqrt(norm))
                values.append((rows * scale, cols * scale))
            for (c, tile), (rows, cols) in zip(both, values):
                dual_rows[c, tile, at, :] = rows
                dual_cols[c, tile, own, :] = cols

        def primal(k, step=step, final=final):
            data = pl.ds(data_row(k), chunk)
            row = GUARD + k * chunk if isinstance(k, int) else pl.multiple_of(GUARD + k * chunk, SUB)
            own = pl.ds(k * chunk if isinstance(k, int) else pl.multiple_of(k * chunk, SUB), chunk)
            at = pl.ds(row, chunk)
            masks = masks_of(own)
            along = [columns([dual_cols[c, tile, own, :] for tile in range(planes)]) for c in range(2)]
            for tile in range(planes):
                start = [initial[c, tile, at, :] for c in range(2)]
                if step > 0:
                    moved = [extrap[c, tile, at, :] - start[c] for c in range(2)]
                pulls = [None, None]
                duals = []
                for band in range(bands):
                    gradient = (grads_rows[tile][band, data, :], grads_cols[tile][band, data, :])
                    value = offsets[tile][band, data, :]
                    if step > 0:
                        value = value + gradient[0] * moved[0] + gradient[1] * moved[1]
                        value = value + dual_data[band, tile, own, :]
                    value = jnp.clip(value, -LIMIT, LIMIT)
                    duals.append(value)
                    for c in range(2):
                        term = value * gradient[c]
                        pulls[c] = term if pulls[c] is None else pulls[c] + term
                movings = []
                for c in range(2):
                    divergence = (
                        dual_rows[c, tile, pl.ds(row + 1, chunk), :]
                        - dual_rows[c, tile, pl.ds(row - 1, chunk), :]
                        + along[c][tile]
                    )
                    movings.append((masks[tile] * (1.0 / 64.0)) * divergence - pulls[c])
                if step > 0:
                    olds = [change[c, tile, own, :] for c in range(2)]
                for c in range(2):
                    if step == 0:
                        change[c, tile, own, :] = movings[c]
                        extrap[c, tile, at, :] = start[c] + 2.0 * movings[c]
                    else:
                        new = olds[c] + movings[c]
                        if final:
                            result[c, tile, own, :] = start[c] + new
                        else:
                            change[c, tile, own, :] = new
                            extrap[c, tile, at, :] = start[c] + (new + movings[c])
                if not final:
                    for band in range(bands):
                        dual_data[band, tile, own, :] = duals[band]

        dual(0)

        def body(k, carry, dual=dual, primal=primal):
            dual(k)
            primal(k - 1)
            return carry

        lax.fori_loop(1, chunks, body, 0)
        primal(chunks - 1)


def clear_guards(*refs):
    for ref in refs:
        rows = ref.shape[2]
        zero = jnp.zeros((GUARD, LANES), jnp.float32)
        for c in range(2):
            for tile in range(ref.shape[1]):
                ref[c, tile, 0:GUARD, :] = zero
                ref[c, tile, rows - GUARD : rows, :] = zero


def fine_scratch(bands, planes, rows):
    guarded = pltpu.VMEM((2, planes, rows + 2 * GUARD, LANES), jnp.float32)
    plain = pltpu.VMEM((2, planes, rows, LANES), jnp.float32)
    return [guarded, guarded, guarded, plain, plain, pltpu.VMEM((bands, planes, rows, LANES), jnp.float32)]


def blocks(height, body):
    def step_of(step, carry):
        body(pl.multiple_of(SUB + step * BLOCK, SUB))
        return carry

    lax.fori_loop(0, (height - 2 * SUB) // BLOCK, step_of, 0)


def whole_terms_kernel(
    second_0, second_1, first_0, first_1, coarse, own_meta,
    swap, offset, grad_rows, grad_cols, strip_e, strip_f, up, down, moved,
):
    seconds, firsts = (second_0, second_1), (first_0, first_1)
    bands, height, _ = second_0.shape
    shift_rows, shift_cols = scalar_at(own_meta, 0, 0), scalar_at(own_meta, 0, HALF)
    centre = (shift_rows.astype(jnp.int32), shift_cols.astype(jnp.int32))
    odd = lax.axis_index("col") % 2

    @pl.when(odd == 1)
    def _():
        pack_message(swap, True, seconds, firsts, coarse, shift_rows, shift_cols)

    @pl.when(odd == 0)
    def _():
        pack_message(swap, False, seconds, firsts, coarse, shift_rows, shift_cols)

    def windows(band, row, rows):
        here = [ref[band, pl.ds(row + centre[0], rows), :] for ref in seconds]
        return shift_whole(here, centre[1])

    ends = (SUB // 2, height - SUB - SUB // 2)
    values = [(row, band, windows(band, row, SUB)) for row in ends for band in range(bands)]
    for row, band, value in values:
        for tile in range(2):
            moved[tile, band, row : row + SUB, :] = value[tile]

    edges = edge_lanes(BLOCK)

    def values_of(row):
        results = []
        rows = pl.ds(row, BLOCK)
        data = pl.ds(pl.multiple_of(row + HALO, SUB), BLOCK)
        for band in range(bands):
            values = windows(band, row, BLOCK)
            along = columns_whole(values, edges)
            own = [ref[band, rows, :] for ref in firsts]
            results.append((values, [0.25 * (x - y) for x, y in zip(values, own)], [0.125 * x for x in along]))
        for band in range(bands):
            for tile in range(2):
                moved[tile, band, rows, :] = results[band][0][tile]
                offset[tile, band, data, :] = results[band][1][tile]
                grad_cols[tile, band, data, :] = results[band][2][tile]

    blocks(height, values_of)

    def row_gradients(row):
        data = pl.ds(pl.multiple_of(row + HALO, SUB), BLOCK)
        for tile in range(2):
            for band in range(bands):
                grad_rows[tile, band, data, :] = 0.125 * (
                    moved[tile, band, pl.ds(row + 1, BLOCK), :] - moved[tile, band, pl.ds(row - 1, BLOCK), :]
                )

    blocks(height, row_gradients)

    def strips(step, carry):
        rows = pl.ds(pl.multiple_of(step * HALF, SUB), HALF)
        for band in range(bands):
            strip_e[band, rows, :] = strip_own([ref[band, rows, :] for ref in seconds])
            strip_f[band, rows, :] = strip_own([ref[band, rows, :] for ref in firsts])
        return carry

    lax.fori_loop(0, height // HALF, strips, 0)

    up[...] = jnp.zeros_like(up)
    down[...] = jnp.zeros_like(down)
    for band in range(bands):
        for tile in range(3):
            second = (second_0, second_1, strip_e)[tile]
            first = (first_0, first_1, strip_f)[tile]
            k = band * 3 + tile
            up[E8 + 8 * k : E8 + 8 * k + 8, :] = second[band, 0:8, :]
            up[E1 + k : E1 + k + 1, :] = second[band, 8:9, :]
            up[F4 + 4 * k : F4 + 4 * k + 4, :] = first[band, 0:4, :]
            down[E8 + 8 * k : E8 + 8 * k + 8, :] = second[band, height - 8 : height, :]
            down[E1 + k : E1 + k + 1, :] = second[band, height - 9 : height - 8, :]
            down[F4 + 4 * k : F4 + 4 * k + 4, :] = first[band, height - 4 : height, :]


def whole_steps_kernel(
    coarse, offset, grad_rows, grad_cols, result, spread, initial, extrap, dual_rows, dual_cols, change, dual_data
):
    bands = offset.shape[1]
    coarse_height = coarse.shape[0] // (2 * bands)
    rows_total = result.shape[2]
    planes = [coarse[k * coarse_height : (k + 1) * coarse_height, :] for k in range(2 * bands)]
    flow = coarse_flow_of(planes[:bands], planes[bands:], 1.0)
    upsample(flow, ("whole",), spread)
    clear_guards(initial, extrap, dual_rows)
    repeat_rows(spread, initial, [BEGIN // FACTOR + k for k in range(rows_total // SUB)])
    edges = edge_lanes(32)
    fine_steps(
        rows_total, 32, lambda fields: columns_whole(fields, edges),
        initial, extrap, dual_rows, dual_cols, change, dual_data,
        *[[ref.at[tile] for tile in range(2)] for ref in (offset, grad_rows, grad_cols)],
        lambda k: pl.multiple_of(HALO + BEGIN + k * 32, SUB), lambda own: (1.0, 1.0), result,
    )


def strip_kernel(
    strip_e, strip_f, from_left, from_right, wide, own_meta, whole,
    middle, strip_second_out, strip_first_out, offset, grad_rows, grad_cols,
    moved, result, spread, initial, extrap, dual_rows, dual_cols, change, dual_data,
):
    bands, height, _ = strip_e.shape
    coarse_height = height // FACTOR
    coarse_width = COLUMNS // FACTOR
    rows_total = height - 2 * BEGIN
    lane = lanes_of()
    centre = (int_at(own_meta, 0, 0), int_at(own_meta, 0, HALF))
    right, has_right = column_meta(from_right)
    left, has_left = column_meta(from_left)
    exists = jnp.where(lane < S_RIGHT, 1.0, jnp.where(lane < S_LEFT, has_right, has_left))
    factor = 0.125 * jnp.concatenate([exists] * (BLOCK // SUB), axis=0)

    def fill(step, carry):
        values = []
        rows = pl.ds(pl.multiple_of(step * 32, SUB), 32)
        for half in range(2):
            into = pl.ds(pl.multiple_of(step * 32 + half * (height // 2), SUB), 32)
            for band in range(bands):
                values.append((
                    band, into,
                    strip_second(strip_e[band, into, :], from_left, from_right, rows, half, band),
                    strip_first(strip_f[band, into, :], from_left, from_right, rows, half, band),
                ))
        for band, into, second, first in values:
            strip_second_out[band, into, :] = second
            strip_first_out[band, into, :] = first
        return carry

    lax.fori_loop(0, height // 2 // 32, fill, 0)

    def windows(band, row, rows):
        return strip_windows(
            lambda shift: strip_second_out[band, pl.ds(row + shift, rows), :], centre, right, left
        )

    ends = (SUB // 2, height - SUB - SUB // 2)
    values = [(row, band, windows(band, row, SUB)[0]) for row in ends for band in range(bands)]
    for row, band, value in values:
        moved[band, row : row + SUB, :] = value

    def values_of(row):
        rows = pl.ds(row, BLOCK)
        data = pl.ds(pl.multiple_of(row + HALO, SUB), BLOCK)
        results = []
        for band in range(bands):
            value, along = windows(band, row, BLOCK)
            results.append((value, 0.25 * (value - strip_first_out[band, rows, :]), factor * along))
        for band in range(bands):
            moved[band, rows, :], offset[band, data, :], grad_cols[band, data, :] = results[band]

    blocks(height, values_of)

    def row_gradients(row):
        data = pl.ds(pl.multiple_of(row + HALO, SUB), BLOCK)
        for band in range(bands):
            grad_rows[band, data, :] = factor * (
                moved[band, pl.ds(row + 1, BLOCK), :] - moved[band, pl.ds(row - 1, BLOCK), :]
            )

    blocks(height, row_gradients)

    mask = jnp.where(lane < LEAD, has_left, jnp.where(lane < LEAD + coarse_width, 1.0, has_right))
    mask = jnp.concatenate([mask] * (coarse_height // SUB), axis=0)
    flow = coarse_flow_of(
        [wide[band] for band in range(bands)], [wide[bands + band] for band in range(bands)], mask
    )
    upsample(flow, ("strip",), spread)
    clear_guards(initial, extrap, dual_rows)
    repeat_rows(spread, initial, [BEGIN // FACTOR + k for k in range(rows_total // SUB)])

    chunk = 64
    masks = jnp.concatenate([exists] * (chunk // SUB), axis=0)
    fine_steps(
        rows_total, chunk, lambda fields: [columns_strip(fields[0])],
        initial, extrap, dual_rows, dual_cols, change, dual_data, [offset], [grad_rows], [grad_cols],
        lambda k: pl.multiple_of(HALO + BEGIN + k * chunk, SUB), lambda own: (masks,), result,
    )
    join(lambda c, tile, rows: whole[c, tile, rows, :], lambda c, rows: result[c, 0, rows, :], middle)


def join(whole, strip, target):
    lane = lanes_of()

    def step_of(step, carry):
        rows = aligned(step * SUB)
        for c in range(2):
            edge = strip(c, rows)
            target[c, rows, 0:LANES] = jnp.where(lane < EDGE, edge, whole(c, 0, rows))
            target[c, rows, LANES:COLUMNS] = jnp.where(lane >= LANES - EDGE, turn(edge, S_TURN), whole(c, 1, rows))
        return carry

    lax.fori_loop(0, target.shape[1] // SUB, step_of, 0, unroll=4)


def outer_kernel(
    count, second_0, second_1, first_0, first_1, strip_e, strip_f, from_left, from_right, wide, got_0, got_1, middle, own_meta,
    _wo, _wr, _wc, _so, _sr, _sc,
    flow_out, coarse_out, whole_offset, whole_rows, whole_cols, strip_offset, strip_rows, strip_cols,
    from_up, from_down, extended, tall, spread, masks, result, joined, coarse_result, sems,
    initial, extrap, dual_rows, dual_cols, change, dual_data,
):
    bands, height, _ = second_0.shape
    coarse_height = height // FACTOR
    coarse_width = COLUMNS // FACTOR
    rows_total = 2 * EACH
    lane = lanes_of()

    put_middle = pltpu.make_async_copy(
        middle.at[:, pl.ds(MARGIN - BEGIN, height - 2 * MARGIN), :],
        flow_out.at[:, pl.ds(MARGIN, height - 2 * MARGIN), :],
        sems.at[0],
    )
    put_middle.start()

    other = without_wrap(got_1, "row", count)
    even = is_even("row", got_0)
    from_down[...] = jnp.where(even, got_0[...], other)
    from_up[...] = jnp.where(even, other, got_0[...])

    own = (int_at(own_meta, 0, 0), int_at(own_meta, 0, HALF))
    own_right, has_right = column_meta(from_right)
    own_left, has_left = column_meta(from_left)
    has_up = scalar_at(from_up, META, 32)
    has_down = scalar_at(from_down, META, 32)
    exists = jnp.where(lane < S_RIGHT, 1.0, jnp.where(lane < S_LEFT, has_right, has_left))

    def trio(message):
        return (
            (int_at(message, META, 0), int_at(message, META, 16)),
            (int_at(message, META, 80), int_at(message, META, 96)),
            (int_at(message, META, 48), int_at(message, META, 64)),
        )

    above = trio(from_up)
    below = trio(from_down)

    zero = jnp.zeros((SUB, LANES), jnp.float32)
    tall_rows = coarse_height + 2 * LEAD
    for band in range(bands):
        for plane, at, count in ((band, CS, C_SECOND), (bands + band, CF, C_FIRST)):
            start = at + count * band
            tall[plane, 0:LEAD, :] = zero
            tall[plane, LEAD - count : LEAD, :] = from_up[start : start + count, :]
            tall[plane, LEAD : LEAD + coarse_height, :] = wide[plane]
            tall[plane, LEAD + coarse_height : tall_rows, :] = zero
            tall[plane, LEAD + coarse_height : LEAD + coarse_height + count, :] = from_down[start : start + count, :]
    across = jnp.where(lane < LEAD, has_left, jnp.where(lane < LEAD + coarse_width, 1.0, has_right))
    mask = jnp.concatenate([across * has_up] + [across] * (coarse_height // SUB) + [across * has_down], axis=0)
    flow = coarse_flow_of(
        [tall[band] for band in range(bands)], [tall[bands + band] for band in range(bands)], mask
    )
    for c in range(2):
        coarse_result[c] = turn(flow[c][LEAD : LEAD + coarse_height], -LEAD)[:, :coarse_width]
    put_coarse = pltpu.make_async_copy(coarse_result, coarse_out, sems.at[1])
    put_coarse.start()
    upsample(flow, ("whole", "strip"), spread)
    clear_guards(initial, extrap, dual_rows)
    each = EACH // SUB
    repeat_rows(
        spread, initial,
        [LEAD - 1 + k for k in range(each)] + [tall_rows - LEAD + 1 - each + k for k in range(each)],
    )

    for end in range(2):
        message = (from_up, from_down)[end]
        for band in range(bands):
            for tile in range(3):
                k = band * 3 + tile
                eight = message[E8 + 8 * k : E8 + 8 * k + 8, :]
                one = message[E1 + k : E1 + k + 1, :]
                source = (second_0, second_1, strip_e)[tile]
                if end == 0:
                    extended[end, tile, band, 0:8, :] = zero
                    extended[end, tile, band, 7:8, :] = one
                    extended[end, tile, band, 8:16, :] = eight
                    extended[end, tile, band, 16:40, :] = source[band, 0:24, :]
                else:
                    extended[end, tile, band, 0:24, :] = source[band, height - 24 : height, :]
                    extended[end, tile, band, 24:32, :] = eight
                    extended[end, tile, band, 32:40, :] = zero
                    extended[end, tile, band, 32:33, :] = one
    quarter = jnp.zeros((DEPTH, LANES), jnp.float32)
    edges = edge_lanes(SUB)
    rows_data = whole_offset.shape[2]
    for halo in (True, False):
        results = []
        for end, band in [(end, band) for end in range(2) for band in range(bands)]:
            message = (from_up, from_down)[end]
            own_rows = slice(0, SUB) if end == 0 else slice(height - SUB, height)
            if halo:
                rows = slice(0, SUB) if end == 0 else slice(rows_data - SUB, rows_data)
                base = (SUB, 3 * SUB)[end]
                shifts = (above, below)[end]
                factor = 0.125 * (has_up, has_down)[end]
            else:
                rows = slice(HALO, HALO + SUB) if end == 0 else slice(rows_data - HALO - SUB, rows_data - HALO)
                base = 2 * SUB
                shifts = (own, own_right, own_left)
                factor = 0.125

            def here(tile, shift, band=band, end=end, base=base):
                return extended[end, tile, band, pl.ds(base + shift, SUB), :]

            def down_up(tile, shift, here=here):
                return here(tile, shift + 1) - here(tile, shift - 1)

            firsts = []
            for tile in range(3):
                k = band * 3 + tile
                if halo:
                    four = message[F4 + 4 * k : F4 + 4 * k + 4, :]
                    firsts.append(jnp.concatenate([quarter, four] if end == 0 else [four, quarter], axis=0))
                else:
                    firsts.append((first_0, first_1, strip_f)[tile][band, own_rows, :])
            centre = shifts[0]
            values = shift_whole([here(tile, centre[0]) for tile in range(2)], centre[1])
            changes = shift_whole([down_up(tile, centre[0]) for tile in range(2)], centre[1])
            along = columns_whole(values, edges)
            value, across_cols = strip_windows(lambda shift, here=here: here(2, shift), *shifts)
            change_rows, _ = strip_windows(lambda shift, down_up=down_up: down_up(2, shift), *shifts)
            results.append((
                band, rows,
                [0.25 * (x - y) for x, y in zip([*values, value], firsts)],
                [*[factor * x for x in changes], (factor * exists) * change_rows],
                [*[factor * x for x in along], (factor * exists) * across_cols],
            ))
        for band, rows, offsets, by_rows, by_cols in results:
            for tile in range(2):
                whole_offset[tile, band, rows, :] = offsets[tile]
                whole_rows[tile, band, rows, :] = by_rows[tile]
                whole_cols[tile, band, rows, :] = by_cols[tile]
            strip_offset[band, rows, :] = offsets[2]
            strip_rows[band, rows, :] = by_rows[2]
            strip_cols[band, rows, :] = by_cols[2]

    for i, value in enumerate((jnp.ones((SUB, LANES), jnp.float32), exists)):
        masks[i] = jnp.concatenate([value * has_up] + [value] * (rows_total // SUB - 2) + [value * has_down], axis=0)

    def masks_of(rows):
        whole = masks[0, rows, :]
        return (whole, whole, masks[1, rows, :])

    edges = edge_lanes(32)

    def data_row(k):
        return pl.multiple_of(k * 32 + jnp.where(k >= EACH // 32, rows_data - rows_total, 0), SUB)

    fine_steps(
        rows_total, 32, lambda fields: columns_whole(fields[:2], edges) + [columns_strip(fields[2])],
        initial, extrap, dual_rows, dual_cols, change, dual_data,
        [whole_offset.at[0], whole_offset.at[1], strip_offset],
        [whole_rows.at[0], whole_rows.at[1], strip_rows],
        [whole_cols.at[0], whole_cols.at[1], strip_cols],
        data_row, masks_of, result,
    )
    join(lambda c, tile, rows: result[c, tile, rows, :], lambda c, rows: result[c, 2, rows, :], joined)
    put_top = pltpu.make_async_copy(joined.at[:, pl.ds(SUB, MARGIN), :], flow_out.at[:, pl.ds(0, MARGIN), :], sems.at[2])
    put_bottom = pltpu.make_async_copy(
        joined.at[:, pl.ds(EACH + SUB, MARGIN), :], flow_out.at[:, pl.ds(height - MARGIN, MARGIN), :], sems.at[3]
    )
    put_top.start()
    put_bottom.start()
    put_middle.wait()
    put_coarse.wait()
    put_top.wait()
    put_bottom.wait()


def swap_with(message, axis, start):
    count = lax.axis_size(axis)
    pairs = [(i, (i + 1) % count) for i in range(start, count, 2)]
    return lax.ppermute(message, axis, pairs + [(j, i) for i, j in pairs])


def local(frame_first, frame_second, shifts):
    bands, height, width = frame_first.shape
    assert bands == 4 and width == COLUMNS and height % LANES == 0 and (height - 2 * SUB) % BLOCK == 0
    assert lax.axis_size("row") % 2 == 0 and lax.axis_size("col") % 2 == 0
    coarse_height = height // FACTOR
    coarse_width = width // FACTOR
    vmem = pl.BlockSpec(memory_space=pltpu.VMEM)
    hbm = pl.BlockSpec(memory_space=pltpu.HBM)
    tall_rows = coarse_height + 2 * LEAD
    inner_rows = height - 2 * BEGIN

    def shape(*sizes):
        return jax.ShapeDtypeStruct(sizes, jnp.float32)

    def scratch(*sizes):
        return pltpu.VMEM(sizes, jnp.float32)

    def call(kernel, name, arguments, outs, scratches=(), flops=1_000_000, **more):
        more = {"in_specs": [vmem] * len(arguments), "out_specs": (vmem,) * len(outs), **more}
        return pl.pallas_call(
            kernel,
            out_shape=tuple(outs),
            scratch_shapes=list(scratches),
            compiler_params=pltpu.CompilerParams(vmem_limit_bytes=24 * 1024 * 1024),
            cost_estimate=pl.CostEstimate(flops=flops, bytes_accessed=1_000_000, transcendentals=0),
            name=name,
            **more,
        )(*arguments)

    plane = shape(bands, height, LANES)
    column_message = shape(height // 2, LANES)
    row_message = shape(ROW_MESSAGE, LANES)
    whole_data = shape(2, bands, height + 2 * HALO, LANES)
    strip_data = shape(bands, height + 2 * HALO, LANES)

    *frames, coarse, swap, own_meta = call(
        first_kernel,
        "means_and_message",
        [pltpu.with_memory_space_constraint(x, pltpu.HBM) for x in (frame_second, frame_first, shifts)],
        [*[plane] * 4, shape(2 * bands * coarse_height, LANES), column_message, shape(SUB, LANES)],
        [
            scratch(2 * bands * coarse_height, width),
            pltpu.SMEM((1, 1, 2), jnp.int32),
            pltpu.SemaphoreType.DMA((2, bands, 2)),
            pltpu.SemaphoreType.DMA,
        ],
        in_specs=[hbm] * 3,
    )
    got_0 = swap_with(swap, "col", 0)

    swap, *whole_terms, strip_e, strip_f, up_part, down_part = call(
        whole_terms_kernel,
        "whole_terms",
        [*frames, coarse, own_meta],
        [column_message, *[whole_data] * 3, plane, plane, row_message, row_message],
        [scratch(2, bands, height, LANES)],
        flops=8_000_000,
    )
    got_1 = swap_with(swap, "col", 1)

    (whole,) = call(
        whole_steps_kernel,
        "whole_steps",
        [coarse, *whole_terms],
        [shape(2, 2, inner_rows, LANES)],
        [scratch(2, 2, coarse_height, LANES), *fine_scratch(bands, 2, inner_rows)],
        flops=20_000_000,
    )

    swap_0, swap_1, from_left, from_right, wide = call(
        functools.partial(message_kernel, lax.axis_size("col")),
        "row_messages",
        [coarse, own_meta, got_0, got_1, up_part, down_part, whole],
        [row_message, row_message, column_message, column_message, shape(2 * bands, coarse_height, LANES)],
        [scratch(ROW_MESSAGE, LANES)] * 2,
    )
    got_0 = swap_with(swap_0, "row", 0)
    got_1 = swap_with(swap_1, "row", 1)

    middle, strip_e, strip_f, *strip_terms = call(
        strip_kernel,
        "strip",
        [strip_e, strip_f, from_left, from_right, wide, own_meta, whole],
        [shape(2, inner_rows, width), plane, plane, *[strip_data] * 3],
        [
            scratch(bands, height, LANES),
            scratch(2, 1, inner_rows, LANES),
            scratch(2, 1, coarse_height, LANES),
            *fine_scratch(bands, 1, inner_rows),
        ],
        flops=16_000_000,
    )

    flow, coarse_flow, *_ = call(
        functools.partial(outer_kernel, lax.axis_size("row")),
        "outer_rows",
        [
            *frames, strip_e, strip_f, from_left, from_right, wide, got_0, got_1, middle, own_meta,
            *whole_terms, *strip_terms,
        ],
        [shape(2, height, width), shape(2, coarse_height, coarse_width), *[whole_data] * 3, *[strip_data] * 3],
        [
            scratch(ROW_MESSAGE, LANES),
            scratch(ROW_MESSAGE, LANES),
            scratch(2, 3, bands, 40, LANES),
            scratch(2 * bands, tall_rows, LANES),
            scratch(2, 3, tall_rows, LANES),
            scratch(2, 2 * EACH, LANES),
            scratch(2, 3, 2 * EACH, LANES),
            scratch(2, 2 * EACH, width),
            scratch(2, coarse_height, coarse_width),
            pltpu.SemaphoreType.DMA((4,)),
            *fine_scratch(bands, 3, 2 * EACH),
        ],
        out_specs=(hbm, hbm) + (vmem,) * 6,
        input_output_aliases={13 + k: 2 + k for k in range(6)},
    )
    return (flow, coarse_flow)


def solution(mesh):
    return jax.shard_map(
        local,
        mesh=mesh,
        in_specs=(P(None, "row", "col"), P(None, "row", "col"), P("row", "col", None)),
        out_specs=(P(None, "row", "col"), P(None, "row", "col")),
        check_vma=False,
    )
```

```python
import functools

import jax
import jax.numpy as jnp
from jax import lax
from jax.experimental import pallas as pl
from jax.experimental.pallas import tpu as pltpu
from jax.sharding import PartitionSpec as P

FACTOR = 8
MAXD = 4
STEPS = 3
LANES = 128
COLUMNS = 2 * LANES
HALF = 64
SUB = 8
DEPTH = 4
REACH = DEPTH + MAXD + 1
SLOT = 16
C_SECOND = 6
C_FIRST = 5
LEAD = 8
MARGIN = 48
EDGE = 46
GUARD = 8
HALO = 8
BEGIN = 32
EACH = MARGIN + 16
LIMIT = 0.3
ALPHA = 0.3

S_MID = 55
S_RIGHT = 110
S_LEFT = LANES - REACH
S_TURN = COLUMNS - S_RIGHT - LANES

E8 = 0
E1 = 96
F4 = 112
CS = 160
CF = CS + 4 * C_SECOND
META = 208
ROW_MESSAGE = 216

COARSE_A = REACH + DEPTH
COARSE_B = SLOT + REACH + DEPTH
SHIFT_R = 2 * SLOT + REACH + DEPTH
SHIFT_C = SHIFT_R + 1
EXISTS = SHIFT_R + 2


def lanes_of(rows=SUB):
    return lax.broadcasted_iota(jnp.int32, (rows, LANES), 1)


def lanes_like(x):
    return lax.broadcasted_iota(jnp.int32, x.shape, 1)


def turn(x, amount):
    amount = amount % LANES
    return x if amount == 0 else pltpu.roll(x, amount, 1)


def turn_back(x, shift):
    return pltpu.roll(x, lax.rem(LANES - shift, LANES), 1)


def split_dot(x, exact):
    high = x.astype(jnp.bfloat16)
    rest = x - high.astype(jnp.float32)
    middle = rest.astype(jnp.bfloat16)
    low = (rest - middle.astype(jnp.float32)).astype(jnp.bfloat16)
    parts = [jnp.dot(part, exact, preferred_element_type=jnp.float32) for part in (low, middle, high)]
    return parts[0] + parts[1] + parts[2]


def scalar_at(ref, row, lane):
    return ref[row : row + 1, lane : lane + 1][0, 0]


def int_at(ref, row, lane):
    return scalar_at(ref, row, lane).astype(jnp.int32)


def is_even(axis, like):
    return jnp.broadcast_to(lax.axis_index(axis) % 2, like.shape) == 0


def without_ends(message, axis, count):
    place = jnp.broadcast_to(lax.axis_index(axis), message.shape)
    return jnp.where((place > 0) & (place < count - 1), message[...], 0.0)


def aligned(row):
    return pl.ds(pl.multiple_of(row, SUB), SUB)


def pack_message(target, to_right, seconds, firsts, coarse, shift_rows, shift_cols):
    bands, height, _ = seconds[0].shape
    second, first = seconds[int(to_right)], firsts[int(to_right)]
    second_from = LANES - REACH if to_right else 0
    first_from = LANES - DEPTH if to_right else 0
    coarse_from = LEAD + COLUMNS // FACTOR - C_SECOND if to_right else LEAD
    lane = lanes_of()

    def pack(step, carry):
        packed = jnp.zeros((SUB, LANES), jnp.float32)
        for half in range(2):
            rows = aligned(step * SUB + half * (height // 2))
            cells = coarse[rows, :]
            base = half * HALF
            for band in range(bands):
                at = base + band * SLOT
                packed = jnp.where(lane >= at, turn(second[band, rows, :], at - second_from), packed)
                packed = jnp.where(lane >= at + REACH, turn(first[band, rows, :], at + REACH - first_from), packed)
                if band == 0:
                    packed = jnp.where(lane >= base + COARSE_A, turn(cells, base + COARSE_A - coarse_from), packed)
                if band == 1:
                    packed = jnp.where(lane >= base + COARSE_B, turn(cells, base + COARSE_B - coarse_from - 3), packed)
                if band == 2:
                    packed = jnp.where(lane >= base + SHIFT_R, shift_rows, packed)
                    packed = jnp.where(lane >= base + SHIFT_C, shift_cols, packed)
                    packed = jnp.where(lane >= base + EXISTS, 1.0, packed)
        target[aligned(step * SUB), :] = packed
        return carry

    lax.fori_loop(0, height // 2 // SUB, pack, 0, unroll=4)


def column_meta(message):
    return (int_at(message, 0, SHIFT_R), int_at(message, 0, SHIFT_C)), scalar_at(message, 0, EXISTS)


def strip_second(base, from_left, from_right, rows, half, band):
    at = half * HALF + band * SLOT
    lane = lanes_like(base)
    cells = jnp.where(lane >= S_RIGHT, turn(from_right[rows, :], S_RIGHT - at), base)
    return jnp.where(lane >= S_LEFT, turn(from_left[rows, :], S_LEFT - at), cells)


def strip_first(base, from_left, from_right, rows, half, band):
    at = half * HALF + band * SLOT + REACH
    lane = lanes_like(base)
    cells = jnp.where(lane >= S_RIGHT, turn(from_right[rows, :], S_RIGHT - at), base)
    return jnp.where(lane >= S_LEFT, turn(from_left[rows, :], LANES - DEPTH - at), cells)


def strip_own(planes):
    return jnp.where(lanes_like(planes[0]) < S_MID, planes[0], turn(planes[1], -S_TURN))


def first_kernel(
    second_hbm, first_hbm, shifts_hbm, second_0, second_1, first_0, first_1, coarse, swap, own_meta,
    sums, shifts, sems, shift_sem,
):
    seconds, firsts = (second_0, second_1), (first_0, first_1)
    bands, height, _ = second_0.shape
    width = COLUMNS
    coarse_height = height // FACTOR
    lane = lanes_of()
    get_shifts = pltpu.make_async_copy(shifts_hbm, shifts, shift_sem)
    get_shifts.start()
    copies = []
    for image, (source, refs) in enumerate(((second_hbm, seconds), (first_hbm, firsts))):
        for band in range(bands):
            for tile, ref in enumerate(refs):
                copy = pltpu.make_async_copy(
                    source.at[band, :, pl.ds(tile * LANES, LANES)], ref.at[band], sems.at[image, band, tile]
                )
                copy.start()
                copies.append((image * bands + band, tile, ref, band, copy))
    cell = lax.broadcasted_iota(jnp.int32, (width, LANES), 0)
    place = lax.broadcasted_iota(jnp.int32, (width, LANES), 1)
    weights = jnp.where(place - LEAD == cell // FACTOR, 1.0 / (FACTOR * FACTOR), 0.0).astype(jnp.bfloat16)
    for plane, tile, ref, band, copy in copies:
        copy.wait()
        total = ref[band, pl.ds(0, coarse_height, stride=FACTOR), :]
        for k in range(1, FACTOR):
            total = total + ref[band, pl.ds(k, coarse_height, stride=FACTOR), :]
        at = slice(tile * LANES, (tile + 1) * LANES)
        sums[plane * coarse_height : (plane + 1) * coarse_height, at] = total
    coarse[...] = split_dot(sums[...], weights)
    get_shifts.wait()
    shift_rows = shifts[0, 0, 0].astype(jnp.float32)
    shift_cols = shifts[0, 0, 1].astype(jnp.float32)
    own_meta[...] = jnp.where(lane < HALF, shift_rows, shift_cols)
    odd = lax.axis_index("col") % 2

    @pl.when(odd == 0)
    def _():
        pack_message(swap, True, seconds, firsts, coarse, shift_rows, shift_cols)

    @pl.when(odd == 1)
    def _():
        pack_message(swap, False, seconds, firsts, coarse, shift_rows, shift_cols)


def message_kernel(
    count, coarse, own_meta, got_0, got_1, up_part, down_part, _whole, swap_0, swap_1, from_left, from_right, wide, up, down
):
    other = without_ends(got_1, "col", count)
    even = is_even("col", got_0)
    from_right[...] = jnp.where(even, got_0[...], other)
    from_left[...] = jnp.where(even, other, got_0[...])
    planes_coarse, coarse_height, _ = wide.shape
    bands = planes_coarse // 2
    end = from_left.shape[0]
    coarse_width = COLUMNS // FACTOR
    lane = lanes_of()
    for plane in range(planes_coarse):
        half, block = divmod(plane, planes_coarse // 2)
        for step in range(coarse_height // SUB):
            own = slice(plane * coarse_height + step * SUB, plane * coarse_height + (step + 1) * SUB)
            rows = slice(block * coarse_height + step * SUB, block * coarse_height + (step + 1) * SUB)
            at = half * HALF
            left = from_left[rows, :]
            right = from_right[rows, :]
            start = LEAD - C_SECOND
            cells = turn(left, start - at - COARSE_A)
            cells = jnp.where(lane >= start + 3, turn(left, start + 3 - at - COARSE_B), cells)
            cells = jnp.where(lane >= LEAD, coarse[own, :], cells)
            start = LEAD + coarse_width
            cells = jnp.where(lane >= start, turn(right, start - at - COARSE_A), cells)
            cells = jnp.where(lane >= start + 3, turn(right, start + 3 - at - COARSE_B), cells)
            wide[plane, step * SUB : (step + 1) * SUB, :] = cells
    up[...] = up_part[...]
    down[...] = down_part[...]
    for band in range(bands):
        k = band * 3 + 2
        for target, half, near, next_rows, row_of in (
            (up, 0, slice(0, 8), slice(8, 16), 0),
            (down, 1, slice(end - 8, end), slice(end - 16, end - 8), 7),
        ):
            at = slice(E8 + 8 * k, E8 + 8 * k + 8)
            target[at, :] = strip_second(target[at, :], from_left, from_right, near, half, band)
            one = jnp.broadcast_to(target[E1 + k : E1 + k + 1, :], (SUB, LANES))
            one = strip_second(one, from_left, from_right, next_rows, half, band)
            target[E1 + k : E1 + k + 1, :] = one[row_of : row_of + 1]
            four = target[F4 + 4 * k : F4 + 4 * k + 4, :]
            four = strip_first(jnp.concatenate([four, four], axis=0), from_left, from_right, near, half, band)
            target[F4 + 4 * k : F4 + 4 * k + 4, :] = four[4 * half : 4 * half + 4]
        for at, plane, count in ((CS, band, C_SECOND), (CF, bands + band, C_FIRST)):
            up[at + count * band : at + count * band + count, :] = wide[plane, 0:count, :]
            down[at + count * band : at + count * band + count, :] = wide[
                plane, coarse_height - count : coarse_height, :
            ]
    packed = jnp.where(lane < 16, own_meta[...], jnp.where(lane < 32, turn(own_meta[...], HALF), 1.0))
    for message, at in ((from_left, 48), (from_right, 80)):
        meta = message[0:SUB, :]
        rows = jnp.broadcast_to(meta[:, SHIFT_R : SHIFT_R + 1], (SUB, LANES))
        cols = jnp.broadcast_to(meta[:, SHIFT_C : SHIFT_C + 1], (SUB, LANES))
        packed = jnp.where(lane >= at, rows, packed)
        packed = jnp.where(lane >= at + 16, cols, packed)
    up[META : META + SUB, :] = packed
    down[META : META + SUB, :] = packed
    even = is_even("row", up)
    swap_0[...] = jnp.where(even, down[...], up[...])
    swap_1[...] = jnp.where(even, up[...], down[...])


def coarse_flow_of(second, first, mask):
    def along_rows(x):
        size = x.shape[0]
        return pltpu.roll(x, size - 1, 0) - pltpu.roll(x, 1, 0)

    def along_cols(x):
        return pltpu.roll(x, LANES - 1, 1) - pltpu.roll(x, 1, 1)

    grad_rows = [0.125 * along_rows(x) for x in second]
    grad_cols = [0.125 * along_cols(x) for x in second]
    offset = [0.25 * (x - y) for x, y in zip(second, first)]
    data = [jnp.clip(x, -LIMIT, LIMIT) for x in offset]

    def pull(duals, grads):
        total = duals[0] * grads[0]
        for x, y in zip(duals[1:], grads[1:]):
            total = total + x * y
        return total

    flow = [-mask * pull(data, grad_rows), -mask * pull(data, grad_cols)]
    extrapolated = [2.0 * x for x in flow]
    dual_rows = [0.0, 0.0]
    dual_cols = [0.0, 0.0]
    for step in range(1, STEPS):
        for c in range(2):
            rows = dual_rows[c] + 0.125 * along_rows(extrapolated[c])
            cols = dual_cols[c] + 0.125 * along_cols(extrapolated[c])
            norm = jnp.maximum(rows * rows + cols * cols, 1e-30)
            scale = jnp.minimum(mask, ALPHA * lax.rsqrt(norm))
            dual_rows[c] = rows * scale
            dual_cols[c] = cols * scale
        data = [
            jnp.clip(q + o + g * extrapolated[0] + h * extrapolated[1], -LIMIT, LIMIT)
            for q, o, g, h in zip(data, offset, grad_rows, grad_cols)
        ]
        pulls = [pull(data, grad_rows), pull(data, grad_cols)]
        for c in range(2):
            divergence = along_rows(dual_rows[c]) + along_cols(dual_cols[c])
            following = flow[c] + mask * (0.125 * divergence - pulls[c])
            extrapolated[c] = 2.0 * following - flow[c]
            flow[c] = following
    return flow


def columns_of_planes(planes):
    whole = lax.broadcasted_iota(jnp.int32, (LANES, COLUMNS), 1)
    lane = lax.broadcasted_iota(jnp.int32, (LANES, LANES), 1)
    strip = jnp.where(lane < S_MID, lane, jnp.where(lane < S_LEFT, lane + (COLUMNS - S_RIGHT), lane - LANES))
    return jnp.concatenate([x for x, wanted in ((whole, "whole"), (strip, "strip")) if wanted in planes], axis=1)


def upsample(flow, planes, target):
    column = columns_of_planes(planes)
    source = lax.broadcasted_iota(jnp.int32, column.shape, 0)
    spread = jnp.where(source - LEAD == lax.shift_right_arithmetic(column, 3), float(FACTOR), 0.0).astype(jnp.bfloat16)
    rows = flow[0].shape[0]
    wide = split_dot(jnp.concatenate(flow, axis=0), spread)
    for c in range(2):
        for tile in range(column.shape[1] // LANES):
            target[c, tile] = wide[c * rows : (c + 1) * rows, tile * LANES : (tile + 1) * LANES]


def repeat_rows(spread, initial, cells):
    for k, cell in enumerate(cells):
        row = GUARD + k * SUB
        for c in range(2):
            for tile in range(initial.shape[1]):
                initial[c, tile, row : row + SUB, :] = jnp.broadcast_to(
                    spread[c, tile, cell : cell + 1, :], (SUB, LANES)
                )


def shift_whole(here, shift):
    turned = [turn_back(x, shift) for x in here]
    lane = lanes_like(here[0])
    return [
        jnp.where(lane + shift >= LANES, turned[1], turned[0]),
        jnp.where(lane + shift < 0, turned[0], turned[1]),
    ]


def edge_lanes(rows):
    lane = lanes_of(rows)
    return lane == LANES - 1, lane == 0


def columns_whole(fields, edges):
    last, first = edges
    ahead = [pltpu.roll(x, LANES - 1, 1) for x in fields]
    behind = [pltpu.roll(x, 1, 1) for x in fields]
    return [
        jnp.where(last, ahead[1], ahead[0]) - behind[0],
        ahead[1] - jnp.where(first, behind[0], behind[1]),
    ]


def columns_strip(field):
    return pltpu.roll(field, LANES - 1, 1) - pltpu.roll(field, 1, 1)


def strip_windows(window, centre, right, left):
    own = turn_back(window(centre[0]), centre[1])
    beyond_left = turn_back(window(left[0]), left[1])
    beyond_right = turn_back(window(right[0]), right[1])
    lane = lanes_like(own)
    beyond = jnp.where((lane >= S_LEFT) | (lane < S_MID), beyond_left, beyond_right)
    is_beyond = lane >= S_RIGHT
    return jnp.where(is_beyond, beyond, own), jnp.where(is_beyond, columns_strip(beyond), columns_strip(own))


def fine_steps(
    rows_total, chunk, columns, initial, extrap, dual_rows, dual_cols, change, dual_data,
    offsets, grads_rows, grads_cols, data_row, masks_of, result,
):
    planes = len(offsets)
    bands = offsets[0].shape[0]
    chunks = rows_total // chunk
    both = [(c, tile) for c in range(2) for tile in range(planes)]

    for step in range(STEPS):
        source = initial if step == 0 else extrap
        final = step == STEPS - 1

        def dual(k, source=source, step=step):
            row = GUARD + k * chunk if isinstance(k, int) else pl.multiple_of(GUARD + k * chunk, SUB)
            own = pl.ds(k * chunk if isinstance(k, int) else pl.multiple_of(k * chunk, SUB), chunk)
            at = pl.ds(row, chunk)
            masks = masks_of(own)
            along = [columns([source[c, tile, at, :] for tile in range(planes)]) for c in range(2)]
            values = []
            for c, tile in both:
                rows = source[c, tile, pl.ds(row + 1, chunk), :] - source[c, tile, pl.ds(row - 1, chunk), :]
                cols = along[c][tile]
                if step > 0:
                    rows = rows + dual_rows[c, tile, at, :]
                    cols = cols + dual_cols[c, tile, own, :]
                norm = jnp.maximum(rows * rows + cols * cols, 1e-30)
                scale = jnp.minimum(masks[tile], (8.0 * ALPHA) * lax.rsqrt(norm))
                values.append((rows * scale, cols * scale))
            for (c, tile), (rows, cols) in zip(both, values):
                dual_rows[c, tile, at, :] = rows
                dual_cols[c, tile, own, :] = cols

        def primal(k, step=step, final=final):
            data = pl.ds(data_row(k), chunk)
            row = GUARD + k * chunk if isinstance(k, int) else pl.multiple_of(GUARD + k * chunk, SUB)
            own = pl.ds(k * chunk if isinstance(k, int) else pl.multiple_of(k * chunk, SUB), chunk)
            at = pl.ds(row, chunk)
            masks = masks_of(own)
            along = [columns([dual_cols[c, tile, own, :] for tile in range(planes)]) for c in range(2)]
            for tile in range(planes):
                start = [initial[c, tile, at, :] for c in range(2)]
                if step > 0:
                    moved = [extrap[c, tile, at, :] - start[c] for c in range(2)]
                pulls = [None, None]
                duals = []
                for band in range(bands):
                    gradient = (grads_rows[tile][band, data, :], grads_cols[tile][band, data, :])
                    value = offsets[tile][band, data, :]
                    if step > 0:
                        value = value + gradient[0] * moved[0] + gradient[1] * moved[1]
                        value = value + dual_data[band, tile, own, :]
                    value = jnp.clip(value, -LIMIT, LIMIT)
                    duals.append(value)
                    for c in range(2):
                        term = value * gradient[c]
                        pulls[c] = term if pulls[c] is None else pulls[c] + term
                movings = []
                for c in range(2):
                    divergence = (
                        dual_rows[c, tile, pl.ds(row + 1, chunk), :]
                        - dual_rows[c, tile, pl.ds(row - 1, chunk), :]
                        + along[c][tile]
                    )
                    movings.append((masks[tile] * (1.0 / 64.0)) * divergence - pulls[c])
                if step > 0:
                    olds = [change[c, tile, own, :] for c in range(2)]
                for c in range(2):
                    if step == 0:
                        change[c, tile, own, :] = movings[c]
                        extrap[c, tile, at, :] = start[c] + 2.0 * movings[c]
                    else:
                        new = olds[c] + movings[c]
                        if final:
                            result[c, tile, own, :] = start[c] + new
                        else:
                            change[c, tile, own, :] = new
                            extrap[c, tile, at, :] = start[c] + (new + movings[c])
                if not final:
                    for band in range(bands):
                        dual_data[band, tile, own, :] = duals[band]

        dual(0)

        def body(k, carry, dual=dual, primal=primal):
            dual(k)
            primal(k - 1)
            return carry

        lax.fori_loop(1, chunks, body, 0)
        primal(chunks - 1)


def clear_guards(*refs):
    for ref in refs:
        rows = ref.shape[2]
        zero = jnp.zeros((GUARD, LANES), jnp.float32)
        for c in range(2):
            for tile in range(ref.shape[1]):
                ref[c, tile, 0:GUARD, :] = zero
                ref[c, tile, rows - GUARD : rows, :] = zero


def fine_scratch(bands, planes, rows):
    guarded = pltpu.VMEM((2, planes, rows + 2 * GUARD, LANES), jnp.float32)
    plain = pltpu.VMEM((2, planes, rows, LANES), jnp.float32)
    return [guarded, guarded, guarded, plain, plain, pltpu.VMEM((bands, planes, rows, LANES), jnp.float32)]


def blocks(height, block, body):
    assert (height - 2 * SUB) % block == 0

    def step_of(step, carry):
        body(pl.multiple_of(SUB + step * block, SUB))
        return carry

    lax.fori_loop(0, (height - 2 * SUB) // block, step_of, 0)


def whole_terms_kernel(
    second_0, second_1, first_0, first_1, coarse, own_meta,
    swap, offset, grad_rows, grad_cols, strip_e, strip_f, up, down, moved,
):
    seconds, firsts = (second_0, second_1), (first_0, first_1)
    bands, height, _ = second_0.shape
    block = 24
    shift_rows, shift_cols = scalar_at(own_meta, 0, 0), scalar_at(own_meta, 0, HALF)
    centre = (shift_rows.astype(jnp.int32), shift_cols.astype(jnp.int32))
    odd = lax.axis_index("col") % 2

    @pl.when(odd == 1)
    def _():
        pack_message(swap, True, seconds, firsts, coarse, shift_rows, shift_cols)

    @pl.when(odd == 0)
    def _():
        pack_message(swap, False, seconds, firsts, coarse, shift_rows, shift_cols)

    def windows(band, row, rows):
        here = [ref[band, pl.ds(row + centre[0], rows), :] for ref in seconds]
        return shift_whole(here, centre[1])

    ends = (SUB // 2, height - SUB - SUB // 2)
    values = [(row, band, windows(band, row, SUB)) for row in ends for band in range(bands)]
    for row, band, value in values:
        for tile in range(2):
            moved[tile, band, row : row + SUB, :] = value[tile]

    edges = edge_lanes(block)

    def values_of(row):
        results = []
        rows = pl.ds(row, block)
        data = pl.ds(pl.multiple_of(row + HALO, SUB), block)
        for band in range(bands):
            values = windows(band, row, block)
            along = columns_whole(values, edges)
            own = [ref[band, rows, :] for ref in firsts]
            results.append((values, [0.25 * (x - y) for x, y in zip(values, own)], [0.125 * x for x in along]))
        for band in range(bands):
            for tile in range(2):
                moved[tile, band, rows, :] = results[band][0][tile]
                offset[tile, band, data, :] = results[band][1][tile]
                grad_cols[tile, band, data, :] = results[band][2][tile]

    blocks(height, block, values_of)

    def row_gradients(row):
        data = pl.ds(pl.multiple_of(row + HALO, SUB), block)
        for tile in range(2):
            for band in range(bands):
                grad_rows[tile, band, data, :] = 0.125 * (
                    moved[tile, band, pl.ds(row + 1, block), :] - moved[tile, band, pl.ds(row - 1, block), :]
                )

    blocks(height, block, row_gradients)

    def strips(step, carry):
        rows = pl.ds(pl.multiple_of(step * HALF, SUB), HALF)
        for band in range(bands):
            strip_e[band, rows, :] = strip_own([ref[band, rows, :] for ref in seconds])
            strip_f[band, rows, :] = strip_own([ref[band, rows, :] for ref in firsts])
        return carry

    lax.fori_loop(0, height // HALF, strips, 0)

    up[...] = jnp.zeros_like(up)
    down[...] = jnp.zeros_like(down)
    for band in range(bands):
        for tile in range(3):
            second = (second_0, second_1, strip_e)[tile]
            first = (first_0, first_1, strip_f)[tile]
            k = band * 3 + tile
            up[E8 + 8 * k : E8 + 8 * k + 8, :] = second[band, 0:8, :]
            up[E1 + k : E1 + k + 1, :] = second[band, 8:9, :]
            up[F4 + 4 * k : F4 + 4 * k + 4, :] = first[band, 0:4, :]
            down[E8 + 8 * k : E8 + 8 * k + 8, :] = second[band, height - 8 : height, :]
            down[E1 + k : E1 + k + 1, :] = second[band, height - 9 : height - 8, :]
            down[F4 + 4 * k : F4 + 4 * k + 4, :] = first[band, height - 4 : height, :]


def whole_steps_kernel(
    coarse, offset, grad_rows, grad_cols, result, spread, initial, extrap, dual_rows, dual_cols, change, dual_data
):
    bands = offset.shape[1]
    coarse_height = coarse.shape[0] // (2 * bands)
    rows_total = result.shape[2]
    planes = [coarse[k * coarse_height : (k + 1) * coarse_height, :] for k in range(2 * bands)]
    flow = coarse_flow_of(planes[:bands], planes[bands:], 1.0)
    upsample(flow, ("whole",), spread)
    clear_guards(initial, extrap, dual_rows)
    repeat_rows(spread, initial, [BEGIN // FACTOR + k for k in range(rows_total // SUB)])
    chunk = 64
    edges = edge_lanes(chunk)
    fine_steps(
        rows_total, chunk, lambda fields: columns_whole(fields, edges),
        initial, extrap, dual_rows, dual_cols, change, dual_data,
        *[[ref.at[tile] for tile in range(2)] for ref in (offset, grad_rows, grad_cols)],
        lambda k: pl.multiple_of(HALO + BEGIN + k * chunk, SUB), lambda own: (1.0, 1.0), result,
    )


def strip_kernel(
    strip_e, strip_f, from_left, from_right, wide, own_meta, whole,
    middle, strip_second_out, strip_first_out, offset, grad_rows, grad_cols,
    moved, result, spread, initial, extrap, dual_rows, dual_cols, change, dual_data,
):
    bands, height, _ = strip_e.shape
    block = 80
    coarse_height = height // FACTOR
    coarse_width = COLUMNS // FACTOR
    rows_total = height - 2 * BEGIN
    lane = lanes_of()
    centre = (int_at(own_meta, 0, 0), int_at(own_meta, 0, HALF))
    right, has_right = column_meta(from_right)
    left, has_left = column_meta(from_left)
    exists = jnp.where(lane < S_RIGHT, 1.0, jnp.where(lane < S_LEFT, has_right, has_left))
    factor = 0.125 * jnp.concatenate([exists] * (block // SUB), axis=0)

    def fill(step, carry):
        values = []
        rows = pl.ds(pl.multiple_of(step * 32, SUB), 32)
        for half in range(2):
            into = pl.ds(pl.multiple_of(step * 32 + half * (height // 2), SUB), 32)
            for band in range(bands):
                values.append((
                    band, into,
                    strip_second(strip_e[band, into, :], from_left, from_right, rows, half, band),
                    strip_first(strip_f[band, into, :], from_left, from_right, rows, half, band),
                ))
        for band, into, second, first in values:
            strip_second_out[band, into, :] = second
            strip_first_out[band, into, :] = first
        return carry

    lax.fori_loop(0, height // 2 // 32, fill, 0)

    def windows(band, row, rows):
        return strip_windows(
            lambda shift: strip_second_out[band, pl.ds(row + shift, rows), :], centre, right, left
        )

    ends = (SUB // 2, height - SUB - SUB // 2)
    values = [(row, band, windows(band, row, SUB)[0]) for row in ends for band in range(bands)]
    for row, band, value in values:
        moved[band, row : row + SUB, :] = value

    def values_of(row):
        rows = pl.ds(row, block)
        data = pl.ds(pl.multiple_of(row + HALO, SUB), block)
        results = []
        for band in range(bands):
            value, along = windows(band, row, block)
            results.append((value, 0.25 * (value - strip_first_out[band, rows, :]), factor * along))
        for band in range(bands):
            moved[band, rows, :], offset[band, data, :], grad_cols[band, data, :] = results[band]

    blocks(height, block, values_of)

    def row_gradients(row):
        data = pl.ds(pl.multiple_of(row + HALO, SUB), block)
        for band in range(bands):
            grad_rows[band, data, :] = factor * (
                moved[band, pl.ds(row + 1, block), :] - moved[band, pl.ds(row - 1, block), :]
            )

    blocks(height, block, row_gradients)

    mask = jnp.where(lane < LEAD, has_left, jnp.where(lane < LEAD + coarse_width, 1.0, has_right))
    mask = jnp.concatenate([mask] * (coarse_height // SUB), axis=0)
    flow = coarse_flow_of(
        [wide[band] for band in range(bands)], [wide[bands + band] for band in range(bands)], mask
    )
    upsample(flow, ("strip",), spread)
    clear_guards(initial, extrap, dual_rows)
    repeat_rows(spread, initial, [BEGIN // FACTOR + k for k in range(rows_total // SUB)])

    chunk = 96
    masks = jnp.concatenate([exists] * (chunk // SUB), axis=0)
    fine_steps(
        rows_total, chunk, lambda fields: [columns_strip(fields[0])],
        initial, extrap, dual_rows, dual_cols, change, dual_data, [offset], [grad_rows], [grad_cols],
        lambda k: pl.multiple_of(HALO + BEGIN + k * chunk, SUB), lambda own: (masks,), result,
    )
    join(lambda c, tile, rows: whole[c, tile, rows, :], lambda c, rows: result[c, 0, rows, :], middle)


def join(whole, strip, target):
    lane = lanes_of()

    def step_of(step, carry):
        rows = aligned(step * SUB)
        for c in range(2):
            edge = strip(c, rows)
            target[c, rows, 0:LANES] = jnp.where(lane < EDGE, edge, whole(c, 0, rows))
            target[c, rows, LANES:COLUMNS] = jnp.where(lane >= LANES - EDGE, turn(edge, S_TURN), whole(c, 1, rows))
        return carry

    lax.fori_loop(0, target.shape[1] // SUB, step_of, 0, unroll=4)


def outer_kernel(
    count, second_0, second_1, first_0, first_1, strip_e, strip_f, from_left, from_right, wide, got_0, got_1, middle, own_meta,
    _wo, _wr, _wc, _so, _sr, _sc,
    flow_out, coarse_out, whole_offset, whole_rows, whole_cols, strip_offset, strip_rows, strip_cols,
    from_up, from_down, extended, tall, spread, masks, result, joined, coarse_result, sems,
    initial, extrap, dual_rows, dual_cols, change, dual_data,
):
    bands, height, _ = second_0.shape
    coarse_height = height // FACTOR
    coarse_width = COLUMNS // FACTOR
    rows_total = 2 * EACH
    lane = lanes_of()

    put_middle = pltpu.make_async_copy(
        middle.at[:, pl.ds(MARGIN - BEGIN, height - 2 * MARGIN), :],
        flow_out.at[:, pl.ds(MARGIN, height - 2 * MARGIN), :],
        sems.at[0],
    )
    put_middle.start()

    other = without_ends(got_1, "row", count)
    even = is_even("row", got_0)
    from_down[...] = jnp.where(even, got_0[...], other)
    from_up[...] = jnp.where(even, other, got_0[...])

    own = (int_at(own_meta, 0, 0), int_at(own_meta, 0, HALF))
    own_right, has_right = column_meta(from_right)
    own_left, has_left = column_meta(from_left)
    has_up = scalar_at(from_up, META, 32)
    has_down = scalar_at(from_down, META, 32)
    exists = jnp.where(lane < S_RIGHT, 1.0, jnp.where(lane < S_LEFT, has_right, has_left))

    def trio(message):
        return (
            (int_at(message, META, 0), int_at(message, META, 16)),
            (int_at(message, META, 80), int_at(message, META, 96)),
            (int_at(message, META, 48), int_at(message, META, 64)),
        )

    above = trio(from_up)
    below = trio(from_down)

    zero = jnp.zeros((SUB, LANES), jnp.float32)
    tall_rows = coarse_height + 2 * LEAD
    for band in range(bands):
        for plane, at, count in ((band, CS, C_SECOND), (bands + band, CF, C_FIRST)):
            start = at + count * band
            tall[plane, 0:LEAD, :] = zero
            tall[plane, LEAD - count : LEAD, :] = from_up[start : start + count, :]
            tall[plane, LEAD : LEAD + coarse_height, :] = wide[plane]
            tall[plane, LEAD + coarse_height : tall_rows, :] = zero
            tall[plane, LEAD + coarse_height : LEAD + coarse_height + count, :] = from_down[start : start + count, :]
    across = jnp.where(lane < LEAD, has_left, jnp.where(lane < LEAD + coarse_width, 1.0, has_right))
    mask = jnp.concatenate([across * has_up] + [across] * (coarse_height // SUB) + [across * has_down], axis=0)
    flow = coarse_flow_of(
        [tall[band] for band in range(bands)], [tall[bands + band] for band in range(bands)], mask
    )
    for c in range(2):
        coarse_result[c] = turn(flow[c][LEAD : LEAD + coarse_height], -LEAD)[:, :coarse_width]
    put_coarse = pltpu.make_async_copy(coarse_result, coarse_out, sems.at[1])
    put_coarse.start()
    upsample(flow, ("whole", "strip"), spread)
    clear_guards(initial, extrap, dual_rows)
    each = EACH // SUB
    repeat_rows(
        spread, initial,
        [LEAD - 1 + k for k in range(each)] + [tall_rows - LEAD + 1 - each + k for k in range(each)],
    )

    for end in range(2):
        message = (from_up, from_down)[end]
        for band in range(bands):
            for tile in range(3):
                k = band * 3 + tile
                eight = message[E8 + 8 * k : E8 + 8 * k + 8, :]
                one = message[E1 + k : E1 + k + 1, :]
                source = (second_0, second_1, strip_e)[tile]
                if end == 0:
                    extended[end, tile, band, 0:8, :] = zero
                    extended[end, tile, band, 7:8, :] = one
                    extended[end, tile, band, 8:16, :] = eight
                    extended[end, tile, band, 16:40, :] = source[band, 0:24, :]
                else:
                    extended[end, tile, band, 0:24, :] = source[band, height - 24 : height, :]
                    extended[end, tile, band, 24:32, :] = eight
                    extended[end, tile, band, 32:40, :] = zero
                    extended[end, tile, band, 32:33, :] = one
    quarter = jnp.zeros((DEPTH, LANES), jnp.float32)
    edges = edge_lanes(SUB)
    rows_data = whole_offset.shape[2]
    for halo in (True, False):
        results = []
        for end, band in [(end, band) for end in range(2) for band in range(bands)]:
            message = (from_up, from_down)[end]
            own_rows = slice(0, SUB) if end == 0 else slice(height - SUB, height)
            if halo:
                rows = slice(0, SUB) if end == 0 else slice(rows_data - SUB, rows_data)
                base = (SUB, 3 * SUB)[end]
                shifts = (above, below)[end]
                factor = 0.125 * (has_up, has_down)[end]
            else:
                rows = slice(HALO, HALO + SUB) if end == 0 else slice(rows_data - HALO - SUB, rows_data - HALO)
                base = 2 * SUB
                shifts = (own, own_right, own_left)
                factor = 0.125

            def here(tile, shift, band=band, end=end, base=base):
                return extended[end, tile, band, pl.ds(base + shift, SUB), :]

            def down_up(tile, shift, here=here):
                return here(tile, shift + 1) - here(tile, shift - 1)

            firsts = []
            for tile in range(3):
                k = band * 3 + tile
                if halo:
                    four = message[F4 + 4 * k : F4 + 4 * k + 4, :]
                    firsts.append(jnp.concatenate([quarter, four] if end == 0 else [four, quarter], axis=0))
                else:
                    firsts.append((first_0, first_1, strip_f)[tile][band, own_rows, :])
            centre = shifts[0]
            values = shift_whole([here(tile, centre[0]) for tile in range(2)], centre[1])
            changes = shift_whole([down_up(tile, centre[0]) for tile in range(2)], centre[1])
            along = columns_whole(values, edges)
            value, across_cols = strip_windows(lambda shift, here=here: here(2, shift), *shifts)
            change_rows, _ = strip_windows(lambda shift, down_up=down_up: down_up(2, shift), *shifts)
            results.append((
                band, rows,
                [0.25 * (x - y) for x, y in zip([*values, value], firsts)],
                [*[factor * x for x in changes], (factor * exists) * change_rows],
                [*[factor * x for x in along], (factor * exists) * across_cols],
            ))
        for band, rows, offsets, by_rows, by_cols in results:
            for tile in range(2):
                whole_offset[tile, band, rows, :] = offsets[tile]
                whole_rows[tile, band, rows, :] = by_rows[tile]
                whole_cols[tile, band, rows, :] = by_cols[tile]
            strip_offset[band, rows, :] = offsets[2]
            strip_rows[band, rows, :] = by_rows[2]
            strip_cols[band, rows, :] = by_cols[2]

    for i, value in enumerate((jnp.ones((SUB, LANES), jnp.float32), exists)):
        masks[i] = jnp.concatenate([value * has_up] + [value] * (rows_total // SUB - 2) + [value * has_down], axis=0)

    def masks_of(rows):
        whole = masks[0, rows, :]
        return (whole, whole, masks[1, rows, :])

    chunk = 64
    edges = edge_lanes(chunk)

    def data_row(k):
        return pl.multiple_of(k * chunk + jnp.where(k >= EACH // chunk, rows_data - rows_total, 0), SUB)

    fine_steps(
        rows_total, chunk, lambda fields: columns_whole(fields[:2], edges) + [columns_strip(fields[2])],
        initial, extrap, dual_rows, dual_cols, change, dual_data,
        [whole_offset.at[0], whole_offset.at[1], strip_offset],
        [whole_rows.at[0], whole_rows.at[1], strip_rows],
        [whole_cols.at[0], whole_cols.at[1], strip_cols],
        data_row, masks_of, result,
    )
    join(lambda c, tile, rows: result[c, tile, rows, :], lambda c, rows: result[c, 2, rows, :], joined)
    put_top = pltpu.make_async_copy(joined.at[:, pl.ds(SUB, MARGIN), :], flow_out.at[:, pl.ds(0, MARGIN), :], sems.at[2])
    put_bottom = pltpu.make_async_copy(
        joined.at[:, pl.ds(EACH + SUB, MARGIN), :], flow_out.at[:, pl.ds(height - MARGIN, MARGIN), :], sems.at[3]
    )
    put_top.start()
    put_bottom.start()
    put_middle.wait()
    put_coarse.wait()
    put_top.wait()
    put_bottom.wait()


def swap_with(message, axis, start):
    count = lax.axis_size(axis)
    pairs = [(i, i + 1) for i in range(start, count - 1, 2)]
    ends = [(i, i) for i in (0, count - 1)] if start else []
    return lax.ppermute(message, axis, pairs + [(j, i) for i, j in pairs] + ends)


def local(frame_first, frame_second, shifts):
    bands, height, width = frame_first.shape
    assert bands == 4 and width == COLUMNS and height % LANES == 0
    assert lax.axis_size("row") % 2 == 0 and lax.axis_size("col") % 2 == 0
    coarse_height = height // FACTOR
    coarse_width = width // FACTOR
    vmem = pl.BlockSpec(memory_space=pltpu.VMEM)
    hbm = pl.BlockSpec(memory_space=pltpu.HBM)
    tall_rows = coarse_height + 2 * LEAD
    inner_rows = height - 2 * BEGIN

    def shape(*sizes):
        return jax.ShapeDtypeStruct(sizes, jnp.float32)

    def scratch(*sizes):
        return pltpu.VMEM(sizes, jnp.float32)

    def call(kernel, name, arguments, outs, scratches=(), flops=1_000_000, **more):
        more = {"in_specs": [vmem] * len(arguments), "out_specs": (vmem,) * len(outs), **more}
        return pl.pallas_call(
            kernel,
            out_shape=tuple(outs),
            scratch_shapes=list(scratches),
            compiler_params=pltpu.CompilerParams(vmem_limit_bytes=24 * 1024 * 1024),
            cost_estimate=pl.CostEstimate(flops=flops, bytes_accessed=1_000_000, transcendentals=0),
            name=name,
            **more,
        )(*arguments)

    plane = shape(bands, height, LANES)
    column_message = shape(height // 2, LANES)
    row_message = shape(ROW_MESSAGE, LANES)
    whole_data = shape(2, bands, height + 2 * HALO, LANES)
    strip_data = shape(bands, height + 2 * HALO, LANES)

    *frames, coarse, swap, own_meta = call(
        first_kernel,
        "means_and_message",
        [pltpu.with_memory_space_constraint(x, pltpu.HBM) for x in (frame_second, frame_first, shifts)],
        [*[plane] * 4, shape(2 * bands * coarse_height, LANES), column_message, shape(SUB, LANES)],
        [
            scratch(2 * bands * coarse_height, width),
            pltpu.SMEM((1, 1, 2), jnp.int32),
            pltpu.SemaphoreType.DMA((2, bands, 2)),
            pltpu.SemaphoreType.DMA,
        ],
        in_specs=[hbm] * 3,
    )
    got_0 = swap_with(swap, "col", 0)

    swap, *whole_terms, strip_e, strip_f, up_part, down_part = call(
        whole_terms_kernel,
        "whole_terms",
        [*frames, coarse, own_meta],
        [column_message, *[whole_data] * 3, plane, plane, row_message, row_message],
        [scratch(2, bands, height, LANES)],
        flops=8_000_000,
    )
    got_1 = swap_with(swap, "col", 1)

    (whole,) = call(
        whole_steps_kernel,
        "whole_steps",
        [coarse, *whole_terms],
        [shape(2, 2, inner_rows, LANES)],
        [scratch(2, 2, coarse_height, LANES), *fine_scratch(bands, 2, inner_rows)],
        flops=20_000_000,
    )

    swap_0, swap_1, from_left, from_right, wide = call(
        functools.partial(message_kernel, lax.axis_size("col")),
        "row_messages",
        [coarse, own_meta, got_0, got_1, up_part, down_part, whole],
        [row_message, row_message, column_message, column_message, shape(2 * bands, coarse_height, LANES)],
        [scratch(ROW_MESSAGE, LANES)] * 2,
    )
    got_0 = swap_with(swap_0, "row", 0)
    got_1 = swap_with(swap_1, "row", 1)

    middle, strip_e, strip_f, *strip_terms = call(
        strip_kernel,
        "strip",
        [strip_e, strip_f, from_left, from_right, wide, own_meta, whole],
        [shape(2, inner_rows, width), plane, plane, *[strip_data] * 3],
        [
            scratch(bands, height, LANES),
            scratch(2, 1, inner_rows, LANES),
            scratch(2, 1, coarse_height, LANES),
            *fine_scratch(bands, 1, inner_rows),
        ],
        flops=16_000_000,
    )

    flow, coarse_flow, *_ = call(
        functools.partial(outer_kernel, lax.axis_size("row")),
        "outer_rows",
        [
            *frames, strip_e, strip_f, from_left, from_right, wide, got_0, got_1, middle, own_meta,
            *whole_terms, *strip_terms,
        ],
        [shape(2, height, width), shape(2, coarse_height, coarse_width), *[whole_data] * 3, *[strip_data] * 3],
        [
            scratch(ROW_MESSAGE, LANES),
            scratch(ROW_MESSAGE, LANES),
            scratch(2, 3, bands, 40, LANES),
            scratch(2 * bands, tall_rows, LANES),
            scratch(2, 3, tall_rows, LANES),
            scratch(2, 2 * EACH, LANES),
            scratch(2, 3, 2 * EACH, LANES),
            scratch(2, 2 * EACH, width),
            scratch(2, coarse_height, coarse_width),
            pltpu.SemaphoreType.DMA((4,)),
            *fine_scratch(bands, 3, 2 * EACH),
        ],
        out_specs=(hbm, hbm) + (vmem,) * 6,
        input_output_aliases={13 + k: 2 + k for k in range(6)},
    )
    return (flow, coarse_flow)


def solution(mesh):
    return jax.shard_map(
        local,
        mesh=mesh,
        in_specs=(P(None, "row", "col"), P(None, "row", "col"), P("row", "col", None)),
        out_specs=(P(None, "row", "col"), P(None, "row", "col")),
        check_vma=False,
    )
```

```python
import functools

import jax
import jax.numpy as jnp
from jax import lax
from jax.experimental import pallas as pl
from jax.experimental.pallas import tpu as pltpu
from jax.sharding import PartitionSpec as P

FACTOR = 8
MAXD = 4
STEPS = 3
LANES = 128
COLUMNS = 2 * LANES
HALF = 64
SUB = 8
DEPTH = 4
REACH = DEPTH + MAXD + 1
SLOT = 16
C_SECOND = 6
C_FIRST = 5
LEAD = 8
MARGIN = 48
EDGE = 46
GUARD = 8
HALO = 8
BEGIN = 40
EACH = MARGIN + 16
LIMIT = 0.3
ALPHA = 0.3

S_MID = 55
S_RIGHT = 110
S_LEFT = LANES - REACH
S_TURN = COLUMNS - S_RIGHT - LANES

E8 = 0
E1 = 96
F4 = 112
CS = 160
CF = CS + 4 * C_SECOND
META = 208
ROW_MESSAGE = 216

COARSE_A = REACH + DEPTH
COARSE_B = SLOT + REACH + DEPTH
SHIFT_R = 2 * SLOT + REACH + DEPTH
SHIFT_C = SHIFT_R + 1
EXISTS = SHIFT_R + 2


def lanes_of(rows=SUB):
    return lax.broadcasted_iota(jnp.int32, (rows, LANES), 1)


def lanes_like(x):
    return lax.broadcasted_iota(jnp.int32, x.shape, 1)


def turn(x, amount):
    amount = amount % LANES
    return x if amount == 0 else pltpu.roll(x, amount, 1)


def turn_back(x, shift):
    return pltpu.roll(x, lax.rem(LANES - shift, LANES), 1)


def split_dot(x, exact):
    high = x.astype(jnp.bfloat16)
    rest = x - high.astype(jnp.float32)
    middle = rest.astype(jnp.bfloat16)
    low = (rest - middle.astype(jnp.float32)).astype(jnp.bfloat16)
    parts = [jnp.dot(part, exact, preferred_element_type=jnp.float32) for part in (low, middle, high)]
    return parts[0] + parts[1] + parts[2]


def scalar_at(ref, row, lane):
    return ref[row : row + 1, lane : lane + 1][0, 0]


def int_at(ref, row, lane):
    return scalar_at(ref, row, lane).astype(jnp.int32)


def is_even(axis, like):
    return jnp.broadcast_to(lax.axis_index(axis) % 2, like.shape) == 0


def without_ends(message, axis, count):
    place = jnp.broadcast_to(lax.axis_index(axis), message.shape)
    return jnp.where((place > 0) & (place < count - 1), message[...], 0.0)


def aligned(row):
    return pl.ds(pl.multiple_of(row, SUB), SUB)


def pack_message(target, to_right, seconds, firsts, coarse, shift_rows, shift_cols):
    bands, height, _ = seconds[0].shape
    second, first = seconds[int(to_right)], firsts[int(to_right)]
    second_from = LANES - REACH if to_right else 0
    first_from = LANES - DEPTH if to_right else 0
    coarse_from = LEAD + COLUMNS // FACTOR - C_SECOND if to_right else LEAD
    lane = lanes_of()

    def pack(step, carry):
        packed = jnp.zeros((SUB, LANES), jnp.float32)
        for half in range(2):
            rows = aligned(step * SUB + half * (height // 2))
            cells = coarse[rows, :]
            base = half * HALF
            for band in range(bands):
                at = base + band * SLOT
                packed = jnp.where(lane >= at, turn(second[band, rows, :], at - second_from), packed)
                packed = jnp.where(lane >= at + REACH, turn(first[band, rows, :], at + REACH - first_from), packed)
                if band == 0:
                    packed = jnp.where(lane >= base + COARSE_A, turn(cells, base + COARSE_A - coarse_from), packed)
                if band == 1:
                    packed = jnp.where(lane >= base + COARSE_B, turn(cells, base + COARSE_B - coarse_from - 3), packed)
                if band == 2:
                    packed = jnp.where(lane >= base + SHIFT_R, shift_rows, packed)
                    packed = jnp.where(lane >= base + SHIFT_C, shift_cols, packed)
                    packed = jnp.where(lane >= base + EXISTS, 1.0, packed)
        target[aligned(step * SUB), :] = packed
        return carry

    lax.fori_loop(0, height // 2 // SUB, pack, 0, unroll=4)


def column_meta(message):
    return (int_at(message, 0, SHIFT_R), int_at(message, 0, SHIFT_C)), scalar_at(message, 0, EXISTS)


def strip_second(base, from_left, from_right, rows, half, band):
    at = half * HALF + band * SLOT
    lane = lanes_like(base)
    cells = jnp.where(lane >= S_RIGHT, turn(from_right[rows, :], S_RIGHT - at), base)
    return jnp.where(lane >= S_LEFT, turn(from_left[rows, :], S_LEFT - at), cells)


def strip_first(base, from_left, from_right, rows, half, band):
    at = half * HALF + band * SLOT + REACH
    lane = lanes_like(base)
    cells = jnp.where(lane >= S_RIGHT, turn(from_right[rows, :], S_RIGHT - at), base)
    return jnp.where(lane >= S_LEFT, turn(from_left[rows, :], LANES - DEPTH - at), cells)


def strip_own(planes):
    return jnp.where(lanes_like(planes[0]) < S_MID, planes[0], turn(planes[1], -S_TURN))


def first_kernel(
    second_hbm, first_hbm, shifts_hbm, second_0, second_1, first_0, first_1, coarse, swap, own_meta,
    sums, shifts, sems, shift_sem,
):
    seconds, firsts = (second_0, second_1), (first_0, first_1)
    bands, height, _ = second_0.shape
    width = COLUMNS
    coarse_height = height // FACTOR
    lane = lanes_of()
    get_shifts = pltpu.make_async_copy(shifts_hbm, shifts, shift_sem)
    get_shifts.start()
    copies = []
    for image, (source, refs) in enumerate(((second_hbm, seconds), (first_hbm, firsts))):
        for band in range(bands):
            for tile, ref in enumerate(refs):
                copy = pltpu.make_async_copy(
                    source.at[band, :, pl.ds(tile * LANES, LANES)], ref.at[band], sems.at[image, band, tile]
                )
                copy.start()
                copies.append((image * bands + band, tile, ref, band, copy))
    cell = lax.broadcasted_iota(jnp.int32, (width, LANES), 0)
    place = lax.broadcasted_iota(jnp.int32, (width, LANES), 1)
    weights = jnp.where(place - LEAD == cell // FACTOR, 1.0 / (FACTOR * FACTOR), 0.0).astype(jnp.bfloat16)
    for plane, tile, ref, band, copy in copies:
        copy.wait()
        total = ref[band, pl.ds(0, coarse_height, stride=FACTOR), :]
        for k in range(1, FACTOR):
            total = total + ref[band, pl.ds(k, coarse_height, stride=FACTOR), :]
        at = slice(tile * LANES, (tile + 1) * LANES)
        sums[plane * coarse_height : (plane + 1) * coarse_height, at] = total
    coarse[...] = split_dot(sums[...], weights)
    get_shifts.wait()
    shift_rows = shifts[0, 0, 0].astype(jnp.float32)
    shift_cols = shifts[0, 0, 1].astype(jnp.float32)
    own_meta[...] = jnp.where(lane < HALF, shift_rows, shift_cols)
    odd = lax.axis_index("col") % 2

    @pl.when(odd == 0)
    def _():
        pack_message(swap, True, seconds, firsts, coarse, shift_rows, shift_cols)

    @pl.when(odd == 1)
    def _():
        pack_message(swap, False, seconds, firsts, coarse, shift_rows, shift_cols)


def message_kernel(
    count, coarse, own_meta, got_0, got_1, up_part, down_part, _whole, swap_0, swap_1, from_left, from_right, wide, up, down
):
    other = without_ends(got_1, "col", count)
    even = is_even("col", got_0)
    from_right[...] = jnp.where(even, got_0[...], other)
    from_left[...] = jnp.where(even, other, got_0[...])
    planes_coarse, coarse_height, _ = wide.shape
    bands = planes_coarse // 2
    end = from_left.shape[0]
    coarse_width = COLUMNS // FACTOR
    lane = lanes_of()
    for plane in range(planes_coarse):
        half, block = divmod(plane, planes_coarse // 2)
        for step in range(coarse_height // SUB):
            own = slice(plane * coarse_height + step * SUB, plane * coarse_height + (step + 1) * SUB)
            rows = slice(block * coarse_height + step * SUB, block * coarse_height + (step + 1) * SUB)
            at = half * HALF
            left = from_left[rows, :]
            right = from_right[rows, :]
            start = LEAD - C_SECOND
            cells = turn(left, start - at - COARSE_A)
            cells = jnp.where(lane >= start + 3, turn(left, start + 3 - at - COARSE_B), cells)
            cells = jnp.where(lane >= LEAD, coarse[own, :], cells)
            start = LEAD + coarse_width
            cells = jnp.where(lane >= start, turn(right, start - at - COARSE_A), cells)
            cells = jnp.where(lane >= start + 3, turn(right, start + 3 - at - COARSE_B), cells)
            wide[plane, step * SUB : (step + 1) * SUB, :] = cells
    up[...] = up_part[...]
    down[...] = down_part[...]
    for band in range(bands):
        k = band * 3 + 2
        for target, half, near, next_rows, row_of in (
            (up, 0, slice(0, 8), slice(8, 16), 0),
            (down, 1, slice(end - 8, end), slice(end - 16, end - 8), 7),
        ):
            at = slice(E8 + 8 * k, E8 + 8 * k + 8)
            target[at, :] = strip_second(target[at, :], from_left, from_right, near, half, band)
            one = jnp.broadcast_to(target[E1 + k : E1 + k + 1, :], (SUB, LANES))
            one = strip_second(one, from_left, from_right, next_rows, half, band)
            target[E1 + k : E1 + k + 1, :] = one[row_of : row_of + 1]
            four = target[F4 + 4 * k : F4 + 4 * k + 4, :]
            four = strip_first(jnp.concatenate([four, four], axis=0), from_left, from_right, near, half, band)
            target[F4 + 4 * k : F4 + 4 * k + 4, :] = four[4 * half : 4 * half + 4]
        for at, plane, count in ((CS, band, C_SECOND), (CF, bands + band, C_FIRST)):
            up[at + count * band : at + count * band + count, :] = wide[plane, 0:count, :]
            down[at + count * band : at + count * band + count, :] = wide[
                plane, coarse_height - count : coarse_height, :
            ]
    packed = jnp.where(lane < 16, own_meta[...], jnp.where(lane < 32, turn(own_meta[...], HALF), 1.0))
    for message, at in ((from_left, 48), (from_right, 80)):
        meta = message[0:SUB, :]
        rows = jnp.broadcast_to(meta[:, SHIFT_R : SHIFT_R + 1], (SUB, LANES))
        cols = jnp.broadcast_to(meta[:, SHIFT_C : SHIFT_C + 1], (SUB, LANES))
        packed = jnp.where(lane >= at, rows, packed)
        packed = jnp.where(lane >= at + 16, cols, packed)
    up[META : META + SUB, :] = packed
    down[META : META + SUB, :] = packed
    even = is_even("row", up)
    swap_0[...] = jnp.where(even, down[...], up[...])
    swap_1[...] = jnp.where(even, up[...], down[...])


def coarse_flow_of(second, first, mask):
    def along_rows(x):
        size = x.shape[0]
        return pltpu.roll(x, size - 1, 0) - pltpu.roll(x, 1, 0)

    def along_cols(x):
        return pltpu.roll(x, LANES - 1, 1) - pltpu.roll(x, 1, 1)

    grad_rows = [0.125 * along_rows(x) for x in second]
    grad_cols = [0.125 * along_cols(x) for x in second]
    offset = [0.25 * (x - y) for x, y in zip(second, first)]
    data = [jnp.clip(x, -LIMIT, LIMIT) for x in offset]

    def pull(duals, grads):
        total = duals[0] * grads[0]
        for x, y in zip(duals[1:], grads[1:]):
            total = total + x * y
        return total

    flow = [-mask * pull(data, grad_rows), -mask * pull(data, grad_cols)]
    extrapolated = [2.0 * x for x in flow]
    dual_rows = [0.0, 0.0]
    dual_cols = [0.0, 0.0]
    for step in range(1, STEPS):
        for c in range(2):
            rows = dual_rows[c] + 0.125 * along_rows(extrapolated[c])
            cols = dual_cols[c] + 0.125 * along_cols(extrapolated[c])
            norm = jnp.maximum(rows * rows + cols * cols, 1e-30)
            scale = jnp.minimum(mask, ALPHA * lax.rsqrt(norm))
            dual_rows[c] = rows * scale
            dual_cols[c] = cols * scale
        data = [
            jnp.clip(q + o + g * extrapolated[0] + h * extrapolated[1], -LIMIT, LIMIT)
            for q, o, g, h in zip(data, offset, grad_rows, grad_cols)
        ]
        pulls = [pull(data, grad_rows), pull(data, grad_cols)]
        for c in range(2):
            divergence = along_rows(dual_rows[c]) + along_cols(dual_cols[c])
            following = flow[c] + mask * (0.125 * divergence - pulls[c])
            extrapolated[c] = 2.0 * following - flow[c]
            flow[c] = following
    return flow


def columns_of_planes(planes):
    whole = lax.broadcasted_iota(jnp.int32, (LANES, COLUMNS), 1)
    lane = lax.broadcasted_iota(jnp.int32, (LANES, LANES), 1)
    strip = jnp.where(lane < S_MID, lane, jnp.where(lane < S_LEFT, lane + (COLUMNS - S_RIGHT), lane - LANES))
    return jnp.concatenate([x for x, wanted in ((whole, "whole"), (strip, "strip")) if wanted in planes], axis=1)


def upsample(flow, planes, target):
    column = columns_of_planes(planes)
    source = lax.broadcasted_iota(jnp.int32, column.shape, 0)
    spread = jnp.where(source - LEAD == lax.shift_right_arithmetic(column, 3), float(FACTOR), 0.0).astype(jnp.bfloat16)
    rows = flow[0].shape[0]
    wide = split_dot(jnp.concatenate(flow, axis=0), spread)
    for c in range(2):
        for tile in range(column.shape[1] // LANES):
            target[c, tile] = wide[c * rows : (c + 1) * rows, tile * LANES : (tile + 1) * LANES]


def repeat_rows(spread, initial, cells):
    for k, cell in enumerate(cells):
        row = GUARD + k * SUB
        for c in range(2):
            for tile in range(initial.shape[1]):
                initial[c, tile, row : row + SUB, :] = jnp.broadcast_to(
                    spread[c, tile, cell : cell + 1, :], (SUB, LANES)
                )


def shift_whole(here, shift):
    turned = [turn_back(x, shift) for x in here]
    lane = lanes_like(here[0])
    return [
        jnp.where(lane + shift >= LANES, turned[1], turned[0]),
        jnp.where(lane + shift < 0, turned[0], turned[1]),
    ]


def edge_lanes(rows):
    lane = lanes_of(rows)
    return lane == LANES - 1, lane == 0


def columns_whole(fields, edges):
    last, first = edges
    ahead = [pltpu.roll(x, LANES - 1, 1) for x in fields]
    behind = [pltpu.roll(x, 1, 1) for x in fields]
    return [
        jnp.where(last, ahead[1], ahead[0]) - behind[0],
        ahead[1] - jnp.where(first, behind[0], behind[1]),
    ]


def columns_strip(field):
    return pltpu.roll(field, LANES - 1, 1) - pltpu.roll(field, 1, 1)


def strip_windows(window, centre, right, left):
    own = turn_back(window(centre[0]), centre[1])
    beyond_left = turn_back(window(left[0]), left[1])
    beyond_right = turn_back(window(right[0]), right[1])
    lane = lanes_like(own)
    beyond = jnp.where((lane >= S_LEFT) | (lane < S_MID), beyond_left, beyond_right)
    is_beyond = lane >= S_RIGHT
    return jnp.where(is_beyond, beyond, own), jnp.where(is_beyond, columns_strip(beyond), columns_strip(own))


def fine_steps(
    rows_total, chunk, columns, initial, extrap, dual_rows, dual_cols, change, dual_data,
    offsets, grads_rows, grads_cols, data_row, masks_of, result,
):
    planes = len(offsets)
    bands = offsets[0].shape[0]
    chunks = rows_total // chunk
    both = [(c, tile) for c in range(2) for tile in range(planes)]

    for step in range(STEPS):
        source = initial if step == 0 else extrap
        final = step == STEPS - 1

        def dual(k, source=source, step=step):
            row = GUARD + k * chunk
            own = pl.ds(k * chunk, chunk)
            at = pl.ds(row, chunk)
            masks = masks_of(own)
            along = [columns([source[c, tile, at, :] for tile in range(planes)]) for c in range(2)]
            values = []
            for c, tile in both:
                rows = source[c, tile, pl.ds(row + 1, chunk), :] - source[c, tile, pl.ds(row - 1, chunk), :]
                cols = along[c][tile]
                if step > 0:
                    rows = rows + dual_rows[c, tile, at, :]
                    cols = cols + dual_cols[c, tile, own, :]
                norm = jnp.maximum(rows * rows + cols * cols, 1e-30)
                scale = jnp.minimum(masks[tile], (8.0 * ALPHA) * lax.rsqrt(norm))
                values.append((rows * scale, cols * scale))
            for (c, tile), (rows, cols) in zip(both, values):
                dual_rows[c, tile, at, :] = rows
                dual_cols[c, tile, own, :] = cols

        def primal(k, step=step, final=final):
            data = pl.ds(data_row(k), chunk)
            row = GUARD + k * chunk
            own = pl.ds(k * chunk, chunk)
            at = pl.ds(row, chunk)
            masks = masks_of(own)
            along = [columns([dual_cols[c, tile, own, :] for tile in range(planes)]) for c in range(2)]
            for tile in range(planes):
                start = [initial[c, tile, at, :] for c in range(2)]
                if step > 0:
                    moved = [extrap[c, tile, at, :] - start[c] for c in range(2)]
                pulls = [None, None]
                duals = []
                for band in range(bands):
                    gradient = (grads_rows[tile][band, data, :], grads_cols[tile][band, data, :])
                    value = offsets[tile][band, data, :]
                    if step > 0:
                        value = value + gradient[0] * moved[0] + gradient[1] * moved[1]
                        value = value + dual_data[band, tile, own, :]
                    value = jnp.clip(value, -LIMIT, LIMIT)
                    duals.append(value)
                    for c in range(2):
                        term = value * gradient[c]
                        pulls[c] = term if pulls[c] is None else pulls[c] + term
                movings = []
                for c in range(2):
                    divergence = (
                        dual_rows[c, tile, pl.ds(row + 1, chunk), :]
                        - dual_rows[c, tile, pl.ds(row - 1, chunk), :]
                        + along[c][tile]
                    )
                    movings.append((masks[tile] * (1.0 / 64.0)) * divergence - pulls[c])
                if step > 0:
                    olds = [change[c, tile, own, :] for c in range(2)]
                for c in range(2):
                    if step == 0:
                        change[c, tile, own, :] = movings[c]
                        extrap[c, tile, at, :] = start[c] + 2.0 * movings[c]
                    else:
                        new = olds[c] + movings[c]
                        if final:
                            result[c, tile, own, :] = start[c] + new
                        else:
                            change[c, tile, own, :] = new
                            extrap[c, tile, at, :] = start[c] + (new + movings[c])
                if not final:
                    for band in range(bands):
                        dual_data[band, tile, own, :] = duals[band]

        dual(0)
        for k in range(1, chunks):
            dual(k)
            primal(k - 1)
        primal(chunks - 1)


def clear_guards(*refs):
    for ref in refs:
        rows = ref.shape[2]
        zero = jnp.zeros((GUARD, LANES), jnp.float32)
        for c in range(2):
            for tile in range(ref.shape[1]):
                ref[c, tile, 0:GUARD, :] = zero
                ref[c, tile, rows - GUARD : rows, :] = zero


def fine_scratch(bands, planes, rows):
    guarded = pltpu.VMEM((2, planes, rows + 2 * GUARD, LANES), jnp.float32)
    plain = pltpu.VMEM((2, planes, rows, LANES), jnp.float32)
    return [guarded, guarded, guarded, plain, plain, pltpu.VMEM((bands, planes, rows, LANES), jnp.float32)]


def blocks(height, block, body):
    assert (height - 2 * SUB) % block == 0

    for step in range((height - 2 * SUB) // block):
        body(SUB + step * block)


def whole_terms_kernel(
    second_0, second_1, first_0, first_1, coarse, own_meta,
    swap, offset, grad_rows, grad_cols, strip_e, strip_f, up, down, moved,
):
    seconds, firsts = (second_0, second_1), (first_0, first_1)
    bands, height, _ = second_0.shape
    block = 80
    shift_rows, shift_cols = scalar_at(own_meta, 0, 0), scalar_at(own_meta, 0, HALF)
    centre = (shift_rows.astype(jnp.int32), shift_cols.astype(jnp.int32))
    odd = lax.axis_index("col") % 2

    @pl.when(odd == 1)
    def _():
        pack_message(swap, True, seconds, firsts, coarse, shift_rows, shift_cols)

    @pl.when(odd == 0)
    def _():
        pack_message(swap, False, seconds, firsts, coarse, shift_rows, shift_cols)

    def windows(band, row, rows):
        here = [ref[band, pl.ds(row + centre[0], rows), :] for ref in seconds]
        return shift_whole(here, centre[1])

    ends = (SUB // 2, height - SUB - SUB // 2)
    values = [(row, band, windows(band, row, SUB)) for row in ends for band in range(bands)]
    for row, band, value in values:
        for tile in range(2):
            moved[tile, band, row : row + SUB, :] = value[tile]

    edges = edge_lanes(block)

    def values_of(row):
        results = []
        rows = pl.ds(row, block)
        data = pl.ds(row + HALO, block)
        for band in range(bands):
            values = windows(band, row, block)
            along = columns_whole(values, edges)
            own = [ref[band, rows, :] for ref in firsts]
            results.append((values, [0.25 * (x - y) for x, y in zip(values, own)], [0.125 * x for x in along]))
        for band in range(bands):
            for tile in range(2):
                moved[tile, band, rows, :] = results[band][0][tile]
                offset[tile, band, data, :] = results[band][1][tile]
                grad_cols[tile, band, data, :] = results[band][2][tile]

    blocks(height, block, values_of)

    def row_gradients(row):
        data = pl.ds(row + HALO, block)
        for tile in range(2):
            for band in range(bands):
                grad_rows[tile, band, data, :] = 0.125 * (
                    moved[tile, band, pl.ds(row + 1, block), :] - moved[tile, band, pl.ds(row - 1, block), :]
                )

    blocks(height, block, row_gradients)

    def strips(step, carry):
        rows = pl.ds(pl.multiple_of(step * HALF, SUB), HALF)
        for band in range(bands):
            strip_e[band, rows, :] = strip_own([ref[band, rows, :] for ref in seconds])
            strip_f[band, rows, :] = strip_own([ref[band, rows, :] for ref in firsts])
        return carry

    lax.fori_loop(0, height // HALF, strips, 0)

    up[...] = jnp.zeros_like(up)
    down[...] = jnp.zeros_like(down)
    for band in range(bands):
        for tile in range(3):
            second = (second_0, second_1, strip_e)[tile]
            first = (first_0, first_1, strip_f)[tile]
            k = band * 3 + tile
            up[E8 + 8 * k : E8 + 8 * k + 8, :] = second[band, 0:8, :]
            up[E1 + k : E1 + k + 1, :] = second[band, 8:9, :]
            up[F4 + 4 * k : F4 + 4 * k + 4, :] = first[band, 0:4, :]
            down[E8 + 8 * k : E8 + 8 * k + 8, :] = second[band, height - 8 : height, :]
            down[E1 + k : E1 + k + 1, :] = second[band, height - 9 : height - 8, :]
            down[F4 + 4 * k : F4 + 4 * k + 4, :] = first[band, height - 4 : height, :]


def whole_steps_kernel(
    coarse, offset, grad_rows, grad_cols, result, spread, initial, extrap, dual_rows, dual_cols, change, dual_data
):
    bands = offset.shape[1]
    coarse_height = coarse.shape[0] // (2 * bands)
    rows_total = result.shape[2]
    planes = [coarse[k * coarse_height : (k + 1) * coarse_height, :] for k in range(2 * bands)]
    flow = coarse_flow_of(planes[:bands], planes[bands:], 1.0)
    upsample(flow, ("whole",), spread)
    clear_guards(initial, extrap, dual_rows)
    repeat_rows(spread, initial, [BEGIN // FACTOR + k for k in range(rows_total // SUB)])
    chunk = 88
    edges = edge_lanes(chunk)
    fine_steps(
        rows_total, chunk, lambda fields: columns_whole(fields, edges),
        initial, extrap, dual_rows, dual_cols, change, dual_data,
        *[[ref.at[tile] for tile in range(2)] for ref in (offset, grad_rows, grad_cols)],
        lambda k: HALO + BEGIN + k * chunk, lambda own: (1.0, 1.0), result,
    )


def strip_kernel(
    strip_e, strip_f, from_left, from_right, wide, own_meta, whole,
    middle, strip_second_out, strip_first_out, offset, grad_rows, grad_cols,
    moved, result, spread, initial, extrap, dual_rows, dual_cols, change, dual_data,
):
    bands, height, _ = strip_e.shape
    block = 120
    coarse_height = height // FACTOR
    coarse_width = COLUMNS // FACTOR
    rows_total = height - 2 * BEGIN
    lane = lanes_of()
    centre = (int_at(own_meta, 0, 0), int_at(own_meta, 0, HALF))
    right, has_right = column_meta(from_right)
    left, has_left = column_meta(from_left)
    exists = jnp.where(lane < S_RIGHT, 1.0, jnp.where(lane < S_LEFT, has_right, has_left))
    factor = 0.125 * jnp.concatenate([exists] * (block // SUB), axis=0)

    def fill(step, carry):
        values = []
        rows = pl.ds(pl.multiple_of(step * 32, SUB), 32)
        for half in range(2):
            into = pl.ds(pl.multiple_of(step * 32 + half * (height // 2), SUB), 32)
            for band in range(bands):
                values.append((
                    band, into,
                    strip_second(strip_e[band, into, :], from_left, from_right, rows, half, band),
                    strip_first(strip_f[band, into, :], from_left, from_right, rows, half, band),
                ))
        for band, into, second, first in values:
            strip_second_out[band, into, :] = second
            strip_first_out[band, into, :] = first
        return carry

    lax.fori_loop(0, height // 2 // 32, fill, 0)

    def windows(band, row, rows):
        return strip_windows(
            lambda shift: strip_second_out[band, pl.ds(row + shift, rows), :], centre, right, left
        )

    ends = (SUB // 2, height - SUB - SUB // 2)
    values = [(row, band, windows(band, row, SUB)[0]) for row in ends for band in range(bands)]
    for row, band, value in values:
        moved[band, row : row + SUB, :] = value

    def values_of(row):
        rows = pl.ds(row, block)
        data = pl.ds(row + HALO, block)
        results = []
        for band in range(bands):
            value, along = windows(band, row, block)
            results.append((value, 0.25 * (value - strip_first_out[band, rows, :]), factor * along))
        for band in range(bands):
            moved[band, rows, :], offset[band, data, :], grad_cols[band, data, :] = results[band]

    blocks(height, block, values_of)

    def row_gradients(row):
        data = pl.ds(row + HALO, block)
        for band in range(bands):
            grad_rows[band, data, :] = factor * (
                moved[band, pl.ds(row + 1, block), :] - moved[band, pl.ds(row - 1, block), :]
            )

    blocks(height, block, row_gradients)

    mask = jnp.where(lane < LEAD, has_left, jnp.where(lane < LEAD + coarse_width, 1.0, has_right))
    mask = jnp.concatenate([mask] * (coarse_height // SUB), axis=0)
    flow = coarse_flow_of(
        [wide[band] for band in range(bands)], [wide[bands + band] for band in range(bands)], mask
    )
    upsample(flow, ("strip",), spread)
    clear_guards(initial, extrap, dual_rows)
    repeat_rows(spread, initial, [BEGIN // FACTOR + k for k in range(rows_total // SUB)])

    chunk = 176
    masks = jnp.concatenate([exists] * (chunk // SUB), axis=0)
    fine_steps(
        rows_total, chunk, lambda fields: [columns_strip(fields[0])],
        initial, extrap, dual_rows, dual_cols, change, dual_data, [offset], [grad_rows], [grad_cols],
        lambda k: HALO + BEGIN + k * chunk, lambda own: (masks,), result,
    )
    join(lambda c, tile, rows: whole[c, tile, rows, :], lambda c, rows: result[c, 0, rows, :], middle)


def join(whole, strip, target):
    lane = lanes_of()

    def step_of(step, carry):
        rows = aligned(step * SUB)
        for c in range(2):
            edge = strip(c, rows)
            target[c, rows, 0:LANES] = jnp.where(lane < EDGE, edge, whole(c, 0, rows))
            target[c, rows, LANES:COLUMNS] = jnp.where(lane >= LANES - EDGE, turn(edge, S_TURN), whole(c, 1, rows))
        return carry

    lax.fori_loop(0, target.shape[1] // SUB, step_of, 0, unroll=4)


def outer_kernel(
    count, second_0, second_1, first_0, first_1, strip_e, strip_f, from_left, from_right, wide, got_0, got_1, middle, own_meta,
    _wo, _wr, _wc, _so, _sr, _sc,
    flow_out, coarse_out, whole_offset, whole_rows, whole_cols, strip_offset, strip_rows, strip_cols,
    from_up, from_down, extended, tall, spread, masks, result, joined, coarse_result, sems,
    initial, extrap, dual_rows, dual_cols, change, dual_data,
):
    bands, height, _ = second_0.shape
    coarse_height = height // FACTOR
    coarse_width = COLUMNS // FACTOR
    rows_total = 2 * EACH
    lane = lanes_of()

    put_middle = pltpu.make_async_copy(
        middle.at[:, pl.ds(MARGIN - BEGIN, height - 2 * MARGIN), :],
        flow_out.at[:, pl.ds(MARGIN, height - 2 * MARGIN), :],
        sems.at[0],
    )
    put_middle.start()

    other = without_ends(got_1, "row", count)
    even = is_even("row", got_0)
    from_down[...] = jnp.where(even, got_0[...], other)
    from_up[...] = jnp.where(even, other, got_0[...])

    own = (int_at(own_meta, 0, 0), int_at(own_meta, 0, HALF))
    own_right, has_right = column_meta(from_right)
    own_left, has_left = column_meta(from_left)
    has_up = scalar_at(from_up, META, 32)
    has_down = scalar_at(from_down, META, 32)
    exists = jnp.where(lane < S_RIGHT, 1.0, jnp.where(lane < S_LEFT, has_right, has_left))

    def trio(message):
        return (
            (int_at(message, META, 0), int_at(message, META, 16)),
            (int_at(message, META, 80), int_at(message, META, 96)),
            (int_at(message, META, 48), int_at(message, META, 64)),
        )

    above = trio(from_up)
    below = trio(from_down)

    zero = jnp.zeros((SUB, LANES), jnp.float32)
    tall_rows = coarse_height + 2 * LEAD
    for band in range(bands):
        for plane, at, count in ((band, CS, C_SECOND), (bands + band, CF, C_FIRST)):
            start = at + count * band
            tall[plane, 0:LEAD, :] = zero
            tall[plane, LEAD - count : LEAD, :] = from_up[start : start + count, :]
            tall[plane, LEAD : LEAD + coarse_height, :] = wide[plane]
            tall[plane, LEAD + coarse_height : tall_rows, :] = zero
            tall[plane, LEAD + coarse_height : LEAD + coarse_height + count, :] = from_down[start : start + count, :]
    across = jnp.where(lane < LEAD, has_left, jnp.where(lane < LEAD + coarse_width, 1.0, has_right))
    mask = jnp.concatenate([across * has_up] + [across] * (coarse_height // SUB) + [across * has_down], axis=0)
    flow = coarse_flow_of(
        [tall[band] for band in range(bands)], [tall[bands + band] for band in range(bands)], mask
    )
    for c in range(2):
        coarse_result[c] = turn(flow[c][LEAD : LEAD + coarse_height], -LEAD)[:, :coarse_width]
    put_coarse = pltpu.make_async_copy(coarse_result, coarse_out, sems.at[1])
    put_coarse.start()
    upsample(flow, ("whole", "strip"), spread)
    clear_guards(initial, extrap, dual_rows)
    each = EACH // SUB
    repeat_rows(
        spread, initial,
        [LEAD - 1 + k for k in range(each)] + [tall_rows - LEAD + 1 - each + k for k in range(each)],
    )

    for end in range(2):
        message = (from_up, from_down)[end]
        for band in range(bands):
            for tile in range(3):
                k = band * 3 + tile
                eight = message[E8 + 8 * k : E8 + 8 * k + 8, :]
                one = message[E1 + k : E1 + k + 1, :]
                source = (second_0, second_1, strip_e)[tile]
                if end == 0:
                    extended[end, tile, band, 0:8, :] = zero
                    extended[end, tile, band, 7:8, :] = one
                    extended[end, tile, band, 8:16, :] = eight
                    extended[end, tile, band, 16:40, :] = source[band, 0:24, :]
                else:
                    extended[end, tile, band, 0:24, :] = source[band, height - 24 : height, :]
                    extended[end, tile, band, 24:32, :] = eight
                    extended[end, tile, band, 32:40, :] = zero
                    extended[end, tile, band, 32:33, :] = one
    quarter = jnp.zeros((DEPTH, LANES), jnp.float32)
    edges = edge_lanes(SUB)
    rows_data = whole_offset.shape[2]
    for halo in (True, False):
        results = []
        for end, band in [(end, band) for end in range(2) for band in range(bands)]:
            message = (from_up, from_down)[end]
            own_rows = slice(0, SUB) if end == 0 else slice(height - SUB, height)
            if halo:
                rows = slice(0, SUB) if end == 0 else slice(rows_data - SUB, rows_data)
                base = (SUB, 3 * SUB)[end]
                shifts = (above, below)[end]
                factor = 0.125 * (has_up, has_down)[end]
            else:
                rows = slice(HALO, HALO + SUB) if end == 0 else slice(rows_data - HALO - SUB, rows_data - HALO)
                base = 2 * SUB
                shifts = (own, own_right, own_left)
                factor = 0.125

            def here(tile, shift, band=band, end=end, base=base):
                return extended[end, tile, band, pl.ds(base + shift, SUB), :]

            def down_up(tile, shift, here=here):
                return here(tile, shift + 1) - here(tile, shift - 1)

            firsts = []
            for tile in range(3):
                k = band * 3 + tile
                if halo:
                    four = message[F4 + 4 * k : F4 + 4 * k + 4, :]
                    firsts.append(jnp.concatenate([quarter, four] if end == 0 else [four, quarter], axis=0))
                else:
                    firsts.append((first_0, first_1, strip_f)[tile][band, own_rows, :])
            centre = shifts[0]
            values = shift_whole([here(tile, centre[0]) for tile in range(2)], centre[1])
            changes = shift_whole([down_up(tile, centre[0]) for tile in range(2)], centre[1])
            along = columns_whole(values, edges)
            value, across_cols = strip_windows(lambda shift, here=here: here(2, shift), *shifts)
            change_rows, _ = strip_windows(lambda shift, down_up=down_up: down_up(2, shift), *shifts)
            results.append((
                band, rows,
                [0.25 * (x - y) for x, y in zip([*values, value], firsts)],
                [*[factor * x for x in changes], (factor * exists) * change_rows],
                [*[factor * x for x in along], (factor * exists) * across_cols],
            ))
        for band, rows, offsets, by_rows, by_cols in results:
            for tile in range(2):
                whole_offset[tile, band, rows, :] = offsets[tile]
                whole_rows[tile, band, rows, :] = by_rows[tile]
                whole_cols[tile, band, rows, :] = by_cols[tile]
            strip_offset[band, rows, :] = offsets[2]
            strip_rows[band, rows, :] = by_rows[2]
            strip_cols[band, rows, :] = by_cols[2]

    for i, value in enumerate((jnp.ones((SUB, LANES), jnp.float32), exists)):
        masks[i] = jnp.concatenate([value * has_up] + [value] * (rows_total // SUB - 2) + [value * has_down], axis=0)

    def masks_of(rows):
        whole = masks[0, rows, :]
        return (whole, whole, masks[1, rows, :])

    chunk = 64
    edges = edge_lanes(chunk)

    def data_row(k):
        return k * chunk + (rows_data - rows_total if k >= EACH // chunk else 0)

    fine_steps(
        rows_total, chunk, lambda fields: columns_whole(fields[:2], edges) + [columns_strip(fields[2])],
        initial, extrap, dual_rows, dual_cols, change, dual_data,
        [whole_offset.at[0], whole_offset.at[1], strip_offset],
        [whole_rows.at[0], whole_rows.at[1], strip_rows],
        [whole_cols.at[0], whole_cols.at[1], strip_cols],
        data_row, masks_of, result,
    )
    join(lambda c, tile, rows: result[c, tile, rows, :], lambda c, rows: result[c, 2, rows, :], joined)
    put_top = pltpu.make_async_copy(joined.at[:, pl.ds(SUB, MARGIN), :], flow_out.at[:, pl.ds(0, MARGIN), :], sems.at[2])
    put_bottom = pltpu.make_async_copy(
        joined.at[:, pl.ds(EACH + SUB, MARGIN), :], flow_out.at[:, pl.ds(height - MARGIN, MARGIN), :], sems.at[3]
    )
    put_top.start()
    put_bottom.start()
    put_middle.wait()
    put_coarse.wait()
    put_top.wait()
    put_bottom.wait()


def swap_with(message, axis, start):
    names = ("row", "col")
    sizes = [lax.axis_size(name) for name in names]
    along = names.index(axis)
    count, others = sizes[along], sizes[1 - along]

    def number(place, other):
        row, col = (place, other) if along == 0 else (other, place)
        return row * sizes[1] + col

    pairs = [(number(i, k), number(i + 1, k)) for i in range(start, count - 1, 2) for k in range(others)]
    if start:
        pairs += [(number(i, k), number(i, k + 1)) for i in (0, count - 1) for k in range(0, others, 2)]
    return lax.ppermute(message, names, pairs + [(j, i) for i, j in pairs])


def local(frame_first, frame_second, shifts):
    bands, height, width = frame_first.shape
    assert bands == 4 and width == COLUMNS and height % LANES == 0
    assert lax.axis_size("row") % 2 == 0 and lax.axis_size("col") % 2 == 0
    coarse_height = height // FACTOR
    coarse_width = width // FACTOR
    vmem = pl.BlockSpec(memory_space=pltpu.VMEM)
    hbm = pl.BlockSpec(memory_space=pltpu.HBM)
    tall_rows = coarse_height + 2 * LEAD
    inner_rows = height - 2 * BEGIN

    def shape(*sizes):
        return jax.ShapeDtypeStruct(sizes, jnp.float32)

    def scratch(*sizes):
        return pltpu.VMEM(sizes, jnp.float32)

    def call(kernel, name, arguments, outs, scratches=(), flops=1_000_000, **more):
        more = {"in_specs": [vmem] * len(arguments), "out_specs": (vmem,) * len(outs), **more}
        return pl.pallas_call(
            kernel,
            out_shape=tuple(outs),
            scratch_shapes=list(scratches),
            compiler_params=pltpu.CompilerParams(vmem_limit_bytes=24 * 1024 * 1024),
            cost_estimate=pl.CostEstimate(flops=flops, bytes_accessed=1_000_000, transcendentals=0),
            name=name,
            **more,
        )(*arguments)

    plane = shape(bands, height, LANES)
    column_message = shape(height // 2, LANES)
    row_message = shape(ROW_MESSAGE, LANES)
    whole_data = shape(2, bands, height + 2 * HALO, LANES)
    strip_data = shape(bands, height + 2 * HALO, LANES)

    *frames, coarse, swap, own_meta = call(
        first_kernel,
        "means_and_message",
        [pltpu.with_memory_space_constraint(x, pltpu.HBM) for x in (frame_second, frame_first, shifts)],
        [*[plane] * 4, shape(2 * bands * coarse_height, LANES), column_message, shape(SUB, LANES)],
        [
            scratch(2 * bands * coarse_height, width),
            pltpu.SMEM((1, 1, 2), jnp.int32),
            pltpu.SemaphoreType.DMA((2, bands, 2)),
            pltpu.SemaphoreType.DMA,
        ],
        in_specs=[hbm] * 3,
    )
    got_0 = swap_with(swap, "col", 0)

    swap, *whole_terms, strip_e, strip_f, up_part, down_part = call(
        whole_terms_kernel,
        "whole_terms",
        [*frames, coarse, own_meta],
        [column_message, *[whole_data] * 3, plane, plane, row_message, row_message],
        [scratch(2, bands, height, LANES)],
        flops=8_000_000,
    )
    got_1 = swap_with(swap, "col", 1)

    (whole,) = call(
        whole_steps_kernel,
        "whole_steps",
        [coarse, *whole_terms],
        [shape(2, 2, inner_rows, LANES)],
        [scratch(2, 2, coarse_height, LANES), *fine_scratch(bands, 2, inner_rows)],
        flops=20_000_000,
    )

    swap_0, swap_1, from_left, from_right, wide = call(
        functools.partial(message_kernel, lax.axis_size("col")),
        "row_messages",
        [coarse, own_meta, got_0, got_1, up_part, down_part, whole],
        [row_message, row_message, column_message, column_message, shape(2 * bands, coarse_height, LANES)],
        [scratch(ROW_MESSAGE, LANES)] * 2,
    )
    got_0 = swap_with(swap_0, "row", 0)
    got_1 = swap_with(swap_1, "row", 1)

    middle, strip_e, strip_f, *strip_terms = call(
        strip_kernel,
        "strip",
        [strip_e, strip_f, from_left, from_right, wide, own_meta, whole],
        [shape(2, inner_rows, width), plane, plane, *[strip_data] * 3],
        [
            scratch(bands, height, LANES),
            scratch(2, 1, inner_rows, LANES),
            scratch(2, 1, coarse_height, LANES),
            *fine_scratch(bands, 1, inner_rows),
        ],
        flops=16_000_000,
    )

    flow, coarse_flow, *_ = call(
        functools.partial(outer_kernel, lax.axis_size("row")),
        "outer_rows",
        [
            *frames, strip_e, strip_f, from_left, from_right, wide, got_0, got_1, middle, own_meta,
            *whole_terms, *strip_terms,
        ],
        [shape(2, height, width), shape(2, coarse_height, coarse_width), *[whole_data] * 3, *[strip_data] * 3],
        [
            scratch(ROW_MESSAGE, LANES),
            scratch(ROW_MESSAGE, LANES),
            scratch(2, 3, bands, 40, LANES),
            scratch(2 * bands, tall_rows, LANES),
            scratch(2, 3, tall_rows, LANES),
            scratch(2, 2 * EACH, LANES),
            scratch(2, 3, 2 * EACH, LANES),
            scratch(2, 2 * EACH, width),
            scratch(2, coarse_height, coarse_width),
            pltpu.SemaphoreType.DMA((4,)),
            *fine_scratch(bands, 3, 2 * EACH),
        ],
        out_specs=(hbm, hbm) + (vmem,) * 6,
        input_output_aliases={13 + k: 2 + k for k in range(6)},
    )
    return (flow, coarse_flow)


def solution(mesh):
    return jax.shard_map(
        local,
        mesh=mesh,
        in_specs=(P(None, "row", "col"), P(None, "row", "col"), P("row", "col", None)),
        out_specs=(P(None, "row", "col"), P(None, "row", "col")),
        check_vma=False,
    )
```

```python
import functools

import jax
import jax.numpy as jnp
from jax import lax
from jax.experimental import pallas as pl
from jax.experimental.pallas import tpu as pltpu
from jax.sharding import PartitionSpec as P

FACTOR = 8
MAXD = 4
STEPS = 3
LANES = 128
COLUMNS = 2 * LANES
HALF = 64
SUB = 8
DEPTH = 4
REACH = DEPTH + MAXD + 1
SLOT = 16
C_SECOND = 6
C_FIRST = 5
LEAD = 8
MARGIN = 48
EDGE = 46
GUARD = 8
HALO = 8
BEGIN = 40
EACH = MARGIN + 16
LIMIT = 0.3
ALPHA = 0.3

S_MID = 55
S_RIGHT = 110
S_LEFT = LANES - REACH
S_TURN = COLUMNS - S_RIGHT - LANES

E8 = 0
E1 = 96
F4 = 112
CS = 160
CF = CS + 4 * C_SECOND
META = 208
ROW_MESSAGE = 216

COARSE_A = REACH + DEPTH
COARSE_B = SLOT + REACH + DEPTH
SHIFT_R = 2 * SLOT + REACH + DEPTH
SHIFT_C = SHIFT_R + 1
EXISTS = SHIFT_R + 2


def lanes_of(rows=SUB):
    return lax.broadcasted_iota(jnp.int32, (rows, LANES), 1)


def lanes_like(x):
    return lax.broadcasted_iota(jnp.int32, x.shape, 1)


def turn(x, amount):
    amount = amount % LANES
    return x if amount == 0 else pltpu.roll(x, amount, 1)


def turn_back(x, shift):
    return pltpu.roll(x, lax.rem(LANES - shift, LANES), 1)


def split_dot(x, exact):
    high = x.astype(jnp.bfloat16)
    rest = x - high.astype(jnp.float32)
    middle = rest.astype(jnp.bfloat16)
    low = (rest - middle.astype(jnp.float32)).astype(jnp.bfloat16)
    parts = [jnp.dot(part, exact, preferred_element_type=jnp.float32) for part in (low, middle, high)]
    return parts[0] + parts[1] + parts[2]


def scalar_at(ref, row, lane):
    return ref[row : row + 1, lane : lane + 1][0, 0]


def int_at(ref, row, lane):
    return scalar_at(ref, row, lane).astype(jnp.int32)


def is_even(axis, like):
    return jnp.broadcast_to(lax.axis_index(axis) % 2, like.shape) == 0


def without_ends(message, axis, count):
    place = jnp.broadcast_to(lax.axis_index(axis), message.shape)
    return jnp.where((place > 0) & (place < count - 1), message[...], 0.0)


def staggered(items, compute, store, depth):
    pending = []
    for item in items:
        pending.append((item, compute(item)))
        if len(pending) > depth:
            store(*pending.pop(0))
    for entry in pending:
        store(*entry)


def aligned(row):
    return pl.ds(pl.multiple_of(row, SUB), SUB)


def pack_message(target, to_right, seconds, firsts, coarse, shift_rows, shift_cols):
    bands, height, _ = seconds[0].shape
    second, first = seconds[int(to_right)], firsts[int(to_right)]
    second_from = LANES - REACH if to_right else 0
    first_from = LANES - DEPTH if to_right else 0
    coarse_from = LEAD + COLUMNS // FACTOR - C_SECOND if to_right else LEAD
    lane = lanes_of()

    def compute(step):
        packed = jnp.zeros((SUB, LANES), jnp.float32)
        for half in range(2):
            row = step * SUB + half * (height // 2)
            rows = slice(row, row + SUB)
            cells = coarse[rows, :]
            base = half * HALF
            for band in range(bands):
                at = base + band * SLOT
                packed = jnp.where(lane >= at, turn(second[band, rows, :], at - second_from), packed)
                packed = jnp.where(lane >= at + REACH, turn(first[band, rows, :], at + REACH - first_from), packed)
                if band == 0:
                    packed = jnp.where(lane >= base + COARSE_A, turn(cells, base + COARSE_A - coarse_from), packed)
                if band == 1:
                    packed = jnp.where(lane >= base + COARSE_B, turn(cells, base + COARSE_B - coarse_from - 3), packed)
                if band == 2:
                    packed = jnp.where(lane >= base + SHIFT_R, shift_rows, packed)
                    packed = jnp.where(lane >= base + SHIFT_C, shift_cols, packed)
                    packed = jnp.where(lane >= base + EXISTS, 1.0, packed)
        return packed

    def store(step, packed):
        target[step * SUB : (step + 1) * SUB, :] = packed

    staggered(range(height // 2 // SUB), compute, store, 4)


def column_meta(message):
    return (int_at(message, 0, SHIFT_R), int_at(message, 0, SHIFT_C)), scalar_at(message, 0, EXISTS)


def strip_second(base, from_left, from_right, rows, half, band):
    at = half * HALF + band * SLOT
    lane = lanes_like(base)
    cells = jnp.where(lane >= S_RIGHT, turn(from_right[rows, :], S_RIGHT - at), base)
    return jnp.where(lane >= S_LEFT, turn(from_left[rows, :], S_LEFT - at), cells)


def strip_first(base, from_left, from_right, rows, half, band):
    at = half * HALF + band * SLOT + REACH
    lane = lanes_like(base)
    cells = jnp.where(lane >= S_RIGHT, turn(from_right[rows, :], S_RIGHT - at), base)
    return jnp.where(lane >= S_LEFT, turn(from_left[rows, :], LANES - DEPTH - at), cells)


def strip_own(planes):
    return jnp.where(lanes_like(planes[0]) < S_MID, planes[0], turn(planes[1], -S_TURN))


def first_kernel(
    second_hbm, first_hbm, shifts_hbm, second_0, second_1, first_0, first_1, coarse, swap, own_meta,
    sums, shifts, sems, shift_sem,
):
    seconds, firsts = (second_0, second_1), (first_0, first_1)
    bands, height, _ = second_0.shape
    width = COLUMNS
    coarse_height = height // FACTOR
    lane = lanes_of()
    get_shifts = pltpu.make_async_copy(shifts_hbm, shifts, shift_sem)
    get_shifts.start()
    copies = []
    for image, (source, refs) in enumerate(((second_hbm, seconds), (first_hbm, firsts))):
        for band in range(bands):
            for tile, ref in enumerate(refs):
                copy = pltpu.make_async_copy(
                    source.at[band, :, pl.ds(tile * LANES, LANES)], ref.at[band], sems.at[image, band, tile]
                )
                copy.start()
                copies.append((image * bands + band, tile, ref, band, copy))
    cell = lax.broadcasted_iota(jnp.int32, (width, LANES), 0)
    place = lax.broadcasted_iota(jnp.int32, (width, LANES), 1)
    weights = jnp.where(place - LEAD == cell // FACTOR, 1.0 / (FACTOR * FACTOR), 0.0).astype(jnp.bfloat16)
    for plane, tile, ref, band, copy in copies:
        copy.wait()
        total = ref[band, pl.ds(0, coarse_height, stride=FACTOR), :]
        for k in range(1, FACTOR):
            total = total + ref[band, pl.ds(k, coarse_height, stride=FACTOR), :]
        at = slice(tile * LANES, (tile + 1) * LANES)
        sums[plane * coarse_height : (plane + 1) * coarse_height, at] = total
    coarse[...] = split_dot(sums[...], weights)
    get_shifts.wait()
    shift_rows = shifts[0, 0, 0].astype(jnp.float32)
    shift_cols = shifts[0, 0, 1].astype(jnp.float32)
    own_meta[...] = jnp.where(lane < HALF, shift_rows, shift_cols)
    odd = lax.axis_index("col") % 2

    @pl.when(odd == 0)
    def _():
        pack_message(swap, True, seconds, firsts, coarse, shift_rows, shift_cols)

    @pl.when(odd == 1)
    def _():
        pack_message(swap, False, seconds, firsts, coarse, shift_rows, shift_cols)


def message_kernel(
    count, coarse, own_meta, got_0, got_1, up_part, down_part, _whole, swap_0, swap_1, from_left, from_right, wide, up, down
):
    other = without_ends(got_1, "col", count)
    even = is_even("col", got_0)
    from_right[...] = jnp.where(even, got_0[...], other)
    from_left[...] = jnp.where(even, other, got_0[...])
    planes_coarse, coarse_height, _ = wide.shape
    bands = planes_coarse // 2
    end = from_left.shape[0]
    coarse_width = COLUMNS // FACTOR
    lane = lanes_of()
    for plane in range(planes_coarse):
        half, block = divmod(plane, planes_coarse // 2)
        for step in range(coarse_height // SUB):
            own = slice(plane * coarse_height + step * SUB, plane * coarse_height + (step + 1) * SUB)
            rows = slice(block * coarse_height + step * SUB, block * coarse_height + (step + 1) * SUB)
            at = half * HALF
            left = from_left[rows, :]
            right = from_right[rows, :]
            start = LEAD - C_SECOND
            cells = turn(left, start - at - COARSE_A)
            cells = jnp.where(lane >= start + 3, turn(left, start + 3 - at - COARSE_B), cells)
            cells = jnp.where(lane >= LEAD, coarse[own, :], cells)
            start = LEAD + coarse_width
            cells = jnp.where(lane >= start, turn(right, start - at - COARSE_A), cells)
            cells = jnp.where(lane >= start + 3, turn(right, start + 3 - at - COARSE_B), cells)
            wide[plane, step * SUB : (step + 1) * SUB, :] = cells
    up[...] = up_part[...]
    down[...] = down_part[...]
    for band in range(bands):
        k = band * 3 + 2
        for target, half, near, next_rows, row_of in (
            (up, 0, slice(0, 8), slice(8, 16), 0),
            (down, 1, slice(end - 8, end), slice(end - 16, end - 8), 7),
        ):
            at = slice(E8 + 8 * k, E8 + 8 * k + 8)
            target[at, :] = strip_second(target[at, :], from_left, from_right, near, half, band)
            one = jnp.broadcast_to(target[E1 + k : E1 + k + 1, :], (SUB, LANES))
            one = strip_second(one, from_left, from_right, next_rows, half, band)
            target[E1 + k : E1 + k + 1, :] = one[row_of : row_of + 1]
            four = target[F4 + 4 * k : F4 + 4 * k + 4, :]
            four = strip_first(jnp.concatenate([four, four], axis=0), from_left, from_right, near, half, band)
            target[F4 + 4 * k : F4 + 4 * k + 4, :] = four[4 * half : 4 * half + 4]
        for at, plane, count in ((CS, band, C_SECOND), (CF, bands + band, C_FIRST)):
            up[at + count * band : at + count * band + count, :] = wide[plane, 0:count, :]
            down[at + count * band : at + count * band + count, :] = wide[
                plane, coarse_height - count : coarse_height, :
            ]
    packed = jnp.where(lane < 16, own_meta[...], jnp.where(lane < 32, turn(own_meta[...], HALF), 1.0))
    for message, at in ((from_left, 48), (from_right, 80)):
        meta = message[0:SUB, :]
        rows = jnp.broadcast_to(meta[:, SHIFT_R : SHIFT_R + 1], (SUB, LANES))
        cols = jnp.broadcast_to(meta[:, SHIFT_C : SHIFT_C + 1], (SUB, LANES))
        packed = jnp.where(lane >= at, rows, packed)
        packed = jnp.where(lane >= at + 16, cols, packed)
    up[META : META + SUB, :] = packed
    down[META : META + SUB, :] = packed
    even = is_even("row", up)
    swap_0[...] = jnp.where(even, down[...], up[...])
    swap_1[...] = jnp.where(even, up[...], down[...])


def coarse_flow_of(second, first, mask):
    def along_rows(x):
        size = x.shape[0]
        return pltpu.roll(x, size - 1, 0) - pltpu.roll(x, 1, 0)

    def along_cols(x):
        return pltpu.roll(x, LANES - 1, 1) - pltpu.roll(x, 1, 1)

    grad_rows = [0.125 * along_rows(x) for x in second]
    grad_cols = [0.125 * along_cols(x) for x in second]
    offset = [0.25 * (x - y) for x, y in zip(second, first)]
    data = [jnp.clip(x, -LIMIT, LIMIT) for x in offset]

    def pull(duals, grads):
        total = duals[0] * grads[0]
        for x, y in zip(duals[1:], grads[1:]):
            total = total + x * y
        return total

    flow = [-mask * pull(data, grad_rows), -mask * pull(data, grad_cols)]
    extrapolated = [2.0 * x for x in flow]
    dual_rows = [0.0, 0.0]
    dual_cols = [0.0, 0.0]
    for step in range(1, STEPS):
        for c in range(2):
            rows = dual_rows[c] + 0.125 * along_rows(extrapolated[c])
            cols = dual_cols[c] + 0.125 * along_cols(extrapolated[c])
            norm = jnp.maximum(rows * rows + cols * cols, 1e-30)
            scale = jnp.minimum(mask, ALPHA * lax.rsqrt(norm))
            dual_rows[c] = rows * scale
            dual_cols[c] = cols * scale
        data = [
            jnp.clip(q + o + g * extrapolated[0] + h * extrapolated[1], -LIMIT, LIMIT)
            for q, o, g, h in zip(data, offset, grad_rows, grad_cols)
        ]
        pulls = [pull(data, grad_rows), pull(data, grad_cols)]
        for c in range(2):
            divergence = along_rows(dual_rows[c]) + along_cols(dual_cols[c])
            following = flow[c] + mask * (0.125 * divergence - pulls[c])
            extrapolated[c] = 2.0 * following - flow[c]
            flow[c] = following
    return flow


def columns_of_planes(planes):
    whole = lax.broadcasted_iota(jnp.int32, (LANES, COLUMNS), 1)
    lane = lax.broadcasted_iota(jnp.int32, (LANES, LANES), 1)
    strip = jnp.where(lane < S_MID, lane, jnp.where(lane < S_LEFT, lane + (COLUMNS - S_RIGHT), lane - LANES))
    return jnp.concatenate([x for x, wanted in ((whole, "whole"), (strip, "strip")) if wanted in planes], axis=1)


def upsample(flow, planes, target):
    column = columns_of_planes(planes)
    source = lax.broadcasted_iota(jnp.int32, column.shape, 0)
    spread = jnp.where(source - LEAD == lax.shift_right_arithmetic(column, 3), float(FACTOR), 0.0).astype(jnp.bfloat16)
    rows = flow[0].shape[0]
    wide = split_dot(jnp.concatenate(flow, axis=0), spread)
    for c in range(2):
        for tile in range(column.shape[1] // LANES):
            target[c, tile] = wide[c * rows : (c + 1) * rows, tile * LANES : (tile + 1) * LANES]


def repeat_rows(spread, initial, cells):
    for k, cell in enumerate(cells):
        row = GUARD + k * SUB
        for c in range(2):
            for tile in range(initial.shape[1]):
                initial[c, tile, row : row + SUB, :] = jnp.broadcast_to(
                    spread[c, tile, cell : cell + 1, :], (SUB, LANES)
                )


def shift_whole(here, shift):
    turned = [turn_back(x, shift) for x in here]
    lane = lanes_like(here[0])
    return [
        jnp.where(lane + shift >= LANES, turned[1], turned[0]),
        jnp.where(lane + shift < 0, turned[0], turned[1]),
    ]


def edge_lanes(rows):
    lane = lanes_of(rows)
    return lane == LANES - 1, lane == 0


def columns_whole(fields, edges):
    last, first = edges
    ahead = [pltpu.roll(x, LANES - 1, 1) for x in fields]
    behind = [pltpu.roll(x, 1, 1) for x in fields]
    return [
        jnp.where(last, ahead[1], ahead[0]) - behind[0],
        ahead[1] - jnp.where(first, behind[0], behind[1]),
    ]


def columns_strip(field):
    return pltpu.roll(field, LANES - 1, 1) - pltpu.roll(field, 1, 1)


def strip_windows(window, centre, right, left):
    own = turn_back(window(centre[0]), centre[1])
    beyond_left = turn_back(window(left[0]), left[1])
    beyond_right = turn_back(window(right[0]), right[1])
    lane = lanes_like(own)
    beyond = jnp.where((lane >= S_LEFT) | (lane < S_MID), beyond_left, beyond_right)
    is_beyond = lane >= S_RIGHT
    return jnp.where(is_beyond, beyond, own), jnp.where(is_beyond, columns_strip(beyond), columns_strip(own))


def fine_steps(
    rows_total, chunk, columns, initial, extrap, dual_rows, dual_cols, change, dual_data,
    offsets, grads_rows, grads_cols, data_row, masks_of, result,
):
    planes = len(offsets)
    bands = offsets[0].shape[0]
    chunks = rows_total // chunk
    both = [(c, tile) for c in range(2) for tile in range(planes)]

    for step in range(STEPS):
        source = initial if step == 0 else extrap
        final = step == STEPS - 1

        def dual(k, source=source, step=step):
            row = GUARD + k * chunk
            own = pl.ds(k * chunk, chunk)
            at = pl.ds(row, chunk)
            masks = masks_of(own)
            along = [columns([source[c, tile, at, :] for tile in range(planes)]) for c in range(2)]
            values = []
            for c, tile in both:
                rows = source[c, tile, pl.ds(row + 1, chunk), :] - source[c, tile, pl.ds(row - 1, chunk), :]
                cols = along[c][tile]
                if step > 0:
                    rows = rows + dual_rows[c, tile, at, :]
                    cols = cols + dual_cols[c, tile, own, :]
                norm = jnp.maximum(rows * rows + cols * cols, 1e-30)
                scale = jnp.minimum(masks[tile], (8.0 * ALPHA) * lax.rsqrt(norm))
                values.append((rows * scale, cols * scale))
            for (c, tile), (rows, cols) in zip(both, values):
                dual_rows[c, tile, at, :] = rows
                dual_cols[c, tile, own, :] = cols

        def primal(k, step=step, final=final):
            data = pl.ds(data_row(k), chunk)
            row = GUARD + k * chunk
            own = pl.ds(k * chunk, chunk)
            at = pl.ds(row, chunk)
            masks = masks_of(own)
            along = [columns([dual_cols[c, tile, own, :] for tile in range(planes)]) for c in range(2)]
            for tile in range(planes):
                start = [initial[c, tile, at, :] for c in range(2)]
                if step > 0:
                    moved = [extrap[c, tile, at, :] - start[c] for c in range(2)]
                pulls = [None, None]
                duals = []
                for band in range(bands):
                    gradient = (grads_rows[tile][band, data, :], grads_cols[tile][band, data, :])
                    value = offsets[tile][band, data, :]
                    if step > 0:
                        value = value + gradient[0] * moved[0] + gradient[1] * moved[1]
                        value = value + dual_data[band, tile, own, :]
                    value = jnp.clip(value, -LIMIT, LIMIT)
                    duals.append(value)
                    for c in range(2):
                        term = value * gradient[c]
                        pulls[c] = term if pulls[c] is None else pulls[c] + term
                movings = []
                for c in range(2):
                    divergence = (
                        dual_rows[c, tile, pl.ds(row + 1, chunk), :]
                        - dual_rows[c, tile, pl.ds(row - 1, chunk), :]
                        + along[c][tile]
                    )
                    movings.append((masks[tile] * (1.0 / 64.0)) * divergence - pulls[c])
                if step > 0:
                    olds = [change[c, tile, own, :] for c in range(2)]
                for c in range(2):
                    if step == 0:
                        change[c, tile, own, :] = movings[c]
                        extrap[c, tile, at, :] = start[c] + 2.0 * movings[c]
                    else:
                        new = olds[c] + movings[c]
                        if final:
                            result[c, tile, own, :] = start[c] + new
                        else:
                            change[c, tile, own, :] = new
                            extrap[c, tile, at, :] = start[c] + (new + movings[c])
                if not final:
                    for band in range(bands):
                        dual_data[band, tile, own, :] = duals[band]

        dual(0)
        for k in range(1, chunks):
            dual(k)
            primal(k - 1)
        primal(chunks - 1)


def clear_guards(*refs):
    for ref in refs:
        rows = ref.shape[2]
        zero = jnp.zeros((GUARD, LANES), jnp.float32)
        for c in range(2):
            for tile in range(ref.shape[1]):
                ref[c, tile, 0:GUARD, :] = zero
                ref[c, tile, rows - GUARD : rows, :] = zero


def fine_scratch(bands, planes, rows):
    guarded = pltpu.VMEM((2, planes, rows + 2 * GUARD, LANES), jnp.float32)
    plain = pltpu.VMEM((2, planes, rows, LANES), jnp.float32)
    return [guarded, guarded, guarded, plain, plain, pltpu.VMEM((bands, planes, rows, LANES), jnp.float32)]


def pieces(bands, height, rows):
    assert (height - 2 * SUB) % rows == 0
    return [(band, row) for row in range(SUB, height - SUB, rows) for band in range(bands)]


def whole_terms_kernel(
    second_0, second_1, first_0, first_1, coarse, own_meta,
    swap, offset, grad_rows, grad_cols, initial, strip_e, strip_f, up, down, moved, spread,
):
    seconds, firsts = (second_0, second_1), (first_0, first_1)
    bands, height, _ = second_0.shape
    block = 24
    coarse_height = coarse.shape[0] // (2 * bands)
    shift_rows, shift_cols = scalar_at(own_meta, 0, 0), scalar_at(own_meta, 0, HALF)
    centre = (shift_rows.astype(jnp.int32), shift_cols.astype(jnp.int32))
    odd = lax.axis_index("col") % 2

    @pl.when(odd == 1)
    def _():
        pack_message(swap, True, seconds, firsts, coarse, shift_rows, shift_cols)

    @pl.when(odd == 0)
    def _():
        pack_message(swap, False, seconds, firsts, coarse, shift_rows, shift_cols)

    def windows(band, row, rows):
        here = [ref[band, pl.ds(row + centre[0], rows), :] for ref in seconds]
        return shift_whole(here, centre[1])

    planes = [coarse[k * coarse_height : (k + 1) * coarse_height, :] for k in range(2 * bands)]
    flow = coarse_flow_of(planes[:bands], planes[bands:], 1.0)
    upsample(flow, ("whole",), spread)

    def store_moved(item, values):
        band, row = item
        for tile in range(2):
            moved[tile, band, row : row + SUB, :] = values[tile]

    ends = [(band, row) for row in (SUB // 2, height - SUB - SUB // 2) for band in range(bands)]
    staggered(ends, lambda item: windows(*item, SUB), store_moved, 4)

    edges = edge_lanes(block)

    def values_of(item):
        band, row = item
        values = windows(band, row, block)
        along = columns_whole(values, edges)
        own = [ref[band, row : row + block, :] for ref in firsts]
        return values, [0.25 * (x - y) for x, y in zip(values, own)], [0.125 * x for x in along]

    def store_values(item, results):
        band, row = item
        values, offsets, gradients = results
        data = slice(row + HALO, row + HALO + block)
        for tile in range(2):
            moved[tile, band, row : row + block, :] = values[tile]
            offset[tile, band, data, :] = offsets[tile]
            grad_cols[tile, band, data, :] = gradients[tile]

    staggered(pieces(bands, height, block), values_of, store_values, 3)

    def strips_of(item):
        band, row = item
        rows = slice(row, row + 32)
        return strip_own([ref[band, rows, :] for ref in seconds]), strip_own([ref[band, rows, :] for ref in firsts])

    def store_strips(item, results):
        band, row = item
        strip_e[band, row : row + 32, :], strip_f[band, row : row + 32, :] = results

    staggered([(band, row) for band in range(bands) for row in range(0, height, 32)], strips_of, store_strips, 3)

    def gradient_of(item):
        band, row = item
        return [0.125 * (moved[tile, band, pl.ds(row + 1, 40), :] - moved[tile, band, pl.ds(row - 1, 40), :]) for tile in range(2)]

    def store_gradient(item, results):
        band, row = item
        for tile in range(2):
            grad_rows[tile, band, row + HALO : row + HALO + 40, :] = results[tile]

    staggered(pieces(bands, height, 40), gradient_of, store_gradient, 2)

    clear_guards(initial)
    rows_total = initial.shape[2] - 2 * GUARD
    repeat_rows(spread, initial, [BEGIN // FACTOR + k for k in range(rows_total // SUB)])

    up[...] = jnp.zeros_like(up)
    down[...] = jnp.zeros_like(down)
    for band in range(bands):
        for tile in range(3):
            second = (second_0, second_1, strip_e)[tile]
            first = (first_0, first_1, strip_f)[tile]
            k = band * 3 + tile
            up[E8 + 8 * k : E8 + 8 * k + 8, :] = second[band, 0:8, :]
            up[E1 + k : E1 + k + 1, :] = second[band, 8:9, :]
            up[F4 + 4 * k : F4 + 4 * k + 4, :] = first[band, 0:4, :]
            down[E8 + 8 * k : E8 + 8 * k + 8, :] = second[band, height - 8 : height, :]
            down[E1 + k : E1 + k + 1, :] = second[band, height - 9 : height - 8, :]
            down[F4 + 4 * k : F4 + 4 * k + 4, :] = first[band, height - 4 : height, :]


def whole_steps_kernel(
    initial, offset, grad_rows, grad_cols, result, extrap, dual_rows, dual_cols, change, dual_data
):
    rows_total = result.shape[2]
    clear_guards(extrap, dual_rows)
    chunk = 88
    edges = edge_lanes(chunk)
    fine_steps(
        rows_total, chunk, lambda fields: columns_whole(fields, edges),
        initial, extrap, dual_rows, dual_cols, change, dual_data,
        *[[ref.at[tile] for tile in range(2)] for ref in (offset, grad_rows, grad_cols)],
        lambda k: HALO + BEGIN + k * chunk, lambda own: (1.0, 1.0), result,
    )


def strip_kernel(
    strip_e, strip_f, from_left, from_right, wide, own_meta, whole,
    middle, strip_out, first_ends, offset, grad_rows, grad_cols,
    moved, result, spread, initial, extrap, dual_rows, dual_cols, change, dual_data,
):
    bands, height, _ = strip_e.shape
    block = 24
    coarse_height = height // FACTOR
    coarse_width = COLUMNS // FACTOR
    rows_total = height - 2 * BEGIN
    lane = lanes_of()
    centre = (int_at(own_meta, 0, 0), int_at(own_meta, 0, HALF))
    right, has_right = column_meta(from_right)
    left, has_left = column_meta(from_left)
    exists = jnp.where(lane < S_RIGHT, 1.0, jnp.where(lane < S_LEFT, has_right, has_left))

    def tall_factor(rows):
        return 0.125 * jnp.concatenate([exists] * (rows // SUB), axis=0)

    mask = jnp.where(lane < LEAD, has_left, jnp.where(lane < LEAD + coarse_width, 1.0, has_right))
    mask = jnp.concatenate([mask] * (coarse_height // SUB), axis=0)
    flow = coarse_flow_of(
        [wide[band] for band in range(bands)], [wide[bands + band] for band in range(bands)], mask
    )
    upsample(flow, ("strip",), spread)

    def halves(row, rows):
        half = row // (height // 2)
        start = row - half * (height // 2)
        return half, slice(start, start + rows)

    def second_of(item):
        band, row = item
        half, message = halves(row, 32)
        return strip_second(strip_e[band, row : row + 32, :], from_left, from_right, message, half, band)

    def store_second(item, value):
        band, row = item
        strip_out[band, row : row + 32, :] = value

    staggered([(band, row) for row in range(0, height, 32) for band in range(bands)], second_of, store_second, 4)

    def first_of(band, row, rows):
        parts = []
        for start in range(row, row + rows, SUB):
            half, message = halves(start, SUB)
            parts.append(strip_first(strip_f[band, start : start + SUB, :], from_left, from_right, message, half, band))
        return parts[0] if rows == SUB else jnp.concatenate(parts, axis=0)

    for band in range(bands):
        for end, row in enumerate((0, height - SUB)):
            first_ends[end, band] = first_of(band, row, SUB)

    def windows(band, row, rows):
        return strip_windows(lambda shift: strip_out[band, pl.ds(row + shift, rows), :], centre, right, left)

    def store_moved(item, value):
        band, row = item
        moved[band, row : row + SUB, :] = value

    ends = [(band, row) for row in (SUB // 2, height - SUB - SUB // 2) for band in range(bands)]
    staggered(ends, lambda item: windows(*item, SUB)[0], store_moved, 4)

    factor = tall_factor(block)

    def values_of(item):
        band, row = item
        value, along = windows(band, row, block)
        return value, 0.25 * (value - first_of(band, row, block)), factor * along

    def store_values(item, results):
        band, row = item
        data = slice(row + HALO, row + HALO + block)
        moved[band, row : row + block, :], offset[band, data, :], grad_cols[band, data, :] = results

    staggered(pieces(bands, height, block), values_of, store_values, 4)

    factor_rows = tall_factor(40)

    def gradient_of(item):
        band, row = item
        return factor_rows * (moved[band, pl.ds(row + 1, 40), :] - moved[band, pl.ds(row - 1, 40), :])

    def store_gradient(item, value):
        band, row = item
        grad_rows[band, row + HALO : row + HALO + 40, :] = value

    staggered(pieces(bands, height, 40), gradient_of, store_gradient, 3)

    clear_guards(initial, extrap, dual_rows)
    repeat_rows(spread, initial, [BEGIN // FACTOR + k for k in range(rows_total // SUB)])

    chunk = 176
    masks = jnp.concatenate([exists] * (chunk // SUB), axis=0)
    fine_steps(
        rows_total, chunk, lambda fields: [columns_strip(fields[0])],
        initial, extrap, dual_rows, dual_cols, change, dual_data, [offset], [grad_rows], [grad_cols],
        lambda k: HALO + BEGIN + k * chunk, lambda own: (masks,), result,
    )
    join(lambda c, tile, rows: whole[c, tile, rows, :], lambda c, rows: result[c, 0, rows, :], middle)


def join(whole, strip, target):
    lane = lanes_of()

    def step_of(step, carry):
        rows = aligned(step * SUB)
        for c in range(2):
            edge = strip(c, rows)
            target[c, rows, 0:LANES] = jnp.where(lane < EDGE, edge, whole(c, 0, rows))
            target[c, rows, LANES:COLUMNS] = jnp.where(lane >= LANES - EDGE, turn(edge, S_TURN), whole(c, 1, rows))
        return carry

    lax.fori_loop(0, target.shape[1] // SUB, step_of, 0, unroll=4)


def outer_kernel(
    count, second_0, second_1, first_0, first_1, strip_e, first_ends, from_left, from_right, wide, got_0, got_1, middle, own_meta,
    _wo, _wr, _wc, _so, _sr, _sc,
    flow_out, coarse_out, whole_offset, whole_rows, whole_cols, strip_offset, strip_rows, strip_cols,
    from_up, from_down, extended, tall, spread, masks, result, joined, coarse_result, sems,
    initial, extrap, dual_rows, dual_cols, change, dual_data,
):
    bands, height, _ = second_0.shape
    coarse_height = height // FACTOR
    coarse_width = COLUMNS // FACTOR
    rows_total = 2 * EACH
    lane = lanes_of()

    put_middle = pltpu.make_async_copy(
        middle.at[:, pl.ds(MARGIN - BEGIN, height - 2 * MARGIN), :],
        flow_out.at[:, pl.ds(MARGIN, height - 2 * MARGIN), :],
        sems.at[0],
    )
    put_middle.start()

    other = without_ends(got_1, "row", count)
    even = is_even("row", got_0)
    from_down[...] = jnp.where(even, got_0[...], other)
    from_up[...] = jnp.where(even, other, got_0[...])

    own = (int_at(own_meta, 0, 0), int_at(own_meta, 0, HALF))
    own_right, has_right = column_meta(from_right)
    own_left, has_left = column_meta(from_left)
    has_up = scalar_at(from_up, META, 32)
    has_down = scalar_at(from_down, META, 32)
    exists = jnp.where(lane < S_RIGHT, 1.0, jnp.where(lane < S_LEFT, has_right, has_left))

    def trio(message):
        return (
            (int_at(message, META, 0), int_at(message, META, 16)),
            (int_at(message, META, 80), int_at(message, META, 96)),
            (int_at(message, META, 48), int_at(message, META, 64)),
        )

    above = trio(from_up)
    below = trio(from_down)

    zero = jnp.zeros((SUB, LANES), jnp.float32)
    tall_rows = coarse_height + 2 * LEAD
    for band in range(bands):
        for plane, at, count in ((band, CS, C_SECOND), (bands + band, CF, C_FIRST)):
            start = at + count * band
            tall[plane, 0:LEAD, :] = zero
            tall[plane, LEAD - count : LEAD, :] = from_up[start : start + count, :]
            tall[plane, LEAD : LEAD + coarse_height, :] = wide[plane]
            tall[plane, LEAD + coarse_height : tall_rows, :] = zero
            tall[plane, LEAD + coarse_height : LEAD + coarse_height + count, :] = from_down[start : start + count, :]
    across = jnp.where(lane < LEAD, has_left, jnp.where(lane < LEAD + coarse_width, 1.0, has_right))
    mask = jnp.concatenate([across * has_up] + [across] * (coarse_height // SUB) + [across * has_down], axis=0)
    flow = coarse_flow_of(
        [tall[band] for band in range(bands)], [tall[bands + band] for band in range(bands)], mask
    )
    for c in range(2):
        coarse_result[c] = turn(flow[c][LEAD : LEAD + coarse_height], -LEAD)[:, :coarse_width]
    put_coarse = pltpu.make_async_copy(coarse_result, coarse_out, sems.at[1])
    put_coarse.start()
    upsample(flow, ("whole", "strip"), spread)
    clear_guards(initial, extrap, dual_rows)
    each = EACH // SUB
    repeat_rows(
        spread, initial,
        [LEAD - 1 + k for k in range(each)] + [tall_rows - LEAD + 1 - each + k for k in range(each)],
    )

    for end in range(2):
        message = (from_up, from_down)[end]
        for band in range(bands):
            for tile in range(3):
                k = band * 3 + tile
                eight = message[E8 + 8 * k : E8 + 8 * k + 8, :]
                one = message[E1 + k : E1 + k + 1, :]
                source = (second_0, second_1, strip_e)[tile]
                if end == 0:
                    extended[end, tile, band, 0:8, :] = zero
                    extended[end, tile, band, 7:8, :] = one
                    extended[end, tile, band, 8:16, :] = eight
                    extended[end, tile, band, 16:40, :] = source[band, 0:24, :]
                else:
                    extended[end, tile, band, 0:24, :] = source[band, height - 24 : height, :]
                    extended[end, tile, band, 24:32, :] = eight
                    extended[end, tile, band, 32:40, :] = zero
                    extended[end, tile, band, 32:33, :] = one
    quarter = jnp.zeros((DEPTH, LANES), jnp.float32)
    edges = edge_lanes(SUB)
    rows_data = whole_offset.shape[2]

    def rows_of(halo, end):
        if halo:
            return slice(0, SUB) if end == 0 else slice(rows_data - SUB, rows_data)
        return slice(HALO, HALO + SUB) if end == 0 else slice(rows_data - HALO - SUB, rows_data - HALO)

    def values_of(item):
        halo, end, band = item
        message = (from_up, from_down)[end]
        base = (SUB, 3 * SUB)[end] if halo else 2 * SUB
        shifts = (above, below)[end] if halo else (own, own_right, own_left)
        factor = 0.125 * (has_up, has_down)[end] if halo else 0.125

        def here(tile, shift):
            return extended[end, tile, band, pl.ds(base + shift, SUB), :]

        def down_up(tile, shift):
            return here(tile, shift + 1) - here(tile, shift - 1)

        own_rows = slice(0, SUB) if end == 0 else slice(height - SUB, height)
        if halo:
            firsts = []
            for k in range(band * 3, band * 3 + 3):
                four = message[F4 + 4 * k : F4 + 4 * k + 4, :]
                firsts.append(jnp.concatenate([quarter, four] if end == 0 else [four, quarter], axis=0))
        else:
            firsts = [first_0[band, own_rows, :], first_1[band, own_rows, :], first_ends[end, band]]
        centre = shifts[0]
        values = shift_whole([here(tile, centre[0]) for tile in range(2)], centre[1])
        changes = shift_whole([down_up(tile, centre[0]) for tile in range(2)], centre[1])
        along = columns_whole(values, edges)
        value, across_cols = strip_windows(lambda shift: here(2, shift), *shifts)
        change_rows, _ = strip_windows(lambda shift: down_up(2, shift), *shifts)
        return (
            [0.25 * (x - y) for x, y in zip([*values, value], firsts)],
            [*[factor * x for x in changes], (factor * exists) * change_rows],
            [*[factor * x for x in along], (factor * exists) * across_cols],
        )

    def store_values(item, results):
        halo, end, band = item
        rows = rows_of(halo, end)
        for values, whole, strip in zip(
            results, (whole_offset, whole_rows, whole_cols), (strip_offset, strip_rows, strip_cols)
        ):
            for tile in range(2):
                whole[tile, band, rows, :] = values[tile]
            strip[band, rows, :] = values[2]

    items = [(halo, end, band) for halo in (True, False) for end in range(2) for band in range(bands)]
    staggered(items, values_of, store_values, 4)

    for i, value in enumerate((jnp.ones((SUB, LANES), jnp.float32), exists)):
        masks[i] = jnp.concatenate([value * has_up] + [value] * (rows_total // SUB - 2) + [value * has_down], axis=0)

    def masks_of(rows):
        whole = masks[0, rows, :]
        return (whole, whole, masks[1, rows, :])

    chunk = 64
    edges = edge_lanes(chunk)

    def data_row(k):
        return k * chunk + (rows_data - rows_total if k >= EACH // chunk else 0)

    fine_steps(
        rows_total, chunk, lambda fields: columns_whole(fields[:2], edges) + [columns_strip(fields[2])],
        initial, extrap, dual_rows, dual_cols, change, dual_data,
        [whole_offset.at[0], whole_offset.at[1], strip_offset],
        [whole_rows.at[0], whole_rows.at[1], strip_rows],
        [whole_cols.at[0], whole_cols.at[1], strip_cols],
        data_row, masks_of, result,
    )
    join(lambda c, tile, rows: result[c, tile, rows, :], lambda c, rows: result[c, 2, rows, :], joined)
    put_top = pltpu.make_async_copy(joined.at[:, pl.ds(SUB, MARGIN), :], flow_out.at[:, pl.ds(0, MARGIN), :], sems.at[2])
    put_bottom = pltpu.make_async_copy(
        joined.at[:, pl.ds(EACH + SUB, MARGIN), :], flow_out.at[:, pl.ds(height - MARGIN, MARGIN), :], sems.at[3]
    )
    put_top.start()
    put_bottom.start()
    put_middle.wait()
    put_coarse.wait()
    put_top.wait()
    put_bottom.wait()


def swap_with(message, axis, start):
    names = ("row", "col")
    sizes = [lax.axis_size(name) for name in names]
    along = names.index(axis)
    count, others = sizes[along], sizes[1 - along]

    def number(place, other):
        row, col = (place, other) if along == 0 else (other, place)
        return row * sizes[1] + col

    pairs = [(number(i, k), number(i + 1, k)) for i in range(start, count - 1, 2) for k in range(others)]
    if start:
        pairs += [(number(i, k), number(i, k + 1)) for i in (0, count - 1) for k in range(0, others, 2)]
    return lax.ppermute(message, names, pairs + [(j, i) for i, j in pairs])


def local(frame_first, frame_second, shifts):
    bands, height, width = frame_first.shape
    assert bands == 4 and width == COLUMNS and height % LANES == 0
    assert lax.axis_size("row") % 2 == 0 and lax.axis_size("col") % 2 == 0
    coarse_height = height // FACTOR
    coarse_width = width // FACTOR
    vmem = pl.BlockSpec(memory_space=pltpu.VMEM)
    hbm = pl.BlockSpec(memory_space=pltpu.HBM)
    tall_rows = coarse_height + 2 * LEAD
    inner_rows = height - 2 * BEGIN

    def shape(*sizes):
        return jax.ShapeDtypeStruct(sizes, jnp.float32)

    def scratch(*sizes):
        return pltpu.VMEM(sizes, jnp.float32)

    def call(kernel, name, arguments, outs, scratches=(), flops=1_000_000, **more):
        more = {"in_specs": [vmem] * len(arguments), "out_specs": (vmem,) * len(outs), **more}
        return pl.pallas_call(
            kernel,
            out_shape=tuple(outs),
            scratch_shapes=list(scratches),
            compiler_params=pltpu.CompilerParams(vmem_limit_bytes=24 * 1024 * 1024),
            cost_estimate=pl.CostEstimate(flops=flops, bytes_accessed=1_000_000, transcendentals=0),
            name=name,
            **more,
        )(*arguments)

    plane = shape(bands, height, LANES)
    column_message = shape(height // 2, LANES)
    row_message = shape(ROW_MESSAGE, LANES)
    whole_data = shape(2, bands, height + 2 * HALO, LANES)
    strip_data = shape(bands, height + 2 * HALO, LANES)

    *frames, coarse, swap, own_meta = call(
        first_kernel,
        "means_and_message",
        [pltpu.with_memory_space_constraint(x, pltpu.HBM) for x in (frame_second, frame_first, shifts)],
        [*[plane] * 4, shape(2 * bands * coarse_height, LANES), column_message, shape(SUB, LANES)],
        [
            scratch(2 * bands * coarse_height, width),
            pltpu.SMEM((1, 1, 2), jnp.int32),
            pltpu.SemaphoreType.DMA((2, bands, 2)),
            pltpu.SemaphoreType.DMA,
        ],
        in_specs=[hbm] * 3,
    )
    got_0 = swap_with(swap, "col", 0)

    swap, *whole_terms, initial, strip_e, strip_f, up_part, down_part = call(
        whole_terms_kernel,
        "whole_terms",
        [*frames, coarse, own_meta],
        [
            column_message, *[whole_data] * 3, shape(2, 2, inner_rows + 2 * GUARD, LANES),
            plane, plane, row_message, row_message,
        ],
        [scratch(2, bands, height, LANES), scratch(2, 2, coarse_height, LANES)],
        flops=8_000_000,
    )
    got_1 = swap_with(swap, "col", 1)

    (whole,) = call(
        whole_steps_kernel,
        "whole_steps",
        [initial, *whole_terms],
        [shape(2, 2, inner_rows, LANES)],
        fine_scratch(bands, 2, inner_rows)[1:],
        flops=20_000_000,
    )

    swap_0, swap_1, from_left, from_right, wide = call(
        functools.partial(message_kernel, lax.axis_size("col")),
        "row_messages",
        [coarse, own_meta, got_0, got_1, up_part, down_part, whole],
        [row_message, row_message, column_message, column_message, shape(2 * bands, coarse_height, LANES)],
        [scratch(ROW_MESSAGE, LANES)] * 2,
    )
    got_0 = swap_with(swap_0, "row", 0)
    got_1 = swap_with(swap_1, "row", 1)

    middle, strip_e, first_ends, *strip_terms = call(
        strip_kernel,
        "strip",
        [strip_e, strip_f, from_left, from_right, wide, own_meta, whole],
        [shape(2, inner_rows, width), plane, shape(2, bands, SUB, LANES), *[strip_data] * 3],
        [
            scratch(bands, height, LANES),
            scratch(2, 1, inner_rows, LANES),
            scratch(2, 1, coarse_height, LANES),
            *fine_scratch(bands, 1, inner_rows),
        ],
        flops=16_000_000,
    )

    flow, coarse_flow, *_ = call(
        functools.partial(outer_kernel, lax.axis_size("row")),
        "outer_rows",
        [
            *frames, strip_e, first_ends, from_left, from_right, wide, got_0, got_1, middle, own_meta,
            *whole_terms, *strip_terms,
        ],
        [shape(2, height, width), shape(2, coarse_height, coarse_width), *[whole_data] * 3, *[strip_data] * 3],
        [
            scratch(ROW_MESSAGE, LANES),
            scratch(ROW_MESSAGE, LANES),
            scratch(2, 3, bands, 40, LANES),
            scratch(2 * bands, tall_rows, LANES),
            scratch(2, 3, tall_rows, LANES),
            scratch(2, 2 * EACH, LANES),
            scratch(2, 3, 2 * EACH, LANES),
            scratch(2, 2 * EACH, width),
            scratch(2, coarse_height, coarse_width),
            pltpu.SemaphoreType.DMA((4,)),
            *fine_scratch(bands, 3, 2 * EACH),
        ],
        out_specs=(hbm, hbm) + (vmem,) * 6,
        input_output_aliases={13 + k: 2 + k for k in range(6)},
    )
    return (flow, coarse_flow)


def solution(mesh):
    return jax.shard_map(
        local,
        mesh=mesh,
        in_specs=(P(None, "row", "col"), P(None, "row", "col"), P("row", "col", None)),
        out_specs=(P(None, "row", "col"), P(None, "row", "col")),
        check_vma=False,
    )
```

```python
import functools

import jax
import jax.numpy as jnp
from jax import lax
from jax.experimental import pallas as pl
from jax.experimental.pallas import tpu as pltpu
from jax.sharding import PartitionSpec as P

FACTOR = 8
MAXD = 4
BANDS = 4
STEPS = 3
LANES = 128
COLUMNS = 2 * LANES
HALF = 64
SUB = 8
DEPTH = 4
REACH = DEPTH + MAXD + 1
SLOT = 16
C_SECOND = 6
C_FIRST = 5
LEAD = 8
MARGIN = 48
EDGE = 46
GUARD = 8
HALO = 8
BEGIN = 40
EACH = MARGIN + 16
LIMIT = 0.3
ALPHA = 0.3

S_MID = 55
S_RIGHT = 110
S_LEFT = LANES - REACH
S_TURN = COLUMNS - S_RIGHT - LANES

E8 = 0
E1 = 96
F4 = 112
CS = 160
CF = CS + 4 * C_SECOND
META = 208
ROW_MESSAGE = 216

COARSE_A = REACH + DEPTH
COARSE_B = SLOT + REACH + DEPTH
SHIFT_R = 2 * SLOT + REACH + DEPTH
SHIFT_C = SHIFT_R + 1
EXISTS = SHIFT_R + 2


def lanes_of(rows=SUB):
    return lax.broadcasted_iota(jnp.int32, (rows, LANES), 1)


def lanes_like(x):
    return lax.broadcasted_iota(jnp.int32, x.shape, 1)


def turn(x, amount):
    amount = amount % LANES
    return x if amount == 0 else pltpu.roll(x, amount, 1)


def turn_back(x, shift):
    return pltpu.roll(x, lax.rem(LANES - shift, LANES), 1)


def split_dot(x, exact):
    high = x.astype(jnp.bfloat16)
    rest = x - high.astype(jnp.float32)
    middle = rest.astype(jnp.bfloat16)
    low = (rest - middle.astype(jnp.float32)).astype(jnp.bfloat16)
    parts = [jnp.dot(part, exact, preferred_element_type=jnp.float32) for part in (low, middle, high)]
    return parts[0] + parts[1] + parts[2]


def scalar_at(ref, row, lane):
    return ref[row : row + 1, lane : lane + 1][0, 0]


def int_at(ref, row, lane):
    return scalar_at(ref, row, lane).astype(jnp.int32)


def is_even(axis, like):
    return jnp.broadcast_to(lax.axis_index(axis) % 2, like.shape) == 0


def without_ends(message, axis, count):
    place = jnp.broadcast_to(lax.axis_index(axis), message.shape)
    return jnp.where((place > 0) & (place < count - 1), message[...], 0.0)


def staggered(items, compute, store, depth):
    pending = []
    for item in items:
        pending.append((item, compute(item)))
        if len(pending) > depth:
            store(*pending.pop(0))
    for entry in pending:
        store(*entry)


def aligned(row):
    return pl.ds(pl.multiple_of(row, SUB), SUB)


def pack_message(target, to_right, seconds, firsts, coarse, shift_rows, shift_cols):
    bands, height, _ = seconds[0].shape
    second, first = seconds[int(to_right)], firsts[int(to_right)]
    second_from = LANES - REACH if to_right else 0
    first_from = LANES - DEPTH if to_right else 0
    coarse_from = LEAD + COLUMNS // FACTOR - C_SECOND if to_right else LEAD
    length = height // 2
    lane = lanes_of(length)
    packed = jnp.zeros((length, LANES), jnp.float32)
    for half in range(2):
        rows = slice(half * length, (half + 1) * length)
        cells = coarse[rows, :]
        base = half * HALF
        for band in range(bands):
            at = base + band * SLOT
            packed = jnp.where(lane >= at, turn(second[band, rows, :], at - second_from), packed)
            packed = jnp.where(lane >= at + REACH, turn(first[band, rows, :], at + REACH - first_from), packed)
            if band == 0:
                packed = jnp.where(lane >= base + COARSE_A, turn(cells, base + COARSE_A - coarse_from), packed)
            if band == 1:
                packed = jnp.where(lane >= base + COARSE_B, turn(cells, base + COARSE_B - coarse_from - 3), packed)
            if band == 2:
                packed = jnp.where(lane >= base + SHIFT_R, shift_rows, packed)
                packed = jnp.where(lane >= base + SHIFT_C, shift_cols, packed)
                packed = jnp.where(lane >= base + EXISTS, 1.0, packed)
    target[...] = packed


def column_meta(message):
    return (int_at(message, 0, SHIFT_R), int_at(message, 0, SHIFT_C)), scalar_at(message, 0, EXISTS)


def strip_second(base, from_left, from_right, rows, half, band):
    at = half * HALF + band * SLOT
    lane = lanes_like(base)
    cells = jnp.where(lane >= S_RIGHT, turn(from_right[rows, :], S_RIGHT - at), base)
    return jnp.where(lane >= S_LEFT, turn(from_left[rows, :], S_LEFT - at), cells)


def strip_first(base, from_left, from_right, rows, half, band):
    at = half * HALF + band * SLOT + REACH
    lane = lanes_like(base)
    cells = jnp.where(lane >= S_RIGHT, turn(from_right[rows, :], S_RIGHT - at), base)
    return jnp.where(lane >= S_LEFT, turn(from_left[rows, :], LANES - DEPTH - at), cells)


def strip_own(planes):
    return jnp.where(lanes_like(planes[0]) < S_MID, planes[0], turn(planes[1], -S_TURN))


def first_kernel(
    second_hbm, first_hbm, shifts_hbm, second_0, second_1, first_0, first_1, coarse, swap, own_meta,
    shifts, sems, shift_sem,
):
    seconds, firsts = (second_0, second_1), (first_0, first_1)
    bands, height, _ = second_0.shape
    width = COLUMNS
    coarse_height = height // FACTOR
    lane = lanes_of()
    get_shifts = pltpu.make_async_copy(shifts_hbm, shifts, shift_sem)
    get_shifts.start()
    copies = []
    for image, (source, refs) in enumerate(((second_hbm, seconds), (first_hbm, firsts))):
        for band in range(bands):
            for tile, ref in enumerate(refs):
                copy = pltpu.make_async_copy(
                    source.at[band, :, pl.ds(tile * LANES, LANES)], ref.at[band], sems.at[image, band, tile]
                )
                copy.start()
                copies.append((image * bands + band, tile, ref, band, copy))
    cell = lax.broadcasted_iota(jnp.int32, (width, LANES), 0)
    place = lax.broadcasted_iota(jnp.int32, (width, LANES), 1)
    weights = jnp.where(place - LEAD == cell // FACTOR, 1.0 / (FACTOR * FACTOR), 0.0).astype(jnp.bfloat16)
    sums = {}
    for group in (copies[: len(copies) // 2], copies[len(copies) // 2 :]):
        for *_, copy in group:
            copy.wait()
        for plane, tile, ref, band, _ in group:
            parts = [ref[band, pl.ds(k, coarse_height, stride=FACTOR), :] for k in range(FACTOR)]
            while len(parts) > 1:
                parts = [x + y for x, y in zip(parts[::2], parts[1::2])]
            sums[plane, tile] = parts[0]
    sums = [jnp.concatenate([sums[plane, tile] for tile in range(2)], axis=1) for plane in range(2 * bands)]
    coarse[...] = split_dot(jnp.concatenate(sums, axis=0), weights)
    get_shifts.wait()
    shift_rows = shifts[0, 0, 0].astype(jnp.float32)
    shift_cols = shifts[0, 0, 1].astype(jnp.float32)
    own_meta[...] = jnp.where(lane < HALF, shift_rows, shift_cols)
    odd = lax.axis_index("col") % 2

    @pl.when(odd == 0)
    def _():
        pack_message(swap, True, seconds, firsts, coarse, shift_rows, shift_cols)

    @pl.when(odd == 1)
    def _():
        pack_message(swap, False, seconds, firsts, coarse, shift_rows, shift_cols)


def message_kernel(
    count, coarse, own_meta, got_0, got_1, up_part, down_part, _whole, swap_0, swap_1, from_left, from_right, wide, up, down
):
    other = without_ends(got_1, "col", count)
    even = is_even("col", got_0)
    from_right[...] = jnp.where(even, got_0[...], other)
    from_left[...] = jnp.where(even, other, got_0[...])
    planes_coarse, coarse_height, _ = wide.shape
    bands = planes_coarse // 2
    end = from_left.shape[0]
    coarse_width = COLUMNS // FACTOR
    lane = lanes_of()
    wides = []
    for plane in range(planes_coarse):
        half, block = divmod(plane, planes_coarse // 2)
        for step in range(coarse_height // SUB):
            own = slice(plane * coarse_height + step * SUB, plane * coarse_height + (step + 1) * SUB)
            rows = slice(block * coarse_height + step * SUB, block * coarse_height + (step + 1) * SUB)
            at = half * HALF
            left = from_left[rows, :]
            right = from_right[rows, :]
            start = LEAD - C_SECOND
            cells = turn(left, start - at - COARSE_A)
            cells = jnp.where(lane >= start + 3, turn(left, start + 3 - at - COARSE_B), cells)
            cells = jnp.where(lane >= LEAD, coarse[own, :], cells)
            start = LEAD + coarse_width
            cells = jnp.where(lane >= start, turn(right, start - at - COARSE_A), cells)
            cells = jnp.where(lane >= start + 3, turn(right, start + 3 - at - COARSE_B), cells)
            wides.append((plane, step, cells))
    for plane, step, cells in wides:
        wide[plane, step * SUB : (step + 1) * SUB, :] = cells
    up[...] = up_part[...]
    down[...] = down_part[...]
    stores = []
    for band in range(bands):
        k = band * 3 + 2
        for target, half, near, next_rows, row_of in (
            (up, 0, slice(0, 8), slice(8, 16), 0),
            (down, 1, slice(end - 8, end), slice(end - 16, end - 8), 7),
        ):
            at = slice(E8 + 8 * k, E8 + 8 * k + 8)
            stores.append((target, at, strip_second(target[at, :], from_left, from_right, near, half, band)))
            at = slice(E1 + k, E1 + k + 1)
            one = jnp.broadcast_to(target[at, :], (SUB, LANES))
            one = strip_second(one, from_left, from_right, next_rows, half, band)
            stores.append((target, at, one[row_of : row_of + 1]))
            at = slice(F4 + 4 * k, F4 + 4 * k + 4)
            four = target[at, :]
            four = strip_first(jnp.concatenate([four, four], axis=0), from_left, from_right, near, half, band)
            stores.append((target, at, four[4 * half : 4 * half + 4]))
        for at, plane, count in ((CS, band, C_SECOND), (CF, bands + band, C_FIRST)):
            at = slice(at + count * band, at + count * band + count)
            stores.append((up, at, wide[plane, 0:count, :]))
            stores.append((down, at, wide[plane, coarse_height - count : coarse_height, :]))
    for target, at, value in stores:
        target[at, :] = value
    packed = jnp.where(lane < 16, own_meta[...], jnp.where(lane < 32, turn(own_meta[...], HALF), 1.0))
    for message, at in ((from_left, 48), (from_right, 80)):
        meta = message[0:SUB, :]
        rows = jnp.broadcast_to(meta[:, SHIFT_R : SHIFT_R + 1], (SUB, LANES))
        cols = jnp.broadcast_to(meta[:, SHIFT_C : SHIFT_C + 1], (SUB, LANES))
        packed = jnp.where(lane >= at, rows, packed)
        packed = jnp.where(lane >= at + 16, cols, packed)
    up[META : META + SUB, :] = packed
    down[META : META + SUB, :] = packed
    even = is_even("row", up)
    swap_0[...] = jnp.where(even, down[...], up[...])
    swap_1[...] = jnp.where(even, up[...], down[...])


def coarse_flow_of(second, first, mask):
    def along_rows(x):
        return pltpu.roll(x, x.shape[0] - 1, 0) - pltpu.roll(x, 1, 0)

    def along_cols(x):
        return pltpu.roll(x, LANES - 1, 1) - pltpu.roll(x, 1, 1)

    bands = BANDS
    size = second.shape[0] // bands
    grad_rows = 0.125 * along_rows(second)
    grad_cols = 0.125 * along_cols(second)
    offset = 0.25 * (second - first)
    data = jnp.clip(offset, -LIMIT, LIMIT)

    def pull(grads):
        terms = data * grads
        return sum(terms[k * size : (k + 1) * size] for k in range(bands))

    def tall(x):
        return jnp.concatenate([x] * bands, axis=0)

    flow = [-mask * pull(grad_rows), -mask * pull(grad_cols)]
    extrapolated = [2.0 * x for x in flow]
    dual_rows = [0.0, 0.0]
    dual_cols = [0.0, 0.0]
    for step in range(1, STEPS):
        changes = [(along_rows(x), along_cols(x)) for x in extrapolated]
        data = data + offset + grad_rows * tall(extrapolated[0]) + grad_cols * tall(extrapolated[1])
        data = jnp.clip(data, -LIMIT, LIMIT)
        for c in range(2):
            rows = dual_rows[c] + changes[c][0]
            cols = dual_cols[c] + changes[c][1]
            norm = jnp.maximum(rows * rows + cols * cols, 1e-30)
            scale = jnp.minimum(mask, (8.0 * ALPHA) * lax.rsqrt(norm))
            dual_rows[c] = rows * scale
            dual_cols[c] = cols * scale
        pulls = [pull(grad_rows), pull(grad_cols)]
        for c in range(2):
            divergence = along_rows(dual_rows[c]) + along_cols(dual_cols[c])
            following = flow[c] + mask * ((1.0 / 64.0) * divergence - pulls[c])
            extrapolated[c] = 2.0 * following - flow[c]
            flow[c] = following
    return flow


def columns_of_planes(planes):
    whole = lax.broadcasted_iota(jnp.int32, (LANES, COLUMNS), 1)
    lane = lax.broadcasted_iota(jnp.int32, (LANES, LANES), 1)
    strip = jnp.where(lane < S_MID, lane, jnp.where(lane < S_LEFT, lane + (COLUMNS - S_RIGHT), lane - LANES))
    return jnp.concatenate([x for x, wanted in ((whole, "whole"), (strip, "strip")) if wanted in planes], axis=1)


def upsample(flow, planes, target):
    column = columns_of_planes(planes)
    source = lax.broadcasted_iota(jnp.int32, column.shape, 0)
    spread = jnp.where(source - LEAD == lax.shift_right_arithmetic(column, 3), float(FACTOR), 0.0).astype(jnp.bfloat16)
    rows = flow[0].shape[0]
    wide = split_dot(jnp.concatenate(flow, axis=0), spread)
    for c in range(2):
        for tile in range(column.shape[1] // LANES):
            target[c, tile] = wide[c * rows : (c + 1) * rows, tile * LANES : (tile + 1) * LANES]


def repeat_rows(spread, initial, cells):
    for c in range(2):
        for tile in range(initial.shape[1]):
            rows = [jnp.broadcast_to(spread[c, tile, cell : cell + 1, :], (SUB, LANES)) for cell in cells]
            initial[c, tile, GUARD : GUARD + SUB * len(cells), :] = jnp.concatenate(rows, axis=0)


def shift_whole(here, shift):
    turned = [turn_back(x, shift) for x in here]
    lane = lanes_like(here[0])
    return [
        jnp.where(lane + shift >= LANES, turned[1], turned[0]),
        jnp.where(lane + shift < 0, turned[0], turned[1]),
    ]


def edge_lanes(rows):
    lane = lanes_of(rows)
    return lane == LANES - 1, lane == 0


def columns_whole(fields, edges):
    last, first = edges
    ahead = [pltpu.roll(x, LANES - 1, 1) for x in fields]
    behind = [pltpu.roll(x, 1, 1) for x in fields]
    return [
        jnp.where(last, ahead[1], ahead[0]) - behind[0],
        ahead[1] - jnp.where(first, behind[0], behind[1]),
    ]


def columns_strip(field):
    return pltpu.roll(field, LANES - 1, 1) - pltpu.roll(field, 1, 1)


def strip_windows(window, centre, right, left):
    own = turn_back(window(centre[0]), centre[1])
    beyond_left = turn_back(window(left[0]), left[1])
    beyond_right = turn_back(window(right[0]), right[1])
    lane = lanes_like(own)
    beyond = jnp.where((lane >= S_LEFT) | (lane < S_MID), beyond_left, beyond_right)
    is_beyond = lane >= S_RIGHT
    return jnp.where(is_beyond, beyond, own), jnp.where(is_beyond, columns_strip(beyond), columns_strip(own))


def fine_steps(
    rows_total, chunk, columns, initial, extrap, dual_rows, dual_cols, change, dual_data,
    offsets, grads_rows, grads_cols, data_row, masks_of, result,
):
    planes = len(offsets)
    bands = offsets[0].shape[0]
    chunks = rows_total // chunk
    both = [(c, tile) for c in range(2) for tile in range(planes)]

    for step in range(STEPS):
        source = initial if step == 0 else extrap
        final = step == STEPS - 1

        def dual(k, source=source, step=step):
            row = GUARD + k * chunk
            own = pl.ds(k * chunk, chunk)
            at = pl.ds(row, chunk)
            masks = masks_of(own)
            along = [columns([source[c, tile, at, :] for tile in range(planes)]) for c in range(2)]
            values = []
            for c, tile in both:
                rows = source[c, tile, pl.ds(row + 1, chunk), :] - source[c, tile, pl.ds(row - 1, chunk), :]
                cols = along[c][tile]
                if step > 0:
                    rows = rows + dual_rows[c, tile, at, :]
                    cols = cols + dual_cols[c, tile, own, :]
                norm = jnp.maximum(rows * rows + cols * cols, 1e-30)
                scale = jnp.minimum(masks[tile], (8.0 * ALPHA) * lax.rsqrt(norm))
                values.append((rows * scale, cols * scale))
            for (c, tile), (rows, cols) in zip(both, values):
                dual_rows[c, tile, at, :] = rows
                dual_cols[c, tile, own, :] = cols

        def primal(k, step=step, final=final):
            data = pl.ds(data_row(k), chunk)
            row = GUARD + k * chunk
            own = pl.ds(k * chunk, chunk)
            at = pl.ds(row, chunk)
            masks = masks_of(own)
            along = [columns([dual_cols[c, tile, own, :] for tile in range(planes)]) for c in range(2)]
            for tile in range(planes):
                start = [initial[c, tile, at, :] for c in range(2)]
                if step > 0:
                    moved = [extrap[c, tile, at, :] - start[c] for c in range(2)]
                pulls = [None, None]
                duals = []
                for band in range(bands):
                    gradient = (grads_rows[tile][band, data, :], grads_cols[tile][band, data, :])
                    value = offsets[tile][band, data, :]
                    if step > 0:
                        value = value + gradient[0] * moved[0] + gradient[1] * moved[1]
                        value = value + dual_data[band, tile, own, :]
                    value = jnp.clip(value, -LIMIT, LIMIT)
                    duals.append(value)
                    for c in range(2):
                        term = value * gradient[c]
                        pulls[c] = term if pulls[c] is None else pulls[c] + term
                movings = []
                for c in range(2):
                    divergence = (
                        dual_rows[c, tile, pl.ds(row + 1, chunk), :]
                        - dual_rows[c, tile, pl.ds(row - 1, chunk), :]
                        + along[c][tile]
                    )
                    movings.append((masks[tile] * (1.0 / 64.0)) * divergence - pulls[c])
                if step > 0:
                    olds = [change[c, tile, own, :] for c in range(2)]
                for c in range(2):
                    if step == 0:
                        change[c, tile, own, :] = movings[c]
                        extrap[c, tile, at, :] = start[c] + 2.0 * movings[c]
                    else:
                        new = olds[c] + movings[c]
                        if final:
                            result[c, tile, own, :] = start[c] + new
                        else:
                            change[c, tile, own, :] = new
                            extrap[c, tile, at, :] = start[c] + (new + movings[c])
                if not final:
                    for band in range(bands):
                        dual_data[band, tile, own, :] = duals[band]

        dual(0)
        for k in range(1, chunks):
            dual(k)
            primal(k - 1)
        primal(chunks - 1)


def clear_guards(*refs):
    for ref in refs:
        rows = ref.shape[2]
        zero = jnp.zeros((GUARD, LANES), jnp.float32)
        for c in range(2):
            for tile in range(ref.shape[1]):
                ref[c, tile, 0:GUARD, :] = zero
                ref[c, tile, rows - GUARD : rows, :] = zero


def fine_scratch(bands, planes, rows):
    guarded = pltpu.VMEM((2, planes, rows + 2 * GUARD, LANES), jnp.float32)
    plain = pltpu.VMEM((2, planes, rows, LANES), jnp.float32)
    return [guarded, guarded, guarded, plain, plain, pltpu.VMEM((bands, planes, rows, LANES), jnp.float32)]


def pieces(bands, height, rows):
    assert (height - 2 * SUB) % rows == 0
    return [(band, row) for row in range(SUB, height - SUB, rows) for band in range(bands)]


def whole_terms_kernel(
    second_0, second_1, first_0, first_1, coarse, own_meta,
    swap, offset, grad_rows, grad_cols, initial, strip_e, strip_f, up, down, moved, spread,
):
    seconds, firsts = (second_0, second_1), (first_0, first_1)
    bands, height, _ = second_0.shape
    block = 80
    coarse_height = coarse.shape[0] // (2 * bands)
    shift_rows, shift_cols = scalar_at(own_meta, 0, 0), scalar_at(own_meta, 0, HALF)
    centre = (shift_rows.astype(jnp.int32), shift_cols.astype(jnp.int32))
    odd = lax.axis_index("col") % 2

    @pl.when(odd == 1)
    def _():
        pack_message(swap, True, seconds, firsts, coarse, shift_rows, shift_cols)

    @pl.when(odd == 0)
    def _():
        pack_message(swap, False, seconds, firsts, coarse, shift_rows, shift_cols)

    def windows(band, row, rows):
        here = [ref[band, pl.ds(row + centre[0], rows), :].reshape(-1, LANES) for ref in seconds]
        return shift_whole(here, centre[1])

    flow = coarse_flow_of(coarse[0 : bands * coarse_height, :], coarse[bands * coarse_height :, :], 1.0)
    upsample(flow, ("whole",), spread)

    ends = [(row, windows(slice(None), row, SUB)) for row in (SUB // 2, height - SUB - SUB // 2)]
    for row, values in ends:
        for tile in range(2):
            moved[tile, :, row : row + SUB, :] = values[tile].reshape(bands, SUB, LANES)

    edges = edge_lanes(block)

    def values_of(item):
        band, row = item
        values = windows(band, row, block)
        along = columns_whole(values, edges)
        own = [ref[band, row : row + block, :] for ref in firsts]
        return values, [0.25 * (x - y) for x, y in zip(values, own)], [0.125 * x for x in along]

    def store_values(item, results):
        band, row = item
        values, offsets, gradients = results
        data = slice(row + HALO, row + HALO + block)
        for tile in range(2):
            moved[tile, band, row : row + block, :] = values[tile]
            offset[tile, band, data, :] = offsets[tile]
            grad_cols[tile, band, data, :] = gradients[tile]

    staggered(pieces(bands, height, block), values_of, store_values, 1)

    def strips_of(item):
        band, row = item
        rows = slice(row, row + LANES)
        return strip_own([ref[band, rows, :] for ref in seconds]), strip_own([ref[band, rows, :] for ref in firsts])

    def store_strips(item, results):
        band, row = item
        strip_e[band, row : row + LANES, :], strip_f[band, row : row + LANES, :] = results

    staggered([(band, row) for band in range(bands) for row in range(0, height, LANES)], strips_of, store_strips, 1)

    def gradient_of(item):
        band, row = item
        return [
            0.125 * (moved[tile, band, pl.ds(row + 1, 120), :] - moved[tile, band, pl.ds(row - 1, 120), :])
            for tile in range(2)
        ]

    def store_gradient(item, results):
        band, row = item
        for tile in range(2):
            grad_rows[tile, band, row + HALO : row + HALO + 120, :] = results[tile]

    staggered(pieces(bands, height, 120), gradient_of, store_gradient, 1)

    clear_guards(initial)
    rows_total = initial.shape[2] - 2 * GUARD
    repeat_rows(spread, initial, [BEGIN // FACTOR + k for k in range(rows_total // SUB)])

    parts = []
    for band in range(bands):
        for tile in range(3):
            second = (second_0, second_1, strip_e)[tile]
            first = (first_0, first_1, strip_f)[tile]
            parts.append((
                second[band, 0:16, :], first[band, 0:8, :],
                second[band, height - 16 : height, :], first[band, height - 8 : height, :],
            ))
    for k, (second_top, first_top, second_end, first_end) in enumerate(parts):
        up[E8 + 8 * k : E8 + 8 * k + 8, :] = second_top[0:8]
        up[E1 + k : E1 + k + 1, :] = second_top[8:9]
        up[F4 + 4 * k : F4 + 4 * k + 4, :] = first_top[0:4]
        down[E8 + 8 * k : E8 + 8 * k + 8, :] = second_end[8:16]
        down[E1 + k : E1 + k + 1, :] = second_end[7:8]
        down[F4 + 4 * k : F4 + 4 * k + 4, :] = first_end[4:8]
    for target in (up, down):
        for start, end in ((E1 + 3 * bands, F4), (CS, ROW_MESSAGE)):
            target[start:end, :] = jnp.zeros((end - start, LANES), jnp.float32)


def whole_steps_kernel(
    initial, offset, grad_rows, grad_cols, result, extrap, dual_rows, dual_cols, change, dual_data
):
    rows_total = result.shape[2]
    clear_guards(extrap, dual_rows)
    chunk = 88
    edges = edge_lanes(chunk)
    fine_steps(
        rows_total, chunk, lambda fields: columns_whole(fields, edges),
        initial, extrap, dual_rows, dual_cols, change, dual_data,
        *[[ref.at[tile] for tile in range(2)] for ref in (offset, grad_rows, grad_cols)],
        lambda k: HALO + BEGIN + k * chunk, lambda own: (1.0, 1.0), result,
    )


def strip_kernel(
    strip_e, strip_f, from_left, from_right, wide, own_meta, whole,
    middle, strip_out, first_ends, offset, grad_rows, grad_cols,
    moved, result, spread, initial, extrap, dual_rows, dual_cols, change, dual_data,
):
    bands, height, _ = strip_e.shape
    block = 120
    coarse_height = height // FACTOR
    coarse_width = COLUMNS // FACTOR
    rows_total = height - 2 * BEGIN
    lane = lanes_of()
    centre = (int_at(own_meta, 0, 0), int_at(own_meta, 0, HALF))
    right, has_right = column_meta(from_right)
    left, has_left = column_meta(from_left)
    exists = jnp.where(lane < S_RIGHT, 1.0, jnp.where(lane < S_LEFT, has_right, has_left))

    def tall_factor(rows):
        return 0.125 * jnp.concatenate([exists] * (rows // SUB), axis=0)

    mask = jnp.where(lane < LEAD, has_left, jnp.where(lane < LEAD + coarse_width, 1.0, has_right))
    mask = jnp.concatenate([mask] * (coarse_height // SUB), axis=0)
    cells = [wide[k * bands : (k + 1) * bands].reshape(bands * coarse_height, LANES) for k in range(2)]
    flow = coarse_flow_of(*cells, mask)
    upsample(flow, ("strip",), spread)

    def halves(row, rows):
        half = row // (height // 2)
        start = row - half * (height // 2)
        return half, slice(start, start + rows)

    def second_of(item):
        band, row = item
        half, message = halves(row, LANES)
        return strip_second(strip_e[band, row : row + LANES, :], from_left, from_right, message, half, band)

    def store_second(item, value):
        band, row = item
        strip_out[band, row : row + LANES, :] = value

    staggered([(band, row) for row in range(0, height, LANES) for band in range(bands)], second_of, store_second, 1)

    def first_of(band, row, rows):
        half, message = halves(row, rows)
        return strip_first(strip_f[band, row : row + rows, :], from_left, from_right, message, half, band)

    firsts = [(end, band, first_of(band, (0, height - SUB)[end], SUB)) for end in range(2) for band in range(bands)]
    for end, band, value in firsts:
        first_ends[end, band] = value

    def windows(band, row, rows):
        return strip_windows(
            lambda shift: strip_out[band, pl.ds(row + shift, rows), :].reshape(-1, LANES), centre, right, left
        )

    ends = [(row, windows(slice(None), row, SUB)[0]) for row in (SUB // 2, height - SUB - SUB // 2)]
    for row, value in ends:
        moved[:, row : row + SUB, :] = value.reshape(bands, SUB, LANES)

    factor = tall_factor(block)

    def values_of(item):
        band, row = item
        value, along = windows(band, row, block)
        return value, 0.25 * (value - first_of(band, row, block)), factor * along

    def store_values(item, results):
        band, row = item
        data = slice(row + HALO, row + HALO + block)
        moved[band, row : row + block, :], offset[band, data, :], grad_cols[band, data, :] = results

    staggered(pieces(bands, height, block), values_of, store_values, 1)

    def gradient_of(item):
        band, row = item
        return factor * (moved[band, pl.ds(row + 1, block), :] - moved[band, pl.ds(row - 1, block), :])

    def store_gradient(item, value):
        band, row = item
        grad_rows[band, row + HALO : row + HALO + block, :] = value

    staggered(pieces(bands, height, block), gradient_of, store_gradient, 1)

    clear_guards(initial, extrap, dual_rows)
    repeat_rows(spread, initial, [BEGIN // FACTOR + k for k in range(rows_total // SUB)])

    chunk = 176
    masks = jnp.concatenate([exists] * (chunk // SUB), axis=0)
    fine_steps(
        rows_total, chunk, lambda fields: [columns_strip(fields[0])],
        initial, extrap, dual_rows, dual_cols, change, dual_data, [offset], [grad_rows], [grad_cols],
        lambda k: HALO + BEGIN + k * chunk, lambda own: (masks,), result,
    )
    join(lambda c, tile: whole[c, tile], lambda c: result[c, 0], middle)


def join(whole, strip, target):
    rows = target.shape[1]
    lane = lanes_of(rows)
    for c in range(2):
        edge = strip(c)
        start = jnp.where(lane < EDGE, edge, whole(c, 0))
        end = jnp.where(lane >= LANES - EDGE, turn(edge, S_TURN), whole(c, 1))
        target[c, :, 0:LANES] = start
        target[c, :, LANES:COLUMNS] = end


def outer_kernel(
    count, second_0, second_1, first_0, first_1, strip_e, first_ends, from_left, from_right, wide, got_0, got_1, middle, own_meta,
    _wo, _wr, _wc, _so, _sr, _sc,
    flow_out, coarse_out, whole_offset, whole_rows, whole_cols, strip_offset, strip_rows, strip_cols,
    from_up, from_down, extended, tall, spread, masks, result, joined, coarse_result, sems,
    initial, extrap, dual_rows, dual_cols, change, dual_data,
):
    bands, height, _ = second_0.shape
    coarse_height = height // FACTOR
    coarse_width = COLUMNS // FACTOR
    rows_total = 2 * EACH
    lane = lanes_of()

    put_middle = pltpu.make_async_copy(
        middle.at[:, pl.ds(MARGIN - BEGIN, height - 2 * MARGIN), :],
        flow_out.at[:, pl.ds(MARGIN, height - 2 * MARGIN), :],
        sems.at[0],
    )
    put_middle.start()

    other = without_ends(got_1, "row", count)
    even = is_even("row", got_0)
    from_down[...] = jnp.where(even, got_0[...], other)
    from_up[...] = jnp.where(even, other, got_0[...])

    own = (int_at(own_meta, 0, 0), int_at(own_meta, 0, HALF))
    own_right, has_right = column_meta(from_right)
    own_left, has_left = column_meta(from_left)
    has_up = scalar_at(from_up, META, 32)
    has_down = scalar_at(from_down, META, 32)
    exists = jnp.where(lane < S_RIGHT, 1.0, jnp.where(lane < S_LEFT, has_right, has_left))

    def trio(message):
        return (
            (int_at(message, META, 0), int_at(message, META, 16)),
            (int_at(message, META, 80), int_at(message, META, 96)),
            (int_at(message, META, 48), int_at(message, META, 64)),
        )

    above = trio(from_up)
    below = trio(from_down)

    zero = jnp.zeros((SUB, LANES), jnp.float32)
    tall_rows = coarse_height + 2 * LEAD
    for band in range(bands):
        for plane, at, count in ((band, CS, C_SECOND), (bands + band, CF, C_FIRST)):
            start = at + count * band
            tall[plane, 0:LEAD, :] = zero
            tall[plane, LEAD - count : LEAD, :] = from_up[start : start + count, :]
            tall[plane, LEAD : LEAD + coarse_height, :] = wide[plane]
            tall[plane, LEAD + coarse_height : tall_rows, :] = zero
            tall[plane, LEAD + coarse_height : LEAD + coarse_height + count, :] = from_down[start : start + count, :]
    across = jnp.where(lane < LEAD, has_left, jnp.where(lane < LEAD + coarse_width, 1.0, has_right))
    mask = jnp.concatenate([across * has_up] + [across] * (coarse_height // SUB) + [across * has_down], axis=0)
    cells = [tall[k * bands : (k + 1) * bands].reshape(bands * tall_rows, LANES) for k in range(2)]
    flow = coarse_flow_of(*cells, mask)
    for c in range(2):
        coarse_result[c] = turn(flow[c][LEAD : LEAD + coarse_height], -LEAD)[:, :coarse_width]
    put_coarse = pltpu.make_async_copy(coarse_result, coarse_out, sems.at[1])
    put_coarse.start()
    upsample(flow, ("whole", "strip"), spread)
    clear_guards(initial, extrap, dual_rows)
    each = EACH // SUB
    repeat_rows(
        spread, initial,
        [LEAD - 1 + k for k in range(each)] + [tall_rows - LEAD + 1 - each + k for k in range(each)],
    )

    for end in range(2):
        message = (from_up, from_down)[end]
        parts = []
        for band in range(bands):
            for tile in range(3):
                k = band * 3 + tile
                eight = message[E8 + 8 * k : E8 + 8 * k + 8, :]
                one = jnp.broadcast_to(message[E1 + k : E1 + k + 1, :], (SUB, LANES))
                source = (second_0, second_1, strip_e)[tile]
                if end == 0:
                    parts.append((tile, band, [one, eight, source[band, 0:24, :]]))
                else:
                    parts.append((tile, band, [source[band, height - 24 : height, :], eight, one]))
        for tile, band, values in parts:
            extended[end, tile, band] = jnp.concatenate(values, axis=0)
    edges = edge_lanes(bands * SUB)
    rows_data = whole_offset.shape[2]
    exists_tall = jnp.concatenate([exists] * bands, axis=0)

    def rows_of(halo, end):
        if halo:
            return slice(0, SUB) if end == 0 else slice(rows_data - SUB, rows_data)
        return slice(HALO, HALO + SUB) if end == 0 else slice(rows_data - HALO - SUB, rows_data - HALO)

    def values_of(item):
        halo, end = item
        message = (from_up, from_down)[end]
        base = (SUB, 3 * SUB)[end] if halo else 2 * SUB
        shifts = (above, below)[end] if halo else (own, own_right, own_left)
        factor = 0.125 * (has_up, has_down)[end] if halo else 0.125

        def here(tile, shift):
            return extended[end, tile, :, pl.ds(base + shift, SUB), :].reshape(-1, LANES)

        def down_up(tile, shift):
            return here(tile, shift + 1) - here(tile, shift - 1)

        own_rows = slice(0, SUB) if end == 0 else slice(height - SUB, height)
        if halo:
            firsts = []
            for tile in range(3):
                fours = []
                for k in range(tile, 3 * bands, 3):
                    four = message[F4 + 4 * k : F4 + 4 * k + 4, :]
                    fours += [four, four]
                firsts.append(jnp.concatenate(fours, axis=0))
        else:
            firsts = [x.reshape(-1, LANES) for x in (first_0[:, own_rows, :], first_1[:, own_rows, :], first_ends[end])]
        centre = shifts[0]
        values = shift_whole([here(tile, centre[0]) for tile in range(2)], centre[1])
        changes = shift_whole([down_up(tile, centre[0]) for tile in range(2)], centre[1])
        along = columns_whole(values, edges)
        value, across_cols = strip_windows(lambda shift: here(2, shift), *shifts)
        change_rows, _ = strip_windows(lambda shift: down_up(2, shift), *shifts)
        return (
            [0.25 * (x - y) for x, y in zip([*values, value], firsts)],
            [*[factor * x for x in changes], (factor * exists_tall) * change_rows],
            [*[factor * x for x in along], (factor * exists_tall) * across_cols],
        )

    def store_values(item, results):
        rows = rows_of(*item)
        for values, whole, strip in zip(
            results, (whole_offset, whole_rows, whole_cols), (strip_offset, strip_rows, strip_cols)
        ):
            values = [x.reshape(bands, SUB, LANES) for x in values]
            for tile in range(2):
                whole[tile, :, rows, :] = values[tile]
            strip[:, rows, :] = values[2]

    staggered([(halo, end) for halo in (True, False) for end in range(2)], values_of, store_values, 1)

    for i, value in enumerate((jnp.ones((SUB, LANES), jnp.float32), exists)):
        masks[i] = jnp.concatenate([value * has_up] + [value] * (rows_total // SUB - 2) + [value * has_down], axis=0)

    def masks_of(rows):
        whole = masks[0, rows, :]
        return (whole, whole, masks[1, rows, :])

    chunk = 64
    edges = edge_lanes(chunk)

    def data_row(k):
        return k * chunk + (rows_data - rows_total if k >= EACH // chunk else 0)

    fine_steps(
        rows_total, chunk, lambda fields: columns_whole(fields[:2], edges) + [columns_strip(fields[2])],
        initial, extrap, dual_rows, dual_cols, change, dual_data,
        [whole_offset.at[0], whole_offset.at[1], strip_offset],
        [whole_rows.at[0], whole_rows.at[1], strip_rows],
        [whole_cols.at[0], whole_cols.at[1], strip_cols],
        data_row, masks_of, result,
    )
    join(lambda c, tile: result[c, tile], lambda c: result[c, 2], joined)
    put_top = pltpu.make_async_copy(joined.at[:, pl.ds(SUB, MARGIN), :], flow_out.at[:, pl.ds(0, MARGIN), :], sems.at[2])
    put_bottom = pltpu.make_async_copy(
        joined.at[:, pl.ds(EACH + SUB, MARGIN), :], flow_out.at[:, pl.ds(height - MARGIN, MARGIN), :], sems.at[3]
    )
    put_top.start()
    put_bottom.start()
    put_middle.wait()
    put_coarse.wait()
    put_top.wait()
    put_bottom.wait()


def swap_with(message, axis, start):
    names = ("row", "col")
    sizes = [lax.axis_size(name) for name in names]
    along = names.index(axis)
    count, others = sizes[along], sizes[1 - along]

    def number(place, other):
        row, col = (place, other) if along == 0 else (other, place)
        return row * sizes[1] + col

    pairs = [(number(i, k), number(i + 1, k)) for i in range(start, count - 1, 2) for k in range(others)]
    if start:
        pairs += [(number(i, k), number(i, k + 1)) for i in (0, count - 1) for k in range(0, others, 2)]
    return lax.ppermute(message, names, pairs + [(j, i) for i, j in pairs])


def local(frame_first, frame_second, shifts):
    bands, height, width = frame_first.shape
    assert bands == 4 and width == COLUMNS and height % LANES == 0
    assert lax.axis_size("row") % 2 == 0 and lax.axis_size("col") % 2 == 0
    coarse_height = height // FACTOR
    coarse_width = width // FACTOR
    vmem = pl.BlockSpec(memory_space=pltpu.VMEM)
    hbm = pl.BlockSpec(memory_space=pltpu.HBM)
    tall_rows = coarse_height + 2 * LEAD
    inner_rows = height - 2 * BEGIN

    def shape(*sizes):
        return jax.ShapeDtypeStruct(sizes, jnp.float32)

    def scratch(*sizes):
        return pltpu.VMEM(sizes, jnp.float32)

    def call(kernel, name, arguments, outs, scratches=(), flops=1_000_000, **more):
        more = {"in_specs": [vmem] * len(arguments), "out_specs": (vmem,) * len(outs), **more}
        return pl.pallas_call(
            kernel,
            out_shape=tuple(outs),
            scratch_shapes=list(scratches),
            compiler_params=pltpu.CompilerParams(vmem_limit_bytes=24 * 1024 * 1024),
            cost_estimate=pl.CostEstimate(flops=flops, bytes_accessed=1_000_000, transcendentals=0),
            name=name,
            **more,
        )(*arguments)

    plane = shape(bands, height, LANES)
    column_message = shape(height // 2, LANES)
    row_message = shape(ROW_MESSAGE, LANES)
    whole_data = shape(2, bands, height + 2 * HALO, LANES)
    strip_data = shape(bands, height + 2 * HALO, LANES)

    *frames, coarse, swap, own_meta = call(
        first_kernel,
        "means_and_message",
        [pltpu.with_memory_space_constraint(x, pltpu.HBM) for x in (frame_second, frame_first, shifts)],
        [*[plane] * 4, shape(2 * bands * coarse_height, LANES), column_message, shape(SUB, LANES)],
        [
            pltpu.SMEM((1, 1, 2), jnp.int32),
            pltpu.SemaphoreType.DMA((2, bands, 2)),
            pltpu.SemaphoreType.DMA,
        ],
        in_specs=[hbm] * 3,
    )
    got_0 = swap_with(swap, "col", 0)

    swap, *whole_terms, initial, strip_e, strip_f, up_part, down_part = call(
        whole_terms_kernel,
        "whole_terms",
        [*frames, coarse, own_meta],
        [
            column_message, *[whole_data] * 3, shape(2, 2, inner_rows + 2 * GUARD, LANES),
            plane, plane, row_message, row_message,
        ],
        [scratch(2, bands, height, LANES), scratch(2, 2, coarse_height, LANES)],
        flops=8_000_000,
    )
    got_1 = swap_with(swap, "col", 1)

    (whole,) = call(
        whole_steps_kernel,
        "whole_steps",
        [initial, *whole_terms],
        [shape(2, 2, inner_rows, LANES)],
        fine_scratch(bands, 2, inner_rows)[1:],
        flops=20_000_000,
    )

    swap_0, swap_1, from_left, from_right, wide = call(
        functools.partial(message_kernel, lax.axis_size("col")),
        "row_messages",
        [coarse, own_meta, got_0, got_1, up_part, down_part, whole],
        [row_message, row_message, column_message, column_message, shape(2 * bands, coarse_height, LANES)],
        [scratch(ROW_MESSAGE, LANES)] * 2,
    )
    got_0 = swap_with(swap_0, "row", 0)
    got_1 = swap_with(swap_1, "row", 1)

    middle, strip_e, first_ends, *strip_terms = call(
        strip_kernel,
        "strip",
        [strip_e, strip_f, from_left, from_right, wide, own_meta, whole],
        [shape(2, inner_rows, width), plane, shape(2, bands, SUB, LANES), *[strip_data] * 3],
        [
            scratch(bands, height, LANES),
            scratch(2, 1, inner_rows, LANES),
            scratch(2, 1, coarse_height, LANES),
            *fine_scratch(bands, 1, inner_rows),
        ],
        flops=16_000_000,
    )

    flow, coarse_flow, *_ = call(
        functools.partial(outer_kernel, lax.axis_size("row")),
        "outer_rows",
        [
            *frames, strip_e, first_ends, from_left, from_right, wide, got_0, got_1, middle, own_meta,
            *whole_terms, *strip_terms,
        ],
        [shape(2, height, width), shape(2, coarse_height, coarse_width), *[whole_data] * 3, *[strip_data] * 3],
        [
            scratch(ROW_MESSAGE, LANES),
            scratch(ROW_MESSAGE, LANES),
            scratch(2, 3, bands, 40, LANES),
            scratch(2 * bands, tall_rows, LANES),
            scratch(2, 3, tall_rows, LANES),
            scratch(2, 2 * EACH, LANES),
            scratch(2, 3, 2 * EACH, LANES),
            scratch(2, 2 * EACH, width),
            scratch(2, coarse_height, coarse_width),
            pltpu.SemaphoreType.DMA((4,)),
            *fine_scratch(bands, 3, 2 * EACH),
        ],
        out_specs=(hbm, hbm) + (vmem,) * 6,
        input_output_aliases={13 + k: 2 + k for k in range(6)},
    )
    return (flow, coarse_flow)


def solution(mesh):
    return jax.shard_map(
        local,
        mesh=mesh,
        in_specs=(P(None, "row", "col"), P(None, "row", "col"), P("row", "col", None)),
        out_specs=(P(None, "row", "col"), P(None, "row", "col")),
        check_vma=False,
    )
```

```python
import functools

import jax
import jax.numpy as jnp
from jax import lax
from jax.experimental import pallas as pl
from jax.experimental.pallas import tpu as pltpu
from jax.sharding import PartitionSpec as P

FACTOR = 8
MAXD = 4
BANDS = 4
STEPS = 3
LANES = 128
COLUMNS = 2 * LANES
HALF = 64
SUB = 8
DEPTH = 4
REACH = DEPTH + MAXD + 1
SLOT = 16
C_SECOND = 6
C_FIRST = 5
LEAD = 8
MARGIN = 48
EDGE = 46
GUARD = 8
HALO = 8
BEGIN = 40
EACH = MARGIN + 16
LIMIT = 0.3
ALPHA = 0.3

S_MID = 55
S_RIGHT = 110
S_LEFT = LANES - REACH
S_TURN = COLUMNS - S_RIGHT - LANES

E8 = 0
H8 = 64
E1 = 72
H1 = 80
META = 81
F4 = 88
CS = 120
ROW_MESSAGE = 144
H_BAND = 32

COARSE_A = REACH + DEPTH
COARSE_B = SLOT + REACH + DEPTH
SHIFT_R = 2 * SLOT + REACH + DEPTH
SHIFT_C = SHIFT_R + 1
EXISTS = SHIFT_R + 2


def lanes_of(rows=SUB):
    return lax.broadcasted_iota(jnp.int32, (rows, LANES), 1)


def lanes_like(x):
    return lax.broadcasted_iota(jnp.int32, x.shape, 1)


def turn(x, amount):
    amount = amount % LANES
    return x if amount == 0 else pltpu.roll(x, amount, 1)


def turn_back(x, shift):
    return pltpu.roll(x, lax.rem(LANES - shift, LANES), 1)


def split_dot(x, exact):
    high = x.astype(jnp.bfloat16)
    rest = x - high.astype(jnp.float32)
    middle = rest.astype(jnp.bfloat16)
    low = (rest - middle.astype(jnp.float32)).astype(jnp.bfloat16)
    parts = [jnp.dot(part, exact, preferred_element_type=jnp.float32) for part in (low, middle, high)]
    return parts[0] + parts[1] + parts[2]


def scalar_at(ref, row, lane):
    return ref[row : row + 1, lane : lane + 1][0, 0]


def int_at(ref, row, lane):
    return scalar_at(ref, row, lane).astype(jnp.int32)


def is_even(axis, like):
    return jnp.broadcast_to(lax.axis_index(axis) % 2, like.shape) == 0


def without_ends(message, axis, count):
    place = jnp.broadcast_to(lax.axis_index(axis), message.shape)
    return jnp.where((place > 0) & (place < count - 1), message[...], 0.0)


def staggered(items, compute, store, depth):
    pending = []
    for item in items:
        pending.append((item, compute(item)))
        if len(pending) > depth:
            store(*pending.pop(0))
    for entry in pending:
        store(*entry)


def aligned(row):
    return pl.ds(pl.multiple_of(row, SUB), SUB)


def pack_message(to_right, seconds, firsts, coarse, shift_rows, shift_cols):
    bands, height, _ = seconds[0].shape
    second, first = seconds[int(to_right)], firsts[int(to_right)]
    second_from = LANES - REACH if to_right else 0
    first_from = LANES - DEPTH if to_right else 0
    coarse_from = LEAD + COLUMNS // FACTOR - C_SECOND if to_right else LEAD
    length = height // 2
    lane = lanes_of(length)
    packed = jnp.zeros((length, LANES), jnp.float32)
    for half in range(2):
        rows = slice(half * length, (half + 1) * length)
        cells = coarse[rows, :]
        base = half * HALF
        for band in range(bands):
            at = base + band * SLOT
            packed = jnp.where(lane >= at, turn(second[band, rows, :], at - second_from), packed)
            packed = jnp.where(lane >= at + REACH, turn(first[band, rows, :], at + REACH - first_from), packed)
            if band == 0:
                packed = jnp.where(lane >= base + COARSE_A, turn(cells, base + COARSE_A - coarse_from), packed)
            if band == 1:
                packed = jnp.where(lane >= base + COARSE_B, turn(cells, base + COARSE_B - coarse_from - 3), packed)
            if band == 2:
                packed = jnp.where(lane >= base + SHIFT_R, shift_rows, packed)
                packed = jnp.where(lane >= base + SHIFT_C, shift_cols, packed)
                packed = jnp.where(lane >= base + EXISTS, 1.0, packed)
    return packed


def column_meta(message):
    return (int_at(message, 0, SHIFT_R), int_at(message, 0, SHIFT_C)), scalar_at(message, 0, EXISTS)


def strip_second(base, from_left, from_right, rows, half, band):
    at = half * HALF + band * SLOT
    lane = lanes_like(base)
    cells = jnp.where(lane >= S_RIGHT, turn(from_right[rows, :], S_RIGHT - at), base)
    return jnp.where(lane >= S_LEFT, turn(from_left[rows, :], S_LEFT - at), cells)


def strip_first(base, from_left, from_right, rows, half, band):
    at = half * HALF + band * SLOT + REACH
    lane = lanes_like(base)
    cells = jnp.where(lane >= S_RIGHT, turn(from_right[rows, :], S_RIGHT - at), base)
    return jnp.where(lane >= S_LEFT, turn(from_left[rows, :], LANES - DEPTH - at), cells)


def strip_halo(base, beside, band, start, count):
    at = band * H_BAND + start
    lane = lanes_like(base)
    cells = jnp.where(lane >= S_RIGHT, turn(beside, S_RIGHT - at), base)
    return jnp.where(lane >= S_LEFT, turn(beside, LANES - count - at - SLOT), cells)


def strip_own(planes):
    return jnp.where(lanes_like(planes[0]) < S_MID, planes[0], turn(planes[1], -S_TURN))


def first_kernel(
    second_hbm, first_hbm, shifts_hbm, second_0, second_1, first_0, first_1, coarse, swap_0, swap_1, own_meta,
    shifts, sems, shift_sem,
):
    seconds, firsts = (second_0, second_1), (first_0, first_1)
    bands, height, _ = second_0.shape
    width = COLUMNS
    coarse_height = height // FACTOR
    lane = lanes_of()
    get_shifts = pltpu.make_async_copy(shifts_hbm, shifts, shift_sem)
    get_shifts.start()
    copies = []
    for image, (source, refs) in enumerate(((second_hbm, seconds), (first_hbm, firsts))):
        for band in range(bands):
            for tile, ref in enumerate(refs):
                copy = pltpu.make_async_copy(
                    source.at[band, :, pl.ds(tile * LANES, LANES)], ref.at[band], sems.at[image, band, tile]
                )
                copy.start()
                copies.append((image * bands + band, tile, ref, band, copy))
    cell = lax.broadcasted_iota(jnp.int32, (width, LANES), 0)
    place = lax.broadcasted_iota(jnp.int32, (width, LANES), 1)
    weights = jnp.where(place - LEAD == cell // FACTOR, 1.0 / (FACTOR * FACTOR), 0.0).astype(jnp.bfloat16)
    sums = {}
    for group in (copies[: len(copies) // 2], copies[len(copies) // 2 :]):
        for *_, copy in group:
            copy.wait()
        for plane, tile, ref, band, _ in group:
            parts = [ref[band, pl.ds(k, coarse_height, stride=FACTOR), :] for k in range(FACTOR)]
            while len(parts) > 1:
                parts = [x + y for x, y in zip(parts[::2], parts[1::2])]
            sums[plane, tile] = parts[0]
    sums = [jnp.concatenate([sums[plane, tile] for tile in range(2)], axis=1) for plane in range(2 * bands)]
    coarse[...] = split_dot(jnp.concatenate(sums, axis=0), weights)
    get_shifts.wait()
    shift_rows = shifts[0, 0, 0].astype(jnp.float32)
    shift_cols = shifts[0, 0, 1].astype(jnp.float32)
    own_meta[...] = jnp.where(lane < HALF, shift_rows, shift_cols)
    to_left, to_right = [
        pack_message(to_right, seconds, firsts, coarse, shift_rows, shift_cols) for to_right in (False, True)
    ]
    even = is_even("col", swap_0)
    swap_0[...] = jnp.where(even, to_right, to_left)
    swap_1[...] = jnp.where(even, to_left, to_right)


def message_kernel(
    count, coarse, own_meta, got_1, got_0, up_part, down_part, _whole, swap_0, swap_1, from_left, from_right, wide
):
    other = without_ends(got_1, "col", count)
    even = is_even("col", got_0)
    from_right[...] = jnp.where(even, got_0[...], other)
    from_left[...] = jnp.where(even, other, got_0[...])
    planes_coarse, coarse_height, _ = wide.shape
    bands = planes_coarse // 2
    end = from_left.shape[0]
    coarse_width = COLUMNS // FACTOR
    lane = lanes_of()
    wides = []
    for plane in range(planes_coarse):
        half, block = divmod(plane, planes_coarse // 2)
        for step in range(coarse_height // SUB):
            own = slice(plane * coarse_height + step * SUB, plane * coarse_height + (step + 1) * SUB)
            rows = slice(block * coarse_height + step * SUB, block * coarse_height + (step + 1) * SUB)
            at = half * HALF
            left = from_left[rows, :]
            right = from_right[rows, :]
            start = LEAD - C_SECOND
            cells = turn(left, start - at - COARSE_A)
            cells = jnp.where(lane >= start + 3, turn(left, start + 3 - at - COARSE_B), cells)
            cells = jnp.where(lane >= LEAD, coarse[own, :], cells)
            start = LEAD + coarse_width
            cells = jnp.where(lane >= start, turn(right, start - at - COARSE_A), cells)
            cells = jnp.where(lane >= start + 3, turn(right, start + 3 - at - COARSE_B), cells)
            wides.append((plane, step, cells))
    for plane, step, cells in wides:
        wide[plane, step * SUB : (step + 1) * SUB, :] = cells
    row = lax.broadcasted_iota(jnp.int32, (SUB, LANES), 0)
    meta = jnp.where(lane < 16, own_meta[...], jnp.where(lane < 32, turn(own_meta[...], HALF), 1.0))
    for message, at in ((from_left, 48), (from_right, 80)):
        first_rows = message[0:SUB, :]
        rows = jnp.broadcast_to(first_rows[:, SHIFT_R : SHIFT_R + 1], (SUB, LANES))
        cols = jnp.broadcast_to(first_rows[:, SHIFT_C : SHIFT_C + 1], (SUB, LANES))
        meta = jnp.where(lane >= at, rows, meta)
        meta = jnp.where(lane >= at + 16, cols, meta)

    def beside(rows, half):
        left = from_left[rows, :]
        right = from_right[rows, :]
        cells = jnp.zeros((SUB, LANES), jnp.float32)
        for band in range(bands):
            at = half * HALF + band * SLOT
            cells = jnp.where(lane >= band * H_BAND, turn(right, band * H_BAND - at), cells)
            cells = jnp.where(lane >= band * H_BAND + SLOT, turn(left, band * H_BAND + SLOT - at), cells)
        return cells

    even = is_even("row", meta)
    parts = []
    for part, half, near, next_rows, row_of in (
        (up_part, 0, slice(0, 8), slice(8, 16), 0),
        (down_part, 1, slice(end - 8, end), slice(end - 16, end - 8), 7),
    ):
        eight = beside(near, half)
        one = beside(next_rows, half)
        one = jnp.broadcast_to(one[row_of : row_of + 1], (SUB, LANES))
        coarse_rows = []
        for band in range(bands):
            rows = slice(0, C_SECOND) if half == 0 else slice(coarse_height - C_SECOND, coarse_height)
            second = wide[band, rows, :]
            first = turn(wide[bands + band, rows, :], HALF)
            coarse_rows.append(jnp.where(lanes_like(second) < HALF, second, first))
        parts.append([
            (part[E8:H8, :], E8), (eight, H8), (part[E1:H1, :], E1), (jnp.where(row == 0, one, meta), H1),
            (part[F4:CS, :], F4), *[(x, CS + k * C_SECOND) for k, x in enumerate(coarse_rows)],
        ])
    for (up, at), (down, _) in zip(*parts):
        even = is_even("row", up)
        swap_0[at : at + up.shape[0], :] = jnp.where(even, down, up)
        swap_1[at : at + up.shape[0], :] = jnp.where(even, up, down)


def coarse_flow_of(second, first, mask):
    def along_rows(x):
        return pltpu.roll(x, x.shape[0] - 1, 0) - pltpu.roll(x, 1, 0)

    def along_cols(x):
        return pltpu.roll(x, LANES - 1, 1) - pltpu.roll(x, 1, 1)

    bands = BANDS
    size = second.shape[0] // bands
    grad_rows = 0.125 * along_rows(second)
    grad_cols = 0.125 * along_cols(second)
    offset = 0.25 * (second - first)
    data = jnp.clip(offset, -LIMIT, LIMIT)

    def pull(grads):
        terms = data * grads
        return sum(terms[k * size : (k + 1) * size] for k in range(bands))

    def tall(x):
        return jnp.concatenate([x] * bands, axis=0)

    flow = [-mask * pull(grad_rows), -mask * pull(grad_cols)]
    extrapolated = [2.0 * x for x in flow]
    dual_rows = [0.0, 0.0]
    dual_cols = [0.0, 0.0]
    for step in range(1, STEPS):
        changes = [(along_rows(x), along_cols(x)) for x in extrapolated]
        data = data + offset + grad_rows * tall(extrapolated[0]) + grad_cols * tall(extrapolated[1])
        data = jnp.clip(data, -LIMIT, LIMIT)
        for c in range(2):
            rows = dual_rows[c] + changes[c][0]
            cols = dual_cols[c] + changes[c][1]
            norm = jnp.maximum(rows * rows + cols * cols, 1e-30)
            scale = jnp.minimum(mask, (8.0 * ALPHA) * lax.rsqrt(norm))
            dual_rows[c] = rows * scale
            dual_cols[c] = cols * scale
        pulls = [pull(grad_rows), pull(grad_cols)]
        for c in range(2):
            divergence = along_rows(dual_rows[c]) + along_cols(dual_cols[c])
            following = flow[c] + mask * ((1.0 / 64.0) * divergence - pulls[c])
            extrapolated[c] = 2.0 * following - flow[c]
            flow[c] = following
    return flow


def columns_of_planes(planes):
    whole = lax.broadcasted_iota(jnp.int32, (LANES, COLUMNS), 1)
    lane = lax.broadcasted_iota(jnp.int32, (LANES, LANES), 1)
    strip = jnp.where(lane < S_MID, lane, jnp.where(lane < S_LEFT, lane + (COLUMNS - S_RIGHT), lane - LANES))
    return jnp.concatenate([x for x, wanted in ((whole, "whole"), (strip, "strip")) if wanted in planes], axis=1)


def upsample(flow, planes, target):
    column = columns_of_planes(planes)
    source = lax.broadcasted_iota(jnp.int32, column.shape, 0)
    spread = jnp.where(source - LEAD == lax.shift_right_arithmetic(column, 3), float(FACTOR), 0.0).astype(jnp.bfloat16)
    rows = flow[0].shape[0]
    wide = split_dot(jnp.concatenate(flow, axis=0), spread)
    for c in range(2):
        for tile in range(column.shape[1] // LANES):
            target[c, tile] = wide[c * rows : (c + 1) * rows, tile * LANES : (tile + 1) * LANES]


def repeat_rows(spread, initial, cells):
    for c in range(2):
        for tile in range(initial.shape[1]):
            rows = [jnp.broadcast_to(spread[c, tile, cell : cell + 1, :], (SUB, LANES)) for cell in cells]
            initial[c, tile, GUARD : GUARD + SUB * len(cells), :] = jnp.concatenate(rows, axis=0)


def shift_whole(here, shift):
    turned = [turn_back(x, shift) for x in here]
    lane = lanes_like(here[0])
    return [
        jnp.where(lane + shift >= LANES, turned[1], turned[0]),
        jnp.where(lane + shift < 0, turned[0], turned[1]),
    ]


def edge_lanes(rows):
    lane = lanes_of(rows)
    return lane == LANES - 1, lane == 0


def columns_whole(fields, edges):
    last, first = edges
    ahead = [pltpu.roll(x, LANES - 1, 1) for x in fields]
    behind = [pltpu.roll(x, 1, 1) for x in fields]
    return [
        jnp.where(last, ahead[1], ahead[0]) - behind[0],
        ahead[1] - jnp.where(first, behind[0], behind[1]),
    ]


def columns_strip(field):
    return pltpu.roll(field, LANES - 1, 1) - pltpu.roll(field, 1, 1)


def strip_windows(window, centre, right, left):
    own = turn_back(window(centre[0]), centre[1])
    beyond_left = turn_back(window(left[0]), left[1])
    beyond_right = turn_back(window(right[0]), right[1])
    lane = lanes_like(own)
    beyond = jnp.where((lane >= S_LEFT) | (lane < S_MID), beyond_left, beyond_right)
    is_beyond = lane >= S_RIGHT
    return jnp.where(is_beyond, beyond, own), jnp.where(is_beyond, columns_strip(beyond), columns_strip(own))


def fine_steps(
    rows_total, chunk, columns, initial, extrap, dual_rows, dual_cols, change, dual_data,
    offsets, grads_rows, grads_cols, data_row, masks_of, result,
):
    planes = len(offsets)
    bands = offsets[0].shape[0]
    chunks = rows_total // chunk
    both = [(c, tile) for c in range(2) for tile in range(planes)]

    for step in range(STEPS):
        source = initial if step == 0 else extrap
        final = step == STEPS - 1

        def dual(k, source=source, step=step):
            row = GUARD + k * chunk
            own = pl.ds(k * chunk, chunk)
            at = pl.ds(row, chunk)
            masks = masks_of(own)
            along = [columns([source[c, tile, at, :] for tile in range(planes)]) for c in range(2)]
            values = []
            for c, tile in both:
                rows = source[c, tile, pl.ds(row + 1, chunk), :] - source[c, tile, pl.ds(row - 1, chunk), :]
                cols = along[c][tile]
                if step > 0:
                    rows = rows + dual_rows[c, tile, at, :]
                    cols = cols + dual_cols[c, tile, own, :]
                norm = jnp.maximum(rows * rows + cols * cols, 1e-30)
                scale = jnp.minimum(masks[tile], (8.0 * ALPHA) * lax.rsqrt(norm))
                values.append((rows * scale, cols * scale))
            for (c, tile), (rows, cols) in zip(both, values):
                dual_rows[c, tile, at, :] = rows
                dual_cols[c, tile, own, :] = cols

        def primal(k, step=step, final=final):
            data = pl.ds(data_row(k), chunk)
            row = GUARD + k * chunk
            own = pl.ds(k * chunk, chunk)
            at = pl.ds(row, chunk)
            masks = masks_of(own)
            along = [columns([dual_cols[c, tile, own, :] for tile in range(planes)]) for c in range(2)]
            for tile in range(planes):
                start = [initial[c, tile, at, :] for c in range(2)]
                if step > 0:
                    moved = [extrap[c, tile, at, :] - start[c] for c in range(2)]
                pulls = [None, None]
                duals = []
                for band in range(bands):
                    gradient = (grads_rows[tile][band, data, :], grads_cols[tile][band, data, :])
                    value = offsets[tile][band, data, :]
                    if step > 0:
                        value = value + gradient[0] * moved[0] + gradient[1] * moved[1]
                        value = value + dual_data[band, tile, own, :]
                    value = jnp.clip(value, -LIMIT, LIMIT)
                    duals.append(value)
                    for c in range(2):
                        term = value * gradient[c]
                        pulls[c] = term if pulls[c] is None else pulls[c] + term
                movings = []
                for c in range(2):
                    divergence = (
                        dual_rows[c, tile, pl.ds(row + 1, chunk), :]
                        - dual_rows[c, tile, pl.ds(row - 1, chunk), :]
                        + along[c][tile]
                    )
                    movings.append((masks[tile] * (1.0 / 64.0)) * divergence - pulls[c])
                if step > 0:
                    olds = [change[c, tile, own, :] for c in range(2)]
                for c in range(2):
                    if step == 0:
                        change[c, tile, own, :] = movings[c]
                        extrap[c, tile, at, :] = start[c] + 2.0 * movings[c]
                    else:
                        new = olds[c] + movings[c]
                        if final:
                            result[c, tile, own, :] = start[c] + new
                        else:
                            change[c, tile, own, :] = new
                            extrap[c, tile, at, :] = start[c] + (new + movings[c])
                if not final:
                    for band in range(bands):
                        dual_data[band, tile, own, :] = duals[band]

        dual(0)
        for k in range(1, chunks):
            dual(k)
            primal(k - 1)
        primal(chunks - 1)


def clear_guards(*refs):
    for ref in refs:
        rows = ref.shape[2]
        zero = jnp.zeros((GUARD, LANES), jnp.float32)
        for c in range(2):
            for tile in range(ref.shape[1]):
                ref[c, tile, 0:GUARD, :] = zero
                ref[c, tile, rows - GUARD : rows, :] = zero


def fine_scratch(bands, planes, rows):
    guarded = pltpu.VMEM((2, planes, rows + 2 * GUARD, LANES), jnp.float32)
    plain = pltpu.VMEM((2, planes, rows, LANES), jnp.float32)
    return [guarded, guarded, guarded, plain, plain, pltpu.VMEM((bands, planes, rows, LANES), jnp.float32)]


def pieces(bands, height, rows):
    assert (height - 2 * SUB) % rows == 0
    return [(band, row) for row in range(SUB, height - SUB, rows) for band in range(bands)]


def whole_terms_kernel(
    second_0, second_1, first_0, first_1, coarse, own_meta,
    offset, grad_rows, grad_cols, initial, strip_e, strip_f, up, down, moved, spread,
):
    seconds, firsts = (second_0, second_1), (first_0, first_1)
    bands, height, _ = second_0.shape
    block = 80
    coarse_height = coarse.shape[0] // (2 * bands)
    shift_rows, shift_cols = scalar_at(own_meta, 0, 0), scalar_at(own_meta, 0, HALF)
    centre = (shift_rows.astype(jnp.int32), shift_cols.astype(jnp.int32))
    def windows(band, row, rows):
        here = [ref[band, pl.ds(row + centre[0], rows), :].reshape(-1, LANES) for ref in seconds]
        return shift_whole(here, centre[1])

    flow = coarse_flow_of(coarse[0 : bands * coarse_height, :], coarse[bands * coarse_height :, :], 1.0)
    upsample(flow, ("whole",), spread)

    ends = [(row, windows(slice(None), row, SUB)) for row in (SUB // 2, height - SUB - SUB // 2)]
    for row, values in ends:
        for tile in range(2):
            moved[tile, :, row : row + SUB, :] = values[tile].reshape(bands, SUB, LANES)

    edges = edge_lanes(block)

    def values_of(item):
        band, row = item
        values = windows(band, row, block)
        along = columns_whole(values, edges)
        own = [ref[band, row : row + block, :] for ref in firsts]
        return values, [0.25 * (x - y) for x, y in zip(values, own)], [0.125 * x for x in along]

    def store_values(item, results):
        band, row = item
        values, offsets, gradients = results
        data = slice(row + HALO, row + HALO + block)
        for tile in range(2):
            moved[tile, band, row : row + block, :] = values[tile]
            offset[tile, band, data, :] = offsets[tile]
            grad_cols[tile, band, data, :] = gradients[tile]

    staggered(pieces(bands, height, block), values_of, store_values, 1)

    def strips_of(item):
        band, row = item
        rows = slice(row, row + LANES)
        return strip_own([ref[band, rows, :] for ref in seconds]), strip_own([ref[band, rows, :] for ref in firsts])

    def store_strips(item, results):
        band, row = item
        strip_e[band, row : row + LANES, :], strip_f[band, row : row + LANES, :] = results

    staggered([(band, row) for band in range(bands) for row in range(0, height, LANES)], strips_of, store_strips, 1)

    def gradient_of(item):
        band, row = item
        return [
            0.125 * (moved[tile, band, pl.ds(row + 1, 120), :] - moved[tile, band, pl.ds(row - 1, 120), :])
            for tile in range(2)
        ]

    def store_gradient(item, results):
        band, row = item
        for tile in range(2):
            grad_rows[tile, band, row + HALO : row + HALO + 120, :] = results[tile]

    staggered(pieces(bands, height, 120), gradient_of, store_gradient, 1)

    clear_guards(initial)
    rows_total = initial.shape[2] - 2 * GUARD
    repeat_rows(spread, initial, [BEGIN // FACTOR + k for k in range(rows_total // SUB)])

    parts = []
    for band in range(bands):
        for second, first in zip(seconds, firsts):
            parts.append((
                second[band, 0:16, :], first[band, 0:8, :],
                second[band, height - 16 : height, :], first[band, height - 8 : height, :],
            ))
    for k, (second_top, first_top, second_end, first_end) in enumerate(parts):
        up[E8 + 8 * k : E8 + 8 * k + 8, :] = second_top[0:8]
        up[E1 + k : E1 + k + 1, :] = second_top[8:9]
        up[F4 + 4 * k : F4 + 4 * k + 4, :] = first_top[0:4]
        down[E8 + 8 * k : E8 + 8 * k + 8, :] = second_end[8:16]
        down[E1 + k : E1 + k + 1, :] = second_end[7:8]
        down[F4 + 4 * k : F4 + 4 * k + 4, :] = first_end[4:8]
    for target in (up, down):
        for start, end in ((H8, E1), (H1, F4), (CS, ROW_MESSAGE)):
            target[start:end, :] = jnp.zeros((end - start, LANES), jnp.float32)


def whole_steps_kernel(
    initial, offset, grad_rows, grad_cols, result, extrap, dual_rows, dual_cols, change, dual_data
):
    rows_total = result.shape[2]
    clear_guards(extrap, dual_rows)
    chunk = 88
    edges = edge_lanes(chunk)
    fine_steps(
        rows_total, chunk, lambda fields: columns_whole(fields, edges),
        initial, extrap, dual_rows, dual_cols, change, dual_data,
        *[[ref.at[tile] for tile in range(2)] for ref in (offset, grad_rows, grad_cols)],
        lambda k: HALO + BEGIN + k * chunk, lambda own: (1.0, 1.0), result,
    )


def strip_kernel(
    strip_e, strip_f, from_left, from_right, wide, own_meta, whole,
    middle, strip_out, first_ends, offset, grad_rows, grad_cols,
    moved, result, spread, initial, extrap, dual_rows, dual_cols, change, dual_data,
):
    bands, height, _ = strip_e.shape
    block = 120
    coarse_height = height // FACTOR
    coarse_width = COLUMNS // FACTOR
    rows_total = height - 2 * BEGIN
    lane = lanes_of()
    centre = (int_at(own_meta, 0, 0), int_at(own_meta, 0, HALF))
    right, has_right = column_meta(from_right)
    left, has_left = column_meta(from_left)
    exists = jnp.where(lane < S_RIGHT, 1.0, jnp.where(lane < S_LEFT, has_right, has_left))

    def tall_factor(rows):
        return 0.125 * jnp.concatenate([exists] * (rows // SUB), axis=0)

    mask = jnp.where(lane < LEAD, has_left, jnp.where(lane < LEAD + coarse_width, 1.0, has_right))
    mask = jnp.concatenate([mask] * (coarse_height // SUB), axis=0)
    cells = [wide[k * bands : (k + 1) * bands].reshape(bands * coarse_height, LANES) for k in range(2)]
    flow = coarse_flow_of(*cells, mask)
    upsample(flow, ("strip",), spread)

    def halves(row, rows):
        half = row // (height // 2)
        start = row - half * (height // 2)
        return half, slice(start, start + rows)

    def second_of(item):
        band, row = item
        half, message = halves(row, LANES)
        return strip_second(strip_e[band, row : row + LANES, :], from_left, from_right, message, half, band)

    def store_second(item, value):
        band, row = item
        strip_out[band, row : row + LANES, :] = value

    staggered([(band, row) for row in range(0, height, LANES) for band in range(bands)], second_of, store_second, 1)

    def first_of(band, row, rows):
        half, message = halves(row, rows)
        return strip_first(strip_f[band, row : row + rows, :], from_left, from_right, message, half, band)

    firsts = [(end, band, first_of(band, (0, height - SUB)[end], SUB)) for end in range(2) for band in range(bands)]
    for end, band, value in firsts:
        first_ends[end, band] = value

    def windows(band, row, rows):
        return strip_windows(
            lambda shift: strip_out[band, pl.ds(row + shift, rows), :].reshape(-1, LANES), centre, right, left
        )

    ends = [(row, windows(slice(None), row, SUB)[0]) for row in (SUB // 2, height - SUB - SUB // 2)]
    for row, value in ends:
        moved[:, row : row + SUB, :] = value.reshape(bands, SUB, LANES)

    factor = tall_factor(block)

    def values_of(item):
        band, row = item
        value, along = windows(band, row, block)
        return value, 0.25 * (value - first_of(band, row, block)), factor * along

    def store_values(item, results):
        band, row = item
        data = slice(row + HALO, row + HALO + block)
        moved[band, row : row + block, :], offset[band, data, :], grad_cols[band, data, :] = results

    staggered(pieces(bands, height, block), values_of, store_values, 1)

    def gradient_of(item):
        band, row = item
        return factor * (moved[band, pl.ds(row + 1, block), :] - moved[band, pl.ds(row - 1, block), :])

    def store_gradient(item, value):
        band, row = item
        grad_rows[band, row + HALO : row + HALO + block, :] = value

    staggered(pieces(bands, height, block), gradient_of, store_gradient, 1)

    clear_guards(initial, extrap, dual_rows)
    repeat_rows(spread, initial, [BEGIN // FACTOR + k for k in range(rows_total // SUB)])

    chunk = 176
    masks = jnp.concatenate([exists] * (chunk // SUB), axis=0)
    fine_steps(
        rows_total, chunk, lambda fields: [columns_strip(fields[0])],
        initial, extrap, dual_rows, dual_cols, change, dual_data, [offset], [grad_rows], [grad_cols],
        lambda k: HALO + BEGIN + k * chunk, lambda own: (masks,), result,
    )
    join(lambda c, tile: whole[c, tile], lambda c: result[c, 0], middle)


def join(whole, strip, target):
    rows = target.shape[1]
    lane = lanes_of(rows)
    for c in range(2):
        edge = strip(c)
        start = jnp.where(lane < EDGE, edge, whole(c, 0))
        end = jnp.where(lane >= LANES - EDGE, turn(edge, S_TURN), whole(c, 1))
        target[c, :, 0:LANES] = start
        target[c, :, LANES:COLUMNS] = end


def outer_kernel(
    count, second_0, second_1, first_0, first_1, strip_e, first_ends, from_left, from_right, wide, got_1, got_0, middle, own_meta,
    _wo, _wr, _wc, _so, _sr, _sc,
    flow_out, coarse_out, whole_offset, whole_rows, whole_cols, strip_offset, strip_rows, strip_cols,
    from_up, from_down, extended, tall, spread, masks, result, joined, coarse_result, sems,
    initial, extrap, dual_rows, dual_cols, change, dual_data,
):
    bands, height, _ = second_0.shape
    coarse_height = height // FACTOR
    coarse_width = COLUMNS // FACTOR
    rows_total = 2 * EACH
    lane = lanes_of()

    put_middle = pltpu.make_async_copy(
        middle.at[:, pl.ds(MARGIN - BEGIN, height - 2 * MARGIN), :],
        flow_out.at[:, pl.ds(MARGIN, height - 2 * MARGIN), :],
        sems.at[0],
    )
    put_middle.start()

    other = without_ends(got_1, "row", count)
    even = is_even("row", got_0)
    from_down[...] = jnp.where(even, got_0[...], other)
    from_up[...] = jnp.where(even, other, got_0[...])

    own = (int_at(own_meta, 0, 0), int_at(own_meta, 0, HALF))
    own_right, has_right = column_meta(from_right)
    own_left, has_left = column_meta(from_left)
    has_up = scalar_at(from_up, META, 32)
    has_down = scalar_at(from_down, META, 32)
    exists = jnp.where(lane < S_RIGHT, 1.0, jnp.where(lane < S_LEFT, has_right, has_left))

    def trio(message):
        return (
            (int_at(message, META, 0), int_at(message, META, 16)),
            (int_at(message, META, 80), int_at(message, META, 96)),
            (int_at(message, META, 48), int_at(message, META, 64)),
        )

    above = trio(from_up)
    below = trio(from_down)

    zero = jnp.zeros((SUB, LANES), jnp.float32)
    tall_rows = coarse_height + 2 * LEAD
    parts = []
    fill = jnp.zeros((LEAD - C_SECOND, LANES), jnp.float32)
    for plane in range(2 * bands):
        at = CS + C_SECOND * (plane % bands)
        ends = [turn(message[at : at + C_SECOND, :], HALF * (plane // bands)) for message in (from_up, from_down)]
        parts.append([fill, ends[0], wide[plane], ends[1], fill])
    for plane, values in enumerate(parts):
        tall[plane] = jnp.concatenate(values, axis=0)
    across = jnp.where(lane < LEAD, has_left, jnp.where(lane < LEAD + coarse_width, 1.0, has_right))
    mask = jnp.concatenate([across * has_up] + [across] * (coarse_height // SUB) + [across * has_down], axis=0)
    cells = [tall[k * bands : (k + 1) * bands].reshape(bands * tall_rows, LANES) for k in range(2)]
    flow = coarse_flow_of(*cells, mask)
    for c in range(2):
        coarse_result[c] = turn(flow[c][LEAD : LEAD + coarse_height], -LEAD)[:, :coarse_width]
    put_coarse = pltpu.make_async_copy(coarse_result, coarse_out, sems.at[1])
    put_coarse.start()
    upsample(flow, ("whole", "strip"), spread)
    clear_guards(initial, extrap, dual_rows)
    each = EACH // SUB
    repeat_rows(
        spread, initial,
        [LEAD - 1 + k for k in range(each)] + [tall_rows - LEAD + 1 - each + k for k in range(each)],
    )

    for end in range(2):
        message = (from_up, from_down)[end]
        beside = message[H8 : H8 + 8, :]
        beside_one = jnp.broadcast_to(message[H1 : H1 + 1, :], (SUB, LANES))
        parts = []
        for band in range(bands):
            eights = [message[E8 + 8 * k : E8 + 8 * k + 8, :] for k in (2 * band, 2 * band + 1)]
            ones = [jnp.broadcast_to(message[E1 + k : E1 + k + 1, :], (SUB, LANES)) for k in (2 * band, 2 * band + 1)]
            eights.append(strip_halo(strip_own(eights), beside, band, 0, REACH))
            ones.append(strip_halo(strip_own(ones), beside_one, band, 0, REACH))
            for tile, (eight, one) in enumerate(zip(eights, ones)):
                source = (second_0, second_1, strip_e)[tile]
                if end == 0:
                    parts.append((tile, band, [one, eight, source[band, 0:24, :]]))
                else:
                    parts.append((tile, band, [source[band, height - 24 : height, :], eight, one]))
        for tile, band, values in parts:
            extended[end, tile, band] = jnp.concatenate(values, axis=0)
    edges = edge_lanes(bands * SUB)
    rows_data = whole_offset.shape[2]
    exists_tall = jnp.concatenate([exists] * bands, axis=0)

    def rows_of(halo, end):
        if halo:
            return slice(0, SUB) if end == 0 else slice(rows_data - SUB, rows_data)
        return slice(HALO, HALO + SUB) if end == 0 else slice(rows_data - HALO - SUB, rows_data - HALO)

    def values_of(item):
        halo, end = item
        message = (from_up, from_down)[end]
        base = (SUB, 3 * SUB)[end] if halo else 2 * SUB
        shifts = (above, below)[end] if halo else (own, own_right, own_left)
        factor = 0.125 * (has_up, has_down)[end] if halo else 0.125

        def here(tile, shift):
            return extended[end, tile, :, pl.ds(base + shift, SUB), :].reshape(-1, LANES)

        def down_up(tile, shift):
            return here(tile, shift + 1) - here(tile, shift - 1)

        own_rows = slice(0, SUB) if end == 0 else slice(height - SUB, height)
        if halo:
            firsts = [[], [], []]
            for band in range(bands):
                eights = []
                for k in (2 * band, 2 * band + 1):
                    four = message[F4 + 4 * k : F4 + 4 * k + 4, :]
                    eights.append(jnp.concatenate([four, four], axis=0))
                eights.append(strip_halo(strip_own(eights), message[H8 : H8 + 8, :], band, REACH, DEPTH))
                for tile in range(3):
                    firsts[tile].append(eights[tile])
            firsts = [jnp.concatenate(x, axis=0) for x in firsts]
        else:
            firsts = [x.reshape(-1, LANES) for x in (first_0[:, own_rows, :], first_1[:, own_rows, :], first_ends[end])]
        centre = shifts[0]
        values = shift_whole([here(tile, centre[0]) for tile in range(2)], centre[1])
        changes = shift_whole([down_up(tile, centre[0]) for tile in range(2)], centre[1])
        along = columns_whole(values, edges)
        value, across_cols = strip_windows(lambda shift: here(2, shift), *shifts)
        change_rows, _ = strip_windows(lambda shift: down_up(2, shift), *shifts)
        return (
            [0.25 * (x - y) for x, y in zip([*values, value], firsts)],
            [*[factor * x for x in changes], (factor * exists_tall) * change_rows],
            [*[factor * x for x in along], (factor * exists_tall) * across_cols],
        )

    def store_values(item, results):
        rows = rows_of(*item)
        for values, whole, strip in zip(
            results, (whole_offset, whole_rows, whole_cols), (strip_offset, strip_rows, strip_cols)
        ):
            values = [x.reshape(bands, SUB, LANES) for x in values]
            for tile in range(2):
                whole[tile, :, rows, :] = values[tile]
            strip[:, rows, :] = values[2]

    staggered([(halo, end) for halo in (True, False) for end in range(2)], values_of, store_values, 1)

    for i, value in enumerate((jnp.ones((SUB, LANES), jnp.float32), exists)):
        masks[i] = jnp.concatenate([value * has_up] + [value] * (rows_total // SUB - 2) + [value * has_down], axis=0)

    def masks_of(rows):
        whole = masks[0, rows, :]
        return (whole, whole, masks[1, rows, :])

    chunk = 64
    edges = edge_lanes(chunk)

    def data_row(k):
        return k * chunk + (rows_data - rows_total if k >= EACH // chunk else 0)

    fine_steps(
        rows_total, chunk, lambda fields: columns_whole(fields[:2], edges) + [columns_strip(fields[2])],
        initial, extrap, dual_rows, dual_cols, change, dual_data,
        [whole_offset.at[0], whole_offset.at[1], strip_offset],
        [whole_rows.at[0], whole_rows.at[1], strip_rows],
        [whole_cols.at[0], whole_cols.at[1], strip_cols],
        data_row, masks_of, result,
    )
    join(lambda c, tile: result[c, tile], lambda c: result[c, 2], joined)
    put_top = pltpu.make_async_copy(joined.at[:, pl.ds(SUB, MARGIN), :], flow_out.at[:, pl.ds(0, MARGIN), :], sems.at[2])
    put_bottom = pltpu.make_async_copy(
        joined.at[:, pl.ds(EACH + SUB, MARGIN), :], flow_out.at[:, pl.ds(height - MARGIN, MARGIN), :], sems.at[3]
    )
    put_top.start()
    put_bottom.start()
    put_middle.wait()
    put_coarse.wait()
    put_top.wait()
    put_bottom.wait()


def swap_with(message, axis, start):
    names = ("row", "col")
    sizes = [lax.axis_size(name) for name in names]
    along = names.index(axis)
    count, others = sizes[along], sizes[1 - along]

    def number(place, other):
        row, col = (place, other) if along == 0 else (other, place)
        return row * sizes[1] + col

    pairs = [(number(i, k), number(i + 1, k)) for i in range(start, count - 1, 2) for k in range(others)]
    if start:
        pairs += [(number(i, k), number(i, k + 1)) for i in (0, count - 1) for k in range(0, others, 2)]
    return lax.ppermute(message, names, pairs + [(j, i) for i, j in pairs])


def local(frame_first, frame_second, shifts):
    bands, height, width = frame_first.shape
    assert bands == 4 and width == COLUMNS and height % LANES == 0
    assert lax.axis_size("row") % 2 == 0 and lax.axis_size("col") % 2 == 0
    coarse_height = height // FACTOR
    coarse_width = width // FACTOR
    vmem = pl.BlockSpec(memory_space=pltpu.VMEM)
    hbm = pl.BlockSpec(memory_space=pltpu.HBM)
    tall_rows = coarse_height + 2 * LEAD
    inner_rows = height - 2 * BEGIN

    def shape(*sizes):
        return jax.ShapeDtypeStruct(sizes, jnp.float32)

    def scratch(*sizes):
        return pltpu.VMEM(sizes, jnp.float32)

    def call(kernel, name, arguments, outs, scratches=(), flops=1_000_000, **more):
        more = {"in_specs": [vmem] * len(arguments), "out_specs": (vmem,) * len(outs), **more}
        return pl.pallas_call(
            kernel,
            out_shape=tuple(outs),
            scratch_shapes=list(scratches),
            compiler_params=pltpu.CompilerParams(vmem_limit_bytes=24 * 1024 * 1024),
            cost_estimate=pl.CostEstimate(flops=flops, bytes_accessed=1_000_000, transcendentals=0),
            name=name,
            **more,
        )(*arguments)

    plane = shape(bands, height, LANES)
    column_message = shape(height // 2, LANES)
    row_message = shape(ROW_MESSAGE, LANES)
    whole_data = shape(2, bands, height + 2 * HALO, LANES)
    strip_data = shape(bands, height + 2 * HALO, LANES)

    *frames, coarse, swap_0, swap_1, own_meta = call(
        first_kernel,
        "means_and_message",
        [pltpu.with_memory_space_constraint(x, pltpu.HBM) for x in (frame_second, frame_first, shifts)],
        [*[plane] * 4, shape(2 * bands * coarse_height, LANES), column_message, column_message, shape(SUB, LANES)],
        [
            pltpu.SMEM((1, 1, 2), jnp.int32),
            pltpu.SemaphoreType.DMA((2, bands, 2)),
            pltpu.SemaphoreType.DMA,
        ],
        in_specs=[hbm] * 3,
    )
    got_1 = swap_with(swap_1, "col", 1)
    got_0 = swap_with(swap_0, "col", 0)

    *whole_terms, initial, strip_e, strip_f, up_part, down_part = call(
        whole_terms_kernel,
        "whole_terms",
        [*frames, coarse, own_meta],
        [
            *[whole_data] * 3, shape(2, 2, inner_rows + 2 * GUARD, LANES),
            plane, plane, row_message, row_message,
        ],
        [scratch(2, bands, height, LANES), scratch(2, 2, coarse_height, LANES)],
        flops=8_000_000,
    )
    (whole,) = call(
        whole_steps_kernel,
        "whole_steps",
        [initial, *whole_terms],
        [shape(2, 2, inner_rows, LANES)],
        fine_scratch(bands, 2, inner_rows)[1:],
        flops=20_000_000,
    )

    swap_0, swap_1, from_left, from_right, wide = call(
        functools.partial(message_kernel, lax.axis_size("col")),
        "row_messages",
        [coarse, own_meta, got_1, got_0, up_part, down_part, whole],
        [row_message, row_message, column_message, column_message, shape(2 * bands, coarse_height, LANES)],
    )
    got_1 = swap_with(swap_1, "row", 1)
    got_0 = swap_with(swap_0, "row", 0)

    middle, strip_e, first_ends, *strip_terms = call(
        strip_kernel,
        "strip",
        [strip_e, strip_f, from_left, from_right, wide, own_meta, whole],
        [shape(2, inner_rows, width), plane, shape(2, bands, SUB, LANES), *[strip_data] * 3],
        [
            scratch(bands, height, LANES),
            scratch(2, 1, inner_rows, LANES),
            scratch(2, 1, coarse_height, LANES),
            *fine_scratch(bands, 1, inner_rows),
        ],
        flops=16_000_000,
    )

    flow, coarse_flow, *_ = call(
        functools.partial(outer_kernel, lax.axis_size("row")),
        "outer_rows",
        [
            *frames, strip_e, first_ends, from_left, from_right, wide, got_1, got_0, middle, own_meta,
            *whole_terms, *strip_terms,
        ],
        [shape(2, height, width), shape(2, coarse_height, coarse_width), *[whole_data] * 3, *[strip_data] * 3],
        [
            scratch(ROW_MESSAGE, LANES),
            scratch(ROW_MESSAGE, LANES),
            scratch(2, 3, bands, 40, LANES),
            scratch(2 * bands, tall_rows, LANES),
            scratch(2, 3, tall_rows, LANES),
            scratch(2, 2 * EACH, LANES),
            scratch(2, 3, 2 * EACH, LANES),
            scratch(2, 2 * EACH, width),
            scratch(2, coarse_height, coarse_width),
            pltpu.SemaphoreType.DMA((4,)),
            *fine_scratch(bands, 3, 2 * EACH),
        ],
        out_specs=(hbm, hbm) + (vmem,) * 6,
        input_output_aliases={13 + k: 2 + k for k in range(6)},
    )
    return (flow, coarse_flow)


def solution(mesh):
    return jax.shard_map(
        local,
        mesh=mesh,
        in_specs=(P(None, "row", "col"), P(None, "row", "col"), P("row", "col", None)),
        out_specs=(P(None, "row", "col"), P(None, "row", "col")),
        check_vma=False,
    )
```

```python
import functools

import jax
import jax.numpy as jnp
from jax import lax
from jax.experimental import pallas as pl
from jax.experimental.pallas import tpu as pltpu
from jax.sharding import PartitionSpec as P

FACTOR = 8
MAXD = 4
BANDS = 4
STEPS = 3
LANES = 128
COLUMNS = 2 * LANES
HALF = 64
SUB = 8
DEPTH = 4
REACH = DEPTH + MAXD + 1
SLOT = 16
C_SECOND = 6
C_FIRST = 5
LEAD = 8
MARGIN = 48
EDGE = 46
GUARD = 8
HALO = 8
BEGIN = 40
EACH = MARGIN + 16
LIMIT = 0.3
ALPHA = 0.3

S_MID = 55
S_RIGHT = 110
S_LEFT = LANES - REACH
S_TURN = COLUMNS - S_RIGHT - LANES

E8 = 0
H8 = 64
E1 = 72
H1 = 80
META = 81
F4 = 88
CS = 120
ROW_MESSAGE = 144
H_BAND = 32

COARSE_A = REACH + DEPTH
COARSE_B = SLOT + REACH + DEPTH
SHIFT_R = 2 * SLOT + REACH + DEPTH
SHIFT_C = SHIFT_R + 1
EXISTS = SHIFT_R + 2


def lanes_of(rows=SUB):
    return lax.broadcasted_iota(jnp.int32, (rows, LANES), 1)


def lanes_like(x):
    return lax.broadcasted_iota(jnp.int32, x.shape, 1)


def turn(x, amount):
    amount = amount % LANES
    return x if amount == 0 else pltpu.roll(x, amount, 1)


def turn_back(x, shift):
    return pltpu.roll(x, lax.rem(LANES - shift, LANES), 1)


def split_dot(x, exact):
    high = x.astype(jnp.bfloat16)
    rest = x - high.astype(jnp.float32)
    middle = rest.astype(jnp.bfloat16)
    low = (rest - middle.astype(jnp.float32)).astype(jnp.bfloat16)
    parts = [jnp.dot(part, exact, preferred_element_type=jnp.float32) for part in (low, middle, high)]
    return parts[0] + parts[1] + parts[2]


def scalar_at(ref, row, lane):
    return ref[row : row + 1, lane : lane + 1][0, 0]


def int_at(ref, row, lane):
    return scalar_at(ref, row, lane).astype(jnp.int32)


def is_even(axis, like):
    return jnp.broadcast_to(lax.axis_index(axis) % 2, like.shape) == 0


def without_ends(message, axis, count):
    place = jnp.broadcast_to(lax.axis_index(axis), message.shape)
    return jnp.where((place > 0) & (place < count - 1), message[...], 0.0)


def staggered(items, compute, store, depth):
    pending = []
    for item in items:
        pending.append((item, compute(item)))
        if len(pending) > depth:
            store(*pending.pop(0))
    for entry in pending:
        store(*entry)


def aligned(row):
    return pl.ds(pl.multiple_of(row, SUB), SUB)


def pack_images(to_right, seconds, firsts, shift_rows, shift_cols):
    bands, height, _ = seconds[0].shape
    second, first = seconds[int(to_right)], firsts[int(to_right)]
    second_from = LANES - REACH if to_right else 0
    first_from = LANES - DEPTH if to_right else 0
    length = height // 2
    lane = lanes_of(length)
    packed = jnp.zeros((length, LANES), jnp.float32)
    for half in range(2):
        rows = slice(half * length, (half + 1) * length)
        for band in range(bands):
            at = half * HALF + band * SLOT
            packed = jnp.where(lane >= at, turn(second[band, rows, :], at - second_from), packed)
            packed = jnp.where(lane >= at + REACH, turn(first[band, rows, :], at + REACH - first_from), packed)
            if band == 2:
                at = half * HALF
                packed = jnp.where(lane >= at + SHIFT_R, shift_rows, packed)
                packed = jnp.where(lane >= at + SHIFT_C, shift_cols, packed)
                packed = jnp.where(lane >= at + EXISTS, 1.0, packed)
    return packed


def pack_means(packed, to_right, means):
    length = packed.shape[0]
    start = LEAD + COLUMNS // FACTOR - C_SECOND if to_right else LEAD
    lane = lanes_of(length)
    for half in range(2):
        cells = means[half * length : (half + 1) * length]
        for at, first in ((half * HALF + COARSE_A, start), (half * HALF + COARSE_B, start + 3)):
            packed = jnp.where((lane >= at) & (lane < at + 3), turn(cells, at - first), packed)
    return packed


def column_meta(message):
    return (int_at(message, 0, SHIFT_R), int_at(message, 0, SHIFT_C)), scalar_at(message, 0, EXISTS)


def strip_second(base, from_left, from_right, rows, half, band):
    at = half * HALF + band * SLOT
    lane = lanes_like(base)
    cells = jnp.where(lane >= S_RIGHT, turn(from_right[rows, :], S_RIGHT - at), base)
    return jnp.where(lane >= S_LEFT, turn(from_left[rows, :], S_LEFT - at), cells)


def strip_first(base, from_left, from_right, rows, half, band):
    at = half * HALF + band * SLOT + REACH
    lane = lanes_like(base)
    cells = jnp.where(lane >= S_RIGHT, turn(from_right[rows, :], S_RIGHT - at), base)
    return jnp.where(lane >= S_LEFT, turn(from_left[rows, :], LANES - DEPTH - at), cells)


def strip_halo(base, beside, band, start, count):
    at = band * H_BAND + start
    lane = lanes_like(base)
    cells = jnp.where(lane >= S_RIGHT, turn(beside, S_RIGHT - at), base)
    return jnp.where(lane >= S_LEFT, turn(beside, LANES - count - at - SLOT), cells)


def strip_own(planes):
    return jnp.where(lanes_like(planes[0]) < S_MID, planes[0], turn(planes[1], -S_TURN))


def first_kernel(
    second_hbm, first_hbm, shifts_hbm, second_0, second_1, first_0, first_1, coarse, swap_0, swap_1, own_meta,
    shifts, sems, shift_sem,
):
    seconds, firsts = (second_0, second_1), (first_0, first_1)
    bands, height, _ = second_0.shape
    width = COLUMNS
    coarse_height = height // FACTOR
    lane = lanes_of()
    get_shifts = pltpu.make_async_copy(shifts_hbm, shifts, shift_sem)
    get_shifts.start()
    copies = []
    for image, (source, refs) in enumerate(((second_hbm, seconds), (first_hbm, firsts))):
        for band in range(bands):
            for tile, ref in enumerate(refs):
                copy = pltpu.make_async_copy(
                    source.at[band, :, pl.ds(tile * LANES, LANES)], ref.at[band], sems.at[image, band, tile]
                )
                copy.start()
                copies.append((image * bands + band, tile, ref, band, copy))
    cell = lax.broadcasted_iota(jnp.int32, (width, LANES), 0)
    place = lax.broadcasted_iota(jnp.int32, (width, LANES), 1)
    weights = jnp.where(place - LEAD == cell // FACTOR, 1.0 / (FACTOR * FACTOR), 0.0).astype(jnp.bfloat16)
    sums = {}
    for group in (copies[: len(copies) // 2], copies[len(copies) // 2 :]):
        for *_, copy in group:
            copy.wait()
        for plane, tile, ref, band, _ in group:
            parts = [ref[band, pl.ds(k, coarse_height, stride=FACTOR), :] for k in range(FACTOR)]
            while len(parts) > 1:
                parts = [x + y for x, y in zip(parts[::2], parts[1::2])]
            sums[plane, tile] = parts[0]
    sums = [jnp.concatenate([sums[plane, tile] for tile in range(2)], axis=1) for plane in range(2 * bands)]
    get_shifts.wait()
    shift_rows = shifts[0, 0, 0].astype(jnp.float32)
    shift_cols = shifts[0, 0, 1].astype(jnp.float32)
    packed = [pack_images(to_right, seconds, firsts, shift_rows, shift_cols) for to_right in (False, True)]
    means = split_dot(jnp.concatenate(sums, axis=0), weights)
    to_left, to_right = [pack_means(packed[side], bool(side), means) for side in range(2)]
    coarse[...] = means
    own_meta[...] = jnp.where(lane < HALF, shift_rows, shift_cols)
    even = is_even("col", swap_0)
    swap_0[...] = jnp.where(even, to_right, to_left)
    swap_1[...] = jnp.where(even, to_left, to_right)


def message_kernel(
    count, coarse, own_meta, got_1, got_0, up_part, down_part, _whole, swap_0, swap_1, from_left, from_right, wide
):
    other = without_ends(got_1, "col", count)
    even = is_even("col", got_0)
    from_right[...] = jnp.where(even, got_0[...], other)
    from_left[...] = jnp.where(even, other, got_0[...])
    planes_coarse, coarse_height, _ = wide.shape
    bands = planes_coarse // 2
    end = from_left.shape[0]
    coarse_width = COLUMNS // FACTOR
    lane = lanes_of()
    wides = []
    for plane in range(planes_coarse):
        half, block = divmod(plane, planes_coarse // 2)
        for step in range(coarse_height // SUB):
            own = slice(plane * coarse_height + step * SUB, plane * coarse_height + (step + 1) * SUB)
            rows = slice(block * coarse_height + step * SUB, block * coarse_height + (step + 1) * SUB)
            at = half * HALF
            left = from_left[rows, :]
            right = from_right[rows, :]
            start = LEAD - C_SECOND
            cells = turn(left, start - at - COARSE_A)
            cells = jnp.where(lane >= start + 3, turn(left, start + 3 - at - COARSE_B), cells)
            cells = jnp.where(lane >= LEAD, coarse[own, :], cells)
            start = LEAD + coarse_width
            cells = jnp.where(lane >= start, turn(right, start - at - COARSE_A), cells)
            cells = jnp.where(lane >= start + 3, turn(right, start + 3 - at - COARSE_B), cells)
            wides.append((plane, step, cells))
    for plane, step, cells in wides:
        wide[plane, step * SUB : (step + 1) * SUB, :] = cells
    row = lax.broadcasted_iota(jnp.int32, (SUB, LANES), 0)
    meta = jnp.where(lane < 16, own_meta[...], jnp.where(lane < 32, turn(own_meta[...], HALF), 1.0))
    for message, at in ((from_left, 48), (from_right, 80)):
        first_rows = message[0:SUB, :]
        rows = jnp.broadcast_to(first_rows[:, SHIFT_R : SHIFT_R + 1], (SUB, LANES))
        cols = jnp.broadcast_to(first_rows[:, SHIFT_C : SHIFT_C + 1], (SUB, LANES))
        meta = jnp.where(lane >= at, rows, meta)
        meta = jnp.where(lane >= at + 16, cols, meta)

    def beside(rows, half):
        left = from_left[rows, :]
        right = from_right[rows, :]
        cells = jnp.zeros((SUB, LANES), jnp.float32)
        for band in range(bands):
            at = half * HALF + band * SLOT
            cells = jnp.where(lane >= band * H_BAND, turn(right, band * H_BAND - at), cells)
            cells = jnp.where(lane >= band * H_BAND + SLOT, turn(left, band * H_BAND + SLOT - at), cells)
        return cells

    even = is_even("row", meta)
    parts = []
    for part, half, near, next_rows, row_of in (
        (up_part, 0, slice(0, 8), slice(8, 16), 0),
        (down_part, 1, slice(end - 8, end), slice(end - 16, end - 8), 7),
    ):
        eight = beside(near, half)
        one = beside(next_rows, half)
        one = jnp.broadcast_to(one[row_of : row_of + 1], (SUB, LANES))
        coarse_rows = []
        for band in range(bands):
            rows = slice(0, C_SECOND) if half == 0 else slice(coarse_height - C_SECOND, coarse_height)
            second = wide[band, rows, :]
            first = turn(wide[bands + band, rows, :], HALF)
            coarse_rows.append(jnp.where(lanes_like(second) < HALF, second, first))
        parts.append([
            (part[E8:H8, :], E8), (eight, H8), (part[E1:H1, :], E1), (jnp.where(row == 0, one, meta), H1),
            (part[F4:CS, :], F4), *[(x, CS + k * C_SECOND) for k, x in enumerate(coarse_rows)],
        ])
    for (up, at), (down, _) in zip(*parts):
        even = is_even("row", up)
        swap_0[at : at + up.shape[0], :] = jnp.where(even, down, up)
        swap_1[at : at + up.shape[0], :] = jnp.where(even, up, down)


def coarse_flow_of(second, first, mask):
    def along_rows(x):
        return pltpu.roll(x, x.shape[0] - 1, 0) - pltpu.roll(x, 1, 0)

    def along_cols(x):
        return pltpu.roll(x, LANES - 1, 1) - pltpu.roll(x, 1, 1)

    bands = BANDS
    size = second.shape[0] // bands
    grad_rows = 0.125 * along_rows(second)
    grad_cols = 0.125 * along_cols(second)
    offset = 0.25 * (second - first)
    data = jnp.clip(offset, -LIMIT, LIMIT)

    def pull(grads):
        terms = data * grads
        return sum(terms[k * size : (k + 1) * size] for k in range(bands))

    def tall(x):
        return jnp.concatenate([x] * bands, axis=0)

    flow = [-mask * pull(grad_rows), -mask * pull(grad_cols)]
    extrapolated = [2.0 * x for x in flow]
    dual_rows = [0.0, 0.0]
    dual_cols = [0.0, 0.0]
    for step in range(1, STEPS):
        changes = [(along_rows(x), along_cols(x)) for x in extrapolated]
        data = data + offset + grad_rows * tall(extrapolated[0]) + grad_cols * tall(extrapolated[1])
        data = jnp.clip(data, -LIMIT, LIMIT)
        for c in range(2):
            rows = dual_rows[c] + changes[c][0]
            cols = dual_cols[c] + changes[c][1]
            norm = jnp.maximum(rows * rows + cols * cols, 1e-30)
            scale = jnp.minimum(mask, (8.0 * ALPHA) * lax.rsqrt(norm))
            dual_rows[c] = rows * scale
            dual_cols[c] = cols * scale
        pulls = [pull(grad_rows), pull(grad_cols)]
        for c in range(2):
            divergence = along_rows(dual_rows[c]) + along_cols(dual_cols[c])
            following = flow[c] + mask * ((1.0 / 64.0) * divergence - pulls[c])
            extrapolated[c] = 2.0 * following - flow[c]
            flow[c] = following
    return flow


def columns_of_planes(planes):
    whole = lax.broadcasted_iota(jnp.int32, (LANES, COLUMNS), 1)
    lane = lax.broadcasted_iota(jnp.int32, (LANES, LANES), 1)
    strip = jnp.where(lane < S_MID, lane, jnp.where(lane < S_LEFT, lane + (COLUMNS - S_RIGHT), lane - LANES))
    return jnp.concatenate([x for x, wanted in ((whole, "whole"), (strip, "strip")) if wanted in planes], axis=1)


def upsample(flow, planes, target):
    column = columns_of_planes(planes)
    source = lax.broadcasted_iota(jnp.int32, column.shape, 0)
    spread = jnp.where(source - LEAD == lax.shift_right_arithmetic(column, 3), float(FACTOR), 0.0).astype(jnp.bfloat16)
    rows = flow[0].shape[0]
    wide = split_dot(jnp.concatenate(flow, axis=0), spread)
    for c in range(2):
        for tile in range(column.shape[1] // LANES):
            target[c, tile] = wide[c * rows : (c + 1) * rows, tile * LANES : (tile + 1) * LANES]


def repeat_rows(spread, initial, cells):
    for c in range(2):
        for tile in range(initial.shape[1]):
            rows = [jnp.broadcast_to(spread[c, tile, cell : cell + 1, :], (SUB, LANES)) for cell in cells]
            initial[c, tile, GUARD : GUARD + SUB * len(cells), :] = jnp.concatenate(rows, axis=0)


def shift_whole(here, shift):
    turned = [turn_back(x, shift) for x in here]
    lane = lanes_like(here[0])
    return [
        jnp.where(lane + shift >= LANES, turned[1], turned[0]),
        jnp.where(lane + shift < 0, turned[0], turned[1]),
    ]


def edge_lanes(rows):
    lane = lanes_of(rows)
    return lane == LANES - 1, lane == 0


def columns_whole(fields, edges):
    last, first = edges
    ahead = [pltpu.roll(x, LANES - 1, 1) for x in fields]
    behind = [pltpu.roll(x, 1, 1) for x in fields]
    return [
        jnp.where(last, ahead[1], ahead[0]) - behind[0],
        ahead[1] - jnp.where(first, behind[0], behind[1]),
    ]


def columns_strip(field):
    return pltpu.roll(field, LANES - 1, 1) - pltpu.roll(field, 1, 1)


def strip_windows(window, centre, right, left):
    own = turn_back(window(centre[0]), centre[1])
    beyond_left = turn_back(window(left[0]), left[1])
    beyond_right = turn_back(window(right[0]), right[1])
    lane = lanes_like(own)
    beyond = jnp.where((lane >= S_LEFT) | (lane < S_MID), beyond_left, beyond_right)
    is_beyond = lane >= S_RIGHT
    return jnp.where(is_beyond, beyond, own), jnp.where(is_beyond, columns_strip(beyond), columns_strip(own))


def fine_steps(
    rows_total, chunk, columns, initial, extrap, dual_rows, dual_cols, change, dual_data,
    offsets, grads_rows, grads_cols, data_row, masks_of, result, done=lambda k: None,
):
    planes = len(offsets)
    bands = offsets[0].shape[0]
    chunks = rows_total // chunk
    tiles = range(planes)

    for step in range(STEPS):
        source = initial if step == 0 else extrap
        final = step == STEPS - 1

        def dual(item, source=source, step=step):
            k, c = item
            row = GUARD + k * chunk
            at, own = pl.ds(row, chunk), pl.ds(k * chunk, chunk)
            masks = masks_of(own)
            along = columns([source[c, tile, at, :] for tile in tiles])
            values = []
            for tile in tiles:
                rows = source[c, tile, pl.ds(row + 1, chunk), :] - source[c, tile, pl.ds(row - 1, chunk), :]
                cols = along[tile]
                if step > 0:
                    rows = rows + dual_rows[c, tile, at, :]
                    cols = cols + dual_cols[c, tile, own, :]
                norm = jnp.maximum(rows * rows + cols * cols, 1e-30)
                scale = jnp.minimum(masks[tile], (8.0 * ALPHA) * lax.rsqrt(norm))
                values.append((rows * scale, cols * scale))
            return values

        def store_dual(item, values):
            k, c = item
            for tile, (rows, cols) in enumerate(values):
                dual_rows[c, tile, pl.ds(GUARD + k * chunk, chunk), :] = rows
                dual_cols[c, tile, pl.ds(k * chunk, chunk), :] = cols

        staggered([(k, c) for k in range(chunks) for c in range(2)], dual, store_dual, 1)
        along_of = {}

        def primal(item, step=step, final=final, along_of=along_of):
            k, tile = item
            row = GUARD + k * chunk
            at, own, data = pl.ds(row, chunk), pl.ds(k * chunk, chunk), pl.ds(data_row(k), chunk)
            if k not in along_of:
                along_of[k] = [columns([dual_cols[c, t, own, :] for t in tiles]) for c in range(2)]
            mask = masks_of(own)[tile]
            start = [initial[c, tile, at, :] for c in range(2)]
            if step > 0:
                moved = [extrap[c, tile, at, :] - start[c] for c in range(2)]
            pulls = [None, None]
            duals = []
            for band in range(bands):
                gradient = (grads_rows[tile][band, data, :], grads_cols[tile][band, data, :])
                value = offsets[tile][band, data, :]
                if step > 0:
                    value = value + gradient[0] * moved[0] + gradient[1] * moved[1]
                    value = value + dual_data[band, tile, own, :]
                value = jnp.clip(value, -LIMIT, LIMIT)
                duals.append(value)
                for c in range(2):
                    term = value * gradient[c]
                    pulls[c] = term if pulls[c] is None else pulls[c] + term
            flows, nexts = [], []
            for c in range(2):
                divergence = (
                    dual_rows[c, tile, pl.ds(row + 1, chunk), :]
                    - dual_rows[c, tile, pl.ds(row - 1, chunk), :]
                    + along_of[k][c][tile]
                )
                moving = (mask * (1.0 / 64.0)) * divergence - pulls[c]
                total = moving if step == 0 else change[c, tile, own, :] + moving
                flows.append(start[c] + total if final else total)
                nexts.append(None if final else start[c] + (total + moving))
            return flows, nexts, duals

        def store_primal(item, results, final=final):
            k, tile = item
            flows, nexts, duals = results
            own = pl.ds(k * chunk, chunk)
            for c in range(2):
                if final:
                    result[c, tile, own, :] = flows[c]
                else:
                    change[c, tile, own, :] = flows[c]
                    extrap[c, tile, pl.ds(GUARD + k * chunk, chunk), :] = nexts[c]
            if final:
                if tile == planes - 1:
                    done(k)
            else:
                for band in range(bands):
                    dual_data[band, tile, own, :] = duals[band]

        staggered([(k, tile) for k in range(chunks) for tile in tiles], primal, store_primal, 1)


def clear_guards(*refs):
    for ref in refs:
        rows = ref.shape[2]
        zero = jnp.zeros((GUARD, LANES), jnp.float32)
        for c in range(2):
            for tile in range(ref.shape[1]):
                ref[c, tile, 0:GUARD, :] = zero
                ref[c, tile, rows - GUARD : rows, :] = zero


def fine_scratch(bands, planes, rows):
    guarded = pltpu.VMEM((2, planes, rows + 2 * GUARD, LANES), jnp.float32)
    plain = pltpu.VMEM((2, planes, rows, LANES), jnp.float32)
    return [guarded, guarded, guarded, plain, plain, pltpu.VMEM((bands, planes, rows, LANES), jnp.float32)]


def pieces(bands, height, rows):
    assert (height - 2 * SUB) % rows == 0
    return [(band, row) for row in range(SUB, height - SUB, rows) for band in range(bands)]


def whole_terms_kernel(
    second_0, second_1, first_0, first_1, coarse, own_meta,
    offset, grad_rows, grad_cols, initial, strip_e, strip_f, up, down, moved, spread,
):
    seconds, firsts = (second_0, second_1), (first_0, first_1)
    bands, height, _ = second_0.shape
    block = 120
    coarse_height = coarse.shape[0] // (2 * bands)
    shift_rows, shift_cols = scalar_at(own_meta, 0, 0), scalar_at(own_meta, 0, HALF)
    centre = (shift_rows.astype(jnp.int32), shift_cols.astype(jnp.int32))
    def windows(band, row, rows):
        here = [ref[band, pl.ds(row + centre[0], rows), :].reshape(-1, LANES) for ref in seconds]
        return shift_whole(here, centre[1])

    flow = coarse_flow_of(coarse[0 : bands * coarse_height, :], coarse[bands * coarse_height :, :], 1.0)
    upsample(flow, ("whole",), spread)

    ends = [(row, windows(slice(None), row, SUB)) for row in (SUB // 2, height - SUB - SUB // 2)]
    for row, values in ends:
        for tile in range(2):
            moved[tile, :, row : row + SUB, :] = values[tile].reshape(bands, SUB, LANES)

    edges = edge_lanes(block)

    def values_of(item):
        band, row = item
        values = windows(band, row, block)
        along = columns_whole(values, edges)
        own = [ref[band, row : row + block, :] for ref in firsts]
        return values, [0.25 * (x - y) for x, y in zip(values, own)], [0.125 * x for x in along]

    def store_values(item, results):
        band, row = item
        values, offsets, gradients = results
        data = slice(row + HALO, row + HALO + block)
        for tile in range(2):
            moved[tile, band, row : row + block, :] = values[tile]
            offset[tile, band, data, :] = offsets[tile]
            grad_cols[tile, band, data, :] = gradients[tile]

    staggered(pieces(bands, height, block), values_of, store_values, 1)

    def strips_of(item):
        band, row = item
        rows = slice(row, row + LANES)
        return strip_own([ref[band, rows, :] for ref in seconds]), strip_own([ref[band, rows, :] for ref in firsts])

    def store_strips(item, results):
        band, row = item
        strip_e[band, row : row + LANES, :], strip_f[band, row : row + LANES, :] = results

    staggered([(band, row) for band in range(bands) for row in range(0, height, LANES)], strips_of, store_strips, 1)

    def gradient_of(item):
        band, row = item
        return [
            0.125 * (moved[tile, band, pl.ds(row + 1, 120), :] - moved[tile, band, pl.ds(row - 1, 120), :])
            for tile in range(2)
        ]

    def store_gradient(item, results):
        band, row = item
        for tile in range(2):
            grad_rows[tile, band, row + HALO : row + HALO + 120, :] = results[tile]

    staggered(pieces(bands, height, 120), gradient_of, store_gradient, 1)

    clear_guards(initial)
    rows_total = initial.shape[2] - 2 * GUARD
    repeat_rows(spread, initial, [BEGIN // FACTOR + k for k in range(rows_total // SUB)])

    parts = []
    for band in range(bands):
        for second, first in zip(seconds, firsts):
            parts.append((
                second[band, 0:16, :], first[band, 0:8, :],
                second[band, height - 16 : height, :], first[band, height - 8 : height, :],
            ))
    for k, (second_top, first_top, second_end, first_end) in enumerate(parts):
        up[E8 + 8 * k : E8 + 8 * k + 8, :] = second_top[0:8]
        up[E1 + k : E1 + k + 1, :] = second_top[8:9]
        up[F4 + 4 * k : F4 + 4 * k + 4, :] = first_top[0:4]
        down[E8 + 8 * k : E8 + 8 * k + 8, :] = second_end[8:16]
        down[E1 + k : E1 + k + 1, :] = second_end[7:8]
        down[F4 + 4 * k : F4 + 4 * k + 4, :] = first_end[4:8]
    for target in (up, down):
        for start, end in ((H8, E1), (H1, F4), (CS, ROW_MESSAGE)):
            target[start:end, :] = jnp.zeros((end - start, LANES), jnp.float32)


def whole_steps_kernel(
    initial, offset, grad_rows, grad_cols, result, extrap, dual_rows, dual_cols, change, dual_data
):
    rows_total = result.shape[2]
    clear_guards(extrap, dual_rows)
    chunk = 88
    edges = edge_lanes(chunk)
    fine_steps(
        rows_total, chunk, lambda fields: columns_whole(fields, edges),
        initial, extrap, dual_rows, dual_cols, change, dual_data,
        *[[ref.at[tile] for tile in range(2)] for ref in (offset, grad_rows, grad_cols)],
        lambda k: HALO + BEGIN + k * chunk, lambda own: (1.0, 1.0), result,
    )


def strip_kernel(
    strip_e, strip_f, from_left, from_right, wide, own_meta, whole,
    middle, strip_out, first_ends, offset, grad_rows, grad_cols,
    moved, result, spread, initial, extrap, dual_rows, dual_cols, change, dual_data,
):
    bands, height, _ = strip_e.shape
    block = 120
    coarse_height = height // FACTOR
    coarse_width = COLUMNS // FACTOR
    rows_total = height - 2 * BEGIN
    lane = lanes_of()
    centre = (int_at(own_meta, 0, 0), int_at(own_meta, 0, HALF))
    right, has_right = column_meta(from_right)
    left, has_left = column_meta(from_left)
    exists = jnp.where(lane < S_RIGHT, 1.0, jnp.where(lane < S_LEFT, has_right, has_left))

    def tall_factor(rows):
        return 0.125 * jnp.concatenate([exists] * (rows // SUB), axis=0)

    mask = jnp.where(lane < LEAD, has_left, jnp.where(lane < LEAD + coarse_width, 1.0, has_right))
    mask = jnp.concatenate([mask] * (coarse_height // SUB), axis=0)
    cells = [wide[k * bands : (k + 1) * bands].reshape(bands * coarse_height, LANES) for k in range(2)]
    flow = coarse_flow_of(*cells, mask)
    upsample(flow, ("strip",), spread)

    def halves(row, rows):
        half = row // (height // 2)
        start = row - half * (height // 2)
        return half, slice(start, start + rows)

    def second_of(item):
        band, row = item
        half, message = halves(row, LANES)
        return strip_second(strip_e[band, row : row + LANES, :], from_left, from_right, message, half, band)

    def store_second(item, value):
        band, row = item
        strip_out[band, row : row + LANES, :] = value

    staggered([(band, row) for row in range(0, height, LANES) for band in range(bands)], second_of, store_second, 1)

    def first_of(band, row, rows):
        half, message = halves(row, rows)
        return strip_first(strip_f[band, row : row + rows, :], from_left, from_right, message, half, band)

    firsts = [(end, band, first_of(band, (0, height - SUB)[end], SUB)) for end in range(2) for band in range(bands)]
    for end, band, value in firsts:
        first_ends[end, band] = value

    def windows(band, row, rows):
        return strip_windows(
            lambda shift: strip_out[band, pl.ds(row + shift, rows), :].reshape(-1, LANES), centre, right, left
        )

    ends = [(row, windows(slice(None), row, SUB)[0]) for row in (SUB // 2, height - SUB - SUB // 2)]
    for row, value in ends:
        moved[:, row : row + SUB, :] = value.reshape(bands, SUB, LANES)

    factor = tall_factor(block)

    def values_of(item):
        band, row = item
        value, along = windows(band, row, block)
        return value, 0.25 * (value - first_of(band, row, block)), factor * along

    def store_values(item, results):
        band, row = item
        data = slice(row + HALO, row + HALO + block)
        moved[band, row : row + block, :], offset[band, data, :], grad_cols[band, data, :] = results

    staggered(pieces(bands, height, block), values_of, store_values, 1)

    def gradient_of(item):
        band, row = item
        return factor * (moved[band, pl.ds(row + 1, block), :] - moved[band, pl.ds(row - 1, block), :])

    def store_gradient(item, value):
        band, row = item
        grad_rows[band, row + HALO : row + HALO + block, :] = value

    staggered(pieces(bands, height, block), gradient_of, store_gradient, 1)

    clear_guards(initial, extrap, dual_rows)
    repeat_rows(spread, initial, [BEGIN // FACTOR + k for k in range(rows_total // SUB)])

    chunk = 176
    masks = jnp.concatenate([exists] * (chunk // SUB), axis=0)
    fine_steps(
        rows_total, chunk, lambda fields: [columns_strip(fields[0])],
        initial, extrap, dual_rows, dual_cols, change, dual_data, [offset], [grad_rows], [grad_cols],
        lambda k: HALO + BEGIN + k * chunk, lambda own: (masks,), result,
    )
    join(whole, result.at[:, 0], middle, slice(0, rows_total))


def join(whole, strip, target, rows):
    lane = lanes_of(rows.stop - rows.start)
    values = []
    for c in range(2):
        edge = strip[c, rows, :]
        start = jnp.where(lane < EDGE, edge, whole[c, 0, rows, :])
        values.append((start, jnp.where(lane >= LANES - EDGE, turn(edge, S_TURN), whole[c, 1, rows, :])))
    for c in range(2):
        target[c, rows, 0:LANES], target[c, rows, LANES:COLUMNS] = values[c]


def outer_kernel(
    count, second_0, second_1, first_0, first_1, strip_e, first_ends, from_left, from_right, wide, got_1, got_0, middle, own_meta,
    _wo, _wr, _wc, _so, _sr, _sc,
    flow_out, coarse_out, whole_offset, whole_rows, whole_cols, strip_offset, strip_rows, strip_cols,
    from_up, from_down, extended, tall, spread, masks, result, joined, coarse_result, sems,
    initial, extrap, dual_rows, dual_cols, change, dual_data,
):
    bands, height, _ = second_0.shape
    coarse_height = height // FACTOR
    coarse_width = COLUMNS // FACTOR
    rows_total = 2 * EACH
    lane = lanes_of()

    put_middle = pltpu.make_async_copy(
        middle.at[:, pl.ds(MARGIN - BEGIN, height - 2 * MARGIN), :],
        flow_out.at[:, pl.ds(MARGIN, height - 2 * MARGIN), :],
        sems.at[0],
    )
    put_middle.start()

    other = without_ends(got_1, "row", count)
    even = is_even("row", got_0)
    from_down[...] = jnp.where(even, got_0[...], other)
    from_up[...] = jnp.where(even, other, got_0[...])

    own = (int_at(own_meta, 0, 0), int_at(own_meta, 0, HALF))
    own_right, has_right = column_meta(from_right)
    own_left, has_left = column_meta(from_left)
    has_up = scalar_at(from_up, META, 32)
    has_down = scalar_at(from_down, META, 32)
    exists = jnp.where(lane < S_RIGHT, 1.0, jnp.where(lane < S_LEFT, has_right, has_left))

    def trio(message):
        return (
            (int_at(message, META, 0), int_at(message, META, 16)),
            (int_at(message, META, 80), int_at(message, META, 96)),
            (int_at(message, META, 48), int_at(message, META, 64)),
        )

    above = trio(from_up)
    below = trio(from_down)

    zero = jnp.zeros((SUB, LANES), jnp.float32)
    tall_rows = coarse_height + 2 * LEAD
    parts = []
    fill = jnp.zeros((LEAD - C_SECOND, LANES), jnp.float32)
    for plane in range(2 * bands):
        at = CS + C_SECOND * (plane % bands)
        ends = [turn(message[at : at + C_SECOND, :], HALF * (plane // bands)) for message in (from_up, from_down)]
        parts.append([fill, ends[0], wide[plane], ends[1], fill])
    for plane, values in enumerate(parts):
        tall[plane] = jnp.concatenate(values, axis=0)
    across = jnp.where(lane < LEAD, has_left, jnp.where(lane < LEAD + coarse_width, 1.0, has_right))
    mask = jnp.concatenate([across * has_up] + [across] * (coarse_height // SUB) + [across * has_down], axis=0)
    cells = [tall[k * bands : (k + 1) * bands].reshape(bands * tall_rows, LANES) for k in range(2)]
    flow = coarse_flow_of(*cells, mask)
    for c in range(2):
        coarse_result[c] = turn(flow[c][LEAD : LEAD + coarse_height], -LEAD)[:, :coarse_width]
    put_coarse = pltpu.make_async_copy(coarse_result, coarse_out, sems.at[1])
    put_coarse.start()
    upsample(flow, ("whole", "strip"), spread)
    clear_guards(initial, extrap, dual_rows)
    each = EACH // SUB
    repeat_rows(
        spread, initial,
        [LEAD - 1 + k for k in range(each)] + [tall_rows - LEAD + 1 - each + k for k in range(each)],
    )

    for end in range(2):
        message = (from_up, from_down)[end]
        beside = message[H8 : H8 + 8, :]
        beside_one = jnp.broadcast_to(message[H1 : H1 + 1, :], (SUB, LANES))
        parts = []
        for band in range(bands):
            eights = [message[E8 + 8 * k : E8 + 8 * k + 8, :] for k in (2 * band, 2 * band + 1)]
            ones = [jnp.broadcast_to(message[E1 + k : E1 + k + 1, :], (SUB, LANES)) for k in (2 * band, 2 * band + 1)]
            eights.append(strip_halo(strip_own(eights), beside, band, 0, REACH))
            ones.append(strip_halo(strip_own(ones), beside_one, band, 0, REACH))
            for tile, (eight, one) in enumerate(zip(eights, ones)):
                source = (second_0, second_1, strip_e)[tile]
                if end == 0:
                    parts.append((tile, band, [one, eight, source[band, 0:24, :]]))
                else:
                    parts.append((tile, band, [source[band, height - 24 : height, :], eight, one]))
        for tile, band, values in parts:
            extended[end, tile, band] = jnp.concatenate(values, axis=0)
    edges = edge_lanes(bands * SUB)
    rows_data = whole_offset.shape[2]
    exists_tall = jnp.concatenate([exists] * bands, axis=0)

    def rows_of(halo, end):
        if halo:
            return slice(0, SUB) if end == 0 else slice(rows_data - SUB, rows_data)
        return slice(HALO, HALO + SUB) if end == 0 else slice(rows_data - HALO - SUB, rows_data - HALO)

    def values_of(item):
        halo, end = item
        message = (from_up, from_down)[end]
        base = (SUB, 3 * SUB)[end] if halo else 2 * SUB
        shifts = (above, below)[end] if halo else (own, own_right, own_left)
        factor = 0.125 * (has_up, has_down)[end] if halo else 0.125

        def here(tile, shift):
            return extended[end, tile, :, pl.ds(base + shift, SUB), :].reshape(-1, LANES)

        def down_up(tile, shift):
            return here(tile, shift + 1) - here(tile, shift - 1)

        own_rows = slice(0, SUB) if end == 0 else slice(height - SUB, height)
        if halo:
            firsts = [[], [], []]
            for band in range(bands):
                eights = []
                for k in (2 * band, 2 * band + 1):
                    four = message[F4 + 4 * k : F4 + 4 * k + 4, :]
                    eights.append(jnp.concatenate([four, four], axis=0))
                eights.append(strip_halo(strip_own(eights), message[H8 : H8 + 8, :], band, REACH, DEPTH))
                for tile in range(3):
                    firsts[tile].append(eights[tile])
            firsts = [jnp.concatenate(x, axis=0) for x in firsts]
        else:
            firsts = [x.reshape(-1, LANES) for x in (first_0[:, own_rows, :], first_1[:, own_rows, :], first_ends[end])]
        centre = shifts[0]
        values = shift_whole([here(tile, centre[0]) for tile in range(2)], centre[1])
        changes = shift_whole([down_up(tile, centre[0]) for tile in range(2)], centre[1])
        along = columns_whole(values, edges)
        value, across_cols = strip_windows(lambda shift: here(2, shift), *shifts)
        change_rows, _ = strip_windows(lambda shift: down_up(2, shift), *shifts)
        return (
            [0.25 * (x - y) for x, y in zip([*values, value], firsts)],
            [*[factor * x for x in changes], (factor * exists_tall) * change_rows],
            [*[factor * x for x in along], (factor * exists_tall) * across_cols],
        )

    def store_values(item, results):
        rows = rows_of(*item)
        for values, whole, strip in zip(
            results, (whole_offset, whole_rows, whole_cols), (strip_offset, strip_rows, strip_cols)
        ):
            values = [x.reshape(bands, SUB, LANES) for x in values]
            for tile in range(2):
                whole[tile, :, rows, :] = values[tile]
            strip[:, rows, :] = values[2]

    staggered([(halo, end) for halo in (True, False) for end in range(2)], values_of, store_values, 1)

    for i, value in enumerate((jnp.ones((SUB, LANES), jnp.float32), exists)):
        masks[i] = jnp.concatenate([value * has_up] + [value] * (rows_total // SUB - 2) + [value * has_down], axis=0)

    def masks_of(rows):
        whole = masks[0, rows, :]
        return (whole, whole, masks[1, rows, :])

    chunk = EACH
    edges = edge_lanes(chunk)
    puts = [
        pltpu.make_async_copy(
            joined.at[:, pl.ds(k * EACH + SUB, MARGIN), :],
            flow_out.at[:, pl.ds(k * (height - MARGIN), MARGIN), :],
            sems.at[2 + k],
        )
        for k in range(2)
    ]

    def finish(k):
        join(result, result.at[:, 2], joined, slice(k * EACH + SUB, k * EACH + SUB + MARGIN))
        puts[k].start()

    def data_row(k):
        return k * (rows_data - EACH)

    fine_steps(
        rows_total, chunk, lambda fields: columns_whole(fields[:2], edges) + [columns_strip(fields[2])],
        initial, extrap, dual_rows, dual_cols, change, dual_data,
        [whole_offset.at[0], whole_offset.at[1], strip_offset],
        [whole_rows.at[0], whole_rows.at[1], strip_rows],
        [whole_cols.at[0], whole_cols.at[1], strip_cols],
        data_row, masks_of, result, finish,
    )
    put_middle.wait()
    put_coarse.wait()
    for put in puts:
        put.wait()


def swap_with(message, axis, start):
    names = ("row", "col")
    sizes = [lax.axis_size(name) for name in names]
    along = names.index(axis)
    count, others = sizes[along], sizes[1 - along]

    def number(place, other):
        row, col = (place, other) if along == 0 else (other, place)
        return row * sizes[1] + col

    pairs = [(number(i, k), number(i + 1, k)) for i in range(start, count - 1, 2) for k in range(others)]
    if start:
        pairs += [(number(i, k), number(i, k + 1)) for i in (0, count - 1) for k in range(0, others, 2)]
    return lax.ppermute(message, names, pairs + [(j, i) for i, j in pairs])


def local(frame_first, frame_second, shifts):
    bands, height, width = frame_first.shape
    assert bands == 4 and width == COLUMNS and height % LANES == 0
    assert lax.axis_size("row") % 2 == 0 and lax.axis_size("col") % 2 == 0
    coarse_height = height // FACTOR
    coarse_width = width // FACTOR
    vmem = pl.BlockSpec(memory_space=pltpu.VMEM)
    hbm = pl.BlockSpec(memory_space=pltpu.HBM)
    tall_rows = coarse_height + 2 * LEAD
    inner_rows = height - 2 * BEGIN

    def shape(*sizes):
        return jax.ShapeDtypeStruct(sizes, jnp.float32)

    def scratch(*sizes):
        return pltpu.VMEM(sizes, jnp.float32)

    def call(kernel, name, arguments, outs, scratches=(), flops=1_000_000, **more):
        more = {"in_specs": [vmem] * len(arguments), "out_specs": (vmem,) * len(outs), **more}
        return pl.pallas_call(
            kernel,
            out_shape=tuple(outs),
            scratch_shapes=list(scratches),
            compiler_params=pltpu.CompilerParams(vmem_limit_bytes=24 * 1024 * 1024),
            cost_estimate=pl.CostEstimate(flops=flops, bytes_accessed=1_000_000, transcendentals=0),
            name=name,
            **more,
        )(*arguments)

    plane = shape(bands, height, LANES)
    column_message = shape(height // 2, LANES)
    row_message = shape(ROW_MESSAGE, LANES)
    whole_data = shape(2, bands, height + 2 * HALO, LANES)
    strip_data = shape(bands, height + 2 * HALO, LANES)

    *frames, coarse, swap_0, swap_1, own_meta = call(
        first_kernel,
        "means_and_message",
        [pltpu.with_memory_space_constraint(x, pltpu.HBM) for x in (frame_second, frame_first, shifts)],
        [*[plane] * 4, shape(2 * bands * coarse_height, LANES), column_message, column_message, shape(SUB, LANES)],
        [
            pltpu.SMEM((1, 1, 2), jnp.int32),
            pltpu.SemaphoreType.DMA((2, bands, 2)),
            pltpu.SemaphoreType.DMA,
        ],
        in_specs=[hbm] * 3,
    )
    got_1 = swap_with(swap_1, "col", 1)
    got_0 = swap_with(swap_0, "col", 0)

    *whole_terms, initial, strip_e, strip_f, up_part, down_part = call(
        whole_terms_kernel,
        "whole_terms",
        [*frames, coarse, own_meta],
        [
            *[whole_data] * 3, shape(2, 2, inner_rows + 2 * GUARD, LANES),
            plane, plane, row_message, row_message,
        ],
        [scratch(2, bands, height, LANES), scratch(2, 2, coarse_height, LANES)],
        flops=8_000_000,
    )
    (whole,) = call(
        whole_steps_kernel,
        "whole_steps",
        [initial, *whole_terms],
        [shape(2, 2, inner_rows, LANES)],
        fine_scratch(bands, 2, inner_rows)[1:],
        flops=20_000_000,
    )

    swap_0, swap_1, from_left, from_right, wide = call(
        functools.partial(message_kernel, lax.axis_size("col")),
        "row_messages",
        [coarse, own_meta, got_1, got_0, up_part, down_part, whole],
        [row_message, row_message, column_message, column_message, shape(2 * bands, coarse_height, LANES)],
    )
    got_1 = swap_with(swap_1, "row", 1)
    got_0 = swap_with(swap_0, "row", 0)

    middle, strip_e, first_ends, *strip_terms = call(
        strip_kernel,
        "strip",
        [strip_e, strip_f, from_left, from_right, wide, own_meta, whole],
        [shape(2, inner_rows, width), plane, shape(2, bands, SUB, LANES), *[strip_data] * 3],
        [
            scratch(bands, height, LANES),
            scratch(2, 1, inner_rows, LANES),
            scratch(2, 1, coarse_height, LANES),
            *fine_scratch(bands, 1, inner_rows),
        ],
        flops=16_000_000,
    )

    flow, coarse_flow, *_ = call(
        functools.partial(outer_kernel, lax.axis_size("row")),
        "outer_rows",
        [
            *frames, strip_e, first_ends, from_left, from_right, wide, got_1, got_0, middle, own_meta,
            *whole_terms, *strip_terms,
        ],
        [shape(2, height, width), shape(2, coarse_height, coarse_width), *[whole_data] * 3, *[strip_data] * 3],
        [
            scratch(ROW_MESSAGE, LANES),
            scratch(ROW_MESSAGE, LANES),
            scratch(2, 3, bands, 40, LANES),
            scratch(2 * bands, tall_rows, LANES),
            scratch(2, 3, tall_rows, LANES),
            scratch(2, 2 * EACH, LANES),
            scratch(2, 3, 2 * EACH, LANES),
            scratch(2, 2 * EACH, width),
            scratch(2, coarse_height, coarse_width),
            pltpu.SemaphoreType.DMA((4,)),
            *fine_scratch(bands, 3, 2 * EACH),
        ],
        out_specs=(hbm, hbm) + (vmem,) * 6,
        input_output_aliases={13 + k: 2 + k for k in range(6)},
    )
    return (flow, coarse_flow)


def solution(mesh):
    return jax.shard_map(
        local,
        mesh=mesh,
        in_specs=(P(None, "row", "col"), P(None, "row", "col"), P("row", "col", None)),
        out_specs=(P(None, "row", "col"), P(None, "row", "col")),
        check_vma=False,
    )
```

```python
import functools

import jax
import jax.numpy as jnp
from jax import lax
from jax.experimental import pallas as pl
from jax.experimental.pallas import tpu as pltpu
from jax.sharding import PartitionSpec as P

FACTOR = 8
MAXD = 4
BANDS = 4
STEPS = 3
LANES = 128
COLUMNS = 2 * LANES
HALF = 64
SUB = 8
DEPTH = 4
REACH = DEPTH + MAXD + 1
SLOT = 16
C_SECOND = 6
C_FIRST = 5
LEAD = 8
MARGIN = 48
EDGE = 46
GUARD = 8
HALO = 8
BEGIN = 40
EACH = MARGIN + 16
LIMIT = 0.3
ALPHA = 0.3
UNIT = 0.125 / ALPHA

S_MID = 55
S_RIGHT = 110
S_LEFT = LANES - REACH
S_TURN = COLUMNS - S_RIGHT - LANES

E8 = 0
H8 = 64
E1 = 72
H1 = 80
META = 81
F4 = 88
CS = 120
ROW_MESSAGE = 144
H_BAND = 32

COARSE_A = REACH + DEPTH
COARSE_B = SLOT + REACH + DEPTH
SHIFT_R = 2 * SLOT + REACH + DEPTH
SHIFT_C = SHIFT_R + 1
EXISTS = SHIFT_R + 2


def lanes_of(rows=SUB):
    return lax.broadcasted_iota(jnp.int32, (rows, LANES), 1)


def lanes_like(x):
    return lax.broadcasted_iota(jnp.int32, x.shape, 1)


def turn(x, amount):
    amount = amount % LANES
    return x if amount == 0 else pltpu.roll(x, amount, 1)


def turn_back(x, shift):
    return pltpu.roll(x, lax.rem(LANES - shift, LANES), 1)


def split_dot(x, exact):
    high = x.astype(jnp.bfloat16)
    rest = x - high.astype(jnp.float32)
    middle = rest.astype(jnp.bfloat16)
    low = (rest - middle.astype(jnp.float32)).astype(jnp.bfloat16)
    parts = [jnp.dot(part, exact, preferred_element_type=jnp.float32) for part in (low, middle, high)]
    return parts[0] + parts[1] + parts[2]


def scalar_at(ref, row, lane):
    return ref[row : row + 1, lane : lane + 1][0, 0]


def int_at(ref, row, lane):
    return scalar_at(ref, row, lane).astype(jnp.int32)


def is_even(axis, like):
    return jnp.broadcast_to(lax.axis_index(axis) % 2, like.shape) == 0


def without_ends(message, axis, count):
    place = jnp.broadcast_to(lax.axis_index(axis), message.shape)
    return jnp.where((place > 0) & (place < count - 1), message[...], 0.0)


def staggered(items, compute, store, depth, woven=None):
    pending = []
    for item in items:
        pending.append((item, compute(item)))
        if woven is not None:
            woven.advance()
        if len(pending) > depth:
            store(*pending.pop(0))
    for entry in pending:
        store(*entry)


class Woven:
    def __init__(self, stages):
        self.stages = stages
        self.result = None

    def advance(self):
        try:
            next(self.stages)
            return True
        except StopIteration as end:
            self.result = end.value if self.result is None else self.result
            return False

    def finish(self):
        while self.advance():
            pass
        return self.result


def pack_image(packed, to_right, planes, count, offset):
    bands, height, _ = planes[0].shape
    plane = planes[int(to_right)]
    start = LANES - count if to_right else 0
    length = height // 2
    lane = lanes_of(length)
    for half in range(2):
        for band in range(bands):
            at = half * HALF + band * SLOT + offset
            cells = turn(plane[band, half * length : (half + 1) * length, :], at - start)
            packed = cells if packed is None else jnp.where((lane >= at) & (lane < at + count), cells, packed)
    return packed


def pack_means(packed, to_right, means):
    length = packed.shape[0]
    start = LEAD + COLUMNS // FACTOR - C_SECOND if to_right else LEAD
    lane = lanes_of(length)
    for half in range(2):
        cells = means[half * length : (half + 1) * length]
        for at, first in ((half * HALF + COARSE_A, start), (half * HALF + COARSE_B, start + 3)):
            packed = jnp.where((lane >= at) & (lane < at + 3), turn(cells, at - first), packed)
    return packed


def column_meta(message):
    return (int_at(message, 0, SHIFT_R), int_at(message, 0, SHIFT_C)), scalar_at(message, 0, EXISTS)


def strip_second(base, from_left, from_right, rows, half, band):
    at = half * HALF + band * SLOT
    lane = lanes_like(base)
    cells = jnp.where(lane >= S_RIGHT, turn(from_right[rows, :], S_RIGHT - at), base)
    return jnp.where(lane >= S_LEFT, turn(from_left[rows, :], S_LEFT - at), cells)


def strip_first(base, from_left, from_right, rows, half, band):
    at = half * HALF + band * SLOT + REACH
    lane = lanes_like(base)
    cells = jnp.where(lane >= S_RIGHT, turn(from_right[rows, :], S_RIGHT - at), base)
    return jnp.where(lane >= S_LEFT, turn(from_left[rows, :], LANES - DEPTH - at), cells)


def strip_halo(base, beside, band, start, count):
    at = band * H_BAND + start
    lane = lanes_like(base)
    cells = jnp.where(lane >= S_RIGHT, turn(beside, S_RIGHT - at), base)
    return jnp.where(lane >= S_LEFT, turn(beside, LANES - count - at - SLOT), cells)


def strip_own(planes):
    return jnp.where(lanes_like(planes[0]) < S_MID, planes[0], turn(planes[1], -S_TURN))


def first_kernel(
    second_hbm, first_hbm, shifts_hbm, second_0, second_1, first_0, first_1, coarse, swap_0, swap_1, own_meta,
    shifts, sems, shift_sem,
):
    seconds, firsts = (second_0, second_1), (first_0, first_1)
    bands, height, _ = second_0.shape
    width = COLUMNS
    coarse_height = height // FACTOR
    lane = lanes_of()
    get_shifts = pltpu.make_async_copy(shifts_hbm, shifts, shift_sem)
    get_shifts.start()
    copies = []
    for image, (source, refs) in enumerate(((second_hbm, seconds), (first_hbm, firsts))):
        for band in range(bands):
            for tile, ref in enumerate(refs):
                copy = pltpu.make_async_copy(
                    source.at[band, :, pl.ds(tile * LANES, LANES)], ref.at[band], sems.at[image, band, tile]
                )
                copy.start()
                copies.append((image * bands + band, tile, ref, band, copy))
    cell = lax.broadcasted_iota(jnp.int32, (width, LANES), 0)
    place = lax.broadcasted_iota(jnp.int32, (width, LANES), 1)
    weights = jnp.where(place - LEAD == cell // FACTOR, 1.0 / (FACTOR * FACTOR), 0.0).astype(jnp.bfloat16)
    means = []
    packed = [None, None]
    for image, (count, offset) in enumerate(((REACH, 0), (DEPTH, REACH))):
        group = copies[image * 2 * bands : (image + 1) * 2 * bands]
        sums = {}
        for *_, copy in group:
            copy.wait()
        for plane, tile, ref, band, _ in group:
            parts = [ref[band, pl.ds(k, coarse_height, stride=FACTOR), :] for k in range(FACTOR)]
            while len(parts) > 1:
                parts = [x + y for x, y in zip(parts[::2], parts[1::2])]
            sums[plane, tile] = parts[0]
        tall = [jnp.concatenate([sums[image * bands + band, tile] for tile in range(2)], axis=1) for band in range(bands)]
        means.append(split_dot(jnp.concatenate(tall, axis=0), weights))
        packed = [
            pack_image(packed[side], bool(side), (seconds, firsts)[image], count, offset) for side in range(2)
        ]
    means = jnp.concatenate(means, axis=0)
    get_shifts.wait()
    shift_rows = shifts[0, 0, 0].astype(jnp.float32)
    shift_cols = shifts[0, 0, 1].astype(jnp.float32)
    place = lanes_of(height // 2) & (HALF - 1)
    packed = [
        jnp.where(place == SHIFT_R, shift_rows, jnp.where(place == SHIFT_C, shift_cols, jnp.where(place == EXISTS, 1.0, x)))
        for x in packed
    ]
    to_left, to_right = [pack_means(packed[side], bool(side), means) for side in range(2)]
    coarse[...] = means
    own_meta[...] = jnp.where(lane < HALF, shift_rows, shift_cols)
    even = is_even("col", swap_0)
    swap_0[...] = jnp.where(even, to_right, to_left)
    swap_1[...] = jnp.where(even, to_left, to_right)


def message_kernel(
    count, coarse, own_meta, got_1, got_0, up_part, down_part, _whole, swap_0, swap_1, from_left, from_right, wide
):
    other = without_ends(got_1, "col", count)
    even = is_even("col", got_0)
    from_right[...] = jnp.where(even, got_0[...], other)
    from_left[...] = jnp.where(even, other, got_0[...])
    planes_coarse, coarse_height, _ = wide.shape
    bands = planes_coarse // 2
    end = from_left.shape[0]
    coarse_width = COLUMNS // FACTOR
    lane = lanes_of()
    wides = []
    for plane in range(planes_coarse):
        half, block = divmod(plane, planes_coarse // 2)
        for step in range(coarse_height // SUB):
            own = slice(plane * coarse_height + step * SUB, plane * coarse_height + (step + 1) * SUB)
            rows = slice(block * coarse_height + step * SUB, block * coarse_height + (step + 1) * SUB)
            at = half * HALF
            left = from_left[rows, :]
            right = from_right[rows, :]
            start = LEAD - C_SECOND
            cells = turn(left, start - at - COARSE_A)
            cells = jnp.where(lane >= start + 3, turn(left, start + 3 - at - COARSE_B), cells)
            cells = jnp.where(lane >= LEAD, coarse[own, :], cells)
            start = LEAD + coarse_width
            cells = jnp.where(lane >= start, turn(right, start - at - COARSE_A), cells)
            cells = jnp.where(lane >= start + 3, turn(right, start + 3 - at - COARSE_B), cells)
            wides.append((plane, step, cells))
    for plane, step, cells in wides:
        wide[plane, step * SUB : (step + 1) * SUB, :] = cells
    row = lax.broadcasted_iota(jnp.int32, (SUB, LANES), 0)
    meta = jnp.where(lane < 16, own_meta[...], jnp.where(lane < 32, turn(own_meta[...], HALF), 1.0))
    for message, at in ((from_left, 48), (from_right, 80)):
        first_rows = message[0:SUB, :]
        rows = jnp.broadcast_to(first_rows[:, SHIFT_R : SHIFT_R + 1], (SUB, LANES))
        cols = jnp.broadcast_to(first_rows[:, SHIFT_C : SHIFT_C + 1], (SUB, LANES))
        meta = jnp.where(lane >= at, rows, meta)
        meta = jnp.where(lane >= at + 16, cols, meta)

    def beside(rows, half):
        left = from_left[rows, :]
        right = from_right[rows, :]
        cells = jnp.zeros((SUB, LANES), jnp.float32)
        for band in range(bands):
            at = half * HALF + band * SLOT
            cells = jnp.where(lane >= band * H_BAND, turn(right, band * H_BAND - at), cells)
            cells = jnp.where(lane >= band * H_BAND + SLOT, turn(left, band * H_BAND + SLOT - at), cells)
        return cells

    even = is_even("row", meta)
    parts = []
    for part, half, near, next_rows, row_of in (
        (up_part, 0, slice(0, 8), slice(8, 16), 0),
        (down_part, 1, slice(end - 8, end), slice(end - 16, end - 8), 7),
    ):
        eight = beside(near, half)
        one = beside(next_rows, half)
        one = jnp.broadcast_to(one[row_of : row_of + 1], (SUB, LANES))
        coarse_rows = []
        for band in range(bands):
            rows = slice(0, C_SECOND) if half == 0 else slice(coarse_height - C_SECOND, coarse_height)
            second = wide[band, rows, :]
            first = turn(wide[bands + band, rows, :], HALF)
            coarse_rows.append(jnp.where(lanes_like(second) < HALF, second, first))
        parts.append([
            (part[E8:H8, :], E8), (eight, H8), (part[E1:H1, :], E1), (jnp.where(row == 0, one, meta), H1),
            (part[F4:CS, :], F4), *[(x, CS + k * C_SECOND) for k, x in enumerate(coarse_rows)],
        ])
    for (up, at), (down, _) in zip(*parts):
        even = is_even("row", up)
        swap_0[at : at + up.shape[0], :] = jnp.where(even, down, up)
        swap_1[at : at + up.shape[0], :] = jnp.where(even, up, down)


def coarse_flow_of(second, first, mask):
    def along_rows(x):
        return pltpu.roll(x, x.shape[0] - 1, 0) - pltpu.roll(x, 1, 0)

    def along_cols(x):
        return pltpu.roll(x, LANES - 1, 1) - pltpu.roll(x, 1, 1)

    bands = BANDS
    size = second.shape[0] // bands
    grad_rows = 0.125 * along_rows(second)
    grad_cols = 0.125 * along_cols(second)
    offset = 0.25 * (second - first)
    data = jnp.clip(offset, -LIMIT, LIMIT)
    yield

    def pull(grads):
        terms = data * grads
        return sum(terms[k * size : (k + 1) * size] for k in range(bands))

    def tall(x):
        return jnp.concatenate([x] * bands, axis=0)

    flow = [-mask * pull(grad_rows), -mask * pull(grad_cols)]
    extrapolated = [2.0 * x for x in flow]
    dual_rows = [0.0, 0.0]
    dual_cols = [0.0, 0.0]
    yield
    for step in range(1, STEPS):
        changes = [(along_rows(x), along_cols(x)) for x in extrapolated]
        yield
        data = data + offset + grad_rows * tall(extrapolated[0]) + grad_cols * tall(extrapolated[1])
        data = jnp.clip(data, -LIMIT, LIMIT)
        yield
        for c in range(2):
            rows = dual_rows[c] + changes[c][0]
            cols = dual_cols[c] + changes[c][1]
            scale = jnp.minimum(mask, (8.0 * ALPHA) * lax.rsqrt(rows * rows + cols * cols))
            dual_rows[c] = rows * scale
            dual_cols[c] = cols * scale
        yield
        divergences = [along_rows(dual_rows[c]) + along_cols(dual_cols[c]) for c in range(2)]
        yield
        pulls = [pull(grad_rows), pull(grad_cols)]
        yield
        for c in range(2):
            following = flow[c] + mask * ((1.0 / 64.0) * divergences[c] - pulls[c])
            extrapolated[c] = 2.0 * following - flow[c]
            flow[c] = following
        yield
    return flow


def columns_of_planes(planes):
    whole = lax.broadcasted_iota(jnp.int32, (LANES, COLUMNS), 1)
    lane = lax.broadcasted_iota(jnp.int32, (LANES, LANES), 1)
    strip = jnp.where(lane < S_MID, lane, jnp.where(lane < S_LEFT, lane + (COLUMNS - S_RIGHT), lane - LANES))
    return jnp.concatenate([x for x, wanted in ((whole, "whole"), (strip, "strip")) if wanted in planes], axis=1)


def upsample(flow, planes, target):
    column = columns_of_planes(planes)
    source = lax.broadcasted_iota(jnp.int32, column.shape, 0)
    spread = jnp.where(source - LEAD == lax.shift_right_arithmetic(column, 3), float(FACTOR), 0.0).astype(jnp.bfloat16)
    rows = flow[0].shape[0]
    wide = split_dot(UNIT * jnp.concatenate(flow, axis=0), spread)
    for c in range(2):
        for tile in range(column.shape[1] // LANES):
            target[c, tile] = wide[c * rows : (c + 1) * rows, tile * LANES : (tile + 1) * LANES]


def repeat_rows(spread, initial, cells):
    for c in range(2):
        for tile in range(initial.shape[1]):
            rows = [jnp.broadcast_to(spread[c, tile, cell : cell + 1, :], (SUB, LANES)) for cell in cells]
            initial[c, tile, GUARD : GUARD + SUB * len(cells), :] = jnp.concatenate(rows, axis=0)


def shift_whole(here, shift):
    turned = [turn_back(x, shift) for x in here]
    lane = lanes_like(here[0])
    return [
        jnp.where(lane + shift >= LANES, turned[1], turned[0]),
        jnp.where(lane + shift < 0, turned[0], turned[1]),
    ]


def edge_lanes(rows):
    lane = lanes_of(rows)
    return lane == LANES - 1, lane == 0


def columns_whole(fields, edges):
    last, first = edges
    ahead = [pltpu.roll(x, LANES - 1, 1) for x in fields]
    behind = [pltpu.roll(x, 1, 1) for x in fields]
    return [
        jnp.where(last, ahead[1], ahead[0]) - behind[0],
        ahead[1] - jnp.where(first, behind[0], behind[1]),
    ]


def columns_strip(field):
    return pltpu.roll(field, LANES - 1, 1) - pltpu.roll(field, 1, 1)


def strip_windows(window, centre, right, left):
    own = turn_back(window(centre[0]), centre[1])
    beyond_left = turn_back(window(left[0]), left[1])
    beyond_right = turn_back(window(right[0]), right[1])
    lane = lanes_like(own)
    beyond = jnp.where((lane >= S_LEFT) | (lane < S_MID), beyond_left, beyond_right)
    is_beyond = lane >= S_RIGHT
    return jnp.where(is_beyond, beyond, own), jnp.where(is_beyond, columns_strip(beyond), columns_strip(own))


def fine_steps(
    rows_total, chunk, columns, initial, extrap, dual_rows, dual_cols, change, dual_data,
    offsets, grads_rows, grads_cols, data_row, masks_of, result, done=lambda k: None,
):
    planes = len(offsets)
    bands = offsets[0].shape[0]
    chunks = rows_total // chunk
    tiles = range(planes)

    for step in range(STEPS):
        source = initial if step == 0 else extrap
        final = step == STEPS - 1

        def dual(item, source=source, step=step):
            k, c = item
            row = GUARD + k * chunk
            at, own = pl.ds(row, chunk), pl.ds(k * chunk, chunk)
            masks = masks_of(own)
            along = columns([source[c, tile, at, :] for tile in tiles])
            values = []
            for tile in tiles:
                rows = source[c, tile, pl.ds(row + 1, chunk), :] - source[c, tile, pl.ds(row - 1, chunk), :]
                cols = along[tile]
                if step > 0:
                    rows = rows + dual_rows[c, tile, at, :]
                    cols = cols + dual_cols[c, tile, own, :]
                scale = jnp.minimum(masks[tile], lax.rsqrt(rows * rows + cols * cols))
                values.append((rows * scale, cols * scale))
            return values

        def store_dual(item, values):
            k, c = item
            for tile, (rows, cols) in enumerate(values):
                dual_rows[c, tile, pl.ds(GUARD + k * chunk, chunk), :] = rows
                dual_cols[c, tile, pl.ds(k * chunk, chunk), :] = cols

        staggered([(k, c) for k in range(chunks) for c in range(2)], dual, store_dual, 1)
        along_of = {}

        def primal(item, step=step, final=final, along_of=along_of):
            k, tile = item
            row = GUARD + k * chunk
            at, own, data = pl.ds(row, chunk), pl.ds(k * chunk, chunk), pl.ds(data_row(k), chunk)
            if k not in along_of:
                along_of[k] = [columns([dual_cols[c, t, own, :] for t in tiles]) for c in range(2)]
            mask = masks_of(own)[tile]
            start = [initial[c, tile, at, :] for c in range(2)]
            if step > 0:
                moved = [extrap[c, tile, at, :] - start[c] for c in range(2)]
            pulls = [None, None]
            duals = []
            for band in range(bands):
                gradient = (grads_rows[tile][band, data, :], grads_cols[tile][band, data, :])
                value = offsets[tile][band, data, :]
                if step > 0:
                    value = value + gradient[0] * moved[0] + gradient[1] * moved[1]
                    value = value + dual_data[band, tile, own, :]
                value = jnp.clip(value, -UNIT * LIMIT, UNIT * LIMIT)
                duals.append(value)
                for c in range(2):
                    term = value * gradient[c]
                    pulls[c] = term if pulls[c] is None else pulls[c] + term
            flows, nexts = [], []
            for c in range(2):
                divergence = (
                    dual_rows[c, tile, pl.ds(row + 1, chunk), :]
                    - dual_rows[c, tile, pl.ds(row - 1, chunk), :]
                    + along_of[k][c][tile]
                )
                moving = (mask * (1.0 / 64.0)) * divergence - pulls[c]
                total = moving if step == 0 else change[c, tile, own, :] + moving
                flows.append((start[c] + total) * (1.0 / UNIT) if final else total)
                nexts.append(None if final else start[c] + (total + moving))
            return flows, nexts, duals

        def store_primal(item, results, final=final):
            k, tile = item
            flows, nexts, duals = results
            own = pl.ds(k * chunk, chunk)
            for c in range(2):
                if final:
                    result[c, tile, own, :] = flows[c]
                else:
                    change[c, tile, own, :] = flows[c]
                    extrap[c, tile, pl.ds(GUARD + k * chunk, chunk), :] = nexts[c]
            if final:
                if tile == planes - 1:
                    done(k)
            else:
                for band in range(bands):
                    dual_data[band, tile, own, :] = duals[band]

        staggered([(k, tile) for k in range(chunks) for tile in tiles], primal, store_primal, 1)


def clear_guards(*refs):
    for ref in refs:
        rows = ref.shape[2]
        zero = jnp.zeros((GUARD, LANES), jnp.float32)
        for c in range(2):
            for tile in range(ref.shape[1]):
                ref[c, tile, 0:GUARD, :] = zero
                ref[c, tile, rows - GUARD : rows, :] = zero


def fine_scratch(bands, planes, rows):
    guarded = pltpu.VMEM((2, planes, rows + 2 * GUARD, LANES), jnp.float32)
    plain = pltpu.VMEM((2, planes, rows, LANES), jnp.float32)
    return [guarded, guarded, guarded, plain, plain, pltpu.VMEM((bands, planes, rows, LANES), jnp.float32)]


def pieces(bands, height, rows):
    assert (height - 2 * SUB) % rows == 0
    return [(band, row) for row in range(SUB, height - SUB, rows) for band in range(bands)]


def whole_terms_kernel(
    second_0, second_1, first_0, first_1, coarse, own_meta,
    offset, grad_rows, grad_cols, initial, strip_e, strip_f, up, down, moved, spread,
):
    seconds, firsts = (second_0, second_1), (first_0, first_1)
    bands, height, _ = second_0.shape
    block = 120
    coarse_height = coarse.shape[0] // (2 * bands)
    shift_rows, shift_cols = scalar_at(own_meta, 0, 0), scalar_at(own_meta, 0, HALF)
    centre = (shift_rows.astype(jnp.int32), shift_cols.astype(jnp.int32))
    def windows(band, row, rows):
        here = [ref[band, pl.ds(row + centre[0], rows), :].reshape(-1, LANES) for ref in seconds]
        return shift_whole(here, centre[1])

    woven = Woven(coarse_flow_of(coarse[0 : bands * coarse_height, :], coarse[bands * coarse_height :, :], 1.0))

    ends = [(row, windows(slice(None), row, SUB)) for row in (SUB // 2, height - SUB - SUB // 2)]
    for row, values in ends:
        for tile in range(2):
            moved[tile, :, row : row + SUB, :] = values[tile].reshape(bands, SUB, LANES)

    edges = edge_lanes(block)

    def values_of(item):
        band, row = item
        values = windows(band, row, block)
        along = columns_whole(values, edges)
        own = [ref[band, row : row + block, :] for ref in firsts]
        return values, [(0.25 * UNIT) * (x - y) for x, y in zip(values, own)], [0.125 * x for x in along]

    def store_values(item, results):
        band, row = item
        values, offsets, gradients = results
        data = slice(row + HALO, row + HALO + block)
        for tile in range(2):
            moved[tile, band, row : row + block, :] = values[tile]
            offset[tile, band, data, :] = offsets[tile]
            grad_cols[tile, band, data, :] = gradients[tile]

    staggered(pieces(bands, height, block), values_of, store_values, 1, woven)

    def strips_of(item):
        band, row = item
        rows = slice(row, row + LANES)
        return strip_own([ref[band, rows, :] for ref in seconds]), strip_own([ref[band, rows, :] for ref in firsts])

    def store_strips(item, results):
        band, row = item
        strip_e[band, row : row + LANES, :], strip_f[band, row : row + LANES, :] = results

    staggered([(band, row) for band in range(bands) for row in range(0, height, LANES)], strips_of, store_strips, 1, woven)

    def gradient_of(item):
        band, row = item
        return [
            0.125 * (moved[tile, band, pl.ds(row + 1, 120), :] - moved[tile, band, pl.ds(row - 1, 120), :])
            for tile in range(2)
        ]

    def store_gradient(item, results):
        band, row = item
        for tile in range(2):
            grad_rows[tile, band, row + HALO : row + HALO + 120, :] = results[tile]

    staggered(pieces(bands, height, 120), gradient_of, store_gradient, 1, woven)

    parts = []
    for band in range(bands):
        for second, first in zip(seconds, firsts):
            parts.append((
                second[band, 0:16, :], first[band, 0:8, :],
                second[band, height - 16 : height, :], first[band, height - 8 : height, :],
            ))
    for k, (second_top, first_top, second_end, first_end) in enumerate(parts):
        up[E8 + 8 * k : E8 + 8 * k + 8, :] = second_top[0:8]
        up[E1 + k : E1 + k + 1, :] = second_top[8:9]
        up[F4 + 4 * k : F4 + 4 * k + 4, :] = first_top[0:4]
        down[E8 + 8 * k : E8 + 8 * k + 8, :] = second_end[8:16]
        down[E1 + k : E1 + k + 1, :] = second_end[7:8]
        down[F4 + 4 * k : F4 + 4 * k + 4, :] = first_end[4:8]
    for target in (up, down):
        for start, end in ((H8, E1), (H1, F4), (CS, ROW_MESSAGE)):
            target[start:end, :] = jnp.zeros((end - start, LANES), jnp.float32)

    upsample(woven.finish(), ("whole",), spread)
    clear_guards(initial)
    rows_total = initial.shape[2] - 2 * GUARD
    repeat_rows(spread, initial, [BEGIN // FACTOR + k for k in range(rows_total // SUB)])


def whole_steps_kernel(
    initial, offset, grad_rows, grad_cols, result, extrap, dual_rows, dual_cols, change, dual_data
):
    rows_total = result.shape[2]
    clear_guards(extrap, dual_rows)
    chunk = 88
    edges = edge_lanes(chunk)
    fine_steps(
        rows_total, chunk, lambda fields: columns_whole(fields, edges),
        initial, extrap, dual_rows, dual_cols, change, dual_data,
        *[[ref.at[tile] for tile in range(2)] for ref in (offset, grad_rows, grad_cols)],
        lambda k: HALO + BEGIN + k * chunk, lambda own: (1.0, 1.0), result,
    )


def strip_kernel(
    strip_e, strip_f, from_left, from_right, wide, own_meta, whole,
    middle, strip_out, first_ends, offset, grad_rows, grad_cols,
    moved, result, spread, initial, extrap, dual_rows, dual_cols, change, dual_data,
):
    bands, height, _ = strip_e.shape
    block = 120
    coarse_height = height // FACTOR
    coarse_width = COLUMNS // FACTOR
    rows_total = height - 2 * BEGIN
    lane = lanes_of()
    centre = (int_at(own_meta, 0, 0), int_at(own_meta, 0, HALF))
    right, has_right = column_meta(from_right)
    left, has_left = column_meta(from_left)
    exists = jnp.where(lane < S_RIGHT, 1.0, jnp.where(lane < S_LEFT, has_right, has_left))

    def tall_factor(rows):
        return 0.125 * jnp.concatenate([exists] * (rows // SUB), axis=0)

    mask = jnp.where(lane < LEAD, has_left, jnp.where(lane < LEAD + coarse_width, 1.0, has_right))
    mask = jnp.concatenate([mask] * (coarse_height // SUB), axis=0)
    cells = [wide[k * bands : (k + 1) * bands].reshape(bands * coarse_height, LANES) for k in range(2)]
    woven = Woven(coarse_flow_of(*cells, mask))

    def halves(row, rows):
        half = row // (height // 2)
        start = row - half * (height // 2)
        return half, slice(start, start + rows)

    def second_of(item):
        band, row = item
        half, message = halves(row, LANES)
        return strip_second(strip_e[band, row : row + LANES, :], from_left, from_right, message, half, band)

    def store_second(item, value):
        band, row = item
        strip_out[band, row : row + LANES, :] = value

    staggered([(band, row) for row in range(0, height, LANES) for band in range(bands)], second_of, store_second, 1, woven)

    def first_of(band, row, rows):
        half, message = halves(row, rows)
        return strip_first(strip_f[band, row : row + rows, :], from_left, from_right, message, half, band)

    firsts = [(end, band, first_of(band, (0, height - SUB)[end], SUB)) for end in range(2) for band in range(bands)]
    for end, band, value in firsts:
        first_ends[end, band] = value

    def windows(band, row, rows):
        return strip_windows(
            lambda shift: strip_out[band, pl.ds(row + shift, rows), :].reshape(-1, LANES), centre, right, left
        )

    ends = [(row, windows(slice(None), row, SUB)[0]) for row in (SUB // 2, height - SUB - SUB // 2)]
    for row, value in ends:
        moved[:, row : row + SUB, :] = value.reshape(bands, SUB, LANES)

    factor = tall_factor(block)

    def values_of(item):
        band, row = item
        value, along = windows(band, row, block)
        return value, (0.25 * UNIT) * (value - first_of(band, row, block)), factor * along

    def store_values(item, results):
        band, row = item
        data = slice(row + HALO, row + HALO + block)
        moved[band, row : row + block, :], offset[band, data, :], grad_cols[band, data, :] = results

    staggered(pieces(bands, height, block), values_of, store_values, 1, woven)

    def gradient_of(item):
        band, row = item
        return factor * (moved[band, pl.ds(row + 1, block), :] - moved[band, pl.ds(row - 1, block), :])

    def store_gradient(item, value):
        band, row = item
        grad_rows[band, row + HALO : row + HALO + block, :] = value

    staggered(pieces(bands, height, block), gradient_of, store_gradient, 1, woven)

    upsample(woven.finish(), ("strip",), spread)
    clear_guards(initial, extrap, dual_rows)
    repeat_rows(spread, initial, [BEGIN // FACTOR + k for k in range(rows_total // SUB)])

    chunk = 176
    masks = jnp.concatenate([exists] * (chunk // SUB), axis=0)
    fine_steps(
        rows_total, chunk, lambda fields: [columns_strip(fields[0])],
        initial, extrap, dual_rows, dual_cols, change, dual_data, [offset], [grad_rows], [grad_cols],
        lambda k: HALO + BEGIN + k * chunk, lambda own: (masks,), result,
    )
    join(whole, result.at[:, 0], middle, slice(0, rows_total))


def join(whole, strip, target, rows):
    lane = lanes_of(rows.stop - rows.start)
    values = []
    for c in range(2):
        edge = strip[c, rows, :]
        start = jnp.where(lane < EDGE, edge, whole[c, 0, rows, :])
        values.append((start, jnp.where(lane >= LANES - EDGE, turn(edge, S_TURN), whole[c, 1, rows, :])))
    for c in range(2):
        target[c, rows, 0:LANES], target[c, rows, LANES:COLUMNS] = values[c]


def outer_kernel(
    count, second_0, second_1, first_0, first_1, strip_e, first_ends, from_left, from_right, wide, got_1, got_0, middle, own_meta,
    _wo, _wr, _wc, _so, _sr, _sc,
    flow_out, coarse_out, whole_offset, whole_rows, whole_cols, strip_offset, strip_rows, strip_cols,
    from_up, from_down, extended, tall, spread, masks, result, joined, coarse_result, sems,
    initial, extrap, dual_rows, dual_cols, change, dual_data,
):
    bands, height, _ = second_0.shape
    coarse_height = height // FACTOR
    coarse_width = COLUMNS // FACTOR
    rows_total = 2 * EACH
    lane = lanes_of()

    put_middle = pltpu.make_async_copy(
        middle.at[:, pl.ds(MARGIN - BEGIN, height - 2 * MARGIN), :],
        flow_out.at[:, pl.ds(MARGIN, height - 2 * MARGIN), :],
        sems.at[0],
    )
    put_middle.start()

    other = without_ends(got_1, "row", count)
    even = is_even("row", got_0)
    from_down[...] = jnp.where(even, got_0[...], other)
    from_up[...] = jnp.where(even, other, got_0[...])

    own = (int_at(own_meta, 0, 0), int_at(own_meta, 0, HALF))
    own_right, has_right = column_meta(from_right)
    own_left, has_left = column_meta(from_left)
    has_up = scalar_at(from_up, META, 32)
    has_down = scalar_at(from_down, META, 32)
    exists = jnp.where(lane < S_RIGHT, 1.0, jnp.where(lane < S_LEFT, has_right, has_left))

    def trio(message):
        return (
            (int_at(message, META, 0), int_at(message, META, 16)),
            (int_at(message, META, 80), int_at(message, META, 96)),
            (int_at(message, META, 48), int_at(message, META, 64)),
        )

    above = trio(from_up)
    below = trio(from_down)

    zero = jnp.zeros((SUB, LANES), jnp.float32)
    tall_rows = coarse_height + 2 * LEAD
    parts = []
    fill = jnp.zeros((LEAD - C_SECOND, LANES), jnp.float32)
    for plane in range(2 * bands):
        at = CS + C_SECOND * (plane % bands)
        ends = [turn(message[at : at + C_SECOND, :], HALF * (plane // bands)) for message in (from_up, from_down)]
        parts.append([fill, ends[0], wide[plane], ends[1], fill])
    for plane, values in enumerate(parts):
        tall[plane] = jnp.concatenate(values, axis=0)
    across = jnp.where(lane < LEAD, has_left, jnp.where(lane < LEAD + coarse_width, 1.0, has_right))
    mask = jnp.concatenate([across * has_up] + [across] * (coarse_height // SUB) + [across * has_down], axis=0)
    for end in range(2):
        message = (from_up, from_down)[end]
        beside = message[H8 : H8 + 8, :]
        beside_one = jnp.broadcast_to(message[H1 : H1 + 1, :], (SUB, LANES))
        parts = []
        for band in range(bands):
            eights = [message[E8 + 8 * k : E8 + 8 * k + 8, :] for k in (2 * band, 2 * band + 1)]
            ones = [jnp.broadcast_to(message[E1 + k : E1 + k + 1, :], (SUB, LANES)) for k in (2 * band, 2 * band + 1)]
            eights.append(strip_halo(strip_own(eights), beside, band, 0, REACH))
            ones.append(strip_halo(strip_own(ones), beside_one, band, 0, REACH))
            for tile, (eight, one) in enumerate(zip(eights, ones)):
                source = (second_0, second_1, strip_e)[tile]
                if end == 0:
                    parts.append((tile, band, [one, eight, source[band, 0:24, :]]))
                else:
                    parts.append((tile, band, [source[band, height - 24 : height, :], eight, one]))
        for tile, band, values in parts:
            extended[end, tile, band] = jnp.concatenate(values, axis=0)
    cells = [tall[k * bands : (k + 1) * bands].reshape(bands * tall_rows, LANES) for k in range(2)]
    woven = Woven(coarse_flow_of(*cells, mask))
    edges = edge_lanes(bands * SUB)
    rows_data = whole_offset.shape[2]
    exists_tall = jnp.concatenate([exists] * bands, axis=0)

    def rows_of(halo, end):
        if halo:
            return slice(0, SUB) if end == 0 else slice(rows_data - SUB, rows_data)
        return slice(HALO, HALO + SUB) if end == 0 else slice(rows_data - HALO - SUB, rows_data - HALO)

    def values_of(item):
        halo, end = item
        message = (from_up, from_down)[end]
        base = (SUB, 3 * SUB)[end] if halo else 2 * SUB
        shifts = (above, below)[end] if halo else (own, own_right, own_left)
        factor = 0.125 * (has_up, has_down)[end] if halo else 0.125

        def here(tile, shift):
            return extended[end, tile, :, pl.ds(base + shift, SUB), :].reshape(-1, LANES)

        def down_up(tile, shift):
            return here(tile, shift + 1) - here(tile, shift - 1)

        own_rows = slice(0, SUB) if end == 0 else slice(height - SUB, height)
        if halo:
            firsts = [[], [], []]
            for band in range(bands):
                eights = []
                for k in (2 * band, 2 * band + 1):
                    four = message[F4 + 4 * k : F4 + 4 * k + 4, :]
                    eights.append(jnp.concatenate([four, four], axis=0))
                eights.append(strip_halo(strip_own(eights), message[H8 : H8 + 8, :], band, REACH, DEPTH))
                for tile in range(3):
                    firsts[tile].append(eights[tile])
            firsts = [jnp.concatenate(x, axis=0) for x in firsts]
        else:
            firsts = [x.reshape(-1, LANES) for x in (first_0[:, own_rows, :], first_1[:, own_rows, :], first_ends[end])]
        centre = shifts[0]
        values = shift_whole([here(tile, centre[0]) for tile in range(2)], centre[1])
        changes = shift_whole([down_up(tile, centre[0]) for tile in range(2)], centre[1])
        along = columns_whole(values, edges)
        value, across_cols = strip_windows(lambda shift: here(2, shift), *shifts)
        change_rows, _ = strip_windows(lambda shift: down_up(2, shift), *shifts)
        return (
            [(0.25 * UNIT) * (x - y) for x, y in zip([*values, value], firsts)],
            [*[factor * x for x in changes], (factor * exists_tall) * change_rows],
            [*[factor * x for x in along], (factor * exists_tall) * across_cols],
        )

    def store_values(item, results):
        rows = rows_of(*item)
        for values, whole, strip in zip(
            results, (whole_offset, whole_rows, whole_cols), (strip_offset, strip_rows, strip_cols)
        ):
            values = [x.reshape(bands, SUB, LANES) for x in values]
            for tile in range(2):
                whole[tile, :, rows, :] = values[tile]
            strip[:, rows, :] = values[2]

    staggered([(halo, end) for halo in (True, False) for end in range(2)], values_of, store_values, 1, woven)

    flow = woven.finish()
    for c in range(2):
        coarse_result[c] = turn(flow[c][LEAD : LEAD + coarse_height], -LEAD)[:, :coarse_width]
    put_coarse = pltpu.make_async_copy(coarse_result, coarse_out, sems.at[1])
    put_coarse.start()
    upsample(flow, ("whole", "strip"), spread)
    clear_guards(initial, extrap, dual_rows)
    each = EACH // SUB
    repeat_rows(
        spread, initial,
        [LEAD - 1 + k for k in range(each)] + [tall_rows - LEAD + 1 - each + k for k in range(each)],
    )

    for i, value in enumerate((jnp.ones((SUB, LANES), jnp.float32), exists)):
        masks[i] = jnp.concatenate([value * has_up] + [value] * (rows_total // SUB - 2) + [value * has_down], axis=0)

    def masks_of(rows):
        whole = masks[0, rows, :]
        return (whole, whole, masks[1, rows, :])

    chunk = EACH
    edges = edge_lanes(chunk)
    puts = [
        pltpu.make_async_copy(
            joined.at[:, pl.ds(k * EACH + SUB, MARGIN), :],
            flow_out.at[:, pl.ds(k * (height - MARGIN), MARGIN), :],
            sems.at[2 + k],
        )
        for k in range(2)
    ]

    def finish(k):
        join(result, result.at[:, 2], joined, slice(k * EACH + SUB, k * EACH + SUB + MARGIN))
        puts[k].start()

    def data_row(k):
        return k * (rows_data - EACH)

    fine_steps(
        rows_total, chunk, lambda fields: columns_whole(fields[:2], edges) + [columns_strip(fields[2])],
        initial, extrap, dual_rows, dual_cols, change, dual_data,
        [whole_offset.at[0], whole_offset.at[1], strip_offset],
        [whole_rows.at[0], whole_rows.at[1], strip_rows],
        [whole_cols.at[0], whole_cols.at[1], strip_cols],
        data_row, masks_of, result, finish,
    )
    put_middle.wait()
    put_coarse.wait()
    for put in puts:
        put.wait()


def swap_with(message, axis, start):
    names = ("row", "col")
    sizes = [lax.axis_size(name) for name in names]
    along = names.index(axis)
    count, others = sizes[along], sizes[1 - along]

    def number(place, other):
        row, col = (place, other) if along == 0 else (other, place)
        return row * sizes[1] + col

    pairs = [(number(i, k), number(i + 1, k)) for i in range(start, count - 1, 2) for k in range(others)]
    if start:
        pairs += [(number(i, k), number(i, k + 1)) for i in (0, count - 1) for k in range(0, others, 2)]
    return lax.ppermute(message, names, pairs + [(j, i) for i, j in pairs])


def local(frame_first, frame_second, shifts):
    bands, height, width = frame_first.shape
    assert bands == 4 and width == COLUMNS and height % LANES == 0
    assert lax.axis_size("row") % 2 == 0 and lax.axis_size("col") % 2 == 0
    coarse_height = height // FACTOR
    coarse_width = width // FACTOR
    vmem = pl.BlockSpec(memory_space=pltpu.VMEM)
    hbm = pl.BlockSpec(memory_space=pltpu.HBM)
    tall_rows = coarse_height + 2 * LEAD
    inner_rows = height - 2 * BEGIN

    def shape(*sizes):
        return jax.ShapeDtypeStruct(sizes, jnp.float32)

    def scratch(*sizes):
        return pltpu.VMEM(sizes, jnp.float32)

    def call(kernel, name, arguments, outs, scratches=(), flops=1_000_000, **more):
        more = {"in_specs": [vmem] * len(arguments), "out_specs": (vmem,) * len(outs), **more}
        return pl.pallas_call(
            kernel,
            out_shape=tuple(outs),
            scratch_shapes=list(scratches),
            compiler_params=pltpu.CompilerParams(vmem_limit_bytes=24 * 1024 * 1024),
            cost_estimate=pl.CostEstimate(flops=flops, bytes_accessed=1_000_000, transcendentals=0),
            name=name,
            **more,
        )(*arguments)

    plane = shape(bands, height, LANES)
    column_message = shape(height // 2, LANES)
    row_message = shape(ROW_MESSAGE, LANES)
    whole_data = shape(2, bands, height + 2 * HALO, LANES)
    strip_data = shape(bands, height + 2 * HALO, LANES)

    *frames, coarse, swap_0, swap_1, own_meta = call(
        first_kernel,
        "means_and_message",
        [pltpu.with_memory_space_constraint(x, pltpu.HBM) for x in (frame_second, frame_first, shifts)],
        [*[plane] * 4, shape(2 * bands * coarse_height, LANES), column_message, column_message, shape(SUB, LANES)],
        [
            pltpu.SMEM((1, 1, 2), jnp.int32),
            pltpu.SemaphoreType.DMA((2, bands, 2)),
            pltpu.SemaphoreType.DMA,
        ],
        in_specs=[hbm] * 3,
    )
    got_1 = swap_with(swap_1, "col", 1)
    got_0 = swap_with(swap_0, "col", 0)

    *whole_terms, initial, strip_e, strip_f, up_part, down_part = call(
        whole_terms_kernel,
        "whole_terms",
        [*frames, coarse, own_meta],
        [
            *[whole_data] * 3, shape(2, 2, inner_rows + 2 * GUARD, LANES),
            plane, plane, row_message, row_message,
        ],
        [scratch(2, bands, height, LANES), scratch(2, 2, coarse_height, LANES)],
        flops=8_000_000,
    )
    (whole,) = call(
        whole_steps_kernel,
        "whole_steps",
        [initial, *whole_terms],
        [shape(2, 2, inner_rows, LANES)],
        fine_scratch(bands, 2, inner_rows)[1:],
        flops=20_000_000,
    )

    swap_0, swap_1, from_left, from_right, wide = call(
        functools.partial(message_kernel, lax.axis_size("col")),
        "row_messages",
        [coarse, own_meta, got_1, got_0, up_part, down_part, whole],
        [row_message, row_message, column_message, column_message, shape(2 * bands, coarse_height, LANES)],
    )
    got_1 = swap_with(swap_1, "row", 1)
    got_0 = swap_with(swap_0, "row", 0)

    middle, strip_e, first_ends, *strip_terms = call(
        strip_kernel,
        "strip",
        [strip_e, strip_f, from_left, from_right, wide, own_meta, whole],
        [shape(2, inner_rows, width), plane, shape(2, bands, SUB, LANES), *[strip_data] * 3],
        [
            scratch(bands, height, LANES),
            scratch(2, 1, inner_rows, LANES),
            scratch(2, 1, coarse_height, LANES),
            *fine_scratch(bands, 1, inner_rows),
        ],
        flops=16_000_000,
    )

    flow, coarse_flow, *_ = call(
        functools.partial(outer_kernel, lax.axis_size("row")),
        "outer_rows",
        [
            *frames, strip_e, first_ends, from_left, from_right, wide, got_1, got_0, middle, own_meta,
            *whole_terms, *strip_terms,
        ],
        [shape(2, height, width), shape(2, coarse_height, coarse_width), *[whole_data] * 3, *[strip_data] * 3],
        [
            scratch(ROW_MESSAGE, LANES),
            scratch(ROW_MESSAGE, LANES),
            scratch(2, 3, bands, 40, LANES),
            scratch(2 * bands, tall_rows, LANES),
            scratch(2, 3, tall_rows, LANES),
            scratch(2, 2 * EACH, LANES),
            scratch(2, 3, 2 * EACH, LANES),
            scratch(2, 2 * EACH, width),
            scratch(2, coarse_height, coarse_width),
            pltpu.SemaphoreType.DMA((4,)),
            *fine_scratch(bands, 3, 2 * EACH),
        ],
        out_specs=(hbm, hbm) + (vmem,) * 6,
        input_output_aliases={13 + k: 2 + k for k in range(6)},
    )
    return (flow, coarse_flow)


def solution(mesh):
    return jax.shard_map(
        local,
        mesh=mesh,
        in_specs=(P(None, "row", "col"), P(None, "row", "col"), P("row", "col", None)),
        out_specs=(P(None, "row", "col"), P(None, "row", "col")),
        check_vma=False,
    )
```

```python
import functools

import jax
import jax.numpy as jnp
from jax import lax
from jax.experimental import pallas as pl
from jax.experimental.pallas import tpu as pltpu
from jax.sharding import PartitionSpec as P

FACTOR = 8
MAXD = 4
BANDS = 4
STEPS = 3
LANES = 128
COLUMNS = 2 * LANES
HALF = 64
SUB = 8
DEPTH = 4
REACH = DEPTH + MAXD + 1
SLOT = 16
C_SECOND = 6
C_FIRST = 5
LEAD = 8
MARGIN = 48
EDGE = 46
GUARD = 8
HALO = 8
BEGIN = 40
EACH = MARGIN + 16
LIMIT = 0.3
ALPHA = 0.3
UNIT = 0.125 / ALPHA

S_MID = 55
S_RIGHT = 110
S_LEFT = LANES - REACH
S_TURN = COLUMNS - S_RIGHT - LANES

E8 = 0
H8 = 64
E1 = 72
H1 = 80
META = 81
F4 = 88
CS = 120
ROW_MESSAGE = 144
H_BAND = 32

COARSE_A = REACH + DEPTH
COARSE_B = SLOT + REACH + DEPTH
SHIFT_R = 2 * SLOT + REACH + DEPTH
SHIFT_C = SHIFT_R + 1
EXISTS = SHIFT_R + 2


def lanes_of(rows=SUB):
    return lax.broadcasted_iota(jnp.int32, (rows, LANES), 1)


def lanes_like(x):
    return lax.broadcasted_iota(jnp.int32, x.shape, 1)


def turn(x, amount):
    amount = amount % LANES
    return x if amount == 0 else pltpu.roll(x, amount, 1)


def turn_back(x, shift):
    return pltpu.roll(x, lax.rem(LANES - shift, LANES), 1)


def split_dot(x, exact):
    high = x.astype(jnp.bfloat16)
    rest = x - high.astype(jnp.float32)
    middle = rest.astype(jnp.bfloat16)
    low = (rest - middle.astype(jnp.float32)).astype(jnp.bfloat16)
    parts = [jnp.dot(part, exact, preferred_element_type=jnp.float32) for part in (low, middle, high)]
    return parts[0] + parts[1] + parts[2]


def scalar_at(ref, row, lane):
    return ref[row : row + 1, lane : lane + 1][0, 0]


def int_at(ref, row, lane):
    return scalar_at(ref, row, lane).astype(jnp.int32)


def is_even(axis, like):
    return jnp.broadcast_to(lax.axis_index(axis) % 2, like.shape) == 0


def without_ends(message, axis, count):
    place = jnp.broadcast_to(lax.axis_index(axis), message.shape)
    return jnp.where((place > 0) & (place < count - 1), message[...], 0.0)


def staggered(items, compute, store, depth, woven=None):
    pending = []
    for item in items:
        pending.append((item, compute(item)))
        if woven is not None:
            woven.advance()
        if len(pending) > depth:
            store(*pending.pop(0))
    for entry in pending:
        store(*entry)


class Woven:
    def __init__(self, stages):
        self.stages = stages
        self.result = None

    def advance(self):
        try:
            next(self.stages)
            return True
        except StopIteration as end:
            self.result = end.value if self.result is None else self.result
            return False

    def finish(self):
        while self.advance():
            pass
        return self.result


def pack_image(packed, to_right, planes, count, offset):
    bands, height, _ = planes[0].shape
    plane = planes[int(to_right)]
    start = LANES - count if to_right else 0
    length = height // 2
    lane = lanes_of(length)
    for half in range(2):
        for band in range(bands):
            at = half * HALF + band * SLOT + offset
            cells = turn(plane[band, half * length : (half + 1) * length, :], at - start)
            packed = cells if packed is None else jnp.where((lane >= at) & (lane < at + count), cells, packed)
    return packed


def pack_means(packed, to_right, means):
    length = packed.shape[0]
    start = LEAD + COLUMNS // FACTOR - C_SECOND if to_right else LEAD
    lane = lanes_of(length)
    for half in range(2):
        cells = means[half * length : (half + 1) * length]
        for at, first in ((half * HALF + COARSE_A, start), (half * HALF + COARSE_B, start + 3)):
            packed = jnp.where((lane >= at) & (lane < at + 3), turn(cells, at - first), packed)
    return packed


def column_meta(message):
    return (int_at(message, 0, SHIFT_R), int_at(message, 0, SHIFT_C)), scalar_at(message, 0, EXISTS)


def strip_second(base, from_left, from_right, rows, half, band):
    at = half * HALF + band * SLOT
    lane = lanes_like(base)
    cells = jnp.where(lane >= S_RIGHT, turn(from_right[rows, :], S_RIGHT - at), base)
    return jnp.where(lane >= S_LEFT, turn(from_left[rows, :], S_LEFT - at), cells)


def strip_first(base, from_left, from_right, rows, half, band):
    at = half * HALF + band * SLOT + REACH
    lane = lanes_like(base)
    cells = jnp.where(lane >= S_RIGHT, turn(from_right[rows, :], S_RIGHT - at), base)
    return jnp.where(lane >= S_LEFT, turn(from_left[rows, :], LANES - DEPTH - at), cells)


def strip_halo(base, beside, band, start, count):
    at = band * H_BAND + start
    lane = lanes_like(base)
    cells = jnp.where(lane >= S_RIGHT, turn(beside, S_RIGHT - at), base)
    return jnp.where(lane >= S_LEFT, turn(beside, LANES - count - at - SLOT), cells)


def strip_own(planes):
    return jnp.where(lanes_like(planes[0]) < S_MID, planes[0], turn(planes[1], -S_TURN))


def first_kernel(
    second_hbm, first_hbm, shifts_hbm, second_0, second_1, first_0, first_1, coarse, swap_0, swap_1, own_meta,
    shifts, sems, shift_sem,
):
    seconds, firsts = (second_0, second_1), (first_0, first_1)
    bands, height, _ = second_0.shape
    width = COLUMNS
    coarse_height = height // FACTOR
    lane = lanes_of()
    get_shifts = pltpu.make_async_copy(shifts_hbm, shifts, shift_sem)
    get_shifts.start()
    copies = []
    for image, (source, refs) in enumerate(((second_hbm, seconds), (first_hbm, firsts))):
        for band in range(bands):
            for tile, ref in enumerate(refs):
                copy = pltpu.make_async_copy(
                    source.at[band, :, pl.ds(tile * LANES, LANES)], ref.at[band], sems.at[image, band, tile]
                )
                copy.start()
                copies.append((image * bands + band, tile, ref, band, copy))
    cell = lax.broadcasted_iota(jnp.int32, (width, LANES), 0)
    place = lax.broadcasted_iota(jnp.int32, (width, LANES), 1)
    weights = jnp.where(place - LEAD == cell // FACTOR, 1.0 / (FACTOR * FACTOR), 0.0).astype(jnp.bfloat16)
    means = []
    packed = [None, None]
    for image, (count, offset) in enumerate(((REACH, 0), (DEPTH, REACH))):
        group = copies[image * 2 * bands : (image + 1) * 2 * bands]
        sums = {}
        for *_, copy in group:
            copy.wait()
        for plane, tile, ref, band, _ in group:
            parts = [ref[band, pl.ds(k, coarse_height, stride=FACTOR), :] for k in range(FACTOR)]
            while len(parts) > 1:
                parts = [x + y for x, y in zip(parts[::2], parts[1::2])]
            sums[plane, tile] = parts[0]
        tall = [jnp.concatenate([sums[image * bands + band, tile] for tile in range(2)], axis=1) for band in range(bands)]
        means.append(split_dot(jnp.concatenate(tall, axis=0), weights))
        packed = [
            pack_image(packed[side], bool(side), (seconds, firsts)[image], count, offset) for side in range(2)
        ]
    means = jnp.concatenate(means, axis=0)
    get_shifts.wait()
    shift_rows = shifts[0, 0, 0].astype(jnp.float32)
    shift_cols = shifts[0, 0, 1].astype(jnp.float32)
    place = lanes_of(height // 2) & (HALF - 1)
    packed = [
        jnp.where(place == SHIFT_R, shift_rows, jnp.where(place == SHIFT_C, shift_cols, jnp.where(place == EXISTS, 1.0, x)))
        for x in packed
    ]
    to_left, to_right = [pack_means(packed[side], bool(side), means) for side in range(2)]
    coarse[...] = means
    own_meta[...] = jnp.where(lane < HALF, shift_rows, shift_cols)
    even = is_even("col", swap_0)
    swap_0[...] = jnp.where(even, to_right, to_left)
    swap_1[...] = jnp.where(even, to_left, to_right)


def message_kernel(
    count, coarse, own_meta, got_1, got_0, up_part, down_part, _whole, swap_0, swap_1, from_left, from_right, wide
):
    other = without_ends(got_1, "col", count)
    even = is_even("col", got_0)
    from_right[...] = jnp.where(even, got_0[...], other)
    from_left[...] = jnp.where(even, other, got_0[...])
    planes_coarse, coarse_height, _ = wide.shape
    bands = planes_coarse // 2
    end = from_left.shape[0]
    coarse_width = COLUMNS // FACTOR
    lane = lanes_of()
    wides = []
    for plane in range(planes_coarse):
        half, block = divmod(plane, planes_coarse // 2)
        for step in range(coarse_height // SUB):
            own = slice(plane * coarse_height + step * SUB, plane * coarse_height + (step + 1) * SUB)
            rows = slice(block * coarse_height + step * SUB, block * coarse_height + (step + 1) * SUB)
            at = half * HALF
            left = from_left[rows, :]
            right = from_right[rows, :]
            start = LEAD - C_SECOND
            cells = turn(left, start - at - COARSE_A)
            cells = jnp.where(lane >= start + 3, turn(left, start + 3 - at - COARSE_B), cells)
            cells = jnp.where(lane >= LEAD, coarse[own, :], cells)
            start = LEAD + coarse_width
            cells = jnp.where(lane >= start, turn(right, start - at - COARSE_A), cells)
            cells = jnp.where(lane >= start + 3, turn(right, start + 3 - at - COARSE_B), cells)
            wides.append((plane, step, cells))
    for plane, step, cells in wides:
        wide[plane, step * SUB : (step + 1) * SUB, :] = cells
    row = lax.broadcasted_iota(jnp.int32, (SUB, LANES), 0)
    meta = jnp.where(lane < 16, own_meta[...], jnp.where(lane < 32, turn(own_meta[...], HALF), 1.0))
    for message, at in ((from_left, 48), (from_right, 80)):
        first_rows = message[0:SUB, :]
        rows = jnp.broadcast_to(first_rows[:, SHIFT_R : SHIFT_R + 1], (SUB, LANES))
        cols = jnp.broadcast_to(first_rows[:, SHIFT_C : SHIFT_C + 1], (SUB, LANES))
        meta = jnp.where(lane >= at, rows, meta)
        meta = jnp.where(lane >= at + 16, cols, meta)

    def beside(rows, half):
        left = from_left[rows, :]
        right = from_right[rows, :]
        cells = jnp.zeros((SUB, LANES), jnp.float32)
        for band in range(bands):
            at = half * HALF + band * SLOT
            cells = jnp.where(lane >= band * H_BAND, turn(right, band * H_BAND - at), cells)
            cells = jnp.where(lane >= band * H_BAND + SLOT, turn(left, band * H_BAND + SLOT - at), cells)
        return cells

    even = is_even("row", meta)
    parts = []
    for part, half, near, next_rows, row_of in (
        (up_part, 0, slice(0, 8), slice(8, 16), 0),
        (down_part, 1, slice(end - 8, end), slice(end - 16, end - 8), 7),
    ):
        eight = beside(near, half)
        one = beside(next_rows, half)
        one = jnp.broadcast_to(one[row_of : row_of + 1], (SUB, LANES))
        coarse_rows = []
        for band in range(bands):
            rows = slice(0, C_SECOND) if half == 0 else slice(coarse_height - C_SECOND, coarse_height)
            second = wide[band, rows, :]
            first = turn(wide[bands + band, rows, :], HALF)
            coarse_rows.append(jnp.where(lanes_like(second) < HALF, second, first))
        parts.append([
            (part[E8:H8, :], E8), (eight, H8), (part[E1:H1, :], E1), (jnp.where(row == 0, one, meta), H1),
            (part[F4:CS, :], F4), *[(x, CS + k * C_SECOND) for k, x in enumerate(coarse_rows)],
        ])
    for (up, at), (down, _) in zip(*parts):
        even = is_even("row", up)
        swap_0[at : at + up.shape[0], :] = jnp.where(even, down, up)
        swap_1[at : at + up.shape[0], :] = jnp.where(even, up, down)


def coarse_flow_of(second, first, mask):
    def along_rows(x):
        return pltpu.roll(x, x.shape[0] - 1, 0) - pltpu.roll(x, 1, 0)

    def along_cols(x):
        return pltpu.roll(x, LANES - 1, 1) - pltpu.roll(x, 1, 1)

    bands = BANDS
    size = second.shape[0] // bands
    grad_rows = 0.125 * along_rows(second)
    grad_cols = 0.125 * along_cols(second)
    offset = 0.25 * (second - first)
    data = jnp.clip(offset, -LIMIT, LIMIT)
    yield

    def pull(grads):
        terms = data * grads
        return sum(terms[k * size : (k + 1) * size] for k in range(bands))

    def tall(x):
        return jnp.concatenate([x] * bands, axis=0)

    flow = [-mask * pull(grad_rows), -mask * pull(grad_cols)]
    extrapolated = [2.0 * x for x in flow]
    dual_rows = [0.0, 0.0]
    dual_cols = [0.0, 0.0]
    yield
    for step in range(1, STEPS):
        changes = [(along_rows(x), along_cols(x)) for x in extrapolated]
        yield
        data = data + offset + grad_rows * tall(extrapolated[0]) + grad_cols * tall(extrapolated[1])
        data = jnp.clip(data, -LIMIT, LIMIT)
        yield
        for c in range(2):
            rows = dual_rows[c] + changes[c][0]
            cols = dual_cols[c] + changes[c][1]
            scale = jnp.minimum(mask, (8.0 * ALPHA) * lax.rsqrt(rows * rows + cols * cols))
            dual_rows[c] = rows * scale
            dual_cols[c] = cols * scale
        yield
        divergences = [along_rows(dual_rows[c]) + along_cols(dual_cols[c]) for c in range(2)]
        yield
        pulls = [pull(grad_rows), pull(grad_cols)]
        yield
        for c in range(2):
            following = flow[c] + mask * ((1.0 / 64.0) * divergences[c] - pulls[c])
            extrapolated[c] = 2.0 * following - flow[c]
            flow[c] = following
        yield
    return flow


def columns_of_planes(planes):
    whole = lax.broadcasted_iota(jnp.int32, (LANES, COLUMNS), 1)
    lane = lax.broadcasted_iota(jnp.int32, (LANES, LANES), 1)
    strip = jnp.where(lane < S_MID, lane, jnp.where(lane < S_LEFT, lane + (COLUMNS - S_RIGHT), lane - LANES))
    return jnp.concatenate([x for x, wanted in ((whole, "whole"), (strip, "strip")) if wanted in planes], axis=1)


def upsample(flow, planes, target):
    column = columns_of_planes(planes)
    source = lax.broadcasted_iota(jnp.int32, column.shape, 0)
    spread = jnp.where(source - LEAD == lax.shift_right_arithmetic(column, 3), float(FACTOR), 0.0).astype(jnp.bfloat16)
    rows = flow[0].shape[0]
    wide = split_dot(UNIT * jnp.concatenate(flow, axis=0), spread)
    for c in range(2):
        for tile in range(column.shape[1] // LANES):
            target[c, tile] = wide[c * rows : (c + 1) * rows, tile * LANES : (tile + 1) * LANES]


def repeat_rows(spread, initial, cells):
    for c in range(2):
        for tile in range(initial.shape[1]):
            rows = [jnp.broadcast_to(spread[c, tile, cell : cell + 1, :], (SUB, LANES)) for cell in cells]
            initial[c, tile, GUARD : GUARD + SUB * len(cells), :] = jnp.concatenate(rows, axis=0)


def shift_whole(here, shift):
    turned = [turn_back(x, shift) for x in here]
    lane = lanes_like(here[0])
    return [
        jnp.where(lane + shift >= LANES, turned[1], turned[0]),
        jnp.where(lane + shift < 0, turned[0], turned[1]),
    ]


def edge_lanes(rows):
    lane = lanes_of(rows)
    return lane == LANES - 1, lane == 0


def columns_whole(fields, edges):
    last, first = edges
    ahead = [pltpu.roll(x, LANES - 1, 1) for x in fields]
    behind = [pltpu.roll(x, 1, 1) for x in fields]
    return [
        jnp.where(last, ahead[1], ahead[0]) - behind[0],
        ahead[1] - jnp.where(first, behind[0], behind[1]),
    ]


def rows_within(tall):
    size = tall.shape[0]
    return (pltpu.roll(tall, size - 1, 0) - pltpu.roll(tall, 1, 0))[SUB : size - SUB]


def columns_strip(field):
    return pltpu.roll(field, LANES - 1, 1) - pltpu.roll(field, 1, 1)


def strip_windows(window, centre, right, left):
    own = turn_back(window(centre[0]), centre[1])
    beyond_left = turn_back(window(left[0]), left[1])
    beyond_right = turn_back(window(right[0]), right[1])
    lane = lanes_like(own)
    beyond = jnp.where((lane >= S_LEFT) | (lane < S_MID), beyond_left, beyond_right)
    is_beyond = lane >= S_RIGHT
    return jnp.where(is_beyond, beyond, own), jnp.where(is_beyond, columns_strip(beyond), columns_strip(own))


def fine_steps(
    rows_total, chunk, columns, initial, extrap, dual_rows, dual_cols, change, dual_data,
    offsets, grads_rows, grads_cols, data_row, masks_of, result, done=lambda k: None,
):
    assert STEPS == 3
    planes = len(offsets)
    bands = offsets[0].shape[0]
    chunks = rows_total // chunk

    def clip(x):
        return jnp.clip(x, -UNIT * LIMIT, UNIT * LIMIT)

    tiles = range(planes)

    for step in range(STEPS):
        source = initial if step == 0 else extrap
        final = step == STEPS - 1

        def dual(item, source=source, step=step):
            k, c = item
            row = GUARD + k * chunk
            at, own = pl.ds(row, chunk), pl.ds(k * chunk, chunk)
            masks = masks_of(own)
            talls = [source[c, tile, pl.ds(row - SUB, chunk + 2 * SUB), :] for tile in tiles]
            along = columns([x[SUB : SUB + chunk] for x in talls])
            values = []
            for tile in tiles:
                rows = rows_within(talls[tile])
                cols = along[tile]
                if step > 0:
                    rows = rows + dual_rows[c, tile, at, :]
                    cols = cols + dual_cols[c, tile, own, :]
                scale = jnp.minimum(masks[tile], lax.rsqrt(rows * rows + cols * cols))
                values.append((rows * scale, cols * scale))
            return values

        def store_dual(item, values):
            k, c = item
            for tile, (rows, cols) in enumerate(values):
                dual_rows[c, tile, pl.ds(GUARD + k * chunk, chunk), :] = rows
                dual_cols[c, tile, pl.ds(k * chunk, chunk), :] = cols

        staggered([(k, c) for k in range(chunks) for c in range(2)], dual, store_dual, 1)
        along_of = {}

        def primal(item, step=step, final=final, along_of=along_of):
            k, tile = item
            row = GUARD + k * chunk
            at, own, data = pl.ds(row, chunk), pl.ds(k * chunk, chunk), pl.ds(data_row(k), chunk)
            if k not in along_of:
                along_of[k] = [columns([dual_cols[c, t, own, :] for t in tiles]) for c in range(2)]
            mask = masks_of(own)[tile]
            start = [initial[c, tile, at, :] for c in range(2)]
            if step > 0:
                moved = [extrap[c, tile, at, :] - start[c] for c in range(2)]
            if step == 1:
                changes = [0.5 * x for x in moved]
            if step == 2:
                changes = [change[c, tile, own, :] for c in range(2)]
            pulls = [None, None]
            duals = []
            for band in range(bands):
                gradient = (grads_rows[tile][band, data, :], grads_cols[tile][band, data, :])
                value = offsets[tile][band, data, :]
                if step > 0:
                    earlier = clip(value) if step == 1 else dual_data[band, tile, own, :]
                    value = (value + earlier) + (gradient[0] * moved[0] + gradient[1] * moved[1])
                value = clip(value)
                duals.append(value)
                for c in range(2):
                    term = value * gradient[c]
                    pulls[c] = term if pulls[c] is None else pulls[c] + term
            flows, nexts = [], []
            for c in range(2):
                tall = dual_rows[c, tile, pl.ds(row - SUB, chunk + 2 * SUB), :]
                divergence = rows_within(tall) + along_of[k][c][tile]
                moving = (mask * (1.0 / 64.0)) * divergence - pulls[c]
                total = moving if step == 0 else changes[c] + moving
                flows.append((start[c] + total) * (1.0 / UNIT) if final else total)
                nexts.append(None if final else start[c] + (total + moving))
            return flows, nexts, duals

        def store_primal(item, results, step=step, final=final):
            k, tile = item
            flows, nexts, duals = results
            own = pl.ds(k * chunk, chunk)
            for c in range(2):
                if final:
                    result[c, tile, own, :] = flows[c]
                else:
                    if step > 0:
                        change[c, tile, own, :] = flows[c]
                    extrap[c, tile, pl.ds(GUARD + k * chunk, chunk), :] = nexts[c]
            if final:
                if tile == planes - 1:
                    done(k)
            elif step > 0:
                for band in range(bands):
                    dual_data[band, tile, own, :] = duals[band]

        staggered([(k, tile) for k in range(chunks) for tile in tiles], primal, store_primal, 1)


def clear_guards(*refs):
    for ref in refs:
        rows = ref.shape[2]
        zero = jnp.zeros((GUARD, LANES), jnp.float32)
        for c in range(2):
            for tile in range(ref.shape[1]):
                ref[c, tile, 0:GUARD, :] = zero
                ref[c, tile, rows - GUARD : rows, :] = zero


def fine_scratch(bands, planes, rows):
    guarded = pltpu.VMEM((2, planes, rows + 2 * GUARD, LANES), jnp.float32)
    plain = pltpu.VMEM((2, planes, rows, LANES), jnp.float32)
    return [guarded, guarded, guarded, plain, plain, pltpu.VMEM((bands, planes, rows, LANES), jnp.float32)]


def pieces(bands, height, rows):
    assert (height - 2 * SUB) % rows == 0
    return [(band, row) for row in range(SUB, height - SUB, rows) for band in range(bands)]


def whole_terms_kernel(
    second_0, second_1, first_0, first_1, coarse, own_meta,
    offset, grad_rows, grad_cols, initial, strip_e, strip_f, up, down, moved, spread,
):
    seconds, firsts = (second_0, second_1), (first_0, first_1)
    bands, height, _ = second_0.shape
    block = 120
    coarse_height = coarse.shape[0] // (2 * bands)
    shift_rows, shift_cols = scalar_at(own_meta, 0, 0), scalar_at(own_meta, 0, HALF)
    centre = (shift_rows.astype(jnp.int32), shift_cols.astype(jnp.int32))
    def windows(band, row, rows):
        here = [ref[band, pl.ds(row + centre[0], rows), :].reshape(-1, LANES) for ref in seconds]
        return shift_whole(here, centre[1])

    woven = Woven(coarse_flow_of(coarse[0 : bands * coarse_height, :], coarse[bands * coarse_height :, :], 1.0))

    ends = [(row, windows(slice(None), row, SUB)) for row in (SUB // 2, height - SUB - SUB // 2)]
    for row, values in ends:
        for tile in range(2):
            moved[tile, :, row : row + SUB, :] = values[tile].reshape(bands, SUB, LANES)

    edges = edge_lanes(block)

    def values_of(item):
        band, row = item
        values = windows(band, row, block)
        along = columns_whole(values, edges)
        own = [ref[band, row : row + block, :] for ref in firsts]
        return values, [(0.25 * UNIT) * (x - y) for x, y in zip(values, own)], [0.125 * x for x in along]

    def store_values(item, results):
        band, row = item
        values, offsets, gradients = results
        data = slice(row + HALO, row + HALO + block)
        for tile in range(2):
            moved[tile, band, row : row + block, :] = values[tile]
            offset[tile, band, data, :] = offsets[tile]
            grad_cols[tile, band, data, :] = gradients[tile]

    staggered(pieces(bands, height, block), values_of, store_values, 1, woven)

    def strips_of(item):
        band, row = item
        rows = slice(row, row + LANES)
        return strip_own([ref[band, rows, :] for ref in seconds]), strip_own([ref[band, rows, :] for ref in firsts])

    def store_strips(item, results):
        band, row = item
        strip_e[band, row : row + LANES, :], strip_f[band, row : row + LANES, :] = results

    staggered([(band, row) for band in range(bands) for row in range(0, height, LANES)], strips_of, store_strips, 1, woven)

    def gradient_of(item):
        band, row = item
        return [0.125 * rows_within(moved[tile, band, row - SUB : row + 120 + SUB, :]) for tile in range(2)]

    def store_gradient(item, results):
        band, row = item
        for tile in range(2):
            grad_rows[tile, band, row + HALO : row + HALO + 120, :] = results[tile]

    staggered(pieces(bands, height, 120), gradient_of, store_gradient, 1, woven)

    parts = []
    for band in range(bands):
        for second, first in zip(seconds, firsts):
            parts.append((
                second[band, 0:16, :], first[band, 0:8, :],
                second[band, height - 16 : height, :], first[band, height - 8 : height, :],
            ))
    for k, (second_top, first_top, second_end, first_end) in enumerate(parts):
        up[E8 + 8 * k : E8 + 8 * k + 8, :] = second_top[0:8]
        up[E1 + k : E1 + k + 1, :] = second_top[8:9]
        up[F4 + 4 * k : F4 + 4 * k + 4, :] = first_top[0:4]
        down[E8 + 8 * k : E8 + 8 * k + 8, :] = second_end[8:16]
        down[E1 + k : E1 + k + 1, :] = second_end[7:8]
        down[F4 + 4 * k : F4 + 4 * k + 4, :] = first_end[4:8]
    for target in (up, down):
        for start, end in ((H8, E1), (H1, F4), (CS, ROW_MESSAGE)):
            target[start:end, :] = jnp.zeros((end - start, LANES), jnp.float32)

    upsample(woven.finish(), ("whole",), spread)
    clear_guards(initial)
    rows_total = initial.shape[2] - 2 * GUARD
    repeat_rows(spread, initial, [BEGIN // FACTOR + k for k in range(rows_total // SUB)])


def whole_steps_kernel(
    initial, offset, grad_rows, grad_cols, result, extrap, dual_rows, dual_cols, change, dual_data
):
    rows_total = result.shape[2]
    clear_guards(extrap, dual_rows)
    chunk = 88
    edges = edge_lanes(chunk)
    fine_steps(
        rows_total, chunk, lambda fields: columns_whole(fields, edges),
        initial, extrap, dual_rows, dual_cols, change, dual_data,
        *[[ref.at[tile] for tile in range(2)] for ref in (offset, grad_rows, grad_cols)],
        lambda k: HALO + BEGIN + k * chunk, lambda own: (1.0, 1.0), result,
    )


def strip_kernel(
    strip_e, strip_f, from_left, from_right, wide, own_meta, whole,
    middle, strip_out, first_ends, offset, grad_rows, grad_cols,
    moved, result, spread, initial, extrap, dual_rows, dual_cols, change, dual_data,
):
    bands, height, _ = strip_e.shape
    block = 120
    coarse_height = height // FACTOR
    coarse_width = COLUMNS // FACTOR
    rows_total = height - 2 * BEGIN
    lane = lanes_of()
    centre = (int_at(own_meta, 0, 0), int_at(own_meta, 0, HALF))
    right, has_right = column_meta(from_right)
    left, has_left = column_meta(from_left)
    exists = jnp.where(lane < S_RIGHT, 1.0, jnp.where(lane < S_LEFT, has_right, has_left))

    def tall_factor(rows):
        return 0.125 * jnp.concatenate([exists] * (rows // SUB), axis=0)

    mask = jnp.where(lane < LEAD, has_left, jnp.where(lane < LEAD + coarse_width, 1.0, has_right))
    mask = jnp.concatenate([mask] * (coarse_height // SUB), axis=0)
    cells = [wide[k * bands : (k + 1) * bands].reshape(bands * coarse_height, LANES) for k in range(2)]
    woven = Woven(coarse_flow_of(*cells, mask))

    def halves(row, rows):
        half = row // (height // 2)
        start = row - half * (height // 2)
        return half, slice(start, start + rows)

    def second_of(item):
        band, row = item
        half, message = halves(row, LANES)
        return strip_second(strip_e[band, row : row + LANES, :], from_left, from_right, message, half, band)

    def store_second(item, value):
        band, row = item
        strip_out[band, row : row + LANES, :] = value

    staggered([(band, row) for row in range(0, height, LANES) for band in range(bands)], second_of, store_second, 1, woven)

    def first_of(band, row, rows):
        half, message = halves(row, rows)
        return strip_first(strip_f[band, row : row + rows, :], from_left, from_right, message, half, band)

    firsts = [(end, band, first_of(band, (0, height - SUB)[end], SUB)) for end in range(2) for band in range(bands)]
    for end, band, value in firsts:
        first_ends[end, band] = value

    def windows(band, row, rows):
        return strip_windows(
            lambda shift: strip_out[band, pl.ds(row + shift, rows), :].reshape(-1, LANES), centre, right, left
        )

    ends = [(row, windows(slice(None), row, SUB)[0]) for row in (SUB // 2, height - SUB - SUB // 2)]
    for row, value in ends:
        moved[:, row : row + SUB, :] = value.reshape(bands, SUB, LANES)

    factor = tall_factor(block)

    def values_of(item):
        band, row = item
        value, along = windows(band, row, block)
        return value, (0.25 * UNIT) * (value - first_of(band, row, block)), factor * along

    def store_values(item, results):
        band, row = item
        data = slice(row + HALO, row + HALO + block)
        moved[band, row : row + block, :], offset[band, data, :], grad_cols[band, data, :] = results

    staggered(pieces(bands, height, block), values_of, store_values, 1, woven)

    def gradient_of(item):
        band, row = item
        return factor * rows_within(moved[band, row - SUB : row + block + SUB, :])

    def store_gradient(item, value):
        band, row = item
        grad_rows[band, row + HALO : row + HALO + block, :] = value

    staggered(pieces(bands, height, block), gradient_of, store_gradient, 1, woven)

    upsample(woven.finish(), ("strip",), spread)
    clear_guards(initial, extrap, dual_rows)
    repeat_rows(spread, initial, [BEGIN // FACTOR + k for k in range(rows_total // SUB)])

    chunk = 176
    masks = jnp.concatenate([exists] * (chunk // SUB), axis=0)
    fine_steps(
        rows_total, chunk, lambda fields: [columns_strip(fields[0])],
        initial, extrap, dual_rows, dual_cols, change, dual_data, [offset], [grad_rows], [grad_cols],
        lambda k: HALO + BEGIN + k * chunk, lambda own: (masks,), result,
    )
    join(whole, result.at[:, 0], middle, slice(0, rows_total))


def join(whole, strip, target, rows):
    lane = lanes_of(rows.stop - rows.start)
    values = []
    for c in range(2):
        edge = strip[c, rows, :]
        start = jnp.where(lane < EDGE, edge, whole[c, 0, rows, :])
        values.append((start, jnp.where(lane >= LANES - EDGE, turn(edge, S_TURN), whole[c, 1, rows, :])))
    for c in range(2):
        target[c, rows, 0:LANES], target[c, rows, LANES:COLUMNS] = values[c]


def outer_kernel(
    count, second_0, second_1, first_0, first_1, strip_e, first_ends, from_left, from_right, wide, got_1, got_0, middle, own_meta,
    _wo, _wr, _wc, _so, _sr, _sc,
    flow_out, coarse_out, whole_offset, whole_rows, whole_cols, strip_offset, strip_rows, strip_cols,
    from_up, from_down, extended, tall, spread, masks, result, joined, coarse_result, sems,
    initial, extrap, dual_rows, dual_cols, change, dual_data,
):
    bands, height, _ = second_0.shape
    coarse_height = height // FACTOR
    coarse_width = COLUMNS // FACTOR
    rows_total = 2 * EACH
    lane = lanes_of()

    put_middle = pltpu.make_async_copy(
        middle.at[:, pl.ds(MARGIN - BEGIN, height - 2 * MARGIN), :],
        flow_out.at[:, pl.ds(MARGIN, height - 2 * MARGIN), :],
        sems.at[0],
    )
    put_middle.start()

    other = without_ends(got_1, "row", count)
    even = is_even("row", got_0)
    from_down[...] = jnp.where(even, got_0[...], other)
    from_up[...] = jnp.where(even, other, got_0[...])

    own = (int_at(own_meta, 0, 0), int_at(own_meta, 0, HALF))
    own_right, has_right = column_meta(from_right)
    own_left, has_left = column_meta(from_left)
    has_up = scalar_at(from_up, META, 32)
    has_down = scalar_at(from_down, META, 32)
    exists = jnp.where(lane < S_RIGHT, 1.0, jnp.where(lane < S_LEFT, has_right, has_left))

    def trio(message):
        return (
            (int_at(message, META, 0), int_at(message, META, 16)),
            (int_at(message, META, 80), int_at(message, META, 96)),
            (int_at(message, META, 48), int_at(message, META, 64)),
        )

    above = trio(from_up)
    below = trio(from_down)

    zero = jnp.zeros((SUB, LANES), jnp.float32)
    tall_rows = coarse_height + 2 * LEAD
    parts = []
    fill = jnp.zeros((LEAD - C_SECOND, LANES), jnp.float32)
    for plane in range(2 * bands):
        at = CS + C_SECOND * (plane % bands)
        ends = [turn(message[at : at + C_SECOND, :], HALF * (plane // bands)) for message in (from_up, from_down)]
        parts.append([fill, ends[0], wide[plane], ends[1], fill])
    for plane, values in enumerate(parts):
        tall[plane] = jnp.concatenate(values, axis=0)
    across = jnp.where(lane < LEAD, has_left, jnp.where(lane < LEAD + coarse_width, 1.0, has_right))
    mask = jnp.concatenate([across * has_up] + [across] * (coarse_height // SUB) + [across * has_down], axis=0)
    for end in range(2):
        message = (from_up, from_down)[end]
        beside = message[H8 : H8 + 8, :]
        beside_one = jnp.broadcast_to(message[H1 : H1 + 1, :], (SUB, LANES))
        parts = []
        for band in range(bands):
            eights = [message[E8 + 8 * k : E8 + 8 * k + 8, :] for k in (2 * band, 2 * band + 1)]
            ones = [jnp.broadcast_to(message[E1 + k : E1 + k + 1, :], (SUB, LANES)) for k in (2 * band, 2 * band + 1)]
            eights.append(strip_halo(strip_own(eights), beside, band, 0, REACH))
            ones.append(strip_halo(strip_own(ones), beside_one, band, 0, REACH))
            for tile, (eight, one) in enumerate(zip(eights, ones)):
                source = (second_0, second_1, strip_e)[tile]
                if end == 0:
                    parts.append((tile, band, [one, eight, source[band, 0:24, :]]))
                else:
                    parts.append((tile, band, [source[band, height - 24 : height, :], eight, one]))
        for tile, band, values in parts:
            extended[end, tile, band] = jnp.concatenate(values, axis=0)
    cells = [tall[k * bands : (k + 1) * bands].reshape(bands * tall_rows, LANES) for k in range(2)]
    woven = Woven(coarse_flow_of(*cells, mask))
    edges = edge_lanes(bands * SUB)
    rows_data = whole_offset.shape[2]
    exists_tall = jnp.concatenate([exists] * bands, axis=0)

    def rows_of(halo, end):
        if halo:
            return slice(0, SUB) if end == 0 else slice(rows_data - SUB, rows_data)
        return slice(HALO, HALO + SUB) if end == 0 else slice(rows_data - HALO - SUB, rows_data - HALO)

    def values_of(item):
        halo, end = item
        message = (from_up, from_down)[end]
        base = (SUB, 3 * SUB)[end] if halo else 2 * SUB
        shifts = (above, below)[end] if halo else (own, own_right, own_left)
        factor = 0.125 * (has_up, has_down)[end] if halo else 0.125

        def here(tile, shift):
            return extended[end, tile, :, pl.ds(base + shift, SUB), :].reshape(-1, LANES)

        def down_up(tile, shift):
            return here(tile, shift + 1) - here(tile, shift - 1)

        own_rows = slice(0, SUB) if end == 0 else slice(height - SUB, height)
        if halo:
            firsts = [[], [], []]
            for band in range(bands):
                eights = []
                for k in (2 * band, 2 * band + 1):
                    four = message[F4 + 4 * k : F4 + 4 * k + 4, :]
                    eights.append(jnp.concatenate([four, four], axis=0))
                eights.append(strip_halo(strip_own(eights), message[H8 : H8 + 8, :], band, REACH, DEPTH))
                for tile in range(3):
                    firsts[tile].append(eights[tile])
            firsts = [jnp.concatenate(x, axis=0) for x in firsts]
        else:
            firsts = [x.reshape(-1, LANES) for x in (first_0[:, own_rows, :], first_1[:, own_rows, :], first_ends[end])]
        centre = shifts[0]
        values = shift_whole([here(tile, centre[0]) for tile in range(2)], centre[1])
        changes = shift_whole([down_up(tile, centre[0]) for tile in range(2)], centre[1])
        along = columns_whole(values, edges)
        value, across_cols = strip_windows(lambda shift: here(2, shift), *shifts)
        change_rows, _ = strip_windows(lambda shift: down_up(2, shift), *shifts)
        return (
            [(0.25 * UNIT) * (x - y) for x, y in zip([*values, value], firsts)],
            [*[factor * x for x in changes], (factor * exists_tall) * change_rows],
            [*[factor * x for x in along], (factor * exists_tall) * across_cols],
        )

    def store_values(item, results):
        rows = rows_of(*item)
        for values, whole, strip in zip(
            results, (whole_offset, whole_rows, whole_cols), (strip_offset, strip_rows, strip_cols)
        ):
            values = [x.reshape(bands, SUB, LANES) for x in values]
            for tile in range(2):
                whole[tile, :, rows, :] = values[tile]
            strip[:, rows, :] = values[2]

    staggered([(halo, end) for halo in (True, False) for end in range(2)], values_of, store_values, 1, woven)

    flow = woven.finish()
    for c in range(2):
        coarse_result[c] = turn(flow[c][LEAD : LEAD + coarse_height], -LEAD)[:, :coarse_width]
    put_coarse = pltpu.make_async_copy(coarse_result, coarse_out, sems.at[1])
    put_coarse.start()
    upsample(flow, ("whole", "strip"), spread)
    clear_guards(initial, extrap, dual_rows)
    each = EACH // SUB
    repeat_rows(
        spread, initial,
        [LEAD - 1 + k for k in range(each)] + [tall_rows - LEAD + 1 - each + k for k in range(each)],
    )

    for i, value in enumerate((jnp.ones((SUB, LANES), jnp.float32), exists)):
        masks[i] = jnp.concatenate([value * has_up] + [value] * (rows_total // SUB - 2) + [value * has_down], axis=0)

    def masks_of(rows):
        whole = masks[0, rows, :]
        return (whole, whole, masks[1, rows, :])

    chunk = EACH
    edges = edge_lanes(chunk)
    puts = [
        pltpu.make_async_copy(
            joined.at[:, pl.ds(k * EACH + SUB, MARGIN), :],
            flow_out.at[:, pl.ds(k * (height - MARGIN), MARGIN), :],
            sems.at[2 + k],
        )
        for k in range(2)
    ]

    def finish(k):
        join(result, result.at[:, 2], joined, slice(k * EACH + SUB, k * EACH + SUB + MARGIN))
        puts[k].start()

    def data_row(k):
        return k * (rows_data - EACH)

    fine_steps(
        rows_total, chunk, lambda fields: columns_whole(fields[:2], edges) + [columns_strip(fields[2])],
        initial, extrap, dual_rows, dual_cols, change, dual_data,
        [whole_offset.at[0], whole_offset.at[1], strip_offset],
        [whole_rows.at[0], whole_rows.at[1], strip_rows],
        [whole_cols.at[0], whole_cols.at[1], strip_cols],
        data_row, masks_of, result, finish,
    )
    put_middle.wait()
    put_coarse.wait()
    for put in puts:
        put.wait()


def swap_with(message, axis, start):
    names = ("row", "col")
    sizes = [lax.axis_size(name) for name in names]
    along = names.index(axis)
    count, others = sizes[along], sizes[1 - along]

    def number(place, other):
        row, col = (place, other) if along == 0 else (other, place)
        return row * sizes[1] + col

    pairs = [(number(i, k), number(i + 1, k)) for i in range(start, count - 1, 2) for k in range(others)]
    if start:
        pairs += [(number(i, k), number(i, k + 1)) for i in (0, count - 1) for k in range(0, others, 2)]
    return lax.ppermute(message, names, pairs + [(j, i) for i, j in pairs])


def local(frame_first, frame_second, shifts):
    bands, height, width = frame_first.shape
    assert bands == 4 and width == COLUMNS and height % LANES == 0
    assert lax.axis_size("row") % 2 == 0 and lax.axis_size("col") % 2 == 0
    coarse_height = height // FACTOR
    coarse_width = width // FACTOR
    vmem = pl.BlockSpec(memory_space=pltpu.VMEM)
    hbm = pl.BlockSpec(memory_space=pltpu.HBM)
    tall_rows = coarse_height + 2 * LEAD
    inner_rows = height - 2 * BEGIN

    def shape(*sizes):
        return jax.ShapeDtypeStruct(sizes, jnp.float32)

    def scratch(*sizes):
        return pltpu.VMEM(sizes, jnp.float32)

    def call(kernel, name, arguments, outs, scratches=(), flops=1_000_000, **more):
        more = {"in_specs": [vmem] * len(arguments), "out_specs": (vmem,) * len(outs), **more}
        return pl.pallas_call(
            kernel,
            out_shape=tuple(outs),
            scratch_shapes=list(scratches),
            compiler_params=pltpu.CompilerParams(vmem_limit_bytes=24 * 1024 * 1024),
            cost_estimate=pl.CostEstimate(flops=flops, bytes_accessed=1_000_000, transcendentals=0),
            name=name,
            **more,
        )(*arguments)

    plane = shape(bands, height, LANES)
    column_message = shape(height // 2, LANES)
    row_message = shape(ROW_MESSAGE, LANES)
    whole_data = shape(2, bands, height + 2 * HALO, LANES)
    strip_data = shape(bands, height + 2 * HALO, LANES)

    *frames, coarse, swap_0, swap_1, own_meta = call(
        first_kernel,
        "means_and_message",
        [pltpu.with_memory_space_constraint(x, pltpu.HBM) for x in (frame_second, frame_first, shifts)],
        [*[plane] * 4, shape(2 * bands * coarse_height, LANES), column_message, column_message, shape(SUB, LANES)],
        [
            pltpu.SMEM((1, 1, 2), jnp.int32),
            pltpu.SemaphoreType.DMA((2, bands, 2)),
            pltpu.SemaphoreType.DMA,
        ],
        in_specs=[hbm] * 3,
    )
    got_1 = swap_with(swap_1, "col", 1)
    got_0 = swap_with(swap_0, "col", 0)

    *whole_terms, initial, strip_e, strip_f, up_part, down_part = call(
        whole_terms_kernel,
        "whole_terms",
        [*frames, coarse, own_meta],
        [
            *[whole_data] * 3, shape(2, 2, inner_rows + 2 * GUARD, LANES),
            plane, plane, row_message, row_message,
        ],
        [scratch(2, bands, height, LANES), scratch(2, 2, coarse_height, LANES)],
        flops=8_000_000,
    )
    (whole,) = call(
        whole_steps_kernel,
        "whole_steps",
        [initial, *whole_terms],
        [shape(2, 2, inner_rows, LANES)],
        fine_scratch(bands, 2, inner_rows)[1:],
        flops=20_000_000,
    )

    swap_0, swap_1, from_left, from_right, wide = call(
        functools.partial(message_kernel, lax.axis_size("col")),
        "row_messages",
        [coarse, own_meta, got_1, got_0, up_part, down_part, whole],
        [row_message, row_message, column_message, column_message, shape(2 * bands, coarse_height, LANES)],
    )
    got_1 = swap_with(swap_1, "row", 1)
    got_0 = swap_with(swap_0, "row", 0)

    middle, strip_e, first_ends, *strip_terms = call(
        strip_kernel,
        "strip",
        [strip_e, strip_f, from_left, from_right, wide, own_meta, whole],
        [shape(2, inner_rows, width), plane, shape(2, bands, SUB, LANES), *[strip_data] * 3],
        [
            scratch(bands, height, LANES),
            scratch(2, 1, inner_rows, LANES),
            scratch(2, 1, coarse_height, LANES),
            *fine_scratch(bands, 1, inner_rows),
        ],
        flops=16_000_000,
    )

    flow, coarse_flow, *_ = call(
        functools.partial(outer_kernel, lax.axis_size("row")),
        "outer_rows",
        [
            *frames, strip_e, first_ends, from_left, from_right, wide, got_1, got_0, middle, own_meta,
            *whole_terms, *strip_terms,
        ],
        [shape(2, height, width), shape(2, coarse_height, coarse_width), *[whole_data] * 3, *[strip_data] * 3],
        [
            scratch(ROW_MESSAGE, LANES),
            scratch(ROW_MESSAGE, LANES),
            scratch(2, 3, bands, 40, LANES),
            scratch(2 * bands, tall_rows, LANES),
            scratch(2, 3, tall_rows, LANES),
            scratch(2, 2 * EACH, LANES),
            scratch(2, 3, 2 * EACH, LANES),
            scratch(2, 2 * EACH, width),
            scratch(2, coarse_height, coarse_width),
            pltpu.SemaphoreType.DMA((4,)),
            *fine_scratch(bands, 3, 2 * EACH),
        ],
        out_specs=(hbm, hbm) + (vmem,) * 6,
        input_output_aliases={13 + k: 2 + k for k in range(6)},
    )
    return (flow, coarse_flow)


def solution(mesh):
    return jax.shard_map(
        local,
        mesh=mesh,
        in_specs=(P(None, "row", "col"), P(None, "row", "col"), P("row", "col", None)),
        out_specs=(P(None, "row", "col"), P(None, "row", "col")),
        check_vma=False,
    )
```

```python
import functools

import jax
import jax.numpy as jnp
from jax import lax
from jax.experimental import pallas as pl
from jax.experimental.pallas import tpu as pltpu
from jax.sharding import PartitionSpec as P

FACTOR = 8
MAXD = 4
BANDS = 4
STEPS = 3
LANES = 128
COLUMNS = 2 * LANES
HALF = 64
SUB = 8
DEPTH = 4
REACH = DEPTH + MAXD + 1
SLOT = 16
C_SECOND = 6
C_FIRST = 5
LEAD = 8
MARGIN = 48
EDGE = 46
GUARD = 8
HALO = 8
BEGIN = 40
EACH = MARGIN + 16
LIMIT = 0.3
ALPHA = 0.3
UNIT = 0.125 / ALPHA

S_MID = 55
S_RIGHT = 110
S_LEFT = LANES - REACH
S_TURN = COLUMNS - S_RIGHT - LANES

E8 = 0
H8 = 64
E1 = 72
H1 = 80
META = 81
F4 = 88
CS = 120
ROW_MESSAGE = 144
H_BAND = 32

COARSE_A = REACH + DEPTH
COARSE_B = SLOT + REACH + DEPTH
SHIFT_R = 2 * SLOT + REACH + DEPTH
SHIFT_C = SHIFT_R + 1
EXISTS = SHIFT_R + 2


def lanes_of(rows=SUB):
    return lax.broadcasted_iota(jnp.int32, (rows, LANES), 1)


def lanes_like(x):
    return lax.broadcasted_iota(jnp.int32, x.shape, 1)


def turn(x, amount):
    amount = amount % LANES
    return x if amount == 0 else pltpu.roll(x, amount, 1)


def turn_back(x, shift):
    return pltpu.roll(x, lax.rem(LANES - shift, LANES), 1)


def split_dot(x, exact):
    high = x.astype(jnp.bfloat16)
    rest = x - high.astype(jnp.float32)
    middle = rest.astype(jnp.bfloat16)
    low = (rest - middle.astype(jnp.float32)).astype(jnp.bfloat16)
    parts = [jnp.dot(part, exact, preferred_element_type=jnp.float32) for part in (low, middle, high)]
    return parts[0] + parts[1] + parts[2]


def scalar_at(ref, row, lane):
    return ref[row : row + 1, lane : lane + 1][0, 0]


def int_at(ref, row, lane):
    return scalar_at(ref, row, lane).astype(jnp.int32)


def is_even(axis, like):
    return jnp.broadcast_to(lax.axis_index(axis) % 2, like.shape) == 0


def without_ends(message, axis, count):
    place = jnp.broadcast_to(lax.axis_index(axis), message.shape)
    return jnp.where((place > 0) & (place < count - 1), message[...], 0.0)


def staggered(items, compute, store, depth, woven=None):
    pending = []
    for item in items:
        pending.append((item, compute(item)))
        if woven is not None:
            woven.advance()
        if len(pending) > depth:
            store(*pending.pop(0))
    for entry in pending:
        store(*entry)


class Woven:
    def __init__(self, stages):
        self.stages = stages
        self.result = None

    def advance(self):
        try:
            next(self.stages)
            return True
        except StopIteration as end:
            self.result = end.value if self.result is None else self.result
            return False

    def finish(self):
        while self.advance():
            pass
        return self.result


def pack_image(packed, to_right, planes, count, offset):
    bands, height, _ = planes[0].shape
    plane = planes[int(to_right)]
    start = LANES - count if to_right else 0
    length = height // 2
    lane = lanes_of(length)
    for half in range(2):
        for band in range(bands):
            at = half * HALF + band * SLOT + offset
            cells = turn(plane[band, half * length : (half + 1) * length, :], at - start)
            packed = cells if packed is None else jnp.where((lane >= at) & (lane < at + count), cells, packed)
    return packed


def pack_means(packed, to_right, means):
    length = packed.shape[0]
    start = LEAD + COLUMNS // FACTOR - C_SECOND if to_right else LEAD
    lane = lanes_of(length)
    for half in range(2):
        cells = means[half * length : (half + 1) * length]
        for at, first in ((half * HALF + COARSE_A, start), (half * HALF + COARSE_B, start + 3)):
            packed = jnp.where((lane >= at) & (lane < at + 3), turn(cells, at - first), packed)
    return packed


def column_meta(message):
    return (int_at(message, 0, SHIFT_R), int_at(message, 0, SHIFT_C)), scalar_at(message, 0, EXISTS)


def strip_second(base, from_left, from_right, rows, half, band):
    at = half * HALF + band * SLOT
    lane = lanes_like(base)
    cells = jnp.where(lane >= S_RIGHT, turn(from_right[rows, :], S_RIGHT - at), base)
    return jnp.where(lane >= S_LEFT, turn(from_left[rows, :], S_LEFT - at), cells)


def strip_first(base, from_left, from_right, rows, half, band):
    at = half * HALF + band * SLOT + REACH
    lane = lanes_like(base)
    cells = jnp.where(lane >= S_RIGHT, turn(from_right[rows, :], S_RIGHT - at), base)
    return jnp.where(lane >= S_LEFT, turn(from_left[rows, :], LANES - DEPTH - at), cells)


def strip_halo(base, beside, band, start, count):
    at = band * H_BAND + start
    lane = lanes_like(base)
    cells = jnp.where(lane >= S_RIGHT, turn(beside, S_RIGHT - at), base)
    return jnp.where(lane >= S_LEFT, turn(beside, LANES - count - at - SLOT), cells)


def strip_own(planes):
    return jnp.where(lanes_like(planes[0]) < S_MID, planes[0], turn(planes[1], -S_TURN))


def first_kernel(
    second_hbm, first_hbm, shifts_hbm, second_0, second_1, first_0, first_1, coarse, swap_0, swap_1, own_meta,
    shifts, sems, shift_sem,
):
    seconds, firsts = (second_0, second_1), (first_0, first_1)
    bands, height, _ = second_0.shape
    width = COLUMNS
    coarse_height = height // FACTOR
    lane = lanes_of()
    get_shifts = pltpu.make_async_copy(shifts_hbm, shifts, shift_sem)
    get_shifts.start()
    copies = []
    for image, (source, refs) in enumerate(((second_hbm, seconds), (first_hbm, firsts))):
        for band in range(bands):
            for tile, ref in enumerate(refs):
                copy = pltpu.make_async_copy(
                    source.at[band, :, pl.ds(tile * LANES, LANES)], ref.at[band], sems.at[image, band, tile]
                )
                copy.start()
                copies.append((image * bands + band, tile, ref, band, copy))
    cell = lax.broadcasted_iota(jnp.int32, (width, LANES), 0)
    place = lax.broadcasted_iota(jnp.int32, (width, LANES), 1)
    weights = jnp.where(place - LEAD == cell // FACTOR, 1.0 / (FACTOR * FACTOR), 0.0).astype(jnp.bfloat16)
    means = []
    packed = [None, None]
    for image, (count, offset) in enumerate(((REACH, 0), (DEPTH, REACH))):
        group = copies[image * 2 * bands : (image + 1) * 2 * bands]
        sums = {}
        for *_, copy in group:
            copy.wait()
        for plane, tile, ref, band, _ in group:
            parts = [ref[band, pl.ds(k, coarse_height, stride=FACTOR), :] for k in range(FACTOR)]
            while len(parts) > 1:
                parts = [x + y for x, y in zip(parts[::2], parts[1::2])]
            sums[plane, tile] = parts[0]
        tall = [jnp.concatenate([sums[image * bands + band, tile] for tile in range(2)], axis=1) for band in range(bands)]
        means.append(split_dot(jnp.concatenate(tall, axis=0), weights))
        packed = [
            pack_image(packed[side], bool(side), (seconds, firsts)[image], count, offset) for side in range(2)
        ]
    means = jnp.concatenate(means, axis=0)
    get_shifts.wait()
    shift_rows = shifts[0, 0, 0].astype(jnp.float32)
    shift_cols = shifts[0, 0, 1].astype(jnp.float32)
    place = lanes_of(height // 2) & (HALF - 1)
    packed = [
        jnp.where(place == SHIFT_R, shift_rows, jnp.where(place == SHIFT_C, shift_cols, jnp.where(place == EXISTS, 1.0, x)))
        for x in packed
    ]
    to_left, to_right = [pack_means(packed[side], bool(side), means) for side in range(2)]
    coarse[...] = means
    own_meta[...] = jnp.where(lane < HALF, shift_rows, shift_cols)
    even = is_even("col", swap_0)
    swap_0[...] = jnp.where(even, to_right, to_left)
    swap_1[...] = jnp.where(even, to_left, to_right)


def message_kernel(
    count, coarse, own_meta, got_1, got_0, up_part, down_part, _whole, swap_0, swap_1, from_left, from_right, wide
):
    other = without_ends(got_1, "col", count)
    even = is_even("col", got_0)
    from_right[...] = jnp.where(even, got_0[...], other)
    from_left[...] = jnp.where(even, other, got_0[...])
    planes_coarse, coarse_height, _ = wide.shape
    bands = planes_coarse // 2
    end = from_left.shape[0]
    coarse_width = COLUMNS // FACTOR
    lane = lanes_of()
    wides = []
    for plane in range(planes_coarse):
        half, block = divmod(plane, planes_coarse // 2)
        for step in range(coarse_height // SUB):
            own = slice(plane * coarse_height + step * SUB, plane * coarse_height + (step + 1) * SUB)
            rows = slice(block * coarse_height + step * SUB, block * coarse_height + (step + 1) * SUB)
            at = half * HALF
            left = from_left[rows, :]
            right = from_right[rows, :]
            start = LEAD - C_SECOND
            cells = turn(left, start - at - COARSE_A)
            cells = jnp.where(lane >= start + 3, turn(left, start + 3 - at - COARSE_B), cells)
            cells = jnp.where(lane >= LEAD, coarse[own, :], cells)
            start = LEAD + coarse_width
            cells = jnp.where(lane >= start, turn(right, start - at - COARSE_A), cells)
            cells = jnp.where(lane >= start + 3, turn(right, start + 3 - at - COARSE_B), cells)
            wides.append((plane, step, cells))
    for plane, step, cells in wides:
        wide[plane, step * SUB : (step + 1) * SUB, :] = cells
    row = lax.broadcasted_iota(jnp.int32, (SUB, LANES), 0)
    meta = jnp.where(lane < 16, own_meta[...], jnp.where(lane < 32, turn(own_meta[...], HALF), 1.0))
    for message, at in ((from_left, 48), (from_right, 80)):
        first_rows = message[0:SUB, :]
        rows = jnp.broadcast_to(first_rows[:, SHIFT_R : SHIFT_R + 1], (SUB, LANES))
        cols = jnp.broadcast_to(first_rows[:, SHIFT_C : SHIFT_C + 1], (SUB, LANES))
        meta = jnp.where(lane >= at, rows, meta)
        meta = jnp.where(lane >= at + 16, cols, meta)

    def beside(rows, half):
        left = from_left[rows, :]
        right = from_right[rows, :]
        cells = jnp.zeros((SUB, LANES), jnp.float32)
        for band in range(bands):
            at = half * HALF + band * SLOT
            cells = jnp.where(lane >= band * H_BAND, turn(right, band * H_BAND - at), cells)
            cells = jnp.where(lane >= band * H_BAND + SLOT, turn(left, band * H_BAND + SLOT - at), cells)
        return cells

    even = is_even("row", meta)
    parts = []
    for part, half, near, next_rows, row_of in (
        (up_part, 0, slice(0, 8), slice(8, 16), 0),
        (down_part, 1, slice(end - 8, end), slice(end - 16, end - 8), 7),
    ):
        eight = beside(near, half)
        one = beside(next_rows, half)
        one = jnp.broadcast_to(one[row_of : row_of + 1], (SUB, LANES))
        coarse_rows = []
        for band in range(bands):
            rows = slice(0, C_SECOND) if half == 0 else slice(coarse_height - C_SECOND, coarse_height)
            second = wide[band, rows, :]
            first = turn(wide[bands + band, rows, :], HALF)
            coarse_rows.append(jnp.where(lanes_like(second) < HALF, second, first))
        parts.append([
            (part[E8:H8, :], E8), (eight, H8), (part[E1:H1, :], E1), (jnp.where(row == 0, one, meta), H1),
            (part[F4:CS, :], F4), *[(x, CS + k * C_SECOND) for k, x in enumerate(coarse_rows)],
        ])
    for (up, at), (down, _) in zip(*parts):
        even = is_even("row", up)
        swap_0[at : at + up.shape[0], :] = jnp.where(even, down, up)
        swap_1[at : at + up.shape[0], :] = jnp.where(even, up, down)


def coarse_flow_of(second, first, mask):
    def along_rows(x):
        return pltpu.roll(x, x.shape[0] - 1, 0) - pltpu.roll(x, 1, 0)

    def along_cols(x):
        return pltpu.roll(x, LANES - 1, 1) - pltpu.roll(x, 1, 1)

    bands = BANDS
    size = second.shape[0] // bands
    grad_rows = 0.125 * along_rows(second)
    grad_cols = 0.125 * along_cols(second)
    offset = 0.25 * (second - first)
    data = jnp.clip(offset, -LIMIT, LIMIT)
    yield

    def pull(grads):
        terms = data * grads
        return sum(terms[k * size : (k + 1) * size] for k in range(bands))

    def tall(x):
        return jnp.concatenate([x] * bands, axis=0)

    flow = [-mask * pull(grad_rows), -mask * pull(grad_cols)]
    extrapolated = [2.0 * x for x in flow]
    dual_rows = [0.0, 0.0]
    dual_cols = [0.0, 0.0]
    yield
    for step in range(1, STEPS):
        changes = [(along_rows(x), along_cols(x)) for x in extrapolated]
        yield
        data = data + offset + grad_rows * tall(extrapolated[0]) + grad_cols * tall(extrapolated[1])
        data = jnp.clip(data, -LIMIT, LIMIT)
        yield
        for c in range(2):
            rows = dual_rows[c] + changes[c][0]
            cols = dual_cols[c] + changes[c][1]
            scale = jnp.minimum(mask, (8.0 * ALPHA) * lax.rsqrt(rows * rows + cols * cols))
            dual_rows[c] = rows * scale
            dual_cols[c] = cols * scale
        yield
        divergences = [along_rows(dual_rows[c]) + along_cols(dual_cols[c]) for c in range(2)]
        yield
        pulls = [pull(grad_rows), pull(grad_cols)]
        yield
        for c in range(2):
            following = flow[c] + mask * ((1.0 / 64.0) * divergences[c] - pulls[c])
            extrapolated[c] = 2.0 * following - flow[c]
            flow[c] = following
        yield
    return flow


def columns_of_planes(planes):
    whole = lax.broadcasted_iota(jnp.int32, (LANES, COLUMNS), 1)
    lane = lax.broadcasted_iota(jnp.int32, (LANES, LANES), 1)
    strip = jnp.where(lane < S_MID, lane, jnp.where(lane < S_LEFT, lane + (COLUMNS - S_RIGHT), lane - LANES))
    return jnp.concatenate([x for x, wanted in ((whole, "whole"), (strip, "strip")) if wanted in planes], axis=1)


def upsample(flow, planes, target):
    column = columns_of_planes(planes)
    source = lax.broadcasted_iota(jnp.int32, column.shape, 0)
    spread = jnp.where(source - LEAD == lax.shift_right_arithmetic(column, 3), float(FACTOR), 0.0).astype(jnp.bfloat16)
    rows = flow[0].shape[0]
    wide = split_dot(UNIT * jnp.concatenate(flow, axis=0), spread)
    for c in range(2):
        for tile in range(column.shape[1] // LANES):
            target[c, tile] = wide[c * rows : (c + 1) * rows, tile * LANES : (tile + 1) * LANES]


def repeat_rows(spread, initial, cells):
    for c in range(2):
        for tile in range(initial.shape[1]):
            rows = [jnp.broadcast_to(spread[c, tile, cell : cell + 1, :], (SUB, LANES)) for cell in cells]
            initial[c, tile, GUARD : GUARD + SUB * len(cells), :] = jnp.concatenate(rows, axis=0)


def shift_whole(here, shift):
    turned = [turn_back(x, shift) for x in here]
    lane = lanes_like(here[0])
    return [
        jnp.where(lane + shift >= LANES, turned[1], turned[0]),
        jnp.where(lane + shift < 0, turned[0], turned[1]),
    ]


def edge_lanes(rows):
    lane = lanes_of(rows)
    return lane == LANES - 1, lane == 0


def columns_whole(fields, edges):
    last, first = edges
    ahead = [pltpu.roll(x, LANES - 1, 1) for x in fields]
    behind = [pltpu.roll(x, 1, 1) for x in fields]
    return [
        jnp.where(last, ahead[1], ahead[0]) - behind[0],
        ahead[1] - jnp.where(first, behind[0], behind[1]),
    ]


def rows_within(tall):
    size = tall.shape[0]
    return (pltpu.roll(tall, size - 1, 0) - pltpu.roll(tall, 1, 0))[SUB : size - SUB]


def columns_strip(field):
    return pltpu.roll(field, LANES - 1, 1) - pltpu.roll(field, 1, 1)


def strip_windows(window, centre, right, left):
    own = turn_back(window(centre[0]), centre[1])
    beyond_left = turn_back(window(left[0]), left[1])
    beyond_right = turn_back(window(right[0]), right[1])
    lane = lanes_like(own)
    beyond = jnp.where((lane >= S_LEFT) | (lane < S_MID), beyond_left, beyond_right)
    is_beyond = lane >= S_RIGHT
    return jnp.where(is_beyond, beyond, own), jnp.where(is_beyond, columns_strip(beyond), columns_strip(own))


def fine_steps(
    rows_total, chunk, columns, initial, extrap, dual_rows, dual_cols, change, dual_data,
    offsets, grads_rows, grads_cols, data_row, masks_of, result, done=lambda k: None, loop=False,
):
    assert STEPS == 3
    planes = len(offsets)
    bands = offsets[0].shape[0]
    chunks = rows_total // chunk

    def multiple(row):
        return row if isinstance(row, int) else pl.multiple_of(row, SUB)

    def places(k):
        return pl.ds(multiple(GUARD + k * chunk), chunk), pl.ds(multiple(k * chunk), chunk)

    def row_change(ref, c, tile, k):
        row = GUARD + k * chunk
        return ref[c, tile, pl.ds(row + 1, chunk), :] - ref[c, tile, pl.ds(row - 1, chunk), :]

    def clip(x):
        return jnp.clip(x, -UNIT * LIMIT, UNIT * LIMIT)

    tiles = range(planes)

    for step in range(STEPS):
        source = initial if step == 0 else extrap
        final = step == STEPS - 1

        def dual(item, source=source, step=step):
            k, c = item
            at, own = places(k)
            masks = masks_of(own)
            along = columns([source[c, tile, at, :] for tile in tiles])
            values = []
            for tile in tiles:
                rows = row_change(source, c, tile, k)
                cols = along[tile]
                if step > 0:
                    rows = rows + dual_rows[c, tile, at, :]
                    cols = cols + dual_cols[c, tile, own, :]
                scale = jnp.minimum(masks[tile], lax.rsqrt(rows * rows + cols * cols))
                values.append((rows * scale, cols * scale))
            return values

        def store_dual(item, values):
            k, c = item
            for tile, (rows, cols) in enumerate(values):
                dual_rows[c, tile, places(k)[0], :] = rows
                dual_cols[c, tile, places(k)[1], :] = cols

        if loop:

            def dual_pass(k, carry, dual=dual, store_dual=store_dual):
                staggered([(k, c) for c in range(2)], dual, store_dual, 1)
                return carry

            lax.fori_loop(0, chunks, dual_pass, 0)
        else:
            staggered([(k, c) for k in range(chunks) for c in range(2)], dual, store_dual, 1)
        along_of = {}

        def primal(item, step=step, final=final, along_of=along_of):
            k, tile = item
            at, own = places(k)
            data = pl.ds(multiple(data_row(k)), chunk)
            key = k if isinstance(k, int) else "pass"
            if key not in along_of:
                along_of[key] = [columns([dual_cols[c, t, own, :] for t in tiles]) for c in range(2)]
            mask = masks_of(own)[tile]
            start = [initial[c, tile, at, :] for c in range(2)]
            if step > 0:
                moved = [extrap[c, tile, at, :] - start[c] for c in range(2)]
            if step == 1:
                changes = [0.5 * x for x in moved]
            if step == 2:
                changes = [change[c, tile, own, :] for c in range(2)]
            pulls = [None, None]
            duals = []
            for band in range(bands):
                gradient = (grads_rows[tile][band, data, :], grads_cols[tile][band, data, :])
                value = offsets[tile][band, data, :]
                if step > 0:
                    earlier = clip(value) if step == 1 else dual_data[band, tile, own, :]
                    value = (value + earlier) + (gradient[0] * moved[0] + gradient[1] * moved[1])
                value = clip(value)
                duals.append(value)
                for c in range(2):
                    term = value * gradient[c]
                    pulls[c] = term if pulls[c] is None else pulls[c] + term
            flows, nexts = [], []
            for c in range(2):
                divergence = row_change(dual_rows, c, tile, k) + along_of[key][c][tile]
                moving = (mask * (1.0 / 64.0)) * divergence - pulls[c]
                total = moving if step == 0 else changes[c] + moving
                flows.append((start[c] + total) * (1.0 / UNIT) if final else total)
                nexts.append(None if final else start[c] + (total + moving))
            return flows, nexts, duals

        def store_primal(item, results, step=step, final=final):
            k, tile = item
            flows, nexts, duals = results
            at, own = places(k)
            for c in range(2):
                if final:
                    result[c, tile, own, :] = flows[c]
                else:
                    if step > 0:
                        change[c, tile, own, :] = flows[c]
                    extrap[c, tile, at, :] = nexts[c]
            if final:
                if tile == planes - 1:
                    done(k)
            elif step > 0:
                for band in range(bands):
                    dual_data[band, tile, own, :] = duals[band]

        if loop:

            def primal_pass(k, carry, primal=primal, store_primal=store_primal, along_of=along_of):
                along_of.clear()
                staggered([(k, tile) for tile in tiles], primal, store_primal, 1)
                along_of.clear()
                return carry

            lax.fori_loop(0, chunks, primal_pass, 0)
        else:
            staggered([(k, tile) for k in range(chunks) for tile in tiles], primal, store_primal, 1)


def clear_guards(*refs):
    for ref in refs:
        rows = ref.shape[2]
        zero = jnp.zeros((GUARD, LANES), jnp.float32)
        for c in range(2):
            for tile in range(ref.shape[1]):
                ref[c, tile, 0:GUARD, :] = zero
                ref[c, tile, rows - GUARD : rows, :] = zero


def fine_scratch(bands, planes, rows):
    guarded = pltpu.VMEM((2, planes, rows + 2 * GUARD, LANES), jnp.float32)
    plain = pltpu.VMEM((2, planes, rows, LANES), jnp.float32)
    return [guarded, guarded, guarded, plain, plain, pltpu.VMEM((bands, planes, rows, LANES), jnp.float32)]


def pieces(bands, height, rows):
    assert (height - 2 * SUB) % rows == 0
    return [(band, row) for row in range(SUB, height - SUB, rows) for band in range(bands)]


def whole_terms_kernel(
    second_0, second_1, first_0, first_1, coarse, own_meta,
    offset, grad_rows, grad_cols, initial, strip_e, strip_f, up, down, moved, spread,
):
    seconds, firsts = (second_0, second_1), (first_0, first_1)
    bands, height, _ = second_0.shape
    block = 120
    coarse_height = coarse.shape[0] // (2 * bands)
    shift_rows, shift_cols = scalar_at(own_meta, 0, 0), scalar_at(own_meta, 0, HALF)
    centre = (shift_rows.astype(jnp.int32), shift_cols.astype(jnp.int32))
    def windows(band, row, rows):
        here = [ref[band, pl.ds(row + centre[0], rows), :].reshape(-1, LANES) for ref in seconds]
        return shift_whole(here, centre[1])

    woven = Woven(coarse_flow_of(coarse[0 : bands * coarse_height, :], coarse[bands * coarse_height :, :], 1.0))

    ends = [(row, windows(slice(None), row, SUB)) for row in (SUB // 2, height - SUB - SUB // 2)]
    for row, values in ends:
        for tile in range(2):
            moved[tile, :, row : row + SUB, :] = values[tile].reshape(bands, SUB, LANES)

    edges = edge_lanes(block)

    def values_of(item):
        band, row = item
        values = windows(band, row, block)
        along = columns_whole(values, edges)
        own = [ref[band, row : row + block, :] for ref in firsts]
        return values, [(0.25 * UNIT) * (x - y) for x, y in zip(values, own)], [0.125 * x for x in along]

    def store_values(item, results):
        band, row = item
        values, offsets, gradients = results
        data = slice(row + HALO, row + HALO + block)
        for tile in range(2):
            moved[tile, band, row : row + block, :] = values[tile]
            offset[tile, band, data, :] = offsets[tile]
            grad_cols[tile, band, data, :] = gradients[tile]

    staggered(pieces(bands, height, block), values_of, store_values, 1, woven)

    def strips_of(item):
        band, row = item
        rows = slice(row, row + LANES)
        return strip_own([ref[band, rows, :] for ref in seconds]), strip_own([ref[band, rows, :] for ref in firsts])

    def store_strips(item, results):
        band, row = item
        strip_e[band, row : row + LANES, :], strip_f[band, row : row + LANES, :] = results

    staggered([(band, row) for band in range(bands) for row in range(0, height, LANES)], strips_of, store_strips, 1, woven)

    def gradient_of(item):
        band, row = item
        return [0.125 * rows_within(moved[tile, band, row - SUB : row + 120 + SUB, :]) for tile in range(2)]

    def store_gradient(item, results):
        band, row = item
        for tile in range(2):
            grad_rows[tile, band, row + HALO : row + HALO + 120, :] = results[tile]

    staggered(pieces(bands, height, 120), gradient_of, store_gradient, 1, woven)

    parts = []
    for band in range(bands):
        for second, first in zip(seconds, firsts):
            parts.append((
                second[band, 0:16, :], first[band, 0:8, :],
                second[band, height - 16 : height, :], first[band, height - 8 : height, :],
            ))
    for k, (second_top, first_top, second_end, first_end) in enumerate(parts):
        up[E8 + 8 * k : E8 + 8 * k + 8, :] = second_top[0:8]
        up[E1 + k : E1 + k + 1, :] = second_top[8:9]
        up[F4 + 4 * k : F4 + 4 * k + 4, :] = first_top[0:4]
        down[E8 + 8 * k : E8 + 8 * k + 8, :] = second_end[8:16]
        down[E1 + k : E1 + k + 1, :] = second_end[7:8]
        down[F4 + 4 * k : F4 + 4 * k + 4, :] = first_end[4:8]
    for target in (up, down):
        for start, end in ((H8, E1), (H1, F4), (CS, ROW_MESSAGE)):
            target[start:end, :] = jnp.zeros((end - start, LANES), jnp.float32)

    upsample(woven.finish(), ("whole",), spread)
    clear_guards(initial)
    rows_total = initial.shape[2] - 2 * GUARD
    repeat_rows(spread, initial, [BEGIN // FACTOR + k for k in range(rows_total // SUB)])


def whole_steps_kernel(
    initial, offset, grad_rows, grad_cols, result, extrap, dual_rows, dual_cols, change, dual_data
):
    rows_total = result.shape[2]
    clear_guards(extrap, dual_rows)
    chunk = 88
    edges = edge_lanes(chunk)
    fine_steps(
        rows_total, chunk, lambda fields: columns_whole(fields, edges),
        initial, extrap, dual_rows, dual_cols, change, dual_data,
        *[[ref.at[tile] for tile in range(2)] for ref in (offset, grad_rows, grad_cols)],
        lambda k: HALO + BEGIN + k * chunk, lambda own: (1.0, 1.0), result, loop=True,
    )


def strip_kernel(
    strip_e, strip_f, from_left, from_right, wide, own_meta, whole,
    middle, strip_out, first_ends, offset, grad_rows, grad_cols,
    moved, result, spread, initial, extrap, dual_rows, dual_cols, change, dual_data,
):
    bands, height, _ = strip_e.shape
    block = 120
    coarse_height = height // FACTOR
    coarse_width = COLUMNS // FACTOR
    rows_total = height - 2 * BEGIN
    lane = lanes_of()
    centre = (int_at(own_meta, 0, 0), int_at(own_meta, 0, HALF))
    right, has_right = column_meta(from_right)
    left, has_left = column_meta(from_left)
    exists = jnp.where(lane < S_RIGHT, 1.0, jnp.where(lane < S_LEFT, has_right, has_left))

    def tall_factor(rows):
        return 0.125 * jnp.concatenate([exists] * (rows // SUB), axis=0)

    mask = jnp.where(lane < LEAD, has_left, jnp.where(lane < LEAD + coarse_width, 1.0, has_right))
    mask = jnp.concatenate([mask] * (coarse_height // SUB), axis=0)
    cells = [wide[k * bands : (k + 1) * bands].reshape(bands * coarse_height, LANES) for k in range(2)]
    woven = Woven(coarse_flow_of(*cells, mask))

    def halves(row, rows):
        half = row // (height // 2)
        start = row - half * (height // 2)
        return half, slice(start, start + rows)

    def second_of(item):
        band, row = item
        half, message = halves(row, LANES)
        return strip_second(strip_e[band, row : row + LANES, :], from_left, from_right, message, half, band)

    def store_second(item, value):
        band, row = item
        strip_out[band, row : row + LANES, :] = value

    staggered([(band, row) for row in range(0, height, LANES) for band in range(bands)], second_of, store_second, 1, woven)

    def first_of(band, row, rows):
        half, message = halves(row, rows)
        return strip_first(strip_f[band, row : row + rows, :], from_left, from_right, message, half, band)

    firsts = [(end, band, first_of(band, (0, height - SUB)[end], SUB)) for end in range(2) for band in range(bands)]
    for end, band, value in firsts:
        first_ends[end, band] = value

    def windows(band, row, rows):
        return strip_windows(
            lambda shift: strip_out[band, pl.ds(row + shift, rows), :].reshape(-1, LANES), centre, right, left
        )

    ends = [(row, windows(slice(None), row, SUB)[0]) for row in (SUB // 2, height - SUB - SUB // 2)]
    for row, value in ends:
        moved[:, row : row + SUB, :] = value.reshape(bands, SUB, LANES)

    factor = tall_factor(block)

    def values_of(item):
        band, row = item
        value, along = windows(band, row, block)
        return value, (0.25 * UNIT) * (value - first_of(band, row, block)), factor * along

    def store_values(item, results):
        band, row = item
        data = slice(row + HALO, row + HALO + block)
        moved[band, row : row + block, :], offset[band, data, :], grad_cols[band, data, :] = results

    staggered(pieces(bands, height, block), values_of, store_values, 1, woven)

    def gradient_of(item):
        band, row = item
        return factor * rows_within(moved[band, row - SUB : row + block + SUB, :])

    def store_gradient(item, value):
        band, row = item
        grad_rows[band, row + HALO : row + HALO + block, :] = value

    staggered(pieces(bands, height, block), gradient_of, store_gradient, 1, woven)

    upsample(woven.finish(), ("strip",), spread)
    clear_guards(initial, extrap, dual_rows)
    repeat_rows(spread, initial, [BEGIN // FACTOR + k for k in range(rows_total // SUB)])

    chunk = 88
    masks = jnp.concatenate([exists] * (chunk // SUB), axis=0)
    fine_steps(
        rows_total, chunk, lambda fields: [columns_strip(fields[0])],
        initial, extrap, dual_rows, dual_cols, change, dual_data, [offset], [grad_rows], [grad_cols],
        lambda k: HALO + BEGIN + k * chunk, lambda own: (masks,), result, loop=True,
    )
    join(whole, result.at[:, 0], middle, slice(0, rows_total))


def join(whole, strip, target, rows):
    lane = lanes_of(rows.stop - rows.start)
    values = []
    for c in range(2):
        edge = strip[c, rows, :]
        start = jnp.where(lane < EDGE, edge, whole[c, 0, rows, :])
        values.append((start, jnp.where(lane >= LANES - EDGE, turn(edge, S_TURN), whole[c, 1, rows, :])))
    for c in range(2):
        target[c, rows, 0:LANES], target[c, rows, LANES:COLUMNS] = values[c]


def outer_kernel(
    count, second_0, second_1, first_0, first_1, strip_e, first_ends, from_left, from_right, wide, got_1, got_0, middle, own_meta,
    _wo, _wr, _wc, _so, _sr, _sc,
    flow_out, coarse_out, whole_offset, whole_rows, whole_cols, strip_offset, strip_rows, strip_cols,
    from_up, from_down, extended, tall, spread, masks, result, joined, coarse_result, sems,
    initial, extrap, dual_rows, dual_cols, change, dual_data,
):
    bands, height, _ = second_0.shape
    coarse_height = height // FACTOR
    coarse_width = COLUMNS // FACTOR
    rows_total = 2 * EACH
    lane = lanes_of()

    put_middle = pltpu.make_async_copy(
        middle.at[:, pl.ds(MARGIN - BEGIN, height - 2 * MARGIN), :],
        flow_out.at[:, pl.ds(MARGIN, height - 2 * MARGIN), :],
        sems.at[0],
    )
    put_middle.start()

    other = without_ends(got_1, "row", count)
    even = is_even("row", got_0)
    from_down[...] = jnp.where(even, got_0[...], other)
    from_up[...] = jnp.where(even, other, got_0[...])

    own = (int_at(own_meta, 0, 0), int_at(own_meta, 0, HALF))
    own_right, has_right = column_meta(from_right)
    own_left, has_left = column_meta(from_left)
    has_up = scalar_at(from_up, META, 32)
    has_down = scalar_at(from_down, META, 32)
    exists = jnp.where(lane < S_RIGHT, 1.0, jnp.where(lane < S_LEFT, has_right, has_left))

    def trio(message):
        return (
            (int_at(message, META, 0), int_at(message, META, 16)),
            (int_at(message, META, 80), int_at(message, META, 96)),
            (int_at(message, META, 48), int_at(message, META, 64)),
        )

    above = trio(from_up)
    below = trio(from_down)

    zero = jnp.zeros((SUB, LANES), jnp.float32)
    tall_rows = coarse_height + 2 * LEAD
    parts = []
    fill = jnp.zeros((LEAD - C_SECOND, LANES), jnp.float32)
    for plane in range(2 * bands):
        at = CS + C_SECOND * (plane % bands)
        ends = [turn(message[at : at + C_SECOND, :], HALF * (plane // bands)) for message in (from_up, from_down)]
        parts.append([fill, ends[0], wide[plane], ends[1], fill])
    for plane, values in enumerate(parts):
        tall[plane] = jnp.concatenate(values, axis=0)
    across = jnp.where(lane < LEAD, has_left, jnp.where(lane < LEAD + coarse_width, 1.0, has_right))
    mask = jnp.concatenate([across * has_up] + [across] * (coarse_height // SUB) + [across * has_down], axis=0)
    for end in range(2):
        message = (from_up, from_down)[end]
        beside = message[H8 : H8 + 8, :]
        beside_one = jnp.broadcast_to(message[H1 : H1 + 1, :], (SUB, LANES))
        parts = []
        for band in range(bands):
            eights = [message[E8 + 8 * k : E8 + 8 * k + 8, :] for k in (2 * band, 2 * band + 1)]
            ones = [jnp.broadcast_to(message[E1 + k : E1 + k + 1, :], (SUB, LANES)) for k in (2 * band, 2 * band + 1)]
            eights.append(strip_halo(strip_own(eights), beside, band, 0, REACH))
            ones.append(strip_halo(strip_own(ones), beside_one, band, 0, REACH))
            for tile, (eight, one) in enumerate(zip(eights, ones)):
                source = (second_0, second_1, strip_e)[tile]
                if end == 0:
                    parts.append((tile, band, [one, eight, source[band, 0:24, :]]))
                else:
                    parts.append((tile, band, [source[band, height - 24 : height, :], eight, one]))
        for tile, band, values in parts:
            extended[end, tile, band] = jnp.concatenate(values, axis=0)
    cells = [tall[k * bands : (k + 1) * bands].reshape(bands * tall_rows, LANES) for k in range(2)]
    woven = Woven(coarse_flow_of(*cells, mask))
    edges = edge_lanes(bands * SUB)
    rows_data = whole_offset.shape[2]
    exists_tall = jnp.concatenate([exists] * bands, axis=0)

    def rows_of(halo, end):
        if halo:
            return slice(0, SUB) if end == 0 else slice(rows_data - SUB, rows_data)
        return slice(HALO, HALO + SUB) if end == 0 else slice(rows_data - HALO - SUB, rows_data - HALO)

    def values_of(item):
        halo, end = item
        message = (from_up, from_down)[end]
        base = (SUB, 3 * SUB)[end] if halo else 2 * SUB
        shifts = (above, below)[end] if halo else (own, own_right, own_left)
        factor = 0.125 * (has_up, has_down)[end] if halo else 0.125

        def here(tile, shift):
            return extended[end, tile, :, pl.ds(base + shift, SUB), :].reshape(-1, LANES)

        def down_up(tile, shift):
            return here(tile, shift + 1) - here(tile, shift - 1)

        own_rows = slice(0, SUB) if end == 0 else slice(height - SUB, height)
        if halo:
            firsts = [[], [], []]
            for band in range(bands):
                eights = []
                for k in (2 * band, 2 * band + 1):
                    four = message[F4 + 4 * k : F4 + 4 * k + 4, :]
                    eights.append(jnp.concatenate([four, four], axis=0))
                eights.append(strip_halo(strip_own(eights), message[H8 : H8 + 8, :], band, REACH, DEPTH))
                for tile in range(3):
                    firsts[tile].append(eights[tile])
            firsts = [jnp.concatenate(x, axis=0) for x in firsts]
        else:
            firsts = [x.reshape(-1, LANES) for x in (first_0[:, own_rows, :], first_1[:, own_rows, :], first_ends[end])]
        centre = shifts[0]
        values = shift_whole([here(tile, centre[0]) for tile in range(2)], centre[1])
        changes = shift_whole([down_up(tile, centre[0]) for tile in range(2)], centre[1])
        along = columns_whole(values, edges)
        value, across_cols = strip_windows(lambda shift: here(2, shift), *shifts)
        change_rows, _ = strip_windows(lambda shift: down_up(2, shift), *shifts)
        return (
            [(0.25 * UNIT) * (x - y) for x, y in zip([*values, value], firsts)],
            [*[factor * x for x in changes], (factor * exists_tall) * change_rows],
            [*[factor * x for x in along], (factor * exists_tall) * across_cols],
        )

    def store_values(item, results):
        rows = rows_of(*item)
        for values, whole, strip in zip(
            results, (whole_offset, whole_rows, whole_cols), (strip_offset, strip_rows, strip_cols)
        ):
            values = [x.reshape(bands, SUB, LANES) for x in values]
            for tile in range(2):
                whole[tile, :, rows, :] = values[tile]
            strip[:, rows, :] = values[2]

    staggered([(halo, end) for halo in (True, False) for end in range(2)], values_of, store_values, 1, woven)

    flow = woven.finish()
    for c in range(2):
        coarse_result[c] = turn(flow[c][LEAD : LEAD + coarse_height], -LEAD)[:, :coarse_width]
    put_coarse = pltpu.make_async_copy(coarse_result, coarse_out, sems.at[1])
    put_coarse.start()
    upsample(flow, ("whole", "strip"), spread)
    clear_guards(initial, extrap, dual_rows)
    each = EACH // SUB
    repeat_rows(
        spread, initial,
        [LEAD - 1 + k for k in range(each)] + [tall_rows - LEAD + 1 - each + k for k in range(each)],
    )

    for i, value in enumerate((jnp.ones((SUB, LANES), jnp.float32), exists)):
        masks[i] = jnp.concatenate([value * has_up] + [value] * (rows_total // SUB - 2) + [value * has_down], axis=0)

    def masks_of(rows):
        whole = masks[0, rows, :]
        return (whole, whole, masks[1, rows, :])

    chunk = EACH
    edges = edge_lanes(chunk)
    puts = [
        pltpu.make_async_copy(
            joined.at[:, pl.ds(k * EACH + SUB, MARGIN), :],
            flow_out.at[:, pl.ds(k * (height - MARGIN), MARGIN), :],
            sems.at[2 + k],
        )
        for k in range(2)
    ]

    def finish(k):
        join(result, result.at[:, 2], joined, slice(k * EACH + SUB, k * EACH + SUB + MARGIN))
        puts[k].start()

    def data_row(k):
        return k * (rows_data - EACH)

    fine_steps(
        rows_total, chunk, lambda fields: columns_whole(fields[:2], edges) + [columns_strip(fields[2])],
        initial, extrap, dual_rows, dual_cols, change, dual_data,
        [whole_offset.at[0], whole_offset.at[1], strip_offset],
        [whole_rows.at[0], whole_rows.at[1], strip_rows],
        [whole_cols.at[0], whole_cols.at[1], strip_cols],
        data_row, masks_of, result, finish,
    )
    put_middle.wait()
    put_coarse.wait()
    for put in puts:
        put.wait()


def swap_with(message, axis, start):
    names = ("row", "col")
    sizes = [lax.axis_size(name) for name in names]
    along = names.index(axis)
    count, others = sizes[along], sizes[1 - along]

    def number(place, other):
        row, col = (place, other) if along == 0 else (other, place)
        return row * sizes[1] + col

    pairs = [(number(i, k), number(i + 1, k)) for i in range(start, count - 1, 2) for k in range(others)]
    if start:
        pairs += [(number(i, k), number(i, k + 1)) for i in (0, count - 1) for k in range(0, others, 2)]
    return lax.ppermute(message, names, pairs + [(j, i) for i, j in pairs])


def local(frame_first, frame_second, shifts):
    bands, height, width = frame_first.shape
    assert bands == 4 and width == COLUMNS and height % LANES == 0
    assert lax.axis_size("row") % 2 == 0 and lax.axis_size("col") % 2 == 0
    coarse_height = height // FACTOR
    coarse_width = width // FACTOR
    vmem = pl.BlockSpec(memory_space=pltpu.VMEM)
    hbm = pl.BlockSpec(memory_space=pltpu.HBM)
    tall_rows = coarse_height + 2 * LEAD
    inner_rows = height - 2 * BEGIN

    def shape(*sizes):
        return jax.ShapeDtypeStruct(sizes, jnp.float32)

    def scratch(*sizes):
        return pltpu.VMEM(sizes, jnp.float32)

    def call(kernel, name, arguments, outs, scratches=(), flops=1_000_000, **more):
        more = {"in_specs": [vmem] * len(arguments), "out_specs": (vmem,) * len(outs), **more}
        return pl.pallas_call(
            kernel,
            out_shape=tuple(outs),
            scratch_shapes=list(scratches),
            compiler_params=pltpu.CompilerParams(vmem_limit_bytes=24 * 1024 * 1024),
            cost_estimate=pl.CostEstimate(flops=flops, bytes_accessed=1_000_000, transcendentals=0),
            name=name,
            **more,
        )(*arguments)

    plane = shape(bands, height, LANES)
    column_message = shape(height // 2, LANES)
    row_message = shape(ROW_MESSAGE, LANES)
    whole_data = shape(2, bands, height + 2 * HALO, LANES)
    strip_data = shape(bands, height + 2 * HALO, LANES)

    *frames, coarse, swap_0, swap_1, own_meta = call(
        first_kernel,
        "means_and_message",
        [pltpu.with_memory_space_constraint(x, pltpu.HBM) for x in (frame_second, frame_first, shifts)],
        [*[plane] * 4, shape(2 * bands * coarse_height, LANES), column_message, column_message, shape(SUB, LANES)],
        [
            pltpu.SMEM((1, 1, 2), jnp.int32),
            pltpu.SemaphoreType.DMA((2, bands, 2)),
            pltpu.SemaphoreType.DMA,
        ],
        in_specs=[hbm] * 3,
    )
    got_1 = swap_with(swap_1, "col", 1)
    got_0 = swap_with(swap_0, "col", 0)

    *whole_terms, initial, strip_e, strip_f, up_part, down_part = call(
        whole_terms_kernel,
        "whole_terms",
        [*frames, coarse, own_meta],
        [
            *[whole_data] * 3, shape(2, 2, inner_rows + 2 * GUARD, LANES),
            plane, plane, row_message, row_message,
        ],
        [scratch(2, bands, height, LANES), scratch(2, 2, coarse_height, LANES)],
        flops=8_000_000,
    )
    (whole,) = call(
        whole_steps_kernel,
        "whole_steps",
        [initial, *whole_terms],
        [shape(2, 2, inner_rows, LANES)],
        fine_scratch(bands, 2, inner_rows)[1:],
        flops=20_000_000,
    )

    swap_0, swap_1, from_left, from_right, wide = call(
        functools.partial(message_kernel, lax.axis_size("col")),
        "row_messages",
        [coarse, own_meta, got_1, got_0, up_part, down_part, whole],
        [row_message, row_message, column_message, column_message, shape(2 * bands, coarse_height, LANES)],
    )
    got_1 = swap_with(swap_1, "row", 1)
    got_0 = swap_with(swap_0, "row", 0)

    middle, strip_e, first_ends, *strip_terms = call(
        strip_kernel,
        "strip",
        [strip_e, strip_f, from_left, from_right, wide, own_meta, whole],
        [shape(2, inner_rows, width), plane, shape(2, bands, SUB, LANES), *[strip_data] * 3],
        [
            scratch(bands, height, LANES),
            scratch(2, 1, inner_rows, LANES),
            scratch(2, 1, coarse_height, LANES),
            *fine_scratch(bands, 1, inner_rows),
        ],
        flops=16_000_000,
    )

    flow, coarse_flow, *_ = call(
        functools.partial(outer_kernel, lax.axis_size("row")),
        "outer_rows",
        [
            *frames, strip_e, first_ends, from_left, from_right, wide, got_1, got_0, middle, own_meta,
            *whole_terms, *strip_terms,
        ],
        [shape(2, height, width), shape(2, coarse_height, coarse_width), *[whole_data] * 3, *[strip_data] * 3],
        [
            scratch(ROW_MESSAGE, LANES),
            scratch(ROW_MESSAGE, LANES),
            scratch(2, 3, bands, 40, LANES),
            scratch(2 * bands, tall_rows, LANES),
            scratch(2, 3, tall_rows, LANES),
            scratch(2, 2 * EACH, LANES),
            scratch(2, 3, 2 * EACH, LANES),
            scratch(2, 2 * EACH, width),
            scratch(2, coarse_height, coarse_width),
            pltpu.SemaphoreType.DMA((4,)),
            *fine_scratch(bands, 3, 2 * EACH),
        ],
        out_specs=(hbm, hbm) + (vmem,) * 6,
        input_output_aliases={13 + k: 2 + k for k in range(6)},
    )
    return (flow, coarse_flow)


def solution(mesh):
    return jax.shard_map(
        local,
        mesh=mesh,
        in_specs=(P(None, "row", "col"), P(None, "row", "col"), P("row", "col", None)),
        out_specs=(P(None, "row", "col"), P(None, "row", "col")),
        check_vma=False,
    )
```

```python
import functools

import jax
import jax.numpy as jnp
from jax import lax
from jax.experimental import pallas as pl
from jax.experimental.pallas import tpu as pltpu
from jax.sharding import PartitionSpec as P

FACTOR = 8
MAXD = 4
BANDS = 4
STEPS = 3
LANES = 128
COLUMNS = 2 * LANES
HALF = 64
SUB = 8
DEPTH = 4
REACH = DEPTH + MAXD + 1
SLOT = 16
C_SECOND = 6
C_FIRST = 5
LEAD = 8
MARGIN = 48
EDGE = 46
GUARD = 8
HALO = 8
BEGIN = 40
EACH = MARGIN + 16
LIMIT = 0.3
ALPHA = 0.3
UNIT = 0.125 / ALPHA

S_MID = 55
S_RIGHT = 110
S_LEFT = LANES - REACH
S_TURN = COLUMNS - S_RIGHT - LANES

E8 = 0
H8 = 64
E1 = 72
H1 = 80
META = 81
F4 = 88
CS = 120
ROW_MESSAGE = 144
H_BAND = 32

COARSE_A = REACH + DEPTH
COARSE_B = SLOT + REACH + DEPTH
SHIFT_R = 2 * SLOT + REACH + DEPTH
SHIFT_C = SHIFT_R + 1
EXISTS = SHIFT_R + 2


def lanes_of(rows=SUB):
    return lax.broadcasted_iota(jnp.int32, (rows, LANES), 1)


def lanes_like(x):
    return lax.broadcasted_iota(jnp.int32, x.shape, 1)


def turn(x, amount):
    amount = amount % LANES
    return x if amount == 0 else pltpu.roll(x, amount, 1)


def turn_back(x, shift):
    return pltpu.roll(x, lax.rem(LANES - shift, LANES), 1)


def split_dot(x, exact):
    high = x.astype(jnp.bfloat16)
    rest = x - high.astype(jnp.float32)
    middle = rest.astype(jnp.bfloat16)
    low = (rest - middle.astype(jnp.float32)).astype(jnp.bfloat16)
    parts = [jnp.dot(part, exact, preferred_element_type=jnp.float32) for part in (low, middle, high)]
    return parts[0] + parts[1] + parts[2]


def scalar_at(ref, row, lane):
    return ref[row : row + 1, lane : lane + 1][0, 0]


def int_at(ref, row, lane):
    return scalar_at(ref, row, lane).astype(jnp.int32)


def is_even(axis, like):
    return jnp.broadcast_to(lax.axis_index(axis) % 2, like.shape) == 0


def without_ends(message, axis, count):
    place = jnp.broadcast_to(lax.axis_index(axis), message.shape)
    return jnp.where((place > 0) & (place < count - 1), message[...], 0.0)


def staggered(items, compute, store, depth, woven=None):
    pending = []
    for item in items:
        pending.append((item, compute(item)))
        if woven is not None:
            woven.advance()
        if len(pending) > depth:
            store(*pending.pop(0))
    for entry in pending:
        store(*entry)


class Woven:
    def __init__(self, stages):
        self.stages = stages
        self.result = None

    def advance(self):
        try:
            next(self.stages)
            return True
        except StopIteration as end:
            self.result = end.value if self.result is None else self.result
            return False

    def finish(self):
        while self.advance():
            pass
        return self.result


def pack_image(packed, to_right, planes, count, offset):
    bands, height, _ = planes[0].shape
    plane = planes[int(to_right)]
    start = LANES - count if to_right else 0
    length = height // 2
    lane = lanes_of(length)
    for half in range(2):
        for band in range(bands):
            at = half * HALF + band * SLOT + offset
            cells = turn(plane[band, half * length : (half + 1) * length, :], at - start)
            packed = cells if packed is None else jnp.where((lane >= at) & (lane < at + count), cells, packed)
    return packed


def pack_means(packed, to_right, means):
    length = packed.shape[0]
    start = LEAD + COLUMNS // FACTOR - C_SECOND if to_right else LEAD
    lane = lanes_of(length)
    for half in range(2):
        cells = means[half * length : (half + 1) * length]
        for at, first in ((half * HALF + COARSE_A, start), (half * HALF + COARSE_B, start + 3)):
            packed = jnp.where((lane >= at) & (lane < at + 3), turn(cells, at - first), packed)
    return packed


def column_meta(message):
    return (int_at(message, 0, SHIFT_R), int_at(message, 0, SHIFT_C)), scalar_at(message, 0, EXISTS)


def strip_second(base, from_left, from_right, rows, half, band):
    at = half * HALF + band * SLOT
    lane = lanes_like(base)
    cells = jnp.where(lane >= S_RIGHT, turn(from_right[rows, :], S_RIGHT - at), base)
    return jnp.where(lane >= S_LEFT, turn(from_left[rows, :], S_LEFT - at), cells)


def strip_first(base, from_left, from_right, rows, half, band):
    at = half * HALF + band * SLOT + REACH
    lane = lanes_like(base)
    cells = jnp.where(lane >= S_RIGHT, turn(from_right[rows, :], S_RIGHT - at), base)
    return jnp.where(lane >= S_LEFT, turn(from_left[rows, :], LANES - DEPTH - at), cells)


def strip_halo(base, beside, band, start, count):
    at = band * H_BAND + start
    lane = lanes_like(base)
    cells = jnp.where(lane >= S_RIGHT, turn(beside, S_RIGHT - at), base)
    return jnp.where(lane >= S_LEFT, turn(beside, LANES - count - at - SLOT), cells)


def strip_own(planes):
    return jnp.where(lanes_like(planes[0]) < S_MID, planes[0], turn(planes[1], -S_TURN))


def first_kernel(
    second_hbm, first_hbm, shifts_hbm, second_0, second_1, first_0, first_1, coarse, swap_0, swap_1, own_meta,
    shifts, sems, shift_sem,
):
    seconds, firsts = (second_0, second_1), (first_0, first_1)
    bands, height, _ = second_0.shape
    width = COLUMNS
    coarse_height = height // FACTOR
    lane = lanes_of()
    get_shifts = pltpu.make_async_copy(shifts_hbm, shifts, shift_sem)
    get_shifts.start()
    copies = []
    for image, (source, refs) in enumerate(((second_hbm, seconds), (first_hbm, firsts))):
        for band in range(bands):
            for tile, ref in enumerate(refs):
                copy = pltpu.make_async_copy(
                    source.at[band, :, pl.ds(tile * LANES, LANES)], ref.at[band], sems.at[image, band, tile]
                )
                copy.start()
                copies.append((image * bands + band, tile, ref, band, copy))
    cell = lax.broadcasted_iota(jnp.int32, (width, LANES), 0)
    place = lax.broadcasted_iota(jnp.int32, (width, LANES), 1)
    weights = jnp.where(place - LEAD == cell // FACTOR, 1.0 / (FACTOR * FACTOR), 0.0).astype(jnp.bfloat16)
    means = []
    packed = [None, None]
    for image, (count, offset) in enumerate(((REACH, 0), (DEPTH, REACH))):
        group = copies[image * 2 * bands : (image + 1) * 2 * bands]
        sums = {}
        for *_, copy in group:
            copy.wait()
        for plane, tile, ref, band, _ in group:
            parts = [ref[band, pl.ds(k, coarse_height, stride=FACTOR), :] for k in range(FACTOR)]
            while len(parts) > 1:
                parts = [x + y for x, y in zip(parts[::2], parts[1::2])]
            sums[plane, tile] = parts[0]
        tall = [jnp.concatenate([sums[image * bands + band, tile] for tile in range(2)], axis=1) for band in range(bands)]
        means.append(split_dot(jnp.concatenate(tall, axis=0), weights))
        packed = [
            pack_image(packed[side], bool(side), (seconds, firsts)[image], count, offset) for side in range(2)
        ]
    means = jnp.concatenate(means, axis=0)
    get_shifts.wait()
    shift_rows = shifts[0, 0, 0].astype(jnp.float32)
    shift_cols = shifts[0, 0, 1].astype(jnp.float32)
    place = lanes_of(height // 2) & (HALF - 1)
    packed = [
        jnp.where(place == SHIFT_R, shift_rows, jnp.where(place == SHIFT_C, shift_cols, jnp.where(place == EXISTS, 1.0, x)))
        for x in packed
    ]
    to_left, to_right = [pack_means(packed[side], bool(side), means) for side in range(2)]
    coarse[...] = means
    own_meta[...] = jnp.where(lane < HALF, shift_rows, shift_cols)
    even = is_even("col", swap_0)
    swap_0[...] = jnp.where(even, to_right, to_left)
    swap_1[...] = jnp.where(even, to_left, to_right)


def message_kernel(
    count, coarse, own_meta, got_0, got_1, up_part, down_part, _whole, swap_0, swap_1, from_left, from_right, wide
):
    other = without_ends(got_1, "col", count)
    even = is_even("col", got_0)
    from_right[...] = jnp.where(even, got_0[...], other)
    from_left[...] = jnp.where(even, other, got_0[...])
    planes_coarse, coarse_height, _ = wide.shape
    bands = planes_coarse // 2
    end = from_left.shape[0]
    coarse_width = COLUMNS // FACTOR
    lane = lanes_of()
    wides = []
    for plane in range(planes_coarse):
        half, block = divmod(plane, planes_coarse // 2)
        for step in range(coarse_height // SUB):
            own = slice(plane * coarse_height + step * SUB, plane * coarse_height + (step + 1) * SUB)
            rows = slice(block * coarse_height + step * SUB, block * coarse_height + (step + 1) * SUB)
            at = half * HALF
            left = from_left[rows, :]
            right = from_right[rows, :]
            start = LEAD - C_SECOND
            cells = turn(left, start - at - COARSE_A)
            cells = jnp.where(lane >= start + 3, turn(left, start + 3 - at - COARSE_B), cells)
            cells = jnp.where(lane >= LEAD, coarse[own, :], cells)
            start = LEAD + coarse_width
            cells = jnp.where(lane >= start, turn(right, start - at - COARSE_A), cells)
            cells = jnp.where(lane >= start + 3, turn(right, start + 3 - at - COARSE_B), cells)
            wides.append((plane, step, cells))
    for plane, step, cells in wides:
        wide[plane, step * SUB : (step + 1) * SUB, :] = cells
    row = lax.broadcasted_iota(jnp.int32, (SUB, LANES), 0)
    meta = jnp.where(lane < 16, own_meta[...], jnp.where(lane < 32, turn(own_meta[...], HALF), 1.0))
    for message, at in ((from_left, 48), (from_right, 80)):
        first_rows = message[0:SUB, :]
        rows = jnp.broadcast_to(first_rows[:, SHIFT_R : SHIFT_R + 1], (SUB, LANES))
        cols = jnp.broadcast_to(first_rows[:, SHIFT_C : SHIFT_C + 1], (SUB, LANES))
        meta = jnp.where(lane >= at, rows, meta)
        meta = jnp.where(lane >= at + 16, cols, meta)

    def beside(rows, half):
        left = from_left[rows, :]
        right = from_right[rows, :]
        cells = jnp.zeros((SUB, LANES), jnp.float32)
        for band in range(bands):
            at = half * HALF + band * SLOT
            cells = jnp.where(lane >= band * H_BAND, turn(right, band * H_BAND - at), cells)
            cells = jnp.where(lane >= band * H_BAND + SLOT, turn(left, band * H_BAND + SLOT - at), cells)
        return cells

    even = is_even("row", meta)
    parts = []
    for part, half, near, next_rows, row_of in (
        (up_part, 0, slice(0, 8), slice(8, 16), 0),
        (down_part, 1, slice(end - 8, end), slice(end - 16, end - 8), 7),
    ):
        eight = beside(near, half)
        one = beside(next_rows, half)
        one = jnp.broadcast_to(one[row_of : row_of + 1], (SUB, LANES))
        coarse_rows = []
        for band in range(bands):
            rows = slice(0, C_SECOND) if half == 0 else slice(coarse_height - C_SECOND, coarse_height)
            second = wide[band, rows, :]
            first = turn(wide[bands + band, rows, :], HALF)
            coarse_rows.append(jnp.where(lanes_like(second) < HALF, second, first))
        parts.append([
            (part[E8:H8, :], E8), (eight, H8), (part[E1:H1, :], E1), (jnp.where(row == 0, one, meta), H1),
            (part[F4:CS, :], F4), *[(x, CS + k * C_SECOND) for k, x in enumerate(coarse_rows)],
        ])
    for (up, at), (down, _) in zip(*parts):
        even = is_even("row", up)
        swap_0[at : at + up.shape[0], :] = jnp.where(even, down, up)
        swap_1[at : at + up.shape[0], :] = jnp.where(even, up, down)


def coarse_flow_of(second, first, mask):
    def along_rows(x):
        return pltpu.roll(x, x.shape[0] - 1, 0) - pltpu.roll(x, 1, 0)

    def along_cols(x):
        return pltpu.roll(x, LANES - 1, 1) - pltpu.roll(x, 1, 1)

    bands = BANDS
    size = second.shape[0] // bands
    grad_rows = 0.125 * along_rows(second)
    grad_cols = 0.125 * along_cols(second)
    offset = 0.25 * (second - first)
    data = jnp.clip(offset, -LIMIT, LIMIT)
    yield

    def pull(grads):
        terms = data * grads
        return sum(terms[k * size : (k + 1) * size] for k in range(bands))

    def tall(x):
        return jnp.concatenate([x] * bands, axis=0)

    flow = [-mask * pull(grad_rows), -mask * pull(grad_cols)]
    extrapolated = [2.0 * x for x in flow]
    dual_rows = [0.0, 0.0]
    dual_cols = [0.0, 0.0]
    yield
    for step in range(1, STEPS):
        changes = [(along_rows(x), along_cols(x)) for x in extrapolated]
        yield
        data = data + offset + grad_rows * tall(extrapolated[0]) + grad_cols * tall(extrapolated[1])
        data = jnp.clip(data, -LIMIT, LIMIT)
        yield
        for c in range(2):
            rows = dual_rows[c] + changes[c][0]
            cols = dual_cols[c] + changes[c][1]
            scale = jnp.minimum(mask, (8.0 * ALPHA) * lax.rsqrt(rows * rows + cols * cols))
            dual_rows[c] = rows * scale
            dual_cols[c] = cols * scale
        yield
        divergences = [along_rows(dual_rows[c]) + along_cols(dual_cols[c]) for c in range(2)]
        yield
        pulls = [pull(grad_rows), pull(grad_cols)]
        yield
        for c in range(2):
            following = flow[c] + mask * ((1.0 / 64.0) * divergences[c] - pulls[c])
            extrapolated[c] = 2.0 * following - flow[c]
            flow[c] = following
        yield
    return flow


def columns_of_planes(planes):
    whole = lax.broadcasted_iota(jnp.int32, (LANES, COLUMNS), 1)
    lane = lax.broadcasted_iota(jnp.int32, (LANES, LANES), 1)
    strip = jnp.where(lane < S_MID, lane, jnp.where(lane < S_LEFT, lane + (COLUMNS - S_RIGHT), lane - LANES))
    return jnp.concatenate([x for x, wanted in ((whole, "whole"), (strip, "strip")) if wanted in planes], axis=1)


def upsample(flow, planes, target):
    column = columns_of_planes(planes)
    source = lax.broadcasted_iota(jnp.int32, column.shape, 0)
    spread = jnp.where(source - LEAD == lax.shift_right_arithmetic(column, 3), float(FACTOR), 0.0).astype(jnp.bfloat16)
    rows = flow[0].shape[0]
    wide = split_dot(UNIT * jnp.concatenate(flow, axis=0), spread)
    for c in range(2):
        for tile in range(column.shape[1] // LANES):
            target[c, tile] = wide[c * rows : (c + 1) * rows, tile * LANES : (tile + 1) * LANES]


def repeat_rows(spread, initial, cells):
    for c in range(2):
        for tile in range(initial.shape[1]):
            rows = [jnp.broadcast_to(spread[c, tile, cell : cell + 1, :], (SUB, LANES)) for cell in cells]
            initial[c, tile, GUARD : GUARD + SUB * len(cells), :] = jnp.concatenate(rows, axis=0)


def shift_whole(here, shift):
    turned = [turn_back(x, shift) for x in here]
    lane = lanes_like(here[0])
    return [
        jnp.where(lane + shift >= LANES, turned[1], turned[0]),
        jnp.where(lane + shift < 0, turned[0], turned[1]),
    ]


def edge_lanes(rows):
    lane = lanes_of(rows)
    return lane == LANES - 1, lane == 0


def columns_whole(fields, edges):
    rows = fields[0].shape[0]
    if rows not in edges:
        edges[rows] = edge_lanes(rows)
    last, first = edges[rows]
    ahead = [pltpu.roll(x, LANES - 1, 1) for x in fields]
    behind = [pltpu.roll(x, 1, 1) for x in fields]
    return [
        jnp.where(last, ahead[1], ahead[0]) - behind[0],
        ahead[1] - jnp.where(first, behind[0], behind[1]),
    ]


def rows_within(tall):
    size = tall.shape[0]
    return (pltpu.roll(tall, size - 1, 0) - pltpu.roll(tall, 1, 0))[SUB : size - SUB]


def columns_strip(field):
    return pltpu.roll(field, LANES - 1, 1) - pltpu.roll(field, 1, 1)


def strip_windows(window, centre, right, left):
    own = turn_back(window(centre[0]), centre[1])
    beyond_left = turn_back(window(left[0]), left[1])
    beyond_right = turn_back(window(right[0]), right[1])
    lane = lanes_like(own)
    beyond = jnp.where((lane >= S_LEFT) | (lane < S_MID), beyond_left, beyond_right)
    is_beyond = lane >= S_RIGHT
    of_next = is_beyond & (lane != S_RIGHT) | (lane == 0)
    of_previous = is_beyond & (lane != LANES - 1) | (lane == S_RIGHT - 1)
    change = turn(jnp.where(of_next, beyond, own), -1) - turn(jnp.where(of_previous, beyond, own), 1)
    return jnp.where(is_beyond, beyond, own), change


def fine_steps(
    rows_total, chunk, columns, initial, extrap, dual_rows, dual_cols, change, dual_data,
    offsets, grads_rows, grads_cols, data_row, masks_of, result, kept, done=lambda k: None,
):
    assert STEPS == 3
    planes = len(offsets)
    bands = offsets[0].shape[0]
    chunks = rows_total // chunk

    def places(k, trim=(0, 0)):
        start, size = k * chunk + trim[0], chunk - sum(trim)
        return pl.ds(GUARD + start, size), pl.ds(start, size), pl.ds(data_row(k) + trim[0], size)

    def row_change(ref, c, tile, at):
        return ref[c, tile, pl.ds(at.start + 1, at.size), :] - ref[c, tile, pl.ds(at.start - 1, at.size), :]

    def clip(x):
        return jnp.clip(x, -UNIT * LIMIT, UNIT * LIMIT)

    tiles = range(planes)

    for step in range(STEPS):
        source = initial if step == 0 else extrap
        final = step == STEPS - 1

        def dual(item, source=source, step=step):
            k, c = item
            at, own, _ = places(k)
            masks = masks_of(own)
            along = columns([source[c, tile, at, :] for tile in tiles])
            values = []
            for tile in tiles:
                rows = row_change(source, c, tile, at)
                cols = along[tile]
                if step > 0:
                    rows = rows + dual_rows[c, tile, at, :]
                    cols = cols + dual_cols[c, tile, own, :]
                scale = jnp.minimum(masks[tile], lax.rsqrt(rows * rows + cols * cols))
                values.append((rows * scale, cols * scale))
            return values

        def store_dual(item, values):
            k, c = item
            for tile, (rows, cols) in enumerate(values):
                dual_rows[c, tile, places(k)[0], :] = rows
                dual_cols[c, tile, places(k)[1], :] = cols

        staggered([(k, c) for k in range(chunks) for c in range(2)], dual, store_dual, 1)
        along_of = {}

        def primal(item, step=step, final=final, along_of=along_of):
            k, tile = item
            at, own, data = places(k, kept(k) if final else (0, 0))
            if k not in along_of:
                along_of[k] = [columns([dual_cols[c, t, own, :] for t in tiles]) for c in range(2)]
            mask = masks_of(own)[tile]
            start = [initial[c, tile, at, :] for c in range(2)]
            if step > 0:
                moved = [extrap[c, tile, at, :] - start[c] for c in range(2)]
            if step == 1:
                changes = [0.5 * x for x in moved]
            if step == 2:
                changes = [change[c, tile, own, :] for c in range(2)]
            pulls = [None, None]
            duals = []
            for band in range(bands):
                gradient = (grads_rows[tile][band, data, :], grads_cols[tile][band, data, :])
                value = offsets[tile][band, data, :]
                if step > 0:
                    earlier = clip(value) if step == 1 else dual_data[band, tile, own, :]
                    value = (value + earlier) + (gradient[0] * moved[0] + gradient[1] * moved[1])
                value = clip(value)
                duals.append(value)
                for c in range(2):
                    term = value * gradient[c]
                    pulls[c] = term if pulls[c] is None else pulls[c] + term
            flows, nexts = [], []
            for c in range(2):
                divergence = row_change(dual_rows, c, tile, at) + along_of[k][c][tile]
                moving = (mask * (1.0 / 64.0)) * divergence - pulls[c]
                total = moving if step == 0 else changes[c] + moving
                flows.append((start[c] + total) * (1.0 / UNIT) if final else total)
                nexts.append(None if final else start[c] + (total + moving))
            return flows, nexts, duals

        def store_primal(item, results, step=step, final=final):
            k, tile = item
            flows, nexts, duals = results
            at, own, _ = places(k, kept(k) if final else (0, 0))
            for c in range(2):
                if final:
                    result[c, tile, own, :] = flows[c]
                else:
                    if step > 0:
                        change[c, tile, own, :] = flows[c]
                    extrap[c, tile, at, :] = nexts[c]
            if final:
                if tile == planes - 1:
                    done(k)
            elif step > 0:
                for band in range(bands):
                    dual_data[band, tile, own, :] = duals[band]

        staggered([(k, tile) for k in range(chunks) for tile in tiles], primal, store_primal, 1)


def clear_guards(*refs):
    for ref in refs:
        rows = ref.shape[2]
        zero = jnp.zeros((GUARD, LANES), jnp.float32)
        for c in range(2):
            for tile in range(ref.shape[1]):
                ref[c, tile, 0:GUARD, :] = zero
                ref[c, tile, rows - GUARD : rows, :] = zero


def fine_scratch(bands, planes, rows):
    guarded = pltpu.VMEM((2, planes, rows + 2 * GUARD, LANES), jnp.float32)
    plain = pltpu.VMEM((2, planes, rows, LANES), jnp.float32)
    return [guarded, guarded, guarded, plain, plain, pltpu.VMEM((bands, planes, rows, LANES), jnp.float32)]


def pieces(bands, height, rows):
    assert (height - 2 * SUB) % rows == 0
    return [(band, row) for row in range(SUB, height - SUB, rows) for band in range(bands)]


def whole_terms_kernel(
    second_0, second_1, first_0, first_1, coarse, own_meta,
    offset, grad_rows, grad_cols, initial, strip_e, strip_f, up, down, moved, spread,
):
    seconds, firsts = (second_0, second_1), (first_0, first_1)
    bands, height, _ = second_0.shape
    block = 120
    coarse_height = coarse.shape[0] // (2 * bands)
    shift_rows, shift_cols = scalar_at(own_meta, 0, 0), scalar_at(own_meta, 0, HALF)
    centre = (shift_rows.astype(jnp.int32), shift_cols.astype(jnp.int32))
    def windows(band, row, rows):
        here = [ref[band, pl.ds(row + centre[0], rows), :].reshape(-1, LANES) for ref in seconds]
        return shift_whole(here, centre[1])

    woven = Woven(coarse_flow_of(coarse[0 : bands * coarse_height, :], coarse[bands * coarse_height :, :], 1.0))

    ends = [(row, windows(slice(None), row, SUB)) for row in (SUB // 2, height - SUB - SUB // 2)]
    for row, values in ends:
        for tile in range(2):
            moved[tile, :, row : row + SUB, :] = values[tile].reshape(bands, SUB, LANES)

    edges = {}

    def values_of(item):
        band, row = item
        values = windows(band, row, block)
        along = columns_whole(values, edges)
        own = [ref[band, row : row + block, :] for ref in firsts]
        return values, [(0.25 * UNIT) * (x - y) for x, y in zip(values, own)], [0.125 * x for x in along]

    def store_values(item, results):
        band, row = item
        values, offsets, gradients = results
        data = slice(row + HALO, row + HALO + block)
        for tile in range(2):
            moved[tile, band, row : row + block, :] = values[tile]
            offset[tile, band, data, :] = offsets[tile]
            grad_cols[tile, band, data, :] = gradients[tile]

    staggered(pieces(bands, height, block), values_of, store_values, 1, woven)

    def strips_of(item):
        band, row = item
        rows = slice(row, row + LANES)
        return strip_own([ref[band, rows, :] for ref in seconds]), strip_own([ref[band, rows, :] for ref in firsts])

    def store_strips(item, results):
        band, row = item
        strip_e[band, row : row + LANES, :], strip_f[band, row : row + LANES, :] = results

    staggered([(band, row) for band in range(bands) for row in range(0, height, LANES)], strips_of, store_strips, 1, woven)

    def gradient_of(item):
        band, row = item
        return [0.125 * rows_within(moved[tile, band, row - SUB : row + 120 + SUB, :]) for tile in range(2)]

    def store_gradient(item, results):
        band, row = item
        for tile in range(2):
            grad_rows[tile, band, row + HALO : row + HALO + 120, :] = results[tile]

    staggered(pieces(bands, height, 120), gradient_of, store_gradient, 1, woven)

    parts = []
    for band in range(bands):
        for second, first in zip(seconds, firsts):
            parts.append((
                second[band, 0:16, :], first[band, 0:8, :],
                second[band, height - 16 : height, :], first[band, height - 8 : height, :],
            ))
    for k, (second_top, first_top, second_end, first_end) in enumerate(parts):
        up[E8 + 8 * k : E8 + 8 * k + 8, :] = second_top[0:8]
        up[E1 + k : E1 + k + 1, :] = second_top[8:9]
        up[F4 + 4 * k : F4 + 4 * k + 4, :] = first_top[0:4]
        down[E8 + 8 * k : E8 + 8 * k + 8, :] = second_end[8:16]
        down[E1 + k : E1 + k + 1, :] = second_end[7:8]
        down[F4 + 4 * k : F4 + 4 * k + 4, :] = first_end[4:8]
    for target in (up, down):
        for start, end in ((H8, E1), (H1, F4), (CS, ROW_MESSAGE)):
            target[start:end, :] = jnp.zeros((end - start, LANES), jnp.float32)

    upsample(woven.finish(), ("whole",), spread)
    clear_guards(initial)
    rows_total = initial.shape[2] - 2 * GUARD
    repeat_rows(spread, initial, [BEGIN // FACTOR + k for k in range(rows_total // SUB)])


def whole_steps_kernel(
    initial, offset, grad_rows, grad_cols, result, extrap, dual_rows, dual_cols, change, dual_data
):
    rows_total = result.shape[2]
    clear_guards(extrap, dual_rows)
    chunk = 88
    edges = {}
    fine_steps(
        rows_total, chunk, lambda fields: columns_whole(fields, edges),
        initial, extrap, dual_rows, dual_cols, change, dual_data,
        *[[ref.at[tile] for tile in range(2)] for ref in (offset, grad_rows, grad_cols)],
        lambda k: HALO + BEGIN + k * chunk, lambda own: (1.0, 1.0), result, lambda k: (SUB * (k == 0), SUB * (k == 1)),
    )


def strip_kernel(
    strip_e, strip_f, from_left, from_right, wide, own_meta, whole,
    middle, strip_out, first_ends, offset, grad_rows, grad_cols,
    moved, result, spread, initial, extrap, dual_rows, dual_cols, change, dual_data,
):
    bands, height, _ = strip_e.shape
    block = 120
    coarse_height = height // FACTOR
    coarse_width = COLUMNS // FACTOR
    rows_total = height - 2 * BEGIN
    lane = lanes_of()
    centre = (int_at(own_meta, 0, 0), int_at(own_meta, 0, HALF))
    right, has_right = column_meta(from_right)
    left, has_left = column_meta(from_left)
    exists = jnp.where(lane < S_RIGHT, 1.0, jnp.where(lane < S_LEFT, has_right, has_left))

    def tall_factor(rows):
        return 0.125 * jnp.concatenate([exists] * (rows // SUB), axis=0)

    mask = jnp.where(lane < LEAD, has_left, jnp.where(lane < LEAD + coarse_width, 1.0, has_right))
    mask = jnp.concatenate([mask] * (coarse_height // SUB), axis=0)
    cells = [wide[k * bands : (k + 1) * bands].reshape(bands * coarse_height, LANES) for k in range(2)]
    woven = Woven(coarse_flow_of(*cells, mask))

    def halves(row, rows):
        half = row // (height // 2)
        start = row - half * (height // 2)
        return half, slice(start, start + rows)

    def second_of(item):
        band, row = item
        half, message = halves(row, LANES)
        return strip_second(strip_e[band, row : row + LANES, :], from_left, from_right, message, half, band)

    def store_second(item, value):
        band, row = item
        strip_out[band, row : row + LANES, :] = value

    staggered([(band, row) for row in range(0, height, LANES) for band in range(bands)], second_of, store_second, 1, woven)

    def first_of(band, row, rows):
        half, message = halves(row, rows)
        return strip_first(strip_f[band, row : row + rows, :], from_left, from_right, message, half, band)

    firsts = [(end, band, first_of(band, (0, height - SUB)[end], SUB)) for end in range(2) for band in range(bands)]
    for end, band, value in firsts:
        first_ends[end, band] = value

    def windows(band, row, rows):
        return strip_windows(
            lambda shift: strip_out[band, pl.ds(row + shift, rows), :].reshape(-1, LANES), centre, right, left
        )

    ends = [(row, windows(slice(None), row, SUB)[0]) for row in (SUB // 2, height - SUB - SUB // 2)]
    for row, value in ends:
        moved[:, row : row + SUB, :] = value.reshape(bands, SUB, LANES)

    factor = tall_factor(block)

    def values_of(item):
        band, row = item
        value, along = windows(band, row, block)
        return value, (0.25 * UNIT) * (value - first_of(band, row, block)), factor * along

    def store_values(item, results):
        band, row = item
        data = slice(row + HALO, row + HALO + block)
        moved[band, row : row + block, :], offset[band, data, :], grad_cols[band, data, :] = results

    staggered(pieces(bands, height, block), values_of, store_values, 1, woven)

    def gradient_of(item):
        band, row = item
        return factor * rows_within(moved[band, row - SUB : row + block + SUB, :])

    def store_gradient(item, value):
        band, row = item
        grad_rows[band, row + HALO : row + HALO + block, :] = value

    staggered(pieces(bands, height, block), gradient_of, store_gradient, 1, woven)

    upsample(woven.finish(), ("strip",), spread)
    clear_guards(initial, extrap, dual_rows)
    repeat_rows(spread, initial, [BEGIN // FACTOR + k for k in range(rows_total // SUB)])

    chunk = 176
    masks = jnp.concatenate([exists] * (chunk // SUB), axis=0)
    fine_steps(
        rows_total, chunk, lambda fields: [columns_strip(fields[0])],
        initial, extrap, dual_rows, dual_cols, change, dual_data, [offset], [grad_rows], [grad_cols],
        lambda k: HALO + BEGIN + k * chunk, lambda own: (masks[: own.size],), result, lambda k: (SUB, SUB),
    )
    join(whole, result.at[:, 0], middle, slice(SUB, rows_total - SUB))


def join(whole, strip, target, rows):
    lane = lanes_of(rows.stop - rows.start)
    values = []
    for c in range(2):
        edge = strip[c, rows, :]
        start = jnp.where(lane < EDGE, edge, whole[c, 0, rows, :])
        values.append((start, jnp.where(lane >= LANES - EDGE, turn(edge, S_TURN), whole[c, 1, rows, :])))
    for c in range(2):
        target[c, rows, 0:LANES], target[c, rows, LANES:COLUMNS] = values[c]


def outer_kernel(
    count, second_0, second_1, first_0, first_1, strip_e, first_ends, from_left, from_right, wide, got_1, got_0, middle, own_meta,
    _wo, _wr, _wc, _so, _sr, _sc,
    flow_out, coarse_out, whole_offset, whole_rows, whole_cols, strip_offset, strip_rows, strip_cols,
    from_up, from_down, extended, tall, spread, masks, result, joined, coarse_result, sems,
    initial, extrap, dual_rows, dual_cols, change, dual_data,
):
    bands, height, _ = second_0.shape
    coarse_height = height // FACTOR
    coarse_width = COLUMNS // FACTOR
    rows_total = 2 * EACH
    lane = lanes_of()

    put_middle = pltpu.make_async_copy(
        middle.at[:, pl.ds(MARGIN - BEGIN, height - 2 * MARGIN), :],
        flow_out.at[:, pl.ds(MARGIN, height - 2 * MARGIN), :],
        sems.at[0],
    )
    put_middle.start()

    other = without_ends(got_1, "row", count)
    even = is_even("row", got_0)
    from_down[...] = jnp.where(even, got_0[...], other)
    from_up[...] = jnp.where(even, other, got_0[...])

    own = (int_at(own_meta, 0, 0), int_at(own_meta, 0, HALF))
    own_right, has_right = column_meta(from_right)
    own_left, has_left = column_meta(from_left)
    has_up = scalar_at(from_up, META, 32)
    has_down = scalar_at(from_down, META, 32)
    exists = jnp.where(lane < S_RIGHT, 1.0, jnp.where(lane < S_LEFT, has_right, has_left))

    def trio(message):
        return (
            (int_at(message, META, 0), int_at(message, META, 16)),
            (int_at(message, META, 80), int_at(message, META, 96)),
            (int_at(message, META, 48), int_at(message, META, 64)),
        )

    above = trio(from_up)
    below = trio(from_down)

    zero = jnp.zeros((SUB, LANES), jnp.float32)
    tall_rows = coarse_height + 2 * LEAD
    parts = []
    fill = jnp.zeros((LEAD - C_SECOND, LANES), jnp.float32)
    for plane in range(2 * bands):
        at = CS + C_SECOND * (plane % bands)
        ends = [turn(message[at : at + C_SECOND, :], HALF * (plane // bands)) for message in (from_up, from_down)]
        parts.append([fill, ends[0], wide[plane], ends[1], fill])
    for plane, values in enumerate(parts):
        tall[plane] = jnp.concatenate(values, axis=0)
    across = jnp.where(lane < LEAD, has_left, jnp.where(lane < LEAD + coarse_width, 1.0, has_right))
    mask = jnp.concatenate([across * has_up] + [across] * (coarse_height // SUB) + [across * has_down], axis=0)
    for end in range(2):
        message = (from_up, from_down)[end]
        beside = message[H8 : H8 + 8, :]
        beside_one = jnp.broadcast_to(message[H1 : H1 + 1, :], (SUB, LANES))
        parts = []
        for band in range(bands):
            eights = [message[E8 + 8 * k : E8 + 8 * k + 8, :] for k in (2 * band, 2 * band + 1)]
            ones = [jnp.broadcast_to(message[E1 + k : E1 + k + 1, :], (SUB, LANES)) for k in (2 * band, 2 * band + 1)]
            eights.append(strip_halo(strip_own(eights), beside, band, 0, REACH))
            ones.append(strip_halo(strip_own(ones), beside_one, band, 0, REACH))
            for tile, (eight, one) in enumerate(zip(eights, ones)):
                source = (second_0, second_1, strip_e)[tile]
                if end == 0:
                    parts.append((tile, band, [one, eight, source[band, 0:24, :]]))
                else:
                    parts.append((tile, band, [source[band, height - 24 : height, :], eight, one]))
        for tile, band, values in parts:
            extended[end, tile, band] = jnp.concatenate(values, axis=0)
    cells = [tall[k * bands : (k + 1) * bands].reshape(bands * tall_rows, LANES) for k in range(2)]
    woven = Woven(coarse_flow_of(*cells, mask))
    edges = {}
    rows_data = whole_offset.shape[2]
    exists_tall = jnp.concatenate([exists] * bands, axis=0)

    def rows_of(halo, end):
        if halo:
            return slice(0, SUB) if end == 0 else slice(rows_data - SUB, rows_data)
        return slice(HALO, HALO + SUB) if end == 0 else slice(rows_data - HALO - SUB, rows_data - HALO)

    def values_of(item):
        halo, end = item
        message = (from_up, from_down)[end]
        base = (SUB, 3 * SUB)[end] if halo else 2 * SUB
        shifts = (above, below)[end] if halo else (own, own_right, own_left)
        factor = 0.125 * (has_up, has_down)[end] if halo else 0.125

        def here(tile, shift):
            return extended[end, tile, :, pl.ds(base + shift, SUB), :].reshape(-1, LANES)

        def down_up(tile, shift):
            return here(tile, shift + 1) - here(tile, shift - 1)

        own_rows = slice(0, SUB) if end == 0 else slice(height - SUB, height)
        if halo:
            firsts = [[], [], []]
            for band in range(bands):
                eights = []
                for k in (2 * band, 2 * band + 1):
                    four = message[F4 + 4 * k : F4 + 4 * k + 4, :]
                    eights.append(jnp.concatenate([four, four], axis=0))
                eights.append(strip_halo(strip_own(eights), message[H8 : H8 + 8, :], band, REACH, DEPTH))
                for tile in range(3):
                    firsts[tile].append(eights[tile])
            firsts = [jnp.concatenate(x, axis=0) for x in firsts]
        else:
            firsts = [x.reshape(-1, LANES) for x in (first_0[:, own_rows, :], first_1[:, own_rows, :], first_ends[end])]
        centre = shifts[0]
        values = shift_whole([here(tile, centre[0]) for tile in range(2)], centre[1])
        changes = shift_whole([down_up(tile, centre[0]) for tile in range(2)], centre[1])
        along = columns_whole(values, edges)
        value, across_cols = strip_windows(lambda shift: here(2, shift), *shifts)
        change_rows, _ = strip_windows(lambda shift: down_up(2, shift), *shifts)
        return (
            [(0.25 * UNIT) * (x - y) for x, y in zip([*values, value], firsts)],
            [*[factor * x for x in changes], (factor * exists_tall) * change_rows],
            [*[factor * x for x in along], (factor * exists_tall) * across_cols],
        )

    def store_values(item, results):
        rows = rows_of(*item)
        for values, whole, strip in zip(
            results, (whole_offset, whole_rows, whole_cols), (strip_offset, strip_rows, strip_cols)
        ):
            values = [x.reshape(bands, SUB, LANES) for x in values]
            for tile in range(2):
                whole[tile, :, rows, :] = values[tile]
            strip[:, rows, :] = values[2]

    staggered([(halo, end) for halo in (True, False) for end in range(2)], values_of, store_values, 1, woven)

    flow = woven.finish()
    for c in range(2):
        coarse_result[c] = turn(flow[c][LEAD : LEAD + coarse_height], -LEAD)[:, :coarse_width]
    put_coarse = pltpu.make_async_copy(coarse_result, coarse_out, sems.at[1])
    put_coarse.start()
    upsample(flow, ("whole", "strip"), spread)
    clear_guards(initial, extrap, dual_rows)
    each = EACH // SUB
    repeat_rows(
        spread, initial,
        [LEAD - 1 + k for k in range(each)] + [tall_rows - LEAD + 1 - each + k for k in range(each)],
    )

    for i, value in enumerate((jnp.ones((SUB, LANES), jnp.float32), exists)):
        masks[i] = jnp.concatenate([value * has_up] + [value] * (rows_total // SUB - 2) + [value * has_down], axis=0)

    def masks_of(rows):
        whole = masks[0, rows, :]
        return (whole, whole, masks[1, rows, :])

    chunk = EACH
    edges = {}
    puts = [
        pltpu.make_async_copy(
            joined.at[:, pl.ds(k * EACH + SUB, MARGIN), :],
            flow_out.at[:, pl.ds(k * (height - MARGIN), MARGIN), :],
            sems.at[2 + k],
        )
        for k in range(2)
    ]

    def finish(k):
        join(result, result.at[:, 2], joined, slice(k * EACH + SUB, k * EACH + SUB + MARGIN))
        puts[k].start()

    def data_row(k):
        return k * (rows_data - EACH)

    fine_steps(
        rows_total, chunk, lambda fields: columns_whole(fields[:2], edges) + [columns_strip(fields[2])],
        initial, extrap, dual_rows, dual_cols, change, dual_data,
        [whole_offset.at[0], whole_offset.at[1], strip_offset],
        [whole_rows.at[0], whole_rows.at[1], strip_rows],
        [whole_cols.at[0], whole_cols.at[1], strip_cols],
        data_row, masks_of, result, lambda k: (SUB, SUB), finish,
    )
    put_middle.wait()
    put_coarse.wait()
    for put in puts:
        put.wait()


def swap_with(message, axis, start):
    names = ("row", "col")
    sizes = [lax.axis_size(name) for name in names]
    along = names.index(axis)
    count, others = sizes[along], sizes[1 - along]

    def number(place, other):
        row, col = (place, other) if along == 0 else (other, place)
        return row * sizes[1] + col

    pairs = [(number(i, k), number(i + 1, k)) for i in range(start, count - 1, 2) for k in range(others)]
    if start and axis == "col":
        pairs += [(number(i, k), number(i, k + 1)) for i in (0, count - 1) for k in range(0, others, 2)]
    elif start:
        pairs += [(number(0, k), number(count - 1, k)) for k in range(others)]
    return lax.ppermute(message, names, pairs + [(j, i) for i, j in pairs])


def local(frame_first, frame_second, shifts):
    bands, height, width = frame_first.shape
    assert bands == 4 and width == COLUMNS and height % LANES == 0
    assert lax.axis_size("row") % 2 == 0 and lax.axis_size("col") % 2 == 0
    coarse_height = height // FACTOR
    coarse_width = width // FACTOR
    vmem = pl.BlockSpec(memory_space=pltpu.VMEM)
    hbm = pl.BlockSpec(memory_space=pltpu.HBM)
    tall_rows = coarse_height + 2 * LEAD
    inner_rows = height - 2 * BEGIN

    def shape(*sizes):
        return jax.ShapeDtypeStruct(sizes, jnp.float32)

    def scratch(*sizes):
        return pltpu.VMEM(sizes, jnp.float32)

    def call(kernel, name, arguments, outs, scratches=(), flops=1_000_000, **more):
        more = {"in_specs": [vmem] * len(arguments), "out_specs": (vmem,) * len(outs), **more}
        return pl.pallas_call(
            kernel,
            out_shape=tuple(outs),
            scratch_shapes=list(scratches),
            compiler_params=pltpu.CompilerParams(vmem_limit_bytes=24 * 1024 * 1024),
            cost_estimate=pl.CostEstimate(flops=flops, bytes_accessed=1_000_000, transcendentals=0),
            name=name,
            **more,
        )(*arguments)

    plane = shape(bands, height, LANES)
    column_message = shape(height // 2, LANES)
    row_message = shape(ROW_MESSAGE, LANES)
    whole_data = shape(2, bands, height + 2 * HALO, LANES)
    strip_data = shape(bands, height + 2 * HALO, LANES)

    *frames, coarse, swap_0, swap_1, own_meta = call(
        first_kernel,
        "means_and_message",
        [pltpu.with_memory_space_constraint(x, pltpu.HBM) for x in (frame_second, frame_first, shifts)],
        [*[plane] * 4, shape(2 * bands * coarse_height, LANES), column_message, column_message, shape(SUB, LANES)],
        [
            pltpu.SMEM((1, 1, 2), jnp.int32),
            pltpu.SemaphoreType.DMA((2, bands, 2)),
            pltpu.SemaphoreType.DMA,
        ],
        in_specs=[hbm] * 3,
    )
    got_0 = swap_with(swap_0, "col", 0)
    got_1 = swap_with(swap_1, "col", 1)

    *whole_terms, initial, strip_e, strip_f, up_part, down_part = call(
        whole_terms_kernel,
        "whole_terms",
        [*frames, coarse, own_meta],
        [
            *[whole_data] * 3, shape(2, 2, inner_rows + 2 * GUARD, LANES),
            plane, plane, row_message, row_message,
        ],
        [scratch(2, bands, height, LANES), scratch(2, 2, coarse_height, LANES)],
        flops=8_000_000,
    )
    (whole,) = call(
        whole_steps_kernel,
        "whole_steps",
        [initial, *whole_terms],
        [shape(2, 2, inner_rows, LANES)],
        fine_scratch(bands, 2, inner_rows)[1:],
        flops=20_000_000,
    )

    swap_0, swap_1, from_left, from_right, wide = call(
        functools.partial(message_kernel, lax.axis_size("col")),
        "row_messages",
        [coarse, own_meta, got_0, got_1, up_part, down_part, whole],
        [row_message, row_message, column_message, column_message, shape(2 * bands, coarse_height, LANES)],
    )
    got_1 = swap_with(swap_1, "row", 1)
    got_0 = swap_with(swap_0, "row", 0)

    middle, strip_e, first_ends, *strip_terms = call(
        strip_kernel,
        "strip",
        [strip_e, strip_f, from_left, from_right, wide, own_meta, whole],
        [shape(2, inner_rows, width), plane, shape(2, bands, SUB, LANES), *[strip_data] * 3],
        [
            scratch(bands, height, LANES),
            scratch(2, 1, inner_rows, LANES),
            scratch(2, 1, coarse_height, LANES),
            *fine_scratch(bands, 1, inner_rows),
        ],
        flops=16_000_000,
    )

    flow, coarse_flow, *_ = call(
        functools.partial(outer_kernel, lax.axis_size("row")),
        "outer_rows",
        [
            *frames, strip_e, first_ends, from_left, from_right, wide, got_1, got_0, middle, own_meta,
            *whole_terms, *strip_terms,
        ],
        [shape(2, height, width), shape(2, coarse_height, coarse_width), *[whole_data] * 3, *[strip_data] * 3],
        [
            scratch(ROW_MESSAGE, LANES),
            scratch(ROW_MESSAGE, LANES),
            scratch(2, 3, bands, 40, LANES),
            scratch(2 * bands, tall_rows, LANES),
            scratch(2, 3, tall_rows, LANES),
            scratch(2, 2 * EACH, LANES),
            scratch(2, 3, 2 * EACH, LANES),
            scratch(2, 2 * EACH, width),
            scratch(2, coarse_height, coarse_width),
            pltpu.SemaphoreType.DMA((4,)),
            *fine_scratch(bands, 3, 2 * EACH),
        ],
        out_specs=(hbm, hbm) + (vmem,) * 6,
        input_output_aliases={13 + k: 2 + k for k in range(6)},
    )
    return (flow, coarse_flow)


def solution(mesh):
    return jax.shard_map(
        local,
        mesh=mesh,
        in_specs=(P(None, "row", "col"), P(None, "row", "col"), P("row", "col", None)),
        out_specs=(P(None, "row", "col"), P(None, "row", "col")),
        check_vma=False,
    )
```

```python
import functools

import jax
import jax.numpy as jnp
from jax import lax
from jax.experimental import pallas as pl
from jax.experimental.pallas import tpu as pltpu
from jax.sharding import PartitionSpec as P

FACTOR = 8
MAXD = 4
BANDS = 4
STEPS = 3
LANES = 128
COLUMNS = 2 * LANES
HALF = 64
SUB = 8
DEPTH = 4
REACH = DEPTH + MAXD + 1
SLOT = 16
C_SECOND = 6
C_FIRST = 5
LEAD = 8
MARGIN = 48
EDGE = 46
GUARD = 8
HALO = 8
BEGIN = 40
EACH = MARGIN + 16
LIMIT = 0.3
ALPHA = 0.3
UNIT = 0.125 / ALPHA

S_MID = 55
S_RIGHT = 110
S_LEFT = LANES - REACH
S_TURN = COLUMNS - S_RIGHT - LANES

E8 = 0
H8 = 64
E1 = 72
H1 = 80
META = 81
F4 = 88
CS = 120
ROW_MESSAGE = 144
H_BAND = 32

COARSE_A = REACH + DEPTH
COARSE_B = SLOT + REACH + DEPTH
SHIFT_R = 2 * SLOT + REACH + DEPTH
SHIFT_C = SHIFT_R + 1
EXISTS = SHIFT_R + 2


def lanes_of(rows=SUB):
    return lax.broadcasted_iota(jnp.int32, (rows, LANES), 1)


def lanes_like(x):
    return lax.broadcasted_iota(jnp.int32, x.shape, 1)


def turn(x, amount):
    amount = amount % LANES
    return x if amount == 0 else pltpu.roll(x, amount, 1)


def turn_back(x, shift):
    return pltpu.roll(x, lax.rem(LANES - shift, LANES), 1)


def split_dot(x, exact):
    high = x.astype(jnp.bfloat16)
    rest = x - high.astype(jnp.float32)
    middle = rest.astype(jnp.bfloat16)
    low = (rest - middle.astype(jnp.float32)).astype(jnp.bfloat16)
    parts = [jnp.dot(part, exact, preferred_element_type=jnp.float32) for part in (low, middle, high)]
    return parts[0] + parts[1] + parts[2]


def neighbours(axis, count):
    place = lax.axis_index(axis)
    return jnp.where(place > 0, 1.0, 0.0), jnp.where(place < count - 1, 1.0, 0.0)


def shift_at(numbers, row, lane):
    return numbers[row, lane].astype(jnp.int32), numbers[row, lane + SLOT].astype(jnp.int32)


def shifts_of(numbers):
    return [shift_at(numbers, META - H1, lane) for lane in (0, 80, 48)]


def is_even(axis, like):
    return jnp.broadcast_to(lax.axis_index(axis) % 2, like.shape) == 0


def without_ends(message, axis, count):
    place = jnp.broadcast_to(lax.axis_index(axis), message.shape)
    return jnp.where((place > 0) & (place < count - 1), message[...], 0.0)


def staggered(items, compute, store, depth, woven=None):
    pending = []
    for item in items:
        pending.append((item, compute(item)))
        if woven is not None:
            woven.advance()
        if len(pending) > depth:
            store(*pending.pop(0))
    for entry in pending:
        store(*entry)


class Woven:
    def __init__(self, stages):
        self.stages = stages
        self.result = None

    def advance(self):
        try:
            next(self.stages)
            return True
        except StopIteration as end:
            self.result = end.value if self.result is None else self.result
            return False

    def finish(self):
        while self.advance():
            pass
        return self.result


def pack_image(packed, to_right, planes, some, count, offset):
    _, height, _ = planes[0].shape
    plane = planes[int(to_right)]
    start = LANES - count if to_right else 0
    length = height // 2
    lane = lanes_of(length)
    for half in range(2):
        for band in some:
            at = half * HALF + band * SLOT + offset
            cells = turn(plane[band, half * length : (half + 1) * length, :], at - start)
            packed = cells if packed is None else jnp.where((lane >= at) & (lane < at + count), cells, packed)
    return packed


def pack_means(packed, to_right, means):
    length = packed.shape[0]
    start = LEAD + COLUMNS // FACTOR - C_SECOND if to_right else LEAD
    lane = lanes_of(length)
    for half in range(2):
        cells = means[half * length : (half + 1) * length]
        for at, first in ((half * HALF + COARSE_A, start), (half * HALF + COARSE_B, start + 3)):
            packed = jnp.where((lane >= at) & (lane < at + 3), turn(cells, at - first), packed)
    return packed


def strip_second(base, from_left, from_right, rows, half, band):
    at = half * HALF + band * SLOT
    lane = lanes_like(base)
    cells = jnp.where(lane >= S_RIGHT, turn(from_right[rows, :], S_RIGHT - at), base)
    return jnp.where(lane >= S_LEFT, turn(from_left[rows, :], S_LEFT - at), cells)


def strip_first(base, from_left, from_right, rows, half, band):
    at = half * HALF + band * SLOT + REACH
    lane = lanes_like(base)
    cells = jnp.where(lane >= S_RIGHT, turn(from_right[rows, :], S_RIGHT - at), base)
    return jnp.where(lane >= S_LEFT, turn(from_left[rows, :], LANES - DEPTH - at), cells)


def strip_halo(base, beside, band, start, count):
    at = band * H_BAND + start
    lane = lanes_like(base)
    cells = jnp.where(lane >= S_RIGHT, turn(beside, S_RIGHT - at), base)
    return jnp.where(lane >= S_LEFT, turn(beside, LANES - count - at - SLOT), cells)


def strip_own(planes):
    return jnp.where(lanes_like(planes[0]) < S_MID, planes[0], turn(planes[1], -S_TURN))


def first_kernel(
    second_hbm, first_hbm, shifts_hbm, second_0, second_1, first_0, first_1, coarse, swap_0, swap_1, own_meta,
    shifts, sems, shift_sem,
):
    seconds, firsts = (second_0, second_1), (first_0, first_1)
    bands, height, _ = second_0.shape
    width = COLUMNS
    coarse_height = height // FACTOR
    lane = lanes_of()
    get_shifts = pltpu.make_async_copy(shifts_hbm, shifts, shift_sem)
    get_shifts.start()
    copies = []
    for image, (source, refs) in enumerate(((second_hbm, seconds), (first_hbm, firsts))):
        for band in range(bands):
            for tile, ref in enumerate(refs):
                copy = pltpu.make_async_copy(
                    source.at[band, :, pl.ds(tile * LANES, LANES)], ref.at[band], sems.at[image, band, tile]
                )
                copy.start()
                copies.append((image * bands + band, tile, ref, band, copy))
    cell = lax.broadcasted_iota(jnp.int32, (width, LANES), 0)
    place = lax.broadcasted_iota(jnp.int32, (width, LANES), 1)
    weights = jnp.where(place - LEAD == cell // FACTOR, 1.0 / (FACTOR * FACTOR), 0.0).astype(jnp.bfloat16)
    means = []
    packed = [None, None]
    for image, (count, offset) in enumerate(((REACH, 0), (DEPTH, REACH))):
        for pair in range(0, bands, 2):
            some = range(pair, pair + 2)
            group = copies[2 * (image * bands + pair) : 2 * (image * bands + pair + 2)]
            for *_, copy in group:
                copy.wait()
            sums = {}
            for plane, tile, ref, band, _ in group:
                parts = [ref[band, pl.ds(k, coarse_height, stride=FACTOR), :] for k in range(FACTOR)]
                while len(parts) > 1:
                    parts = [x + y for x, y in zip(parts[::2], parts[1::2])]
                sums[band, tile] = parts[0]
            tall = [jnp.concatenate([sums[band, tile] for tile in range(2)], axis=1) for band in some]
            means.append(split_dot(jnp.concatenate(tall, axis=0), weights))
            packed = [
                pack_image(packed[side], bool(side), (seconds, firsts)[image], some, count, offset) for side in range(2)
            ]
    means = jnp.concatenate(means, axis=0)
    get_shifts.wait()
    shift_rows = shifts[0, 0, 0].astype(jnp.float32)
    shift_cols = shifts[0, 0, 1].astype(jnp.float32)
    place = lanes_of(height // 2) & (HALF - 1)
    packed = [
        jnp.where(place == SHIFT_R, shift_rows, jnp.where(place == SHIFT_C, shift_cols, jnp.where(place == EXISTS, 1.0, x)))
        for x in packed
    ]
    to_left, to_right = [pack_means(packed[side], bool(side), means) for side in range(2)]
    coarse[...] = means
    own_meta[...] = jnp.where(lane < SLOT, shift_rows, shift_cols)
    even = is_even("col", swap_0)
    swap_0[...] = jnp.where(even, to_right, to_left)
    swap_1[...] = jnp.where(even, to_left, to_right)


def message_kernel(
    count, coarse, own_meta, got_0, got_1, up_part, down_part, _whole, swap_0, swap_1, from_left, from_right, wide
):
    other = without_ends(got_1, "col", count)
    even = is_even("col", got_0)
    from_right[...] = jnp.where(even, got_0[...], other)
    from_left[...] = jnp.where(even, other, got_0[...])
    planes_coarse, coarse_height, _ = wide.shape
    bands = planes_coarse // 2
    end = from_left.shape[0]
    coarse_width = COLUMNS // FACTOR
    lane = lanes_of()
    wides = []
    for plane in range(planes_coarse):
        half, block = divmod(plane, planes_coarse // 2)
        for step in range(coarse_height // SUB):
            own = slice(plane * coarse_height + step * SUB, plane * coarse_height + (step + 1) * SUB)
            rows = slice(block * coarse_height + step * SUB, block * coarse_height + (step + 1) * SUB)
            at = half * HALF
            left = from_left[rows, :]
            right = from_right[rows, :]
            start = LEAD - C_SECOND
            cells = turn(left, start - at - COARSE_A)
            cells = jnp.where(lane >= start + 3, turn(left, start + 3 - at - COARSE_B), cells)
            cells = jnp.where(lane >= LEAD, coarse[own, :], cells)
            start = LEAD + coarse_width
            cells = jnp.where(lane >= start, turn(right, start - at - COARSE_A), cells)
            cells = jnp.where(lane >= start + 3, turn(right, start + 3 - at - COARSE_B), cells)
            wides.append((plane, step, cells))
    for plane, step, cells in wides:
        wide[plane, step * SUB : (step + 1) * SUB, :] = cells
    row = lax.broadcasted_iota(jnp.int32, (SUB, LANES), 0)
    meta = own_meta[...]
    for message, at in ((from_left, 48), (from_right, 80)):
        first_rows = message[0:SUB, :]
        rows = jnp.broadcast_to(first_rows[:, SHIFT_R : SHIFT_R + 1], (SUB, LANES))
        cols = jnp.broadcast_to(first_rows[:, SHIFT_C : SHIFT_C + 1], (SUB, LANES))
        meta = jnp.where(lane >= at, rows, meta)
        meta = jnp.where(lane >= at + 16, cols, meta)

    def beside(rows, half):
        left = from_left[rows, :]
        right = from_right[rows, :]
        cells = jnp.zeros((SUB, LANES), jnp.float32)
        for band in range(bands):
            at = half * HALF + band * SLOT
            cells = jnp.where(lane >= band * H_BAND, turn(right, band * H_BAND - at), cells)
            cells = jnp.where(lane >= band * H_BAND + SLOT, turn(left, band * H_BAND + SLOT - at), cells)
        return cells

    even = is_even("row", meta)
    parts = []
    for part, half, near, next_rows, row_of in (
        (up_part, 0, slice(0, 8), slice(8, 16), 0),
        (down_part, 1, slice(end - 8, end), slice(end - 16, end - 8), 7),
    ):
        eight = beside(near, half)
        one = beside(next_rows, half)
        one = jnp.broadcast_to(one[row_of : row_of + 1], (SUB, LANES))
        coarse_rows = []
        for band in range(bands):
            rows = slice(0, C_SECOND) if half == 0 else slice(coarse_height - C_SECOND, coarse_height)
            second = wide[band, rows, :]
            first = turn(wide[bands + band, rows, :], HALF)
            coarse_rows.append(jnp.where(lanes_like(second) < HALF, second, first))
        parts.append([
            (part[E8:H8, :], E8), (eight, H8), (part[E1:H1, :], E1), (jnp.where(row == 0, one, meta), H1),
            (part[F4:CS, :], F4), *[(x, CS + k * C_SECOND) for k, x in enumerate(coarse_rows)],
        ])
    for (up, at), (down, _) in zip(*parts):
        even = is_even("row", up)
        swap_0[at : at + up.shape[0], :] = jnp.where(even, down, up)
        swap_1[at : at + up.shape[0], :] = jnp.where(even, up, down)


def coarse_flow_of(second, first, mask):
    def along_rows(x):
        return pltpu.roll(x, x.shape[0] - 1, 0) - pltpu.roll(x, 1, 0)

    def along_cols(x):
        return pltpu.roll(x, LANES - 1, 1) - pltpu.roll(x, 1, 1)

    bands = BANDS
    size = second.shape[0] // bands
    grad_rows = 0.125 * along_rows(second)
    grad_cols = 0.125 * along_cols(second)
    offset = 0.25 * (second - first)
    data = jnp.clip(offset, -LIMIT, LIMIT)
    yield

    def pull(grads):
        terms = data * grads
        return sum(terms[k * size : (k + 1) * size] for k in range(bands))

    def tall(x):
        return jnp.concatenate([x] * bands, axis=0)

    flow = [-mask * pull(grad_rows), -mask * pull(grad_cols)]
    extrapolated = [2.0 * x for x in flow]
    dual_rows = [0.0, 0.0]
    dual_cols = [0.0, 0.0]
    yield
    for step in range(1, STEPS):
        changes = [(along_rows(x), along_cols(x)) for x in extrapolated]
        yield
        data = data + offset + grad_rows * tall(extrapolated[0]) + grad_cols * tall(extrapolated[1])
        data = jnp.clip(data, -LIMIT, LIMIT)
        yield
        for c in range(2):
            rows = dual_rows[c] + changes[c][0]
            cols = dual_cols[c] + changes[c][1]
            scale = jnp.minimum(mask, (8.0 * ALPHA) * lax.rsqrt(rows * rows + cols * cols))
            dual_rows[c] = rows * scale
            dual_cols[c] = cols * scale
        yield
        divergences = [along_rows(dual_rows[c]) + along_cols(dual_cols[c]) for c in range(2)]
        yield
        pulls = [pull(grad_rows), pull(grad_cols)]
        yield
        for c in range(2):
            following = flow[c] + mask * ((1.0 / 64.0) * divergences[c] - pulls[c])
            extrapolated[c] = 2.0 * following - flow[c]
            flow[c] = following
        yield
    return flow


def columns_of_planes(planes):
    whole = lax.broadcasted_iota(jnp.int32, (LANES, COLUMNS), 1)
    lane = lax.broadcasted_iota(jnp.int32, (LANES, LANES), 1)
    strip = jnp.where(lane < S_MID, lane, jnp.where(lane < S_LEFT, lane + (COLUMNS - S_RIGHT), lane - LANES))
    return jnp.concatenate([x for x, wanted in ((whole, "whole"), (strip, "strip")) if wanted in planes], axis=1)


def upsample(flow, planes, target):
    column = columns_of_planes(planes)
    source = lax.broadcasted_iota(jnp.int32, column.shape, 0)
    spread = jnp.where(source - LEAD == lax.shift_right_arithmetic(column, 3), float(FACTOR), 0.0).astype(jnp.bfloat16)
    rows = flow[0].shape[0]
    wide = split_dot(UNIT * jnp.concatenate(flow, axis=0), spread)
    for c in range(2):
        for tile in range(column.shape[1] // LANES):
            target[c, tile] = wide[c * rows : (c + 1) * rows, tile * LANES : (tile + 1) * LANES]


def repeat_rows(spread, initial, cells):
    for c in range(2):
        for tile in range(initial.shape[1]):
            rows = [jnp.broadcast_to(spread[c, tile, cell : cell + 1, :], (SUB, LANES)) for cell in cells]
            initial[c, tile, GUARD : GUARD + SUB * len(cells), :] = jnp.concatenate(rows, axis=0)


def shift_whole(here, shift):
    turned = [turn_back(x, shift) for x in here]
    lane = lanes_like(here[0])
    return [
        jnp.where(lane + shift >= LANES, turned[1], turned[0]),
        jnp.where(lane + shift < 0, turned[0], turned[1]),
    ]


def edge_lanes(rows):
    lane = lanes_of(rows)
    return lane == LANES - 1, lane == 0


def columns_whole(fields, edges):
    rows = fields[0].shape[0]
    if rows not in edges:
        edges[rows] = edge_lanes(rows)
    last, first = edges[rows]
    ahead = [pltpu.roll(x, LANES - 1, 1) for x in fields]
    behind = [pltpu.roll(x, 1, 1) for x in fields]
    return [
        jnp.where(last, ahead[1], ahead[0]) - behind[0],
        ahead[1] - jnp.where(first, behind[0], behind[1]),
    ]


def rows_within(tall):
    size = tall.shape[0]
    return (pltpu.roll(tall, size - 1, 0) - pltpu.roll(tall, 1, 0))[SUB : size - SUB]


def columns_strip(field):
    return pltpu.roll(field, LANES - 1, 1) - pltpu.roll(field, 1, 1)


def strip_windows(window, centre, right, left):
    own = turn_back(window(centre[0]), centre[1])
    beyond_left = turn_back(window(left[0]), left[1])
    beyond_right = turn_back(window(right[0]), right[1])
    lane = lanes_like(own)
    beyond = jnp.where((lane >= S_LEFT) | (lane < S_MID), beyond_left, beyond_right)
    is_beyond = lane >= S_RIGHT
    of_next = is_beyond & (lane != S_RIGHT) | (lane == 0)
    of_previous = is_beyond & (lane != LANES - 1) | (lane == S_RIGHT - 1)
    change = turn(jnp.where(of_next, beyond, own), -1) - turn(jnp.where(of_previous, beyond, own), 1)
    return jnp.where(is_beyond, beyond, own), change


def fine_steps(
    rows_total, chunk, columns, initial, extrap, dual_rows, dual_cols, change, dual_data,
    offsets, grads_rows, grads_cols, data_row, masks_of, result, kept, done=lambda k: None,
):
    assert STEPS == 3
    planes = len(offsets)
    bands = offsets[0].shape[0]
    chunks = rows_total // chunk

    def places(k, trim=(0, 0)):
        start, size = k * chunk + trim[0], chunk - sum(trim)
        return pl.ds(GUARD + start, size), pl.ds(start, size), pl.ds(data_row(k) + trim[0], size)

    def row_change(ref, c, tile, at):
        return ref[c, tile, pl.ds(at.start + 1, at.size), :] - ref[c, tile, pl.ds(at.start - 1, at.size), :]

    def clip(x):
        return jnp.clip(x, -UNIT * LIMIT, UNIT * LIMIT)

    tiles = range(planes)

    for step in range(STEPS):
        source = initial if step == 0 else extrap
        final = step == STEPS - 1

        def dual(item, source=source, step=step):
            k, c = item
            at, own, _ = places(k)
            masks = masks_of(own)
            along = columns([source[c, tile, at, :] for tile in tiles])
            values = []
            for tile in tiles:
                rows = row_change(source, c, tile, at)
                cols = along[tile]
                if step > 0:
                    rows = rows + dual_rows[c, tile, at, :]
                    cols = cols + dual_cols[c, tile, own, :]
                scale = jnp.minimum(masks[tile], lax.rsqrt(rows * rows + cols * cols))
                values.append((rows * scale, cols * scale))
            return values

        def store_dual(item, values):
            k, c = item
            for tile, (rows, cols) in enumerate(values):
                dual_rows[c, tile, places(k)[0], :] = rows
                dual_cols[c, tile, places(k)[1], :] = cols

        staggered([(k, c) for k in range(chunks) for c in range(2)], dual, store_dual, 1)
        along_of = {}

        def primal(item, step=step, final=final, along_of=along_of):
            k, tile = item
            at, own, data = places(k, kept(k) if final else (0, 0))
            if k not in along_of:
                along_of[k] = [columns([dual_cols[c, t, own, :] for t in tiles]) for c in range(2)]
            mask = masks_of(own)[tile]
            start = [initial[c, tile, at, :] for c in range(2)]
            if step > 0:
                moved = [extrap[c, tile, at, :] - start[c] for c in range(2)]
            if step == 1:
                changes = [0.5 * x for x in moved]
            if step == 2:
                changes = [change[c, tile, own, :] for c in range(2)]
            pulls = [None, None]
            duals = []
            for band in range(bands):
                gradient = (grads_rows[tile][band, data, :], grads_cols[tile][band, data, :])
                value = offsets[tile][band, data, :]
                if step > 0:
                    earlier = clip(value) if step == 1 else dual_data[band, tile, own, :]
                    value = (value + earlier) + (gradient[0] * moved[0] + gradient[1] * moved[1])
                value = clip(value)
                duals.append(value)
                for c in range(2):
                    term = value * gradient[c]
                    pulls[c] = term if pulls[c] is None else pulls[c] + term
            flows, nexts = [], []
            for c in range(2):
                divergence = row_change(dual_rows, c, tile, at) + along_of[k][c][tile]
                moving = (mask * (1.0 / 64.0)) * divergence - pulls[c]
                total = moving if step == 0 else changes[c] + moving
                flows.append((start[c] + total) * (1.0 / UNIT) if final else total)
                nexts.append(None if final else start[c] + (total + moving))
            return flows, nexts, duals

        def store_primal(item, results, step=step, final=final):
            k, tile = item
            flows, nexts, duals = results
            at, own, _ = places(k, kept(k) if final else (0, 0))
            for c in range(2):
                if final:
                    result[c, tile, own, :] = flows[c]
                else:
                    if step > 0:
                        change[c, tile, own, :] = flows[c]
                    extrap[c, tile, at, :] = nexts[c]
            if final:
                if tile == planes - 1:
                    done(k)
            elif step > 0:
                for band in range(bands):
                    dual_data[band, tile, own, :] = duals[band]

        staggered([(k, tile) for k in range(chunks) for tile in tiles], primal, store_primal, 1)


def clear_guards(*refs):
    for ref in refs:
        rows = ref.shape[2]
        zero = jnp.zeros((GUARD, LANES), jnp.float32)
        for c in range(2):
            for tile in range(ref.shape[1]):
                ref[c, tile, 0:GUARD, :] = zero
                ref[c, tile, rows - GUARD : rows, :] = zero


def fine_scratch(bands, planes, rows):
    guarded = pltpu.VMEM((2, planes, rows + 2 * GUARD, LANES), jnp.float32)
    plain = pltpu.VMEM((2, planes, rows, LANES), jnp.float32)
    return [guarded, guarded, guarded, plain, plain, pltpu.VMEM((bands, planes, rows, LANES), jnp.float32)]


def pieces(bands, height, rows):
    assert (height - 2 * SUB) % rows == 0
    return [(band, row) for row in range(SUB, height - SUB, rows) for band in range(bands)]


def whole_terms_kernel(
    second_0, second_1, first_0, first_1, coarse, own_meta,
    offset, grad_rows, grad_cols, initial, strip_e, strip_f, up, down, moved, spread, numbers, sem,
):
    seconds, firsts = (second_0, second_1), (first_0, first_1)
    bands, height, _ = second_0.shape
    block = 120
    coarse_height = coarse.shape[0] // (2 * bands)
    get_numbers = pltpu.make_async_copy(own_meta, numbers, sem)
    get_numbers.start()
    def windows(band, row, rows):
        here = [ref[band, pl.ds(row + centre[0], rows), :].reshape(-1, LANES) for ref in seconds]
        return shift_whole(here, centre[1])

    woven = Woven(coarse_flow_of(coarse[0 : bands * coarse_height, :], coarse[bands * coarse_height :, :], 1.0))

    def strips_of(item):
        band, row = item
        rows = slice(row, row + LANES)
        return strip_own([ref[band, rows, :] for ref in seconds]), strip_own([ref[band, rows, :] for ref in firsts])

    def store_strips(item, results):
        band, row = item
        strip_e[band, row : row + LANES, :], strip_f[band, row : row + LANES, :] = results

    staggered([(band, row) for band in range(bands) for row in range(0, height, LANES)], strips_of, store_strips, 1, woven)

    get_numbers.wait()
    centre = shift_at(numbers, 0, 0)

    ends = [(row, windows(slice(None), row, SUB)) for row in (SUB // 2, height - SUB - SUB // 2)]
    for row, values in ends:
        for tile in range(2):
            moved[tile, :, row : row + SUB, :] = values[tile].reshape(bands, SUB, LANES)

    edges = {}

    def values_of(item):
        band, row = item
        values = windows(band, row, block)
        along = columns_whole(values, edges)
        own = [ref[band, row : row + block, :] for ref in firsts]
        return values, [(0.25 * UNIT) * (x - y) for x, y in zip(values, own)], [0.125 * x for x in along]

    def store_values(item, results):
        band, row = item
        values, offsets, gradients = results
        data = slice(row + HALO, row + HALO + block)
        for tile in range(2):
            moved[tile, band, row : row + block, :] = values[tile]
            offset[tile, band, data, :] = offsets[tile]
            grad_cols[tile, band, data, :] = gradients[tile]

    staggered(pieces(bands, height, block), values_of, store_values, 1, woven)

    def gradient_of(item):
        band, row = item
        return [0.125 * rows_within(moved[tile, band, row - SUB : row + 120 + SUB, :]) for tile in range(2)]

    def store_gradient(item, results):
        band, row = item
        for tile in range(2):
            grad_rows[tile, band, row + HALO : row + HALO + 120, :] = results[tile]

    staggered(pieces(bands, height, 120), gradient_of, store_gradient, 1, woven)

    parts = []
    for band in range(bands):
        for second, first in zip(seconds, firsts):
            parts.append((
                second[band, 0:16, :], first[band, 0:8, :],
                second[band, height - 16 : height, :], first[band, height - 8 : height, :],
            ))
    for k, (second_top, first_top, second_end, first_end) in enumerate(parts):
        up[E8 + 8 * k : E8 + 8 * k + 8, :] = second_top[0:8]
        up[E1 + k : E1 + k + 1, :] = second_top[8:9]
        up[F4 + 4 * k : F4 + 4 * k + 4, :] = first_top[0:4]
        down[E8 + 8 * k : E8 + 8 * k + 8, :] = second_end[8:16]
        down[E1 + k : E1 + k + 1, :] = second_end[7:8]
        down[F4 + 4 * k : F4 + 4 * k + 4, :] = first_end[4:8]
    for target in (up, down):
        for start, end in ((H8, E1), (H1, F4), (CS, ROW_MESSAGE)):
            target[start:end, :] = jnp.zeros((end - start, LANES), jnp.float32)

    upsample(woven.finish(), ("whole",), spread)
    clear_guards(initial)
    rows_total = initial.shape[2] - 2 * GUARD
    repeat_rows(spread, initial, [BEGIN // FACTOR + k for k in range(rows_total // SUB)])


def whole_steps_kernel(
    initial, offset, grad_rows, grad_cols, result, extrap, dual_rows, dual_cols, change, dual_data
):
    rows_total = result.shape[2]
    clear_guards(extrap, dual_rows)
    chunk = 88
    edges = {}
    fine_steps(
        rows_total, chunk, lambda fields: columns_whole(fields, edges),
        initial, extrap, dual_rows, dual_cols, change, dual_data,
        *[[ref.at[tile] for tile in range(2)] for ref in (offset, grad_rows, grad_cols)],
        lambda k: HALO + BEGIN + k * chunk, lambda own: (1.0, 1.0), result, lambda k: (SUB * (k == 0), SUB * (k == 1)),
    )


def strip_kernel(
    count, strip_e, strip_f, from_left, from_right, wide, own_message, whole,
    middle, strip_out, first_ends, offset, grad_rows, grad_cols,
    moved, result, spread, numbers, sem, initial, extrap, dual_rows, dual_cols, change, dual_data,
):
    bands, height, _ = strip_e.shape
    block = 120
    coarse_height = height // FACTOR
    coarse_width = COLUMNS // FACTOR
    rows_total = height - 2 * BEGIN
    lane = lanes_of()
    get_numbers = pltpu.make_async_copy(own_message.at[pl.ds(H1, SUB), :], numbers, sem)
    get_numbers.start()
    has_left, has_right = neighbours("col", count)
    exists = jnp.where(lane < S_RIGHT, 1.0, jnp.where(lane < S_LEFT, has_right, has_left))

    def tall_factor(rows):
        return 0.125 * jnp.concatenate([exists] * (rows // SUB), axis=0)

    mask = jnp.where(lane < LEAD, has_left, jnp.where(lane < LEAD + coarse_width, 1.0, has_right))
    mask = jnp.concatenate([mask] * (coarse_height // SUB), axis=0)
    cells = [wide[k * bands : (k + 1) * bands].reshape(bands * coarse_height, LANES) for k in range(2)]
    woven = Woven(coarse_flow_of(*cells, mask))

    def halves(row, rows):
        half = row // (height // 2)
        start = row - half * (height // 2)
        return half, slice(start, start + rows)

    def second_of(item):
        band, row = item
        half, message = halves(row, LANES)
        return strip_second(strip_e[band, row : row + LANES, :], from_left, from_right, message, half, band)

    def store_second(item, value):
        band, row = item
        strip_out[band, row : row + LANES, :] = value

    staggered([(band, row) for row in range(0, height, LANES) for band in range(bands)], second_of, store_second, 1, woven)

    def first_of(band, row, rows):
        half, message = halves(row, rows)
        return strip_first(strip_f[band, row : row + rows, :], from_left, from_right, message, half, band)

    firsts = [(end, band, first_of(band, (0, height - SUB)[end], SUB)) for end in range(2) for band in range(bands)]
    for end, band, value in firsts:
        first_ends[end, band] = value

    get_numbers.wait()
    centre, right, left = shifts_of(numbers)

    def windows(band, row, rows):
        return strip_windows(
            lambda shift: strip_out[band, pl.ds(row + shift, rows), :].reshape(-1, LANES), centre, right, left
        )

    ends = [(row, windows(slice(None), row, SUB)[0]) for row in (SUB // 2, height - SUB - SUB // 2)]
    for row, value in ends:
        moved[:, row : row + SUB, :] = value.reshape(bands, SUB, LANES)

    factor = tall_factor(block)

    def values_of(item):
        band, row = item
        value, along = windows(band, row, block)
        return value, (0.25 * UNIT) * (value - first_of(band, row, block)), factor * along

    def store_values(item, results):
        band, row = item
        data = slice(row + HALO, row + HALO + block)
        moved[band, row : row + block, :], offset[band, data, :], grad_cols[band, data, :] = results

    staggered(pieces(bands, height, block), values_of, store_values, 1, woven)

    def gradient_of(item):
        band, row = item
        return factor * rows_within(moved[band, row - SUB : row + block + SUB, :])

    def store_gradient(item, value):
        band, row = item
        grad_rows[band, row + HALO : row + HALO + block, :] = value

    staggered(pieces(bands, height, block), gradient_of, store_gradient, 1, woven)

    upsample(woven.finish(), ("strip",), spread)
    clear_guards(initial, extrap, dual_rows)
    repeat_rows(spread, initial, [BEGIN // FACTOR + k for k in range(rows_total // SUB)])

    chunk = 176
    masks = jnp.concatenate([exists] * (chunk // SUB), axis=0)
    fine_steps(
        rows_total, chunk, lambda fields: [columns_strip(fields[0])],
        initial, extrap, dual_rows, dual_cols, change, dual_data, [offset], [grad_rows], [grad_cols],
        lambda k: HALO + BEGIN + k * chunk, lambda own: (masks[: own.size],), result, lambda k: (SUB, SUB),
    )
    join(whole, result.at[:, 0], middle, slice(SUB, rows_total - SUB))


def join(whole, strip, target, rows):
    lane = lanes_of(rows.stop - rows.start)
    values = []
    for c in range(2):
        edge = strip[c, rows, :]
        start = jnp.where(lane < EDGE, edge, whole[c, 0, rows, :])
        values.append((start, jnp.where(lane >= LANES - EDGE, turn(edge, S_TURN), whole[c, 1, rows, :])))
    for c in range(2):
        target[c, rows, 0:LANES], target[c, rows, LANES:COLUMNS] = values[c]


def outer_kernel(
    counts, second_0, second_1, first_0, first_1, strip_e, first_ends, wide, got_1, got_0, middle, own_message,
    _wo, _wr, _wc, _so, _sr, _sc,
    flow_out, coarse_out, whole_offset, whole_rows, whole_cols, strip_offset, strip_rows, strip_cols,
    from_up, from_down, extended, tall, spread, masks, result, joined, coarse_result, numbers, sems,
    initial, extrap, dual_rows, dual_cols, change, dual_data,
):
    bands, height, _ = second_0.shape
    coarse_height = height // FACTOR
    coarse_width = COLUMNS // FACTOR
    rows_total = 2 * EACH
    lane = lanes_of()

    put_middle = pltpu.make_async_copy(
        middle.at[:, pl.ds(MARGIN - BEGIN, height - 2 * MARGIN), :],
        flow_out.at[:, pl.ds(MARGIN, height - 2 * MARGIN), :],
        sems.at[0],
    )
    put_middle.start()
    get_numbers = [
        pltpu.make_async_copy(message.at[pl.ds(H1, SUB), :], numbers.at[k], sems.at[4 + k])
        for k, message in enumerate((own_message, got_0, got_1))
    ]
    for get in get_numbers:
        get.start()

    other = without_ends(got_1, "row", counts[0])
    even = is_even("row", got_0)
    from_down[...] = jnp.where(even, got_0[...], other)
    from_up[...] = jnp.where(even, other, got_0[...])

    has_up, has_down = neighbours("row", counts[0])
    has_left, has_right = neighbours("col", counts[1])
    exists = jnp.where(lane < S_RIGHT, 1.0, jnp.where(lane < S_LEFT, has_right, has_left))

    zero = jnp.zeros((SUB, LANES), jnp.float32)
    tall_rows = coarse_height + 2 * LEAD
    parts = []
    fill = jnp.zeros((LEAD - C_SECOND, LANES), jnp.float32)
    for plane in range(2 * bands):
        at = CS + C_SECOND * (plane % bands)
        ends = [turn(message[at : at + C_SECOND, :], HALF * (plane // bands)) for message in (from_up, from_down)]
        parts.append([fill, ends[0], wide[plane], ends[1], fill])
    for plane, values in enumerate(parts):
        tall[plane] = jnp.concatenate(values, axis=0)
    across = jnp.where(lane < LEAD, has_left, jnp.where(lane < LEAD + coarse_width, 1.0, has_right))
    mask = jnp.concatenate([across * has_up] + [across] * (coarse_height // SUB) + [across * has_down], axis=0)
    for end in range(2):
        message = (from_up, from_down)[end]
        beside = message[H8 : H8 + 8, :]
        beside_one = jnp.broadcast_to(message[H1 : H1 + 1, :], (SUB, LANES))
        parts = []
        for band in range(bands):
            eights = [message[E8 + 8 * k : E8 + 8 * k + 8, :] for k in (2 * band, 2 * band + 1)]
            ones = [jnp.broadcast_to(message[E1 + k : E1 + k + 1, :], (SUB, LANES)) for k in (2 * band, 2 * band + 1)]
            eights.append(strip_halo(strip_own(eights), beside, band, 0, REACH))
            ones.append(strip_halo(strip_own(ones), beside_one, band, 0, REACH))
            for tile, (eight, one) in enumerate(zip(eights, ones)):
                source = (second_0, second_1, strip_e)[tile]
                if end == 0:
                    parts.append((tile, band, [one, eight, source[band, 0:24, :]]))
                else:
                    parts.append((tile, band, [source[band, height - 24 : height, :], eight, one]))
        for tile, band, values in parts:
            extended[end, tile, band] = jnp.concatenate(values, axis=0)
    cells = [tall[k * bands : (k + 1) * bands].reshape(bands * tall_rows, LANES) for k in range(2)]
    woven = Woven(coarse_flow_of(*cells, mask))
    edges = {}
    rows_data = whole_offset.shape[2]
    exists_tall = jnp.concatenate([exists] * bands, axis=0)

    for get in get_numbers:
        get.wait()
    own, one, other = [shifts_of(numbers.at[k]) for k in range(3)]
    odd = lax.axis_index("row") % 2

    def of_row(for_even, for_odd):
        return [tuple(jnp.where(odd == 0, x, y) for x, y in zip(*pair)) for pair in zip(for_even, for_odd)]

    above, below = of_row(other, one), of_row(one, other)

    def rows_of(halo, end):
        if halo:
            return slice(0, SUB) if end == 0 else slice(rows_data - SUB, rows_data)
        return slice(HALO, HALO + SUB) if end == 0 else slice(rows_data - HALO - SUB, rows_data - HALO)

    def values_of(item):
        halo, end = item
        message = (from_up, from_down)[end]
        base = (SUB, 3 * SUB)[end] if halo else 2 * SUB
        shifts = (above, below)[end] if halo else own
        factor = 0.125 * (has_up, has_down)[end] if halo else 0.125

        def here(tile, shift):
            return extended[end, tile, :, pl.ds(base + shift, SUB), :].reshape(-1, LANES)

        def down_up(tile, shift):
            return here(tile, shift + 1) - here(tile, shift - 1)

        own_rows = slice(0, SUB) if end == 0 else slice(height - SUB, height)
        if halo:
            firsts = [[], [], []]
            for band in range(bands):
                eights = []
                for k in (2 * band, 2 * band + 1):
                    four = message[F4 + 4 * k : F4 + 4 * k + 4, :]
                    eights.append(jnp.concatenate([four, four], axis=0))
                eights.append(strip_halo(strip_own(eights), message[H8 : H8 + 8, :], band, REACH, DEPTH))
                for tile in range(3):
                    firsts[tile].append(eights[tile])
            firsts = [jnp.concatenate(x, axis=0) for x in firsts]
        else:
            firsts = [x.reshape(-1, LANES) for x in (first_0[:, own_rows, :], first_1[:, own_rows, :], first_ends[end])]
        centre = shifts[0]
        values = shift_whole([here(tile, centre[0]) for tile in range(2)], centre[1])
        changes = shift_whole([down_up(tile, centre[0]) for tile in range(2)], centre[1])
        along = columns_whole(values, edges)
        value, across_cols = strip_windows(lambda shift: here(2, shift), *shifts)
        change_rows, _ = strip_windows(lambda shift: down_up(2, shift), *shifts)
        return (
            [(0.25 * UNIT) * (x - y) for x, y in zip([*values, value], firsts)],
            [*[factor * x for x in changes], (factor * exists_tall) * change_rows],
            [*[factor * x for x in along], (factor * exists_tall) * across_cols],
        )

    def store_values(item, results):
        rows = rows_of(*item)
        for values, whole, strip in zip(
            results, (whole_offset, whole_rows, whole_cols), (strip_offset, strip_rows, strip_cols)
        ):
            values = [x.reshape(bands, SUB, LANES) for x in values]
            for tile in range(2):
                whole[tile, :, rows, :] = values[tile]
            strip[:, rows, :] = values[2]

    staggered([(halo, end) for halo in (True, False) for end in range(2)], values_of, store_values, 1, woven)

    flow = woven.finish()
    for c in range(2):
        coarse_result[c] = turn(flow[c][LEAD : LEAD + coarse_height], -LEAD)[:, :coarse_width]
    put_coarse = pltpu.make_async_copy(coarse_result, coarse_out, sems.at[1])
    put_coarse.start()
    upsample(flow, ("whole", "strip"), spread)
    clear_guards(initial, extrap, dual_rows)
    each = EACH // SUB
    repeat_rows(
        spread, initial,
        [LEAD - 1 + k for k in range(each)] + [tall_rows - LEAD + 1 - each + k for k in range(each)],
    )

    for i, value in enumerate((jnp.ones((SUB, LANES), jnp.float32), exists)):
        masks[i] = jnp.concatenate([value * has_up] + [value] * (rows_total // SUB - 2) + [value * has_down], axis=0)

    def masks_of(rows):
        whole = masks[0, rows, :]
        return (whole, whole, masks[1, rows, :])

    chunk = EACH
    edges = {}
    puts = [
        pltpu.make_async_copy(
            joined.at[:, pl.ds(k * EACH + SUB, MARGIN), :],
            flow_out.at[:, pl.ds(k * (height - MARGIN), MARGIN), :],
            sems.at[2 + k],
        )
        for k in range(2)
    ]

    def finish(k):
        join(result, result.at[:, 2], joined, slice(k * EACH + SUB, k * EACH + SUB + MARGIN))
        puts[k].start()

    def data_row(k):
        return k * (rows_data - EACH)

    fine_steps(
        rows_total, chunk, lambda fields: columns_whole(fields[:2], edges) + [columns_strip(fields[2])],
        initial, extrap, dual_rows, dual_cols, change, dual_data,
        [whole_offset.at[0], whole_offset.at[1], strip_offset],
        [whole_rows.at[0], whole_rows.at[1], strip_rows],
        [whole_cols.at[0], whole_cols.at[1], strip_cols],
        data_row, masks_of, result, lambda k: (SUB, SUB), finish,
    )
    put_middle.wait()
    put_coarse.wait()
    for put in puts:
        put.wait()


def swap_with(message, axis, start):
    names = ("row", "col")
    sizes = [lax.axis_size(name) for name in names]
    along = names.index(axis)
    count, others = sizes[along], sizes[1 - along]

    def number(place, other):
        row, col = (place, other) if along == 0 else (other, place)
        return row * sizes[1] + col

    pairs = [(number(i, k), number(i + 1, k)) for i in range(start, count - 1, 2) for k in range(others)]
    if start and axis == "col":
        pairs += [(number(i, k), number(i, k + 1)) for i in (0, count - 1) for k in range(0, others, 2)]
    elif start:
        pairs += [(number(0, k), number(count - 1, k)) for k in range(others)]
    return lax.ppermute(message, names, pairs + [(j, i) for i, j in pairs])


def local(frame_first, frame_second, shifts):
    bands, height, width = frame_first.shape
    assert bands == 4 and width == COLUMNS and height % LANES == 0
    assert lax.axis_size("row") % 2 == 0 and lax.axis_size("col") % 2 == 0
    coarse_height = height // FACTOR
    coarse_width = width // FACTOR
    vmem = pl.BlockSpec(memory_space=pltpu.VMEM)
    hbm = pl.BlockSpec(memory_space=pltpu.HBM)
    tall_rows = coarse_height + 2 * LEAD
    inner_rows = height - 2 * BEGIN

    def shape(*sizes):
        return jax.ShapeDtypeStruct(sizes, jnp.float32)

    def scratch(*sizes):
        return pltpu.VMEM(sizes, jnp.float32)

    def call(kernel, name, arguments, outs, scratches=(), flops=1_000_000, **more):
        more = {"in_specs": [vmem] * len(arguments), "out_specs": (vmem,) * len(outs), **more}
        return pl.pallas_call(
            kernel,
            out_shape=tuple(outs),
            scratch_shapes=list(scratches),
            compiler_params=pltpu.CompilerParams(vmem_limit_bytes=24 * 1024 * 1024),
            cost_estimate=pl.CostEstimate(flops=flops, bytes_accessed=1_000_000, transcendentals=0),
            name=name,
            **more,
        )(*arguments)

    plane = shape(bands, height, LANES)
    column_message = shape(height // 2, LANES)
    row_message = shape(ROW_MESSAGE, LANES)
    whole_data = shape(2, bands, height + 2 * HALO, LANES)
    strip_data = shape(bands, height + 2 * HALO, LANES)

    *frames, coarse, swap_0, swap_1, own_meta = call(
        first_kernel,
        "means_and_message",
        [pltpu.with_memory_space_constraint(x, pltpu.HBM) for x in (frame_second, frame_first, shifts)],
        [*[plane] * 4, shape(2 * bands * coarse_height, LANES), column_message, column_message, shape(SUB, LANES)],
        [
            pltpu.SMEM((1, 1, 2), jnp.int32),
            pltpu.SemaphoreType.DMA((2, bands, 2)),
            pltpu.SemaphoreType.DMA,
        ],
        in_specs=[hbm] * 3,
    )
    got_0 = swap_with(swap_0, "col", 0)
    got_1 = swap_with(swap_1, "col", 1)

    *whole_terms, initial, strip_e, strip_f, up_part, down_part = call(
        whole_terms_kernel,
        "whole_terms",
        [*frames, coarse, own_meta],
        [
            *[whole_data] * 3, shape(2, 2, inner_rows + 2 * GUARD, LANES),
            plane, plane, row_message, row_message,
        ],
        [
            scratch(2, bands, height, LANES), scratch(2, 2, coarse_height, LANES),
            pltpu.SMEM((SUB, LANES), jnp.float32), pltpu.SemaphoreType.DMA,
        ],
        flops=8_000_000,
    )
    (whole,) = call(
        whole_steps_kernel,
        "whole_steps",
        [initial, *whole_terms],
        [shape(2, 2, inner_rows, LANES)],
        fine_scratch(bands, 2, inner_rows)[1:],
        flops=20_000_000,
    )

    swap_0, swap_1, from_left, from_right, wide = call(
        functools.partial(message_kernel, lax.axis_size("col")),
        "row_messages",
        [coarse, own_meta, got_0, got_1, up_part, down_part, whole],
        [row_message, row_message, column_message, column_message, shape(2 * bands, coarse_height, LANES)],
    )
    got_1 = swap_with(swap_1, "row", 1)
    got_0 = swap_with(swap_0, "row", 0)

    middle, strip_e, first_ends, *strip_terms = call(
        functools.partial(strip_kernel, lax.axis_size("col")),
        "strip",
        [strip_e, strip_f, from_left, from_right, wide, swap_0, whole],
        [shape(2, inner_rows, width), plane, shape(2, bands, SUB, LANES), *[strip_data] * 3],
        [
            scratch(bands, height, LANES),
            scratch(2, 1, inner_rows, LANES),
            scratch(2, 1, coarse_height, LANES),
            pltpu.SMEM((SUB, LANES), jnp.float32),
            pltpu.SemaphoreType.DMA,
            *fine_scratch(bands, 1, inner_rows),
        ],
        flops=16_000_000,
    )

    flow, coarse_flow, *_ = call(
        functools.partial(outer_kernel, (lax.axis_size("row"), lax.axis_size("col"))),
        "outer_rows",
        [
            *frames, strip_e, first_ends, wide, got_1, got_0, middle, swap_0,
            *whole_terms, *strip_terms,
        ],
        [shape(2, height, width), shape(2, coarse_height, coarse_width), *[whole_data] * 3, *[strip_data] * 3],
        [
            scratch(ROW_MESSAGE, LANES),
            scratch(ROW_MESSAGE, LANES),
            scratch(2, 3, bands, 40, LANES),
            scratch(2 * bands, tall_rows, LANES),
            scratch(2, 3, tall_rows, LANES),
            scratch(2, 2 * EACH, LANES),
            scratch(2, 3, 2 * EACH, LANES),
            scratch(2, 2 * EACH, width),
            scratch(2, coarse_height, coarse_width),
            pltpu.SMEM((3, SUB, LANES), jnp.float32),
            pltpu.SemaphoreType.DMA((7,)),
            *fine_scratch(bands, 3, 2 * EACH),
        ],
        out_specs=(hbm, hbm) + (vmem,) * 6,
        input_output_aliases={11 + k: 2 + k for k in range(6)},
    )
    return (flow, coarse_flow)


def solution(mesh):
    return jax.shard_map(
        local,
        mesh=mesh,
        in_specs=(P(None, "row", "col"), P(None, "row", "col"), P("row", "col", None)),
        out_specs=(P(None, "row", "col"), P(None, "row", "col")),
        check_vma=False,
    )
```

```python
import functools

import jax
import jax.numpy as jnp
from jax import lax
from jax.experimental import pallas as pl
from jax.experimental.pallas import tpu as pltpu
from jax.sharding import PartitionSpec as P

FACTOR = 8
MAXD = 4
BANDS = 4
STEPS = 3
LANES = 128
COLUMNS = 2 * LANES
HALF = 64
SUB = 8
DEPTH = 4
REACH = DEPTH + MAXD + 1
SLOT = 16
C_SECOND = 6
C_FIRST = 5
LEAD = 8
MARGIN = 48
EDGE = 46
GUARD = 8
HALO = 8
BEGIN = 40
EACH = MARGIN + 16
LIMIT = 0.3
ALPHA = 0.3
UNIT = 0.125 / ALPHA

S_MID = 55
S_RIGHT = 110
S_LEFT = LANES - REACH
S_TURN = COLUMNS - S_RIGHT - LANES

E8 = 0
H8 = 64
E1 = 72
H1 = 80
META = 81
F4 = 88
CS = 120
ROW_MESSAGE = 144
H_BAND = 32

COARSE_A = REACH + DEPTH
COARSE_B = SLOT + REACH + DEPTH
SHIFT_R = 2 * SLOT + REACH + DEPTH
SHIFT_C = SHIFT_R + 1
EXISTS = SHIFT_R + 2


def lanes_of(rows=SUB):
    return lax.broadcasted_iota(jnp.int32, (rows, LANES), 1)


def lanes_like(x):
    return lax.broadcasted_iota(jnp.int32, x.shape, 1)


def turn(x, amount):
    amount = amount % LANES
    return x if amount == 0 else pltpu.roll(x, amount, 1)


def turn_back(x, shift):
    return pltpu.roll(x, lax.rem(LANES - shift, LANES), 1)


def split_dot(x, exact):
    high = x.astype(jnp.bfloat16)
    rest = x - high.astype(jnp.float32)
    middle = rest.astype(jnp.bfloat16)
    low = (rest - middle.astype(jnp.float32)).astype(jnp.bfloat16)
    parts = [jnp.dot(part, exact, preferred_element_type=jnp.float32) for part in (low, middle, high)]
    return parts[0] + parts[1] + parts[2]


def neighbours(axis, count):
    place = lax.axis_index(axis)
    return jnp.where(place > 0, 1.0, 0.0), jnp.where(place < count - 1, 1.0, 0.0)


def shift_at(ref, row, lane):
    numbers = ref[row : row + 1, :].astype(jnp.int32)
    return numbers[0, lane], numbers[0, lane + SLOT]


def shifts_of(message):
    return [shift_at(message, META, lane) for lane in (0, 80, 48)]


def is_even(axis, like):
    return jnp.broadcast_to(lax.axis_index(axis) % 2, like.shape) == 0


def without_ends(message, axis, count):
    place = jnp.broadcast_to(lax.axis_index(axis), message.shape)
    return jnp.where((place > 0) & (place < count - 1), message[...], 0.0)


def staggered(items, compute, store, depth, woven=None):
    pending = []
    for item in items:
        pending.append((item, compute(item)))
        if woven is not None:
            woven.advance()
        if len(pending) > depth:
            store(*pending.pop(0))
    for entry in pending:
        store(*entry)


class Woven:
    def __init__(self, stages):
        self.stages = stages
        self.result = None

    def advance(self):
        try:
            next(self.stages)
            return True
        except StopIteration as end:
            self.result = end.value if self.result is None else self.result
            return False

    def finish(self):
        while self.advance():
            pass
        return self.result


def pack_image(packed, to_right, planes, some, count, offset):
    _, height, _ = planes[0].shape
    plane = planes[int(to_right)]
    start = LANES - count if to_right else 0
    length = height // 2
    lane = lanes_of(length)
    for half in range(2):
        for band in some:
            at = half * HALF + band * SLOT + offset
            cells = turn(plane[band, half * length : (half + 1) * length, :], at - start)
            packed = cells if packed is None else jnp.where((lane >= at) & (lane < at + count), cells, packed)
    return packed


def pack_means(packed, to_right, means):
    length = packed.shape[0]
    start = LEAD + COLUMNS // FACTOR - C_SECOND if to_right else LEAD
    lane = lanes_of(length)
    for half in range(2):
        cells = means[half * length : (half + 1) * length]
        for at, first in ((half * HALF + COARSE_A, start), (half * HALF + COARSE_B, start + 3)):
            packed = jnp.where((lane >= at) & (lane < at + 3), turn(cells, at - first), packed)
    return packed


def strip_second(base, from_left, from_right, rows, half, band):
    at = half * HALF + band * SLOT
    lane = lanes_like(base)
    cells = jnp.where(lane >= S_RIGHT, turn(from_right[rows, :], S_RIGHT - at), base)
    return jnp.where(lane >= S_LEFT, turn(from_left[rows, :], S_LEFT - at), cells)


def strip_first(base, from_left, from_right, rows, half, band):
    at = half * HALF + band * SLOT + REACH
    lane = lanes_like(base)
    cells = jnp.where(lane >= S_RIGHT, turn(from_right[rows, :], S_RIGHT - at), base)
    return jnp.where(lane >= S_LEFT, turn(from_left[rows, :], LANES - DEPTH - at), cells)


def strip_halo(base, beside, band, start, count):
    at = band * H_BAND + start
    lane = lanes_like(base)
    cells = jnp.where(lane >= S_RIGHT, turn(beside, S_RIGHT - at), base)
    return jnp.where(lane >= S_LEFT, turn(beside, LANES - count - at - SLOT), cells)


def strip_own(planes):
    return jnp.where(lanes_like(planes[0]) < S_MID, planes[0], turn(planes[1], -S_TURN))


def first_kernel(
    second_hbm, first_hbm, shifts_hbm, second_0, second_1, first_0, first_1, coarse, swap_0, swap_1, own_meta,
    shifts, sems, shift_sem,
):
    seconds, firsts = (second_0, second_1), (first_0, first_1)
    bands, height, _ = second_0.shape
    width = COLUMNS
    coarse_height = height // FACTOR
    lane = lanes_of()
    get_shifts = pltpu.make_async_copy(shifts_hbm, shifts, shift_sem)
    get_shifts.start()
    copies = []
    for image, (source, refs) in enumerate(((second_hbm, seconds), (first_hbm, firsts))):
        for band in range(bands):
            for tile, ref in enumerate(refs):
                copy = pltpu.make_async_copy(
                    source.at[band, :, pl.ds(tile * LANES, LANES)], ref.at[band], sems.at[image, band, tile]
                )
                copy.start()
                copies.append((image * bands + band, tile, ref, band, copy))
    cell = lax.broadcasted_iota(jnp.int32, (width, LANES), 0)
    place = lax.broadcasted_iota(jnp.int32, (width, LANES), 1)
    weights = jnp.where(place - LEAD == cell // FACTOR, 1.0 / (FACTOR * FACTOR), 0.0).astype(jnp.bfloat16)
    means = []
    packed = [None, None]
    for image, (count, offset) in enumerate(((REACH, 0), (DEPTH, REACH))):
        for pair in range(0, bands, 2):
            some = range(pair, pair + 2)
            group = copies[2 * (image * bands + pair) : 2 * (image * bands + pair + 2)]
            for *_, copy in group:
                copy.wait()
            sums = {}
            for plane, tile, ref, band, _ in group:
                parts = [ref[band, pl.ds(k, coarse_height, stride=FACTOR), :] for k in range(FACTOR)]
                while len(parts) > 1:
                    parts = [x + y for x, y in zip(parts[::2], parts[1::2])]
                sums[band, tile] = parts[0]
            tall = [jnp.concatenate([sums[band, tile] for tile in range(2)], axis=1) for band in some]
            means.append(split_dot(jnp.concatenate(tall, axis=0), weights))
            packed = [
                pack_image(packed[side], bool(side), (seconds, firsts)[image], some, count, offset) for side in range(2)
            ]
    means = jnp.concatenate(means, axis=0)
    get_shifts.wait()
    shift_rows = shifts[0, 0, 0].astype(jnp.float32)
    shift_cols = shifts[0, 0, 1].astype(jnp.float32)
    place = lanes_of(height // 2) & (HALF - 1)
    packed = [
        jnp.where(place == SHIFT_R, shift_rows, jnp.where(place == SHIFT_C, shift_cols, jnp.where(place == EXISTS, 1.0, x)))
        for x in packed
    ]
    to_left, to_right = [pack_means(packed[side], bool(side), means) for side in range(2)]
    coarse[...] = means
    own_meta[...] = jnp.where(lane < SLOT, shift_rows, shift_cols)
    even = is_even("col", swap_0)
    swap_0[...] = jnp.where(even, to_right, to_left)
    swap_1[...] = jnp.where(even, to_left, to_right)


def message_kernel(
    count, coarse, own_meta, got_0, got_1, up_part, down_part, _whole, swap_0, swap_1, from_left, from_right, wide
):
    other = without_ends(got_1, "col", count)
    even = is_even("col", got_0)
    from_right[...] = jnp.where(even, got_0[...], other)
    from_left[...] = jnp.where(even, other, got_0[...])
    planes_coarse, coarse_height, _ = wide.shape
    bands = planes_coarse // 2
    end = from_left.shape[0]
    coarse_width = COLUMNS // FACTOR
    lane = lanes_of()
    wides = []
    for plane in range(planes_coarse):
        half, block = divmod(plane, planes_coarse // 2)
        for step in range(coarse_height // SUB):
            own = slice(plane * coarse_height + step * SUB, plane * coarse_height + (step + 1) * SUB)
            rows = slice(block * coarse_height + step * SUB, block * coarse_height + (step + 1) * SUB)
            at = half * HALF
            left = from_left[rows, :]
            right = from_right[rows, :]
            start = LEAD - C_SECOND
            cells = turn(left, start - at - COARSE_A)
            cells = jnp.where(lane >= start + 3, turn(left, start + 3 - at - COARSE_B), cells)
            cells = jnp.where(lane >= LEAD, coarse[own, :], cells)
            start = LEAD + coarse_width
            cells = jnp.where(lane >= start, turn(right, start - at - COARSE_A), cells)
            cells = jnp.where(lane >= start + 3, turn(right, start + 3 - at - COARSE_B), cells)
            wides.append((plane, step, cells))
    for plane, step, cells in wides:
        wide[plane, step * SUB : (step + 1) * SUB, :] = cells
    row = lax.broadcasted_iota(jnp.int32, (SUB, LANES), 0)
    meta = own_meta[...]
    for message, at in ((from_left, 48), (from_right, 80)):
        first_rows = message[0:SUB, :]
        rows = jnp.broadcast_to(first_rows[:, SHIFT_R : SHIFT_R + 1], (SUB, LANES))
        cols = jnp.broadcast_to(first_rows[:, SHIFT_C : SHIFT_C + 1], (SUB, LANES))
        meta = jnp.where(lane >= at, rows, meta)
        meta = jnp.where(lane >= at + 16, cols, meta)

    def beside(rows, half):
        left = from_left[rows, :]
        right = from_right[rows, :]
        cells = jnp.zeros((SUB, LANES), jnp.float32)
        for band in range(bands):
            at = half * HALF + band * SLOT
            cells = jnp.where(lane >= band * H_BAND, turn(right, band * H_BAND - at), cells)
            cells = jnp.where(lane >= band * H_BAND + SLOT, turn(left, band * H_BAND + SLOT - at), cells)
        return cells

    even = is_even("row", meta)
    parts = []
    for part, half, near, next_rows, row_of in (
        (up_part, 0, slice(0, 8), slice(8, 16), 0),
        (down_part, 1, slice(end - 8, end), slice(end - 16, end - 8), 7),
    ):
        eight = beside(near, half)
        one = beside(next_rows, half)
        one = jnp.broadcast_to(one[row_of : row_of + 1], (SUB, LANES))
        coarse_rows = []
        for band in range(bands):
            rows = slice(0, C_SECOND) if half == 0 else slice(coarse_height - C_SECOND, coarse_height)
            second = wide[band, rows, :]
            first = turn(wide[bands + band, rows, :], HALF)
            coarse_rows.append(jnp.where(lanes_like(second) < HALF, second, first))
        parts.append([
            (part[E8:H8, :], E8), (eight, H8), (part[E1:H1, :], E1), (jnp.where(row == 0, one, meta), H1),
            (part[F4:CS, :], F4), *[(x, CS + k * C_SECOND) for k, x in enumerate(coarse_rows)],
        ])
    for (up, at), (down, _) in zip(*parts):
        even = is_even("row", up)
        swap_0[at : at + up.shape[0], :] = jnp.where(even, down, up)
        swap_1[at : at + up.shape[0], :] = jnp.where(even, up, down)


def coarse_flow_of(second, first, mask):
    def along_rows(x):
        return pltpu.roll(x, x.shape[0] - 1, 0) - pltpu.roll(x, 1, 0)

    def along_cols(x):
        return pltpu.roll(x, LANES - 1, 1) - pltpu.roll(x, 1, 1)

    bands = BANDS
    size = second.shape[0] // bands
    grad_rows = 0.125 * along_rows(second)
    grad_cols = 0.125 * along_cols(second)
    offset = 0.25 * (second - first)
    data = jnp.clip(offset, -LIMIT, LIMIT)
    yield

    def pull(grads):
        terms = data * grads
        return sum(terms[k * size : (k + 1) * size] for k in range(bands))

    def tall(x):
        return jnp.concatenate([x] * bands, axis=0)

    flow = [-mask * pull(grad_rows), -mask * pull(grad_cols)]
    extrapolated = [2.0 * x for x in flow]
    dual_rows = [0.0, 0.0]
    dual_cols = [0.0, 0.0]
    yield
    for step in range(1, STEPS):
        changes = [(along_rows(x), along_cols(x)) for x in extrapolated]
        yield
        data = data + offset + grad_rows * tall(extrapolated[0]) + grad_cols * tall(extrapolated[1])
        data = jnp.clip(data, -LIMIT, LIMIT)
        yield
        for c in range(2):
            rows = dual_rows[c] + changes[c][0]
            cols = dual_cols[c] + changes[c][1]
            scale = jnp.minimum(mask, (8.0 * ALPHA) * lax.rsqrt(rows * rows + cols * cols))
            dual_rows[c] = rows * scale
            dual_cols[c] = cols * scale
        yield
        divergences = [along_rows(dual_rows[c]) + along_cols(dual_cols[c]) for c in range(2)]
        yield
        pulls = [pull(grad_rows), pull(grad_cols)]
        yield
        for c in range(2):
            following = flow[c] + mask * ((1.0 / 64.0) * divergences[c] - pulls[c])
            extrapolated[c] = 2.0 * following - flow[c]
            flow[c] = following
        yield
    return flow


def columns_of_planes(planes):
    whole = lax.broadcasted_iota(jnp.int32, (LANES, COLUMNS), 1)
    lane = lax.broadcasted_iota(jnp.int32, (LANES, LANES), 1)
    strip = jnp.where(lane < S_MID, lane, jnp.where(lane < S_LEFT, lane + (COLUMNS - S_RIGHT), lane - LANES))
    return jnp.concatenate([x for x, wanted in ((whole, "whole"), (strip, "strip")) if wanted in planes], axis=1)


def upsample(flow, planes, target):
    column = columns_of_planes(planes)
    source = lax.broadcasted_iota(jnp.int32, column.shape, 0)
    spread = jnp.where(source - LEAD == lax.shift_right_arithmetic(column, 3), float(FACTOR), 0.0).astype(jnp.bfloat16)
    rows = flow[0].shape[0]
    wide = split_dot(UNIT * jnp.concatenate(flow, axis=0), spread)
    for c in range(2):
        for tile in range(column.shape[1] // LANES):
            target[c, tile] = wide[c * rows : (c + 1) * rows, tile * LANES : (tile + 1) * LANES]


def repeat_rows(spread, initial, cells):
    for c in range(2):
        for tile in range(initial.shape[1]):
            rows = [jnp.broadcast_to(spread[c, tile, cell : cell + 1, :], (SUB, LANES)) for cell in cells]
            initial[c, tile, GUARD : GUARD + SUB * len(cells), :] = jnp.concatenate(rows, axis=0)


def shift_whole(here, shift):
    turned = [turn_back(x, shift) for x in here]
    lane = lanes_like(here[0])
    return [
        jnp.where(lane + shift >= LANES, turned[1], turned[0]),
        jnp.where(lane + shift < 0, turned[0], turned[1]),
    ]


def edge_lanes(rows):
    lane = lanes_of(rows)
    return lane == LANES - 1, lane == 0


def columns_whole(fields, edges):
    rows = fields[0].shape[0]
    if rows not in edges:
        edges[rows] = edge_lanes(rows)
    last, first = edges[rows]
    ahead = [pltpu.roll(x, LANES - 1, 1) for x in fields]
    behind = [pltpu.roll(x, 1, 1) for x in fields]
    return [
        jnp.where(last, ahead[1], ahead[0]) - behind[0],
        ahead[1] - jnp.where(first, behind[0], behind[1]),
    ]


def rows_within(tall):
    size = tall.shape[0]
    return (pltpu.roll(tall, size - 1, 0) - pltpu.roll(tall, 1, 0))[SUB : size - SUB]


def columns_strip(field):
    return pltpu.roll(field, LANES - 1, 1) - pltpu.roll(field, 1, 1)


def strip_windows(window, centre, right, left):
    own = turn_back(window(centre[0]), centre[1])
    beyond_left = turn_back(window(left[0]), left[1])
    beyond_right = turn_back(window(right[0]), right[1])
    lane = lanes_like(own)
    beyond = jnp.where((lane >= S_LEFT) | (lane < S_MID), beyond_left, beyond_right)
    is_beyond = lane >= S_RIGHT
    of_next = is_beyond & (lane != S_RIGHT) | (lane == 0)
    of_previous = is_beyond & (lane != LANES - 1) | (lane == S_RIGHT - 1)
    change = turn(jnp.where(of_next, beyond, own), -1) - turn(jnp.where(of_previous, beyond, own), 1)
    return jnp.where(is_beyond, beyond, own), change


def fine_steps(
    rows_total, chunk, columns, initial, extrap, dual_rows, dual_cols, change, dual_data,
    offsets, grads_rows, grads_cols, data_row, masks_of, result, kept, done=lambda k: None, first_pulls=None,
):
    assert STEPS == 3
    planes = len(offsets)
    bands = offsets[0].shape[0]
    chunks = rows_total // chunk

    def places(k, trim=(0, 0)):
        start, size = k * chunk + trim[0], chunk - sum(trim)
        return pl.ds(GUARD + start, size), pl.ds(start, size), pl.ds(data_row(k) + trim[0], size)

    def row_change(ref, c, tile, at):
        return ref[c, tile, pl.ds(at.start + 1, at.size), :] - ref[c, tile, pl.ds(at.start - 1, at.size), :]

    def clip(x):
        return jnp.clip(x, -UNIT * LIMIT, UNIT * LIMIT)

    tiles = range(planes)

    for step in range(STEPS):
        source = initial if step == 0 else extrap
        final = step == STEPS - 1

        def dual(item, source=source, step=step):
            k, c = item
            at, own, _ = places(k)
            masks = masks_of(own)
            along = columns([source[c, tile, at, :] for tile in tiles])
            values = []
            for tile in tiles:
                rows = row_change(source, c, tile, at)
                cols = along[tile]
                if step > 0:
                    rows = rows + dual_rows[c, tile, at, :]
                    cols = cols + dual_cols[c, tile, own, :]
                scale = jnp.minimum(masks[tile], lax.rsqrt(rows * rows + cols * cols))
                values.append((rows * scale, cols * scale))
            return values

        def store_dual(item, values):
            k, c = item
            for tile, (rows, cols) in enumerate(values):
                dual_rows[c, tile, places(k)[0], :] = rows
                dual_cols[c, tile, places(k)[1], :] = cols

        staggered([(k, c) for k in range(chunks) for c in range(2)], dual, store_dual, 1)
        along_of = {}

        def primal(item, step=step, final=final, along_of=along_of):
            k, tile = item
            at, own, data = places(k, kept(k) if final else (0, 0))
            if k not in along_of:
                along_of[k] = [columns([dual_cols[c, t, own, :] for t in tiles]) for c in range(2)]
            mask = masks_of(own)[tile]
            start = [initial[c, tile, at, :] for c in range(2)]
            if step > 0:
                moved = [extrap[c, tile, at, :] - start[c] for c in range(2)]
            if step == 1:
                changes = [0.5 * x for x in moved]
            if step == 2:
                changes = [change[c, tile, own, :] for c in range(2)]
            pulls = [None, None]
            duals = []
            ready = step == 0 and first_pulls is not None
            if ready:
                pulls = [first_pulls[c, tile, own, :] for c in range(2)]
            for band in range(0 if ready else bands):
                gradient = (grads_rows[tile][band, data, :], grads_cols[tile][band, data, :])
                value = offsets[tile][band, data, :]
                if step > 0:
                    earlier = clip(value) if step == 1 else dual_data[band, tile, own, :]
                    value = (value + earlier) + (gradient[0] * moved[0] + gradient[1] * moved[1])
                value = clip(value)
                duals.append(value)
                for c in range(2):
                    term = value * gradient[c]
                    pulls[c] = term if pulls[c] is None else pulls[c] + term
            flows, nexts = [], []
            for c in range(2):
                divergence = row_change(dual_rows, c, tile, at) + along_of[k][c][tile]
                moving = (mask * (1.0 / 64.0)) * divergence - pulls[c]
                total = moving if step == 0 else changes[c] + moving
                flows.append((start[c] + total) * (1.0 / UNIT) if final else total)
                nexts.append(None if final else start[c] + (total + moving))
            return flows, nexts, duals

        def store_primal(item, results, step=step, final=final):
            k, tile = item
            flows, nexts, duals = results
            at, own, _ = places(k, kept(k) if final else (0, 0))
            for c in range(2):
                if final:
                    result[c, tile, own, :] = flows[c]
                else:
                    if step > 0:
                        change[c, tile, own, :] = flows[c]
                    extrap[c, tile, at, :] = nexts[c]
            if final:
                if tile == planes - 1:
                    done(k)
            elif step > 0:
                for band in range(bands):
                    dual_data[band, tile, own, :] = duals[band]

        staggered([(k, tile) for k in range(chunks) for tile in tiles], primal, store_primal, 1)


def clear_guards(*refs):
    for ref in refs:
        rows = ref.shape[2]
        zero = jnp.zeros((GUARD, LANES), jnp.float32)
        for c in range(2):
            for tile in range(ref.shape[1]):
                ref[c, tile, 0:GUARD, :] = zero
                ref[c, tile, rows - GUARD : rows, :] = zero


def fine_scratch(bands, planes, rows):
    guarded = pltpu.VMEM((2, planes, rows + 2 * GUARD, LANES), jnp.float32)
    plain = pltpu.VMEM((2, planes, rows, LANES), jnp.float32)
    return [guarded, guarded, guarded, plain, plain, pltpu.VMEM((bands, planes, rows, LANES), jnp.float32)]


def pieces(bands, height, rows):
    assert (height - 2 * SUB) % rows == 0
    return [(band, row) for row in range(SUB, height - SUB, rows) for band in range(bands)]


def whole_terms_kernel(
    second_0, second_1, first_0, first_1, coarse, own_meta,
    offset, grad_rows, grad_cols, initial, strip_e, strip_f, up, down, moved, spread,
):
    seconds, firsts = (second_0, second_1), (first_0, first_1)
    bands, height, _ = second_0.shape
    block = 120
    coarse_height = coarse.shape[0] // (2 * bands)
    centre = shift_at(own_meta, 0, 0)
    def windows(band, row, rows):
        here = [ref[band, pl.ds(row + centre[0], rows), :].reshape(-1, LANES) for ref in seconds]
        return shift_whole(here, centre[1])

    woven = Woven(coarse_flow_of(coarse[0 : bands * coarse_height, :], coarse[bands * coarse_height :, :], 1.0))

    def strips_of(item):
        band, row = item
        rows = slice(row, row + LANES)
        return strip_own([ref[band, rows, :] for ref in seconds]), strip_own([ref[band, rows, :] for ref in firsts])

    def store_strips(item, results):
        band, row = item
        strip_e[band, row : row + LANES, :], strip_f[band, row : row + LANES, :] = results

    staggered([(band, row) for band in range(bands) for row in range(0, height, LANES)], strips_of, store_strips, 1, woven)

    ends = [(row, windows(slice(None), row, SUB)) for row in (SUB // 2, height - SUB - SUB // 2)]
    for row, values in ends:
        for tile in range(2):
            moved[tile, :, row : row + SUB, :] = values[tile].reshape(bands, SUB, LANES)

    edges = {}

    def values_of(item):
        band, row = item
        values = windows(band, row, block)
        along = columns_whole(values, edges)
        own = [ref[band, row : row + block, :] for ref in firsts]
        return values, [(0.25 * UNIT) * (x - y) for x, y in zip(values, own)], [0.125 * x for x in along]

    def store_values(item, results):
        band, row = item
        values, offsets, gradients = results
        data = slice(row + HALO, row + HALO + block)
        for tile in range(2):
            moved[tile, band, row : row + block, :] = values[tile]
            offset[tile, band, data, :] = offsets[tile]
            grad_cols[tile, band, data, :] = gradients[tile]

    staggered(pieces(bands, height, block), values_of, store_values, 1, woven)

    def gradient_of(item):
        band, row = item
        return [0.125 * rows_within(moved[tile, band, row - SUB : row + 120 + SUB, :]) for tile in range(2)]

    def store_gradient(item, results):
        band, row = item
        for tile in range(2):
            grad_rows[tile, band, row + HALO : row + HALO + 120, :] = results[tile]

    staggered(pieces(bands, height, 120), gradient_of, store_gradient, 1, woven)

    parts = []
    for band in range(bands):
        for second, first in zip(seconds, firsts):
            parts.append((
                second[band, 0:16, :], first[band, 0:8, :],
                second[band, height - 16 : height, :], first[band, height - 8 : height, :],
            ))
    for k, (second_top, first_top, second_end, first_end) in enumerate(parts):
        up[E8 + 8 * k : E8 + 8 * k + 8, :] = second_top[0:8]
        up[E1 + k : E1 + k + 1, :] = second_top[8:9]
        up[F4 + 4 * k : F4 + 4 * k + 4, :] = first_top[0:4]
        down[E8 + 8 * k : E8 + 8 * k + 8, :] = second_end[8:16]
        down[E1 + k : E1 + k + 1, :] = second_end[7:8]
        down[F4 + 4 * k : F4 + 4 * k + 4, :] = first_end[4:8]
    for target in (up, down):
        for start, end in ((H8, E1), (H1, F4), (CS, ROW_MESSAGE)):
            target[start:end, :] = jnp.zeros((end - start, LANES), jnp.float32)

    upsample(woven.finish(), ("whole",), spread)
    clear_guards(initial)
    rows_total = initial.shape[2] - 2 * GUARD
    repeat_rows(spread, initial, [BEGIN // FACTOR + k for k in range(rows_total // SUB)])


def whole_steps_kernel(
    initial, offset, grad_rows, grad_cols, result, extrap, dual_rows, dual_cols, change, dual_data
):
    rows_total = result.shape[2]
    clear_guards(extrap, dual_rows)
    chunk = 88
    edges = {}
    fine_steps(
        rows_total, chunk, lambda fields: columns_whole(fields, edges),
        initial, extrap, dual_rows, dual_cols, change, dual_data,
        *[[ref.at[tile] for tile in range(2)] for ref in (offset, grad_rows, grad_cols)],
        lambda k: HALO + BEGIN + k * chunk, lambda own: (1.0, 1.0), result, lambda k: (SUB * (k == 0), SUB * (k == 1)),
    )


def strip_kernel(
    count, strip_e, strip_f, from_left, from_right, wide, own_message, whole,
    middle, strip_out, first_ends, offset, grad_rows, grad_cols,
    moved, result, spread, initial, extrap, dual_rows, dual_cols, change, dual_data,
):
    bands, height, _ = strip_e.shape
    block = 120
    coarse_height = height // FACTOR
    coarse_width = COLUMNS // FACTOR
    rows_total = height - 2 * BEGIN
    lane = lanes_of()
    centre, right, left = shifts_of(own_message)
    has_left, has_right = neighbours("col", count)
    exists = jnp.where(lane < S_RIGHT, 1.0, jnp.where(lane < S_LEFT, has_right, has_left))

    def tall_factor(rows):
        return 0.125 * jnp.concatenate([exists] * (rows // SUB), axis=0)

    mask = jnp.where(lane < LEAD, has_left, jnp.where(lane < LEAD + coarse_width, 1.0, has_right))
    mask = jnp.concatenate([mask] * (coarse_height // SUB), axis=0)
    cells = [wide[k * bands : (k + 1) * bands].reshape(bands * coarse_height, LANES) for k in range(2)]
    woven = Woven(coarse_flow_of(*cells, mask))

    def halves(row, rows):
        half = row // (height // 2)
        start = row - half * (height // 2)
        return half, slice(start, start + rows)

    def second_of(item):
        band, row = item
        half, message = halves(row, LANES)
        return strip_second(strip_e[band, row : row + LANES, :], from_left, from_right, message, half, band)

    def store_second(item, value):
        band, row = item
        strip_out[band, row : row + LANES, :] = value

    staggered([(band, row) for row in range(0, height, LANES) for band in range(bands)], second_of, store_second, 1, woven)

    def first_of(band, row, rows):
        half, message = halves(row, rows)
        return strip_first(strip_f[band, row : row + rows, :], from_left, from_right, message, half, band)

    firsts = [(end, band, first_of(band, (0, height - SUB)[end], SUB)) for end in range(2) for band in range(bands)]
    for end, band, value in firsts:
        first_ends[end, band] = value

    def windows(band, row, rows):
        return strip_windows(
            lambda shift: strip_out[band, pl.ds(row + shift, rows), :].reshape(-1, LANES), centre, right, left
        )

    ends = [(row, windows(slice(None), row, SUB)[0]) for row in (SUB // 2, height - SUB - SUB // 2)]
    for row, value in ends:
        moved[:, row : row + SUB, :] = value.reshape(bands, SUB, LANES)

    factor = tall_factor(block)

    def values_of(item):
        band, row = item
        value, along = windows(band, row, block)
        return value, (0.25 * UNIT) * (value - first_of(band, row, block)), factor * along

    def store_values(item, results):
        band, row = item
        data = slice(row + HALO, row + HALO + block)
        moved[band, row : row + block, :], offset[band, data, :], grad_cols[band, data, :] = results

    staggered(pieces(bands, height, block), values_of, store_values, 1, woven)

    def gradient_of(item):
        band, row = item
        return factor * rows_within(moved[band, row - SUB : row + block + SUB, :])

    def store_gradient(item, value):
        band, row = item
        grad_rows[band, row + HALO : row + HALO + block, :] = value

    staggered(pieces(bands, height, block), gradient_of, store_gradient, 1, woven)

    upsample(woven.finish(), ("strip",), spread)
    clear_guards(initial, extrap, dual_rows)
    repeat_rows(spread, initial, [BEGIN // FACTOR + k for k in range(rows_total // SUB)])

    chunk = 176
    masks = jnp.concatenate([exists] * (chunk // SUB), axis=0)
    fine_steps(
        rows_total, chunk, lambda fields: [columns_strip(fields[0])],
        initial, extrap, dual_rows, dual_cols, change, dual_data, [offset], [grad_rows], [grad_cols],
        lambda k: HALO + BEGIN + k * chunk, lambda own: (masks[: own.size],), result, lambda k: (SUB, SUB),
    )
    join(whole, result.at[:, 0], middle, slice(SUB, rows_total - SUB))


def join(whole, strip, target, rows):
    lane = lanes_of(rows.stop - rows.start)
    values = []
    for c in range(2):
        edge = strip[c, rows, :]
        start = jnp.where(lane < EDGE, edge, whole[c, 0, rows, :])
        values.append((start, jnp.where(lane >= LANES - EDGE, turn(edge, S_TURN), whole[c, 1, rows, :])))
    for c in range(2):
        target[c, rows, 0:LANES], target[c, rows, LANES:COLUMNS] = values[c]


def outer_kernel(
    counts, second_0, second_1, first_0, first_1, strip_e, first_ends, wide, got_1, got_0, middle, own_message,
    _wo, _wr, _wc, _so, _sr, _sc,
    flow_out, coarse_out, whole_offset, whole_rows, whole_cols, strip_offset, strip_rows, strip_cols,
    from_up, from_down, extended, tall, spread, masks, result, joined, coarse_result, pulls, sems,
    initial, extrap, dual_rows, dual_cols, change, dual_data,
):
    bands, height, _ = second_0.shape
    coarse_height = height // FACTOR
    coarse_width = COLUMNS // FACTOR
    rows_total = 2 * EACH
    lane = lanes_of()

    put_middle = pltpu.make_async_copy(
        middle.at[:, pl.ds(MARGIN - BEGIN, height - 2 * MARGIN), :],
        flow_out.at[:, pl.ds(MARGIN, height - 2 * MARGIN), :],
        sems.at[0],
    )
    put_middle.start()
    own, one, other = [shifts_of(message) for message in (own_message, got_0, got_1)]
    odd = lax.axis_index("row") % 2

    def of_row(for_even, for_odd):
        return [tuple(jnp.where(odd == 0, x, y) for x, y in zip(*pair)) for pair in zip(for_even, for_odd)]

    above, below = of_row(other, one), of_row(one, other)

    other = without_ends(got_1, "row", counts[0])
    even = is_even("row", got_0)
    from_down[...] = jnp.where(even, got_0[...], other)
    from_up[...] = jnp.where(even, other, got_0[...])

    has_up, has_down = neighbours("row", counts[0])
    has_left, has_right = neighbours("col", counts[1])
    exists = jnp.where(lane < S_RIGHT, 1.0, jnp.where(lane < S_LEFT, has_right, has_left))

    zero = jnp.zeros((SUB, LANES), jnp.float32)
    tall_rows = coarse_height + 2 * LEAD
    parts = []
    fill = jnp.zeros((LEAD - C_SECOND, LANES), jnp.float32)
    for plane in range(2 * bands):
        at = CS + C_SECOND * (plane % bands)
        ends = [turn(message[at : at + C_SECOND, :], HALF * (plane // bands)) for message in (from_up, from_down)]
        parts.append([fill, ends[0], wide[plane], ends[1], fill])
    for plane, values in enumerate(parts):
        tall[plane] = jnp.concatenate(values, axis=0)
    across = jnp.where(lane < LEAD, has_left, jnp.where(lane < LEAD + coarse_width, 1.0, has_right))
    mask = jnp.concatenate([across * has_up] + [across] * (coarse_height // SUB) + [across * has_down], axis=0)
    for end in range(2):
        message = (from_up, from_down)[end]
        beside = message[H8 : H8 + 8, :]
        beside_one = jnp.broadcast_to(message[H1 : H1 + 1, :], (SUB, LANES))
        parts = []
        for band in range(bands):
            eights = [message[E8 + 8 * k : E8 + 8 * k + 8, :] for k in (2 * band, 2 * band + 1)]
            ones = [jnp.broadcast_to(message[E1 + k : E1 + k + 1, :], (SUB, LANES)) for k in (2 * band, 2 * band + 1)]
            eights.append(strip_halo(strip_own(eights), beside, band, 0, REACH))
            ones.append(strip_halo(strip_own(ones), beside_one, band, 0, REACH))
            for tile, (eight, one) in enumerate(zip(eights, ones)):
                source = (second_0, second_1, strip_e)[tile]
                if end == 0:
                    parts.append((tile, band, [one, eight, source[band, 0:24, :]]))
                else:
                    parts.append((tile, band, [source[band, height - 24 : height, :], eight, one]))
        for tile, band, values in parts:
            extended[end, tile, band] = jnp.concatenate(values, axis=0)
    cells = [tall[k * bands : (k + 1) * bands].reshape(bands * tall_rows, LANES) for k in range(2)]
    woven = Woven(coarse_flow_of(*cells, mask))
    edges = {}
    rows_data = whole_offset.shape[2]
    exists_tall = jnp.concatenate([exists] * bands, axis=0)

    def rows_of(halo, end):
        if halo:
            return slice(0, SUB) if end == 0 else slice(rows_data - SUB, rows_data)
        return slice(HALO, HALO + SUB) if end == 0 else slice(rows_data - HALO - SUB, rows_data - HALO)

    def values_of(item):
        halo, end = item
        message = (from_up, from_down)[end]
        base = (SUB, 3 * SUB)[end] if halo else 2 * SUB
        shifts = (above, below)[end] if halo else own
        factor = 0.125 * (has_up, has_down)[end] if halo else 0.125

        def here(tile, shift):
            return extended[end, tile, :, pl.ds(base + shift, SUB), :].reshape(-1, LANES)

        def down_up(tile, shift):
            return here(tile, shift + 1) - here(tile, shift - 1)

        own_rows = slice(0, SUB) if end == 0 else slice(height - SUB, height)
        if halo:
            firsts = [[], [], []]
            for band in range(bands):
                eights = []
                for k in (2 * band, 2 * band + 1):
                    four = message[F4 + 4 * k : F4 + 4 * k + 4, :]
                    eights.append(jnp.concatenate([four, four], axis=0))
                eights.append(strip_halo(strip_own(eights), message[H8 : H8 + 8, :], band, REACH, DEPTH))
                for tile in range(3):
                    firsts[tile].append(eights[tile])
            firsts = [jnp.concatenate(x, axis=0) for x in firsts]
        else:
            firsts = [x.reshape(-1, LANES) for x in (first_0[:, own_rows, :], first_1[:, own_rows, :], first_ends[end])]
        centre = shifts[0]
        values = shift_whole([here(tile, centre[0]) for tile in range(2)], centre[1])
        changes = shift_whole([down_up(tile, centre[0]) for tile in range(2)], centre[1])
        along = columns_whole(values, edges)
        value, across_cols = strip_windows(lambda shift: here(2, shift), *shifts)
        change_rows, _ = strip_windows(lambda shift: down_up(2, shift), *shifts)
        return (
            [(0.25 * UNIT) * (x - y) for x, y in zip([*values, value], firsts)],
            [*[factor * x for x in changes], (factor * exists_tall) * change_rows],
            [*[factor * x for x in along], (factor * exists_tall) * across_cols],
        )

    def store_values(item, results):
        rows = rows_of(*item)
        for values, whole, strip in zip(
            results, (whole_offset, whole_rows, whole_cols), (strip_offset, strip_rows, strip_cols)
        ):
            values = [x.reshape(bands, SUB, LANES) for x in values]
            for tile in range(2):
                whole[tile, :, rows, :] = values[tile]
            strip[:, rows, :] = values[2]

    staggered([(halo, end) for halo in (True, False) for end in range(2)], values_of, store_values, 1, woven)

    def data_row(k):
        return k * (rows_data - EACH)

    offsets = [whole_offset.at[0], whole_offset.at[1], strip_offset]
    grads_rows = [whole_rows.at[0], whole_rows.at[1], strip_rows]
    grads_cols = [whole_cols.at[0], whole_cols.at[1], strip_cols]

    def pulls_of(item):
        k, tile = item
        data = pl.ds(data_row(k), EACH)
        duals = [jnp.clip(offsets[tile][band, data, :], -UNIT * LIMIT, UNIT * LIMIT) for band in range(bands)]
        return [
            sum(duals[band] * grads[tile][band, data, :] for band in range(bands)) for grads in (grads_rows, grads_cols)
        ]

    def store_pulls(item, values):
        k, tile = item
        for c in range(2):
            pulls[c, tile, k * EACH : (k + 1) * EACH, :] = values[c]

    staggered([(k, tile) for k in range(2) for tile in range(3)], pulls_of, store_pulls, 1, woven)

    flow = woven.finish()
    for c in range(2):
        coarse_result[c] = turn(flow[c][LEAD : LEAD + coarse_height], -LEAD)[:, :coarse_width]
    put_coarse = pltpu.make_async_copy(coarse_result, coarse_out, sems.at[1])
    put_coarse.start()
    upsample(flow, ("whole", "strip"), spread)
    clear_guards(initial, extrap, dual_rows)
    each = EACH // SUB
    repeat_rows(
        spread, initial,
        [LEAD - 1 + k for k in range(each)] + [tall_rows - LEAD + 1 - each + k for k in range(each)],
    )

    for i, value in enumerate((jnp.ones((SUB, LANES), jnp.float32), exists)):
        masks[i] = jnp.concatenate([value * has_up] + [value] * (rows_total // SUB - 2) + [value * has_down], axis=0)

    def masks_of(rows):
        whole = masks[0, rows, :]
        return (whole, whole, masks[1, rows, :])

    chunk = EACH
    edges = {}
    puts = [
        pltpu.make_async_copy(
            joined.at[:, pl.ds(k * EACH + SUB, MARGIN), :],
            flow_out.at[:, pl.ds(k * (height - MARGIN), MARGIN), :],
            sems.at[2 + k],
        )
        for k in range(2)
    ]

    def finish(k):
        join(result, result.at[:, 2], joined, slice(k * EACH + SUB, k * EACH + SUB + MARGIN))
        puts[k].start()

    fine_steps(
        rows_total, chunk, lambda fields: columns_whole(fields[:2], edges) + [columns_strip(fields[2])],
        initial, extrap, dual_rows, dual_cols, change, dual_data,
        offsets, grads_rows, grads_cols, data_row, masks_of, result, lambda k: (SUB, SUB), finish, pulls,
    )
    put_middle.wait()
    put_coarse.wait()
    for put in puts:
        put.wait()


def swap_with(message, axis, start):
    names = ("row", "col")
    sizes = [lax.axis_size(name) for name in names]
    along = names.index(axis)
    count, others = sizes[along], sizes[1 - along]

    def number(place, other):
        row, col = (place, other) if along == 0 else (other, place)
        return row * sizes[1] + col

    pairs = [(number(i, k), number(i + 1, k)) for i in range(start, count - 1, 2) for k in range(others)]
    if start and axis == "col":
        pairs += [(number(i, k), number(i, k + 1)) for i in (0, count - 1) for k in range(0, others, 2)]
    elif start:
        pairs += [(number(0, k), number(count - 1, k)) for k in range(others)]
    return lax.ppermute(message, names, pairs + [(j, i) for i, j in pairs])


def local(frame_first, frame_second, shifts):
    bands, height, width = frame_first.shape
    assert bands == 4 and width == COLUMNS and height % LANES == 0
    assert lax.axis_size("row") % 2 == 0 and lax.axis_size("col") % 2 == 0
    coarse_height = height // FACTOR
    coarse_width = width // FACTOR
    vmem = pl.BlockSpec(memory_space=pltpu.VMEM)
    hbm = pl.BlockSpec(memory_space=pltpu.HBM)
    tall_rows = coarse_height + 2 * LEAD
    inner_rows = height - 2 * BEGIN

    def shape(*sizes):
        return jax.ShapeDtypeStruct(sizes, jnp.float32)

    def scratch(*sizes):
        return pltpu.VMEM(sizes, jnp.float32)

    def call(kernel, name, arguments, outs, scratches=(), flops=1_000_000, **more):
        more = {"in_specs": [vmem] * len(arguments), "out_specs": (vmem,) * len(outs), **more}
        return pl.pallas_call(
            kernel,
            out_shape=tuple(outs),
            scratch_shapes=list(scratches),
            compiler_params=pltpu.CompilerParams(vmem_limit_bytes=24 * 1024 * 1024),
            cost_estimate=pl.CostEstimate(flops=flops, bytes_accessed=1_000_000, transcendentals=0),
            name=name,
            **more,
        )(*arguments)

    plane = shape(bands, height, LANES)
    column_message = shape(height // 2, LANES)
    row_message = shape(ROW_MESSAGE, LANES)
    whole_data = shape(2, bands, height + 2 * HALO, LANES)
    strip_data = shape(bands, height + 2 * HALO, LANES)

    *frames, coarse, swap_0, swap_1, own_meta = call(
        first_kernel,
        "means_and_message",
        [pltpu.with_memory_space_constraint(x, pltpu.HBM) for x in (frame_second, frame_first, shifts)],
        [*[plane] * 4, shape(2 * bands * coarse_height, LANES), column_message, column_message, shape(SUB, LANES)],
        [
            pltpu.SMEM((1, 1, 2), jnp.int32),
            pltpu.SemaphoreType.DMA((2, bands, 2)),
            pltpu.SemaphoreType.DMA,
        ],
        in_specs=[hbm] * 3,
    )
    got_0 = swap_with(swap_0, "col", 0)
    got_1 = swap_with(swap_1, "col", 1)

    *whole_terms, initial, strip_e, strip_f, up_part, down_part = call(
        whole_terms_kernel,
        "whole_terms",
        [*frames, coarse, own_meta],
        [
            *[whole_data] * 3, shape(2, 2, inner_rows + 2 * GUARD, LANES),
            plane, plane, row_message, row_message,
        ],
        [
            scratch(2, bands, height, LANES), scratch(2, 2, coarse_height, LANES),
        ],
        flops=8_000_000,
    )
    (whole,) = call(
        whole_steps_kernel,
        "whole_steps",
        [initial, *whole_terms],
        [shape(2, 2, inner_rows, LANES)],
        fine_scratch(bands, 2, inner_rows)[1:],
        flops=20_000_000,
    )

    swap_0, swap_1, from_left, from_right, wide = call(
        functools.partial(message_kernel, lax.axis_size("col")),
        "row_messages",
        [coarse, own_meta, got_0, got_1, up_part, down_part, whole],
        [row_message, row_message, column_message, column_message, shape(2 * bands, coarse_height, LANES)],
    )
    got_1 = swap_with(swap_1, "row", 1)
    got_0 = swap_with(swap_0, "row", 0)

    middle, strip_e, first_ends, *strip_terms = call(
        functools.partial(strip_kernel, lax.axis_size("col")),
        "strip",
        [strip_e, strip_f, from_left, from_right, wide, swap_0, whole],
        [shape(2, inner_rows, width), plane, shape(2, bands, SUB, LANES), *[strip_data] * 3],
        [
            scratch(bands, height, LANES),
            scratch(2, 1, inner_rows, LANES),
            scratch(2, 1, coarse_height, LANES),
            *fine_scratch(bands, 1, inner_rows),
        ],
        flops=16_000_000,
    )

    flow, coarse_flow, *_ = call(
        functools.partial(outer_kernel, (lax.axis_size("row"), lax.axis_size("col"))),
        "outer_rows",
        [
            *frames, strip_e, first_ends, wide, got_1, got_0, middle, swap_0,
            *whole_terms, *strip_terms,
        ],
        [shape(2, height, width), shape(2, coarse_height, coarse_width), *[whole_data] * 3, *[strip_data] * 3],
        [
            scratch(ROW_MESSAGE, LANES),
            scratch(ROW_MESSAGE, LANES),
            scratch(2, 3, bands, 40, LANES),
            scratch(2 * bands, tall_rows, LANES),
            scratch(2, 3, tall_rows, LANES),
            scratch(2, 2 * EACH, LANES),
            scratch(2, 3, 2 * EACH, LANES),
            scratch(2, 2 * EACH, width),
            scratch(2, coarse_height, coarse_width),
            scratch(2, 3, 2 * EACH, LANES),
            pltpu.SemaphoreType.DMA((4,)),
            *fine_scratch(bands, 3, 2 * EACH),
        ],
        out_specs=(hbm, hbm) + (vmem,) * 6,
        input_output_aliases={11 + k: 2 + k for k in range(6)},
    )
    return (flow, coarse_flow)


def solution(mesh):
    return jax.shard_map(
        local,
        mesh=mesh,
        in_specs=(P(None, "row", "col"), P(None, "row", "col"), P("row", "col", None)),
        out_specs=(P(None, "row", "col"), P(None, "row", "col")),
        check_vma=False,
    )
```

```python
import functools

import jax
import jax.numpy as jnp
from jax import lax
from jax.experimental import pallas as pl
from jax.experimental.pallas import tpu as pltpu
from jax.sharding import PartitionSpec as P

FACTOR = 8
MAXD = 4
BANDS = 4
STEPS = 3
LANES = 128
COLUMNS = 2 * LANES
HALF = 64
SUB = 8
DEPTH = 4
REACH = DEPTH + MAXD + 1
SLOT = 16
C_SECOND = 6
C_FIRST = 5
LEAD = 8
MARGIN = 48
EDGE = 46
GUARD = 8
HALO = 8
BEGIN = 40
EACH = MARGIN + 16
LIMIT = 0.3
ALPHA = 0.3
UNIT = 0.125 / ALPHA

S_MID = 55
S_RIGHT = 110
S_LEFT = LANES - REACH
S_TURN = COLUMNS - S_RIGHT - LANES

E8 = 0
H8 = 64
E1 = 72
H1 = 80
META = 81
F4 = 88
CS = 120
ROW_MESSAGE = 144
H_BAND = 32

COARSE_A = REACH + DEPTH
COARSE_B = SLOT + REACH + DEPTH
SHIFT_R = 2 * SLOT + REACH + DEPTH
SHIFT_C = SHIFT_R + 1
EXISTS = SHIFT_R + 2


def lanes_of(rows=SUB):
    return lax.broadcasted_iota(jnp.int32, (rows, LANES), 1)


def lanes_like(x):
    return lax.broadcasted_iota(jnp.int32, x.shape, 1)


def turn(x, amount):
    amount = amount % LANES
    return x if amount == 0 else pltpu.roll(x, amount, 1)


def turn_back(x, shift):
    return pltpu.roll(x, lax.rem(LANES - shift, LANES), 1)


def split_dot(x, exact):
    high = x.astype(jnp.bfloat16)
    rest = x - high.astype(jnp.float32)
    middle = rest.astype(jnp.bfloat16)
    low = (rest - middle.astype(jnp.float32)).astype(jnp.bfloat16)
    parts = [jnp.dot(part, exact, preferred_element_type=jnp.float32) for part in (low, middle, high)]
    return parts[0] + parts[1] + parts[2]


def neighbours(axis, count):
    place = lax.axis_index(axis)
    return jnp.where(place > 0, 1.0, 0.0), jnp.where(place < count - 1, 1.0, 0.0)


def shift_at(ref, row, lane):
    numbers = ref[row : row + 1, :].astype(jnp.int32)
    return numbers[0, lane], numbers[0, lane + SLOT]


def shifts_of(message):
    return [shift_at(message, META, lane) for lane in (0, 80, 48)]


def is_even(axis, like):
    return jnp.broadcast_to(lax.axis_index(axis) % 2, like.shape) == 0


def without_ends(message, axis, count):
    place = jnp.broadcast_to(lax.axis_index(axis), message.shape)
    return jnp.where((place > 0) & (place < count - 1), message[...], 0.0)


def staggered(items, compute, store, depth, woven=None):
    pending = []
    for item in items:
        pending.append((item, compute(item)))
        if woven is not None:
            woven.advance()
        if len(pending) > depth:
            store(*pending.pop(0))
    for entry in pending:
        store(*entry)


class Woven:
    def __init__(self, stages):
        self.stages = stages
        self.result = None

    def advance(self):
        try:
            next(self.stages)
            return True
        except StopIteration as end:
            self.result = end.value if self.result is None else self.result
            return False

    def finish(self):
        while self.advance():
            pass
        return self.result


def pack_image(packed, to_right, planes, some, count, offset):
    _, height, _ = planes[0].shape
    plane = planes[int(to_right)]
    start = LANES - count if to_right else 0
    length = height // 2
    lane = lanes_of(length)
    for half in range(2):
        for band in some:
            at = half * HALF + band * SLOT + offset
            cells = turn(plane[band, half * length : (half + 1) * length, :], at - start)
            packed = cells if packed is None else jnp.where((lane >= at) & (lane < at + count), cells, packed)
    return packed


def pack_means(packed, to_right, means):
    length = packed.shape[0]
    start = LEAD + COLUMNS // FACTOR - C_SECOND if to_right else LEAD
    lane = lanes_of(length)
    for half in range(2):
        cells = means[half * length : (half + 1) * length]
        for at, first in ((half * HALF + COARSE_A, start), (half * HALF + COARSE_B, start + 3)):
            packed = jnp.where((lane >= at) & (lane < at + 3), turn(cells, at - first), packed)
    return packed


def strip_second(base, from_left, from_right, rows, half, band):
    at = half * HALF + band * SLOT
    lane = lanes_like(base)
    cells = jnp.where(lane >= S_RIGHT, turn(from_right[rows, :], S_RIGHT - at), base)
    return jnp.where(lane >= S_LEFT, turn(from_left[rows, :], S_LEFT - at), cells)


def strip_first(base, from_left, from_right, rows, half, band):
    at = half * HALF + band * SLOT + REACH
    lane = lanes_like(base)
    cells = jnp.where(lane >= S_RIGHT, turn(from_right[rows, :], S_RIGHT - at), base)
    return jnp.where(lane >= S_LEFT, turn(from_left[rows, :], LANES - DEPTH - at), cells)


def strip_halo(base, beside, band, start, count):
    at = band * H_BAND + start
    lane = lanes_like(base)
    cells = jnp.where(lane >= S_RIGHT, turn(beside, S_RIGHT - at), base)
    return jnp.where(lane >= S_LEFT, turn(beside, LANES - count - at - SLOT), cells)


def strip_own(planes):
    return jnp.where(lanes_like(planes[0]) < S_MID, planes[0], turn(planes[1], -S_TURN))


def first_kernel(
    second_hbm, first_hbm, shifts_hbm, second_0, second_1, first_0, first_1, coarse, swap_0, swap_1, own_meta,
    shifts, sems, shift_sem,
):
    seconds, firsts = (second_0, second_1), (first_0, first_1)
    bands, height, _ = second_0.shape
    width = COLUMNS
    coarse_height = height // FACTOR
    lane = lanes_of()
    get_shifts = pltpu.make_async_copy(shifts_hbm, shifts, shift_sem)
    get_shifts.start()
    copies = []
    for image, (source, refs) in enumerate(((second_hbm, seconds), (first_hbm, firsts))):
        for band in range(bands):
            for tile, ref in enumerate(refs):
                copy = pltpu.make_async_copy(
                    source.at[band, :, pl.ds(tile * LANES, LANES)], ref.at[band], sems.at[image, band, tile]
                )
                copy.start()
                copies.append((image * bands + band, tile, ref, band, copy))
    cell = lax.broadcasted_iota(jnp.int32, (width, LANES), 0)
    place = lax.broadcasted_iota(jnp.int32, (width, LANES), 1)
    weights = jnp.where(place - LEAD == cell // FACTOR, 1.0 / (FACTOR * FACTOR), 0.0).astype(jnp.bfloat16)
    means = []
    packed = [None, None]
    for image, (count, offset) in enumerate(((REACH, 0), (DEPTH, REACH))):
        for pair in range(0, bands, 2):
            some = range(pair, pair + 2)
            group = copies[2 * (image * bands + pair) : 2 * (image * bands + pair + 2)]
            for *_, copy in group:
                copy.wait()
            sums = {}
            for plane, tile, ref, band, _ in group:
                parts = [ref[band, pl.ds(k, coarse_height, stride=FACTOR), :] for k in range(FACTOR)]
                while len(parts) > 1:
                    parts = [x + y for x, y in zip(parts[::2], parts[1::2])]
                sums[band, tile] = parts[0]
            tall = [jnp.concatenate([sums[band, tile] for tile in range(2)], axis=1) for band in some]
            means.append(split_dot(jnp.concatenate(tall, axis=0), weights))
            packed = [
                pack_image(packed[side], bool(side), (seconds, firsts)[image], some, count, offset) for side in range(2)
            ]
    means = jnp.concatenate(means, axis=0)
    get_shifts.wait()
    shift_rows = shifts[0, 0, 0].astype(jnp.float32)
    shift_cols = shifts[0, 0, 1].astype(jnp.float32)
    place = lanes_of(height // 2) & (HALF - 1)
    packed = [
        jnp.where(place == SHIFT_R, shift_rows, jnp.where(place == SHIFT_C, shift_cols, jnp.where(place == EXISTS, 1.0, x)))
        for x in packed
    ]
    to_left, to_right = [pack_means(packed[side], bool(side), means) for side in range(2)]
    coarse[...] = means
    own_meta[...] = jnp.where(lane < SLOT, shift_rows, shift_cols)
    even = is_even("col", swap_0)
    swap_0[...] = jnp.where(even, to_right, to_left)
    swap_1[...] = jnp.where(even, to_left, to_right)


def message_kernel(
    count, coarse, own_meta, got_0, got_1, up_part, down_part, _whole, swap_0, swap_1, from_left, from_right, wide
):
    other = without_ends(got_1, "col", count)
    even = is_even("col", got_0)
    from_right[...] = jnp.where(even, got_0[...], other)
    from_left[...] = jnp.where(even, other, got_0[...])
    planes_coarse, coarse_height, _ = wide.shape
    bands = planes_coarse // 2
    end = from_left.shape[0]
    coarse_width = COLUMNS // FACTOR
    lane = lanes_of()
    wides = []
    for plane in range(planes_coarse):
        half, block = divmod(plane, planes_coarse // 2)
        for step in range(coarse_height // SUB):
            own = slice(plane * coarse_height + step * SUB, plane * coarse_height + (step + 1) * SUB)
            rows = slice(block * coarse_height + step * SUB, block * coarse_height + (step + 1) * SUB)
            at = half * HALF
            left = from_left[rows, :]
            right = from_right[rows, :]
            start = LEAD - C_SECOND
            cells = turn(left, start - at - COARSE_A)
            cells = jnp.where(lane >= start + 3, turn(left, start + 3 - at - COARSE_B), cells)
            cells = jnp.where(lane >= LEAD, coarse[own, :], cells)
            start = LEAD + coarse_width
            cells = jnp.where(lane >= start, turn(right, start - at - COARSE_A), cells)
            cells = jnp.where(lane >= start + 3, turn(right, start + 3 - at - COARSE_B), cells)
            wides.append((plane, step, cells))
    for plane, step, cells in wides:
        wide[plane, step * SUB : (step + 1) * SUB, :] = cells
    row = lax.broadcasted_iota(jnp.int32, (SUB, LANES), 0)
    meta = own_meta[...]
    for message, at in ((from_left, 48), (from_right, 80)):
        first_rows = message[0:SUB, :]
        rows = jnp.broadcast_to(first_rows[:, SHIFT_R : SHIFT_R + 1], (SUB, LANES))
        cols = jnp.broadcast_to(first_rows[:, SHIFT_C : SHIFT_C + 1], (SUB, LANES))
        meta = jnp.where(lane >= at, rows, meta)
        meta = jnp.where(lane >= at + 16, cols, meta)

    def beside(rows, half):
        left = from_left[rows, :]
        right = from_right[rows, :]
        cells = jnp.zeros((SUB, LANES), jnp.float32)
        for band in range(bands):
            at = half * HALF + band * SLOT
            cells = jnp.where(lane >= band * H_BAND, turn(right, band * H_BAND - at), cells)
            cells = jnp.where(lane >= band * H_BAND + SLOT, turn(left, band * H_BAND + SLOT - at), cells)
        return cells

    even = is_even("row", meta)
    parts = []
    for part, half, near, next_rows, row_of in (
        (up_part, 0, slice(0, 8), slice(8, 16), 0),
        (down_part, 1, slice(end - 8, end), slice(end - 16, end - 8), 7),
    ):
        eight = beside(near, half)
        one = beside(next_rows, half)
        one = jnp.broadcast_to(one[row_of : row_of + 1], (SUB, LANES))
        coarse_rows = []
        for band in range(bands):
            rows = slice(0, C_SECOND) if half == 0 else slice(coarse_height - C_SECOND, coarse_height)
            second = wide[band, rows, :]
            first = turn(wide[bands + band, rows, :], HALF)
            coarse_rows.append(jnp.where(lanes_like(second) < HALF, second, first))
        parts.append([
            (part[E8:H8, :], E8), (eight, H8), (part[E1:H1, :], E1), (jnp.where(row == 0, one, meta), H1),
            (part[F4:CS, :], F4), *[(x, CS + k * C_SECOND) for k, x in enumerate(coarse_rows)],
        ])
    for (up, at), (down, _) in zip(*parts):
        even = is_even("row", up)
        swap_0[at : at + up.shape[0], :] = jnp.where(even, down, up)
        swap_1[at : at + up.shape[0], :] = jnp.where(even, up, down)


def coarse_flow_of(second, first, mask):
    def along_rows(x):
        return pltpu.roll(x, x.shape[0] - 1, 0) - pltpu.roll(x, 1, 0)

    def along_cols(x):
        return pltpu.roll(x, LANES - 1, 1) - pltpu.roll(x, 1, 1)

    bands = BANDS
    size = second.shape[0] // bands
    grad_rows = 0.125 * along_rows(second)
    grad_cols = 0.125 * along_cols(second)
    offset = 0.25 * (second - first)
    data = jnp.clip(offset, -LIMIT, LIMIT)
    yield

    def pull(grads):
        terms = data * grads
        return sum(terms[k * size : (k + 1) * size] for k in range(bands))

    def tall(x):
        return jnp.concatenate([x] * bands, axis=0)

    flow = [-mask * pull(grad_rows), -mask * pull(grad_cols)]
    extrapolated = [2.0 * x for x in flow]
    dual_rows = [0.0, 0.0]
    dual_cols = [0.0, 0.0]
    yield
    for step in range(1, STEPS):
        changes = [(along_rows(x), along_cols(x)) for x in extrapolated]
        yield
        data = data + offset + grad_rows * tall(extrapolated[0]) + grad_cols * tall(extrapolated[1])
        data = jnp.clip(data, -LIMIT, LIMIT)
        yield
        for c in range(2):
            rows = dual_rows[c] + changes[c][0]
            cols = dual_cols[c] + changes[c][1]
            scale = jnp.minimum(mask, (8.0 * ALPHA) * lax.rsqrt(rows * rows + cols * cols))
            dual_rows[c] = rows * scale
            dual_cols[c] = cols * scale
        yield
        divergences = [along_rows(dual_rows[c]) + along_cols(dual_cols[c]) for c in range(2)]
        yield
        pulls = [pull(grad_rows), pull(grad_cols)]
        yield
        for c in range(2):
            following = flow[c] + mask * ((1.0 / 64.0) * divergences[c] - pulls[c])
            extrapolated[c] = 2.0 * following - flow[c]
            flow[c] = following
        yield
    return flow


def columns_of_planes(planes):
    whole = lax.broadcasted_iota(jnp.int32, (LANES, COLUMNS), 1)
    lane = lax.broadcasted_iota(jnp.int32, (LANES, LANES), 1)
    strip = jnp.where(lane < S_MID, lane, jnp.where(lane < S_LEFT, lane + (COLUMNS - S_RIGHT), lane - LANES))
    return jnp.concatenate([x for x, wanted in ((whole, "whole"), (strip, "strip")) if wanted in planes], axis=1)


def upsample(flow, planes, target):
    column = columns_of_planes(planes)
    source = lax.broadcasted_iota(jnp.int32, column.shape, 0)
    spread = jnp.where(source - LEAD == lax.shift_right_arithmetic(column, 3), float(FACTOR), 0.0).astype(jnp.bfloat16)
    rows = flow[0].shape[0]
    wide = split_dot(UNIT * jnp.concatenate(flow, axis=0), spread)
    for c in range(2):
        for tile in range(column.shape[1] // LANES):
            target[c, tile] = wide[c * rows : (c + 1) * rows, tile * LANES : (tile + 1) * LANES]


def repeat_rows(spread, initial, cells):
    for c in range(2):
        for tile in range(initial.shape[1]):
            rows = [jnp.broadcast_to(spread[c, tile, cell : cell + 1, :], (SUB, LANES)) for cell in cells]
            initial[c, tile, GUARD : GUARD + SUB * len(cells), :] = jnp.concatenate(rows, axis=0)


def shift_whole(here, shift):
    turned = [turn_back(x, shift) for x in here]
    lane = lanes_like(here[0])
    return [
        jnp.where(lane + shift >= LANES, turned[1], turned[0]),
        jnp.where(lane + shift < 0, turned[0], turned[1]),
    ]


def edge_lanes(rows):
    lane = lanes_of(rows)
    return lane == LANES - 1, lane == 0


def columns_whole(fields, edges):
    rows = fields[0].shape[0]
    if rows not in edges:
        edges[rows] = edge_lanes(rows)
    last, first = edges[rows]
    ahead = [pltpu.roll(x, LANES - 1, 1) for x in fields]
    behind = [pltpu.roll(x, 1, 1) for x in fields]
    return [
        jnp.where(last, ahead[1], ahead[0]) - behind[0],
        ahead[1] - jnp.where(first, behind[0], behind[1]),
    ]


def rows_within(tall):
    size = tall.shape[0]
    return (pltpu.roll(tall, size - 1, 0) - pltpu.roll(tall, 1, 0))[SUB : size - SUB]


def columns_strip(field):
    return pltpu.roll(field, LANES - 1, 1) - pltpu.roll(field, 1, 1)


def strip_windows(window, centre, right, left):
    own = turn_back(window(centre[0]), centre[1])
    beyond_left = turn_back(window(left[0]), left[1])
    beyond_right = turn_back(window(right[0]), right[1])
    lane = lanes_like(own)
    beyond = jnp.where((lane >= S_LEFT) | (lane < S_MID), beyond_left, beyond_right)
    is_beyond = lane >= S_RIGHT
    of_next = is_beyond & (lane != S_RIGHT) | (lane == 0)
    of_previous = is_beyond & (lane != LANES - 1) | (lane == S_RIGHT - 1)
    change = turn(jnp.where(of_next, beyond, own), -1) - turn(jnp.where(of_previous, beyond, own), 1)
    return jnp.where(is_beyond, beyond, own), change


def fine_steps(
    rows_total, chunk, columns, initial, extrap, dual_rows, dual_cols, change, dual_data,
    offsets, grads_rows, grads_cols, data_row, masks_of, result, kept, done=lambda k: None, first_pulls=None, depth=1,
):
    assert STEPS == 3
    planes = len(offsets)
    bands = offsets[0].shape[0]
    chunks = rows_total // chunk

    def places(k, trim=(0, 0)):
        start, size = k * chunk + trim[0], chunk - sum(trim)
        return pl.ds(GUARD + start, size), pl.ds(start, size), pl.ds(data_row(k) + trim[0], size)

    def row_change(ref, c, tile, at):
        return ref[c, tile, pl.ds(at.start + 1, at.size), :] - ref[c, tile, pl.ds(at.start - 1, at.size), :]

    def clip(x):
        return jnp.clip(x, -UNIT * LIMIT, UNIT * LIMIT)

    tiles = range(planes)

    for step in range(STEPS):
        source = initial if step == 0 else extrap
        final = step == STEPS - 1

        def dual(item, source=source, step=step):
            k, c = item
            at, own, _ = places(k)
            masks = masks_of(own)
            along = columns([source[c, tile, at, :] for tile in tiles])
            values = []
            for tile in tiles:
                rows = row_change(source, c, tile, at)
                cols = along[tile]
                if step > 0:
                    rows = rows + dual_rows[c, tile, at, :]
                    cols = cols + dual_cols[c, tile, own, :]
                scale = jnp.minimum(masks[tile], lax.rsqrt(rows * rows + cols * cols))
                values.append((rows * scale, cols * scale))
            return values

        def store_dual(item, values):
            k, c = item
            for tile, (rows, cols) in enumerate(values):
                dual_rows[c, tile, places(k)[0], :] = rows
                dual_cols[c, tile, places(k)[1], :] = cols

        staggered([(k, c) for k in range(chunks) for c in range(2)], dual, store_dual, depth)
        along_of = {}

        def primal(item, step=step, final=final, along_of=along_of):
            k, tile = item
            at, own, data = places(k, kept(k) if final else (0, 0))
            if k not in along_of:
                along_of[k] = [columns([dual_cols[c, t, own, :] for t in tiles]) for c in range(2)]
            mask = masks_of(own)[tile]
            start = [initial[c, tile, at, :] for c in range(2)]
            if step > 0:
                moved = [extrap[c, tile, at, :] - start[c] for c in range(2)]
            if step == 1:
                changes = [0.5 * x for x in moved]
            if step == 2:
                changes = [change[c, tile, own, :] for c in range(2)]
            pulls = [None, None]
            duals = []
            ready = step == 0 and first_pulls is not None
            if ready:
                pulls = [first_pulls[c, tile, own, :] for c in range(2)]
            for band in range(0 if ready else bands):
                gradient = (grads_rows[tile][band, data, :], grads_cols[tile][band, data, :])
                value = offsets[tile][band, data, :]
                if step > 0:
                    earlier = clip(value) if step == 1 else dual_data[band, tile, own, :]
                    value = (value + earlier) + (gradient[0] * moved[0] + gradient[1] * moved[1])
                value = clip(value)
                duals.append(value)
                for c in range(2):
                    term = value * gradient[c]
                    pulls[c] = term if pulls[c] is None else pulls[c] + term
            flows, nexts = [], []
            for c in range(2):
                divergence = row_change(dual_rows, c, tile, at) + along_of[k][c][tile]
                moving = (mask * (1.0 / 64.0)) * divergence - pulls[c]
                total = moving if step == 0 else changes[c] + moving
                flows.append((start[c] + total) * (1.0 / UNIT) if final else total)
                nexts.append(None if final else start[c] + (total + moving))
            return flows, nexts, duals

        def store_primal(item, results, step=step, final=final):
            k, tile = item
            flows, nexts, duals = results
            at, own, _ = places(k, kept(k) if final else (0, 0))
            for c in range(2):
                if final:
                    result[c, tile, own, :] = flows[c]
                else:
                    if step > 0:
                        change[c, tile, own, :] = flows[c]
                    extrap[c, tile, at, :] = nexts[c]
            if final:
                if tile == planes - 1:
                    done(k)
            elif step > 0:
                for band in range(bands):
                    dual_data[band, tile, own, :] = duals[band]

        staggered([(k, tile) for k in range(chunks) for tile in tiles], primal, store_primal, depth)


def clear_guards(*refs):
    for ref in refs:
        rows = ref.shape[2]
        zero = jnp.zeros((GUARD, LANES), jnp.float32)
        for c in range(2):
            for tile in range(ref.shape[1]):
                ref[c, tile, 0:GUARD, :] = zero
                ref[c, tile, rows - GUARD : rows, :] = zero


def fine_scratch(bands, planes, rows):
    guarded = pltpu.VMEM((2, planes, rows + 2 * GUARD, LANES), jnp.float32)
    plain = pltpu.VMEM((2, planes, rows, LANES), jnp.float32)
    return [guarded, guarded, guarded, plain, plain, pltpu.VMEM((bands, planes, rows, LANES), jnp.float32)]


def pieces(bands, height, rows):
    assert (height - 2 * SUB) % rows == 0
    return [(band, row) for row in range(SUB, height - SUB, rows) for band in range(bands)]


def whole_terms_kernel(
    second_0, second_1, first_0, first_1, coarse, own_meta,
    offset, grad_rows, grad_cols, initial, strip_e, strip_f, up, down, moved, spread,
):
    seconds, firsts = (second_0, second_1), (first_0, first_1)
    bands, height, _ = second_0.shape
    block = 120
    coarse_height = coarse.shape[0] // (2 * bands)
    centre = shift_at(own_meta, 0, 0)
    def windows(band, row, rows):
        here = [ref[band, pl.ds(row + centre[0], rows), :].reshape(-1, LANES) for ref in seconds]
        return shift_whole(here, centre[1])

    woven = Woven(coarse_flow_of(coarse[0 : bands * coarse_height, :], coarse[bands * coarse_height :, :], 1.0))

    def strips_of(item):
        band, row = item
        rows = slice(row, row + LANES)
        return strip_own([ref[band, rows, :] for ref in seconds]), strip_own([ref[band, rows, :] for ref in firsts])

    def store_strips(item, results):
        band, row = item
        strip_e[band, row : row + LANES, :], strip_f[band, row : row + LANES, :] = results

    staggered([(band, row) for band in range(bands) for row in range(0, height, LANES)], strips_of, store_strips, 1, woven)

    ends = [(row, windows(slice(None), row, SUB)) for row in (SUB // 2, height - SUB - SUB // 2)]
    for row, values in ends:
        for tile in range(2):
            moved[tile, :, row : row + SUB, :] = values[tile].reshape(bands, SUB, LANES)

    edges = {}

    def values_of(item):
        band, row = item
        values = windows(band, row, block)
        along = columns_whole(values, edges)
        own = [ref[band, row : row + block, :] for ref in firsts]
        return values, [(0.25 * UNIT) * (x - y) for x, y in zip(values, own)], [0.125 * x for x in along]

    def store_values(item, results):
        band, row = item
        values, offsets, gradients = results
        data = slice(row + HALO, row + HALO + block)
        for tile in range(2):
            moved[tile, band, row : row + block, :] = values[tile]
            offset[tile, band, data, :] = offsets[tile]
            grad_cols[tile, band, data, :] = gradients[tile]

    staggered(pieces(bands, height, block), values_of, store_values, 1, woven)

    def gradient_of(item):
        band, row = item
        return [0.125 * rows_within(moved[tile, band, row - SUB : row + 120 + SUB, :]) for tile in range(2)]

    def store_gradient(item, results):
        band, row = item
        for tile in range(2):
            grad_rows[tile, band, row + HALO : row + HALO + 120, :] = results[tile]

    staggered(pieces(bands, height, 120), gradient_of, store_gradient, 1, woven)

    parts = []
    for band in range(bands):
        for second, first in zip(seconds, firsts):
            parts.append((
                second[band, 0:16, :], first[band, 0:8, :],
                second[band, height - 16 : height, :], first[band, height - 8 : height, :],
            ))
    for k, (second_top, first_top, second_end, first_end) in enumerate(parts):
        up[E8 + 8 * k : E8 + 8 * k + 8, :] = second_top[0:8]
        up[E1 + k : E1 + k + 1, :] = second_top[8:9]
        up[F4 + 4 * k : F4 + 4 * k + 4, :] = first_top[0:4]
        down[E8 + 8 * k : E8 + 8 * k + 8, :] = second_end[8:16]
        down[E1 + k : E1 + k + 1, :] = second_end[7:8]
        down[F4 + 4 * k : F4 + 4 * k + 4, :] = first_end[4:8]
    for target in (up, down):
        for start, end in ((H8, E1), (H1, F4), (CS, ROW_MESSAGE)):
            target[start:end, :] = jnp.zeros((end - start, LANES), jnp.float32)

    upsample(woven.finish(), ("whole",), spread)
    clear_guards(initial)
    rows_total = initial.shape[2] - 2 * GUARD
    repeat_rows(spread, initial, [BEGIN // FACTOR + k for k in range(rows_total // SUB)])


def whole_steps_kernel(
    initial, offset, grad_rows, grad_cols, result, extrap, dual_rows, dual_cols, change, dual_data
):
    rows_total = result.shape[2]
    clear_guards(extrap, dual_rows)
    chunk = 16
    edges = {}
    fine_steps(
        rows_total, chunk, lambda fields: columns_whole(fields, edges),
        initial, extrap, dual_rows, dual_cols, change, dual_data,
        *[[ref.at[tile] for tile in range(2)] for ref in (offset, grad_rows, grad_cols)],
        lambda k: HALO + BEGIN + k * chunk, lambda own: (1.0, 1.0), result,
        lambda k: (SUB * (k == 0), SUB * (k == rows_total // chunk - 1)), depth=3,
    )


def strip_kernel(
    count, strip_e, strip_f, from_left, from_right, wide, own_message, whole,
    middle, strip_out, first_ends, offset, grad_rows, grad_cols,
    moved, result, spread, initial, extrap, dual_rows, dual_cols, change, dual_data,
):
    bands, height, _ = strip_e.shape
    block = 120
    coarse_height = height // FACTOR
    coarse_width = COLUMNS // FACTOR
    rows_total = height - 2 * BEGIN
    lane = lanes_of()
    centre, right, left = shifts_of(own_message)
    has_left, has_right = neighbours("col", count)
    exists = jnp.where(lane < S_RIGHT, 1.0, jnp.where(lane < S_LEFT, has_right, has_left))

    def tall_factor(rows):
        return 0.125 * jnp.concatenate([exists] * (rows // SUB), axis=0)

    mask = jnp.where(lane < LEAD, has_left, jnp.where(lane < LEAD + coarse_width, 1.0, has_right))
    mask = jnp.concatenate([mask] * (coarse_height // SUB), axis=0)
    cells = [wide[k * bands : (k + 1) * bands].reshape(bands * coarse_height, LANES) for k in range(2)]
    woven = Woven(coarse_flow_of(*cells, mask))

    def halves(row, rows):
        half = row // (height // 2)
        start = row - half * (height // 2)
        return half, slice(start, start + rows)

    def second_of(item):
        band, row = item
        half, message = halves(row, LANES)
        return strip_second(strip_e[band, row : row + LANES, :], from_left, from_right, message, half, band)

    def store_second(item, value):
        band, row = item
        strip_out[band, row : row + LANES, :] = value

    staggered([(band, row) for row in range(0, height, LANES) for band in range(bands)], second_of, store_second, 1, woven)

    def first_of(band, row, rows):
        half, message = halves(row, rows)
        return strip_first(strip_f[band, row : row + rows, :], from_left, from_right, message, half, band)

    firsts = [(end, band, first_of(band, (0, height - SUB)[end], SUB)) for end in range(2) for band in range(bands)]
    for end, band, value in firsts:
        first_ends[end, band] = value

    def windows(band, row, rows):
        return strip_windows(
            lambda shift: strip_out[band, pl.ds(row + shift, rows), :].reshape(-1, LANES), centre, right, left
        )

    ends = [(row, windows(slice(None), row, SUB)[0]) for row in (SUB // 2, height - SUB - SUB // 2)]
    for row, value in ends:
        moved[:, row : row + SUB, :] = value.reshape(bands, SUB, LANES)

    factor = tall_factor(block)

    def values_of(item):
        band, row = item
        value, along = windows(band, row, block)
        return value, (0.25 * UNIT) * (value - first_of(band, row, block)), factor * along

    def store_values(item, results):
        band, row = item
        data = slice(row + HALO, row + HALO + block)
        moved[band, row : row + block, :], offset[band, data, :], grad_cols[band, data, :] = results

    staggered(pieces(bands, height, block), values_of, store_values, 1, woven)

    def gradient_of(item):
        band, row = item
        return factor * rows_within(moved[band, row - SUB : row + block + SUB, :])

    def store_gradient(item, value):
        band, row = item
        grad_rows[band, row + HALO : row + HALO + block, :] = value

    staggered(pieces(bands, height, block), gradient_of, store_gradient, 1, woven)

    upsample(woven.finish(), ("strip",), spread)
    clear_guards(initial, extrap, dual_rows)
    repeat_rows(spread, initial, [BEGIN // FACTOR + k for k in range(rows_total // SUB)])

    chunk = 88
    masks = jnp.concatenate([exists] * (chunk // SUB), axis=0)
    fine_steps(
        rows_total, chunk, lambda fields: [columns_strip(fields[0])],
        initial, extrap, dual_rows, dual_cols, change, dual_data, [offset], [grad_rows], [grad_cols],
        lambda k: HALO + BEGIN + k * chunk, lambda own: (masks[: own.size],), result,
        lambda k: (SUB * (k == 0), SUB * (k == rows_total // chunk - 1)),
    )
    join(whole, result.at[:, 0], middle, slice(SUB, rows_total - SUB))


def join(whole, strip, target, rows):
    lane = lanes_of(rows.stop - rows.start)
    values = []
    for c in range(2):
        edge = strip[c, rows, :]
        start = jnp.where(lane < EDGE, edge, whole[c, 0, rows, :])
        values.append((start, jnp.where(lane >= LANES - EDGE, turn(edge, S_TURN), whole[c, 1, rows, :])))
    for c in range(2):
        target[c, rows, 0:LANES], target[c, rows, LANES:COLUMNS] = values[c]


def outer_kernel(
    counts, second_0, second_1, first_0, first_1, strip_e, first_ends, wide, got_1, got_0, middle, own_message,
    _wo, _wr, _wc, _so, _sr, _sc,
    flow_out, coarse_out, whole_offset, whole_rows, whole_cols, strip_offset, strip_rows, strip_cols,
    from_up, from_down, extended, tall, spread, masks, result, joined, coarse_result, pulls, sems,
    initial, extrap, dual_rows, dual_cols, change, dual_data,
):
    bands, height, _ = second_0.shape
    coarse_height = height // FACTOR
    coarse_width = COLUMNS // FACTOR
    rows_total = 2 * EACH
    lane = lanes_of()

    put_middle = pltpu.make_async_copy(
        middle.at[:, pl.ds(MARGIN - BEGIN, height - 2 * MARGIN), :],
        flow_out.at[:, pl.ds(MARGIN, height - 2 * MARGIN), :],
        sems.at[0],
    )
    put_middle.start()
    own, one, other = [shifts_of(message) for message in (own_message, got_0, got_1)]
    odd = lax.axis_index("row") % 2

    def of_row(for_even, for_odd):
        return [tuple(jnp.where(odd == 0, x, y) for x, y in zip(*pair)) for pair in zip(for_even, for_odd)]

    above, below = of_row(other, one), of_row(one, other)

    other = without_ends(got_1, "row", counts[0])
    even = is_even("row", got_0)
    from_down[...] = jnp.where(even, got_0[...], other)
    from_up[...] = jnp.where(even, other, got_0[...])

    has_up, has_down = neighbours("row", counts[0])
    has_left, has_right = neighbours("col", counts[1])
    exists = jnp.where(lane < S_RIGHT, 1.0, jnp.where(lane < S_LEFT, has_right, has_left))

    zero = jnp.zeros((SUB, LANES), jnp.float32)
    tall_rows = coarse_height + 2 * LEAD
    parts = []
    fill = jnp.zeros((LEAD - C_SECOND, LANES), jnp.float32)
    for plane in range(2 * bands):
        at = CS + C_SECOND * (plane % bands)
        ends = [turn(message[at : at + C_SECOND, :], HALF * (plane // bands)) for message in (from_up, from_down)]
        parts.append([fill, ends[0], wide[plane], ends[1], fill])
    for plane, values in enumerate(parts):
        tall[plane] = jnp.concatenate(values, axis=0)
    across = jnp.where(lane < LEAD, has_left, jnp.where(lane < LEAD + coarse_width, 1.0, has_right))
    mask = jnp.concatenate([across * has_up] + [across] * (coarse_height // SUB) + [across * has_down], axis=0)
    for end in range(2):
        message = (from_up, from_down)[end]
        beside = message[H8 : H8 + 8, :]
        beside_one = jnp.broadcast_to(message[H1 : H1 + 1, :], (SUB, LANES))
        parts = []
        for band in range(bands):
            eights = [message[E8 + 8 * k : E8 + 8 * k + 8, :] for k in (2 * band, 2 * band + 1)]
            ones = [jnp.broadcast_to(message[E1 + k : E1 + k + 1, :], (SUB, LANES)) for k in (2 * band, 2 * band + 1)]
            eights.append(strip_halo(strip_own(eights), beside, band, 0, REACH))
            ones.append(strip_halo(strip_own(ones), beside_one, band, 0, REACH))
            for tile, (eight, one) in enumerate(zip(eights, ones)):
                source = (second_0, second_1, strip_e)[tile]
                if end == 0:
                    parts.append((tile, band, [one, eight, source[band, 0:24, :]]))
                else:
                    parts.append((tile, band, [source[band, height - 24 : height, :], eight, one]))
        for tile, band, values in parts:
            extended[end, tile, band] = jnp.concatenate(values, axis=0)
    cells = [tall[k * bands : (k + 1) * bands].reshape(bands * tall_rows, LANES) for k in range(2)]
    woven = Woven(coarse_flow_of(*cells, mask))
    edges = {}
    rows_data = whole_offset.shape[2]
    exists_tall = jnp.concatenate([exists] * bands, axis=0)

    def rows_of(halo, end):
        if halo:
            return slice(0, SUB) if end == 0 else slice(rows_data - SUB, rows_data)
        return slice(HALO, HALO + SUB) if end == 0 else slice(rows_data - HALO - SUB, rows_data - HALO)

    def values_of(item):
        halo, end = item
        message = (from_up, from_down)[end]
        base = (SUB, 3 * SUB)[end] if halo else 2 * SUB
        shifts = (above, below)[end] if halo else own
        factor = 0.125 * (has_up, has_down)[end] if halo else 0.125

        def here(tile, shift):
            return extended[end, tile, :, pl.ds(base + shift, SUB), :].reshape(-1, LANES)

        def down_up(tile, shift):
            return here(tile, shift + 1) - here(tile, shift - 1)

        own_rows = slice(0, SUB) if end == 0 else slice(height - SUB, height)
        if halo:
            firsts = [[], [], []]
            for band in range(bands):
                eights = []
                for k in (2 * band, 2 * band + 1):
                    four = message[F4 + 4 * k : F4 + 4 * k + 4, :]
                    eights.append(jnp.concatenate([four, four], axis=0))
                eights.append(strip_halo(strip_own(eights), message[H8 : H8 + 8, :], band, REACH, DEPTH))
                for tile in range(3):
                    firsts[tile].append(eights[tile])
            firsts = [jnp.concatenate(x, axis=0) for x in firsts]
        else:
            firsts = [x.reshape(-1, LANES) for x in (first_0[:, own_rows, :], first_1[:, own_rows, :], first_ends[end])]
        centre = shifts[0]
        values = shift_whole([here(tile, centre[0]) for tile in range(2)], centre[1])
        changes = shift_whole([down_up(tile, centre[0]) for tile in range(2)], centre[1])
        along = columns_whole(values, edges)
        value, across_cols = strip_windows(lambda shift: here(2, shift), *shifts)
        change_rows, _ = strip_windows(lambda shift: down_up(2, shift), *shifts)
        return (
            [(0.25 * UNIT) * (x - y) for x, y in zip([*values, value], firsts)],
            [*[factor * x for x in changes], (factor * exists_tall) * change_rows],
            [*[factor * x for x in along], (factor * exists_tall) * across_cols],
        )

    def store_values(item, results):
        rows = rows_of(*item)
        for values, whole, strip in zip(
            results, (whole_offset, whole_rows, whole_cols), (strip_offset, strip_rows, strip_cols)
        ):
            values = [x.reshape(bands, SUB, LANES) for x in values]
            for tile in range(2):
                whole[tile, :, rows, :] = values[tile]
            strip[:, rows, :] = values[2]

    staggered([(halo, end) for halo in (True, False) for end in range(2)], values_of, store_values, 1, woven)

    def data_row(k):
        return k // 2 * (rows_data - EACH) + k % 2 * (EACH // 2)

    offsets = [whole_offset.at[0], whole_offset.at[1], strip_offset]
    grads_rows = [whole_rows.at[0], whole_rows.at[1], strip_rows]
    grads_cols = [whole_cols.at[0], whole_cols.at[1], strip_cols]

    def pulls_of(item):
        k, tile = item
        data = pl.ds(data_row(2 * k), EACH)
        duals = [jnp.clip(offsets[tile][band, data, :], -UNIT * LIMIT, UNIT * LIMIT) for band in range(bands)]
        return [
            sum(duals[band] * grads[tile][band, data, :] for band in range(bands)) for grads in (grads_rows, grads_cols)
        ]

    def store_pulls(item, values):
        k, tile = item
        for c in range(2):
            pulls[c, tile, k * EACH : (k + 1) * EACH, :] = values[c]

    staggered([(k, tile) for k in range(2) for tile in range(3)], pulls_of, store_pulls, 1, woven)

    flow = woven.finish()
    for c in range(2):
        coarse_result[c] = turn(flow[c][LEAD : LEAD + coarse_height], -LEAD)[:, :coarse_width]
    put_coarse = pltpu.make_async_copy(coarse_result, coarse_out, sems.at[1])
    put_coarse.start()
    upsample(flow, ("whole", "strip"), spread)
    clear_guards(initial, extrap, dual_rows)
    each = EACH // SUB
    repeat_rows(
        spread, initial,
        [LEAD - 1 + k for k in range(each)] + [tall_rows - LEAD + 1 - each + k for k in range(each)],
    )

    for i, value in enumerate((jnp.ones((SUB, LANES), jnp.float32), exists)):
        masks[i] = jnp.concatenate([value * has_up] + [value] * (rows_total // SUB - 2) + [value * has_down], axis=0)

    def masks_of(rows):
        whole = masks[0, rows, :]
        return (whole, whole, masks[1, rows, :])

    chunk = EACH // 2
    edges = {}
    puts = [
        pltpu.make_async_copy(
            joined.at[:, pl.ds(k * EACH + SUB, MARGIN), :],
            flow_out.at[:, pl.ds(k * (height - MARGIN), MARGIN), :],
            sems.at[2 + k],
        )
        for k in range(2)
    ]

    def finish(k):
        if k % 2 == 1:
            at = k // 2 * EACH + SUB
            join(result, result.at[:, 2], joined, slice(at, at + MARGIN))
            puts[k // 2].start()

    fine_steps(
        rows_total, chunk, lambda fields: columns_whole(fields[:2], edges) + [columns_strip(fields[2])],
        initial, extrap, dual_rows, dual_cols, change, dual_data,
        offsets, grads_rows, grads_cols, data_row, masks_of, result,
        lambda k: (SUB, 0) if k % 2 == 0 else (0, SUB), finish, pulls, depth=2,
    )
    put_middle.wait()
    put_coarse.wait()
    for put in puts:
        put.wait()


def swap_with(message, axis, start):
    names = ("row", "col")
    sizes = [lax.axis_size(name) for name in names]
    along = names.index(axis)
    count, others = sizes[along], sizes[1 - along]

    def number(place, other):
        row, col = (place, other) if along == 0 else (other, place)
        return row * sizes[1] + col

    pairs = [(number(i, k), number(i + 1, k)) for i in range(start, count - 1, 2) for k in range(others)]
    if start and axis == "col":
        pairs += [(number(i, k), number(i, k + 1)) for i in (0, count - 1) for k in range(0, others, 2)]
    elif start:
        pairs += [(number(0, k), number(count - 1, k)) for k in range(others)]
    return lax.ppermute(message, names, pairs + [(j, i) for i, j in pairs])


def local(frame_first, frame_second, shifts):
    bands, height, width = frame_first.shape
    assert bands == 4 and width == COLUMNS and height % LANES == 0
    assert lax.axis_size("row") % 2 == 0 and lax.axis_size("col") % 2 == 0
    coarse_height = height // FACTOR
    coarse_width = width // FACTOR
    vmem = pl.BlockSpec(memory_space=pltpu.VMEM)
    hbm = pl.BlockSpec(memory_space=pltpu.HBM)
    tall_rows = coarse_height + 2 * LEAD
    inner_rows = height - 2 * BEGIN

    def shape(*sizes):
        return jax.ShapeDtypeStruct(sizes, jnp.float32)

    def scratch(*sizes):
        return pltpu.VMEM(sizes, jnp.float32)

    def call(kernel, name, arguments, outs, scratches=(), flops=1_000_000, **more):
        more = {"in_specs": [vmem] * len(arguments), "out_specs": (vmem,) * len(outs), **more}
        return pl.pallas_call(
            kernel,
            out_shape=tuple(outs),
            scratch_shapes=list(scratches),
            compiler_params=pltpu.CompilerParams(vmem_limit_bytes=24 * 1024 * 1024),
            cost_estimate=pl.CostEstimate(flops=flops, bytes_accessed=1_000_000, transcendentals=0),
            name=name,
            **more,
        )(*arguments)

    plane = shape(bands, height, LANES)
    column_message = shape(height // 2, LANES)
    row_message = shape(ROW_MESSAGE, LANES)
    whole_data = shape(2, bands, height + 2 * HALO, LANES)
    strip_data = shape(bands, height + 2 * HALO, LANES)

    *frames, coarse, swap_0, swap_1, own_meta = call(
        first_kernel,
        "means_and_message",
        [pltpu.with_memory_space_constraint(x, pltpu.HBM) for x in (frame_second, frame_first, shifts)],
        [*[plane] * 4, shape(2 * bands * coarse_height, LANES), column_message, column_message, shape(SUB, LANES)],
        [
            pltpu.SMEM((1, 1, 2), jnp.int32),
            pltpu.SemaphoreType.DMA((2, bands, 2)),
            pltpu.SemaphoreType.DMA,
        ],
        in_specs=[hbm] * 3,
    )
    got_0 = swap_with(swap_0, "col", 0)
    got_1 = swap_with(swap_1, "col", 1)

    *whole_terms, initial, strip_e, strip_f, up_part, down_part = call(
        whole_terms_kernel,
        "whole_terms",
        [*frames, coarse, own_meta],
        [
            *[whole_data] * 3, shape(2, 2, inner_rows + 2 * GUARD, LANES),
            plane, plane, row_message, row_message,
        ],
        [
            scratch(2, bands, height, LANES), scratch(2, 2, coarse_height, LANES),
        ],
        flops=8_000_000,
    )
    (whole,) = call(
        whole_steps_kernel,
        "whole_steps",
        [initial, *whole_terms],
        [shape(2, 2, inner_rows, LANES)],
        fine_scratch(bands, 2, inner_rows)[1:],
        flops=20_000_000,
    )

    swap_0, swap_1, from_left, from_right, wide = call(
        functools.partial(message_kernel, lax.axis_size("col")),
        "row_messages",
        [coarse, own_meta, got_0, got_1, up_part, down_part, whole],
        [row_message, row_message, column_message, column_message, shape(2 * bands, coarse_height, LANES)],
    )
    got_1 = swap_with(swap_1, "row", 1)
    got_0 = swap_with(swap_0, "row", 0)

    middle, strip_e, first_ends, *strip_terms = call(
        functools.partial(strip_kernel, lax.axis_size("col")),
        "strip",
        [strip_e, strip_f, from_left, from_right, wide, swap_0, whole],
        [shape(2, inner_rows, width), plane, shape(2, bands, SUB, LANES), *[strip_data] * 3],
        [
            scratch(bands, height, LANES),
            scratch(2, 1, inner_rows, LANES),
            scratch(2, 1, coarse_height, LANES),
            *fine_scratch(bands, 1, inner_rows),
        ],
        flops=16_000_000,
    )

    flow, coarse_flow, *_ = call(
        functools.partial(outer_kernel, (lax.axis_size("row"), lax.axis_size("col"))),
        "outer_rows",
        [
            *frames, strip_e, first_ends, wide, got_1, got_0, middle, swap_0,
            *whole_terms, *strip_terms,
        ],
        [shape(2, height, width), shape(2, coarse_height, coarse_width), *[whole_data] * 3, *[strip_data] * 3],
        [
            scratch(ROW_MESSAGE, LANES),
            scratch(ROW_MESSAGE, LANES),
            scratch(2, 3, bands, 40, LANES),
            scratch(2 * bands, tall_rows, LANES),
            scratch(2, 3, tall_rows, LANES),
            scratch(2, 2 * EACH, LANES),
            scratch(2, 3, 2 * EACH, LANES),
            scratch(2, 2 * EACH, width),
            scratch(2, coarse_height, coarse_width),
            scratch(2, 3, 2 * EACH, LANES),
            pltpu.SemaphoreType.DMA((4,)),
            *fine_scratch(bands, 3, 2 * EACH),
        ],
        out_specs=(hbm, hbm) + (vmem,) * 6,
        input_output_aliases={11 + k: 2 + k for k in range(6)},
    )
    return (flow, coarse_flow)


def solution(mesh):
    return jax.shard_map(
        local,
        mesh=mesh,
        in_specs=(P(None, "row", "col"), P(None, "row", "col"), P("row", "col", None)),
        out_specs=(P(None, "row", "col"), P(None, "row", "col")),
        check_vma=False,
    )
```

```python
import functools

import jax
import jax.numpy as jnp
from jax import lax
from jax.experimental import pallas as pl
from jax.experimental.pallas import tpu as pltpu
from jax.sharding import PartitionSpec as P

FACTOR = 8
MAXD = 4
BANDS = 4
STEPS = 3
LANES = 128
COLUMNS = 2 * LANES
HALF = 64
SUB = 8
DEPTH = 4
REACH = DEPTH + MAXD + 1
SLOT = 16
C_SECOND = 6
C_FIRST = 5
LEAD = 8
MARGIN = 48
EDGE = 46
GUARD = 8
HALO = 8
BEGIN = 40
EACH = MARGIN + 16
LIMIT = 0.3
ALPHA = 0.3
UNIT = 0.125 / ALPHA

S_MID = 55
S_RIGHT = 110
S_LEFT = LANES - REACH
S_TURN = COLUMNS - S_RIGHT - LANES

E8 = 0
H8 = 64
E1 = 72
H1 = 80
META = 81
F4 = 88
CS = 120
ROW_MESSAGE = 144
H_BAND = 32

COARSE_A = REACH + DEPTH
COARSE_B = SLOT + REACH + DEPTH
SHIFT_R = 2 * SLOT + REACH + DEPTH
SHIFT_C = SHIFT_R + 1
EXISTS = SHIFT_R + 2


def lanes_of(rows=SUB):
    return lax.broadcasted_iota(jnp.int32, (rows, LANES), 1)


def lanes_like(x):
    return lax.broadcasted_iota(jnp.int32, x.shape, 1)


def turn(x, amount):
    amount = amount % LANES
    return x if amount == 0 else pltpu.roll(x, amount, 1)


def turn_back(x, shift):
    return pltpu.roll(x, lax.rem(LANES - shift, LANES), 1)


def split_dot(x, exact):
    high = x.astype(jnp.bfloat16)
    rest = x - high.astype(jnp.float32)
    middle = rest.astype(jnp.bfloat16)
    low = (rest - middle.astype(jnp.float32)).astype(jnp.bfloat16)
    parts = [jnp.dot(part, exact, preferred_element_type=jnp.float32) for part in (low, middle, high)]
    return parts[0] + parts[1] + parts[2]


def neighbours(axis, count):
    place = lax.axis_index(axis)
    return jnp.where(place > 0, 1.0, 0.0), jnp.where(place < count - 1, 1.0, 0.0)


def shift_at(ref, row, lane):
    numbers = ref[row : row + 1, :].astype(jnp.int32)
    return numbers[0, lane], numbers[0, lane + SLOT]


def shifts_of(message):
    return [shift_at(message, META, lane) for lane in (0, 80, 48)]


def is_even(axis, like):
    return jnp.broadcast_to(lax.axis_index(axis) % 2, like.shape) == 0


def without_ends(message, axis, count):
    place = jnp.broadcast_to(lax.axis_index(axis), message.shape)
    return jnp.where((place > 0) & (place < count - 1), message[...], 0.0)


def staggered(items, compute, store, depth, woven=None):
    pending = []
    for item in items:
        pending.append((item, compute(item)))
        if woven is not None:
            woven.advance()
        if len(pending) > depth:
            store(*pending.pop(0))
    for entry in pending:
        store(*entry)


class Woven:
    def __init__(self, stages):
        self.stages = stages
        self.result = None

    def advance(self):
        try:
            next(self.stages)
            return True
        except StopIteration as end:
            self.result = end.value if self.result is None else self.result
            return False

    def finish(self):
        while self.advance():
            pass
        return self.result


def pack_image(packed, to_right, planes, some, count, offset):
    _, height, _ = planes[0].shape
    plane = planes[int(to_right)]
    start = LANES - count if to_right else 0
    length = height // 2
    lane = lanes_of(length)
    for half in range(2):
        for band in some:
            at = half * HALF + band * SLOT + offset
            cells = turn(plane[band, half * length : (half + 1) * length, :], at - start)
            packed = cells if packed is None else jnp.where((lane >= at) & (lane < at + count), cells, packed)
    return packed


def pack_means(packed, to_right, means):
    length = packed.shape[0]
    start = LEAD + COLUMNS // FACTOR - C_SECOND if to_right else LEAD
    lane = lanes_of(length)
    for half in range(2):
        cells = means[half * length : (half + 1) * length]
        for at, first in ((half * HALF + COARSE_A, start), (half * HALF + COARSE_B, start + 3)):
            packed = jnp.where((lane >= at) & (lane < at + 3), turn(cells, at - first), packed)
    return packed


def strip_second(base, from_left, from_right, rows, half, band):
    at = half * HALF + band * SLOT
    lane = lanes_like(base)
    cells = jnp.where(lane >= S_RIGHT, turn(from_right[rows, :], S_RIGHT - at), base)
    return jnp.where(lane >= S_LEFT, turn(from_left[rows, :], S_LEFT - at), cells)


def strip_first(base, from_left, from_right, rows, half, band):
    at = half * HALF + band * SLOT + REACH
    lane = lanes_like(base)
    cells = jnp.where(lane >= S_RIGHT, turn(from_right[rows, :], S_RIGHT - at), base)
    return jnp.where(lane >= S_LEFT, turn(from_left[rows, :], LANES - DEPTH - at), cells)


def strip_halo(base, beside, band, start, count):
    at = band * H_BAND + start
    lane = lanes_like(base)
    cells = jnp.where(lane >= S_RIGHT, turn(beside, S_RIGHT - at), base)
    return jnp.where(lane >= S_LEFT, turn(beside, LANES - count - at - SLOT), cells)


def strip_own(planes):
    return jnp.where(lanes_like(planes[0]) < S_MID, planes[0], turn(planes[1], -S_TURN))


def first_kernel(
    second_hbm, first_hbm, shifts_hbm, second_0, second_1, first_0, first_1, coarse, swap_0, swap_1, own_meta,
    shifts, sems, shift_sem,
):
    seconds, firsts = (second_0, second_1), (first_0, first_1)
    bands, height, _ = second_0.shape
    width = COLUMNS
    coarse_height = height // FACTOR
    lane = lanes_of()
    get_shifts = pltpu.make_async_copy(shifts_hbm, shifts, shift_sem)
    get_shifts.start()
    copies = []
    for image, (source, refs) in enumerate(((second_hbm, seconds), (first_hbm, firsts))):
        for band in range(bands):
            for tile, ref in enumerate(refs):
                halves = []
                for half in range(2):
                    rows = pl.ds(half * (height // 2), height // 2)
                    copy = pltpu.make_async_copy(
                        source.at[band, rows, pl.ds(tile * LANES, LANES)], ref.at[band, rows], sems.at[image, band, tile, half]
                    )
                    copy.start()
                    halves.append(copy)
                copies.append((image * bands + band, tile, ref, band, halves))
    cell = lax.broadcasted_iota(jnp.int32, (width, LANES), 0)
    place = lax.broadcasted_iota(jnp.int32, (width, LANES), 1)
    weights = jnp.where(place - LEAD == cell // FACTOR, 1.0 / (FACTOR * FACTOR), 0.0).astype(jnp.bfloat16)
    means = []
    packed = [None, None]
    for image, (count, offset) in enumerate(((REACH, 0), (DEPTH, REACH))):
        for pair in range(0, bands, 2):
            some = range(pair, pair + 2)
            group = copies[2 * (image * bands + pair) : 2 * (image * bands + pair + 2)]
            for *_, halves in group:
                for copy in halves:
                    copy.wait()
            sums = {}
            for plane, tile, ref, band, _ in group:
                parts = [ref[band, pl.ds(k, coarse_height, stride=FACTOR), :] for k in range(FACTOR)]
                while len(parts) > 1:
                    parts = [x + y for x, y in zip(parts[::2], parts[1::2])]
                sums[band, tile] = parts[0]
            tall = [jnp.concatenate([sums[band, tile] for tile in range(2)], axis=1) for band in some]
            means.append(split_dot(jnp.concatenate(tall, axis=0), weights))
            packed = [
                pack_image(packed[side], bool(side), (seconds, firsts)[image], some, count, offset) for side in range(2)
            ]
    means = jnp.concatenate(means, axis=0)
    get_shifts.wait()
    shift_rows = shifts[0, 0, 0].astype(jnp.float32)
    shift_cols = shifts[0, 0, 1].astype(jnp.float32)
    place = lanes_of(height // 2) & (HALF - 1)
    packed = [
        jnp.where(place == SHIFT_R, shift_rows, jnp.where(place == SHIFT_C, shift_cols, jnp.where(place == EXISTS, 1.0, x)))
        for x in packed
    ]
    to_left, to_right = [pack_means(packed[side], bool(side), means) for side in range(2)]
    coarse[...] = means
    own_meta[...] = jnp.where(lane < SLOT, shift_rows, shift_cols)
    even = is_even("col", swap_0)
    swap_0[...] = jnp.where(even, to_right, to_left)
    swap_1[...] = jnp.where(even, to_left, to_right)


def message_kernel(
    count, coarse, own_meta, got_0, got_1, up_part, down_part, _whole, swap_0, swap_1, from_left, from_right, wide
):
    other = without_ends(got_1, "col", count)
    even = is_even("col", got_0)
    from_right[...] = jnp.where(even, got_0[...], other)
    from_left[...] = jnp.where(even, other, got_0[...])
    planes_coarse, coarse_height, _ = wide.shape
    bands = planes_coarse // 2
    end = from_left.shape[0]
    coarse_width = COLUMNS // FACTOR
    lane = lanes_of()
    wides = []
    for plane in range(planes_coarse):
        half, block = divmod(plane, planes_coarse // 2)
        for step in range(coarse_height // SUB):
            own = slice(plane * coarse_height + step * SUB, plane * coarse_height + (step + 1) * SUB)
            rows = slice(block * coarse_height + step * SUB, block * coarse_height + (step + 1) * SUB)
            at = half * HALF
            left = from_left[rows, :]
            right = from_right[rows, :]
            start = LEAD - C_SECOND
            cells = turn(left, start - at - COARSE_A)
            cells = jnp.where(lane >= start + 3, turn(left, start + 3 - at - COARSE_B), cells)
            cells = jnp.where(lane >= LEAD, coarse[own, :], cells)
            start = LEAD + coarse_width
            cells = jnp.where(lane >= start, turn(right, start - at - COARSE_A), cells)
            cells = jnp.where(lane >= start + 3, turn(right, start + 3 - at - COARSE_B), cells)
            wides.append((plane, step, cells))
    for plane, step, cells in wides:
        wide[plane, step * SUB : (step + 1) * SUB, :] = cells
    row = lax.broadcasted_iota(jnp.int32, (SUB, LANES), 0)
    meta = own_meta[...]
    for message, at in ((from_left, 48), (from_right, 80)):
        first_rows = message[0:SUB, :]
        rows = jnp.broadcast_to(first_rows[:, SHIFT_R : SHIFT_R + 1], (SUB, LANES))
        cols = jnp.broadcast_to(first_rows[:, SHIFT_C : SHIFT_C + 1], (SUB, LANES))
        meta = jnp.where(lane >= at, rows, meta)
        meta = jnp.where(lane >= at + 16, cols, meta)

    def beside(rows, half):
        left = from_left[rows, :]
        right = from_right[rows, :]
        cells = jnp.zeros((SUB, LANES), jnp.float32)
        for band in range(bands):
            at = half * HALF + band * SLOT
            cells = jnp.where(lane >= band * H_BAND, turn(right, band * H_BAND - at), cells)
            cells = jnp.where(lane >= band * H_BAND + SLOT, turn(left, band * H_BAND + SLOT - at), cells)
        return cells

    even = is_even("row", meta)
    parts = []
    for part, half, near, next_rows, row_of in (
        (up_part, 0, slice(0, 8), slice(8, 16), 0),
        (down_part, 1, slice(end - 8, end), slice(end - 16, end - 8), 7),
    ):
        eight = beside(near, half)
        one = beside(next_rows, half)
        one = jnp.broadcast_to(one[row_of : row_of + 1], (SUB, LANES))
        coarse_rows = []
        for band in range(bands):
            rows = slice(0, C_SECOND) if half == 0 else slice(coarse_height - C_SECOND, coarse_height)
            second = wide[band, rows, :]
            first = turn(wide[bands + band, rows, :], HALF)
            coarse_rows.append(jnp.where(lanes_like(second) < HALF, second, first))
        parts.append([
            (part[E8:H8, :], E8), (eight, H8), (part[E1:H1, :], E1), (jnp.where(row == 0, one, meta), H1),
            (part[F4:CS, :], F4), *[(x, CS + k * C_SECOND) for k, x in enumerate(coarse_rows)],
        ])
    for (up, at), (down, _) in zip(*parts):
        even = is_even("row", up)
        swap_0[at : at + up.shape[0], :] = jnp.where(even, down, up)
        swap_1[at : at + up.shape[0], :] = jnp.where(even, up, down)


def coarse_flow_of(second, first, mask):
    def along_rows(x):
        return pltpu.roll(x, x.shape[0] - 1, 0) - pltpu.roll(x, 1, 0)

    def along_cols(x):
        return pltpu.roll(x, LANES - 1, 1) - pltpu.roll(x, 1, 1)

    bands = BANDS
    size = second.shape[0] // bands
    grad_rows = 0.125 * along_rows(second)
    grad_cols = 0.125 * along_cols(second)
    offset = 0.25 * (second - first)
    data = jnp.clip(offset, -LIMIT, LIMIT)
    yield

    def pull(grads):
        terms = data * grads
        return sum(terms[k * size : (k + 1) * size] for k in range(bands))

    def tall(x):
        return jnp.concatenate([x] * bands, axis=0)

    flow = [-mask * pull(grad_rows), -mask * pull(grad_cols)]
    extrapolated = [2.0 * x for x in flow]
    dual_rows = [0.0, 0.0]
    dual_cols = [0.0, 0.0]
    yield
    for step in range(1, STEPS):
        changes = [(along_rows(x), along_cols(x)) for x in extrapolated]
        yield
        data = data + offset + grad_rows * tall(extrapolated[0]) + grad_cols * tall(extrapolated[1])
        data = jnp.clip(data, -LIMIT, LIMIT)
        yield
        for c in range(2):
            rows = dual_rows[c] + changes[c][0]
            cols = dual_cols[c] + changes[c][1]
            scale = jnp.minimum(mask, (8.0 * ALPHA) * lax.rsqrt(rows * rows + cols * cols))
            dual_rows[c] = rows * scale
            dual_cols[c] = cols * scale
        yield
        divergences = [along_rows(dual_rows[c]) + along_cols(dual_cols[c]) for c in range(2)]
        yield
        pulls = [pull(grad_rows), pull(grad_cols)]
        yield
        for c in range(2):
            following = flow[c] + mask * ((1.0 / 64.0) * divergences[c] - pulls[c])
            extrapolated[c] = 2.0 * following - flow[c]
            flow[c] = following
        yield
    return flow


def columns_of_planes(planes):
    whole = lax.broadcasted_iota(jnp.int32, (LANES, COLUMNS), 1)
    lane = lax.broadcasted_iota(jnp.int32, (LANES, LANES), 1)
    strip = jnp.where(lane < S_MID, lane, jnp.where(lane < S_LEFT, lane + (COLUMNS - S_RIGHT), lane - LANES))
    return jnp.concatenate([x for x, wanted in ((whole, "whole"), (strip, "strip")) if wanted in planes], axis=1)


def upsample(flow, planes, target):
    column = columns_of_planes(planes)
    source = lax.broadcasted_iota(jnp.int32, column.shape, 0)
    spread = jnp.where(source - LEAD == lax.shift_right_arithmetic(column, 3), float(FACTOR), 0.0).astype(jnp.bfloat16)
    rows = flow[0].shape[0]
    wide = split_dot(UNIT * jnp.concatenate(flow, axis=0), spread)
    for c in range(2):
        for tile in range(column.shape[1] // LANES):
            target[c, tile] = wide[c * rows : (c + 1) * rows, tile * LANES : (tile + 1) * LANES]


def repeat_rows(spread, initial, cells):
    for c in range(2):
        for tile in range(initial.shape[1]):
            rows = [jnp.broadcast_to(spread[c, tile, cell : cell + 1, :], (SUB, LANES)) for cell in cells]
            initial[c, tile, GUARD : GUARD + SUB * len(cells), :] = jnp.concatenate(rows, axis=0)


def shift_whole(here, shift):
    turned = [turn_back(x, shift) for x in here]
    lane = lanes_like(here[0])
    return [
        jnp.where(lane + shift >= LANES, turned[1], turned[0]),
        jnp.where(lane + shift < 0, turned[0], turned[1]),
    ]


def edge_lanes(rows):
    lane = lanes_of(rows)
    return lane == LANES - 1, lane == 0


def columns_whole(fields, edges):
    rows = fields[0].shape[0]
    if rows not in edges:
        edges[rows] = edge_lanes(rows)
    last, first = edges[rows]
    ahead = [pltpu.roll(x, LANES - 1, 1) for x in fields]
    behind = [pltpu.roll(x, 1, 1) for x in fields]
    return [
        jnp.where(last, ahead[1], ahead[0]) - behind[0],
        ahead[1] - jnp.where(first, behind[0], behind[1]),
    ]


def rows_within(tall):
    size = tall.shape[0]
    return (pltpu.roll(tall, size - 1, 0) - pltpu.roll(tall, 1, 0))[SUB : size - SUB]


def columns_strip(field):
    return pltpu.roll(field, LANES - 1, 1) - pltpu.roll(field, 1, 1)


def strip_windows(window, centre, right, left):
    own = turn_back(window(centre[0]), centre[1])
    beyond_left = turn_back(window(left[0]), left[1])
    beyond_right = turn_back(window(right[0]), right[1])
    lane = lanes_like(own)
    beyond = jnp.where((lane >= S_LEFT) | (lane < S_MID), beyond_left, beyond_right)
    is_beyond = lane >= S_RIGHT
    of_next = is_beyond & (lane != S_RIGHT) | (lane == 0)
    of_previous = is_beyond & (lane != LANES - 1) | (lane == S_RIGHT - 1)
    change = turn(jnp.where(of_next, beyond, own), -1) - turn(jnp.where(of_previous, beyond, own), 1)
    return jnp.where(is_beyond, beyond, own), change


def fine_steps(
    rows_total, chunk, columns, initial, extrap, dual_rows, dual_cols, change, dual_data,
    offsets, grads_rows, grads_cols, data_row, masks_of, result, kept, done=lambda k: None, first_pulls=None, depth=1,
):
    assert STEPS == 3
    planes = len(offsets)
    bands = offsets[0].shape[0]
    chunks = rows_total // chunk

    def places(k, trim=(0, 0)):
        start, size = k * chunk + trim[0], chunk - sum(trim)
        return pl.ds(GUARD + start, size), pl.ds(start, size), pl.ds(data_row(k) + trim[0], size)

    def row_change(ref, c, tile, at):
        return ref[c, tile, pl.ds(at.start + 1, at.size), :] - ref[c, tile, pl.ds(at.start - 1, at.size), :]

    def clip(x):
        return jnp.clip(x, -UNIT * LIMIT, UNIT * LIMIT)

    tiles = range(planes)

    for step in range(STEPS):
        source = initial if step == 0 else extrap
        final = step == STEPS - 1

        def dual(item, source=source, step=step):
            k, c = item
            at, own, _ = places(k)
            masks = masks_of(own)
            along = columns([source[c, tile, at, :] for tile in tiles])
            values = []
            for tile in tiles:
                rows = row_change(source, c, tile, at)
                cols = along[tile]
                if step > 0:
                    rows = rows + dual_rows[c, tile, at, :]
                    cols = cols + dual_cols[c, tile, own, :]
                scale = jnp.minimum(masks[tile], lax.rsqrt(rows * rows + cols * cols))
                values.append((rows * scale, cols * scale))
            return values

        def store_dual(item, values):
            k, c = item
            for tile, (rows, cols) in enumerate(values):
                dual_rows[c, tile, places(k)[0], :] = rows
                dual_cols[c, tile, places(k)[1], :] = cols

        staggered([(k, c) for k in range(chunks) for c in range(2)], dual, store_dual, depth)
        along_of = {}

        def primal(item, step=step, final=final, along_of=along_of):
            k, tile = item
            at, own, data = places(k, kept(k) if final else (0, 0))
            if k not in along_of:
                along_of[k] = [columns([dual_cols[c, t, own, :] for t in tiles]) for c in range(2)]
            mask = masks_of(own)[tile]
            start = [initial[c, tile, at, :] for c in range(2)]
            if step > 0:
                moved = [extrap[c, tile, at, :] - start[c] for c in range(2)]
            if step == 1:
                changes = [0.5 * x for x in moved]
            if step == 2:
                changes = [change[c, tile, own, :] for c in range(2)]
            pulls = [None, None]
            duals = []
            ready = step == 0 and first_pulls is not None
            if ready:
                pulls = [first_pulls[c, tile, own, :] for c in range(2)]
            for band in range(0 if ready else bands):
                gradient = (grads_rows[tile][band, data, :], grads_cols[tile][band, data, :])
                value = offsets[tile][band, data, :]
                if step > 0:
                    earlier = clip(value) if step == 1 else dual_data[band, tile, own, :]
                    value = (value + earlier) + (gradient[0] * moved[0] + gradient[1] * moved[1])
                value = clip(value)
                duals.append(value)
                for c in range(2):
                    term = value * gradient[c]
                    pulls[c] = term if pulls[c] is None else pulls[c] + term
            flows, nexts = [], []
            for c in range(2):
                divergence = row_change(dual_rows, c, tile, at) + along_of[k][c][tile]
                moving = (mask * (1.0 / 64.0)) * divergence - pulls[c]
                total = moving if step == 0 else changes[c] + moving
                flows.append((start[c] + total) * (1.0 / UNIT) if final else total)
                nexts.append(None if final else start[c] + (total + moving))
            return flows, nexts, duals

        def store_primal(item, results, step=step, final=final):
            k, tile = item
            flows, nexts, duals = results
            at, own, _ = places(k, kept(k) if final else (0, 0))
            for c in range(2):
                if final:
                    result[c, tile, own, :] = flows[c]
                else:
                    if step > 0:
                        change[c, tile, own, :] = flows[c]
                    extrap[c, tile, at, :] = nexts[c]
            if final:
                if tile == planes - 1:
                    done(k)
            elif step > 0:
                for band in range(bands):
                    dual_data[band, tile, own, :] = duals[band]

        staggered([(k, tile) for k in range(chunks) for tile in tiles], primal, store_primal, depth)


def clear_guards(*refs):
    for ref in refs:
        rows = ref.shape[2]
        zero = jnp.zeros((GUARD, LANES), jnp.float32)
        for c in range(2):
            for tile in range(ref.shape[1]):
                ref[c, tile, 0:GUARD, :] = zero
                ref[c, tile, rows - GUARD : rows, :] = zero


def fine_scratch(bands, planes, rows):
    guarded = pltpu.VMEM((2, planes, rows + 2 * GUARD, LANES), jnp.float32)
    plain = pltpu.VMEM((2, planes, rows, LANES), jnp.float32)
    return [guarded, guarded, guarded, plain, plain, pltpu.VMEM((bands, planes, rows, LANES), jnp.float32)]


def pieces(bands, height, rows):
    assert (height - 2 * SUB) % rows == 0
    return [(band, row) for row in range(SUB, height - SUB, rows) for band in range(bands)]


def whole_terms_kernel(
    second_0, second_1, first_0, first_1, coarse, own_meta,
    offset, grad_rows, grad_cols, initial, strip_e, strip_f, up, down, moved, spread,
):
    seconds, firsts = (second_0, second_1), (first_0, first_1)
    bands, height, _ = second_0.shape
    block = 40
    coarse_height = coarse.shape[0] // (2 * bands)
    centre = shift_at(own_meta, 0, 0)
    def windows(band, row, rows):
        here = [ref[band, pl.ds(row + centre[0], rows), :].reshape(-1, LANES) for ref in seconds]
        return shift_whole(here, centre[1])

    woven = Woven(coarse_flow_of(coarse[0 : bands * coarse_height, :], coarse[bands * coarse_height :, :], 1.0))

    def strips_of(item):
        band, row = item
        rows = slice(row, row + LANES)
        return strip_own([ref[band, rows, :] for ref in seconds]), strip_own([ref[band, rows, :] for ref in firsts])

    def store_strips(item, results):
        band, row = item
        strip_e[band, row : row + LANES, :], strip_f[band, row : row + LANES, :] = results

    staggered([(band, row) for band in range(bands) for row in range(0, height, LANES)], strips_of, store_strips, 1, woven)

    ends = [(row, windows(slice(None), row, SUB)) for row in (SUB // 2, height - SUB - SUB // 2)]
    for row, values in ends:
        for tile in range(2):
            moved[tile, :, row : row + SUB, :] = values[tile].reshape(bands, SUB, LANES)

    edges = {}

    def values_of(item):
        band, row = item
        values = windows(band, row, block)
        along = columns_whole(values, edges)
        own = [ref[band, row : row + block, :] for ref in firsts]
        return values, [(0.25 * UNIT) * (x - y) for x, y in zip(values, own)], [0.125 * x for x in along]

    def store_values(item, results):
        band, row = item
        values, offsets, gradients = results
        data = slice(row + HALO, row + HALO + block)
        for tile in range(2):
            moved[tile, band, row : row + block, :] = values[tile]
            offset[tile, band, data, :] = offsets[tile]
            grad_cols[tile, band, data, :] = gradients[tile]

    staggered(pieces(bands, height, block), values_of, store_values, 3, woven)

    def gradient_of(item):
        band, row = item
        return [0.125 * rows_within(moved[tile, band, row - SUB : row + 40 + SUB, :]) for tile in range(2)]

    def store_gradient(item, results):
        band, row = item
        for tile in range(2):
            grad_rows[tile, band, row + HALO : row + HALO + 40, :] = results[tile]

    staggered(pieces(bands, height, 40), gradient_of, store_gradient, 3, woven)

    parts = []
    for band in range(bands):
        for second, first in zip(seconds, firsts):
            parts.append((
                second[band, 0:16, :], first[band, 0:8, :],
                second[band, height - 16 : height, :], first[band, height - 8 : height, :],
            ))
    for k, (second_top, first_top, second_end, first_end) in enumerate(parts):
        up[E8 + 8 * k : E8 + 8 * k + 8, :] = second_top[0:8]
        up[E1 + k : E1 + k + 1, :] = second_top[8:9]
        up[F4 + 4 * k : F4 + 4 * k + 4, :] = first_top[0:4]
        down[E8 + 8 * k : E8 + 8 * k + 8, :] = second_end[8:16]
        down[E1 + k : E1 + k + 1, :] = second_end[7:8]
        down[F4 + 4 * k : F4 + 4 * k + 4, :] = first_end[4:8]
    for target in (up, down):
        for start, end in ((H8, E1), (H1, F4), (CS, ROW_MESSAGE)):
            target[start:end, :] = jnp.zeros((end - start, LANES), jnp.float32)

    upsample(woven.finish(), ("whole",), spread)
    clear_guards(initial)
    rows_total = initial.shape[2] - 2 * GUARD
    repeat_rows(spread, initial, [BEGIN // FACTOR + k for k in range(rows_total // SUB)])


def whole_steps_kernel(
    initial, offset, grad_rows, grad_cols, result, extrap, dual_rows, dual_cols, change, dual_data
):
    rows_total = result.shape[2]
    clear_guards(extrap, dual_rows)
    chunk = 16
    edges = {}
    fine_steps(
        rows_total, chunk, lambda fields: columns_whole(fields, edges),
        initial, extrap, dual_rows, dual_cols, change, dual_data,
        *[[ref.at[tile] for tile in range(2)] for ref in (offset, grad_rows, grad_cols)],
        lambda k: HALO + BEGIN + k * chunk, lambda own: (1.0, 1.0), result,
        lambda k: (SUB * (k == 0), SUB * (k == rows_total // chunk - 1)), depth=3,
    )


def strip_kernel(
    count, strip_e, strip_f, from_left, from_right, wide, own_message, whole,
    middle, strip_out, first_ends, offset, grad_rows, grad_cols,
    moved, result, spread, initial, extrap, dual_rows, dual_cols, change, dual_data,
):
    bands, height, _ = strip_e.shape
    block = 40
    coarse_height = height // FACTOR
    coarse_width = COLUMNS // FACTOR
    rows_total = height - 2 * BEGIN
    lane = lanes_of()
    centre, right, left = shifts_of(own_message)
    has_left, has_right = neighbours("col", count)
    exists = jnp.where(lane < S_RIGHT, 1.0, jnp.where(lane < S_LEFT, has_right, has_left))

    def tall_factor(rows):
        return 0.125 * jnp.concatenate([exists] * (rows // SUB), axis=0)

    mask = jnp.where(lane < LEAD, has_left, jnp.where(lane < LEAD + coarse_width, 1.0, has_right))
    mask = jnp.concatenate([mask] * (coarse_height // SUB), axis=0)
    cells = [wide[k * bands : (k + 1) * bands].reshape(bands * coarse_height, LANES) for k in range(2)]
    woven = Woven(coarse_flow_of(*cells, mask))

    def halves(row, rows):
        half = row // (height // 2)
        start = row - half * (height // 2)
        return half, slice(start, start + rows)

    def second_of(item):
        band, row = item
        half, message = halves(row, LANES)
        return strip_second(strip_e[band, row : row + LANES, :], from_left, from_right, message, half, band)

    def store_second(item, value):
        band, row = item
        strip_out[band, row : row + LANES, :] = value

    staggered([(band, row) for row in range(0, height, LANES) for band in range(bands)], second_of, store_second, 1, woven)

    def first_of(band, row, rows):
        half, message = halves(row, rows)
        return strip_first(strip_f[band, row : row + rows, :], from_left, from_right, message, half, band)

    firsts = [(end, band, first_of(band, (0, height - SUB)[end], SUB)) for end in range(2) for band in range(bands)]
    for end, band, value in firsts:
        first_ends[end, band] = value

    def windows(band, row, rows):
        return strip_windows(
            lambda shift: strip_out[band, pl.ds(row + shift, rows), :].reshape(-1, LANES), centre, right, left
        )

    ends = [(row, windows(slice(None), row, SUB)[0]) for row in (SUB // 2, height - SUB - SUB // 2)]
    for row, value in ends:
        moved[:, row : row + SUB, :] = value.reshape(bands, SUB, LANES)

    factor = tall_factor(block)

    def values_of(item):
        band, row = item
        value, along = windows(band, row, block)
        return value, (0.25 * UNIT) * (value - first_of(band, row, block)), factor * along

    def store_values(item, results):
        band, row = item
        data = slice(row + HALO, row + HALO + block)
        moved[band, row : row + block, :], offset[band, data, :], grad_cols[band, data, :] = results

    staggered(pieces(bands, height, block), values_of, store_values, 3, woven)

    def gradient_of(item):
        band, row = item
        return factor * rows_within(moved[band, row - SUB : row + block + SUB, :])

    def store_gradient(item, value):
        band, row = item
        grad_rows[band, row + HALO : row + HALO + block, :] = value

    staggered(pieces(bands, height, block), gradient_of, store_gradient, 3, woven)

    upsample(woven.finish(), ("strip",), spread)
    clear_guards(initial, extrap, dual_rows)
    repeat_rows(spread, initial, [BEGIN // FACTOR + k for k in range(rows_total // SUB)])

    chunk = 16
    masks = jnp.concatenate([exists] * (chunk // SUB), axis=0)
    fine_steps(
        rows_total, chunk, lambda fields: [columns_strip(fields[0])],
        initial, extrap, dual_rows, dual_cols, change, dual_data, [offset], [grad_rows], [grad_cols],
        lambda k: HALO + BEGIN + k * chunk, lambda own: (masks[: own.size],), result,
        lambda k: (SUB * (k == 0), SUB * (k == rows_total // chunk - 1)), depth=4,
    )
    join(whole, result.at[:, 0], middle, slice(SUB, rows_total - SUB))


def join(whole, strip, target, rows):
    lane = lanes_of(rows.stop - rows.start)
    values = []
    for c in range(2):
        edge = strip[c, rows, :]
        start = jnp.where(lane < EDGE, edge, whole[c, 0, rows, :])
        values.append((start, jnp.where(lane >= LANES - EDGE, turn(edge, S_TURN), whole[c, 1, rows, :])))
    for c in range(2):
        target[c, rows, 0:LANES], target[c, rows, LANES:COLUMNS] = values[c]


def outer_kernel(
    counts, second_0, second_1, first_0, first_1, strip_e, first_ends, wide, got_1, got_0, middle, own_message,
    _wo, _wr, _wc, _so, _sr, _sc,
    flow_out, coarse_out, whole_offset, whole_rows, whole_cols, strip_offset, strip_rows, strip_cols,
    from_up, from_down, extended, tall, spread, masks, result, joined, coarse_result, pulls, sems,
    initial, extrap, dual_rows, dual_cols, change, dual_data,
):
    bands, height, _ = second_0.shape
    coarse_height = height // FACTOR
    coarse_width = COLUMNS // FACTOR
    rows_total = 2 * EACH
    lane = lanes_of()

    put_middle = pltpu.make_async_copy(
        middle.at[:, pl.ds(MARGIN - BEGIN, height - 2 * MARGIN), :],
        flow_out.at[:, pl.ds(MARGIN, height - 2 * MARGIN), :],
        sems.at[0],
    )
    put_middle.start()
    own, one, other = [shifts_of(message) for message in (own_message, got_0, got_1)]
    odd = lax.axis_index("row") % 2

    def of_row(for_even, for_odd):
        return [tuple(jnp.where(odd == 0, x, y) for x, y in zip(*pair)) for pair in zip(for_even, for_odd)]

    above, below = of_row(other, one), of_row(one, other)

    other = without_ends(got_1, "row", counts[0])
    even = is_even("row", got_0)
    from_down[...] = jnp.where(even, got_0[...], other)
    from_up[...] = jnp.where(even, other, got_0[...])

    has_up, has_down = neighbours("row", counts[0])
    has_left, has_right = neighbours("col", counts[1])
    exists = jnp.where(lane < S_RIGHT, 1.0, jnp.where(lane < S_LEFT, has_right, has_left))

    zero = jnp.zeros((SUB, LANES), jnp.float32)
    tall_rows = coarse_height + 2 * LEAD
    parts = []
    fill = jnp.zeros((LEAD - C_SECOND, LANES), jnp.float32)
    for plane in range(2 * bands):
        at = CS + C_SECOND * (plane % bands)
        ends = [turn(message[at : at + C_SECOND, :], HALF * (plane // bands)) for message in (from_up, from_down)]
        parts.append([fill, ends[0], wide[plane], ends[1], fill])
    for plane, values in enumerate(parts):
        tall[plane] = jnp.concatenate(values, axis=0)
    across = jnp.where(lane < LEAD, has_left, jnp.where(lane < LEAD + coarse_width, 1.0, has_right))
    mask = jnp.concatenate([across * has_up] + [across] * (coarse_height // SUB) + [across * has_down], axis=0)
    for end in range(2):
        message = (from_up, from_down)[end]
        beside = message[H8 : H8 + 8, :]
        beside_one = jnp.broadcast_to(message[H1 : H1 + 1, :], (SUB, LANES))
        parts = []
        for band in range(bands):
            eights = [message[E8 + 8 * k : E8 + 8 * k + 8, :] for k in (2 * band, 2 * band + 1)]
            ones = [jnp.broadcast_to(message[E1 + k : E1 + k + 1, :], (SUB, LANES)) for k in (2 * band, 2 * band + 1)]
            eights.append(strip_halo(strip_own(eights), beside, band, 0, REACH))
            ones.append(strip_halo(strip_own(ones), beside_one, band, 0, REACH))
            for tile, (eight, one) in enumerate(zip(eights, ones)):
                source = (second_0, second_1, strip_e)[tile]
                if end == 0:
                    parts.append((tile, band, [one, eight, source[band, 0:24, :]]))
                else:
                    parts.append((tile, band, [source[band, height - 24 : height, :], eight, one]))
        for tile, band, values in parts:
            extended[end, tile, band] = jnp.concatenate(values, axis=0)
    cells = [tall[k * bands : (k + 1) * bands].reshape(bands * tall_rows, LANES) for k in range(2)]
    woven = Woven(coarse_flow_of(*cells, mask))
    edges = {}
    rows_data = whole_offset.shape[2]
    exists_tall = jnp.concatenate([exists] * bands, axis=0)

    def rows_of(halo, end):
        if halo:
            return slice(0, SUB) if end == 0 else slice(rows_data - SUB, rows_data)
        return slice(HALO, HALO + SUB) if end == 0 else slice(rows_data - HALO - SUB, rows_data - HALO)

    def values_of(item):
        halo, end = item
        message = (from_up, from_down)[end]
        base = (SUB, 3 * SUB)[end] if halo else 2 * SUB
        shifts = (above, below)[end] if halo else own
        factor = 0.125 * (has_up, has_down)[end] if halo else 0.125

        def here(tile, shift):
            return extended[end, tile, :, pl.ds(base + shift, SUB), :].reshape(-1, LANES)

        def down_up(tile, shift):
            return here(tile, shift + 1) - here(tile, shift - 1)

        own_rows = slice(0, SUB) if end == 0 else slice(height - SUB, height)
        if halo:
            firsts = [[], [], []]
            for band in range(bands):
                eights = []
                for k in (2 * band, 2 * band + 1):
                    four = message[F4 + 4 * k : F4 + 4 * k + 4, :]
                    eights.append(jnp.concatenate([four, four], axis=0))
                eights.append(strip_halo(strip_own(eights), message[H8 : H8 + 8, :], band, REACH, DEPTH))
                for tile in range(3):
                    firsts[tile].append(eights[tile])
            firsts = [jnp.concatenate(x, axis=0) for x in firsts]
        else:
            firsts = [x.reshape(-1, LANES) for x in (first_0[:, own_rows, :], first_1[:, own_rows, :], first_ends[end])]
        centre = shifts[0]
        values = shift_whole([here(tile, centre[0]) for tile in range(2)], centre[1])
        changes = shift_whole([down_up(tile, centre[0]) for tile in range(2)], centre[1])
        along = columns_whole(values, edges)
        value, across_cols = strip_windows(lambda shift: here(2, shift), *shifts)
        change_rows, _ = strip_windows(lambda shift: down_up(2, shift), *shifts)
        return (
            [(0.25 * UNIT) * (x - y) for x, y in zip([*values, value], firsts)],
            [*[factor * x for x in changes], (factor * exists_tall) * change_rows],
            [*[factor * x for x in along], (factor * exists_tall) * across_cols],
        )

    def store_values(item, results):
        rows = rows_of(*item)
        for values, whole, strip in zip(
            results, (whole_offset, whole_rows, whole_cols), (strip_offset, strip_rows, strip_cols)
        ):
            values = [x.reshape(bands, SUB, LANES) for x in values]
            for tile in range(2):
                whole[tile, :, rows, :] = values[tile]
            strip[:, rows, :] = values[2]

    staggered([(halo, end) for halo in (True, False) for end in range(2)], values_of, store_values, 1, woven)

    chunk = 16
    per = EACH // chunk

    def data_row(k):
        return k // per * (rows_data - EACH) + k % per * chunk

    offsets = [whole_offset.at[0], whole_offset.at[1], strip_offset]
    grads_rows = [whole_rows.at[0], whole_rows.at[1], strip_rows]
    grads_cols = [whole_cols.at[0], whole_cols.at[1], strip_cols]

    def pulls_of(item):
        k, tile = item
        data = pl.ds(k * (rows_data - EACH), EACH)
        duals = [jnp.clip(offsets[tile][band, data, :], -UNIT * LIMIT, UNIT * LIMIT) for band in range(bands)]
        return [
            sum(duals[band] * grads[tile][band, data, :] for band in range(bands)) for grads in (grads_rows, grads_cols)
        ]

    def store_pulls(item, values):
        k, tile = item
        for c in range(2):
            pulls[c, tile, k * EACH : (k + 1) * EACH, :] = values[c]

    staggered([(k, tile) for k in range(2) for tile in range(3)], pulls_of, store_pulls, 1, woven)

    flow = woven.finish()
    for c in range(2):
        coarse_result[c] = turn(flow[c][LEAD : LEAD + coarse_height], -LEAD)[:, :coarse_width]
    put_coarse = pltpu.make_async_copy(coarse_result, coarse_out, sems.at[1])
    put_coarse.start()
    upsample(flow, ("whole", "strip"), spread)
    clear_guards(initial, extrap, dual_rows)
    each = EACH // SUB
    repeat_rows(
        spread, initial,
        [LEAD - 1 + k for k in range(each)] + [tall_rows - LEAD + 1 - each + k for k in range(each)],
    )

    for i, value in enumerate((jnp.ones((SUB, LANES), jnp.float32), exists)):
        masks[i] = jnp.concatenate([value * has_up] + [value] * (rows_total // SUB - 2) + [value * has_down], axis=0)

    def masks_of(rows):
        whole = masks[0, rows, :]
        return (whole, whole, masks[1, rows, :])

    edges = {}
    puts = [
        pltpu.make_async_copy(
            joined.at[:, pl.ds(k * EACH + SUB, MARGIN), :],
            flow_out.at[:, pl.ds(k * (height - MARGIN), MARGIN), :],
            sems.at[2 + k],
        )
        for k in range(2)
    ]

    def finish(k):
        if k % per == per - 1:
            at = k // per * EACH + SUB
            join(result, result.at[:, 2], joined, slice(at, at + MARGIN))
            puts[k // per].start()

    fine_steps(
        rows_total, chunk, lambda fields: columns_whole(fields[:2], edges) + [columns_strip(fields[2])],
        initial, extrap, dual_rows, dual_cols, change, dual_data,
        offsets, grads_rows, grads_cols, data_row, masks_of, result,
        lambda k: (SUB * (k % per == 0), SUB * (k % per == per - 1)), finish, pulls, depth=4,
    )
    put_middle.wait()
    put_coarse.wait()
    for put in puts:
        put.wait()


def swap_with(message, axis, start):
    names = ("row", "col")
    sizes = [lax.axis_size(name) for name in names]
    along = names.index(axis)
    count, others = sizes[along], sizes[1 - along]

    def number(place, other):
        row, col = (place, other) if along == 0 else (other, place)
        return row * sizes[1] + col

    pairs = [(number(i, k), number(i + 1, k)) for i in range(start, count - 1, 2) for k in range(others)]
    if start and axis == "col":
        pairs += [(number(i, k), number(i, k + 1)) for i in (0, count - 1) for k in range(0, others, 2)]
    elif start:
        pairs += [(number(0, k), number(count - 1, k)) for k in range(others)]
    return lax.ppermute(message, names, pairs + [(j, i) for i, j in pairs])


def local(frame_first, frame_second, shifts):
    bands, height, width = frame_first.shape
    assert bands == 4 and width == COLUMNS and height % LANES == 0
    assert lax.axis_size("row") % 2 == 0 and lax.axis_size("col") % 2 == 0
    coarse_height = height // FACTOR
    coarse_width = width // FACTOR
    vmem = pl.BlockSpec(memory_space=pltpu.VMEM)
    hbm = pl.BlockSpec(memory_space=pltpu.HBM)
    tall_rows = coarse_height + 2 * LEAD
    inner_rows = height - 2 * BEGIN

    def shape(*sizes):
        return jax.ShapeDtypeStruct(sizes, jnp.float32)

    def scratch(*sizes):
        return pltpu.VMEM(sizes, jnp.float32)

    def call(kernel, name, arguments, outs, scratches=(), flops=1_000_000, **more):
        more = {"in_specs": [vmem] * len(arguments), "out_specs": (vmem,) * len(outs), **more}
        return pl.pallas_call(
            kernel,
            out_shape=tuple(outs),
            scratch_shapes=list(scratches),
            compiler_params=pltpu.CompilerParams(vmem_limit_bytes=24 * 1024 * 1024),
            cost_estimate=pl.CostEstimate(flops=flops, bytes_accessed=1_000_000, transcendentals=0),
            name=name,
            **more,
        )(*arguments)

    plane = shape(bands, height, LANES)
    column_message = shape(height // 2, LANES)
    row_message = shape(ROW_MESSAGE, LANES)
    whole_data = shape(2, bands, height + 2 * HALO, LANES)
    strip_data = shape(bands, height + 2 * HALO, LANES)

    *frames, coarse, swap_0, swap_1, own_meta = call(
        first_kernel,
        "means_and_message",
        [pltpu.with_memory_space_constraint(x, pltpu.HBM) for x in (frame_second, frame_first, shifts)],
        [*[plane] * 4, shape(2 * bands * coarse_height, LANES), column_message, column_message, shape(SUB, LANES)],
        [
            pltpu.SMEM((1, 1, 2), jnp.int32),
            pltpu.SemaphoreType.DMA((2, bands, 2, 2)),
            pltpu.SemaphoreType.DMA,
        ],
        in_specs=[hbm] * 3,
    )
    got_0 = swap_with(swap_0, "col", 0)
    got_1 = swap_with(swap_1, "col", 1)

    *whole_terms, initial, strip_e, strip_f, up_part, down_part = call(
        whole_terms_kernel,
        "whole_terms",
        [*frames, coarse, own_meta],
        [
            *[whole_data] * 3, shape(2, 2, inner_rows + 2 * GUARD, LANES),
            plane, plane, row_message, row_message,
        ],
        [
            scratch(2, bands, height, LANES), scratch(2, 2, coarse_height, LANES),
        ],
        flops=8_000_000,
    )
    (whole,) = call(
        whole_steps_kernel,
        "whole_steps",
        [initial, *whole_terms],
        [shape(2, 2, inner_rows, LANES)],
        fine_scratch(bands, 2, inner_rows)[1:],
        flops=20_000_000,
    )

    swap_0, swap_1, from_left, from_right, wide = call(
        functools.partial(message_kernel, lax.axis_size("col")),
        "row_messages",
        [coarse, own_meta, got_0, got_1, up_part, down_part, whole],
        [row_message, row_message, column_message, column_message, shape(2 * bands, coarse_height, LANES)],
    )
    got_1 = swap_with(swap_1, "row", 1)
    got_0 = swap_with(swap_0, "row", 0)

    middle, strip_e, first_ends, *strip_terms = call(
        functools.partial(strip_kernel, lax.axis_size("col")),
        "strip",
        [strip_e, strip_f, from_left, from_right, wide, swap_0, whole],
        [shape(2, inner_rows, width), plane, shape(2, bands, SUB, LANES), *[strip_data] * 3],
        [
            scratch(bands, height, LANES),
            scratch(2, 1, inner_rows, LANES),
            scratch(2, 1, coarse_height, LANES),
            *fine_scratch(bands, 1, inner_rows),
        ],
        flops=16_000_000,
    )

    flow, coarse_flow, *_ = call(
        functools.partial(outer_kernel, (lax.axis_size("row"), lax.axis_size("col"))),
        "outer_rows",
        [
            *frames, strip_e, first_ends, wide, got_1, got_0, middle, swap_0,
            *whole_terms, *strip_terms,
        ],
        [shape(2, height, width), shape(2, coarse_height, coarse_width), *[whole_data] * 3, *[strip_data] * 3],
        [
            scratch(ROW_MESSAGE, LANES),
            scratch(ROW_MESSAGE, LANES),
            scratch(2, 3, bands, 40, LANES),
            scratch(2 * bands, tall_rows, LANES),
            scratch(2, 3, tall_rows, LANES),
            scratch(2, 2 * EACH, LANES),
            scratch(2, 3, 2 * EACH, LANES),
            scratch(2, 2 * EACH, width),
            scratch(2, coarse_height, coarse_width),
            scratch(2, 3, 2 * EACH, LANES),
            pltpu.SemaphoreType.DMA((4,)),
            *fine_scratch(bands, 3, 2 * EACH),
        ],
        out_specs=(hbm, hbm) + (vmem,) * 6,
        input_output_aliases={11 + k: 2 + k for k in range(6)},
    )
    return (flow, coarse_flow)


def solution(mesh):
    return jax.shard_map(
        local,
        mesh=mesh,
        in_specs=(P(None, "row", "col"), P(None, "row", "col"), P("row", "col", None)),
        out_specs=(P(None, "row", "col"), P(None, "row", "col")),
        check_vma=False,
    )
```

```python
import functools

import jax
import jax.numpy as jnp
from jax import lax
from jax.experimental import pallas as pl
from jax.experimental.pallas import tpu as pltpu
from jax.sharding import PartitionSpec as P

FACTOR = 8
MAXD = 4
BANDS = 4
STEPS = 3
LANES = 128
COLUMNS = 2 * LANES
HALF = 64
SUB = 8
DEPTH = 4
REACH = DEPTH + MAXD + 1
SLOT = 16
C_SECOND = 6
C_FIRST = 5
LEAD = 8
MARGIN = 48
EDGE = 46
GUARD = 8
HALO = 8
BEGIN = 40
EACH = MARGIN + 16
LIMIT = 0.3
ALPHA = 0.3
UNIT = 0.125 / ALPHA

S_MID = 55
S_RIGHT = 110
S_LEFT = LANES - REACH
S_TURN = COLUMNS - S_RIGHT - LANES

E8 = 0
H8 = 64
E1 = 72
H1 = 80
META = 81
F4 = 88
CS = 120
ROW_MESSAGE = 144
H_BAND = 32

COARSE_A = REACH + DEPTH
COARSE_B = SLOT + REACH + DEPTH
SHIFT_R = 2 * SLOT + REACH + DEPTH
SHIFT_C = SHIFT_R + 1
EXISTS = SHIFT_R + 2


def lanes_of(rows=SUB):
    return lax.broadcasted_iota(jnp.int32, (rows, LANES), 1)


def lanes_like(x):
    return lax.broadcasted_iota(jnp.int32, x.shape, 1)


def turn(x, amount):
    amount = amount % LANES
    return x if amount == 0 else pltpu.roll(x, amount, 1)


def turn_back(x, shift):
    return pltpu.roll(x, lax.rem(LANES - shift, LANES), 1)


def split_dot(x, exact):
    high = x.astype(jnp.bfloat16)
    rest = x - high.astype(jnp.float32)
    middle = rest.astype(jnp.bfloat16)
    low = (rest - middle.astype(jnp.float32)).astype(jnp.bfloat16)
    parts = [jnp.dot(part, exact, preferred_element_type=jnp.float32) for part in (low, middle, high)]
    return parts[0] + parts[1] + parts[2]


def neighbours(axis, count):
    place = lax.axis_index(axis)
    return jnp.where(place > 0, 1.0, 0.0), jnp.where(place < count - 1, 1.0, 0.0)


def shift_at(ref, row, lane):
    numbers = ref[row : row + 1, :].astype(jnp.int32)
    return numbers[0, lane], numbers[0, lane + SLOT]


def shifts_of(message):
    return [shift_at(message, META, lane) for lane in (0, 80, 48)]


def is_even(axis, like):
    return jnp.broadcast_to(lax.axis_index(axis) % 2, like.shape) == 0


def without_ends(message, axis, count):
    place = jnp.broadcast_to(lax.axis_index(axis), message.shape)
    return jnp.where((place > 0) & (place < count - 1), message[...], 0.0)


def staggered(items, compute, store, depth, woven=None):
    pending = []
    for item in items:
        pending.append((item, compute(item)))
        if woven is not None:
            woven.advance()
        if len(pending) > depth:
            store(*pending.pop(0))
    for entry in pending:
        store(*entry)


class Woven:
    def __init__(self, stages):
        self.stages = stages
        self.result = None

    def advance(self):
        try:
            next(self.stages)
            return True
        except StopIteration as end:
            self.result = end.value if self.result is None else self.result
            return False

    def finish(self):
        while self.advance():
            pass
        return self.result


def pack_image(packed, to_right, planes, some, count, offset):
    _, height, _ = planes[0].shape
    plane = planes[int(to_right)]
    start = LANES - count if to_right else 0
    length = height // 2
    lane = lanes_of(length)
    for half in range(2):
        for band in some:
            at = half * HALF + band * SLOT + offset
            cells = turn(plane[band, half * length : (half + 1) * length, :], at - start)
            packed = cells if packed is None else jnp.where((lane >= at) & (lane < at + count), cells, packed)
    return packed


def pack_means(packed, to_right, means):
    length = packed.shape[0]
    start = LEAD + COLUMNS // FACTOR - C_SECOND if to_right else LEAD
    lane = lanes_of(length)
    for half in range(2):
        cells = means[half * length : (half + 1) * length]
        for at, first in ((half * HALF + COARSE_A, start), (half * HALF + COARSE_B, start + 3)):
            packed = jnp.where((lane >= at) & (lane < at + 3), turn(cells, at - first), packed)
    return packed


def strip_second(base, from_left, from_right, rows, half, band):
    at = half * HALF + band * SLOT
    lane = lanes_like(base)
    cells = jnp.where(lane >= S_RIGHT, turn(from_right[rows, :], S_RIGHT - at), base)
    return jnp.where(lane >= S_LEFT, turn(from_left[rows, :], S_LEFT - at), cells)


def strip_first(base, from_left, from_right, rows, half, band):
    at = half * HALF + band * SLOT + REACH
    lane = lanes_like(base)
    cells = jnp.where(lane >= S_RIGHT, turn(from_right[rows, :], S_RIGHT - at), base)
    return jnp.where(lane >= S_LEFT, turn(from_left[rows, :], LANES - DEPTH - at), cells)


def strip_halo(base, beside, band, start, count):
    at = band * H_BAND + start
    lane = lanes_like(base)
    cells = jnp.where(lane >= S_RIGHT, turn(beside, S_RIGHT - at), base)
    return jnp.where(lane >= S_LEFT, turn(beside, LANES - count - at - SLOT), cells)


def strip_own(planes):
    return jnp.where(lanes_like(planes[0]) < S_MID, planes[0], turn(planes[1], -S_TURN))


def first_kernel(
    second_hbm, first_hbm, shifts_hbm, second_0, second_1, first_0, first_1, coarse, swap_0, swap_1, own_meta,
    shifts, sems, shift_sem,
):
    seconds, firsts = (second_0, second_1), (first_0, first_1)
    bands, height, _ = second_0.shape
    width = COLUMNS
    coarse_height = height // FACTOR
    lane = lanes_of()
    get_shifts = pltpu.make_async_copy(shifts_hbm, shifts, shift_sem)
    get_shifts.start()
    copies = []
    for image, (source, refs) in enumerate(((second_hbm, seconds), (first_hbm, firsts))):
        for band in range(bands):
            for tile, ref in enumerate(refs):
                copy = pltpu.make_async_copy(
                    source.at[band, :, pl.ds(tile * LANES, LANES)], ref.at[band], sems.at[image, band, tile]
                )
                copy.start()
                copies.append((image * bands + band, tile, ref, band, copy))
    cell = lax.broadcasted_iota(jnp.int32, (width, LANES), 0)
    place = lax.broadcasted_iota(jnp.int32, (width, LANES), 1)
    weights = jnp.where(place - LEAD == cell // FACTOR, 1.0 / (FACTOR * FACTOR), 0.0).astype(jnp.bfloat16)
    means = []
    packed = [None, None]
    for image, (count, offset) in enumerate(((REACH, 0), (DEPTH, REACH))):
        for pair in range(0, bands, 2):
            some = range(pair, pair + 2)
            group = copies[2 * (image * bands + pair) : 2 * (image * bands + pair + 2)]
            for *_, copy in group:
                copy.wait()
            sums = {}
            for plane, tile, ref, band, _ in group:
                parts = [ref[band, pl.ds(k, coarse_height, stride=FACTOR), :] for k in range(FACTOR)]
                while len(parts) > 1:
                    parts = [x + y for x, y in zip(parts[::2], parts[1::2])]
                sums[band, tile] = parts[0]
            tall = [jnp.concatenate([sums[band, tile] for tile in range(2)], axis=1) for band in some]
            means.append(split_dot(jnp.concatenate(tall, axis=0), weights))
            packed = [
                pack_image(packed[side], bool(side), (seconds, firsts)[image], some, count, offset) for side in range(2)
            ]
    means = jnp.concatenate(means, axis=0)
    get_shifts.wait()
    shift_rows = shifts[0, 0, 0].astype(jnp.float32)
    shift_cols = shifts[0, 0, 1].astype(jnp.float32)
    place = lanes_of(height // 2) & (HALF - 1)
    packed = [
        jnp.where(place == SHIFT_R, shift_rows, jnp.where(place == SHIFT_C, shift_cols, jnp.where(place == EXISTS, 1.0, x)))
        for x in packed
    ]
    to_left, to_right = [pack_means(packed[side], bool(side), means) for side in range(2)]
    coarse[...] = means
    own_meta[...] = jnp.where(lane < SLOT, shift_rows, shift_cols)
    even = is_even("col", swap_0)
    swap_0[...] = jnp.where(even, to_right, to_left)
    swap_1[...] = jnp.where(even, to_left, to_right)


def message_kernel(
    count, coarse, own_meta, got_0, got_1, up_part, down_part, _whole, swap_0, swap_1, from_left, from_right, wide
):
    other = without_ends(got_1, "col", count)
    even = is_even("col", got_0)
    from_right[...] = jnp.where(even, got_0[...], other)
    from_left[...] = jnp.where(even, other, got_0[...])
    planes_coarse, coarse_height, _ = wide.shape
    bands = planes_coarse // 2
    end = from_left.shape[0]
    coarse_width = COLUMNS // FACTOR
    lane = lanes_of()
    wides = []
    for plane in range(planes_coarse):
        half, block = divmod(plane, planes_coarse // 2)
        for step in range(coarse_height // SUB):
            own = slice(plane * coarse_height + step * SUB, plane * coarse_height + (step + 1) * SUB)
            rows = slice(block * coarse_height + step * SUB, block * coarse_height + (step + 1) * SUB)
            at = half * HALF
            left = from_left[rows, :]
            right = from_right[rows, :]
            start = LEAD - C_SECOND
            cells = turn(left, start - at - COARSE_A)
            cells = jnp.where(lane >= start + 3, turn(left, start + 3 - at - COARSE_B), cells)
            cells = jnp.where(lane >= LEAD, coarse[own, :], cells)
            start = LEAD + coarse_width
            cells = jnp.where(lane >= start, turn(right, start - at - COARSE_A), cells)
            cells = jnp.where(lane >= start + 3, turn(right, start + 3 - at - COARSE_B), cells)
            wides.append((plane, step, cells))
    for plane, step, cells in wides:
        wide[plane, step * SUB : (step + 1) * SUB, :] = cells
    row = lax.broadcasted_iota(jnp.int32, (SUB, LANES), 0)
    meta = own_meta[...]
    for message, at in ((from_left, 48), (from_right, 80)):
        first_rows = message[0:SUB, :]
        rows = jnp.broadcast_to(first_rows[:, SHIFT_R : SHIFT_R + 1], (SUB, LANES))
        cols = jnp.broadcast_to(first_rows[:, SHIFT_C : SHIFT_C + 1], (SUB, LANES))
        meta = jnp.where(lane >= at, rows, meta)
        meta = jnp.where(lane >= at + 16, cols, meta)

    def beside(rows, half):
        left = from_left[rows, :]
        right = from_right[rows, :]
        cells = jnp.zeros((SUB, LANES), jnp.float32)
        for band in range(bands):
            at = half * HALF + band * SLOT
            cells = jnp.where(lane >= band * H_BAND, turn(right, band * H_BAND - at), cells)
            cells = jnp.where(lane >= band * H_BAND + SLOT, turn(left, band * H_BAND + SLOT - at), cells)
        return cells

    even = is_even("row", meta)
    parts = []
    for part, half, near, next_rows, row_of in (
        (up_part, 0, slice(0, 8), slice(8, 16), 0),
        (down_part, 1, slice(end - 8, end), slice(end - 16, end - 8), 7),
    ):
        eight = beside(near, half)
        one = beside(next_rows, half)
        one = jnp.broadcast_to(one[row_of : row_of + 1], (SUB, LANES))
        coarse_rows = []
        for band in range(bands):
            rows = slice(0, C_SECOND) if half == 0 else slice(coarse_height - C_SECOND, coarse_height)
            second = wide[band, rows, :]
            first = turn(wide[bands + band, rows, :], HALF)
            coarse_rows.append(jnp.where(lanes_like(second) < HALF, second, first))
        parts.append([
            (part[E8:H8, :], E8), (eight, H8), (part[E1:H1, :], E1), (jnp.where(row == 0, one, meta), H1),
            (part[F4:CS, :], F4), *[(x, CS + k * C_SECOND) for k, x in enumerate(coarse_rows)],
        ])
    for (up, at), (down, _) in zip(*parts):
        even = is_even("row", up)
        swap_0[at : at + up.shape[0], :] = jnp.where(even, down, up)
        swap_1[at : at + up.shape[0], :] = jnp.where(even, up, down)


def coarse_flow_of(second, first, mask):
    def along_rows(x):
        return pltpu.roll(x, x.shape[0] - 1, 0) - pltpu.roll(x, 1, 0)

    def along_cols(x):
        return pltpu.roll(x, LANES - 1, 1) - pltpu.roll(x, 1, 1)

    bands = BANDS
    size = second.shape[0] // bands
    grad_rows = 0.125 * along_rows(second)
    grad_cols = 0.125 * along_cols(second)
    offset = 0.25 * (second - first)
    data = jnp.clip(offset, -LIMIT, LIMIT)
    yield

    def pull(grads):
        terms = data * grads
        return sum(terms[k * size : (k + 1) * size] for k in range(bands))

    def tall(x):
        return jnp.concatenate([x] * bands, axis=0)

    flow = [-mask * pull(grad_rows), -mask * pull(grad_cols)]
    extrapolated = [2.0 * x for x in flow]
    dual_rows = [0.0, 0.0]
    dual_cols = [0.0, 0.0]
    yield
    for step in range(1, STEPS):
        changes = [(along_rows(x), along_cols(x)) for x in extrapolated]
        yield
        data = data + offset + grad_rows * tall(extrapolated[0]) + grad_cols * tall(extrapolated[1])
        data = jnp.clip(data, -LIMIT, LIMIT)
        yield
        for c in range(2):
            rows = dual_rows[c] + changes[c][0]
            cols = dual_cols[c] + changes[c][1]
            scale = jnp.minimum(mask, (8.0 * ALPHA) * lax.rsqrt(rows * rows + cols * cols))
            dual_rows[c] = rows * scale
            dual_cols[c] = cols * scale
        yield
        divergences = [along_rows(dual_rows[c]) + along_cols(dual_cols[c]) for c in range(2)]
        yield
        pulls = [pull(grad_rows), pull(grad_cols)]
        yield
        for c in range(2):
            following = flow[c] + mask * ((1.0 / 64.0) * divergences[c] - pulls[c])
            extrapolated[c] = 2.0 * following - flow[c]
            flow[c] = following
        yield
    return flow


def columns_of_planes(planes):
    whole = lax.broadcasted_iota(jnp.int32, (LANES, COLUMNS), 1)
    lane = lax.broadcasted_iota(jnp.int32, (LANES, LANES), 1)
    strip = jnp.where(lane < S_MID, lane, jnp.where(lane < S_LEFT, lane + (COLUMNS - S_RIGHT), lane - LANES))
    return jnp.concatenate([x for x, wanted in ((whole, "whole"), (strip, "strip")) if wanted in planes], axis=1)


def upsample(flow, planes, target):
    column = columns_of_planes(planes)
    source = lax.broadcasted_iota(jnp.int32, column.shape, 0)
    spread = jnp.where(source - LEAD == lax.shift_right_arithmetic(column, 3), float(FACTOR), 0.0).astype(jnp.bfloat16)
    rows = flow[0].shape[0]
    wide = split_dot(UNIT * jnp.concatenate(flow, axis=0), spread)
    for c in range(2):
        for tile in range(column.shape[1] // LANES):
            target[c, tile] = wide[c * rows : (c + 1) * rows, tile * LANES : (tile + 1) * LANES]


def repeat_rows(spread, initial, cells):
    for c in range(2):
        for tile in range(initial.shape[1]):
            rows = [jnp.broadcast_to(spread[c, tile, cell : cell + 1, :], (SUB, LANES)) for cell in cells]
            initial[c, tile, GUARD : GUARD + SUB * len(cells), :] = jnp.concatenate(rows, axis=0)


def shift_whole(here, shift):
    turned = [turn_back(x, shift) for x in here]
    lane = lanes_like(here[0])
    return [
        jnp.where(lane + shift >= LANES, turned[1], turned[0]),
        jnp.where(lane + shift < 0, turned[0], turned[1]),
    ]


def edge_lanes(rows):
    lane = lanes_of(rows)
    return lane == LANES - 1, lane == 0


def columns_whole(fields, edges):
    rows = fields[0].shape[0]
    if rows not in edges:
        edges[rows] = edge_lanes(rows)
    last, first = edges[rows]
    ahead = [pltpu.roll(x, LANES - 1, 1) for x in fields]
    behind = [pltpu.roll(x, 1, 1) for x in fields]
    return [
        jnp.where(last, ahead[1], ahead[0]) - behind[0],
        ahead[1] - jnp.where(first, behind[0], behind[1]),
    ]


def rows_within(tall):
    size = tall.shape[0]
    return (pltpu.roll(tall, size - 1, 0) - pltpu.roll(tall, 1, 0))[SUB : size - SUB]


def columns_strip(field):
    return pltpu.roll(field, LANES - 1, 1) - pltpu.roll(field, 1, 1)


def strip_moved(window, centre, right, left):
    own = turn_back(window(centre[0]), centre[1])
    beyond_left = turn_back(window(left[0]), left[1])
    beyond_right = turn_back(window(right[0]), right[1])
    lane = lanes_like(own)
    beyond = jnp.where((lane >= S_LEFT) | (lane < S_MID), beyond_left, beyond_right)
    return own, beyond


def strip_joined(own, beyond):
    lane = lanes_like(own)
    is_beyond = lane >= S_RIGHT
    of_next = is_beyond & (lane != S_RIGHT) | (lane == 0)
    of_previous = is_beyond & (lane != LANES - 1) | (lane == S_RIGHT - 1)
    change = turn(jnp.where(of_next, beyond, own), -1) - turn(jnp.where(of_previous, beyond, own), 1)
    return jnp.where(is_beyond, beyond, own), change


def fine_steps(
    rows_total, chunk, columns, initial, extrap, dual_rows, dual_cols, change, dual_data,
    offsets, grads_rows, grads_cols, data_row, masks_of, result, kept, done=lambda k: None, first_pulls=None, depth=1,
):
    assert STEPS == 3
    planes = len(offsets)
    bands = offsets[0].shape[0]
    chunks = rows_total // chunk

    def places(k, trim=(0, 0)):
        start, size = k * chunk + trim[0], chunk - sum(trim)
        return pl.ds(GUARD + start, size), pl.ds(start, size), pl.ds(data_row(k) + trim[0], size)

    def row_change(ref, c, tile, at):
        return ref[c, tile, pl.ds(at.start + 1, at.size), :] - ref[c, tile, pl.ds(at.start - 1, at.size), :]

    def clip(x):
        return jnp.clip(x, -UNIT * LIMIT, UNIT * LIMIT)

    tiles = range(planes)

    for step in range(STEPS):
        source = initial if step == 0 else extrap
        final = step == STEPS - 1

        def dual(item, source=source, step=step):
            k, c = item
            at, own, _ = places(k)
            masks = masks_of(own)
            along = columns([source[c, tile, at, :] for tile in tiles])
            values = []
            for tile in tiles:
                rows = row_change(source, c, tile, at)
                cols = along[tile]
                if step > 0:
                    rows = rows + dual_rows[c, tile, at, :]
                    cols = cols + dual_cols[c, tile, own, :]
                scale = jnp.minimum(masks[tile], lax.rsqrt(rows * rows + cols * cols))
                values.append((rows * scale, cols * scale))
            return values

        def store_dual(item, values):
            k, c = item
            for tile, (rows, cols) in enumerate(values):
                dual_rows[c, tile, places(k)[0], :] = rows
                dual_cols[c, tile, places(k)[1], :] = cols

        staggered([(k, c) for k in range(chunks) for c in range(2)], dual, store_dual, depth)
        along_of = {}

        def primal(item, step=step, final=final, along_of=along_of):
            k, tile = item
            at, own, data = places(k, kept(k) if final else (0, 0))
            if k not in along_of:
                along_of[k] = [columns([dual_cols[c, t, own, :] for t in tiles]) for c in range(2)]
            mask = masks_of(own)[tile]
            start = [initial[c, tile, at, :] for c in range(2)]
            if step > 0:
                moved = [extrap[c, tile, at, :] - start[c] for c in range(2)]
            if step == 1:
                changes = [0.5 * x for x in moved]
            if step == 2:
                changes = [change[c, tile, own, :] for c in range(2)]
            pulls = [None, None]
            duals = []
            ready = step == 0 and first_pulls is not None
            if ready:
                pulls = [first_pulls[c, tile, own, :] for c in range(2)]
            for band in range(0 if ready else bands):
                gradient = (grads_rows[tile][band, data, :], grads_cols[tile][band, data, :])
                value = offsets[tile][band, data, :]
                if step > 0:
                    earlier = clip(value) if step == 1 else dual_data[band, tile, own, :]
                    value = (value + earlier) + (gradient[0] * moved[0] + gradient[1] * moved[1])
                value = clip(value)
                duals.append(value)
                for c in range(2):
                    term = value * gradient[c]
                    pulls[c] = term if pulls[c] is None else pulls[c] + term
            flows, nexts = [], []
            for c in range(2):
                divergence = row_change(dual_rows, c, tile, at) + along_of[k][c][tile]
                moving = (mask * (1.0 / 64.0)) * divergence - pulls[c]
                total = moving if step == 0 else changes[c] + moving
                flows.append((start[c] + total) * (1.0 / UNIT) if final else total)
                nexts.append(None if final else start[c] + (total + moving))
            return flows, nexts, duals

        def store_primal(item, results, step=step, final=final):
            k, tile = item
            flows, nexts, duals = results
            at, own, _ = places(k, kept(k) if final else (0, 0))
            for c in range(2):
                if final:
                    result[c, tile, own, :] = flows[c]
                else:
                    if step > 0:
                        change[c, tile, own, :] = flows[c]
                    extrap[c, tile, at, :] = nexts[c]
            if final:
                if tile == planes - 1:
                    done(k)
            elif step > 0:
                for band in range(bands):
                    dual_data[band, tile, own, :] = duals[band]

        staggered([(k, tile) for k in range(chunks) for tile in tiles], primal, store_primal, depth)


def clear_guards(*refs):
    for ref in refs:
        rows = ref.shape[2]
        zero = jnp.zeros((GUARD, LANES), jnp.float32)
        for c in range(2):
            for tile in range(ref.shape[1]):
                ref[c, tile, 0:GUARD, :] = zero
                ref[c, tile, rows - GUARD : rows, :] = zero


def fine_scratch(bands, planes, rows):
    guarded = pltpu.VMEM((2, planes, rows + 2 * GUARD, LANES), jnp.float32)
    plain = pltpu.VMEM((2, planes, rows, LANES), jnp.float32)
    return [guarded, guarded, guarded, plain, plain, pltpu.VMEM((bands, planes, rows, LANES), jnp.float32)]


def pieces(bands, height, rows):
    assert (height - 2 * SUB) % rows == 0
    return [(band, row) for row in range(SUB, height - SUB, rows) for band in range(bands)]


def whole_terms_kernel(
    second_0, second_1, first_0, first_1, coarse, own_meta,
    offset, grad_rows, grad_cols, initial, strip_e, strip_f, up, down, moved, spread,
):
    seconds, firsts = (second_0, second_1), (first_0, first_1)
    bands, height, _ = second_0.shape
    block = 40
    coarse_height = coarse.shape[0] // (2 * bands)
    centre = shift_at(own_meta, 0, 0)
    def windows(band, row, rows):
        here = [ref[band, pl.ds(row + centre[0], rows), :].reshape(-1, LANES) for ref in seconds]
        return shift_whole(here, centre[1])

    woven = Woven(coarse_flow_of(coarse[0 : bands * coarse_height, :], coarse[bands * coarse_height :, :], 1.0))

    def strips_of(item):
        band, row = item
        rows = slice(row, row + LANES)
        return strip_own([ref[band, rows, :] for ref in seconds]), strip_own([ref[band, rows, :] for ref in firsts])

    def store_strips(item, results):
        band, row = item
        strip_e[band, row : row + LANES, :], strip_f[band, row : row + LANES, :] = results

    staggered([(band, row) for band in range(bands) for row in range(0, height, LANES)], strips_of, store_strips, 1, woven)

    ends = [(row, windows(slice(None), row, SUB)) for row in (SUB // 2, height - SUB - SUB // 2)]
    for row, values in ends:
        for tile in range(2):
            moved[tile, :, row : row + SUB, :] = values[tile].reshape(bands, SUB, LANES)

    def store_moved(item, values):
        band, row = item
        for tile in range(2):
            moved[tile, band, row : row + 120, :] = values[tile]

    staggered(pieces(bands, height, 120), lambda item: windows(*item, 120), store_moved, 3, woven)

    edges = {}

    def values_of(item):
        band, row = item
        rows = slice(row, row + block)
        values = [moved[tile, band, rows, :] for tile in range(2)]
        along = columns_whole(values, edges)
        own = [ref[band, rows, :] for ref in firsts]
        return [(0.25 * UNIT) * (x - y) for x, y in zip(values, own)], [0.125 * x for x in along]

    def store_values(item, results):
        band, row = item
        offsets, gradients = results
        data = slice(row + HALO, row + HALO + block)
        for tile in range(2):
            offset[tile, band, data, :] = offsets[tile]
            grad_cols[tile, band, data, :] = gradients[tile]

    staggered(pieces(bands, height, block), values_of, store_values, 3, woven)

    def gradient_of(item):
        band, row = item
        return [0.125 * rows_within(moved[tile, band, row - SUB : row + 40 + SUB, :]) for tile in range(2)]

    def store_gradient(item, results):
        band, row = item
        for tile in range(2):
            grad_rows[tile, band, row + HALO : row + HALO + 40, :] = results[tile]

    staggered(pieces(bands, height, 40), gradient_of, store_gradient, 3, woven)

    parts = []
    for band in range(bands):
        for second, first in zip(seconds, firsts):
            parts.append((
                second[band, 0:16, :], first[band, 0:8, :],
                second[band, height - 16 : height, :], first[band, height - 8 : height, :],
            ))
    for k, (second_top, first_top, second_end, first_end) in enumerate(parts):
        up[E8 + 8 * k : E8 + 8 * k + 8, :] = second_top[0:8]
        up[E1 + k : E1 + k + 1, :] = second_top[8:9]
        up[F4 + 4 * k : F4 + 4 * k + 4, :] = first_top[0:4]
        down[E8 + 8 * k : E8 + 8 * k + 8, :] = second_end[8:16]
        down[E1 + k : E1 + k + 1, :] = second_end[7:8]
        down[F4 + 4 * k : F4 + 4 * k + 4, :] = first_end[4:8]
    for target in (up, down):
        for start, end in ((H8, E1), (H1, F4), (CS, ROW_MESSAGE)):
            target[start:end, :] = jnp.zeros((end - start, LANES), jnp.float32)

    upsample(woven.finish(), ("whole",), spread)
    clear_guards(initial)
    rows_total = initial.shape[2] - 2 * GUARD
    repeat_rows(spread, initial, [BEGIN // FACTOR + k for k in range(rows_total // SUB)])


def whole_steps_kernel(
    initial, offset, grad_rows, grad_cols, result, extrap, dual_rows, dual_cols, change, dual_data
):
    rows_total = result.shape[2]
    clear_guards(extrap, dual_rows)
    chunk = 16
    edges = {}
    fine_steps(
        rows_total, chunk, lambda fields: columns_whole(fields, edges),
        initial, extrap, dual_rows, dual_cols, change, dual_data,
        *[[ref.at[tile] for tile in range(2)] for ref in (offset, grad_rows, grad_cols)],
        lambda k: HALO + BEGIN + k * chunk, lambda own: (1.0, 1.0), result,
        lambda k: (SUB * (k == 0), SUB * (k == rows_total // chunk - 1)), depth=3,
    )


def strip_kernel(
    count, strip_e, strip_f, from_left, from_right, wide, own_message, whole,
    middle, strip_out, first_ends, offset, grad_rows, grad_cols,
    both, moved, result, spread, initial, extrap, dual_rows, dual_cols, change, dual_data,
):
    bands, height, _ = strip_e.shape
    block = 40
    coarse_height = height // FACTOR
    coarse_width = COLUMNS // FACTOR
    rows_total = height - 2 * BEGIN
    lane = lanes_of()
    centre, right, left = shifts_of(own_message)
    has_left, has_right = neighbours("col", count)
    exists = jnp.where(lane < S_RIGHT, 1.0, jnp.where(lane < S_LEFT, has_right, has_left))

    def tall_factor(rows):
        return 0.125 * jnp.concatenate([exists] * (rows // SUB), axis=0)

    mask = jnp.where(lane < LEAD, has_left, jnp.where(lane < LEAD + coarse_width, 1.0, has_right))
    mask = jnp.concatenate([mask] * (coarse_height // SUB), axis=0)
    cells = [wide[k * bands : (k + 1) * bands].reshape(bands * coarse_height, LANES) for k in range(2)]
    woven = Woven(coarse_flow_of(*cells, mask))

    def halves(row, rows):
        half = row // (height // 2)
        start = row - half * (height // 2)
        return half, slice(start, start + rows)

    def second_of(item):
        band, row = item
        half, message = halves(row, LANES)
        return strip_second(strip_e[band, row : row + LANES, :], from_left, from_right, message, half, band)

    def store_second(item, value):
        band, row = item
        strip_out[band, row : row + LANES, :] = value

    staggered([(band, row) for row in range(0, height, LANES) for band in range(bands)], second_of, store_second, 1, woven)

    def first_of(band, row, rows):
        half, message = halves(row, rows)
        return strip_first(strip_f[band, row : row + rows, :], from_left, from_right, message, half, band)

    firsts = [(end, band, first_of(band, (0, height - SUB)[end], SUB)) for end in range(2) for band in range(bands)]
    for end, band, value in firsts:
        first_ends[end, band] = value

    def windows(band, row, rows):
        return strip_moved(
            lambda shift: strip_out[band, pl.ds(row + shift, rows), :].reshape(-1, LANES), centre, right, left
        )

    ends = [
        (row, strip_joined(*windows(slice(None), row, SUB))[0]) for row in (SUB // 2, height - SUB - SUB // 2)
    ]
    for row, value in ends:
        moved[:, row : row + SUB, :] = value.reshape(bands, SUB, LANES)

    def store_moved(item, values):
        band, row = item
        for k in range(2):
            both[k, band, row : row + 120, :] = values[k]

    staggered(pieces(bands, height, 120), lambda item: windows(*item, 120), store_moved, 3, woven)

    factor = tall_factor(block)

    def values_of(item):
        band, row = item
        value, along = strip_joined(*[both[k, band, row : row + block, :] for k in range(2)])
        return value, (0.25 * UNIT) * (value - first_of(band, row, block)), factor * along

    def store_values(item, results):
        band, row = item
        data = slice(row + HALO, row + HALO + block)
        moved[band, row : row + block, :], offset[band, data, :], grad_cols[band, data, :] = results

    staggered(pieces(bands, height, block), values_of, store_values, 3, woven)

    def gradient_of(item):
        band, row = item
        return factor * rows_within(moved[band, row - SUB : row + block + SUB, :])

    def store_gradient(item, value):
        band, row = item
        grad_rows[band, row + HALO : row + HALO + block, :] = value

    staggered(pieces(bands, height, block), gradient_of, store_gradient, 3, woven)

    upsample(woven.finish(), ("strip",), spread)
    clear_guards(initial, extrap, dual_rows)
    repeat_rows(spread, initial, [BEGIN // FACTOR + k for k in range(rows_total // SUB)])

    chunk = 16
    masks = jnp.concatenate([exists] * (chunk // SUB), axis=0)
    fine_steps(
        rows_total, chunk, lambda fields: [columns_strip(fields[0])],
        initial, extrap, dual_rows, dual_cols, change, dual_data, [offset], [grad_rows], [grad_cols],
        lambda k: HALO + BEGIN + k * chunk, lambda own: (masks[: own.size],), result,
        lambda k: (SUB * (k == 0), SUB * (k == rows_total // chunk - 1)), depth=4,
    )
    join(whole, result.at[:, 0], middle, slice(SUB, rows_total - SUB))


def join(whole, strip, target, rows):
    lane = lanes_of(rows.stop - rows.start)
    values = []
    for c in range(2):
        edge = strip[c, rows, :]
        start = jnp.where(lane < EDGE, edge, whole[c, 0, rows, :])
        values.append((start, jnp.where(lane >= LANES - EDGE, turn(edge, S_TURN), whole[c, 1, rows, :])))
    for c in range(2):
        target[c, rows, 0:LANES], target[c, rows, LANES:COLUMNS] = values[c]


def outer_kernel(
    counts, second_0, second_1, first_0, first_1, strip_e, first_ends, wide, got_1, got_0, middle, own_message,
    _wo, _wr, _wc, _so, _sr, _sc,
    flow_out, coarse_out, whole_offset, whole_rows, whole_cols, strip_offset, strip_rows, strip_cols,
    from_up, from_down, extended, tall, spread, masks, result, joined, coarse_result, pulls, sems,
    initial, extrap, dual_rows, dual_cols, change, dual_data,
):
    bands, height, _ = second_0.shape
    coarse_height = height // FACTOR
    coarse_width = COLUMNS // FACTOR
    rows_total = 2 * EACH
    lane = lanes_of()

    put_middle = pltpu.make_async_copy(
        middle.at[:, pl.ds(MARGIN - BEGIN, height - 2 * MARGIN), :],
        flow_out.at[:, pl.ds(MARGIN, height - 2 * MARGIN), :],
        sems.at[0],
    )
    put_middle.start()
    own, one, other = [shifts_of(message) for message in (own_message, got_0, got_1)]
    odd = lax.axis_index("row") % 2

    def of_row(for_even, for_odd):
        return [tuple(jnp.where(odd == 0, x, y) for x, y in zip(*pair)) for pair in zip(for_even, for_odd)]

    above, below = of_row(other, one), of_row(one, other)

    other = without_ends(got_1, "row", counts[0])
    even = is_even("row", got_0)
    from_down[...] = jnp.where(even, got_0[...], other)
    from_up[...] = jnp.where(even, other, got_0[...])

    has_up, has_down = neighbours("row", counts[0])
    has_left, has_right = neighbours("col", counts[1])
    exists = jnp.where(lane < S_RIGHT, 1.0, jnp.where(lane < S_LEFT, has_right, has_left))

    zero = jnp.zeros((SUB, LANES), jnp.float32)
    tall_rows = coarse_height + 2 * LEAD
    parts = []
    fill = jnp.zeros((LEAD - C_SECOND, LANES), jnp.float32)
    for plane in range(2 * bands):
        at = CS + C_SECOND * (plane % bands)
        ends = [turn(message[at : at + C_SECOND, :], HALF * (plane // bands)) for message in (from_up, from_down)]
        parts.append([fill, ends[0], wide[plane], ends[1], fill])
    for plane, values in enumerate(parts):
        tall[plane] = jnp.concatenate(values, axis=0)
    across = jnp.where(lane < LEAD, has_left, jnp.where(lane < LEAD + coarse_width, 1.0, has_right))
    mask = jnp.concatenate([across * has_up] + [across] * (coarse_height // SUB) + [across * has_down], axis=0)
    for end in range(2):
        message = (from_up, from_down)[end]
        beside = message[H8 : H8 + 8, :]
        beside_one = jnp.broadcast_to(message[H1 : H1 + 1, :], (SUB, LANES))
        parts = []
        for band in range(bands):
            eights = [message[E8 + 8 * k : E8 + 8 * k + 8, :] for k in (2 * band, 2 * band + 1)]
            ones = [jnp.broadcast_to(message[E1 + k : E1 + k + 1, :], (SUB, LANES)) for k in (2 * band, 2 * band + 1)]
            eights.append(strip_halo(strip_own(eights), beside, band, 0, REACH))
            ones.append(strip_halo(strip_own(ones), beside_one, band, 0, REACH))
            for tile, (eight, one) in enumerate(zip(eights, ones)):
                source = (second_0, second_1, strip_e)[tile]
                if end == 0:
                    parts.append((tile, band, [one, eight, source[band, 0:24, :]]))
                else:
                    parts.append((tile, band, [source[band, height - 24 : height, :], eight, one]))
        for tile, band, values in parts:
            extended[end, tile, band] = jnp.concatenate(values, axis=0)
    cells = [tall[k * bands : (k + 1) * bands].reshape(bands * tall_rows, LANES) for k in range(2)]
    woven = Woven(coarse_flow_of(*cells, mask))
    edges = {}
    rows_data = whole_offset.shape[2]
    exists_tall = jnp.concatenate([exists] * bands, axis=0)

    def rows_of(halo, end):
        if halo:
            return slice(0, SUB) if end == 0 else slice(rows_data - SUB, rows_data)
        return slice(HALO, HALO + SUB) if end == 0 else slice(rows_data - HALO - SUB, rows_data - HALO)

    def values_of(item):
        halo, end = item
        message = (from_up, from_down)[end]
        base = (SUB, 3 * SUB)[end] if halo else 2 * SUB
        shifts = (above, below)[end] if halo else own
        factor = 0.125 * (has_up, has_down)[end] if halo else 0.125

        def here(tile, shift):
            return extended[end, tile, :, pl.ds(base + shift, SUB), :].reshape(-1, LANES)

        def down_up(tile, shift):
            return here(tile, shift + 1) - here(tile, shift - 1)

        own_rows = slice(0, SUB) if end == 0 else slice(height - SUB, height)
        if halo:
            firsts = [[], [], []]
            for band in range(bands):
                eights = []
                for k in (2 * band, 2 * band + 1):
                    four = message[F4 + 4 * k : F4 + 4 * k + 4, :]
                    eights.append(jnp.concatenate([four, four], axis=0))
                eights.append(strip_halo(strip_own(eights), message[H8 : H8 + 8, :], band, REACH, DEPTH))
                for tile in range(3):
                    firsts[tile].append(eights[tile])
            firsts = [jnp.concatenate(x, axis=0) for x in firsts]
        else:
            firsts = [x.reshape(-1, LANES) for x in (first_0[:, own_rows, :], first_1[:, own_rows, :], first_ends[end])]
        centre = shifts[0]
        values = shift_whole([here(tile, centre[0]) for tile in range(2)], centre[1])
        changes = shift_whole([down_up(tile, centre[0]) for tile in range(2)], centre[1])
        along = columns_whole(values, edges)
        value, across_cols = strip_joined(*strip_moved(lambda shift: here(2, shift), *shifts))
        change_rows, _ = strip_joined(*strip_moved(lambda shift: down_up(2, shift), *shifts))
        return (
            [(0.25 * UNIT) * (x - y) for x, y in zip([*values, value], firsts)],
            [*[factor * x for x in changes], (factor * exists_tall) * change_rows],
            [*[factor * x for x in along], (factor * exists_tall) * across_cols],
        )

    def store_values(item, results):
        rows = rows_of(*item)
        for values, whole, strip in zip(
            results, (whole_offset, whole_rows, whole_cols), (strip_offset, strip_rows, strip_cols)
        ):
            values = [x.reshape(bands, SUB, LANES) for x in values]
            for tile in range(2):
                whole[tile, :, rows, :] = values[tile]
            strip[:, rows, :] = values[2]

    staggered([(halo, end) for halo in (True, False) for end in range(2)], values_of, store_values, 1, woven)

    chunk = 16
    per = EACH // chunk

    def data_row(k):
        return k // per * (rows_data - EACH) + k % per * chunk

    offsets = [whole_offset.at[0], whole_offset.at[1], strip_offset]
    grads_rows = [whole_rows.at[0], whole_rows.at[1], strip_rows]
    grads_cols = [whole_cols.at[0], whole_cols.at[1], strip_cols]

    def pulls_of(item):
        k, tile = item
        data = pl.ds(k * (rows_data - EACH), EACH)
        duals = [jnp.clip(offsets[tile][band, data, :], -UNIT * LIMIT, UNIT * LIMIT) for band in range(bands)]
        return [
            sum(duals[band] * grads[tile][band, data, :] for band in range(bands)) for grads in (grads_rows, grads_cols)
        ]

    def store_pulls(item, values):
        k, tile = item
        for c in range(2):
            pulls[c, tile, k * EACH : (k + 1) * EACH, :] = values[c]

    staggered([(k, tile) for k in range(2) for tile in range(3)], pulls_of, store_pulls, 1, woven)

    flow = woven.finish()
    for c in range(2):
        coarse_result[c] = turn(flow[c][LEAD : LEAD + coarse_height], -LEAD)[:, :coarse_width]
    put_coarse = pltpu.make_async_copy(coarse_result, coarse_out, sems.at[1])
    put_coarse.start()
    upsample(flow, ("whole", "strip"), spread)
    clear_guards(initial, extrap, dual_rows)
    each = EACH // SUB
    repeat_rows(
        spread, initial,
        [LEAD - 1 + k for k in range(each)] + [tall_rows - LEAD + 1 - each + k for k in range(each)],
    )

    for i, value in enumerate((jnp.ones((SUB, LANES), jnp.float32), exists)):
        masks[i] = jnp.concatenate([value * has_up] + [value] * (rows_total // SUB - 2) + [value * has_down], axis=0)

    def masks_of(rows):
        whole = masks[0, rows, :]
        return (whole, whole, masks[1, rows, :])

    edges = {}
    puts = [
        pltpu.make_async_copy(
            joined.at[:, pl.ds(k * EACH + SUB, MARGIN), :],
            flow_out.at[:, pl.ds(k * (height - MARGIN), MARGIN), :],
            sems.at[2 + k],
        )
        for k in range(2)
    ]

    def finish(k):
        if k % per == per - 1:
            at = k // per * EACH + SUB
            join(result, result.at[:, 2], joined, slice(at, at + MARGIN))
            puts[k // per].start()

    fine_steps(
        rows_total, chunk, lambda fields: columns_whole(fields[:2], edges) + [columns_strip(fields[2])],
        initial, extrap, dual_rows, dual_cols, change, dual_data,
        offsets, grads_rows, grads_cols, data_row, masks_of, result,
        lambda k: (SUB * (k % per == 0), SUB * (k % per == per - 1)), finish, pulls, depth=4,
    )
    put_middle.wait()
    put_coarse.wait()
    for put in puts:
        put.wait()


def swap_with(message, axis, start):
    names = ("row", "col")
    sizes = [lax.axis_size(name) for name in names]
    along = names.index(axis)
    count, others = sizes[along], sizes[1 - along]

    def number(place, other):
        row, col = (place, other) if along == 0 else (other, place)
        return row * sizes[1] + col

    pairs = [(number(i, k), number(i + 1, k)) for i in range(start, count - 1, 2) for k in range(others)]
    if start and axis == "col":
        pairs += [(number(i, k), number(i, k + 1)) for i in (0, count - 1) for k in range(0, others, 2)]
    elif start:
        pairs += [(number(0, k), number(count - 1, k)) for k in range(others)]
    return lax.ppermute(message, names, pairs + [(j, i) for i, j in pairs])


def local(frame_first, frame_second, shifts):
    bands, height, width = frame_first.shape
    assert bands == 4 and width == COLUMNS and height % LANES == 0
    assert lax.axis_size("row") % 2 == 0 and lax.axis_size("col") % 2 == 0
    coarse_height = height // FACTOR
    coarse_width = width // FACTOR
    vmem = pl.BlockSpec(memory_space=pltpu.VMEM)
    hbm = pl.BlockSpec(memory_space=pltpu.HBM)
    tall_rows = coarse_height + 2 * LEAD
    inner_rows = height - 2 * BEGIN

    def shape(*sizes):
        return jax.ShapeDtypeStruct(sizes, jnp.float32)

    def scratch(*sizes):
        return pltpu.VMEM(sizes, jnp.float32)

    def call(kernel, name, arguments, outs, scratches=(), flops=1_000_000, **more):
        more = {"in_specs": [vmem] * len(arguments), "out_specs": (vmem,) * len(outs), **more}
        return pl.pallas_call(
            kernel,
            out_shape=tuple(outs),
            scratch_shapes=list(scratches),
            compiler_params=pltpu.CompilerParams(vmem_limit_bytes=24 * 1024 * 1024),
            cost_estimate=pl.CostEstimate(flops=flops, bytes_accessed=1_000_000, transcendentals=0),
            name=name,
            **more,
        )(*arguments)

    plane = shape(bands, height, LANES)
    column_message = shape(height // 2, LANES)
    row_message = shape(ROW_MESSAGE, LANES)
    whole_data = shape(2, bands, height + 2 * HALO, LANES)
    strip_data = shape(bands, height + 2 * HALO, LANES)

    *frames, coarse, swap_0, swap_1, own_meta = call(
        first_kernel,
        "means_and_message",
        [pltpu.with_memory_space_constraint(x, pltpu.HBM) for x in (frame_second, frame_first, shifts)],
        [*[plane] * 4, shape(2 * bands * coarse_height, LANES), column_message, column_message, shape(SUB, LANES)],
        [
            pltpu.SMEM((1, 1, 2), jnp.int32),
            pltpu.SemaphoreType.DMA((2, bands, 2)),
            pltpu.SemaphoreType.DMA,
        ],
        in_specs=[hbm] * 3,
    )
    got_0 = swap_with(swap_0, "col", 0)
    got_1 = swap_with(swap_1, "col", 1)

    *whole_terms, initial, strip_e, strip_f, up_part, down_part = call(
        whole_terms_kernel,
        "whole_terms",
        [*frames, coarse, own_meta],
        [
            *[whole_data] * 3, shape(2, 2, inner_rows + 2 * GUARD, LANES),
            plane, plane, row_message, row_message,
        ],
        [
            scratch(2, bands, height, LANES), scratch(2, 2, coarse_height, LANES),
        ],
        flops=8_000_000,
    )
    (whole,) = call(
        whole_steps_kernel,
        "whole_steps",
        [initial, *whole_terms],
        [shape(2, 2, inner_rows, LANES)],
        fine_scratch(bands, 2, inner_rows)[1:],
        flops=20_000_000,
    )

    swap_0, swap_1, from_left, from_right, wide = call(
        functools.partial(message_kernel, lax.axis_size("col")),
        "row_messages",
        [coarse, own_meta, got_0, got_1, up_part, down_part, whole],
        [row_message, row_message, column_message, column_message, shape(2 * bands, coarse_height, LANES)],
    )
    got_1 = swap_with(swap_1, "row", 1)
    got_0 = swap_with(swap_0, "row", 0)

    middle, strip_e, first_ends, *strip_terms = call(
        functools.partial(strip_kernel, lax.axis_size("col")),
        "strip",
        [strip_e, strip_f, from_left, from_right, wide, swap_0, whole],
        [shape(2, inner_rows, width), plane, shape(2, bands, SUB, LANES), *[strip_data] * 3],
        [
            scratch(2, bands, height, LANES),
            scratch(bands, height, LANES),
            scratch(2, 1, inner_rows, LANES),
            scratch(2, 1, coarse_height, LANES),
            *fine_scratch(bands, 1, inner_rows),
        ],
        flops=16_000_000,
    )

    flow, coarse_flow, *_ = call(
        functools.partial(outer_kernel, (lax.axis_size("row"), lax.axis_size("col"))),
        "outer_rows",
        [
            *frames, strip_e, first_ends, wide, got_1, got_0, middle, swap_0,
            *whole_terms, *strip_terms,
        ],
        [shape(2, height, width), shape(2, coarse_height, coarse_width), *[whole_data] * 3, *[strip_data] * 3],
        [
            scratch(ROW_MESSAGE, LANES),
            scratch(ROW_MESSAGE, LANES),
            scratch(2, 3, bands, 40, LANES),
            scratch(2 * bands, tall_rows, LANES),
            scratch(2, 3, tall_rows, LANES),
            scratch(2, 2 * EACH, LANES),
            scratch(2, 3, 2 * EACH, LANES),
            scratch(2, 2 * EACH, width),
            scratch(2, coarse_height, coarse_width),
            scratch(2, 3, 2 * EACH, LANES),
            pltpu.SemaphoreType.DMA((4,)),
            *fine_scratch(bands, 3, 2 * EACH),
        ],
        out_specs=(hbm, hbm) + (vmem,) * 6,
        input_output_aliases={11 + k: 2 + k for k in range(6)},
    )
    return (flow, coarse_flow)


def solution(mesh):
    return jax.shard_map(
        local,
        mesh=mesh,
        in_specs=(P(None, "row", "col"), P(None, "row", "col"), P("row", "col", None)),
        out_specs=(P(None, "row", "col"), P(None, "row", "col")),
        check_vma=False,
    )
```

```python
import functools

import jax
import jax.numpy as jnp
from jax import lax
from jax.experimental import pallas as pl
from jax.experimental.pallas import tpu as pltpu
from jax.sharding import PartitionSpec as P

FACTOR = 8
MAXD = 4
BANDS = 4
STEPS = 3
LANES = 128
COLUMNS = 2 * LANES
HALF = 64
SUB = 8
DEPTH = 4
REACH = DEPTH + MAXD + 1
SLOT = 16
C_SECOND = 6
C_FIRST = 5
LEAD = 8
MARGIN = 48
EDGE = 46
GUARD = 8
HALO = 8
BEGIN = 40
EACH = MARGIN + 16
LIMIT = 0.3
ALPHA = 0.3
UNIT = 0.125 / ALPHA

S_MID = 55
S_RIGHT = 110
S_LEFT = LANES - REACH
S_TURN = COLUMNS - S_RIGHT - LANES

E8 = 0
H8 = 64
E1 = 72
H1 = 80
META = 81
F4 = 88
CS = 120
ROW_MESSAGE = 144
H_BAND = 32

COARSE_A = REACH + DEPTH
COARSE_B = SLOT + REACH + DEPTH
SHIFT_R = 2 * SLOT + REACH + DEPTH
SHIFT_C = SHIFT_R + 1
EXISTS = SHIFT_R + 2


def lanes_of(rows=SUB):
    return lax.broadcasted_iota(jnp.int32, (rows, LANES), 1)


def lanes_like(x):
    return lax.broadcasted_iota(jnp.int32, x.shape, 1)


def turn(x, amount):
    amount = amount % LANES
    return x if amount == 0 else pltpu.roll(x, amount, 1)


def turn_back(x, shift):
    return pltpu.roll(x, lax.rem(LANES - shift, LANES), 1)


def split_dot(x, exact):
    high = x.astype(jnp.bfloat16)
    rest = x - high.astype(jnp.float32)
    middle = rest.astype(jnp.bfloat16)
    low = (rest - middle.astype(jnp.float32)).astype(jnp.bfloat16)
    parts = [jnp.dot(part, exact, preferred_element_type=jnp.float32) for part in (low, middle, high)]
    return parts[0] + parts[1] + parts[2]


def neighbours(axis, count):
    place = lax.axis_index(axis)
    return jnp.where(place > 0, 1.0, 0.0), jnp.where(place < count - 1, 1.0, 0.0)


def shift_at(ref, row, lane):
    numbers = ref[row : row + 1, :].astype(jnp.int32)
    return numbers[0, lane], numbers[0, lane + SLOT]


def shifts_of(message):
    return [shift_at(message, META, lane) for lane in (0, 80, 48)]


def is_even(axis, like):
    return jnp.broadcast_to(lax.axis_index(axis) % 2, like.shape) == 0


def without_ends(message, axis, count):
    place = jnp.broadcast_to(lax.axis_index(axis), message.shape)
    return jnp.where((place > 0) & (place < count - 1), message[...], 0.0)


def staggered(items, compute, store, depth, woven=None):
    pending = []
    for item in items:
        pending.append((item, compute(item)))
        if woven is not None:
            woven.advance()
        if len(pending) > depth:
            store(*pending.pop(0))
    for entry in pending:
        store(*entry)


class Woven:
    def __init__(self, stages):
        self.stages = stages
        self.result = None

    def advance(self):
        try:
            next(self.stages)
            return True
        except StopIteration as end:
            self.result = end.value if self.result is None else self.result
            return False

    def finish(self):
        while self.advance():
            pass
        return self.result


def pack_image(packed, to_right, planes, some, count, offset):
    _, height, _ = planes[0].shape
    plane = planes[int(to_right)]
    start = LANES - count if to_right else 0
    length = height // 2
    lane = lanes_of(length)
    for half in range(2):
        for band in some:
            at = half * HALF + band * SLOT + offset
            cells = turn(plane[band, half * length : (half + 1) * length, :], at - start)
            packed = cells if packed is None else jnp.where((lane >= at) & (lane < at + count), cells, packed)
    return packed


def pack_means(packed, to_right, means):
    length = packed.shape[0]
    start = LEAD + COLUMNS // FACTOR - C_SECOND if to_right else LEAD
    lane = lanes_of(length)
    for half in range(2):
        cells = means[half * length : (half + 1) * length]
        for at, first in ((half * HALF + COARSE_A, start), (half * HALF + COARSE_B, start + 3)):
            packed = jnp.where((lane >= at) & (lane < at + 3), turn(cells, at - first), packed)
    return packed


def strip_second(base, from_left, from_right, rows, half, band):
    at = half * HALF + band * SLOT
    lane = lanes_like(base)
    cells = jnp.where(lane >= S_RIGHT, turn(from_right[rows, :], S_RIGHT - at), base)
    return jnp.where(lane >= S_LEFT, turn(from_left[rows, :], S_LEFT - at), cells)


def strip_first(base, from_left, from_right, rows, half, band):
    at = half * HALF + band * SLOT + REACH
    lane = lanes_like(base)
    cells = jnp.where(lane >= S_RIGHT, turn(from_right[rows, :], S_RIGHT - at), base)
    return jnp.where(lane >= S_LEFT, turn(from_left[rows, :], LANES - DEPTH - at), cells)


def strip_halo(base, beside, band, start, count):
    at = band * H_BAND + start
    lane = lanes_like(base)
    cells = jnp.where(lane >= S_RIGHT, turn(beside, S_RIGHT - at), base)
    return jnp.where(lane >= S_LEFT, turn(beside, LANES - count - at - SLOT), cells)


def strip_own(planes):
    return jnp.where(lanes_like(planes[0]) < S_MID, planes[0], turn(planes[1], -S_TURN))


def first_kernel(
    second_hbm, first_hbm, shifts_hbm, second_0, second_1, first_0, first_1, coarse, swap_0, swap_1, own_meta,
    shifts, sems, shift_sem,
):
    seconds, firsts = (second_0, second_1), (first_0, first_1)
    bands, height, _ = second_0.shape
    width = COLUMNS
    coarse_height = height // FACTOR
    lane = lanes_of()
    get_shifts = pltpu.make_async_copy(shifts_hbm, shifts, shift_sem)
    get_shifts.start()
    copies = []
    for image, (source, refs) in enumerate(((second_hbm, seconds), (first_hbm, firsts))):
        for band in range(bands):
            for tile, ref in enumerate(refs):
                copy = pltpu.make_async_copy(
                    source.at[band, :, pl.ds(tile * LANES, LANES)], ref.at[band], sems.at[image, band, tile]
                )
                copy.start()
                copies.append((image * bands + band, tile, ref, band, copy))
    cell = lax.broadcasted_iota(jnp.int32, (width, LANES), 0)
    place = lax.broadcasted_iota(jnp.int32, (width, LANES), 1)
    weights = jnp.where(place - LEAD == cell // FACTOR, 1.0 / (FACTOR * FACTOR), 0.0).astype(jnp.bfloat16)
    means = []
    packed = [None, None]
    for image, (count, offset) in enumerate(((REACH, 0), (DEPTH, REACH))):
        for pair in range(0, bands, 2):
            some = range(pair, pair + 2)
            group = copies[2 * (image * bands + pair) : 2 * (image * bands + pair + 2)]
            for *_, copy in group:
                copy.wait()
            sums = {}
            for plane, tile, ref, band, _ in group:
                parts = [ref[band, pl.ds(k, coarse_height, stride=FACTOR), :] for k in range(FACTOR)]
                while len(parts) > 1:
                    parts = [x + y for x, y in zip(parts[::2], parts[1::2])]
                sums[band, tile] = parts[0]
            tall = [jnp.concatenate([sums[band, tile] for tile in range(2)], axis=1) for band in some]
            means.append(split_dot(jnp.concatenate(tall, axis=0), weights))
            packed = [
                pack_image(packed[side], bool(side), (seconds, firsts)[image], some, count, offset) for side in range(2)
            ]
    means = jnp.concatenate(means, axis=0)
    get_shifts.wait()
    shift_rows = shifts[0, 0, 0].astype(jnp.float32)
    shift_cols = shifts[0, 0, 1].astype(jnp.float32)
    place = lanes_of(height // 2) & (HALF - 1)
    packed = [
        jnp.where(place == SHIFT_R, shift_rows, jnp.where(place == SHIFT_C, shift_cols, jnp.where(place == EXISTS, 1.0, x)))
        for x in packed
    ]
    to_left, to_right = [pack_means(packed[side], bool(side), means) for side in range(2)]
    coarse[...] = means
    own_meta[...] = jnp.where(lane < SLOT, shift_rows, shift_cols)
    even = is_even("col", swap_0)
    swap_0[...] = jnp.where(even, to_right, to_left)
    swap_1[...] = jnp.where(even, to_left, to_right)


def message_kernel(
    count, coarse, own_meta, got_0, got_1, up_part, down_part, _whole, swap_0, swap_1, from_left, from_right, wide
):
    other = without_ends(got_1, "col", count)
    even = is_even("col", got_0)
    from_right[...] = jnp.where(even, got_0[...], other)
    from_left[...] = jnp.where(even, other, got_0[...])
    planes_coarse, coarse_height, _ = wide.shape
    bands = planes_coarse // 2
    end = from_left.shape[0]
    coarse_width = COLUMNS // FACTOR
    lane = lanes_of()
    wides = []
    for plane in range(planes_coarse):
        half, block = divmod(plane, planes_coarse // 2)
        for step in range(coarse_height // SUB):
            own = slice(plane * coarse_height + step * SUB, plane * coarse_height + (step + 1) * SUB)
            rows = slice(block * coarse_height + step * SUB, block * coarse_height + (step + 1) * SUB)
            at = half * HALF
            left = from_left[rows, :]
            right = from_right[rows, :]
            start = LEAD - C_SECOND
            cells = turn(left, start - at - COARSE_A)
            cells = jnp.where(lane >= start + 3, turn(left, start + 3 - at - COARSE_B), cells)
            cells = jnp.where(lane >= LEAD, coarse[own, :], cells)
            start = LEAD + coarse_width
            cells = jnp.where(lane >= start, turn(right, start - at - COARSE_A), cells)
            cells = jnp.where(lane >= start + 3, turn(right, start + 3 - at - COARSE_B), cells)
            wides.append((plane, step, cells))
    for plane, step, cells in wides:
        wide[plane, step * SUB : (step + 1) * SUB, :] = cells
    row = lax.broadcasted_iota(jnp.int32, (SUB, LANES), 0)
    meta = own_meta[...]
    for message, at in ((from_left, 48), (from_right, 80)):
        first_rows = message[0:SUB, :]
        rows = jnp.broadcast_to(first_rows[:, SHIFT_R : SHIFT_R + 1], (SUB, LANES))
        cols = jnp.broadcast_to(first_rows[:, SHIFT_C : SHIFT_C + 1], (SUB, LANES))
        meta = jnp.where(lane >= at, rows, meta)
        meta = jnp.where(lane >= at + 16, cols, meta)

    def beside(rows, half):
        left = from_left[rows, :]
        right = from_right[rows, :]
        cells = jnp.zeros((SUB, LANES), jnp.float32)
        for band in range(bands):
            at = half * HALF + band * SLOT
            cells = jnp.where(lane >= band * H_BAND, turn(right, band * H_BAND - at), cells)
            cells = jnp.where(lane >= band * H_BAND + SLOT, turn(left, band * H_BAND + SLOT - at), cells)
        return cells

    even = is_even("row", meta)
    parts = []
    for part, half, near, next_rows, row_of in (
        (up_part, 0, slice(0, 8), slice(8, 16), 0),
        (down_part, 1, slice(end - 8, end), slice(end - 16, end - 8), 7),
    ):
        eight = beside(near, half)
        one = beside(next_rows, half)
        one = jnp.broadcast_to(one[row_of : row_of + 1], (SUB, LANES))
        coarse_rows = []
        for band in range(bands):
            rows = slice(0, C_SECOND) if half == 0 else slice(coarse_height - C_SECOND, coarse_height)
            second = wide[band, rows, :]
            first = turn(wide[bands + band, rows, :], HALF)
            coarse_rows.append(jnp.where(lanes_like(second) < HALF, second, first))
        parts.append([
            (part[E8:H8, :], E8), (eight, H8), (part[E1:H1, :], E1), (jnp.where(row == 0, one, meta), H1),
            (part[F4:CS, :], F4), *[(x, CS + k * C_SECOND) for k, x in enumerate(coarse_rows)],
        ])
    for (up, at), (down, _) in zip(*parts):
        even = is_even("row", up)
        swap_0[at : at + up.shape[0], :] = jnp.where(even, down, up)
        swap_1[at : at + up.shape[0], :] = jnp.where(even, up, down)


def coarse_flow_of(second, first, mask):
    def along_rows(x):
        return pltpu.roll(x, x.shape[0] - 1, 0) - pltpu.roll(x, 1, 0)

    def along_cols(x):
        return pltpu.roll(x, LANES - 1, 1) - pltpu.roll(x, 1, 1)

    bands = BANDS
    size = second.shape[0] // bands
    grad_rows = 0.125 * along_rows(second)
    grad_cols = 0.125 * along_cols(second)
    offset = 0.25 * (second - first)
    data = jnp.clip(offset, -LIMIT, LIMIT)
    yield

    def pull(grads):
        terms = data * grads
        return sum(terms[k * size : (k + 1) * size] for k in range(bands))

    def tall(x):
        return jnp.concatenate([x] * bands, axis=0)

    flow = [-mask * pull(grad_rows), -mask * pull(grad_cols)]
    extrapolated = [2.0 * x for x in flow]
    dual_rows = [0.0, 0.0]
    dual_cols = [0.0, 0.0]
    yield
    for step in range(1, STEPS):
        changes = [(along_rows(x), along_cols(x)) for x in extrapolated]
        yield
        data = data + offset + grad_rows * tall(extrapolated[0]) + grad_cols * tall(extrapolated[1])
        data = jnp.clip(data, -LIMIT, LIMIT)
        yield
        for c in range(2):
            rows = dual_rows[c] + changes[c][0]
            cols = dual_cols[c] + changes[c][1]
            scale = jnp.minimum(mask, (8.0 * ALPHA) * lax.rsqrt(rows * rows + cols * cols))
            dual_rows[c] = rows * scale
            dual_cols[c] = cols * scale
        yield
        divergences = [along_rows(dual_rows[c]) + along_cols(dual_cols[c]) for c in range(2)]
        yield
        pulls = [pull(grad_rows), pull(grad_cols)]
        yield
        for c in range(2):
            following = flow[c] + mask * ((1.0 / 64.0) * divergences[c] - pulls[c])
            extrapolated[c] = 2.0 * following - flow[c]
            flow[c] = following
        yield
    return flow


def columns_of_planes(planes):
    whole = lax.broadcasted_iota(jnp.int32, (LANES, COLUMNS), 1)
    lane = lax.broadcasted_iota(jnp.int32, (LANES, LANES), 1)
    strip = jnp.where(lane < S_MID, lane, jnp.where(lane < S_LEFT, lane + (COLUMNS - S_RIGHT), lane - LANES))
    return jnp.concatenate([x for x, wanted in ((whole, "whole"), (strip, "strip")) if wanted in planes], axis=1)


def upsample(flow, planes, target):
    column = columns_of_planes(planes)
    source = lax.broadcasted_iota(jnp.int32, column.shape, 0)
    spread = jnp.where(source - LEAD == lax.shift_right_arithmetic(column, 3), float(FACTOR), 0.0).astype(jnp.bfloat16)
    rows = flow[0].shape[0]
    wide = split_dot(UNIT * jnp.concatenate(flow, axis=0), spread)
    for c in range(2):
        for tile in range(column.shape[1] // LANES):
            target[c, tile] = wide[c * rows : (c + 1) * rows, tile * LANES : (tile + 1) * LANES]


def repeat_rows(spread, initial, cells):
    for c in range(2):
        for tile in range(initial.shape[1]):
            rows = [jnp.broadcast_to(spread[c, tile, cell : cell + 1, :], (SUB, LANES)) for cell in cells]
            initial[c, tile, GUARD : GUARD + SUB * len(cells), :] = jnp.concatenate(rows, axis=0)


def shift_whole(here, shift):
    turned = [turn_back(x, shift) for x in here]
    lane = lanes_like(here[0])
    return [
        jnp.where(lane + shift >= LANES, turned[1], turned[0]),
        jnp.where(lane + shift < 0, turned[0], turned[1]),
    ]


def edge_lanes(rows):
    lane = lanes_of(rows)
    return lane == LANES - 1, lane == 0


def columns_whole(fields, edges):
    rows = fields[0].shape[0]
    if rows not in edges:
        edges[rows] = edge_lanes(rows)
    last, first = edges[rows]
    ahead = [pltpu.roll(x, LANES - 1, 1) for x in fields]
    behind = [pltpu.roll(x, 1, 1) for x in fields]
    return [
        jnp.where(last, ahead[1], ahead[0]) - behind[0],
        ahead[1] - jnp.where(first, behind[0], behind[1]),
    ]


def rows_within(tall):
    size = tall.shape[0]
    return (pltpu.roll(tall, size - 1, 0) - pltpu.roll(tall, 1, 0))[SUB : size - SUB]


def columns_strip(field):
    return pltpu.roll(field, LANES - 1, 1) - pltpu.roll(field, 1, 1)


def strip_moved(window, centre, right, left):
    own = turn_back(window(centre[0]), centre[1])
    beyond_left = turn_back(window(left[0]), left[1])
    beyond_right = turn_back(window(right[0]), right[1])
    lane = lanes_like(own)
    beyond = jnp.where((lane >= S_LEFT) | (lane < S_MID), beyond_left, beyond_right)
    return own, beyond


def strip_joined(own, beyond):
    lane = lanes_like(own)
    is_beyond = lane >= S_RIGHT
    of_next = is_beyond & (lane != S_RIGHT) | (lane == 0)
    of_previous = is_beyond & (lane != LANES - 1) | (lane == S_RIGHT - 1)
    change = turn(jnp.where(of_next, beyond, own), -1) - turn(jnp.where(of_previous, beyond, own), 1)
    return jnp.where(is_beyond, beyond, own), change


def fine_steps(
    rows_total, chunk, columns, initial, extrap, dual_rows, dual_cols, change, dual_data,
    offsets, grads_rows, grads_cols, data_row, masks_of, result, kept, done=lambda k: None, first_pulls=None, depth=1,
):
    assert STEPS == 3
    planes = len(offsets)
    bands = offsets[0].shape[0]
    chunks = rows_total // chunk

    def places(k, trim=(0, 0)):
        start, size = k * chunk + trim[0], chunk - sum(trim)
        return pl.ds(GUARD + start, size), pl.ds(start, size), pl.ds(data_row(k) + trim[0], size)

    def row_change(ref, c, tile, at):
        return ref[c, tile, pl.ds(at.start + 1, at.size), :] - ref[c, tile, pl.ds(at.start - 1, at.size), :]

    def clip(x):
        return jnp.clip(x, -UNIT * LIMIT, UNIT * LIMIT)

    tiles = range(planes)

    for step in range(STEPS):
        source = initial if step == 0 else extrap
        final = step == STEPS - 1

        def dual(item, source=source, step=step):
            k, c = item
            at, own, _ = places(k)
            masks = masks_of(own)
            along = columns([source[c, tile, at, :] for tile in tiles])
            values = []
            for tile in tiles:
                rows = row_change(source, c, tile, at)
                cols = along[tile]
                if step > 0:
                    rows = rows + dual_rows[c, tile, at, :]
                    cols = cols + dual_cols[c, tile, own, :]
                scale = jnp.minimum(masks[tile], lax.rsqrt(rows * rows + cols * cols))
                values.append((rows * scale, cols * scale))
            return values

        def store_dual(item, values):
            k, c = item
            for tile, (rows, cols) in enumerate(values):
                dual_rows[c, tile, places(k)[0], :] = rows
                dual_cols[c, tile, places(k)[1], :] = cols

        staggered([(k, c) for k in range(chunks) for c in range(2)], dual, store_dual, depth)
        along_of = {}

        def primal(item, step=step, final=final, along_of=along_of):
            k, tile = item
            at, own, data = places(k, kept(k) if final else (0, 0))
            if k not in along_of:
                along_of[k] = [columns([dual_cols[c, t, own, :] for t in tiles]) for c in range(2)]
            mask = masks_of(own)[tile]
            start = [initial[c, tile, at, :] for c in range(2)]
            if step > 0:
                moved = [extrap[c, tile, at, :] - start[c] for c in range(2)]
            if step == 1:
                changes = [0.5 * x for x in moved]
            if step == 2:
                changes = [change[c, tile, own, :] for c in range(2)]
            pulls = [None, None]
            duals = []
            ready = step == 0 and first_pulls is not None
            if ready:
                pulls = [first_pulls[c, tile, own, :] for c in range(2)]
            for band in range(0 if ready else bands):
                gradient = (grads_rows[tile][band, data, :], grads_cols[tile][band, data, :])
                value = offsets[tile][band, data, :]
                if step > 0:
                    earlier = clip(value) if step == 1 else dual_data[band, tile, own, :]
                    value = (value + earlier) + (gradient[0] * moved[0] + gradient[1] * moved[1])
                value = clip(value)
                duals.append(value)
                for c in range(2):
                    term = value * gradient[c]
                    pulls[c] = term if pulls[c] is None else pulls[c] + term
            flows, nexts = [], []
            for c in range(2):
                divergence = row_change(dual_rows, c, tile, at) + along_of[k][c][tile]
                moving = (mask * (1.0 / 64.0)) * divergence - pulls[c]
                total = moving if step == 0 else changes[c] + moving
                flows.append((start[c] + total) * (1.0 / UNIT) if final else total)
                nexts.append(None if final else start[c] + (total + moving))
            return flows, nexts, duals

        def store_primal(item, results, step=step, final=final):
            k, tile = item
            flows, nexts, duals = results
            at, own, _ = places(k, kept(k) if final else (0, 0))
            for c in range(2):
                if final:
                    result[c, tile, own, :] = flows[c]
                else:
                    if step > 0:
                        change[c, tile, own, :] = flows[c]
                    extrap[c, tile, at, :] = nexts[c]
            if final:
                if tile == planes - 1:
                    done(k)
            elif step > 0:
                for band in range(bands):
                    dual_data[band, tile, own, :] = duals[band]

        staggered([(k, tile) for k in range(chunks) for tile in tiles], primal, store_primal, depth)


def clear_guards(*refs):
    for ref in refs:
        rows = ref.shape[2]
        zero = jnp.zeros((GUARD, LANES), jnp.float32)
        for c in range(2):
            for tile in range(ref.shape[1]):
                ref[c, tile, 0:GUARD, :] = zero
                ref[c, tile, rows - GUARD : rows, :] = zero


def fine_scratch(bands, planes, rows):
    guarded = pltpu.VMEM((2, planes, rows + 2 * GUARD, LANES), jnp.float32)
    plain = pltpu.VMEM((2, planes, rows, LANES), jnp.float32)
    return [guarded, guarded, guarded, plain, plain, pltpu.VMEM((bands, planes, rows, LANES), jnp.float32)]


def pieces(bands, height, rows):
    assert (height - 2 * SUB) % rows == 0
    return [(band, row) for row in range(SUB, height - SUB, rows) for band in range(bands)]


def whole_terms_kernel(
    second_0, second_1, first_0, first_1, coarse, own_meta,
    offset, grad_rows, grad_cols, initial, strip_e, strip_f, up, down, moved, spread,
):
    seconds, firsts = (second_0, second_1), (first_0, first_1)
    bands, height, _ = second_0.shape
    block = 40
    coarse_height = coarse.shape[0] // (2 * bands)
    centre = shift_at(own_meta, 0, 0)
    def windows(band, row, rows):
        here = [ref[band, pl.ds(row + centre[0], rows), :].reshape(-1, LANES) for ref in seconds]
        return shift_whole(here, centre[1])

    woven = Woven(coarse_flow_of(coarse[0 : bands * coarse_height, :], coarse[bands * coarse_height :, :], 1.0))

    def strips_of(item):
        band, row = item
        rows = slice(row, row + LANES)
        return strip_own([ref[band, rows, :] for ref in seconds]), strip_own([ref[band, rows, :] for ref in firsts])

    def store_strips(item, results):
        band, row = item
        strip_e[band, row : row + LANES, :], strip_f[band, row : row + LANES, :] = results

    staggered([(band, row) for band in range(bands) for row in range(0, height, LANES)], strips_of, store_strips, 1, woven)

    ends = [(row, windows(slice(None), row, SUB)) for row in (SUB // 2, height - SUB - SUB // 2)]
    for row, values in ends:
        for tile in range(2):
            moved[tile, :, row : row + SUB, :] = values[tile].reshape(bands, SUB, LANES)

    def store_moved(item, values):
        band, row = item
        for tile in range(2):
            moved[tile, band, row : row + 120, :] = values[tile]

    staggered(pieces(bands, height, 120), lambda item: windows(*item, 120), store_moved, 3, woven)

    edges = {}

    def values_of(item):
        band, row = item
        rows = slice(row, row + block)
        values = [moved[tile, band, rows, :] for tile in range(2)]
        along = columns_whole(values, edges)
        own = [ref[band, rows, :] for ref in firsts]
        return [(0.25 * UNIT) * (x - y) for x, y in zip(values, own)], [0.125 * x for x in along]

    def store_values(item, results):
        band, row = item
        offsets, gradients = results
        data = slice(row + HALO, row + HALO + block)
        for tile in range(2):
            offset[tile, band, data, :] = offsets[tile]
            grad_cols[tile, band, data, :] = gradients[tile]

    staggered(pieces(bands, height, block), values_of, store_values, 3, woven)

    def gradient_of(item):
        band, row = item
        return [0.125 * rows_within(moved[tile, band, row - SUB : row + 40 + SUB, :]) for tile in range(2)]

    def store_gradient(item, results):
        band, row = item
        for tile in range(2):
            grad_rows[tile, band, row + HALO : row + HALO + 40, :] = results[tile]

    staggered(pieces(bands, height, 40), gradient_of, store_gradient, 3, woven)

    parts = []
    for band in range(bands):
        for second, first in zip(seconds, firsts):
            parts.append((
                second[band, 0:16, :], first[band, 0:8, :],
                second[band, height - 16 : height, :], first[band, height - 8 : height, :],
            ))
    for k, (second_top, first_top, second_end, first_end) in enumerate(parts):
        up[E8 + 8 * k : E8 + 8 * k + 8, :] = second_top[0:8]
        up[E1 + k : E1 + k + 1, :] = second_top[8:9]
        up[F4 + 4 * k : F4 + 4 * k + 4, :] = first_top[0:4]
        down[E8 + 8 * k : E8 + 8 * k + 8, :] = second_end[8:16]
        down[E1 + k : E1 + k + 1, :] = second_end[7:8]
        down[F4 + 4 * k : F4 + 4 * k + 4, :] = first_end[4:8]
    for target in (up, down):
        for start, end in ((H8, E1), (H1, F4), (CS, ROW_MESSAGE)):
            target[start:end, :] = jnp.zeros((end - start, LANES), jnp.float32)

    upsample(woven.finish(), ("whole",), spread)
    clear_guards(initial)
    rows_total = initial.shape[2] - 2 * GUARD
    repeat_rows(spread, initial, [BEGIN // FACTOR + k for k in range(rows_total // SUB)])


def whole_steps_kernel(
    initial, offset, grad_rows, grad_cols, result, extrap, dual_rows, dual_cols, change, dual_data
):
    rows_total = result.shape[2]
    clear_guards(extrap, dual_rows)
    chunk = 16
    edges = {}
    fine_steps(
        rows_total, chunk, lambda fields: columns_whole(fields, edges),
        initial, extrap, dual_rows, dual_cols, change, dual_data,
        *[[ref.at[tile] for tile in range(2)] for ref in (offset, grad_rows, grad_cols)],
        lambda k: HALO + BEGIN + k * chunk, lambda own: (1.0, 1.0), result,
        lambda k: (SUB * (k == 0), SUB * (k == rows_total // chunk - 1)), depth=3,
    )


def strip_kernel(
    count, strip_e, strip_f, from_left, from_right, wide, own_message, whole,
    middle, strip_out, first_ends, offset, grad_rows, grad_cols,
    both, moved, result, spread, initial, extrap, dual_rows, dual_cols, change, dual_data,
):
    bands, height, _ = strip_e.shape
    block = 40
    coarse_height = height // FACTOR
    coarse_width = COLUMNS // FACTOR
    rows_total = height - 2 * BEGIN
    lane = lanes_of()
    centre, right, left = shifts_of(own_message)
    has_left, has_right = neighbours("col", count)
    exists = jnp.where(lane < S_RIGHT, 1.0, jnp.where(lane < S_LEFT, has_right, has_left))

    def tall_factor(rows):
        return 0.125 * jnp.concatenate([exists] * (rows // SUB), axis=0)

    mask = jnp.where(lane < LEAD, has_left, jnp.where(lane < LEAD + coarse_width, 1.0, has_right))
    mask = jnp.concatenate([mask] * (coarse_height // SUB), axis=0)
    cells = [wide[k * bands : (k + 1) * bands].reshape(bands * coarse_height, LANES) for k in range(2)]
    woven = Woven(coarse_flow_of(*cells, mask))

    def halves(row, rows):
        half = row // (height // 2)
        start = row - half * (height // 2)
        return half, slice(start, start + rows)

    def second_of(item):
        band, row = item
        half, message = halves(row, LANES)
        return strip_second(strip_e[band, row : row + LANES, :], from_left, from_right, message, half, band)

    def store_second(item, value):
        band, row = item
        strip_out[band, row : row + LANES, :] = value

    staggered([(band, row) for row in range(0, height, LANES) for band in range(bands)], second_of, store_second, 1, woven)

    def first_of(band, row, rows):
        half, message = halves(row, rows)
        return strip_first(strip_f[band, row : row + rows, :], from_left, from_right, message, half, band)

    firsts = [(end, band, first_of(band, (0, height - SUB)[end], SUB)) for end in range(2) for band in range(bands)]
    for end, band, value in firsts:
        first_ends[end, band] = value

    def windows(band, row, rows):
        return strip_moved(
            lambda shift: strip_out[band, pl.ds(row + shift, rows), :].reshape(-1, LANES), centre, right, left
        )

    ends = [
        (row, strip_joined(*windows(slice(None), row, SUB))[0]) for row in (SUB // 2, height - SUB - SUB // 2)
    ]
    for row, value in ends:
        moved[:, row : row + SUB, :] = value.reshape(bands, SUB, LANES)

    def store_moved(item, values):
        band, row = item
        for k in range(2):
            both[k, band, row : row + 120, :] = values[k]

    staggered(pieces(bands, height, 120), lambda item: windows(*item, 120), store_moved, 3, woven)

    factor = tall_factor(block)

    def values_of(item):
        band, row = item
        value, along = strip_joined(*[both[k, band, row : row + block, :] for k in range(2)])
        return value, (0.25 * UNIT) * (value - first_of(band, row, block)), factor * along

    def store_values(item, results):
        band, row = item
        data = slice(row + HALO, row + HALO + block)
        moved[band, row : row + block, :], offset[band, data, :], grad_cols[band, data, :] = results

    staggered(pieces(bands, height, block), values_of, store_values, 3, woven)

    def gradient_of(item):
        band, row = item
        return factor * rows_within(moved[band, row - SUB : row + block + SUB, :])

    def store_gradient(item, value):
        band, row = item
        grad_rows[band, row + HALO : row + HALO + block, :] = value

    staggered(pieces(bands, height, block), gradient_of, store_gradient, 3, woven)

    upsample(woven.finish(), ("strip",), spread)
    clear_guards(initial, extrap, dual_rows)
    repeat_rows(spread, initial, [BEGIN // FACTOR + k for k in range(rows_total // SUB)])

    chunk = 16
    masks = jnp.concatenate([exists] * (chunk // SUB), axis=0)
    fine_steps(
        rows_total, chunk, lambda fields: [columns_strip(fields[0])],
        initial, extrap, dual_rows, dual_cols, change, dual_data, [offset], [grad_rows], [grad_cols],
        lambda k: HALO + BEGIN + k * chunk, lambda own: (masks[: own.size],), result,
        lambda k: (SUB * (k == 0), SUB * (k == rows_total // chunk - 1)), depth=4,
    )
    join(whole, result.at[:, 0], middle, slice(SUB, rows_total - SUB))


def join(whole, strip, target, rows):
    lane = lanes_of(rows.stop - rows.start)
    values = []
    for c in range(2):
        edge = strip[c, rows, :]
        start = jnp.where(lane < EDGE, edge, whole[c, 0, rows, :])
        values.append((start, jnp.where(lane >= LANES - EDGE, turn(edge, S_TURN), whole[c, 1, rows, :])))
    for c in range(2):
        target[c, rows, 0:LANES], target[c, rows, LANES:COLUMNS] = values[c]


def outer_kernel(
    counts, second_0, second_1, first_0, first_1, strip_e, first_ends, wide, got_1, got_0, middle, own_message,
    _wo, _wr, _wc, _so, _sr, _sc,
    flow_out, coarse_out, whole_offset, whole_rows, whole_cols, strip_offset, strip_rows, strip_cols,
    from_up, from_down, extended, tall, spread, masks, result, joined, coarse_result, pulls, sems,
    initial, extrap, dual_rows, dual_cols, change, dual_data,
):
    bands, height, _ = second_0.shape
    coarse_height = height // FACTOR
    coarse_width = COLUMNS // FACTOR
    rows_total = 2 * EACH
    lane = lanes_of()

    put_middle = pltpu.make_async_copy(
        middle.at[:, pl.ds(MARGIN - BEGIN, height - 2 * MARGIN), :],
        flow_out.at[:, pl.ds(MARGIN, height - 2 * MARGIN), :],
        sems.at[0],
    )
    put_middle.start()
    own, one, other = [shifts_of(message) for message in (own_message, got_0, got_1)]
    odd = lax.axis_index("row") % 2

    def of_row(for_even, for_odd):
        return [tuple(jnp.where(odd == 0, x, y) for x, y in zip(*pair)) for pair in zip(for_even, for_odd)]

    above, below = of_row(other, one), of_row(one, other)

    other = without_ends(got_1, "row", counts[0])
    even = is_even("row", got_0)
    from_down[...] = jnp.where(even, got_0[...], other)
    from_up[...] = jnp.where(even, other, got_0[...])

    has_up, has_down = neighbours("row", counts[0])
    has_left, has_right = neighbours("col", counts[1])
    exists = jnp.where(lane < S_RIGHT, 1.0, jnp.where(lane < S_LEFT, has_right, has_left))

    zero = jnp.zeros((SUB, LANES), jnp.float32)
    tall_rows = coarse_height + 2 * LEAD
    parts = []
    fill = jnp.zeros((LEAD - C_SECOND, LANES), jnp.float32)
    for plane in range(2 * bands):
        at = CS + C_SECOND * (plane % bands)
        ends = [turn(message[at : at + C_SECOND, :], HALF * (plane // bands)) for message in (from_up, from_down)]
        parts.append([fill, ends[0], wide[plane], ends[1], fill])
    for plane, values in enumerate(parts):
        tall[plane] = jnp.concatenate(values, axis=0)
    across = jnp.where(lane < LEAD, has_left, jnp.where(lane < LEAD + coarse_width, 1.0, has_right))
    mask = jnp.concatenate([across * has_up] + [across] * (coarse_height // SUB) + [across * has_down], axis=0)
    for end in range(2):
        message = (from_up, from_down)[end]
        beside = message[H8 : H8 + 8, :]
        beside_one = jnp.broadcast_to(message[H1 : H1 + 1, :], (SUB, LANES))
        parts = []
        for band in range(bands):
            eights = [message[E8 + 8 * k : E8 + 8 * k + 8, :] for k in (2 * band, 2 * band + 1)]
            ones = [jnp.broadcast_to(message[E1 + k : E1 + k + 1, :], (SUB, LANES)) for k in (2 * band, 2 * band + 1)]
            eights.append(strip_halo(strip_own(eights), beside, band, 0, REACH))
            ones.append(strip_halo(strip_own(ones), beside_one, band, 0, REACH))
            for tile, (eight, one) in enumerate(zip(eights, ones)):
                source = (second_0, second_1, strip_e)[tile]
                if end == 0:
                    parts.append((tile, band, [one, eight, source[band, 0:24, :]]))
                else:
                    parts.append((tile, band, [source[band, height - 24 : height, :], eight, one]))
        for tile, band, values in parts:
            extended[end, tile, band] = jnp.concatenate(values, axis=0)
    cells = [tall[k * bands : (k + 1) * bands].reshape(bands * tall_rows, LANES) for k in range(2)]
    woven = Woven(coarse_flow_of(*cells, mask))
    edges = {}
    rows_data = whole_offset.shape[2]
    exists_tall = jnp.concatenate([exists] * bands, axis=0)

    def rows_of(halo, end):
        if halo:
            return slice(0, SUB) if end == 0 else slice(rows_data - SUB, rows_data)
        return slice(HALO, HALO + SUB) if end == 0 else slice(rows_data - HALO - SUB, rows_data - HALO)

    def values_of(item):
        halo, end = item
        message = (from_up, from_down)[end]
        base = (SUB, 3 * SUB)[end] if halo else 2 * SUB
        shifts = (above, below)[end] if halo else own
        factor = 0.125 * (has_up, has_down)[end] if halo else 0.125

        def here(tile, shift):
            return extended[end, tile, :, pl.ds(base + shift, SUB), :].reshape(-1, LANES)

        def down_up(tile, shift):
            return here(tile, shift + 1) - here(tile, shift - 1)

        own_rows = slice(0, SUB) if end == 0 else slice(height - SUB, height)
        if halo:
            firsts = [[], [], []]
            for band in range(bands):
                eights = []
                for k in (2 * band, 2 * band + 1):
                    four = message[F4 + 4 * k : F4 + 4 * k + 4, :]
                    eights.append(jnp.concatenate([four, four], axis=0))
                eights.append(strip_halo(strip_own(eights), message[H8 : H8 + 8, :], band, REACH, DEPTH))
                for tile in range(3):
                    firsts[tile].append(eights[tile])
            firsts = [jnp.concatenate(x, axis=0) for x in firsts]
        else:
            firsts = [x.reshape(-1, LANES) for x in (first_0[:, own_rows, :], first_1[:, own_rows, :], first_ends[end])]
        centre = shifts[0]
        values = shift_whole([here(tile, centre[0]) for tile in range(2)], centre[1])
        changes = shift_whole([down_up(tile, centre[0]) for tile in range(2)], centre[1])
        along = columns_whole(values, edges)
        value, across_cols = strip_joined(*strip_moved(lambda shift: here(2, shift), *shifts))
        change_rows, _ = strip_joined(*strip_moved(lambda shift: down_up(2, shift), *shifts))
        return (
            [(0.25 * UNIT) * (x - y) for x, y in zip([*values, value], firsts)],
            [*[factor * x for x in changes], (factor * exists_tall) * change_rows],
            [*[factor * x for x in along], (factor * exists_tall) * across_cols],
        )

    def store_values(item, results):
        rows = rows_of(*item)
        for values, whole, strip in zip(
            results, (whole_offset, whole_rows, whole_cols), (strip_offset, strip_rows, strip_cols)
        ):
            values = [x.reshape(bands, SUB, LANES) for x in values]
            for tile in range(2):
                whole[tile, :, rows, :] = values[tile]
            strip[:, rows, :] = values[2]

    staggered([(halo, end) for halo in (True, False) for end in range(2)], values_of, store_values, 3, woven)

    chunk = 16
    per = EACH // chunk

    def data_row(k):
        return k // per * (rows_data - EACH) + k % per * chunk

    offsets = [whole_offset.at[0], whole_offset.at[1], strip_offset]
    grads_rows = [whole_rows.at[0], whole_rows.at[1], strip_rows]
    grads_cols = [whole_cols.at[0], whole_cols.at[1], strip_cols]

    def pulls_of(item):
        k, tile = item
        data = pl.ds(k * (rows_data - EACH), EACH)
        duals = [jnp.clip(offsets[tile][band, data, :], -UNIT * LIMIT, UNIT * LIMIT) for band in range(bands)]
        return [
            sum(duals[band] * grads[tile][band, data, :] for band in range(bands)) for grads in (grads_rows, grads_cols)
        ]

    def store_pulls(item, values):
        k, tile = item
        for c in range(2):
            pulls[c, tile, k * EACH : (k + 1) * EACH, :] = values[c]

    staggered([(k, tile) for k in range(2) for tile in range(3)], pulls_of, store_pulls, 1, woven)

    flow = woven.finish()
    for c in range(2):
        coarse_result[c] = turn(flow[c][LEAD : LEAD + coarse_height], -LEAD)[:, :coarse_width]
    put_coarse = pltpu.make_async_copy(coarse_result, coarse_out, sems.at[1])
    upsample(flow, ("whole", "strip"), spread)
    clear_guards(initial, extrap, dual_rows)
    each = EACH // SUB
    repeat_rows(
        spread, initial,
        [LEAD - 1 + k for k in range(each)] + [tall_rows - LEAD + 1 - each + k for k in range(each)],
    )

    for i, value in enumerate((jnp.ones((SUB, LANES), jnp.float32), exists)):
        masks[i] = jnp.concatenate([value * has_up] + [value] * (rows_total // SUB - 2) + [value * has_down], axis=0)

    def masks_of(rows):
        whole = masks[0, rows, :]
        return (whole, whole, masks[1, rows, :])

    edges = {}
    puts = [
        pltpu.make_async_copy(
            joined.at[:, pl.ds(k * EACH + SUB, MARGIN), :],
            flow_out.at[:, pl.ds(k * (height - MARGIN), MARGIN), :],
            sems.at[2 + k],
        )
        for k in range(2)
    ]

    def finish(k):
        if k % per == per - 1:
            at = k // per * EACH + SUB
            join(result, result.at[:, 2], joined, slice(at, at + MARGIN))

    fine_steps(
        rows_total, chunk, lambda fields: columns_whole(fields[:2], edges) + [columns_strip(fields[2])],
        initial, extrap, dual_rows, dual_cols, change, dual_data,
        offsets, grads_rows, grads_cols, data_row, masks_of, result,
        lambda k: (SUB * (k % per == 0), SUB * (k % per == per - 1)), finish, pulls, depth=4,
    )
    puts.append(put_coarse)
    for put in puts:
        put.start()
    put_middle.wait()
    for put in puts:
        put.wait()


def swap_with(message, axis, start):
    names = ("row", "col")
    sizes = [lax.axis_size(name) for name in names]
    along = names.index(axis)
    count, others = sizes[along], sizes[1 - along]

    def number(place, other):
        row, col = (place, other) if along == 0 else (other, place)
        return row * sizes[1] + col

    pairs = [(number(i, k), number(i + 1, k)) for i in range(start, count - 1, 2) for k in range(others)]
    if start and axis == "col":
        pairs += [(number(i, k), number(i, k + 1)) for i in (0, count - 1) for k in range(0, others, 2)]
    elif start:
        pairs += [(number(0, k), number(count - 1, k)) for k in (0, others - 1)]
        pairs += [(number(i, k), number(i, k + 1)) for i in (0, count - 1) for k in range(1, others - 1, 2)]
    return lax.ppermute(message, names, pairs + [(j, i) for i, j in pairs])


def local(frame_first, frame_second, shifts):
    bands, height, width = frame_first.shape
    assert bands == 4 and width == COLUMNS and height % LANES == 0
    assert lax.axis_size("row") % 2 == 0 and lax.axis_size("col") % 2 == 0
    coarse_height = height // FACTOR
    coarse_width = width // FACTOR
    vmem = pl.BlockSpec(memory_space=pltpu.VMEM)
    hbm = pl.BlockSpec(memory_space=pltpu.HBM)
    tall_rows = coarse_height + 2 * LEAD
    inner_rows = height - 2 * BEGIN

    def shape(*sizes):
        return jax.ShapeDtypeStruct(sizes, jnp.float32)

    def scratch(*sizes):
        return pltpu.VMEM(sizes, jnp.float32)

    def call(kernel, name, arguments, outs, scratches=(), flops=1_000_000, **more):
        more = {"in_specs": [vmem] * len(arguments), "out_specs": (vmem,) * len(outs), **more}
        return pl.pallas_call(
            kernel,
            out_shape=tuple(outs),
            scratch_shapes=list(scratches),
            compiler_params=pltpu.CompilerParams(vmem_limit_bytes=24 * 1024 * 1024),
            cost_estimate=pl.CostEstimate(flops=flops, bytes_accessed=1_000_000, transcendentals=0),
            name=name,
            **more,
        )(*arguments)

    plane = shape(bands, height, LANES)
    column_message = shape(height // 2, LANES)
    row_message = shape(ROW_MESSAGE, LANES)
    whole_data = shape(2, bands, height + 2 * HALO, LANES)
    strip_data = shape(bands, height + 2 * HALO, LANES)

    *frames, coarse, swap_0, swap_1, own_meta = call(
        first_kernel,
        "means_and_message",
        [pltpu.with_memory_space_constraint(x, pltpu.HBM) for x in (frame_second, frame_first, shifts)],
        [*[plane] * 4, shape(2 * bands * coarse_height, LANES), column_message, column_message, shape(SUB, LANES)],
        [
            pltpu.SMEM((1, 1, 2), jnp.int32),
            pltpu.SemaphoreType.DMA((2, bands, 2)),
            pltpu.SemaphoreType.DMA,
        ],
        in_specs=[hbm] * 3,
    )
    got_0 = swap_with(swap_0, "col", 0)
    got_1 = swap_with(swap_1, "col", 1)

    *whole_terms, initial, strip_e, strip_f, up_part, down_part = call(
        whole_terms_kernel,
        "whole_terms",
        [*frames, coarse, own_meta],
        [
            *[whole_data] * 3, shape(2, 2, inner_rows + 2 * GUARD, LANES),
            plane, plane, row_message, row_message,
        ],
        [
            scratch(2, bands, height, LANES), scratch(2, 2, coarse_height, LANES),
        ],
        flops=8_000_000,
    )
    (whole,) = call(
        whole_steps_kernel,
        "whole_steps",
        [initial, *whole_terms],
        [shape(2, 2, inner_rows, LANES)],
        fine_scratch(bands, 2, inner_rows)[1:],
        flops=20_000_000,
    )

    swap_0, swap_1, from_left, from_right, wide = call(
        functools.partial(message_kernel, lax.axis_size("col")),
        "row_messages",
        [coarse, own_meta, got_0, got_1, up_part, down_part, whole],
        [row_message, row_message, column_message, column_message, shape(2 * bands, coarse_height, LANES)],
    )
    got_1 = swap_with(swap_1, "row", 1)
    got_0 = swap_with(swap_0, "row", 0)

    middle, strip_e, first_ends, *strip_terms = call(
        functools.partial(strip_kernel, lax.axis_size("col")),
        "strip",
        [strip_e, strip_f, from_left, from_right, wide, swap_0, whole],
        [shape(2, inner_rows, width), plane, shape(2, bands, SUB, LANES), *[strip_data] * 3],
        [
            scratch(2, bands, height, LANES),
            scratch(bands, height, LANES),
            scratch(2, 1, inner_rows, LANES),
            scratch(2, 1, coarse_height, LANES),
            *fine_scratch(bands, 1, inner_rows),
        ],
        flops=16_000_000,
    )

    flow, coarse_flow, *_ = call(
        functools.partial(outer_kernel, (lax.axis_size("row"), lax.axis_size("col"))),
        "outer_rows",
        [
            *frames, strip_e, first_ends, wide, got_1, got_0, middle, swap_0,
            *whole_terms, *strip_terms,
        ],
        [shape(2, height, width), shape(2, coarse_height, coarse_width), *[whole_data] * 3, *[strip_data] * 3],
        [
            scratch(ROW_MESSAGE, LANES),
            scratch(ROW_MESSAGE, LANES),
            scratch(2, 3, bands, 40, LANES),
            scratch(2 * bands, tall_rows, LANES),
            scratch(2, 3, tall_rows, LANES),
            scratch(2, 2 * EACH, LANES),
            scratch(2, 3, 2 * EACH, LANES),
            scratch(2, 2 * EACH, width),
            scratch(2, coarse_height, coarse_width),
            scratch(2, 3, 2 * EACH, LANES),
            pltpu.SemaphoreType.DMA((4,)),
            *fine_scratch(bands, 3, 2 * EACH),
        ],
        out_specs=(hbm, hbm) + (vmem,) * 6,
        input_output_aliases={11 + k: 2 + k for k in range(6)},
    )
    return (flow, coarse_flow)


def solution(mesh):
    return jax.shard_map(
        local,
        mesh=mesh,
        in_specs=(P(None, "row", "col"), P(None, "row", "col"), P("row", "col", None)),
        out_specs=(P(None, "row", "col"), P(None, "row", "col")),
        check_vma=False,
    )
```

```python
import functools

import jax
import jax.numpy as jnp
from jax import lax
from jax.experimental import pallas as pl
from jax.experimental.pallas import tpu as pltpu
from jax.sharding import PartitionSpec as P

FACTOR = 8
MAXD = 4
BANDS = 4
STEPS = 3
LANES = 128
COLUMNS = 2 * LANES
HALF = 64
SUB = 8
DEPTH = 4
REACH = DEPTH + MAXD + 1
SLOT = 16
C_SECOND = 6
C_FIRST = 5
LEAD = 8
MARGIN = 48
EDGE = 46
GUARD = 8
HALO = 8
BEGIN = 40
EACH = MARGIN + 16
LIMIT = 0.3
ALPHA = 0.3
UNIT = 0.125 / ALPHA

S_MID = 55
S_RIGHT = 110
S_LEFT = LANES - REACH
S_TURN = COLUMNS - S_RIGHT - LANES

E8 = 0
H8 = 64
E1 = 72
H1 = 80
META = 81
F4 = 88
CS = 120
ROW_MESSAGE = 144
H_BAND = 32

COARSE_A = REACH + DEPTH
COARSE_B = SLOT + REACH + DEPTH
SHIFT_R = 2 * SLOT + REACH + DEPTH
SHIFT_C = SHIFT_R + 1
EXISTS = SHIFT_R + 2


def lanes_of(rows=SUB):
    return lax.broadcasted_iota(jnp.int32, (rows, LANES), 1)


def lanes_like(x):
    return lax.broadcasted_iota(jnp.int32, x.shape, 1)


def turn(x, amount):
    amount = amount % LANES
    return x if amount == 0 else pltpu.roll(x, amount, 1)


def turn_back(x, shift):
    return pltpu.roll(x, lax.rem(LANES - shift, LANES), 1)


def split_dot(x, exact):
    high = x.astype(jnp.bfloat16)
    rest = x - high.astype(jnp.float32)
    middle = rest.astype(jnp.bfloat16)
    low = (rest - middle.astype(jnp.float32)).astype(jnp.bfloat16)
    parts = [jnp.dot(part, exact, preferred_element_type=jnp.float32) for part in (low, middle, high)]
    return parts[0] + parts[1] + parts[2]


def neighbours(axis, count):
    place = lax.axis_index(axis)
    return jnp.where(place > 0, 1.0, 0.0), jnp.where(place < count - 1, 1.0, 0.0)


def shift_at(ref, row, lane):
    numbers = ref[row : row + 1, :].astype(jnp.int32)
    return numbers[0, lane], numbers[0, lane + SLOT]


def shifts_of(message):
    return [shift_at(message, META, lane) for lane in (0, 80, 48)]


def is_even(axis, like):
    return jnp.broadcast_to(lax.axis_index(axis) % 2, like.shape) == 0


def without_ends(message, axis, count):
    place = jnp.broadcast_to(lax.axis_index(axis), message.shape)
    return jnp.where((place > 0) & (place < count - 1), message[...], 0.0)


def staggered(items, compute, store, depth, woven=None):
    pending = []
    for item in items:
        pending.append((item, compute(item)))
        if woven is not None:
            woven.advance()
        if len(pending) > depth:
            store(*pending.pop(0))
    for entry in pending:
        store(*entry)


class Woven:
    def __init__(self, stages):
        self.stages = stages
        self.result = None

    def advance(self):
        try:
            next(self.stages)
            return True
        except StopIteration as end:
            self.result = end.value if self.result is None else self.result
            return False

    def finish(self):
        while self.advance():
            pass
        return self.result


def pack_image(packed, to_right, planes, some, count, offset):
    _, height, _ = planes[0].shape
    plane = planes[int(to_right)]
    start = LANES - count if to_right else 0
    length = height // 2
    lane = lanes_of(length)
    for half in range(2):
        for band in some:
            at = half * HALF + band * SLOT + offset
            cells = turn(plane[band, half * length : (half + 1) * length, :], at - start)
            packed = cells if packed is None else jnp.where((lane >= at) & (lane < at + count), cells, packed)
    return packed


def place_of(lane):
    place = lane & (HALF - 1)
    first = (place >= COARSE_A) & (place < COARSE_A + 3)
    second = (place >= COARSE_B) & (place < COARSE_B + 3)
    return jnp.where(first, place - COARSE_A, jnp.where(second, place - COARSE_B + 3, -COLUMNS))


def pack_means(packed, cells):
    length = packed.shape[0]
    lane = lanes_of(length)
    own = place_of(lane) >= 0
    for half in range(2):
        mask = own & (lane >= half * HALF) & (lane < (half + 1) * HALF)
        packed = jnp.where(mask, cells[half * length : (half + 1) * length], packed)
    return packed


def strip_second(base, from_left, from_right, rows, half, band):
    at = half * HALF + band * SLOT
    lane = lanes_like(base)
    cells = jnp.where(lane >= S_RIGHT, turn(from_right[rows, :], S_RIGHT - at), base)
    return jnp.where(lane >= S_LEFT, turn(from_left[rows, :], S_LEFT - at), cells)


def strip_first(base, from_left, from_right, rows, half, band):
    at = half * HALF + band * SLOT + REACH
    lane = lanes_like(base)
    cells = jnp.where(lane >= S_RIGHT, turn(from_right[rows, :], S_RIGHT - at), base)
    return jnp.where(lane >= S_LEFT, turn(from_left[rows, :], LANES - DEPTH - at), cells)


def strip_halo(base, beside, band, start, count):
    at = band * H_BAND + start
    lane = lanes_like(base)
    cells = jnp.where(lane >= S_RIGHT, turn(beside, S_RIGHT - at), base)
    return jnp.where(lane >= S_LEFT, turn(beside, LANES - count - at - SLOT), cells)


def strip_own(planes):
    return jnp.where(lanes_like(planes[0]) < S_MID, planes[0], turn(planes[1], -S_TURN))


def first_kernel(
    second_hbm, first_hbm, shifts_hbm, second_0, second_1, first_0, first_1, coarse, swap_0, swap_1, own_meta,
    shifts, sems, shift_sem,
):
    seconds, firsts = (second_0, second_1), (first_0, first_1)
    bands, height, _ = second_0.shape
    width = COLUMNS
    coarse_height = height // FACTOR
    lane = lanes_of()
    get_shifts = pltpu.make_async_copy(shifts_hbm, shifts, shift_sem)
    get_shifts.start()
    copies = []
    for image, (source, refs) in enumerate(((second_hbm, seconds), (first_hbm, firsts))):
        for band in range(bands):
            for tile, ref in enumerate(refs):
                copy = pltpu.make_async_copy(
                    source.at[band, :, pl.ds(tile * LANES, LANES)], ref.at[band], sems.at[image, band, tile]
                )
                copy.start()
                copies.append((image * bands + band, tile, ref, band, copy))
    cell = lax.broadcasted_iota(jnp.int32, (width, LANES), 0)
    lanes = lax.broadcasted_iota(jnp.int32, (width, LANES), 1)
    near = place_of(lanes)
    wanted = jnp.concatenate([lanes - LEAD, near, near + (width // FACTOR - C_SECOND)], axis=1)
    cell = jnp.concatenate([cell] * 3, axis=1)
    weights = jnp.where(wanted == cell // FACTOR, 1.0 / (FACTOR * FACTOR), 0.0).astype(jnp.bfloat16)
    means = []
    packed = [None, None]
    for image, (count, offset) in enumerate(((REACH, 0), (DEPTH, REACH))):
        for pair in range(0, bands, 2):
            some = range(pair, pair + 2)
            group = copies[2 * (image * bands + pair) : 2 * (image * bands + pair + 2)]
            for *_, copy in group:
                copy.wait()
            sums = {}
            for plane, tile, ref, band, _ in group:
                parts = [ref[band, pl.ds(k, coarse_height, stride=FACTOR), :] for k in range(FACTOR)]
                while len(parts) > 1:
                    parts = [x + y for x, y in zip(parts[::2], parts[1::2])]
                sums[band, tile] = parts[0]
            tall = [jnp.concatenate([sums[band, tile] for tile in range(2)], axis=1) for band in some]
            means.append(split_dot(jnp.concatenate(tall, axis=0), weights))
            packed = [
                pack_image(packed[side], bool(side), (seconds, firsts)[image], some, count, offset) for side in range(2)
            ]
    means = jnp.concatenate(means, axis=0)
    get_shifts.wait()
    shift_rows = shifts[0, 0, 0].astype(jnp.float32)
    shift_cols = shifts[0, 0, 1].astype(jnp.float32)
    place = lanes_of(height // 2) & (HALF - 1)
    packed = [
        jnp.where(place == SHIFT_R, shift_rows, jnp.where(place == SHIFT_C, shift_cols, jnp.where(place == EXISTS, 1.0, x)))
        for x in packed
    ]
    to_left, to_right = [pack_means(packed[side], means[:, (side + 1) * LANES : (side + 2) * LANES]) for side in range(2)]
    coarse[...] = means[:, :LANES]
    own_meta[...] = jnp.where(lane < SLOT, shift_rows, shift_cols)
    even = is_even("col", swap_0)
    swap_0[...] = jnp.where(even, to_right, to_left)
    swap_1[...] = jnp.where(even, to_left, to_right)


def message_kernel(
    count, coarse, own_meta, got_0, got_1, up_part, down_part, _whole, swap_0, swap_1, from_left, from_right, wide
):
    other = without_ends(got_1, "col", count)
    even = is_even("col", got_0)
    from_right[...] = jnp.where(even, got_0[...], other)
    from_left[...] = jnp.where(even, other, got_0[...])
    planes_coarse, coarse_height, _ = wide.shape
    bands = planes_coarse // 2
    end = from_left.shape[0]
    coarse_width = COLUMNS // FACTOR
    lane = lanes_of()
    wides = []
    for plane in range(planes_coarse):
        half, block = divmod(plane, planes_coarse // 2)
        for step in range(coarse_height // SUB):
            own = slice(plane * coarse_height + step * SUB, plane * coarse_height + (step + 1) * SUB)
            rows = slice(block * coarse_height + step * SUB, block * coarse_height + (step + 1) * SUB)
            at = half * HALF
            left = from_left[rows, :]
            right = from_right[rows, :]
            start = LEAD - C_SECOND
            cells = turn(left, start - at - COARSE_A)
            cells = jnp.where(lane >= start + 3, turn(left, start + 3 - at - COARSE_B), cells)
            cells = jnp.where(lane >= LEAD, coarse[own, :], cells)
            start = LEAD + coarse_width
            cells = jnp.where(lane >= start, turn(right, start - at - COARSE_A), cells)
            cells = jnp.where(lane >= start + 3, turn(right, start + 3 - at - COARSE_B), cells)
            wides.append((plane, step, cells))
    for plane, step, cells in wides:
        wide[plane, step * SUB : (step + 1) * SUB, :] = cells
    row = lax.broadcasted_iota(jnp.int32, (SUB, LANES), 0)
    meta = own_meta[...]
    for message, at in ((from_left, 48), (from_right, 80)):
        first_rows = message[0:SUB, :]
        rows = jnp.broadcast_to(first_rows[:, SHIFT_R : SHIFT_R + 1], (SUB, LANES))
        cols = jnp.broadcast_to(first_rows[:, SHIFT_C : SHIFT_C + 1], (SUB, LANES))
        meta = jnp.where(lane >= at, rows, meta)
        meta = jnp.where(lane >= at + 16, cols, meta)

    def beside(rows, half):
        left = from_left[rows, :]
        right = from_right[rows, :]
        cells = jnp.zeros((SUB, LANES), jnp.float32)
        for band in range(bands):
            at = half * HALF + band * SLOT
            cells = jnp.where(lane >= band * H_BAND, turn(right, band * H_BAND - at), cells)
            cells = jnp.where(lane >= band * H_BAND + SLOT, turn(left, band * H_BAND + SLOT - at), cells)
        return cells

    even = is_even("row", meta)
    parts = []
    for part, half, near, next_rows, row_of in (
        (up_part, 0, slice(0, 8), slice(8, 16), 0),
        (down_part, 1, slice(end - 8, end), slice(end - 16, end - 8), 7),
    ):
        eight = beside(near, half)
        one = beside(next_rows, half)
        one = jnp.broadcast_to(one[row_of : row_of + 1], (SUB, LANES))
        coarse_rows = []
        for band in range(bands):
            rows = slice(0, C_SECOND) if half == 0 else slice(coarse_height - C_SECOND, coarse_height)
            second = wide[band, rows, :]
            first = turn(wide[bands + band, rows, :], HALF)
            coarse_rows.append(jnp.where(lanes_like(second) < HALF, second, first))
        parts.append([
            (part[E8:H8, :], E8), (eight, H8), (part[E1:H1, :], E1), (jnp.where(row == 0, one, meta), H1),
            (part[F4:CS, :], F4), *[(x, CS + k * C_SECOND) for k, x in enumerate(coarse_rows)],
        ])
    for (up, at), (down, _) in zip(*parts):
        even = is_even("row", up)
        swap_0[at : at + up.shape[0], :] = jnp.where(even, down, up)
        swap_1[at : at + up.shape[0], :] = jnp.where(even, up, down)


def coarse_flow_of(second, first, mask):
    def along_rows(x):
        return pltpu.roll(x, x.shape[0] - 1, 0) - pltpu.roll(x, 1, 0)

    def along_cols(x):
        return pltpu.roll(x, LANES - 1, 1) - pltpu.roll(x, 1, 1)

    bands = BANDS
    size = second.shape[0] // bands
    grad_rows = 0.125 * along_rows(second)
    grad_cols = 0.125 * along_cols(second)
    offset = 0.25 * (second - first)
    data = jnp.clip(offset, -LIMIT, LIMIT)
    yield

    def pull(grads):
        terms = data * grads
        return sum(terms[k * size : (k + 1) * size] for k in range(bands))

    def tall(x):
        return jnp.concatenate([x] * bands, axis=0)

    flow = [-mask * pull(grad_rows), -mask * pull(grad_cols)]
    extrapolated = [2.0 * x for x in flow]
    dual_rows = [0.0, 0.0]
    dual_cols = [0.0, 0.0]
    yield
    for step in range(1, STEPS):
        changes = [(along_rows(x), along_cols(x)) for x in extrapolated]
        yield
        data = data + offset + grad_rows * tall(extrapolated[0]) + grad_cols * tall(extrapolated[1])
        data = jnp.clip(data, -LIMIT, LIMIT)
        yield
        for c in range(2):
            rows = dual_rows[c] + changes[c][0]
            cols = dual_cols[c] + changes[c][1]
            scale = jnp.minimum(mask, (8.0 * ALPHA) * lax.rsqrt(rows * rows + cols * cols))
            dual_rows[c] = rows * scale
            dual_cols[c] = cols * scale
        yield
        divergences = [along_rows(dual_rows[c]) + along_cols(dual_cols[c]) for c in range(2)]
        yield
        pulls = [pull(grad_rows), pull(grad_cols)]
        yield
        for c in range(2):
            following = flow[c] + mask * ((1.0 / 64.0) * divergences[c] - pulls[c])
            extrapolated[c] = 2.0 * following - flow[c]
            flow[c] = following
        yield
    return flow


def columns_of_planes(planes):
    whole = lax.broadcasted_iota(jnp.int32, (LANES, COLUMNS), 1)
    lane = lax.broadcasted_iota(jnp.int32, (LANES, LANES), 1)
    strip = jnp.where(lane < S_MID, lane, jnp.where(lane < S_LEFT, lane + (COLUMNS - S_RIGHT), lane - LANES))
    return jnp.concatenate([x for x, wanted in ((whole, "whole"), (strip, "strip")) if wanted in planes], axis=1)


def upsample(flow, planes, target):
    column = columns_of_planes(planes)
    source = lax.broadcasted_iota(jnp.int32, column.shape, 0)
    spread = jnp.where(source - LEAD == lax.shift_right_arithmetic(column, 3), float(FACTOR), 0.0).astype(jnp.bfloat16)
    rows = flow[0].shape[0]
    wide = split_dot(UNIT * jnp.concatenate(flow, axis=0), spread)
    for c in range(2):
        for tile in range(column.shape[1] // LANES):
            target[c, tile] = wide[c * rows : (c + 1) * rows, tile * LANES : (tile + 1) * LANES]


def repeat_rows(spread, initial, cells):
    for c in range(2):
        for tile in range(initial.shape[1]):
            rows = [jnp.broadcast_to(spread[c, tile, cell : cell + 1, :], (SUB, LANES)) for cell in cells]
            initial[c, tile, GUARD : GUARD + SUB * len(cells), :] = jnp.concatenate(rows, axis=0)


def shift_whole(here, shift):
    turned = [turn_back(x, shift) for x in here]
    lane = lanes_like(here[0])
    return [
        jnp.where(lane + shift >= LANES, turned[1], turned[0]),
        jnp.where(lane + shift < 0, turned[0], turned[1]),
    ]


def edge_lanes(rows):
    lane = lanes_of(rows)
    return lane == LANES - 1, lane == 0


def columns_whole(fields, edges):
    rows = fields[0].shape[0]
    if rows not in edges:
        edges[rows] = edge_lanes(rows)
    last, first = edges[rows]
    ahead = [pltpu.roll(x, LANES - 1, 1) for x in fields]
    behind = [pltpu.roll(x, 1, 1) for x in fields]
    return [
        jnp.where(last, ahead[1], ahead[0]) - behind[0],
        ahead[1] - jnp.where(first, behind[0], behind[1]),
    ]


def rows_within(tall):
    size = tall.shape[0]
    return (pltpu.roll(tall, size - 1, 0) - pltpu.roll(tall, 1, 0))[SUB : size - SUB]


def columns_strip(field):
    return pltpu.roll(field, LANES - 1, 1) - pltpu.roll(field, 1, 1)


def strip_moved(window, centre, right, left):
    own = turn_back(window(centre[0]), centre[1])
    beyond_left = turn_back(window(left[0]), left[1])
    beyond_right = turn_back(window(right[0]), right[1])
    lane = lanes_like(own)
    beyond = jnp.where((lane >= S_LEFT) | (lane < S_MID), beyond_left, beyond_right)
    return own, beyond


def strip_joined(own, beyond):
    lane = lanes_like(own)
    is_beyond = lane >= S_RIGHT
    of_next = is_beyond & (lane != S_RIGHT) | (lane == 0)
    of_previous = is_beyond & (lane != LANES - 1) | (lane == S_RIGHT - 1)
    change = turn(jnp.where(of_next, beyond, own), -1) - turn(jnp.where(of_previous, beyond, own), 1)
    return jnp.where(is_beyond, beyond, own), change


def fine_steps(
    rows_total, chunk, columns, initial, extrap, dual_rows, dual_cols, change, dual_data,
    offsets, grads_rows, grads_cols, data_row, masks_of, result, kept, done=lambda k: None, first_pulls=None, depth=1,
):
    assert STEPS == 3
    planes = len(offsets)
    bands = offsets[0].shape[0]
    chunks = rows_total // chunk

    def places(k, trim=(0, 0)):
        start, size = k * chunk + trim[0], chunk - sum(trim)
        return pl.ds(GUARD + start, size), pl.ds(start, size), pl.ds(data_row(k) + trim[0], size)

    def row_change(ref, c, tile, at):
        return ref[c, tile, pl.ds(at.start + 1, at.size), :] - ref[c, tile, pl.ds(at.start - 1, at.size), :]

    def clip(x):
        return jnp.clip(x, -UNIT * LIMIT, UNIT * LIMIT)

    tiles = range(planes)

    for step in range(STEPS):
        source = initial if step == 0 else extrap
        final = step == STEPS - 1

        def dual(item, source=source, step=step):
            k, c = item
            at, own, _ = places(k)
            masks = masks_of(own)
            along = columns([source[c, tile, at, :] for tile in tiles])
            values = []
            for tile in tiles:
                rows = row_change(source, c, tile, at)
                cols = along[tile]
                if step > 0:
                    rows = rows + dual_rows[c, tile, at, :]
                    cols = cols + dual_cols[c, tile, own, :]
                scale = jnp.minimum(masks[tile], lax.rsqrt(rows * rows + cols * cols))
                values.append((rows * scale, cols * scale))
            return values

        def store_dual(item, values):
            k, c = item
            for tile, (rows, cols) in enumerate(values):
                dual_rows[c, tile, places(k)[0], :] = rows
                dual_cols[c, tile, places(k)[1], :] = cols

        staggered([(k, c) for k in range(chunks) for c in range(2)], dual, store_dual, depth)
        along_of = {}

        def primal(item, step=step, final=final, along_of=along_of):
            k, tile = item
            at, own, data = places(k, kept(k) if final else (0, 0))
            if k not in along_of:
                along_of[k] = [columns([dual_cols[c, t, own, :] for t in tiles]) for c in range(2)]
            mask = masks_of(own)[tile]
            start = [initial[c, tile, at, :] for c in range(2)]
            if step > 0:
                moved = [extrap[c, tile, at, :] - start[c] for c in range(2)]
            if step == 1:
                changes = [0.5 * x for x in moved]
            if step == 2:
                changes = [change[c, tile, own, :] for c in range(2)]
            pulls = [None, None]
            duals = []
            ready = step == 0 and first_pulls is not None
            if ready:
                pulls = [first_pulls[c, tile, own, :] for c in range(2)]
            for band in range(0 if ready else bands):
                gradient = (grads_rows[tile][band, data, :], grads_cols[tile][band, data, :])
                value = offsets[tile][band, data, :]
                if step > 0:
                    earlier = clip(value) if step == 1 else dual_data[band, tile, own, :]
                    value = (value + earlier) + (gradient[0] * moved[0] + gradient[1] * moved[1])
                value = clip(value)
                duals.append(value)
                for c in range(2):
                    term = value * gradient[c]
                    pulls[c] = term if pulls[c] is None else pulls[c] + term
            flows, nexts = [], []
            for c in range(2):
                divergence = row_change(dual_rows, c, tile, at) + along_of[k][c][tile]
                moving = (mask * (1.0 / 64.0)) * divergence - pulls[c]
                total = moving if step == 0 else changes[c] + moving
                flows.append((start[c] + total) * (1.0 / UNIT) if final else total)
                nexts.append(None if final else start[c] + (total + moving))
            return flows, nexts, duals

        def store_primal(item, results, step=step, final=final):
            k, tile = item
            flows, nexts, duals = results
            at, own, _ = places(k, kept(k) if final else (0, 0))
            for c in range(2):
                if final:
                    result[c, tile, own, :] = flows[c]
                else:
                    if step > 0:
                        change[c, tile, own, :] = flows[c]
                    extrap[c, tile, at, :] = nexts[c]
            if final:
                if tile == planes - 1:
                    done(k)
            elif step > 0:
                for band in range(bands):
                    dual_data[band, tile, own, :] = duals[band]

        staggered([(k, tile) for k in range(chunks) for tile in tiles], primal, store_primal, depth)


def clear_guards(*refs):
    for ref in refs:
        rows = ref.shape[2]
        zero = jnp.zeros((GUARD, LANES), jnp.float32)
        for c in range(2):
            for tile in range(ref.shape[1]):
                ref[c, tile, 0:GUARD, :] = zero
                ref[c, tile, rows - GUARD : rows, :] = zero


def fine_scratch(bands, planes, rows):
    guarded = pltpu.VMEM((2, planes, rows + 2 * GUARD, LANES), jnp.float32)
    plain = pltpu.VMEM((2, planes, rows, LANES), jnp.float32)
    return [guarded, guarded, guarded, plain, plain, pltpu.VMEM((bands, planes, rows, LANES), jnp.float32)]


def pieces(bands, height, rows):
    assert (height - 2 * SUB) % rows == 0
    return [(band, row) for row in range(SUB, height - SUB, rows) for band in range(bands)]


def whole_terms_kernel(
    second_0, second_1, first_0, first_1, coarse, own_meta,
    offset, grad_rows, grad_cols, initial, strip_e, strip_f, up, down, moved, spread,
):
    seconds, firsts = (second_0, second_1), (first_0, first_1)
    bands, height, _ = second_0.shape
    block = 24
    coarse_height = coarse.shape[0] // (2 * bands)
    centre = shift_at(own_meta, 0, 0)
    def windows(band, row, rows):
        here = [ref[band, pl.ds(row + centre[0], rows), :].reshape(-1, LANES) for ref in seconds]
        return shift_whole(here, centre[1])

    woven = Woven(coarse_flow_of(coarse[0 : bands * coarse_height, :], coarse[bands * coarse_height :, :], 1.0))

    def strips_of(item):
        band, row = item
        rows = slice(row, row + LANES)
        return strip_own([ref[band, rows, :] for ref in seconds]), strip_own([ref[band, rows, :] for ref in firsts])

    def store_strips(item, results):
        band, row = item
        strip_e[band, row : row + LANES, :], strip_f[band, row : row + LANES, :] = results

    staggered([(band, row) for band in range(bands) for row in range(0, height, LANES)], strips_of, store_strips, 1, woven)

    ends = [(row, windows(slice(None), row, SUB)) for row in (SUB // 2, height - SUB - SUB // 2)]
    for row, values in ends:
        for tile in range(2):
            moved[tile, :, row : row + SUB, :] = values[tile].reshape(bands, SUB, LANES)

    def store_moved(item, values):
        band, row = item
        for tile in range(2):
            moved[tile, band, row : row + 120, :] = values[tile]

    staggered(pieces(bands, height, 120), lambda item: windows(*item, 120), store_moved, 3, woven)

    edges = {}

    def values_of(item):
        band, row = item
        rows = slice(row, row + block)
        values = [moved[tile, band, rows, :] for tile in range(2)]
        along = columns_whole(values, edges)
        own = [ref[band, rows, :] for ref in firsts]
        return [(0.25 * UNIT) * (x - y) for x, y in zip(values, own)], [0.125 * x for x in along]

    def store_values(item, results):
        band, row = item
        offsets, gradients = results
        data = slice(row + HALO, row + HALO + block)
        for tile in range(2):
            offset[tile, band, data, :] = offsets[tile]
            grad_cols[tile, band, data, :] = gradients[tile]

    staggered(pieces(bands, height, block), values_of, store_values, 3, woven)

    def gradient_of(item):
        band, row = item
        return [0.125 * rows_within(moved[tile, band, row - SUB : row + 40 + SUB, :]) for tile in range(2)]

    def store_gradient(item, results):
        band, row = item
        for tile in range(2):
            grad_rows[tile, band, row + HALO : row + HALO + 40, :] = results[tile]

    staggered(pieces(bands, height, 40), gradient_of, store_gradient, 3, woven)

    parts = []
    for band in range(bands):
        for second, first in zip(seconds, firsts):
            parts.append((
                second[band, 0:16, :], first[band, 0:8, :],
                second[band, height - 16 : height, :], first[band, height - 8 : height, :],
            ))
    for k, (second_top, first_top, second_end, first_end) in enumerate(parts):
        up[E8 + 8 * k : E8 + 8 * k + 8, :] = second_top[0:8]
        up[E1 + k : E1 + k + 1, :] = second_top[8:9]
        up[F4 + 4 * k : F4 + 4 * k + 4, :] = first_top[0:4]
        down[E8 + 8 * k : E8 + 8 * k + 8, :] = second_end[8:16]
        down[E1 + k : E1 + k + 1, :] = second_end[7:8]
        down[F4 + 4 * k : F4 + 4 * k + 4, :] = first_end[4:8]
    for target in (up, down):
        for start, end in ((H8, E1), (H1, F4), (CS, ROW_MESSAGE)):
            target[start:end, :] = jnp.zeros((end - start, LANES), jnp.float32)

    upsample(woven.finish(), ("whole",), spread)
    clear_guards(initial)
    rows_total = initial.shape[2] - 2 * GUARD
    repeat_rows(spread, initial, [BEGIN // FACTOR + k for k in range(rows_total // SUB)])


def whole_steps_kernel(
    initial, offset, grad_rows, grad_cols, result, extrap, dual_rows, dual_cols, change, dual_data
):
    rows_total = result.shape[2]
    clear_guards(extrap, dual_rows)
    chunk = 16
    edges = {}
    fine_steps(
        rows_total, chunk, lambda fields: columns_whole(fields, edges),
        initial, extrap, dual_rows, dual_cols, change, dual_data,
        *[[ref.at[tile] for tile in range(2)] for ref in (offset, grad_rows, grad_cols)],
        lambda k: HALO + BEGIN + k * chunk, lambda own: (1.0, 1.0), result,
        lambda k: (SUB * (k == 0), SUB * (k == rows_total // chunk - 1)), depth=6,
    )


def strip_kernel(
    count, strip_e, strip_f, from_left, from_right, wide, own_message, whole,
    middle, strip_out, first_ends, offset, grad_rows, grad_cols,
    both, moved, result, spread, initial, extrap, dual_rows, dual_cols, change, dual_data,
):
    bands, height, _ = strip_e.shape
    block = 24
    coarse_height = height // FACTOR
    coarse_width = COLUMNS // FACTOR
    rows_total = height - 2 * BEGIN
    lane = lanes_of()
    centre, right, left = shifts_of(own_message)
    has_left, has_right = neighbours("col", count)
    exists = jnp.where(lane < S_RIGHT, 1.0, jnp.where(lane < S_LEFT, has_right, has_left))

    def tall_factor(rows):
        return 0.125 * jnp.concatenate([exists] * (rows // SUB), axis=0)

    mask = jnp.where(lane < LEAD, has_left, jnp.where(lane < LEAD + coarse_width, 1.0, has_right))
    mask = jnp.concatenate([mask] * (coarse_height // SUB), axis=0)
    cells = [wide[k * bands : (k + 1) * bands].reshape(bands * coarse_height, LANES) for k in range(2)]
    woven = Woven(coarse_flow_of(*cells, mask))

    def halves(row, rows):
        half = row // (height // 2)
        start = row - half * (height // 2)
        return half, slice(start, start + rows)

    def second_of(item):
        band, row = item
        half, message = halves(row, LANES)
        return strip_second(strip_e[band, row : row + LANES, :], from_left, from_right, message, half, band)

    def store_second(item, value):
        band, row = item
        strip_out[band, row : row + LANES, :] = value

    staggered([(band, row) for row in range(0, height, LANES) for band in range(bands)], second_of, store_second, 1, woven)

    def first_of(band, row, rows):
        half, message = halves(row, rows)
        return strip_first(strip_f[band, row : row + rows, :], from_left, from_right, message, half, band)

    firsts = [(end, band, first_of(band, (0, height - SUB)[end], SUB)) for end in range(2) for band in range(bands)]
    for end, band, value in firsts:
        first_ends[end, band] = value

    def windows(band, row, rows):
        return strip_moved(
            lambda shift: strip_out[band, pl.ds(row + shift, rows), :].reshape(-1, LANES), centre, right, left
        )

    ends = [
        (row, strip_joined(*windows(slice(None), row, SUB))[0]) for row in (SUB // 2, height - SUB - SUB // 2)
    ]
    for row, value in ends:
        moved[:, row : row + SUB, :] = value.reshape(bands, SUB, LANES)

    def store_moved(item, values):
        band, row = item
        for k in range(2):
            both[k, band, row : row + 120, :] = values[k]

    staggered(pieces(bands, height, 120), lambda item: windows(*item, 120), store_moved, 3, woven)

    factor = tall_factor(block)

    def values_of(item):
        band, row = item
        value, along = strip_joined(*[both[k, band, row : row + block, :] for k in range(2)])
        return value, (0.25 * UNIT) * (value - first_of(band, row, block)), factor * along

    def store_values(item, results):
        band, row = item
        data = slice(row + HALO, row + HALO + block)
        moved[band, row : row + block, :], offset[band, data, :], grad_cols[band, data, :] = results

    staggered(pieces(bands, height, block), values_of, store_values, 3, woven)

    def gradient_of(item):
        band, row = item
        return factor * rows_within(moved[band, row - SUB : row + block + SUB, :])

    def store_gradient(item, value):
        band, row = item
        grad_rows[band, row + HALO : row + HALO + block, :] = value

    staggered(pieces(bands, height, block), gradient_of, store_gradient, 3, woven)

    upsample(woven.finish(), ("strip",), spread)
    clear_guards(initial, extrap, dual_rows)
    repeat_rows(spread, initial, [BEGIN // FACTOR + k for k in range(rows_total // SUB)])

    chunk = 16
    masks = jnp.concatenate([exists] * (chunk // SUB), axis=0)
    fine_steps(
        rows_total, chunk, lambda fields: [columns_strip(fields[0])],
        initial, extrap, dual_rows, dual_cols, change, dual_data, [offset], [grad_rows], [grad_cols],
        lambda k: HALO + BEGIN + k * chunk, lambda own: (masks[: own.size],), result,
        lambda k: (SUB * (k == 0), SUB * (k == rows_total // chunk - 1)), depth=6,
    )
    join(whole, result.at[:, 0], middle, slice(SUB, rows_total - SUB))


def join(whole, strip, target, rows):
    lane = lanes_of(rows.stop - rows.start)
    values = []
    for c in range(2):
        edge = strip[c, rows, :]
        start = jnp.where(lane < EDGE, edge, whole[c, 0, rows, :])
        values.append((start, jnp.where(lane >= LANES - EDGE, turn(edge, S_TURN), whole[c, 1, rows, :])))
    for c in range(2):
        target[c, rows, 0:LANES], target[c, rows, LANES:COLUMNS] = values[c]


def outer_kernel(
    counts, second_0, second_1, first_0, first_1, strip_e, first_ends, wide, got_1, got_0, middle, own_message,
    _wo, _wr, _wc, _so, _sr, _sc,
    flow_out, coarse_out, whole_offset, whole_rows, whole_cols, strip_offset, strip_rows, strip_cols,
    from_up, from_down, extended, tall, spread, masks, result, joined, coarse_result, pulls, sems,
    initial, extrap, dual_rows, dual_cols, change, dual_data,
):
    bands, height, _ = second_0.shape
    coarse_height = height // FACTOR
    coarse_width = COLUMNS // FACTOR
    rows_total = 2 * EACH
    lane = lanes_of()

    put_middle = pltpu.make_async_copy(
        middle.at[:, pl.ds(MARGIN - BEGIN, height - 2 * MARGIN), :],
        flow_out.at[:, pl.ds(MARGIN, height - 2 * MARGIN), :],
        sems.at[0],
    )
    put_middle.start()
    own, one, other = [shifts_of(message) for message in (own_message, got_0, got_1)]
    odd = lax.axis_index("row") % 2

    def of_row(for_even, for_odd):
        return [tuple(jnp.where(odd == 0, x, y) for x, y in zip(*pair)) for pair in zip(for_even, for_odd)]

    above, below = of_row(other, one), of_row(one, other)

    other = without_ends(got_1, "row", counts[0])
    even = is_even("row", got_0)
    from_down[...] = jnp.where(even, got_0[...], other)
    from_up[...] = jnp.where(even, other, got_0[...])

    has_up, has_down = neighbours("row", counts[0])
    has_left, has_right = neighbours("col", counts[1])
    exists = jnp.where(lane < S_RIGHT, 1.0, jnp.where(lane < S_LEFT, has_right, has_left))

    zero = jnp.zeros((SUB, LANES), jnp.float32)
    tall_rows = coarse_height + 2 * LEAD
    parts = []
    fill = jnp.zeros((LEAD - C_SECOND, LANES), jnp.float32)
    for plane in range(2 * bands):
        at = CS + C_SECOND * (plane % bands)
        ends = [turn(message[at : at + C_SECOND, :], HALF * (plane // bands)) for message in (from_up, from_down)]
        parts.append([fill, ends[0], wide[plane], ends[1], fill])
    for plane, values in enumerate(parts):
        tall[plane] = jnp.concatenate(values, axis=0)
    across = jnp.where(lane < LEAD, has_left, jnp.where(lane < LEAD + coarse_width, 1.0, has_right))
    mask = jnp.concatenate([across * has_up] + [across] * (coarse_height // SUB) + [across * has_down], axis=0)
    for end in range(2):
        message = (from_up, from_down)[end]
        beside = message[H8 : H8 + 8, :]
        beside_one = jnp.broadcast_to(message[H1 : H1 + 1, :], (SUB, LANES))
        parts = []
        for band in range(bands):
            eights = [message[E8 + 8 * k : E8 + 8 * k + 8, :] for k in (2 * band, 2 * band + 1)]
            ones = [jnp.broadcast_to(message[E1 + k : E1 + k + 1, :], (SUB, LANES)) for k in (2 * band, 2 * band + 1)]
            eights.append(strip_halo(strip_own(eights), beside, band, 0, REACH))
            ones.append(strip_halo(strip_own(ones), beside_one, band, 0, REACH))
            for tile, (eight, one) in enumerate(zip(eights, ones)):
                source = (second_0, second_1, strip_e)[tile]
                if end == 0:
                    parts.append((tile, band, [one, eight, source[band, 0:24, :]]))
                else:
                    parts.append((tile, band, [source[band, height - 24 : height, :], eight, one]))
        for tile, band, values in parts:
            extended[end, tile, band] = jnp.concatenate(values, axis=0)
    cells = [tall[k * bands : (k + 1) * bands].reshape(bands * tall_rows, LANES) for k in range(2)]
    woven = Woven(coarse_flow_of(*cells, mask))
    edges = {}
    rows_data = whole_offset.shape[2]
    exists_tall = jnp.concatenate([exists] * bands, axis=0)

    def rows_of(halo, end):
        if halo:
            return slice(0, SUB) if end == 0 else slice(rows_data - SUB, rows_data)
        return slice(HALO, HALO + SUB) if end == 0 else slice(rows_data - HALO - SUB, rows_data - HALO)

    def values_of(item):
        halo, end = item
        message = (from_up, from_down)[end]
        base = (SUB, 3 * SUB)[end] if halo else 2 * SUB
        shifts = (above, below)[end] if halo else own
        factor = 0.125 * (has_up, has_down)[end] if halo else 0.125

        def here(tile, shift):
            return extended[end, tile, :, pl.ds(base + shift, SUB), :].reshape(-1, LANES)

        def down_up(tile, shift):
            return here(tile, shift + 1) - here(tile, shift - 1)

        own_rows = slice(0, SUB) if end == 0 else slice(height - SUB, height)
        if halo:
            firsts = [[], [], []]
            for band in range(bands):
                eights = []
                for k in (2 * band, 2 * band + 1):
                    four = message[F4 + 4 * k : F4 + 4 * k + 4, :]
                    eights.append(jnp.concatenate([four, four], axis=0))
                eights.append(strip_halo(strip_own(eights), message[H8 : H8 + 8, :], band, REACH, DEPTH))
                for tile in range(3):
                    firsts[tile].append(eights[tile])
            firsts = [jnp.concatenate(x, axis=0) for x in firsts]
        else:
            firsts = [x.reshape(-1, LANES) for x in (first_0[:, own_rows, :], first_1[:, own_rows, :], first_ends[end])]
        centre = shifts[0]
        values = shift_whole([here(tile, centre[0]) for tile in range(2)], centre[1])
        changes = shift_whole([down_up(tile, centre[0]) for tile in range(2)], centre[1])
        along = columns_whole(values, edges)
        value, across_cols = strip_joined(*strip_moved(lambda shift: here(2, shift), *shifts))
        change_rows, _ = strip_joined(*strip_moved(lambda shift: down_up(2, shift), *shifts))
        return (
            [(0.25 * UNIT) * (x - y) for x, y in zip([*values, value], firsts)],
            [*[factor * x for x in changes], (factor * exists_tall) * change_rows],
            [*[factor * x for x in along], (factor * exists_tall) * across_cols],
        )

    def store_values(item, results):
        rows = rows_of(*item)
        for values, whole, strip in zip(
            results, (whole_offset, whole_rows, whole_cols), (strip_offset, strip_rows, strip_cols)
        ):
            values = [x.reshape(bands, SUB, LANES) for x in values]
            for tile in range(2):
                whole[tile, :, rows, :] = values[tile]
            strip[:, rows, :] = values[2]

    staggered([(halo, end) for halo in (True, False) for end in range(2)], values_of, store_values, 3, woven)

    chunk = 32
    per = EACH // chunk

    def data_row(k):
        return k // per * (rows_data - EACH) + k % per * chunk

    offsets = [whole_offset.at[0], whole_offset.at[1], strip_offset]
    grads_rows = [whole_rows.at[0], whole_rows.at[1], strip_rows]
    grads_cols = [whole_cols.at[0], whole_cols.at[1], strip_cols]

    def pulls_of(item):
        k, tile = item
        data = pl.ds(k * (rows_data - EACH), EACH)
        duals = [jnp.clip(offsets[tile][band, data, :], -UNIT * LIMIT, UNIT * LIMIT) for band in range(bands)]
        return [
            sum(duals[band] * grads[tile][band, data, :] for band in range(bands)) for grads in (grads_rows, grads_cols)
        ]

    def store_pulls(item, values):
        k, tile = item
        for c in range(2):
            pulls[c, tile, k * EACH : (k + 1) * EACH, :] = values[c]

    staggered([(k, tile) for k in range(2) for tile in range(3)], pulls_of, store_pulls, 1, woven)

    flow = woven.finish()
    for c in range(2):
        coarse_result[c] = turn(flow[c][LEAD : LEAD + coarse_height], -LEAD)[:, :coarse_width]
    put_coarse = pltpu.make_async_copy(coarse_result, coarse_out, sems.at[1])
    upsample(flow, ("whole", "strip"), spread)
    clear_guards(initial, extrap, dual_rows)
    each = EACH // SUB
    repeat_rows(
        spread, initial,
        [LEAD - 1 + k for k in range(each)] + [tall_rows - LEAD + 1 - each + k for k in range(each)],
    )

    for i, value in enumerate((jnp.ones((SUB, LANES), jnp.float32), exists)):
        masks[i] = jnp.concatenate([value * has_up] + [value] * (rows_total // SUB - 2) + [value * has_down], axis=0)

    def masks_of(rows):
        whole = masks[0, rows, :]
        return (whole, whole, masks[1, rows, :])

    edges = {}
    puts = [
        pltpu.make_async_copy(
            joined.at[:, pl.ds(k * EACH + SUB, MARGIN), :],
            flow_out.at[:, pl.ds(k * (height - MARGIN), MARGIN), :],
            sems.at[2 + k],
        )
        for k in range(2)
    ]

    def finish(k):
        if k % per == per - 1:
            at = k // per * EACH + SUB
            join(result, result.at[:, 2], joined, slice(at, at + MARGIN))

    fine_steps(
        rows_total, chunk, lambda fields: columns_whole(fields[:2], edges) + [columns_strip(fields[2])],
        initial, extrap, dual_rows, dual_cols, change, dual_data,
        offsets, grads_rows, grads_cols, data_row, masks_of, result,
        lambda k: (SUB * (k % per == 0), SUB * (k % per == per - 1)), finish, pulls, depth=3,
    )
    puts.append(put_coarse)
    for put in puts:
        put.start()
    put_middle.wait()
    for put in puts:
        put.wait()


def swap_with(message, axis, start):
    names = ("row", "col")
    sizes = [lax.axis_size(name) for name in names]
    along = names.index(axis)
    count, others = sizes[along], sizes[1 - along]

    def number(place, other):
        row, col = (place, other) if along == 0 else (other, place)
        return row * sizes[1] + col

    pairs = [(number(i, k), number(i + 1, k)) for i in range(start, count - 1, 2) for k in range(others)]
    if start and axis == "col":
        pairs += [(number(i, k), number(i, k + 1)) for i in (0, count - 1) for k in range(0, others, 2)]
    elif start:
        pairs += [(number(0, k), number(count - 1, k)) for k in (0, others - 1)]
        pairs += [(number(i, k), number(i, k + 1)) for i in (0, count - 1) for k in range(1, others - 1, 2)]
    return lax.ppermute(message, names, pairs + [(j, i) for i, j in pairs])


def local(frame_first, frame_second, shifts):
    bands, height, width = frame_first.shape
    assert bands == 4 and width == COLUMNS and height % LANES == 0
    assert lax.axis_size("row") % 2 == 0 and lax.axis_size("col") % 2 == 0
    coarse_height = height // FACTOR
    coarse_width = width // FACTOR
    vmem = pl.BlockSpec(memory_space=pltpu.VMEM)
    hbm = pl.BlockSpec(memory_space=pltpu.HBM)
    tall_rows = coarse_height + 2 * LEAD
    inner_rows = height - 2 * BEGIN

    def shape(*sizes):
        return jax.ShapeDtypeStruct(sizes, jnp.float32)

    def scratch(*sizes):
        return pltpu.VMEM(sizes, jnp.float32)

    def call(kernel, name, arguments, outs, scratches=(), flops=1_000_000, **more):
        more = {"in_specs": [vmem] * len(arguments), "out_specs": (vmem,) * len(outs), **more}
        return pl.pallas_call(
            kernel,
            out_shape=tuple(outs),
            scratch_shapes=list(scratches),
            compiler_params=pltpu.CompilerParams(vmem_limit_bytes=24 * 1024 * 1024),
            cost_estimate=pl.CostEstimate(flops=flops, bytes_accessed=1_000_000, transcendentals=0),
            name=name,
            **more,
        )(*arguments)

    plane = shape(bands, height, LANES)
    column_message = shape(height // 2, LANES)
    row_message = shape(ROW_MESSAGE, LANES)
    whole_data = shape(2, bands, height + 2 * HALO, LANES)
    strip_data = shape(bands, height + 2 * HALO, LANES)

    *frames, coarse, swap_0, swap_1, own_meta = call(
        first_kernel,
        "means_and_message",
        [pltpu.with_memory_space_constraint(x, pltpu.HBM) for x in (frame_second, frame_first, shifts)],
        [*[plane] * 4, shape(2 * bands * coarse_height, LANES), column_message, column_message, shape(SUB, LANES)],
        [
            pltpu.SMEM((1, 1, 2), jnp.int32),
            pltpu.SemaphoreType.DMA((2, bands, 2)),
            pltpu.SemaphoreType.DMA,
        ],
        in_specs=[hbm] * 3,
    )
    got_0 = swap_with(swap_0, "col", 0)
    got_1 = swap_with(swap_1, "col", 1)

    *whole_terms, initial, strip_e, strip_f, up_part, down_part = call(
        whole_terms_kernel,
        "whole_terms",
        [*frames, coarse, own_meta],
        [
            *[whole_data] * 3, shape(2, 2, inner_rows + 2 * GUARD, LANES),
            plane, plane, row_message, row_message,
        ],
        [
            scratch(2, bands, height, LANES), scratch(2, 2, coarse_height, LANES),
        ],
        flops=8_000_000,
    )
    (whole,) = call(
        whole_steps_kernel,
        "whole_steps",
        [initial, *whole_terms],
        [shape(2, 2, inner_rows, LANES)],
        fine_scratch(bands, 2, inner_rows)[1:],
        flops=20_000_000,
    )

    swap_0, swap_1, from_left, from_right, wide = call(
        functools.partial(message_kernel, lax.axis_size("col")),
        "row_messages",
        [coarse, own_meta, got_0, got_1, up_part, down_part, whole],
        [row_message, row_message, column_message, column_message, shape(2 * bands, coarse_height, LANES)],
    )
    got_1 = swap_with(swap_1, "row", 1)
    got_0 = swap_with(swap_0, "row", 0)

    middle, strip_e, first_ends, *strip_terms = call(
        functools.partial(strip_kernel, lax.axis_size("col")),
        "strip",
        [strip_e, strip_f, from_left, from_right, wide, swap_0, whole],
        [shape(2, inner_rows, width), plane, shape(2, bands, SUB, LANES), *[strip_data] * 3],
        [
            scratch(2, bands, height, LANES),
            scratch(bands, height, LANES),
            scratch(2, 1, inner_rows, LANES),
            scratch(2, 1, coarse_height, LANES),
            *fine_scratch(bands, 1, inner_rows),
        ],
        flops=16_000_000,
    )

    flow, coarse_flow, *_ = call(
        functools.partial(outer_kernel, (lax.axis_size("row"), lax.axis_size("col"))),
        "outer_rows",
        [
            *frames, strip_e, first_ends, wide, got_1, got_0, middle, swap_0,
            *whole_terms, *strip_terms,
        ],
        [shape(2, height, width), shape(2, coarse_height, coarse_width), *[whole_data] * 3, *[strip_data] * 3],
        [
            scratch(ROW_MESSAGE, LANES),
            scratch(ROW_MESSAGE, LANES),
            scratch(2, 3, bands, 40, LANES),
            scratch(2 * bands, tall_rows, LANES),
            scratch(2, 3, tall_rows, LANES),
            scratch(2, 2 * EACH, LANES),
            scratch(2, 3, 2 * EACH, LANES),
            scratch(2, 2 * EACH, width),
            scratch(2, coarse_height, coarse_width),
            scratch(2, 3, 2 * EACH, LANES),
            pltpu.SemaphoreType.DMA((4,)),
            *fine_scratch(bands, 3, 2 * EACH),
        ],
        out_specs=(hbm, hbm) + (vmem,) * 6,
        input_output_aliases={11 + k: 2 + k for k in range(6)},
    )
    return (flow, coarse_flow)


def solution(mesh):
    return jax.shard_map(
        local,
        mesh=mesh,
        in_specs=(P(None, "row", "col"), P(None, "row", "col"), P("row", "col", None)),
        out_specs=(P(None, "row", "col"), P(None, "row", "col")),
        check_vma=False,
    )
```

```python
import functools

import jax
import jax.numpy as jnp
from jax import lax
from jax.experimental import pallas as pl
from jax.experimental.pallas import tpu as pltpu
from jax.sharding import PartitionSpec as P

FACTOR = 8
MAXD = 4
BANDS = 4
STEPS = 3
LANES = 128
COLUMNS = 2 * LANES
HALF = 64
SUB = 8
DEPTH = 4
REACH = DEPTH + MAXD + 1
SLOT = 16
C_SECOND = 6
C_FIRST = 5
LEAD = 8
MARGIN = 48
EDGE = 46
GUARD = 8
HALO = 8
BEGIN = 40
EACH = MARGIN + 16
LIMIT = 0.3
ALPHA = 0.3
UNIT = 0.125 / ALPHA

S_MID = 55
S_RIGHT = 110
S_LEFT = LANES - REACH
S_TURN = COLUMNS - S_RIGHT - LANES

E8 = 0
H8 = 64
E1 = 72
H1 = 80
META = 81
F4 = 88
CS = 120
ROW_MESSAGE = 144
H_BAND = 32

COARSE_A = REACH + DEPTH
COARSE_B = SLOT + REACH + DEPTH
SHIFT_R = 2 * SLOT + REACH + DEPTH
SHIFT_C = SHIFT_R + 1
EXISTS = SHIFT_R + 2


def lanes_of(rows=SUB):
    return lax.broadcasted_iota(jnp.int32, (rows, LANES), 1)


def lanes_like(x):
    return lax.broadcasted_iota(jnp.int32, x.shape, 1)


def turn(x, amount):
    amount = amount % LANES
    return x if amount == 0 else pltpu.roll(x, amount, 1)


def turn_back(x, shift):
    return pltpu.roll(x, lax.rem(LANES - shift, LANES), 1)


def split_dot(x, exact):
    high = x.astype(jnp.bfloat16)
    rest = x - high.astype(jnp.float32)
    middle = rest.astype(jnp.bfloat16)
    low = (rest - middle.astype(jnp.float32)).astype(jnp.bfloat16)
    parts = [jnp.dot(part, exact, preferred_element_type=jnp.float32) for part in (low, middle, high)]
    return parts[0] + parts[1] + parts[2]


def neighbours(axis, count):
    place = lax.axis_index(axis)
    return jnp.where(place > 0, 1.0, 0.0), jnp.where(place < count - 1, 1.0, 0.0)


def shift_at(ref, row, lane):
    numbers = ref[row : row + 1, :].astype(jnp.int32)
    return numbers[0, lane], numbers[0, lane + SLOT]


def shifts_of(message):
    return [shift_at(message, META, lane) for lane in (0, 80, 48)]


def is_even(axis, like):
    return jnp.broadcast_to(lax.axis_index(axis) % 2, like.shape) == 0


def without_ends(message, axis, count):
    place = jnp.broadcast_to(lax.axis_index(axis), message.shape)
    return jnp.where((place > 0) & (place < count - 1), message[...], 0.0)


def staggered(items, compute, store, depth, woven=None):
    pending = []
    for item in items:
        pending.append((item, compute(item)))
        if woven is not None:
            woven.advance()
        if len(pending) > depth:
            store(*pending.pop(0))
    for entry in pending:
        store(*entry)


class Woven:
    def __init__(self, stages):
        self.stages = stages
        self.result = None

    def advance(self):
        try:
            next(self.stages)
            return True
        except StopIteration as end:
            self.result = end.value if self.result is None else self.result
            return False

    def finish(self):
        while self.advance():
            pass
        return self.result


def pack_image(packed, to_right, planes, some, count, offset):
    _, height, _ = planes[0].shape
    plane = planes[int(to_right)]
    start = LANES - count if to_right else 0
    length = height // 2
    lane = lanes_of(length)
    for half in range(2):
        for band in some:
            at = half * HALF + band * SLOT + offset
            cells = turn(plane[band, half * length : (half + 1) * length, :], at - start)
            packed = cells if packed is None else jnp.where((lane >= at) & (lane < at + count), cells, packed)
    return packed


def pack_means(packed, to_right, means):
    length = packed.shape[0]
    start = LEAD + COLUMNS // FACTOR - C_SECOND if to_right else LEAD
    lane = lanes_of(length)
    for half in range(2):
        cells = means[half * length : (half + 1) * length]
        for at, first in ((half * HALF + COARSE_A, start), (half * HALF + COARSE_B, start + 3)):
            packed = jnp.where((lane >= at) & (lane < at + 3), turn(cells, at - first), packed)
    return packed


def strip_second(base, from_left, from_right, rows, half, band):
    at = half * HALF + band * SLOT
    lane = lanes_like(base)
    cells = jnp.where(lane >= S_RIGHT, turn(from_right[rows, :], S_RIGHT - at), base)
    return jnp.where(lane >= S_LEFT, turn(from_left[rows, :], S_LEFT - at), cells)


def strip_first(base, from_left, from_right, rows, half, band):
    at = half * HALF + band * SLOT + REACH
    lane = lanes_like(base)
    cells = jnp.where(lane >= S_RIGHT, turn(from_right[rows, :], S_RIGHT - at), base)
    return jnp.where(lane >= S_LEFT, turn(from_left[rows, :], LANES - DEPTH - at), cells)


def strip_halo(base, beside, band, start, count):
    at = band * H_BAND + start
    lane = lanes_like(base)
    cells = jnp.where(lane >= S_RIGHT, turn(beside, S_RIGHT - at), base)
    return jnp.where(lane >= S_LEFT, turn(beside, LANES - count - at - SLOT), cells)


def strip_own(planes):
    return jnp.where(lanes_like(planes[0]) < S_MID, planes[0], turn(planes[1], -S_TURN))


def first_kernel(
    second_hbm, first_hbm, shifts_hbm, second_0, second_1, first_0, first_1, coarse, swap_0, swap_1, own_meta,
    shifts, sems, shift_sem,
):
    seconds, firsts = (second_0, second_1), (first_0, first_1)
    bands, height, _ = second_0.shape
    width = COLUMNS
    coarse_height = height // FACTOR
    lane = lanes_of()
    get_shifts = pltpu.make_async_copy(shifts_hbm, shifts, shift_sem)
    get_shifts.start()
    copies = []
    for image, (source, refs) in enumerate(((second_hbm, seconds), (first_hbm, firsts))):
        for band in range(bands):
            for tile, ref in enumerate(refs):
                copy = pltpu.make_async_copy(
                    source.at[band, :, pl.ds(tile * LANES, LANES)], ref.at[band], sems.at[image, band, tile]
                )
                copy.start()
                copies.append((image * bands + band, tile, ref, band, copy))
    cell = lax.broadcasted_iota(jnp.int32, (width, LANES), 0)
    place = lax.broadcasted_iota(jnp.int32, (width, LANES), 1)
    weights = jnp.where(place - LEAD == cell // FACTOR, 1.0 / (FACTOR * FACTOR), 0.0).astype(jnp.bfloat16)
    means = []
    packed = [None, None]
    for image, (count, offset) in enumerate(((REACH, 0), (DEPTH, REACH))):
        for one in range(bands):
            some = range(one, one + 1)
            group = copies[2 * (image * bands + one) : 2 * (image * bands + one + 1)]
            for *_, copy in group:
                copy.wait()
            sums = {}
            for plane, tile, ref, band, _ in group:
                parts = [ref[band, pl.ds(k, coarse_height, stride=FACTOR), :] for k in range(FACTOR)]
                while len(parts) > 1:
                    parts = [x + y for x, y in zip(parts[::2], parts[1::2])]
                sums[band, tile] = parts[0]
            tall = [jnp.concatenate([sums[band, tile] for tile in range(2)], axis=1) for band in some]
            means.append(split_dot(jnp.concatenate(tall, axis=0), weights))
            packed = [
                pack_image(packed[side], bool(side), (seconds, firsts)[image], some, count, offset) for side in range(2)
            ]
    means = jnp.concatenate(means, axis=0)
    get_shifts.wait()
    shift_rows = shifts[0, 0, 0].astype(jnp.float32)
    shift_cols = shifts[0, 0, 1].astype(jnp.float32)
    place = lanes_of(height // 2) & (HALF - 1)
    packed = [
        jnp.where(place == SHIFT_R, shift_rows, jnp.where(place == SHIFT_C, shift_cols, jnp.where(place == EXISTS, 1.0, x)))
        for x in packed
    ]
    to_left, to_right = [pack_means(packed[side], bool(side), means) for side in range(2)]
    coarse[...] = means
    own_meta[...] = jnp.where(lane < SLOT, shift_rows, shift_cols)
    even = is_even("col", swap_0)
    swap_0[...] = jnp.where(even, to_right, to_left)
    swap_1[...] = jnp.where(even, to_left, to_right)


def message_kernel(
    count, coarse, own_meta, got_0, got_1, up_part, down_part, _whole, swap_0, swap_1, from_left, from_right, wide
):
    other = without_ends(got_1, "col", count)
    even = is_even("col", got_0)
    from_right[...] = jnp.where(even, got_0[...], other)
    from_left[...] = jnp.where(even, other, got_0[...])
    planes_coarse, coarse_height, _ = wide.shape
    bands = planes_coarse // 2
    end = from_left.shape[0]
    coarse_width = COLUMNS // FACTOR
    lane = lanes_of()
    wides = []
    for plane in range(planes_coarse):
        half, block = divmod(plane, planes_coarse // 2)
        for step in range(coarse_height // SUB):
            own = slice(plane * coarse_height + step * SUB, plane * coarse_height + (step + 1) * SUB)
            rows = slice(block * coarse_height + step * SUB, block * coarse_height + (step + 1) * SUB)
            at = half * HALF
            left = from_left[rows, :]
            right = from_right[rows, :]
            start = LEAD - C_SECOND
            cells = turn(left, start - at - COARSE_A)
            cells = jnp.where(lane >= start + 3, turn(left, start + 3 - at - COARSE_B), cells)
            cells = jnp.where(lane >= LEAD, coarse[own, :], cells)
            start = LEAD + coarse_width
            cells = jnp.where(lane >= start, turn(right, start - at - COARSE_A), cells)
            cells = jnp.where(lane >= start + 3, turn(right, start + 3 - at - COARSE_B), cells)
            wides.append((plane, step, cells))
    for plane, step, cells in wides:
        wide[plane, step * SUB : (step + 1) * SUB, :] = cells
    row = lax.broadcasted_iota(jnp.int32, (SUB, LANES), 0)
    meta = own_meta[...]
    for message, at in ((from_left, 48), (from_right, 80)):
        first_rows = message[0:SUB, :]
        rows = jnp.broadcast_to(first_rows[:, SHIFT_R : SHIFT_R + 1], (SUB, LANES))
        cols = jnp.broadcast_to(first_rows[:, SHIFT_C : SHIFT_C + 1], (SUB, LANES))
        meta = jnp.where(lane >= at, rows, meta)
        meta = jnp.where(lane >= at + 16, cols, meta)

    def beside(rows, half):
        left = from_left[rows, :]
        right = from_right[rows, :]
        cells = jnp.zeros((SUB, LANES), jnp.float32)
        for band in range(bands):
            at = half * HALF + band * SLOT
            cells = jnp.where(lane >= band * H_BAND, turn(right, band * H_BAND - at), cells)
            cells = jnp.where(lane >= band * H_BAND + SLOT, turn(left, band * H_BAND + SLOT - at), cells)
        return cells

    even = is_even("row", meta)
    parts = []
    for part, half, near, next_rows, row_of in (
        (up_part, 0, slice(0, 8), slice(8, 16), 0),
        (down_part, 1, slice(end - 8, end), slice(end - 16, end - 8), 7),
    ):
        eight = beside(near, half)
        one = beside(next_rows, half)
        one = jnp.broadcast_to(one[row_of : row_of + 1], (SUB, LANES))
        coarse_rows = []
        for band in range(bands):
            rows = slice(0, C_SECOND) if half == 0 else slice(coarse_height - C_SECOND, coarse_height)
            second = wide[band, rows, :]
            first = turn(wide[bands + band, rows, :], HALF)
            coarse_rows.append(jnp.where(lanes_like(second) < HALF, second, first))
        parts.append([
            (part[E8:H8, :], E8), (eight, H8), (part[E1:H1, :], E1), (jnp.where(row == 0, one, meta), H1),
            (part[F4:CS, :], F4), *[(x, CS + k * C_SECOND) for k, x in enumerate(coarse_rows)],
        ])
    for (up, at), (down, _) in zip(*parts):
        even = is_even("row", up)
        swap_0[at : at + up.shape[0], :] = jnp.where(even, down, up)
        swap_1[at : at + up.shape[0], :] = jnp.where(even, up, down)


def coarse_flow_of(second, first, mask):
    def along_rows(x):
        return pltpu.roll(x, x.shape[0] - 1, 0) - pltpu.roll(x, 1, 0)

    def along_cols(x):
        return pltpu.roll(x, LANES - 1, 1) - pltpu.roll(x, 1, 1)

    bands = BANDS
    size = second.shape[0] // bands
    grad_rows = 0.125 * along_rows(second)
    grad_cols = 0.125 * along_cols(second)
    offset = 0.25 * (second - first)
    data = jnp.clip(offset, -LIMIT, LIMIT)
    yield

    def pull(grads):
        terms = data * grads
        return sum(terms[k * size : (k + 1) * size] for k in range(bands))

    def tall(x):
        return jnp.concatenate([x] * bands, axis=0)

    flow = [-mask * pull(grad_rows), -mask * pull(grad_cols)]
    extrapolated = [2.0 * x for x in flow]
    dual_rows = [0.0, 0.0]
    dual_cols = [0.0, 0.0]
    yield
    for step in range(1, STEPS):
        changes = [(along_rows(x), along_cols(x)) for x in extrapolated]
        yield
        data = data + offset + grad_rows * tall(extrapolated[0]) + grad_cols * tall(extrapolated[1])
        data = jnp.clip(data, -LIMIT, LIMIT)
        yield
        for c in range(2):
            rows = dual_rows[c] + changes[c][0]
            cols = dual_cols[c] + changes[c][1]
            scale = jnp.minimum(mask, (8.0 * ALPHA) * lax.rsqrt(rows * rows + cols * cols))
            dual_rows[c] = rows * scale
            dual_cols[c] = cols * scale
        yield
        divergences = [along_rows(dual_rows[c]) + along_cols(dual_cols[c]) for c in range(2)]
        yield
        pulls = [pull(grad_rows), pull(grad_cols)]
        yield
        for c in range(2):
            following = flow[c] + mask * ((1.0 / 64.0) * divergences[c] - pulls[c])
            extrapolated[c] = 2.0 * following - flow[c]
            flow[c] = following
        yield
    return flow


def columns_of_planes(planes):
    whole = lax.broadcasted_iota(jnp.int32, (LANES, COLUMNS), 1)
    lane = lax.broadcasted_iota(jnp.int32, (LANES, LANES), 1)
    strip = jnp.where(lane < S_MID, lane, jnp.where(lane < S_LEFT, lane + (COLUMNS - S_RIGHT), lane - LANES))
    return jnp.concatenate([x for x, wanted in ((whole, "whole"), (strip, "strip")) if wanted in planes], axis=1)


def upsample(flow, planes, target):
    column = columns_of_planes(planes)
    source = lax.broadcasted_iota(jnp.int32, column.shape, 0)
    spread = jnp.where(source - LEAD == lax.shift_right_arithmetic(column, 3), float(FACTOR), 0.0).astype(jnp.bfloat16)
    rows = flow[0].shape[0]
    wide = split_dot(UNIT * jnp.concatenate(flow, axis=0), spread)
    for c in range(2):
        for tile in range(column.shape[1] // LANES):
            target[c, tile] = wide[c * rows : (c + 1) * rows, tile * LANES : (tile + 1) * LANES]


def repeat_rows(spread, initial, cells):
    for c in range(2):
        for tile in range(initial.shape[1]):
            rows = [jnp.broadcast_to(spread[c, tile, cell : cell + 1, :], (SUB, LANES)) for cell in cells]
            initial[c, tile, GUARD : GUARD + SUB * len(cells), :] = jnp.concatenate(rows, axis=0)


def shift_whole(here, shift):
    turned = [turn_back(x, shift) for x in here]
    lane = lanes_like(here[0])
    return [
        jnp.where(lane + shift >= LANES, turned[1], turned[0]),
        jnp.where(lane + shift < 0, turned[0], turned[1]),
    ]


def edge_lanes(rows):
    lane = lanes_of(rows)
    return lane == LANES - 1, lane == 0


def columns_whole(fields, edges):
    rows = fields[0].shape[0]
    if rows not in edges:
        edges[rows] = edge_lanes(rows)
    last, first = edges[rows]
    ahead = [pltpu.roll(x, LANES - 1, 1) for x in fields]
    behind = [pltpu.roll(x, 1, 1) for x in fields]
    return [
        jnp.where(last, ahead[1], ahead[0]) - behind[0],
        ahead[1] - jnp.where(first, behind[0], behind[1]),
    ]


def rows_within(tall):
    size = tall.shape[0]
    return (pltpu.roll(tall, size - 1, 0) - pltpu.roll(tall, 1, 0))[SUB : size - SUB]


def columns_strip(field):
    return pltpu.roll(field, LANES - 1, 1) - pltpu.roll(field, 1, 1)


def strip_moved(window, centre, right, left):
    own = turn_back(window(centre[0]), centre[1])
    beyond_left = turn_back(window(left[0]), left[1])
    beyond_right = turn_back(window(right[0]), right[1])
    lane = lanes_like(own)
    beyond = jnp.where((lane >= S_LEFT) | (lane < S_MID), beyond_left, beyond_right)
    return own, beyond


def strip_joined(own, beyond):
    lane = lanes_like(own)
    is_beyond = lane >= S_RIGHT
    of_next = is_beyond & (lane != S_RIGHT) | (lane == 0)
    of_previous = is_beyond & (lane != LANES - 1) | (lane == S_RIGHT - 1)
    change = turn(jnp.where(of_next, beyond, own), -1) - turn(jnp.where(of_previous, beyond, own), 1)
    return jnp.where(is_beyond, beyond, own), change


def fine_steps(
    rows_total, chunk, columns, initial, extrap, dual_rows, dual_cols, change, dual_data,
    offsets, grads_rows, grads_cols, data_row, masks_of, result, kept, done=lambda k: None, first_pulls=None, depth=1,
):
    assert STEPS == 3
    planes = len(offsets)
    bands = offsets[0].shape[0]
    chunks = rows_total // chunk

    def places(k, trim=(0, 0)):
        start, size = k * chunk + trim[0], chunk - sum(trim)
        return pl.ds(GUARD + start, size), pl.ds(start, size), pl.ds(data_row(k) + trim[0], size)

    def row_change(ref, c, tile, at):
        return ref[c, tile, pl.ds(at.start + 1, at.size), :] - ref[c, tile, pl.ds(at.start - 1, at.size), :]

    def clip(x):
        return jnp.clip(x, -UNIT * LIMIT, UNIT * LIMIT)

    tiles = range(planes)

    for step in range(STEPS):
        source = initial if step == 0 else extrap
        final = step == STEPS - 1

        def dual(item, source=source, step=step):
            k, c = item
            at, own, _ = places(k)
            masks = masks_of(own)
            along = columns([source[c, tile, at, :] for tile in tiles])
            values = []
            for tile in tiles:
                rows = row_change(source, c, tile, at)
                cols = along[tile]
                if step > 0:
                    rows = rows + dual_rows[c, tile, at, :]
                    cols = cols + dual_cols[c, tile, own, :]
                scale = jnp.minimum(masks[tile], lax.rsqrt(rows * rows + cols * cols))
                values.append((rows * scale, cols * scale))
            return values

        def store_dual(item, values):
            k, c = item
            for tile, (rows, cols) in enumerate(values):
                dual_rows[c, tile, places(k)[0], :] = rows
                dual_cols[c, tile, places(k)[1], :] = cols

        staggered([(k, c) for k in range(chunks) for c in range(2)], dual, store_dual, depth)
        along_of = {}

        def primal(item, step=step, final=final, along_of=along_of):
            k, tile = item
            at, own, data = places(k, kept(k) if final else (0, 0))
            if k not in along_of:
                along_of[k] = [columns([dual_cols[c, t, own, :] for t in tiles]) for c in range(2)]
            mask = masks_of(own)[tile]
            start = [initial[c, tile, at, :] for c in range(2)]
            if step > 0:
                moved = [extrap[c, tile, at, :] - start[c] for c in range(2)]
            if step == 1:
                changes = [0.5 * x for x in moved]
            if step == 2:
                changes = [change[c, tile, own, :] for c in range(2)]
            pulls = [None, None]
            duals = []
            ready = step == 0 and first_pulls is not None
            if ready:
                pulls = [first_pulls[c, tile, own, :] for c in range(2)]
            for band in range(0 if ready else bands):
                gradient = (grads_rows[tile][band, data, :], grads_cols[tile][band, data, :])
                value = offsets[tile][band, data, :]
                if step > 0:
                    earlier = clip(value) if step == 1 else dual_data[band, tile, own, :]
                    value = (value + earlier) + (gradient[0] * moved[0] + gradient[1] * moved[1])
                value = clip(value)
                duals.append(value)
                for c in range(2):
                    term = value * gradient[c]
                    pulls[c] = term if pulls[c] is None else pulls[c] + term
            flows, nexts = [], []
            for c in range(2):
                divergence = row_change(dual_rows, c, tile, at) + along_of[k][c][tile]
                moving = (mask * (1.0 / 64.0)) * divergence - pulls[c]
                total = moving if step == 0 else changes[c] + moving
                flows.append((start[c] + total) * (1.0 / UNIT) if final else total)
                nexts.append(None if final else start[c] + (total + moving))
            return flows, nexts, duals

        def store_primal(item, results, step=step, final=final):
            k, tile = item
            flows, nexts, duals = results
            at, own, _ = places(k, kept(k) if final else (0, 0))
            for c in range(2):
                if final:
                    result[c, tile, own, :] = flows[c]
                else:
                    if step > 0:
                        change[c, tile, own, :] = flows[c]
                    extrap[c, tile, at, :] = nexts[c]
            if final:
                if tile == planes - 1:
                    done(k)
            elif step > 0:
                for band in range(bands):
                    dual_data[band, tile, own, :] = duals[band]

        staggered([(k, tile) for k in range(chunks) for tile in tiles], primal, store_primal, depth)


def clear_guards(*refs):
    for ref in refs:
        rows = ref.shape[2]
        zero = jnp.zeros((GUARD, LANES), jnp.float32)
        for c in range(2):
            for tile in range(ref.shape[1]):
                ref[c, tile, 0:GUARD, :] = zero
                ref[c, tile, rows - GUARD : rows, :] = zero


def fine_scratch(bands, planes, rows):
    guarded = pltpu.VMEM((2, planes, rows + 2 * GUARD, LANES), jnp.float32)
    plain = pltpu.VMEM((2, planes, rows, LANES), jnp.float32)
    return [guarded, guarded, guarded, plain, plain, pltpu.VMEM((bands, planes, rows, LANES), jnp.float32)]


def pieces(bands, height, rows):
    assert (height - 2 * SUB) % rows == 0
    return [(band, row) for row in range(SUB, height - SUB, rows) for band in range(bands)]


def whole_terms_kernel(
    second_0, second_1, first_0, first_1, coarse, own_meta,
    offset, grad_rows, grad_cols, initial, strip_e, strip_f, up, down, moved, spread,
):
    seconds, firsts = (second_0, second_1), (first_0, first_1)
    bands, height, _ = second_0.shape
    block = 40
    coarse_height = coarse.shape[0] // (2 * bands)
    centre = shift_at(own_meta, 0, 0)
    def windows(band, row, rows):
        here = [ref[band, pl.ds(row + centre[0], rows), :].reshape(-1, LANES) for ref in seconds]
        return shift_whole(here, centre[1])

    woven = Woven(coarse_flow_of(coarse[0 : bands * coarse_height, :], coarse[bands * coarse_height :, :], 1.0))

    def strips_of(item):
        band, row = item
        rows = slice(row, row + LANES)
        return strip_own([ref[band, rows, :] for ref in seconds]), strip_own([ref[band, rows, :] for ref in firsts])

    def store_strips(item, results):
        band, row = item
        strip_e[band, row : row + LANES, :], strip_f[band, row : row + LANES, :] = results

    staggered([(band, row) for band in range(bands) for row in range(0, height, LANES)], strips_of, store_strips, 1, woven)

    ends = [(row, windows(slice(None), row, SUB)) for row in (SUB // 2, height - SUB - SUB // 2)]
    for row, values in ends:
        for tile in range(2):
            moved[tile, :, row : row + SUB, :] = values[tile].reshape(bands, SUB, LANES)

    def store_moved(item, values):
        band, row = item
        for tile in range(2):
            moved[tile, band, row : row + 120, :] = values[tile]

    staggered(pieces(bands, height, 120), lambda item: windows(*item, 120), store_moved, 3, woven)

    edges = {}

    def values_of(item):
        band, row = item
        rows = slice(row, row + block)
        values = [moved[tile, band, rows, :] for tile in range(2)]
        along = columns_whole(values, edges)
        own = [ref[band, rows, :] for ref in firsts]
        return [(0.25 * UNIT) * (x - y) for x, y in zip(values, own)], [0.125 * x for x in along]

    def store_values(item, results):
        band, row = item
        offsets, gradients = results
        data = slice(row + HALO, row + HALO + block)
        for tile in range(2):
            offset[tile, band, data, :] = offsets[tile]
            grad_cols[tile, band, data, :] = gradients[tile]

    staggered(pieces(bands, height, block), values_of, store_values, 3, woven)

    def gradient_of(item):
        band, row = item
        return [0.125 * rows_within(moved[tile, band, row - SUB : row + 40 + SUB, :]) for tile in range(2)]

    def store_gradient(item, results):
        band, row = item
        for tile in range(2):
            grad_rows[tile, band, row + HALO : row + HALO + 40, :] = results[tile]

    staggered(pieces(bands, height, 40), gradient_of, store_gradient, 3, woven)

    parts = []
    for band in range(bands):
        for second, first in zip(seconds, firsts):
            parts.append((
                second[band, 0:16, :], first[band, 0:8, :],
                second[band, height - 16 : height, :], first[band, height - 8 : height, :],
            ))
    for k, (second_top, first_top, second_end, first_end) in enumerate(parts):
        up[E8 + 8 * k : E8 + 8 * k + 8, :] = second_top[0:8]
        up[E1 + k : E1 + k + 1, :] = second_top[8:9]
        up[F4 + 4 * k : F4 + 4 * k + 4, :] = first_top[0:4]
        down[E8 + 8 * k : E8 + 8 * k + 8, :] = second_end[8:16]
        down[E1 + k : E1 + k + 1, :] = second_end[7:8]
        down[F4 + 4 * k : F4 + 4 * k + 4, :] = first_end[4:8]
    for target in (up, down):
        for start, end in ((H8, E1), (H1, F4), (CS, ROW_MESSAGE)):
            target[start:end, :] = jnp.zeros((end - start, LANES), jnp.float32)

    upsample(woven.finish(), ("whole",), spread)
    clear_guards(initial)
    rows_total = initial.shape[2] - 2 * GUARD
    repeat_rows(spread, initial, [BEGIN // FACTOR + k for k in range(rows_total // SUB)])


def whole_steps_kernel(
    initial, offset, grad_rows, grad_cols, result, extrap, dual_rows, dual_cols, change, dual_data
):
    rows_total = result.shape[2]
    clear_guards(extrap, dual_rows)
    chunk = 16
    edges = {}
    fine_steps(
        rows_total, chunk, lambda fields: columns_whole(fields, edges),
        initial, extrap, dual_rows, dual_cols, change, dual_data,
        *[[ref.at[tile] for tile in range(2)] for ref in (offset, grad_rows, grad_cols)],
        lambda k: HALO + BEGIN + k * chunk, lambda own: (1.0, 1.0), result,
        lambda k: (SUB * (k == 0), SUB * (k == rows_total // chunk - 1)), depth=3,
    )


def strip_kernel(
    count, strip_e, strip_f, from_left, from_right, wide, own_message, whole,
    middle, strip_out, first_ends, offset, grad_rows, grad_cols,
    both, moved, result, spread, initial, extrap, dual_rows, dual_cols, change, dual_data,
):
    bands, height, _ = strip_e.shape
    block = 40
    coarse_height = height // FACTOR
    coarse_width = COLUMNS // FACTOR
    rows_total = height - 2 * BEGIN
    lane = lanes_of()
    centre, right, left = shifts_of(own_message)
    has_left, has_right = neighbours("col", count)
    exists = jnp.where(lane < S_RIGHT, 1.0, jnp.where(lane < S_LEFT, has_right, has_left))

    def tall_factor(rows):
        return 0.125 * jnp.concatenate([exists] * (rows // SUB), axis=0)

    mask = jnp.where(lane < LEAD, has_left, jnp.where(lane < LEAD + coarse_width, 1.0, has_right))
    mask = jnp.concatenate([mask] * (coarse_height // SUB), axis=0)
    cells = [wide[k * bands : (k + 1) * bands].reshape(bands * coarse_height, LANES) for k in range(2)]
    woven = Woven(coarse_flow_of(*cells, mask))

    def halves(row, rows):
        half = row // (height // 2)
        start = row - half * (height // 2)
        return half, slice(start, start + rows)

    def second_of(item):
        band, row = item
        half, message = halves(row, LANES)
        return strip_second(strip_e[band, row : row + LANES, :], from_left, from_right, message, half, band)

    def store_second(item, value):
        band, row = item
        strip_out[band, row : row + LANES, :] = value

    staggered([(band, row) for row in range(0, height, LANES) for band in range(bands)], second_of, store_second, 1, woven)

    def first_of(band, row, rows):
        half, message = halves(row, rows)
        return strip_first(strip_f[band, row : row + rows, :], from_left, from_right, message, half, band)

    firsts = [(end, band, first_of(band, (0, height - SUB)[end], SUB)) for end in range(2) for band in range(bands)]
    for end, band, value in firsts:
        first_ends[end, band] = value

    def windows(band, row, rows):
        return strip_moved(
            lambda shift: strip_out[band, pl.ds(row + shift, rows), :].reshape(-1, LANES), centre, right, left
        )

    ends = [
        (row, strip_joined(*windows(slice(None), row, SUB))[0]) for row in (SUB // 2, height - SUB - SUB // 2)
    ]
    for row, value in ends:
        moved[:, row : row + SUB, :] = value.reshape(bands, SUB, LANES)

    def store_moved(item, values):
        band, row = item
        for k in range(2):
            both[k, band, row : row + 120, :] = values[k]

    staggered(pieces(bands, height, 120), lambda item: windows(*item, 120), store_moved, 3, woven)

    factor = tall_factor(block)

    def values_of(item):
        band, row = item
        value, along = strip_joined(*[both[k, band, row : row + block, :] for k in range(2)])
        return value, (0.25 * UNIT) * (value - first_of(band, row, block)), factor * along

    def store_values(item, results):
        band, row = item
        data = slice(row + HALO, row + HALO + block)
        moved[band, row : row + block, :], offset[band, data, :], grad_cols[band, data, :] = results

    staggered(pieces(bands, height, block), values_of, store_values, 3, woven)

    def gradient_of(item):
        band, row = item
        return factor * rows_within(moved[band, row - SUB : row + block + SUB, :])

    def store_gradient(item, value):
        band, row = item
        grad_rows[band, row + HALO : row + HALO + block, :] = value

    staggered(pieces(bands, height, block), gradient_of, store_gradient, 3, woven)

    upsample(woven.finish(), ("strip",), spread)
    clear_guards(initial, extrap, dual_rows)
    repeat_rows(spread, initial, [BEGIN // FACTOR + k for k in range(rows_total // SUB)])

    chunk = 16
    masks = jnp.concatenate([exists] * (chunk // SUB), axis=0)
    fine_steps(
        rows_total, chunk, lambda fields: [columns_strip(fields[0])],
        initial, extrap, dual_rows, dual_cols, change, dual_data, [offset], [grad_rows], [grad_cols],
        lambda k: HALO + BEGIN + k * chunk, lambda own: (masks[: own.size],), result,
        lambda k: (SUB * (k == 0), SUB * (k == rows_total // chunk - 1)), depth=4,
    )
    join(whole, result.at[:, 0], middle, slice(SUB, rows_total - SUB))


def join(whole, strip, target, rows):
    lane = lanes_of(rows.stop - rows.start)
    values = []
    for c in range(2):
        edge = strip[c, rows, :]
        start = jnp.where(lane < EDGE, edge, whole[c, 0, rows, :])
        values.append((start, jnp.where(lane >= LANES - EDGE, turn(edge, S_TURN), whole[c, 1, rows, :])))
    for c in range(2):
        target[c, rows, 0:LANES], target[c, rows, LANES:COLUMNS] = values[c]


def outer_kernel(
    counts, second_0, second_1, first_0, first_1, strip_e, first_ends, wide, got_1, got_0, middle, own_message,
    _wo, _wr, _wc, _so, _sr, _sc,
    flow_out, coarse_out, whole_offset, whole_rows, whole_cols, strip_offset, strip_rows, strip_cols,
    from_up, from_down, extended, tall, spread, masks, result, joined, coarse_result, pulls, sems,
    initial, extrap, dual_rows, dual_cols, change, dual_data,
):
    bands, height, _ = second_0.shape
    coarse_height = height // FACTOR
    coarse_width = COLUMNS // FACTOR
    rows_total = 2 * EACH
    lane = lanes_of()

    put_middle = pltpu.make_async_copy(
        middle.at[:, pl.ds(MARGIN - BEGIN, height - 2 * MARGIN), :],
        flow_out.at[:, pl.ds(MARGIN, height - 2 * MARGIN), :],
        sems.at[0],
    )
    put_middle.start()
    own, one, other = [shifts_of(message) for message in (own_message, got_0, got_1)]
    odd = lax.axis_index("row") % 2

    def of_row(for_even, for_odd):
        return [tuple(jnp.where(odd == 0, x, y) for x, y in zip(*pair)) for pair in zip(for_even, for_odd)]

    above, below = of_row(other, one), of_row(one, other)

    other = without_ends(got_1, "row", counts[0])
    even = is_even("row", got_0)
    from_down[...] = jnp.where(even, got_0[...], other)
    from_up[...] = jnp.where(even, other, got_0[...])

    has_up, has_down = neighbours("row", counts[0])
    has_left, has_right = neighbours("col", counts[1])
    exists = jnp.where(lane < S_RIGHT, 1.0, jnp.where(lane < S_LEFT, has_right, has_left))

    zero = jnp.zeros((SUB, LANES), jnp.float32)
    tall_rows = coarse_height + 2 * LEAD
    parts = []
    fill = jnp.zeros((LEAD - C_SECOND, LANES), jnp.float32)
    for plane in range(2 * bands):
        at = CS + C_SECOND * (plane % bands)
        ends = [turn(message[at : at + C_SECOND, :], HALF * (plane // bands)) for message in (from_up, from_down)]
        parts.append([fill, ends[0], wide[plane], ends[1], fill])
    for plane, values in enumerate(parts):
        tall[plane] = jnp.concatenate(values, axis=0)
    across = jnp.where(lane < LEAD, has_left, jnp.where(lane < LEAD + coarse_width, 1.0, has_right))
    mask = jnp.concatenate([across * has_up] + [across] * (coarse_height // SUB) + [across * has_down], axis=0)
    for end in range(2):
        message = (from_up, from_down)[end]
        beside = message[H8 : H8 + 8, :]
        beside_one = jnp.broadcast_to(message[H1 : H1 + 1, :], (SUB, LANES))
        parts = []
        for band in range(bands):
            eights = [message[E8 + 8 * k : E8 + 8 * k + 8, :] for k in (2 * band, 2 * band + 1)]
            ones = [jnp.broadcast_to(message[E1 + k : E1 + k + 1, :], (SUB, LANES)) for k in (2 * band, 2 * band + 1)]
            eights.append(strip_halo(strip_own(eights), beside, band, 0, REACH))
            ones.append(strip_halo(strip_own(ones), beside_one, band, 0, REACH))
            for tile, (eight, one) in enumerate(zip(eights, ones)):
                source = (second_0, second_1, strip_e)[tile]
                if end == 0:
                    parts.append((tile, band, [one, eight, source[band, 0:24, :]]))
                else:
                    parts.append((tile, band, [source[band, height - 24 : height, :], eight, one]))
        for tile, band, values in parts:
            extended[end, tile, band] = jnp.concatenate(values, axis=0)
    cells = [tall[k * bands : (k + 1) * bands].reshape(bands * tall_rows, LANES) for k in range(2)]
    woven = Woven(coarse_flow_of(*cells, mask))
    edges = {}
    rows_data = whole_offset.shape[2]
    exists_tall = jnp.concatenate([exists] * bands, axis=0)

    def rows_of(halo, end):
        if halo:
            return slice(0, SUB) if end == 0 else slice(rows_data - SUB, rows_data)
        return slice(HALO, HALO + SUB) if end == 0 else slice(rows_data - HALO - SUB, rows_data - HALO)

    def values_of(item):
        halo, end = item
        message = (from_up, from_down)[end]
        base = (SUB, 3 * SUB)[end] if halo else 2 * SUB
        shifts = (above, below)[end] if halo else own
        factor = 0.125 * (has_up, has_down)[end] if halo else 0.125

        def here(tile, shift):
            return extended[end, tile, :, pl.ds(base + shift, SUB), :].reshape(-1, LANES)

        def down_up(tile, shift):
            return here(tile, shift + 1) - here(tile, shift - 1)

        own_rows = slice(0, SUB) if end == 0 else slice(height - SUB, height)
        if halo:
            firsts = [[], [], []]
            for band in range(bands):
                eights = []
                for k in (2 * band, 2 * band + 1):
                    four = message[F4 + 4 * k : F4 + 4 * k + 4, :]
                    eights.append(jnp.concatenate([four, four], axis=0))
                eights.append(strip_halo(strip_own(eights), message[H8 : H8 + 8, :], band, REACH, DEPTH))
                for tile in range(3):
                    firsts[tile].append(eights[tile])
            firsts = [jnp.concatenate(x, axis=0) for x in firsts]
        else:
            firsts = [x.reshape(-1, LANES) for x in (first_0[:, own_rows, :], first_1[:, own_rows, :], first_ends[end])]
        centre = shifts[0]
        values = shift_whole([here(tile, centre[0]) for tile in range(2)], centre[1])
        changes = shift_whole([down_up(tile, centre[0]) for tile in range(2)], centre[1])
        along = columns_whole(values, edges)
        value, across_cols = strip_joined(*strip_moved(lambda shift: here(2, shift), *shifts))
        change_rows, _ = strip_joined(*strip_moved(lambda shift: down_up(2, shift), *shifts))
        return (
            [(0.25 * UNIT) * (x - y) for x, y in zip([*values, value], firsts)],
            [*[factor * x for x in changes], (factor * exists_tall) * change_rows],
            [*[factor * x for x in along], (factor * exists_tall) * across_cols],
        )

    def store_values(item, results):
        rows = rows_of(*item)
        for values, whole, strip in zip(
            results, (whole_offset, whole_rows, whole_cols), (strip_offset, strip_rows, strip_cols)
        ):
            values = [x.reshape(bands, SUB, LANES) for x in values]
            for tile in range(2):
                whole[tile, :, rows, :] = values[tile]
            strip[:, rows, :] = values[2]

    staggered([(halo, end) for halo in (True, False) for end in range(2)], values_of, store_values, 3, woven)

    chunk = 16
    per = EACH // chunk

    def data_row(k):
        return k // per * (rows_data - EACH) + k % per * chunk

    offsets = [whole_offset.at[0], whole_offset.at[1], strip_offset]
    grads_rows = [whole_rows.at[0], whole_rows.at[1], strip_rows]
    grads_cols = [whole_cols.at[0], whole_cols.at[1], strip_cols]

    def pulls_of(item):
        k, tile = item
        data = pl.ds(k * (rows_data - EACH), EACH)
        duals = [jnp.clip(offsets[tile][band, data, :], -UNIT * LIMIT, UNIT * LIMIT) for band in range(bands)]
        return [
            sum(duals[band] * grads[tile][band, data, :] for band in range(bands)) for grads in (grads_rows, grads_cols)
        ]

    def store_pulls(item, values):
        k, tile = item
        for c in range(2):
            pulls[c, tile, k * EACH : (k + 1) * EACH, :] = values[c]

    staggered([(k, tile) for k in range(2) for tile in range(3)], pulls_of, store_pulls, 1, woven)

    flow = woven.finish()
    for c in range(2):
        coarse_result[c] = turn(flow[c][LEAD : LEAD + coarse_height], -LEAD)[:, :coarse_width]
    put_coarse = pltpu.make_async_copy(coarse_result, coarse_out, sems.at[1])
    upsample(flow, ("whole", "strip"), spread)
    clear_guards(initial, extrap, dual_rows)
    each = EACH // SUB
    repeat_rows(
        spread, initial,
        [LEAD - 1 + k for k in range(each)] + [tall_rows - LEAD + 1 - each + k for k in range(each)],
    )

    for i, value in enumerate((jnp.ones((SUB, LANES), jnp.float32), exists)):
        masks[i] = jnp.concatenate([value * has_up] + [value] * (rows_total // SUB - 2) + [value * has_down], axis=0)

    def masks_of(rows):
        if SUB <= rows.start and rows.start + rows.size <= rows_total - SUB:
            return (1.0, 1.0, jnp.concatenate([exists] * (rows.size // SUB), axis=0))
        whole = masks[0, rows, :]
        return (whole, whole, masks[1, rows, :])

    edges = {}
    puts = [
        pltpu.make_async_copy(
            joined.at[:, pl.ds(k * EACH + SUB, MARGIN), :],
            flow_out.at[:, pl.ds(k * (height - MARGIN), MARGIN), :],
            sems.at[2 + k],
        )
        for k in range(2)
    ]

    def finish(k):
        if k % per == per - 1:
            at = k // per * EACH + SUB
            join(result, result.at[:, 2], joined, slice(at, at + MARGIN))

    fine_steps(
        rows_total, chunk, lambda fields: columns_whole(fields[:2], edges) + [columns_strip(fields[2])],
        initial, extrap, dual_rows, dual_cols, change, dual_data,
        offsets, grads_rows, grads_cols, data_row, masks_of, result,
        lambda k: (SUB * (k % per == 0), SUB * (k % per == per - 1)), finish, pulls, depth=4,
    )
    puts.append(put_coarse)
    for put in puts:
        put.start()
    put_middle.wait()
    for put in puts:
        put.wait()


def swap_with(message, axis, start):
    names = ("row", "col")
    sizes = [lax.axis_size(name) for name in names]
    along = names.index(axis)
    count, others = sizes[along], sizes[1 - along]

    def number(place, other):
        row, col = (place, other) if along == 0 else (other, place)
        return row * sizes[1] + col

    pairs = [(number(i, k), number(i + 1, k)) for i in range(start, count - 1, 2) for k in range(others)]
    if start and axis == "col":
        pairs += [(number(i, k), number(i, k + 1)) for i in (0, count - 1) for k in range(0, others, 2)]
    elif start:
        pairs += [(number(0, k), number(count - 1, k)) for k in (0, others - 1)]
        pairs += [(number(i, k), number(i, k + 1)) for i in (0, count - 1) for k in range(1, others - 1, 2)]
    return lax.ppermute(message, names, pairs + [(j, i) for i, j in pairs])


def local(frame_first, frame_second, shifts):
    bands, height, width = frame_first.shape
    assert bands == 4 and width == COLUMNS and height % LANES == 0
    assert lax.axis_size("row") % 2 == 0 and lax.axis_size("col") % 2 == 0
    coarse_height = height // FACTOR
    coarse_width = width // FACTOR
    vmem = pl.BlockSpec(memory_space=pltpu.VMEM)
    hbm = pl.BlockSpec(memory_space=pltpu.HBM)
    tall_rows = coarse_height + 2 * LEAD
    inner_rows = height - 2 * BEGIN

    def shape(*sizes):
        return jax.ShapeDtypeStruct(sizes, jnp.float32)

    def scratch(*sizes):
        return pltpu.VMEM(sizes, jnp.float32)

    def call(kernel, name, arguments, outs, scratches=(), flops=1_000_000, **more):
        more = {"in_specs": [vmem] * len(arguments), "out_specs": (vmem,) * len(outs), **more}
        return pl.pallas_call(
            kernel,
            out_shape=tuple(outs),
            scratch_shapes=list(scratches),
            compiler_params=pltpu.CompilerParams(vmem_limit_bytes=24 * 1024 * 1024),
            cost_estimate=pl.CostEstimate(flops=flops, bytes_accessed=1_000_000, transcendentals=0),
            name=name,
            **more,
        )(*arguments)

    plane = shape(bands, height, LANES)
    column_message = shape(height // 2, LANES)
    row_message = shape(ROW_MESSAGE, LANES)
    whole_data = shape(2, bands, height + 2 * HALO, LANES)
    strip_data = shape(bands, height + 2 * HALO, LANES)

    *frames, coarse, swap_0, swap_1, own_meta = call(
        first_kernel,
        "means_and_message",
        [pltpu.with_memory_space_constraint(x, pltpu.HBM) for x in (frame_second, frame_first, shifts)],
        [*[plane] * 4, shape(2 * bands * coarse_height, LANES), column_message, column_message, shape(SUB, LANES)],
        [
            pltpu.SMEM((1, 1, 2), jnp.int32),
            pltpu.SemaphoreType.DMA((2, bands, 2)),
            pltpu.SemaphoreType.DMA,
        ],
        in_specs=[hbm] * 3,
    )
    got_0 = swap_with(swap_0, "col", 0)
    got_1 = swap_with(swap_1, "col", 1)

    *whole_terms, initial, strip_e, strip_f, up_part, down_part = call(
        whole_terms_kernel,
        "whole_terms",
        [*frames, coarse, own_meta],
        [
            *[whole_data] * 3, shape(2, 2, inner_rows + 2 * GUARD, LANES),
            plane, plane, row_message, row_message,
        ],
        [
            scratch(2, bands, height, LANES), scratch(2, 2, coarse_height, LANES),
        ],
        flops=8_000_000,
    )
    (whole,) = call(
        whole_steps_kernel,
        "whole_steps",
        [initial, *whole_terms],
        [shape(2, 2, inner_rows, LANES)],
        fine_scratch(bands, 2, inner_rows)[1:],
        flops=20_000_000,
    )

    swap_0, swap_1, from_left, from_right, wide = call(
        functools.partial(message_kernel, lax.axis_size("col")),
        "row_messages",
        [coarse, own_meta, got_0, got_1, up_part, down_part, whole],
        [row_message, row_message, column_message, column_message, shape(2 * bands, coarse_height, LANES)],
    )
    got_1 = swap_with(swap_1, "row", 1)
    got_0 = swap_with(swap_0, "row", 0)

    middle, strip_e, first_ends, *strip_terms = call(
        functools.partial(strip_kernel, lax.axis_size("col")),
        "strip",
        [strip_e, strip_f, from_left, from_right, wide, swap_0, whole],
        [shape(2, inner_rows, width), plane, shape(2, bands, SUB, LANES), *[strip_data] * 3],
        [
            scratch(2, bands, height, LANES),
            scratch(bands, height, LANES),
            scratch(2, 1, inner_rows, LANES),
            scratch(2, 1, coarse_height, LANES),
            *fine_scratch(bands, 1, inner_rows),
        ],
        flops=16_000_000,
    )

    flow, coarse_flow, *_ = call(
        functools.partial(outer_kernel, (lax.axis_size("row"), lax.axis_size("col"))),
        "outer_rows",
        [
            *frames, strip_e, first_ends, wide, got_1, got_0, middle, swap_0,
            *whole_terms, *strip_terms,
        ],
        [shape(2, height, width), shape(2, coarse_height, coarse_width), *[whole_data] * 3, *[strip_data] * 3],
        [
            scratch(ROW_MESSAGE, LANES),
            scratch(ROW_MESSAGE, LANES),
            scratch(2, 3, bands, 40, LANES),
            scratch(2 * bands, tall_rows, LANES),
            scratch(2, 3, tall_rows, LANES),
            scratch(2, 2 * EACH, LANES),
            scratch(2, 3, 2 * EACH, LANES),
            scratch(2, 2 * EACH, width),
            scratch(2, coarse_height, coarse_width),
            scratch(2, 3, 2 * EACH, LANES),
            pltpu.SemaphoreType.DMA((4,)),
            *fine_scratch(bands, 3, 2 * EACH),
        ],
        out_specs=(hbm, hbm) + (vmem,) * 6,
        input_output_aliases={11 + k: 2 + k for k in range(6)},
    )
    return (flow, coarse_flow)


def solution(mesh):
    return jax.shard_map(
        local,
        mesh=mesh,
        in_specs=(P(None, "row", "col"), P(None, "row", "col"), P("row", "col", None)),
        out_specs=(P(None, "row", "col"), P(None, "row", "col")),
        check_vma=False,
    )
```
